32 devices in a mesh: runs: 2 (over x), xb: 8 (over z, y), yb: 2 (over core).
Axes of the slice: x: 2, y: 2, z: 4, core: 2. Of those that a mesh axis runs over, the one named last changes fastest.
Arguments:
- state: float32 [64, 3, 256, 256], P(('runs', 'xb', 'yb')), parts along dimension 0, may hold values from -12 to 12, as said below
- bed: float32 [64, 256, 256], P(('runs', 'xb', 'yb')), parts along dimension 0, may hold values from 0 to 1.5
- manning: float32 [64, 256, 256], P(('runs', 'xb', 'yb')), parts along dimension 0, may hold values from 0.02 to 0.3
- neighbours: int32 [64, 4], P('runs'), parts along dimension 0, may hold values from -1 to 31, as said below
- wet: int32 [3, 64], P(None, 'runs'), parts along dimension 1, may hold values from 0 to 1
- moves: int32 [3, 32], P(None, 'runs'), parts along dimension 1, may hold values from 0 to 1
Outputs:
- final: float32 [64, 3, 256, 256], P(('runs', 'xb', 'yb')), parts along dimension 0
The draws below stay inside these ranges and needn't reach their ends.
There are 2 independent parts, one for each index of `runs`. The reference program is written for one: setup_inputs(seed, part) draws one part's arguments, and reference() takes and returns one part's arrays. A program takes and returns all parts, laid end to end along the dimension named above; each array names one. Nothing has to cross between parts.
Inputs may be any that keep to these rules, and one draw needn't show every extreme that they name: `state`: component 0 is the depth h, positive; components 1 and 2 are momenta with magnitude below 1.5 h. `neighbours`: the tiles form a grid of 8 by 4 tiles, entries 0 to 3 naming the tile to the west, east, south and north; the device of xb index i and yb index j starts with the 1 by 2 block of x-blocks i * 1 onward and y-blocks j * 2 onward, in any order within it.
All inputs are finite; a program needn't handle non-finite values.
Results may differ from the reference program's by a relative error of at most 0.00002.
Values sent between devices are 32-bit elements; how exact they have to be, the bound alone decides.
No kernel may reach another device: no remote copies, remote signals or barrier semaphores. Data moves between devices by JAX's collectives and lax.ppermute only.
A program may use at most 64 MiB of HBM per device.

```python
import math
import jax
import jax.numpy as jnp
from jax import lax

TILE = 256
TBX = 1
TBY = 2
STEPS = 3
TILES_DEV = 2
DEVS = 16
TILES = 32
N_XB = 8
N_YB = 2


def draw_state(key, part):
    key = jax.random.fold_in(key, 11)
    keys = jax.random.split(key, 4)
    depth_tile = jnp.exp(jax.random.uniform(keys[0], (TILES, 1, 1), jnp.float32, jnp.log(0.4), jnp.log(4.0)))
    spread = jax.random.uniform(keys[1], (TILES, TILE, TILE), jnp.float32, 0.5, 1.5)
    pace = jax.random.uniform(keys[2], (TILES, 1, 1, 1), jnp.float32, 0.2, 1.0)
    depth = depth_tile * spread
    velocity = pace * jax.random.uniform(keys[3], (TILES, 2, TILE, TILE), jnp.float32, -1.0, 1.0)
    return jnp.concatenate([depth[:, None], depth[:, None] * velocity], axis=1)


def draw_neighbours(key, part):
    key = jax.random.fold_in(key, 23)
    block = TBX * TBY
    devices = N_XB * N_YB
    orders = jax.vmap(lambda sub: jax.random.permutation(sub, block))(jax.random.split(key, devices)).astype(jnp.int32)
    grid_x = TBX * N_XB
    grid_y = TBY * N_YB
    cell_x = jnp.broadcast_to(jnp.arange(grid_x, dtype=jnp.int32)[:, None], (grid_x, grid_y))
    cell_y = jnp.broadcast_to(jnp.arange(grid_y, dtype=jnp.int32)[None, :], (grid_x, grid_y))

    def slot_of(along_x, along_y):
        along_x = jnp.clip(along_x, 0, grid_x - 1)
        along_y = jnp.clip(along_y, 0, grid_y - 1)
        owner = along_x // TBX * N_YB + along_y // TBY
        position = along_x % TBX * TBY + along_y % TBY
        return owner * block + orders[owner, position]
    west = jnp.where(cell_x > 0, slot_of(cell_x - 1, cell_y), -1)
    east = jnp.where(cell_x < grid_x - 1, slot_of(cell_x + 1, cell_y), -1)
    south = jnp.where(cell_y > 0, slot_of(cell_x, cell_y - 1), -1)
    north = jnp.where(cell_y < grid_y - 1, slot_of(cell_x, cell_y + 1), -1)
    values = jnp.stack([west, east, south, north], -1).reshape(-1, 4)
    own = slot_of(cell_x, cell_y).reshape(-1)
    return jnp.zeros((TILES, 4), jnp.int32).at[own].set(values.astype(jnp.int32))


def draw_wet(key, part):
    key = jax.random.fold_in(key, 37)
    first, second = jax.random.split(key)
    devices = N_XB * N_YB
    level = jax.random.randint(first, (STEPS, devices, 1), 15, 101)
    chance = jax.random.randint(second, (STEPS, devices, TILES_DEV), 0, 100)
    flags = (chance < level).astype(jnp.int32).reshape(STEPS, TILES)
    return flags.at[:, 0].set(1)


def place_ends(result, stream_key, smallest, high):
    shape = result.shape
    spot = [jax.random.randint(jax.random.fold_in(stream_key, axis), (), 0, shape[axis]) for axis in range(len(shape))]
    result = result.at[tuple(spot)].set(smallest)
    longest = shape.index(max(shape))
    spot[longest] = (spot[longest] + 1) % shape[longest]
    return result.at[tuple(spot)].set(high)


def steps_of(stream_key, extent, pieces, least, top_value):
    def one(dim, shards_of):
        draws = jax.random.uniform(jax.random.fold_in(jax.random.fold_in(stream_key, 6), dim), (shards_of,), jnp.float32, least / len(pieces), top_value / len(pieces))
        return jnp.repeat(jnp.exp(draws), extent[dim] // shards_of).reshape((-1,) + (1,) * (len(extent) - dim - 1))

    level = one(*pieces[0])
    for cut in pieces[1:]:
        level = level * one(*cut)
    return level


def setup_inputs(seed: int = 0, part: int = 0) -> dict:
    key_list = jax.random.split(jax.random.key(seed), 7)
    part_splits = jax.random.split(jax.random.fold_in(key_list[6], part), 7)
    state = draw_state(jax.random.fold_in(jax.random.fold_in(key_list[6], part), 71), part)
    bed = jnp.clip(1.5 * jax.random.uniform(part_splits[1], (TILES, TILE, TILE), jnp.float32) ** steps_of(part_splits[1], (TILES, TILE, TILE), ((0, 16),), -0.2, 0.2), 0.0, 1.5)
    manning = jnp.clip(jnp.exp(math.log(0.3) - 2.7080503 * jax.random.uniform(part_splits[2], (TILES, TILE, TILE), jnp.float32) ** steps_of(part_splits[2], (TILES, TILE, TILE), ((0, 16),), -0.2, 0.2)), 0.02, 0.3)
    neighbours = draw_neighbours(jax.random.fold_in(jax.random.fold_in(key_list[6], part), 71), part)
    wet = draw_wet(jax.random.fold_in(jax.random.fold_in(key_list[6], part), 71), part)
    moves = place_ends(jax.random.randint(part_splits[5], (STEPS, DEVS), 0, TILES_DEV), jax.random.fold_in(part_splits[5], 1), 0, TILES_DEV - 1).astype(jnp.int32)
    return {"state": state, "bed": bed, "manning": manning, "neighbours": neighbours, "wet": wet, "moves": moves}


GRAVITY = 9.81
SPACING = 5.0
COURANT = 0.2
OPPOSITE = (1, 0, 3, 2)
MIRROR = ((1.0, -1.0, 1.0, 1.0), (1.0, -1.0, 1.0, 1.0), (1.0, 1.0, -1.0, 1.0), (1.0, 1.0, -1.0, 1.0))

def physical(fields, normal):
    depth = fields[0]
    push_x = fields[1]
    push_y = fields[2]
    vel_x = push_x / depth
    vel_y = push_y / depth
    celerity = jnp.sqrt(GRAVITY * depth)
    pressure = 0.5 * GRAVITY * depth * depth
    if normal == 0:
        flux = jnp.stack([push_x, push_x * vel_x + pressure, push_x * vel_y])
        speed = jnp.abs(vel_x) + celerity
    else:
        flux = jnp.stack([push_y, push_y * vel_x, push_y * vel_y + pressure])
        speed = jnp.abs(vel_y) + celerity
    return (flux, speed)

def sweep(fields, lower, upper, axis, normal):
    extended = jnp.concatenate([jnp.expand_dims(lower, axis + 1), fields, jnp.expand_dims(upper, axis + 1)], axis=axis + 1)
    count = extended.shape[axis + 1]
    left = lax.slice_in_dim(extended, 0, count - 1, axis=axis + 1)
    right = lax.slice_in_dim(extended, 1, count, axis=axis + 1)
    flux_left, speed_left = physical(left, normal)
    flux_right, speed_right = physical(right, normal)
    wave = jnp.maximum(speed_left, speed_right)
    face = 0.5 * (flux_left + flux_right) - 0.5 * wave * (right[:3] - left[:3])
    change = lax.slice_in_dim(face, 1, count - 1, axis=axis + 1) - lax.slice_in_dim(face, 0, count - 2, axis=axis + 1)
    ground = extended[3]
    slope = (lax.slice_in_dim(ground, 2, count, axis=axis) - lax.slice_in_dim(ground, 0, count - 2, axis=axis)) / (2.0 * SPACING)
    return (change, slope)

def advance(tile, ground, rough, ghost, delta):
    fields = jnp.concatenate([tile, ground[None]], 0)
    change_x, slope_x = sweep(fields, ghost[0], ghost[1], 0, 0)
    change_y, slope_y = sweep(fields, ghost[2], ghost[3], 1, 1)
    ratio = delta / SPACING
    change = change_x + change_y
    depth = tile[0] - ratio * change[0]
    push_x = tile[1] - ratio * change[1] - delta * GRAVITY * tile[0] * slope_x
    push_y = tile[2] - ratio * change[2] - delta * GRAVITY * tile[0] * slope_y
    vel_x = push_x / depth
    vel_y = push_y / depth
    drag = GRAVITY * rough * rough * jnp.sqrt(vel_x * vel_x + vel_y * vel_y) / (depth * jnp.cbrt(depth))
    factor = 1.0 / (1.0 + delta * drag)
    return jnp.stack([depth, push_x * factor, push_y * factor])

def fastest_cell(tile):
    depth = tile[0]
    return jnp.max(jnp.maximum(jnp.abs(tile[1] / depth), jnp.abs(tile[2] / depth)) + jnp.sqrt(GRAVITY * depth))

def boundary_lines(state, bed):
    planes = [state[:, 0], state[:, 1], state[:, 2], bed]
    west = jnp.stack([plane[:, 0, :] for plane in planes], 1)
    east = jnp.stack([plane[:, -1, :] for plane in planes], 1)
    south = jnp.stack([plane[:, :, 0] for plane in planes], 1)
    north = jnp.stack([plane[:, :, -1] for plane in planes], 1)
    return jnp.stack([west, east, south, north], 1)

def ghost_lines(lines, table, found, valid):
    flat = table.reshape(-1, table.shape[2], table.shape[3])
    facing = found * 4 + jnp.array(OPPOSITE, jnp.int32)[None, :]
    fetched = jnp.take(flat, facing, axis=0)
    mirrored = lines * jnp.array(MIRROR, lines.dtype)[None, :, :, None]
    return jnp.where(valid[:, :, None, None], fetched, mirrored)

def routes(choose, width_x, width_y, local):
    device_rank = jnp.arange(width_x * width_y, dtype=jnp.int32)
    target = (device_rank // width_y + 1) % width_x * width_y + device_rank % width_y
    source = device_rank * local + choose
    arrival = target * local + jnp.take(choose, target)
    return (source, arrival)

def reference(state, bed, manning, neighbours, wet, moves):
    slots = state.shape[0]
    held = jnp.arange(slots, dtype=jnp.int32)
    for step in range(STEPS):
        flags = jnp.take(wet[step], held)
        speeds = lax.map(fastest_cell, state)
        top = jnp.max(jnp.where(flags > 0, speeds, 0.0))
        delta = COURANT * SPACING / top
        place = jnp.zeros((slots,), jnp.int32).at[held].set(jnp.arange(slots, dtype=jnp.int32))
        lines = boundary_lines(state, bed)
        near = jnp.take(neighbours, held, axis=0)
        valid = near >= 0
        found = jnp.where(valid, jnp.take(place, jnp.maximum(near, 0)), 0)
        ghosts = ghost_lines(lines, lines, found, valid)
        fresh = lax.map(lambda item: advance(item[0], item[1], item[2], item[3], delta), (state, bed, manning, ghosts))
        state = jnp.where(flags[:, None, None, None] > 0, fresh, state)
        if step + 1 < STEPS:
            source, arrival = routes(moves[step], N_XB, N_YB, TILES_DEV)
            state = state.at[arrival].set(jnp.take(state, source, axis=0))
            bed = bed.at[arrival].set(jnp.take(bed, source, axis=0))
            manning = manning.at[arrival].set(jnp.take(manning, source, axis=0))
            held = held.at[arrival].set(jnp.take(held, source))
    return state
```

```python
import functools

import jax
import jax.numpy as jnp
from jax import lax
from jax.experimental import pallas as pl
from jax.experimental.pallas import tpu as pltpu
from jax.sharding import PartitionSpec as P

STEPS = 3
GRAVITY = 9.81
ROOT_G = GRAVITY**0.5
SPACING = 5.0
COURANT = 0.2
ROWS = 32
LANES = 128
TILE = 256
VMEM_BYTES = 24 * 1024 * 1024
SLOT_LOW, WALL_WEST, WALL_EAST, WALL_OUTER, WET, MOVE = 0, 1, 3, 5, 7, 13
CONTROLS = 16


def shifted(value, axis, steps):
    count = lax.axis_size(axis)
    pairs = [(source, (source + steps) % count) for source in range(count)]
    return lax.ppermute(value, axis, pairs)


def cell(h, hu, hv):
    root = lax.rsqrt(h)
    inverse = root * root
    u = hu * inverse
    v = hv * inverse
    celerity = ROOT_G * (h * root)
    pressure = (0.5 * GRAVITY) * (h * h)
    cross = hu * v
    speed_x = jnp.abs(u) + celerity
    speed_y = jnp.abs(v) + celerity
    along_x = (h, hu, hv, hu * u + pressure, cross, speed_x)
    along_y = (h, hv, hu, hv * v + pressure, cross, speed_y)
    return along_x, along_y


def face(left, right):
    wave = jnp.maximum(left[5], right[5])
    return (
        (left[1] + right[1]) - wave * (right[0] - left[0]),
        (left[3] + right[3]) - wave * (right[1] - left[1]),
        (left[4] + right[4]) - wave * (right[2] - left[2]),
    )


def flag(ctl, index):
    return ctl[index] > 0


def slot_of(ctl, position):
    low = ctl[SLOT_LOW]
    return low if position == 0 else 1 - low


def lines_out(ctl, upper, state, bed, west, east, pack):
    for position in range(2):
        slot = slot_of(ctl, position)
        for field in range(4):
            row = position * 4 + field
            if field < 3:
                west[row : row + 1, :] = state[slot, field, 0:1, :]
                east[row : row + 1, :] = state[slot, field, TILE - 1 : TILE, :]
            else:
                west[row : row + 1, :] = bed[slot, 0:1, :]
                east[row : row + 1, :] = bed[slot, TILE - 1 : TILE, :]
    is_upper = upper.astype(jnp.int32)
    slot = jnp.where(upper > 0, ctl[SLOT_LOW], 1 - ctl[SLOT_LOW])
    start = pl.multiple_of((1 - is_upper) * LANES, LANES)
    turn = 1 + is_upper * (LANES - 2)
    lane = lax.broadcasted_iota(jnp.int32, (TILE, LANES), 1)
    group = lax.rem(lane + is_upper, LANES) // 32
    packed = None
    for field in range(4):
        if field < 3:
            block = state[slot, field, :, pl.ds(start, LANES)]
        else:
            block = bed[slot, :, pl.ds(start, LANES)]
        turned = pltpu.roll(block, lax.rem(turn + 32 * field, LANES), 1)
        packed = turned if field == 0 else jnp.where(group == field, turned, packed)
    pack[...] = packed


def opening(state, bed, neighbours, wet, moves, place, west, east, pack, fast, ctl):
    device = place[0]
    upper = place[1]
    first = device * 2
    low = jnp.where(neighbours[first, 3] == first + 1, 0, 1)
    ctl[SLOT_LOW] = low
    for position in range(2):
        slot = low if position == 0 else 1 - low
        tile = first + slot
        ctl[WALL_WEST + position] = (neighbours[tile, 0] < 0).astype(jnp.int32)
        ctl[WALL_EAST + position] = (neighbours[tile, 1] < 0).astype(jnp.int32)
        ctl[WALL_OUTER + position] = (neighbours[tile, 2 + position] < 0).astype(jnp.int32)
        for step in range(STEPS):
            ctl[WET + 2 * step + position] = wet[step, tile]
    for step in range(STEPS):
        ctl[MOVE + step] = moves[step, device]
    lines_out(ctl, upper, state, bed, west, east, pack)

    total = jnp.zeros((ROWS, TILE), jnp.float32)
    for position in range(2):
        slot = slot_of(ctl, position)

        def group(index, best, slot=slot):
            rows = pl.ds(pl.multiple_of(index * ROWS, ROWS), ROWS)
            along_x, along_y = cell(*(state[slot, field, rows, :] for field in range(3)))
            return jnp.maximum(best, jnp.maximum(along_x[5], along_y[5]))

        best = lax.fori_loop(0, TILE // ROWS, group, jnp.zeros((ROWS, TILE), jnp.float32))
        total = jnp.maximum(total, jnp.where(flag(ctl, WET + position), best, 0.0))
    fast[...] = jnp.broadcast_to(jnp.max(total, keepdims=True), fast.shape)


def rates(ctl, state, bed, from_west, from_east, from_pack, rate):
    row_ids = lax.broadcasted_iota(jnp.int32, (ROWS, TILE), 0)
    lane = lax.broadcasted_iota(jnp.int32, (ROWS, LANES), 1)
    last = TILE // ROWS - 1
    for position in range(2):
        slot = slot_of(ctl, position)
        other = 1 - slot
        outer = flag(ctl, WALL_OUTER + position)
        wall_west = flag(ctl, WALL_WEST + position)
        wall_east = flag(ctl, WALL_EAST + position)

        def field_ref(which, field):
            return bed.at[which] if field == 3 else state.at[which, field]

        def ghost_row(received, wall, edge):
            out = []
            for field in range(4):
                own = field_ref(slot, field)[edge : edge + 1, :]
                if field == 1:
                    own = -own
                row = position * 4 + field
                line = jnp.where(wall, own, received[row : row + 1, :])
                out.append(jnp.broadcast_to(line, (8, TILE)))
            return out

        ghost_west = ghost_row(from_west, wall_west, 0)
        ghost_east = ghost_row(from_east, wall_east, TILE - 1)
        first_rows = [field_ref(slot, field)[0:8, :] for field in range(3)]
        left, _ = cell(*ghost_west[:3])
        right, _ = cell(*first_rows)
        start = tuple(part[0:1, :] for part in face(left, right)) + (ghost_west[3][0:1, :],)

        def group(index, carry):
            base = pl.multiple_of(index * ROWS, ROWS)
            rows = pl.ds(base, ROWS)
            after = pl.ds(pl.multiple_of(jnp.minimum(base + ROWS, TILE - 8), 8), 8)
            at_end = index == last
            fields = []
            for field in range(4):
                ref = field_ref(slot, field)
                following = jnp.where(at_end, ghost_east[field], ref[after, :])
                fields.append(jnp.concatenate([ref[rows, :], following], 0))
            cells_x, cells_y = cell(*fields[:3])

            def down(value):
                return pltpu.roll(value, ROWS + 7, 0)[:ROWS]

            here = tuple(value[:ROWS] for value in cells_x)
            faces = face(here, tuple(down(value) for value in cells_x))
            turned = tuple(pltpu.roll(value, 1, 0) for value in faces)
            change_x = tuple(
                value - jnp.where(row_ids == 0, before, moved)
                for value, before, moved in zip(faces, carry[:3], turned)
            )
            ground = fields[3][:ROWS]
            ground_up = pltpu.roll(ground, 1, 0)
            slope_x = down(fields[3]) - jnp.where(row_ids == 0, carry[3], ground_up)
            carried = tuple(value[0:1, :] for value in turned) + (ground_up[0:1, :],)

            inner_lane = LANES - 1 if position == 0 else 0
            inner_cols = slice(0, LANES) if position == 0 else slice(LANES, TILE)
            inner_turn = LANES - 1 if position == 0 else 1
            outer_cols = inner_cols
            packed = from_pack[rows, :]
            ghosts = []
            for field in range(4):
                inner = pltpu.roll(field_ref(other, field)[rows, inner_cols], inner_turn, 1)
                own = fields[field][:ROWS, outer_cols]
                if field == 2:
                    own = -own
                received = packed if field == 0 else pltpu.roll(packed, LANES - 32 * field, 1)
                ghosts.append(
                    jnp.where(lane == inner_lane, inner, jnp.where(outer, own, received))
                )
            _, ghost_y = cell(*ghosts[:3])
            low = tuple(value[:ROWS, :LANES] for value in cells_y)
            high = tuple(value[:ROWS, LANES:] for value in cells_y)

            def right_of(low_part, high_part, ghost_part):
                turned_low = pltpu.roll(low_part, LANES - 1, 1)
                turned_high = pltpu.roll(high_part, LANES - 1, 1)
                return (
                    jnp.where(lane == LANES - 1, turned_high, turned_low),
                    jnp.where(lane == LANES - 1, ghost_part, turned_high),
                )

            pairs = [right_of(a, b, c) for a, b, c in zip(low, high, ghost_y)]
            faces_low = face(low, tuple(pair[0] for pair in pairs))
            faces_high = face(high, tuple(pair[1] for pair in pairs))
            faces_edge = face(ghost_y, low)
            change_y = []
            for a, b, c in zip(faces_low, faces_high, faces_edge):
                turned_a = pltpu.roll(a, 1, 1)
                turned_b = pltpu.roll(b, 1, 1)
                change_y.append(
                    jnp.concatenate(
                        [
                            a - jnp.where(lane == 0, c, turned_a),
                            b - jnp.where(lane == 0, turned_a, turned_b),
                        ],
                        1,
                    )
                )
            ground_low = ground[:, :LANES]
            ground_high = ground[:, LANES:]
            north = right_of(ground_low, ground_high, ghosts[3])
            turned_low = pltpu.roll(ground_low, 1, 1)
            turned_high = pltpu.roll(ground_high, 1, 1)
            slope_y = jnp.concatenate(
                [
                    north[0] - jnp.where(lane == 0, ghosts[3], turned_low),
                    north[1] - jnp.where(lane == 0, turned_low, turned_high),
                ],
                1,
            )
            weight = (GRAVITY / (2.0 * SPACING)) * fields[0][:ROWS]
            scale = 0.5 / SPACING
            rate[slot, 0, rows, :] = scale * (change_x[0] + change_y[0])
            rate[slot, 1, rows, :] = scale * (change_x[1] + change_y[2]) + weight * slope_x
            rate[slot, 2, rows, :] = scale * (change_x[2] + change_y[1]) + weight * slope_y
            return carried

        lax.fori_loop(0, TILE // ROWS, group, start)


def update_tile(ctl, step, position, delta, state, manning, rate, fresh):
    slot = slot_of(ctl, position)
    wet_now = flag(ctl, WET + 2 * step + position)

    def group(index, best):
        rows = pl.ds(pl.multiple_of(index * ROWS, ROWS), ROWS)
        h0, hu0, hv0 = (state[slot, field, rows, :] for field in range(3))
        h = h0 - delta * rate[slot, 0, rows, :]
        hu = hu0 - delta * rate[slot, 1, rows, :]
        hv = hv0 - delta * rate[slot, 2, rows, :]
        rough = manning[slot, rows, :]
        inverse = 1.0 / h
        u = hu * inverse
        v = hv * inverse
        speed = jnp.sqrt(u * u + v * v)
        power = jnp.exp((-4.0 / 3.0) * jnp.log(jnp.abs(h)))
        drag = (GRAVITY * delta) * (rough * rough) * (speed * power)
        factor = 1.0 / (1.0 + drag)
        hu = hu * factor
        hv = hv * factor
        h = jnp.where(wet_now, h, h0)
        hu = jnp.where(wet_now, hu, hu0)
        hv = jnp.where(wet_now, hv, hv0)
        fresh[slot, 0, rows, :] = h
        fresh[slot, 1, rows, :] = hu
        fresh[slot, 2, rows, :] = hv
        if step + 1 < STEPS:
            along_x, along_y = cell(h, hu, hv)
            best = jnp.maximum(best, jnp.maximum(along_x[5], along_y[5]))
        return best

    best = lax.fori_loop(0, TILE // ROWS, group, jnp.zeros((ROWS, TILE), jnp.float32))
    if step + 1 < STEPS:
        best = jnp.where(flag(ctl, WET + 2 * step + 2 + position), best, 0.0)
    return best


def update(step, ctl, place, tops, state, bed, manning, rate, *outs):
    delta = (COURANT * SPACING) / jnp.max(tops[...], keepdims=True)
    fresh = outs[0]
    best = jnp.maximum(
        update_tile(ctl, step, 0, delta, state, manning, rate, fresh),
        update_tile(ctl, step, 1, delta, state, manning, rate, fresh),
    )
    if step + 1 < STEPS:
        _, west, east, pack, fast = outs
        lines_out(ctl, place[1], fresh, bed, west, east, pack)
        fast[...] = jnp.broadcast_to(jnp.max(best, keepdims=True), fast.shape)


def vmem():
    return pl.BlockSpec(memory_space=pltpu.VMEM)


def smem():
    return pl.BlockSpec(memory_space=pltpu.SMEM)


def call(kernel, outs, out_specs, in_specs, flops):
    return pl.pallas_call(
        kernel,
        out_shape=outs,
        in_specs=in_specs,
        out_specs=out_specs,
        compiler_params=pltpu.CompilerParams(vmem_limit_bytes=VMEM_BYTES),
        cost_estimate=pl.CostEstimate(flops=flops, bytes_accessed=4 << 20, transcendentals=0),
    )


def f32(*shape):
    return jax.ShapeDtypeStruct(shape, jnp.float32)


LINES = (f32(8, TILE), f32(8, TILE), f32(TILE, LANES), f32(8, LANES))


def exchange(west, east, pack):
    from_west = shifted(east, "xb", 1)
    from_east = shifted(west, "xb", -1)
    from_pack = shifted(pack, "yb", 1)
    return from_west, from_east, from_pack


def body(state, bed, manning, neighbours, wet, moves):
    width_y = lax.axis_size("yb")
    upper = lax.axis_index("yb")
    device = lax.axis_index("xb") * width_y + upper
    place = jnp.stack([device, upper]).astype(jnp.int32)
    shape = f32(*state.shape)
    west, east, pack, fast, ctl = call(
        opening,
        LINES + (jax.ShapeDtypeStruct((CONTROLS,), jnp.int32),),
        (vmem(),) * 4 + (smem(),),
        [vmem(), vmem(), smem(), smem(), smem(), smem()],
        4 << 20,
    )(state, bed, neighbours, wet, moves, place)
    for step in range(STEPS):
        got = exchange(west, east, pack)
        tops = lax.all_gather(fast, ("xb", "yb"), axis=0, tiled=True)
        rate = call(rates, shape, vmem(), [smem()] + [vmem()] * 5, 16 << 20)(ctl, state, bed, *got)
        more = step + 1 < STEPS
        outs = call(
            functools.partial(update, step),
            (shape,) + LINES if more else (shape,),
            (vmem(),) * (5 if more else 1),
            [smem(), smem()] + [vmem()] * 5,
            8 << 20,
        )(ctl, place, tops, state, bed, manning, rate)
        state = outs[0]
        if more:
            _, west, east, pack, fast = outs
    one, two = ctl[MOVE], ctl[MOVE + 1]
    again = one == two
    leaving = lax.dynamic_index_in_dim(state, one, 0, keepdims=False)
    staying = lax.dynamic_index_in_dim(state, 1 - one, 0, keepdims=False)
    arrived = shifted(leaving, "xb", 1)
    arrived_next = shifted(jnp.where(again, arrived, staying), "xb", 1)
    remains = jnp.where(again, staying, arrived)
    is_first = two == 0
    return jnp.stack(
        [jnp.where(is_first, arrived_next, remains), jnp.where(is_first, remains, arrived_next)]
    )


def solution(mesh):
    placed = (
        P(("runs", "xb", "yb"), None, None, None),
        P(("runs", "xb", "yb"), None, None),
        P(("runs", "xb", "yb"), None, None),
        P("runs", None),
        P(None, "runs"),
        P(None, "runs"),
    )
    return jax.shard_map(
        body,
        mesh=mesh,
        in_specs=placed,
        out_specs=P(("runs", "xb", "yb"), None, None, None),
        check_vma=False,
    )
```

```python
import functools

import jax
import jax.numpy as jnp
from jax import lax
from jax.experimental import pallas as pl
from jax.experimental.pallas import tpu as pltpu
from jax.sharding import PartitionSpec as P

STEPS = 3
GRAVITY = 9.81
ROOT_G = GRAVITY**0.5
SPACING = 5.0
COURANT = 0.2
ROWS = 32
LANES = 128
TILE = 256
VMEM_BYTES = 24 * 1024 * 1024
SLOT_LOW, WALL_WEST, WALL_EAST, WALL_OUTER, WET, MOVE = 0, 1, 3, 5, 7, 13
CONTROLS = 16


def shifted(value, axis, steps):
    count = lax.axis_size(axis)
    pairs = [(source, (source + steps) % count) for source in range(count)]
    return lax.ppermute(value, axis, pairs)


def cell(h, hu, hv):
    root = lax.rsqrt(h)
    inverse = root * root
    u = hu * inverse
    v = hv * inverse
    celerity = ROOT_G * (h * root)
    pressure = (0.5 * GRAVITY) * (h * h)
    cross = hu * v
    speed_x = jnp.abs(u) + celerity
    speed_y = jnp.abs(v) + celerity
    along_x = (h, hu, hv, hu * u + pressure, cross, speed_x)
    along_y = (h, hv, hu, hv * v + pressure, cross, speed_y)
    return along_x, along_y


def face(left, right):
    wave = jnp.maximum(left[5], right[5])
    return (
        (left[1] + right[1]) - wave * (right[0] - left[0]),
        (left[3] + right[3]) - wave * (right[1] - left[1]),
        (left[4] + right[4]) - wave * (right[2] - left[2]),
    )


def flag(ctl, index):
    return ctl[index] > 0


def slot_of(ctl, position):
    low = ctl[SLOT_LOW]
    return low if position == 0 else 1 - low


def lines_out(ctl, upper, state, bed, west, east, pack):
    for position in range(2):
        slot = slot_of(ctl, position)
        for field in range(4):
            row = position * 4 + field
            if field < 3:
                west[row : row + 1, :] = state[slot, field, 0:1, :]
                east[row : row + 1, :] = state[slot, field, TILE - 1 : TILE, :]
            else:
                west[row : row + 1, :] = bed[slot, 0:1, :]
                east[row : row + 1, :] = bed[slot, TILE - 1 : TILE, :]
    is_upper = upper.astype(jnp.int32)
    slot = jnp.where(upper > 0, ctl[SLOT_LOW], 1 - ctl[SLOT_LOW])
    start = pl.multiple_of((1 - is_upper) * LANES, LANES)
    turn = 1 + is_upper * (LANES - 2)
    lane = lax.broadcasted_iota(jnp.int32, (TILE, LANES), 1)
    group = lax.rem(lane + is_upper, LANES) // 32
    packed = None
    for field in range(4):
        if field < 3:
            block = state[slot, field, :, pl.ds(start, LANES)]
        else:
            block = bed[slot, :, pl.ds(start, LANES)]
        turned = pltpu.roll(block, lax.rem(turn + 32 * field, LANES), 1)
        packed = turned if field == 0 else jnp.where(group == field, turned, packed)
    pack[...] = packed


def copy_all(pairs, sems):
    copies = [pltpu.make_async_copy(src, dst, sems.at[k]) for k, (src, dst) in enumerate(pairs)]
    for copy in copies:
        copy.start()
    return copies


def opening(
    state_in, bed_in, neighbours_in, wet_in, moves_in,
    west, east, pack, fast, ctl,
    state, bed, neighbours, wet, moves, sems,
):
    small = ((neighbours_in, neighbours), (wet_in, wet), (moves_in, moves))
    pieces = [(state_in.at[slot], state.at[slot]) for slot in range(2)]
    copies = copy_all(small + tuple(pieces) + ((bed_in, bed),), sems)
    upper = lax.axis_index("yb")
    device = lax.axis_index("xb") * 2 + upper
    for copy in copies[:3]:
        copy.wait()
    first = device * 2
    low = jnp.where(neighbours[first, 3] == first + 1, 0, 1)
    ctl[SLOT_LOW] = low
    for position in range(2):
        slot = low if position == 0 else 1 - low
        tile = first + slot
        ctl[WALL_WEST + position] = (neighbours[tile, 0] < 0).astype(jnp.int32)
        ctl[WALL_EAST + position] = (neighbours[tile, 1] < 0).astype(jnp.int32)
        ctl[WALL_OUTER + position] = (neighbours[tile, 2 + position] < 0).astype(jnp.int32)
        for step in range(STEPS):
            ctl[WET + 2 * step + position] = wet[step, tile]
    for step in range(STEPS):
        ctl[MOVE + step] = moves[step, device]

    total = jnp.zeros((ROWS, TILE), jnp.float32)
    for slot in range(2):
        copies[3 + slot].wait()

        def group(index, best, slot=slot):
            rows = pl.ds(pl.multiple_of(index * ROWS, ROWS), ROWS)
            along_x, along_y = cell(*(state[slot, field, rows, :] for field in range(3)))
            return jnp.maximum(best, jnp.maximum(along_x[5], along_y[5]))

        best = lax.fori_loop(0, TILE // ROWS, group, jnp.zeros((ROWS, TILE), jnp.float32))
        total = jnp.maximum(total, jnp.where(wet[0, first + slot] > 0, best, 0.0))
    fast[...] = jnp.broadcast_to(jnp.max(total, keepdims=True), fast.shape)
    copies[5].wait()
    lines_out(ctl, upper, state, bed, west, east, pack)


def rates(ctl, state, bed, from_west, from_east, from_pack, rate):
    row_ids = lax.broadcasted_iota(jnp.int32, (ROWS, TILE), 0)
    lane = lax.broadcasted_iota(jnp.int32, (ROWS, LANES), 1)
    last = TILE // ROWS - 1
    for position in range(2):
        slot = slot_of(ctl, position)
        other = 1 - slot
        outer = flag(ctl, WALL_OUTER + position)
        wall_west = flag(ctl, WALL_WEST + position)
        wall_east = flag(ctl, WALL_EAST + position)

        def field_ref(which, field):
            return bed.at[which] if field == 3 else state.at[which, field]

        def ghost_row(received, wall, edge):
            out = []
            for field in range(4):
                own = field_ref(slot, field)[edge : edge + 1, :]
                if field == 1:
                    own = -own
                row = position * 4 + field
                line = jnp.where(wall, own, received[row : row + 1, :])
                out.append(jnp.broadcast_to(line, (8, TILE)))
            return out

        ghost_west = ghost_row(from_west, wall_west, 0)
        ghost_east = ghost_row(from_east, wall_east, TILE - 1)
        first_rows = [field_ref(slot, field)[0:8, :] for field in range(3)]
        left, _ = cell(*ghost_west[:3])
        right, _ = cell(*first_rows)
        start = tuple(part[0:1, :] for part in face(left, right)) + (ghost_west[3][0:1, :],)

        def group(index, carry):
            base = pl.multiple_of(index * ROWS, ROWS)
            rows = pl.ds(base, ROWS)
            after = pl.ds(pl.multiple_of(jnp.minimum(base + ROWS, TILE - 8), 8), 8)
            at_end = index == last
            fields = []
            for field in range(4):
                ref = field_ref(slot, field)
                following = jnp.where(at_end, ghost_east[field], ref[after, :])
                fields.append(jnp.concatenate([ref[rows, :], following], 0))
            cells_x, cells_y = cell(*fields[:3])

            def down(value):
                return pltpu.roll(value, ROWS + 7, 0)[:ROWS]

            here = tuple(value[:ROWS] for value in cells_x)
            faces = face(here, tuple(down(value) for value in cells_x))
            turned = tuple(pltpu.roll(value, 1, 0) for value in faces)
            change_x = tuple(
                value - jnp.where(row_ids == 0, before, moved)
                for value, before, moved in zip(faces, carry[:3], turned)
            )
            ground = fields[3][:ROWS]
            ground_up = pltpu.roll(ground, 1, 0)
            slope_x = down(fields[3]) - jnp.where(row_ids == 0, carry[3], ground_up)
            carried = tuple(value[0:1, :] for value in turned) + (ground_up[0:1, :],)

            inner_lane = LANES - 1 if position == 0 else 0
            inner_cols = slice(0, LANES) if position == 0 else slice(LANES, TILE)
            inner_turn = LANES - 1 if position == 0 else 1
            outer_cols = inner_cols
            packed = from_pack[rows, :]
            ghosts = []
            for field in range(4):
                inner = pltpu.roll(field_ref(other, field)[rows, inner_cols], inner_turn, 1)
                own = fields[field][:ROWS, outer_cols]
                if field == 2:
                    own = -own
                received = packed if field == 0 else pltpu.roll(packed, LANES - 32 * field, 1)
                ghosts.append(
                    jnp.where(lane == inner_lane, inner, jnp.where(outer, own, received))
                )
            _, ghost_y = cell(*ghosts[:3])
            low = tuple(value[:ROWS, :LANES] for value in cells_y)
            high = tuple(value[:ROWS, LANES:] for value in cells_y)

            def right_of(low_part, high_part, ghost_part):
                turned_low = pltpu.roll(low_part, LANES - 1, 1)
                turned_high = pltpu.roll(high_part, LANES - 1, 1)
                return (
                    jnp.where(lane == LANES - 1, turned_high, turned_low),
                    jnp.where(lane == LANES - 1, ghost_part, turned_high),
                )

            pairs = [right_of(a, b, c) for a, b, c in zip(low, high, ghost_y)]
            faces_low = face(low, tuple(pair[0] for pair in pairs))
            faces_high = face(high, tuple(pair[1] for pair in pairs))
            faces_edge = face(ghost_y, low)
            change_y = []
            for a, b, c in zip(faces_low, faces_high, faces_edge):
                turned_a = pltpu.roll(a, 1, 1)
                turned_b = pltpu.roll(b, 1, 1)
                change_y.append(
                    jnp.concatenate(
                        [
                            a - jnp.where(lane == 0, c, turned_a),
                            b - jnp.where(lane == 0, turned_a, turned_b),
                        ],
                        1,
                    )
                )
            ground_low = ground[:, :LANES]
            ground_high = ground[:, LANES:]
            north = right_of(ground_low, ground_high, ghosts[3])
            turned_low = pltpu.roll(ground_low, 1, 1)
            turned_high = pltpu.roll(ground_high, 1, 1)
            slope_y = jnp.concatenate(
                [
                    north[0] - jnp.where(lane == 0, ghosts[3], turned_low),
                    north[1] - jnp.where(lane == 0, turned_low, turned_high),
                ],
                1,
            )
            weight = (GRAVITY / (2.0 * SPACING)) * fields[0][:ROWS]
            scale = 0.5 / SPACING
            rate[slot, 0, rows, :] = scale * (change_x[0] + change_y[0])
            rate[slot, 1, rows, :] = scale * (change_x[1] + change_y[2]) + weight * slope_x
            rate[slot, 2, rows, :] = scale * (change_x[2] + change_y[1]) + weight * slope_y
            return carried

        lax.fori_loop(0, TILE // ROWS, group, start)


def update_tile(ctl, step, position, delta, state, manning, rate, fresh):
    slot = slot_of(ctl, position)
    wet_now = flag(ctl, WET + 2 * step + position)

    def group(index, best):
        rows = pl.ds(pl.multiple_of(index * ROWS, ROWS), ROWS)
        h0, hu0, hv0 = (state[slot, field, rows, :] for field in range(3))
        h = h0 - delta * rate[slot, 0, rows, :]
        hu = hu0 - delta * rate[slot, 1, rows, :]
        hv = hv0 - delta * rate[slot, 2, rows, :]
        rough = manning[slot, rows, :]
        inverse = 1.0 / h
        u = hu * inverse
        v = hv * inverse
        speed = jnp.sqrt(u * u + v * v)
        power = jnp.exp((-4.0 / 3.0) * jnp.log(jnp.abs(h)))
        drag = (GRAVITY * delta) * (rough * rough) * (speed * power)
        factor = 1.0 / (1.0 + drag)
        hu = hu * factor
        hv = hv * factor
        h = jnp.where(wet_now, h, h0)
        hu = jnp.where(wet_now, hu, hu0)
        hv = jnp.where(wet_now, hv, hv0)
        fresh[slot, 0, rows, :] = h
        fresh[slot, 1, rows, :] = hu
        fresh[slot, 2, rows, :] = hv
        if step + 1 < STEPS:
            along_x, along_y = cell(h, hu, hv)
            best = jnp.maximum(best, jnp.maximum(along_x[5], along_y[5]))
        return best

    best = lax.fori_loop(0, TILE // ROWS, group, jnp.zeros((ROWS, TILE), jnp.float32))
    if step + 1 < STEPS:
        best = jnp.where(flag(ctl, WET + 2 * step + 2 + position), best, 0.0)
    return best


def update(step, ctl, tops, state, bed, manning, rate, *outs):
    delta = (COURANT * SPACING) / jnp.max(tops[...], keepdims=True)
    fresh = outs[0]
    best = jnp.maximum(
        update_tile(ctl, step, 0, delta, state, manning, rate, fresh),
        update_tile(ctl, step, 1, delta, state, manning, rate, fresh),
    )
    if step + 1 < STEPS:
        _, west, east, pack, fast = outs
        lines_out(ctl, lax.axis_index("yb"), fresh, bed, west, east, pack)
        fast[...] = jnp.broadcast_to(jnp.max(best, keepdims=True), fast.shape)
    else:
        outs[1][...] = fresh[ctl[MOVE]]


def second_leaving(ctl, state, arrived, leaving, sems):
    again = ctl[MOVE] == ctl[MOVE + 1]

    @pl.when(again)
    def _():
        pltpu.make_async_copy(arrived, leaving, sems.at[0]).start()

    @pl.when(jnp.logical_not(again))
    def _():
        pltpu.make_async_copy(state.at[1 - ctl[MOVE]], leaving, sems.at[0]).start()

    pltpu.make_async_copy(arrived, leaving, sems.at[0]).wait()


def keep_rest(ctl, state, arrived, out, sems):
    rest = out.at[1 - ctl[MOVE + 1]]
    again = ctl[MOVE] == ctl[MOVE + 1]

    @pl.when(again)
    def _():
        pltpu.make_async_copy(state.at[1 - ctl[MOVE]], rest, sems.at[0]).start()

    @pl.when(jnp.logical_not(again))
    def _():
        pltpu.make_async_copy(arrived, rest, sems.at[0]).start()

    pltpu.make_async_copy(arrived, rest, sems.at[0]).wait()


def keep_last(ctl, arrived, before, out, sems):
    del before
    copy = pltpu.make_async_copy(arrived, out.at[ctl[MOVE + 1]], sems.at[0])
    copy.start()
    copy.wait()


def vmem():
    return pl.BlockSpec(memory_space=pltpu.VMEM)


def smem():
    return pl.BlockSpec(memory_space=pltpu.SMEM)


def anywhere():
    return pl.BlockSpec(memory_space=pl.ANY)


def call(kernel, outs, out_specs, in_specs, flops, scratch=(), aliases=None):
    return pl.pallas_call(
        kernel,
        scratch_shapes=scratch,
        input_output_aliases=aliases or {},
        out_shape=outs,
        in_specs=in_specs,
        out_specs=out_specs,
        compiler_params=pltpu.CompilerParams(vmem_limit_bytes=VMEM_BYTES),
        cost_estimate=pl.CostEstimate(flops=flops, bytes_accessed=4 << 20, transcendentals=0),
    )


def f32(*shape):
    return jax.ShapeDtypeStruct(shape, jnp.float32)


LINES = (f32(8, TILE), f32(8, TILE), f32(TILE, LANES), f32(8, LANES))


def exchange(west, east, pack):
    from_west = shifted(east, "xb", 1)
    from_east = shifted(west, "xb", -1)
    from_pack = shifted(pack, "yb", 1)
    return from_west, from_east, from_pack


def spread(fast):
    tops = lax.all_gather(fast, "yb", axis=0, tiled=True)
    count = lax.axis_size("xb")
    reach = 1
    while reach < count:
        pairs = [[k, k + reach] for k in range(count) if k // reach % 2 == 0]
        tops = lax.all_gather(tops, "xb", axis=0, axis_index_groups=pairs, tiled=True)
        reach *= 2
    return tops


def body(state, bed, manning, neighbours, wet, moves):
    shape = f32(*state.shape)
    tile_shape = f32(*state.shape[1:])
    sem = [pltpu.SemaphoreType.DMA((1,))]
    west, east, pack, fast, ctl = call(
        opening,
        LINES + (jax.ShapeDtypeStruct((CONTROLS,), jnp.int32),),
        (vmem(),) * 4 + (smem(),),
        [anywhere()] * 5,
        4 << 20,
        [
            pltpu.VMEM(state.shape, jnp.float32),
            pltpu.VMEM(bed.shape, jnp.float32),
            pltpu.SMEM(neighbours.shape, jnp.int32),
            pltpu.SMEM(wet.shape, jnp.int32),
            pltpu.SMEM(moves.shape, jnp.int32),
            pltpu.SemaphoreType.DMA((6,)),
        ],
    )(state, bed, neighbours, wet, moves)
    for step in range(STEPS):
        got = exchange(west, east, pack)
        tops = spread(fast)
        rate = call(rates, shape, vmem(), [smem()] + [vmem()] * 5, 16 << 20)(ctl, state, bed, *got)
        more = step + 1 < STEPS
        extra = LINES if more else (tile_shape,)
        outs = call(
            functools.partial(update, step),
            (shape,) + extra,
            (vmem(),) * (1 + len(extra)),
            [smem()] + [vmem()] * 5,
            8 << 20,
        )(ctl, tops, state, bed, manning, rate)
        state = outs[0]
        if more:
            _, west, east, pack, fast = outs
    arrived = shifted(outs[1], "xb", 1)
    leaving = call(
        second_leaving, tile_shape, anywhere(), [smem(), anywhere(), anywhere()], 1 << 20, sem
    )(ctl, state, arrived)
    arrived_next = shifted(leaving, "xb", 1)
    final = call(
        keep_rest, shape, anywhere(), [smem(), anywhere(), anywhere()], 1 << 20, sem
    )(ctl, state, arrived)
    return call(
        keep_last, shape, anywhere(), [smem(), anywhere(), anywhere()], 1 << 20, sem, {2: 0}
    )(ctl, arrived_next, final)


def solution(mesh):
    placed = (
        P(("runs", "xb", "yb"), None, None, None),
        P(("runs", "xb", "yb"), None, None),
        P(("runs", "xb", "yb"), None, None),
        P("runs", None),
        P(None, "runs"),
        P(None, "runs"),
    )
    return jax.shard_map(
        body,
        mesh=mesh,
        in_specs=placed,
        out_specs=P(("runs", "xb", "yb"), None, None, None),
        check_vma=False,
    )
```

```python
import functools

import jax
import jax.numpy as jnp
from jax import lax
from jax.experimental import pallas as pl
from jax.experimental.pallas import tpu as pltpu
from jax.sharding import PartitionSpec as P

STEPS = 3
GRAVITY = 9.81
ROOT_G = GRAVITY**0.5
SPACING = 5.0
COURANT = 0.2
ROWS = 32
LANES = 128
TILE = 256
VMEM_BYTES = 24 * 1024 * 1024
SLOT_LOW, WALL_WEST, WALL_EAST, WALL_OUTER, WET, MOVE = 0, 1, 3, 5, 7, 13
CONTROLS = 16


def shifted(value, axis, steps, around=True):
    count = lax.axis_size(axis)
    pairs = [(source, (source + steps) % count) for source in range(count)]
    if not around:
        pairs = [pair for pair in pairs if abs(pair[0] - pair[1]) == abs(steps)]
    return lax.ppermute(value, axis, pairs)


def cell(h, hu, hv):
    root = lax.rsqrt(h)
    inverse = root * root
    u = hu * inverse
    v = hv * inverse
    celerity = ROOT_G * (h * root)
    pressure = (0.5 * GRAVITY) * (h * h)
    cross = hu * v
    speed_x = jnp.abs(u) + celerity
    speed_y = jnp.abs(v) + celerity
    along_x = (h, hu, hv, hu * u + pressure, cross, speed_x)
    along_y = (h, hv, hu, hv * v + pressure, cross, speed_y)
    return along_x, along_y


def face(left, right):
    wave = jnp.maximum(left[5], right[5])
    return (
        (left[1] + right[1]) - wave * (right[0] - left[0]),
        (left[3] + right[3]) - wave * (right[1] - left[1]),
        (left[4] + right[4]) - wave * (right[2] - left[2]),
    )


def flag(ctl, index):
    return ctl[index] > 0


def slot_of(ctl, position):
    low = ctl[SLOT_LOW]
    return low if position == 0 else 1 - low


def lines_out(ctl, upper, state, bed, west, east, pack):
    for position in range(2):
        slot = slot_of(ctl, position)
        for field in range(4):
            row = position * 4 + field
            if field < 3:
                west[row : row + 1, :] = state[slot, field, 0:1, :]
                east[row : row + 1, :] = state[slot, field, TILE - 1 : TILE, :]
            else:
                west[row : row + 1, :] = bed[slot, 0:1, :]
                east[row : row + 1, :] = bed[slot, TILE - 1 : TILE, :]
    is_upper = upper.astype(jnp.int32)
    slot = jnp.where(upper > 0, ctl[SLOT_LOW], 1 - ctl[SLOT_LOW])
    start = pl.multiple_of((1 - is_upper) * LANES, LANES)
    turn = 1 + is_upper * (LANES - 2)
    lane = lax.broadcasted_iota(jnp.int32, (TILE, LANES), 1)
    group = lax.rem(lane + is_upper, LANES) // 32
    packed = None
    for field in range(4):
        if field < 3:
            block = state[slot, field, :, pl.ds(start, LANES)]
        else:
            block = bed[slot, :, pl.ds(start, LANES)]
        turned = pltpu.roll(block, lax.rem(turn + 32 * field, LANES), 1)
        packed = turned if field == 0 else jnp.where(group == field, turned, packed)
    pack[...] = packed


def copy_all(pairs, sems):
    copies = [pltpu.make_async_copy(src, dst, sems.at[k]) for k, (src, dst) in enumerate(pairs)]
    for copy in copies:
        copy.start()
    return copies


def opening(
    state_in, bed_in, neighbours_in, wet_in, moves_in,
    west, east, pack, fast, ctl,
    state, bed, neighbours, wet, moves, sems,
):
    small = ((neighbours_in, neighbours), (wet_in, wet), (moves_in, moves))
    pieces = [(state_in.at[slot], state.at[slot]) for slot in range(2)]
    copies = copy_all(small + tuple(pieces) + ((bed_in, bed),), sems)
    upper = lax.axis_index("yb")
    device = lax.axis_index("xb") * 2 + upper
    for copy in copies[:3]:
        copy.wait()
    first = device * 2
    low = jnp.where(neighbours[first, 3] == first + 1, 0, 1)
    ctl[SLOT_LOW] = low
    for position in range(2):
        slot = low if position == 0 else 1 - low
        tile = first + slot
        ctl[WALL_WEST + position] = (neighbours[tile, 0] < 0).astype(jnp.int32)
        ctl[WALL_EAST + position] = (neighbours[tile, 1] < 0).astype(jnp.int32)
        ctl[WALL_OUTER + position] = (neighbours[tile, 2 + position] < 0).astype(jnp.int32)
        for step in range(STEPS):
            ctl[WET + 2 * step + position] = wet[step, tile]
    for step in range(STEPS):
        ctl[MOVE + step] = moves[step, device]

    total = jnp.zeros((ROWS, TILE), jnp.float32)
    for slot in range(2):
        copies[3 + slot].wait()

        def group(index, best, slot=slot):
            rows = pl.ds(pl.multiple_of(index * ROWS, ROWS), ROWS)
            along_x, along_y = cell(*(state[slot, field, rows, :] for field in range(3)))
            return jnp.maximum(best, jnp.maximum(along_x[5], along_y[5]))

        best = lax.fori_loop(0, TILE // ROWS, group, jnp.zeros((ROWS, TILE), jnp.float32))
        total = jnp.maximum(total, jnp.where(wet[0, first + slot] > 0, best, 0.0))
    fast[...] = jnp.broadcast_to(jnp.max(total, keepdims=True), fast.shape)
    copies[5].wait()
    lines_out(ctl, upper, state, bed, west, east, pack)


def rates(ctl, state, bed, from_west, from_east, from_pack, rate):
    row_ids = lax.broadcasted_iota(jnp.int32, (ROWS, TILE), 0)
    lane = lax.broadcasted_iota(jnp.int32, (ROWS, LANES), 1)
    last = TILE // ROWS - 1
    for position in range(2):
        slot = slot_of(ctl, position)
        other = 1 - slot
        outer = flag(ctl, WALL_OUTER + position)
        wall_west = flag(ctl, WALL_WEST + position)
        wall_east = flag(ctl, WALL_EAST + position)

        def field_ref(which, field):
            return bed.at[which] if field == 3 else state.at[which, field]

        def ghost_row(received, wall, edge):
            out = []
            for field in range(4):
                own = field_ref(slot, field)[edge : edge + 1, :]
                if field == 1:
                    own = -own
                row = position * 4 + field
                line = jnp.where(wall, own, received[row : row + 1, :])
                out.append(jnp.broadcast_to(line, (8, TILE)))
            return out

        ghost_west = ghost_row(from_west, wall_west, 0)
        ghost_east = ghost_row(from_east, wall_east, TILE - 1)
        first_rows = [field_ref(slot, field)[0:8, :] for field in range(3)]
        left, _ = cell(*ghost_west[:3])
        right, _ = cell(*first_rows)
        start = tuple(part[0:1, :] for part in face(left, right)) + (ghost_west[3][0:1, :],)

        def group(index, carry):
            base = pl.multiple_of(index * ROWS, ROWS)
            rows = pl.ds(base, ROWS)
            after = pl.ds(pl.multiple_of(jnp.minimum(base + ROWS, TILE - 8), 8), 8)
            at_end = index == last
            fields = []
            for field in range(4):
                ref = field_ref(slot, field)
                following = jnp.where(at_end, ghost_east[field], ref[after, :])
                fields.append(jnp.concatenate([ref[rows, :], following], 0))
            cells_x, cells_y = cell(*fields[:3])

            def down(value):
                return pltpu.roll(value, ROWS + 7, 0)[:ROWS]

            here = tuple(value[:ROWS] for value in cells_x)
            faces = face(here, tuple(down(value) for value in cells_x))
            turned = tuple(pltpu.roll(value, 1, 0) for value in faces)
            change_x = tuple(
                value - jnp.where(row_ids == 0, before, moved)
                for value, before, moved in zip(faces, carry[:3], turned)
            )
            ground = fields[3][:ROWS]
            ground_up = pltpu.roll(ground, 1, 0)
            slope_x = down(fields[3]) - jnp.where(row_ids == 0, carry[3], ground_up)
            carried = tuple(value[0:1, :] for value in turned) + (ground_up[0:1, :],)

            inner_lane = LANES - 1 if position == 0 else 0
            inner_cols = slice(0, LANES) if position == 0 else slice(LANES, TILE)
            inner_turn = LANES - 1 if position == 0 else 1
            outer_cols = inner_cols
            packed = from_pack[rows, :]
            ghosts = []
            for field in range(4):
                inner = pltpu.roll(field_ref(other, field)[rows, inner_cols], inner_turn, 1)
                own = fields[field][:ROWS, outer_cols]
                if field == 2:
                    own = -own
                received = packed if field == 0 else pltpu.roll(packed, LANES - 32 * field, 1)
                ghosts.append(
                    jnp.where(lane == inner_lane, inner, jnp.where(outer, own, received))
                )
            _, ghost_y = cell(*ghosts[:3])
            low = tuple(value[:ROWS, :LANES] for value in cells_y)
            high = tuple(value[:ROWS, LANES:] for value in cells_y)

            def right_of(low_part, high_part, ghost_part):
                turned_low = pltpu.roll(low_part, LANES - 1, 1)
                turned_high = pltpu.roll(high_part, LANES - 1, 1)
                return (
                    jnp.where(lane == LANES - 1, turned_high, turned_low),
                    jnp.where(lane == LANES - 1, ghost_part, turned_high),
                )

            pairs = [right_of(a, b, c) for a, b, c in zip(low, high, ghost_y)]
            faces_low = face(low, tuple(pair[0] for pair in pairs))
            faces_high = face(high, tuple(pair[1] for pair in pairs))
            faces_edge = face(ghost_y, low)
            change_y = []
            for a, b, c in zip(faces_low, faces_high, faces_edge):
                turned_a = pltpu.roll(a, 1, 1)
                turned_b = pltpu.roll(b, 1, 1)
                change_y.append(
                    jnp.concatenate(
                        [
                            a - jnp.where(lane == 0, c, turned_a),
                            b - jnp.where(lane == 0, turned_a, turned_b),
                        ],
                        1,
                    )
                )
            ground_low = ground[:, :LANES]
            ground_high = ground[:, LANES:]
            north = right_of(ground_low, ground_high, ghosts[3])
            turned_low = pltpu.roll(ground_low, 1, 1)
            turned_high = pltpu.roll(ground_high, 1, 1)
            slope_y = jnp.concatenate(
                [
                    north[0] - jnp.where(lane == 0, ghosts[3], turned_low),
                    north[1] - jnp.where(lane == 0, turned_low, turned_high),
                ],
                1,
            )
            weight = (GRAVITY / (2.0 * SPACING)) * fields[0][:ROWS]
            scale = 0.5 / SPACING
            rate[slot, 0, rows, :] = scale * (change_x[0] + change_y[0])
            rate[slot, 1, rows, :] = scale * (change_x[1] + change_y[2]) + weight * slope_x
            rate[slot, 2, rows, :] = scale * (change_x[2] + change_y[1]) + weight * slope_y
            return carried

        lax.fori_loop(0, TILE // ROWS, group, start)


def update_tile(ctl, step, position, delta, state, manning, rate, fresh):
    slot = slot_of(ctl, position)
    wet_now = flag(ctl, WET + 2 * step + position)

    def group(index, best):
        rows = pl.ds(pl.multiple_of(index * ROWS, ROWS), ROWS)
        h0, hu0, hv0 = (state[slot, field, rows, :] for field in range(3))
        h = h0 - delta * rate[slot, 0, rows, :]
        hu = hu0 - delta * rate[slot, 1, rows, :]
        hv = hv0 - delta * rate[slot, 2, rows, :]
        rough = manning[slot, rows, :]
        inverse = 1.0 / h
        u = hu * inverse
        v = hv * inverse
        speed = jnp.sqrt(u * u + v * v)
        power = jnp.exp((-4.0 / 3.0) * jnp.log(jnp.abs(h)))
        drag = (GRAVITY * delta) * (rough * rough) * (speed * power)
        factor = 1.0 / (1.0 + drag)
        hu = hu * factor
        hv = hv * factor
        h = jnp.where(wet_now, h, h0)
        hu = jnp.where(wet_now, hu, hu0)
        hv = jnp.where(wet_now, hv, hv0)
        fresh[slot, 0, rows, :] = h
        fresh[slot, 1, rows, :] = hu
        fresh[slot, 2, rows, :] = hv
        if step + 1 < STEPS:
            along_x, along_y = cell(h, hu, hv)
            best = jnp.maximum(best, jnp.maximum(along_x[5], along_y[5]))
        return best

    best = lax.fori_loop(0, TILE // ROWS, group, jnp.zeros((ROWS, TILE), jnp.float32))
    if step + 1 < STEPS:
        best = jnp.where(flag(ctl, WET + 2 * step + 2 + position), best, 0.0)
    return best


def update(step, ctl, tops, state, bed, manning, rate, *outs):
    delta = (COURANT * SPACING) / jnp.max(tops[...], keepdims=True)
    fresh = outs[0]
    best = jnp.maximum(
        update_tile(ctl, step, 0, delta, state, manning, rate, fresh),
        update_tile(ctl, step, 1, delta, state, manning, rate, fresh),
    )
    if step + 1 < STEPS:
        _, west, east, pack, fast = outs
        lines_out(ctl, lax.axis_index("yb"), fresh, bed, west, east, pack)
        fast[...] = jnp.broadcast_to(jnp.max(best, keepdims=True), fast.shape)
    else:
        outs[1][...] = fresh[ctl[MOVE]]


def second_leaving(ctl, state, arrived, leaving, sems):
    again = ctl[MOVE] == ctl[MOVE + 1]

    @pl.when(again)
    def _():
        pltpu.make_async_copy(arrived, leaving, sems.at[0]).start()

    @pl.when(jnp.logical_not(again))
    def _():
        pltpu.make_async_copy(state.at[1 - ctl[MOVE]], leaving, sems.at[0]).start()

    pltpu.make_async_copy(arrived, leaving, sems.at[0]).wait()


def keep_rest(ctl, state, arrived, out, sems):
    rest = out.at[1 - ctl[MOVE + 1]]
    again = ctl[MOVE] == ctl[MOVE + 1]

    @pl.when(again)
    def _():
        pltpu.make_async_copy(state.at[1 - ctl[MOVE]], rest, sems.at[0]).start()

    @pl.when(jnp.logical_not(again))
    def _():
        pltpu.make_async_copy(arrived, rest, sems.at[0]).start()

    pltpu.make_async_copy(arrived, rest, sems.at[0]).wait()


def keep_last(ctl, arrived, before, out, sems):
    del before
    copy = pltpu.make_async_copy(arrived, out.at[ctl[MOVE + 1]], sems.at[0])
    copy.start()
    copy.wait()


def vmem():
    return pl.BlockSpec(memory_space=pltpu.VMEM)


def smem():
    return pl.BlockSpec(memory_space=pltpu.SMEM)


def anywhere():
    return pl.BlockSpec(memory_space=pl.ANY)


def call(kernel, outs, out_specs, in_specs, flops, scratch=(), aliases=None):
    return pl.pallas_call(
        kernel,
        scratch_shapes=scratch,
        input_output_aliases=aliases or {},
        out_shape=outs,
        in_specs=in_specs,
        out_specs=out_specs,
        compiler_params=pltpu.CompilerParams(vmem_limit_bytes=VMEM_BYTES),
        cost_estimate=pl.CostEstimate(flops=flops, bytes_accessed=4 << 20, transcendentals=0),
    )


def f32(*shape):
    return jax.ShapeDtypeStruct(shape, jnp.float32)


def line_shapes():
    devices = lax.axis_size("xb") * lax.axis_size("yb")
    return f32(8, TILE), f32(8, TILE), f32(TILE, LANES), f32(8 * devices, LANES)


def exchange(west, east, pack):
    from_west = shifted(east, "xb", 1, False)
    from_east = shifted(west, "xb", -1, False)
    from_pack = shifted(pack, "yb", 1)
    return from_west, from_east, from_pack


def spread(fast):
    return lax.all_to_all(fast, ("xb", "yb"), split_axis=0, concat_axis=0, tiled=True)


def body(state, bed, manning, neighbours, wet, moves):
    shape = f32(*state.shape)
    tile_shape = f32(*state.shape[1:])
    lines = line_shapes()
    sem = [pltpu.SemaphoreType.DMA((1,))]
    west, east, pack, fast, ctl = call(
        opening,
        lines + (jax.ShapeDtypeStruct((CONTROLS,), jnp.int32),),
        (vmem(),) * 4 + (smem(),),
        [anywhere()] * 5,
        4 << 20,
        [
            pltpu.VMEM(state.shape, jnp.float32),
            pltpu.VMEM(bed.shape, jnp.float32),
            pltpu.SMEM(neighbours.shape, jnp.int32),
            pltpu.SMEM(wet.shape, jnp.int32),
            pltpu.SMEM(moves.shape, jnp.int32),
            pltpu.SemaphoreType.DMA((6,)),
        ],
    )(state, bed, neighbours, wet, moves)
    for step in range(STEPS):
        got = exchange(west, east, pack)
        tops = spread(fast)
        rate = call(rates, shape, vmem(), [smem()] + [vmem()] * 5, 16 << 20)(ctl, state, bed, *got)
        more = step + 1 < STEPS
        extra = lines if more else (tile_shape,)
        outs = call(
            functools.partial(update, step),
            (shape,) + extra,
            (vmem(),) * (1 + len(extra)),
            [smem()] + [vmem()] * 5,
            8 << 20,
        )(ctl, tops, state, bed, manning, rate)
        state = outs[0]
        if more:
            _, west, east, pack, fast = outs
    arrived = shifted(outs[1], "xb", 1)
    leaving = call(
        second_leaving, tile_shape, anywhere(), [smem(), anywhere(), anywhere()], 1 << 20, sem
    )(ctl, state, arrived)
    arrived_next = shifted(leaving, "xb", 1)
    final = call(
        keep_rest, shape, anywhere(), [smem(), anywhere(), anywhere()], 1 << 20, sem
    )(ctl, state, arrived)
    return call(
        keep_last, shape, anywhere(), [smem(), anywhere(), anywhere()], 1 << 20, sem, {2: 0}
    )(ctl, arrived_next, final)


def solution(mesh):
    placed = (
        P(("runs", "xb", "yb"), None, None, None),
        P(("runs", "xb", "yb"), None, None),
        P(("runs", "xb", "yb"), None, None),
        P("runs", None),
        P(None, "runs"),
        P(None, "runs"),
    )
    return jax.shard_map(
        body,
        mesh=mesh,
        in_specs=placed,
        out_specs=P(("runs", "xb", "yb"), None, None, None),
        check_vma=False,
    )
```

```python
import functools

import jax
import jax.numpy as jnp
from jax import lax
from jax.experimental import pallas as pl
from jax.experimental.pallas import tpu as pltpu
from jax.sharding import PartitionSpec as P

STEPS = 3
GRAVITY = 9.81
ROOT_G = GRAVITY**0.5
SPACING = 5.0
COURANT = 0.2
ROWS = 32
LANES = 128
TILE = 256
VMEM_BYTES = 24 * 1024 * 1024
SLOT_LOW, WALL_WEST, WALL_EAST, WALL_OUTER, WET, MOVE = 0, 1, 3, 5, 7, 13
CONTROLS = 16
CHUNKS = 4
TOP = 6
SCALE = 0.5 / SPACING
SLOPE = GRAVITY / (2.0 * SPACING)


def shifted(value, axis, steps, around=True):
    count = lax.axis_size(axis)
    pairs = [(source, (source + steps) % count) for source in range(count)]
    if not around:
        pairs = [pair for pair in pairs if abs(pair[0] - pair[1]) == abs(steps)]
    return lax.ppermute(value, axis, pairs)


def cell(h, hu, hv):
    root = lax.rsqrt(h)
    inverse = root * root
    u = hu * inverse
    v = hv * inverse
    celerity = ROOT_G * (h * root)
    pressure = (0.5 * GRAVITY) * (h * h)
    cross = hu * v
    speed_x = jnp.abs(u) + celerity
    speed_y = jnp.abs(v) + celerity
    along_x = (h, hu, hv, hu * u + pressure, cross, speed_x)
    along_y = (h, hv, hu, hv * v + pressure, cross, speed_y)
    return along_x, along_y


def face(left, right):
    wave = jnp.maximum(left[5], right[5])
    return (
        (left[1] + right[1]) - wave * (right[0] - left[0]),
        (left[3] + right[3]) - wave * (right[1] - left[1]),
        (left[4] + right[4]) - wave * (right[2] - left[2]),
    )


def slot_of(ctl, position):
    low = ctl[SLOT_LOW]
    return low if position == 0 else 1 - low


def flag(ctl, index):
    return ctl[index] > 0


def start_all(pairs, sems, first=0):
    copies = [
        pltpu.make_async_copy(src, dst, sems.at[first + k]) for k, (src, dst) in enumerate(pairs)
    ]
    for copy in copies:
        copy.start()
    return copies


def wait_all(copies):
    for copy in copies:
        copy.wait()


def sublanes(width=TILE):
    return lax.broadcasted_iota(jnp.int32, (8, width), 0)


def stacked(lines, base):
    row = sublanes()
    for index, line in enumerate(lines):
        base = jnp.where(row == index, jnp.broadcast_to(line, (8, TILE)), base)
    return base


def messages(ctl, state, bed, fastest, out, columns):
    upper = lax.axis_index("yb")
    column = lax.axis_index("xb")
    last = lax.axis_size("xb") - 1
    devices = 2 * (last + 1)
    block = out.shape[0] // devices
    device = column * 2 + upper
    top = jnp.broadcast_to(fastest, (8, TILE))
    for peer in range(devices):
        out[peer * block : peer * block + 8, :] = top
    row = sublanes()

    def edge(line):
        rows = slice(line, line + 1)
        slots = [slot_of(ctl, position) for position in range(2)]
        fields = [state[slot, field, rows, :] for slot in slots for field in range(3)]
        return stacked(fields, top), [bed[slot, rows, :] for slot in slots] if bed is not None else None

    for inside, peer, line in (
        (column > 0, device - 2, 0),
        (column < last, device + 2, TILE - 1),
    ):

        @pl.when(inside)
        def _(peer=peer, line=line):
            lines, ground = edge(line)
            start = pl.multiple_of(peer * block, 8)
            out[pl.ds(start, 8), :] = lines
            if ground:
                out[pl.ds(pl.multiple_of(start + 8, 8), 8), :] = stacked(ground, top)

    slot = jnp.where(upper > 0, ctl[SLOT_LOW], 1 - ctl[SLOT_LOW])
    begin = pl.multiple_of((1 - upper) * LANES, LANES)
    lane = lax.broadcasted_iota(jnp.int32, (TILE, LANES), 1)
    packed = None
    for field in range(4 if bed is not None else 3):
        if field < 3:
            part = state[slot, field, :, pl.ds(begin, LANES)]
        else:
            part = bed[slot, :, pl.ds(begin, LANES)]
        turned = pltpu.roll(part, field + 1 - upper, 1)
        packed = turned if field == 0 else jnp.where(lane == field, turned, packed)
    lines = jnp.transpose(packed)[:8]
    columns[...] = lines
    start = pl.multiple_of((device + 1 - 2 * upper) * block, 8)
    out[pl.ds(start, 8), :] = jnp.where(row == TOP, top, lines)


def opening(
    state_in, bed_in, neighbours_in, wet_in, moves_in,
    out, columns, ctl,
    state, bed, neighbours, wet, moves, sems,
):
    copies = start_all(
        (
            (neighbours_in, neighbours),
            (wet_in, wet),
            (moves_in, moves),
            (state_in.at[0], state.at[0]),
            (state_in.at[1], state.at[1]),
            (bed_in, bed),
        ),
        sems,
    )
    device = lax.axis_index("xb") * 2 + lax.axis_index("yb")
    wait_all(copies[:3])
    first = device * 2
    low = jnp.where(neighbours[first, 3] == first + 1, 0, 1)
    ctl[SLOT_LOW] = low
    for position in range(2):
        slot = low if position == 0 else 1 - low
        tile = first + slot
        ctl[WALL_WEST + position] = (neighbours[tile, 0] < 0).astype(jnp.int32)
        ctl[WALL_EAST + position] = (neighbours[tile, 1] < 0).astype(jnp.int32)
        ctl[WALL_OUTER + position] = (neighbours[tile, 2 + position] < 0).astype(jnp.int32)
    for step in range(STEPS):
        for slot in range(2):
            ctl[WET + 2 * step + slot] = wet[step, first + slot]
        ctl[MOVE + step] = moves[step, device]

    total = jnp.zeros((ROWS, TILE), jnp.float32)
    for slot in range(2):
        copies[3 + slot].wait()

        def group(index, best, slot=slot):
            rows = pl.ds(pl.multiple_of(index * ROWS, ROWS), ROWS)
            along_x, along_y = cell(*(state[slot, field, rows, :] for field in range(3)))
            return jnp.maximum(best, jnp.maximum(along_x[5], along_y[5]))

        best = lax.fori_loop(0, TILE // ROWS, group, jnp.zeros((ROWS, TILE), jnp.float32))
        total = jnp.maximum(total, jnp.where(wet[0, first + slot] > 0, best, 0.0))
    copies[5].wait()
    messages(ctl, state, bed, jnp.max(total, keepdims=True), out, columns)


def rates(ctl, state_in, bed_in, rate_out, state, bed, rate, sems):
    row_ids = lax.broadcasted_iota(jnp.int32, (ROWS, TILE), 0)
    lane = lax.broadcasted_iota(jnp.int32, (ROWS, LANES), 1)
    row8 = sublanes()
    last = TILE // ROWS - 1
    chunk = TILE // CHUNKS
    incoming = []
    for part in range(CHUNKS):
        rows = slice(part * chunk, (part + 1) * chunk)
        incoming.append(
            start_all(
                (
                    (state_in.at[:, :, rows], state.at[:, :, rows]),
                    (bed_in.at[:, rows], bed.at[:, rows]),
                ),
                sems,
                2 * part,
            )
        )
    wait_all(incoming[0])
    outgoing = []

    def field_ref(which, field):
        return bed.at[which] if field == 3 else state.at[which, field]

    def opening_faces(position):
        slot = slot_of(ctl, position)
        keep = jnp.where(flag(ctl, WALL_WEST + position), 1.0, 0.0)
        first = [field_ref(slot, field)[0:8, :] for field in range(4)]
        right, _ = cell(*first[:3])
        left, _ = cell(first[0], -first[1], first[2])
        return tuple(keep * part[0:1, :] for part in face(left, right)) + (keep * first[3][0:1, :],)

    def group_of(position):
        slot = slot_of(ctl, position)
        other = 1 - slot
        keep_outer = jnp.where(flag(ctl, WALL_OUTER + position), 1.0, 0.0)
        keep_east = jnp.where(flag(ctl, WALL_EAST + position), 1.0, 0.0)
        inner_lane = LANES - 1 if position == 0 else 0
        outer_lane = LANES - 1 - inner_lane
        inner_cols = slice(0, LANES) if position == 0 else slice(LANES, TILE)
        inner_turn = LANES - 1 if position == 0 else 1

        def group(index, carry):
            base = pl.multiple_of(index * ROWS, ROWS)
            rows = pl.ds(base, ROWS)
            after = pl.ds(pl.multiple_of(jnp.minimum(base + ROWS, TILE - 8), 8), 8)
            at_end = index == last
            fields = []
            for field in range(4):
                ref = field_ref(slot, field)
                block = ref[rows, :]
                mirrored = jnp.broadcast_to(block[ROWS - 1 : ROWS], (8, TILE))
                if field == 1:
                    mirrored = -mirrored
                if field == 3:
                    mirrored = keep_east * mirrored
                fields.append(
                    jnp.concatenate([block, jnp.where(at_end, mirrored, ref[after, :])], 0)
                )
            cells_x, cells_y = cell(*fields[:3])

            def down(value):
                return pltpu.roll(value, ROWS + 7, 0)[:ROWS]

            here = tuple(value[:ROWS] for value in cells_x)
            keep = jnp.where(row8 == 7, jnp.where(at_end, keep_east, 1.0), 1.0)
            faces = tuple(
                jnp.concatenate([value[: ROWS - 8], value[ROWS - 8 :] * keep], 0)
                for value in face(here, tuple(down(value) for value in cells_x))
            )
            turned = tuple(pltpu.roll(value, 1, 0) for value in faces)
            change_x = tuple(
                value - jnp.where(row_ids == 0, before, moved)
                for value, before, moved in zip(faces, carry[:3], turned)
            )
            ground = fields[3][:ROWS]
            ground_up = pltpu.roll(ground, 1, 0)
            slope_x = down(fields[3]) - jnp.where(row_ids == 0, carry[3], ground_up)
            carried = tuple(value[0:1, :] for value in turned) + (ground_up[0:1, :],)

            ghosts = []
            for field in range(4):
                inner = pltpu.roll(field_ref(other, field)[rows, inner_cols], inner_turn, 1)
                own = fields[field][:ROWS, inner_cols]
                if field == 2:
                    own = -own
                if field == 3:
                    own = keep_outer * own
                ghosts.append(jnp.where(lane == inner_lane, inner, own))
            _, ghost_y = cell(*ghosts[:3])
            low = tuple(value[:ROWS, :LANES] for value in cells_y)
            high = tuple(value[:ROWS, LANES:] for value in cells_y)

            def right_of(low_part, high_part, ghost_part):
                turned_low = pltpu.roll(low_part, LANES - 1, 1)
                turned_high = pltpu.roll(high_part, LANES - 1, 1)
                return (
                    jnp.where(lane == LANES - 1, turned_high, turned_low),
                    jnp.where(lane == LANES - 1, ghost_part, turned_high),
                )

            pairs = [right_of(a, b, c) for a, b, c in zip(low, high, ghost_y)]
            faces_low = face(low, tuple(pair[0] for pair in pairs))
            faces_high = face(high, tuple(pair[1] for pair in pairs))
            faces_edge = face(ghost_y, low)
            if position == 0:
                faces_edge = tuple(keep_outer * value for value in faces_edge)
            else:
                keep_lane = jnp.where(lane == outer_lane, keep_outer, 1.0)
                faces_high = tuple(keep_lane * value for value in faces_high)
            change_y = []
            for a, b, c in zip(faces_low, faces_high, faces_edge):
                turned_a = pltpu.roll(a, 1, 1)
                turned_b = pltpu.roll(b, 1, 1)
                change_y.append(
                    jnp.concatenate(
                        [
                            a - jnp.where(lane == 0, c, turned_a),
                            b - jnp.where(lane == 0, turned_a, turned_b),
                        ],
                        1,
                    )
                )
            ground_low = ground[:, :LANES]
            ground_high = ground[:, LANES:]
            north = right_of(ground_low, ground_high, ghosts[3])
            turned_low = pltpu.roll(ground_low, 1, 1)
            turned_high = pltpu.roll(ground_high, 1, 1)
            slope_y = jnp.concatenate(
                [
                    north[0] - jnp.where(lane == 0, ghosts[3], turned_low),
                    north[1] - jnp.where(lane == 0, turned_low, turned_high),
                ],
                1,
            )
            weight = SLOPE * fields[0][:ROWS]
            rate[slot, 0, rows, :] = SCALE * (change_x[0] + change_y[0])
            rate[slot, 1, rows, :] = SCALE * (change_x[1] + change_y[2]) + weight * slope_x
            rate[slot, 2, rows, :] = SCALE * (change_x[2] + change_y[1]) + weight * slope_y
            return carried

        return group

    carries = [opening_faces(position) for position in range(2)]
    groups = [group_of(position) for position in range(2)]
    per_chunk = chunk // ROWS
    for part in range(CHUNKS):
        if part + 1 < CHUNKS:
            wait_all(incoming[part + 1])
        for position in range(2):
            carries[position] = lax.fori_loop(
                part * per_chunk, (part + 1) * per_chunk, groups[position], carries[position]
            )
        rows = slice(part * chunk, (part + 1) * chunk)
        outgoing += start_all(
            ((rate.at[:, :, rows], rate_out.at[:, :, rows]),), sems, 2 * CHUNKS + part
        )
    wait_all(outgoing)


def correct_rows(ctl, slot, got, ground, block, state, rate, bottom):
    position = jnp.where(ctl[SLOT_LOW] == slot, 0, 1)
    device = lax.axis_index("xb") * 2 + lax.axis_index("yb")
    wall = WALL_WEST if bottom else WALL_EAST

    @pl.when(jnp.logical_not(flag(ctl, wall + position)))
    def _():
        peer = device - 2 if bottom else device + 2
        lines = got[pl.ds(pl.multiple_of(peer * block, 8), 8), :]
        grounds = ground[pl.ds(pl.multiple_of(peer * 16 + 8, 8), 8), :]

        def line(value, offset):
            picked = jnp.where(
                position == 0, value[offset : offset + 1, :], value[offset + 3 : offset + 4, :]
            )
            return jnp.broadcast_to(picked, (8, TILE))

        ghost, _ = cell(*(line(lines, field) for field in range(3)))
        ghost_ground = jnp.where(position == 0, grounds[0:1, :], grounds[1:2, :])
        rows = slice(0, 8) if bottom else slice(TILE - 8, TILE)
        own = [state[slot, field, rows, :] for field in range(3)]
        here, _ = cell(*own)
        fluxes = face(ghost, here) if bottom else face(here, ghost)
        push = SCALE * fluxes[1] + (SLOPE * own[0]) * ghost_ground
        row = sublanes()
        sign = -1.0 if bottom else 1.0
        chosen = row == (0 if bottom else 7)
        for field, value in enumerate((SCALE * fluxes[0], push, SCALE * fluxes[2])):
            rate[slot, field, rows, :] += jnp.where(chosen, sign * value, 0.0)


def column_fix(got, ground, block, columns, bed_columns):
    upper = lax.axis_index("yb")
    device = lax.axis_index("xb") * 2 + upper
    peer = device + 1 - 2 * upper
    lines = got[pl.ds(pl.multiple_of(peer * block, 8), 8), :]
    ghost_ground = ground[pl.ds(pl.multiple_of(peer * 16, 8), 8), :][3:4]
    del bed_columns
    mine = columns[...]
    _, ghost = cell(lines[0:1], lines[1:2], lines[2:3])
    _, own = cell(mine[0:1], mine[1:2], mine[2:3])
    low = upper == 0
    left = tuple(jnp.where(low, a, b) for a, b in zip(own, ghost))
    right = tuple(jnp.where(low, b, a) for a, b in zip(own, ghost))
    fluxes = face(left, right)
    sign = jnp.where(low, 1.0, -1.0)
    push = SCALE * fluxes[1] + (SLOPE * mine[0:1]) * ghost_ground
    block8 = stacked(
        [sign * SCALE * fluxes[0], sign * SCALE * fluxes[2], sign * push],
        jnp.zeros((8, TILE), jnp.float32),
    )
    return jnp.transpose(
        jnp.concatenate([block8, jnp.zeros((LANES - 8, TILE), jnp.float32)], 0)
    )


def update(step, ctl, got, ground, columns, state_in, manning_in, rate_in, *rest):
    more = step + 1 < STEPS
    if more:
        fresh_out, out, columns_out = rest[:3]
        rest = rest[3:]
    else:
        fresh_out, leaving = rest[:2]
        rest = rest[2:]
    state, manning, rate, fresh, sems = rest
    half = TILE // 2
    parts = [(slot, slice(k * half, (k + 1) * half)) for slot in range(2) for k in range(2)]
    incoming = []
    for index, (slot, rows) in enumerate(parts):
        incoming.append(
            start_all(
                (
                    (rate_in.at[slot, :, rows], rate.at[slot, :, rows]),
                    (state_in.at[slot, :, rows], state.at[slot, :, rows]),
                    (manning_in.at[slot, rows], manning.at[slot, rows]),
                ),
                sems,
                3 * index,
            )
        )
    upper = lax.axis_index("yb")
    devices = 2 * lax.axis_size("xb")
    block = got.shape[0] // devices
    tops = got[0:8, :]
    for peer in range(1, devices):
        tops = jnp.maximum(tops, got[peer * block : peer * block + 8, :])
    delta = (COURANT * SPACING) / tops[TOP : TOP + 1, :]
    fix = column_fix(got, ground, block, columns, None)
    facing = jnp.where(upper > 0, ctl[SLOT_LOW], 1 - ctl[SLOT_LOW])
    begin = pl.multiple_of((1 - upper) * LANES, LANES)
    target = (1 - upper) * (LANES - 1)
    lane = lax.broadcasted_iota(jnp.int32, (half, LANES), 1)
    total = jnp.zeros((ROWS, TILE), jnp.float32)
    outgoing = []
    for index, (slot, part_rows) in enumerate(parts):
        wait_all(incoming[index])
        bottom = index % 2 == 0
        correct_rows(ctl, slot, got, ground, block, state, rate, bottom)

        @pl.when(facing == slot)
        def _(slot=slot, part_rows=part_rows):
            for field in range(3):
                turned = pltpu.roll(
                    fix[part_rows], lax.rem(target + LANES - field, LANES), 1
                )
                rate[slot, field, part_rows, pl.ds(begin, LANES)] += jnp.where(
                    lane == target, turned, 0.0
                )

        wet_now = flag(ctl, WET + 2 * step + slot)

        def group(index, best, slot=slot, wet_now=wet_now):
            rows = pl.ds(pl.multiple_of(index * ROWS, ROWS), ROWS)
            h0, hu0, hv0 = (state[slot, field, rows, :] for field in range(3))
            h = h0 - delta * rate[slot, 0, rows, :]
            hu = hu0 - delta * rate[slot, 1, rows, :]
            hv = hv0 - delta * rate[slot, 2, rows, :]
            rough = manning[slot, rows, :]
            inverse = 1.0 / h
            u = hu * inverse
            v = hv * inverse
            speed = jnp.sqrt(u * u + v * v)
            power = jnp.exp((-4.0 / 3.0) * jnp.log(jnp.abs(h)))
            drag = (GRAVITY * delta) * (rough * rough) * (speed * power)
            factor = 1.0 / (1.0 + drag)
            hu = hu * factor
            hv = hv * factor
            h = jnp.where(wet_now, h, h0)
            hu = jnp.where(wet_now, hu, hu0)
            hv = jnp.where(wet_now, hv, hv0)
            fresh[slot, 0, rows, :] = h
            fresh[slot, 1, rows, :] = hu
            fresh[slot, 2, rows, :] = hv
            if more:
                along_x, along_y = cell(h, hu, hv)
                best = jnp.maximum(best, jnp.maximum(along_x[5], along_y[5]))
            return best

        best = lax.fori_loop(
            part_rows.start // ROWS,
            part_rows.stop // ROWS,
            group,
            jnp.zeros((ROWS, TILE), jnp.float32),
        )
        if more:
            best = jnp.where(flag(ctl, WET + 2 * step + 2 + slot), best, 0.0)
            total = jnp.maximum(total, best)
        outgoing += start_all(
            ((fresh.at[slot, :, part_rows], fresh_out.at[slot, :, part_rows]),), sems, 12 + index
        )
    if more:
        messages(ctl, fresh, None, jnp.max(total, keepdims=True), out, columns_out)
    else:
        outgoing += start_all(((fresh.at[ctl[MOVE]], leaving),), sems, 16)
    wait_all(outgoing)


def second_leaving(ctl, state, arrived, leaving, sems):
    again = ctl[MOVE] == ctl[MOVE + 1]

    @pl.when(again)
    def _():
        pltpu.make_async_copy(arrived, leaving, sems.at[0]).start()

    @pl.when(jnp.logical_not(again))
    def _():
        pltpu.make_async_copy(state.at[1 - ctl[MOVE]], leaving, sems.at[0]).start()

    pltpu.make_async_copy(arrived, leaving, sems.at[0]).wait()


def keep_rest(ctl, state, arrived, out, sems):
    rest = out.at[1 - ctl[MOVE + 1]]
    again = ctl[MOVE] == ctl[MOVE + 1]

    @pl.when(again)
    def _():
        pltpu.make_async_copy(state.at[1 - ctl[MOVE]], rest, sems.at[0]).start()

    @pl.when(jnp.logical_not(again))
    def _():
        pltpu.make_async_copy(arrived, rest, sems.at[0]).start()

    pltpu.make_async_copy(arrived, rest, sems.at[0]).wait()


def keep_last(ctl, arrived, before, out, sems):
    del before
    copy = pltpu.make_async_copy(arrived, out.at[ctl[MOVE + 1]], sems.at[0])
    copy.start()
    copy.wait()


def vmem():
    return pl.BlockSpec(memory_space=pltpu.VMEM)


def smem():
    return pl.BlockSpec(memory_space=pltpu.SMEM)


def hbm():
    return pl.BlockSpec(memory_space=pltpu.HBM)


def anywhere():
    return pl.BlockSpec(memory_space=pl.ANY)


def call(kernel, outs, out_specs, in_specs, flops, scratch=(), aliases=None):
    return pl.pallas_call(
        kernel,
        scratch_shapes=scratch,
        input_output_aliases=aliases or {},
        out_shape=outs,
        in_specs=in_specs,
        out_specs=out_specs,
        compiler_params=pltpu.CompilerParams(vmem_limit_bytes=VMEM_BYTES),
        cost_estimate=pl.CostEstimate(flops=flops, bytes_accessed=4 << 20, transcendentals=0),
    )


def f32(*shape):
    return jax.ShapeDtypeStruct(shape, jnp.float32)


def spread(fast):
    return lax.all_to_all(fast, ("xb", "yb"), split_axis=0, concat_axis=0, tiled=True)


def body(state, bed, manning, neighbours, wet, moves):
    shape = f32(*state.shape)
    tile_shape = f32(*state.shape[1:])
    devices = lax.axis_size("xb") * lax.axis_size("yb")
    sem = [pltpu.SemaphoreType.DMA((1,))]
    whole = pltpu.VMEM(state.shape, jnp.float32)
    part = pltpu.VMEM(bed.shape, jnp.float32)
    out, columns, ctl = call(
        opening,
        (
            f32(16 * devices, TILE),
            f32(8, TILE),
            jax.ShapeDtypeStruct((CONTROLS,), jnp.int32),
        ),
        (vmem(), vmem(), smem()),
        [hbm()] * 5,
        4 << 20,
        [
            whole,
            part,
            pltpu.SMEM(neighbours.shape, jnp.int32),
            pltpu.SMEM(wet.shape, jnp.int32),
            pltpu.SMEM(moves.shape, jnp.int32),
            pltpu.SemaphoreType.DMA((6,)),
        ],
    )(state, bed, neighbours, wet, moves)
    ground = None
    for step in range(STEPS):
        got = spread(out)
        ground = got if step == 0 else ground
        rate = call(
            rates,
            shape,
            hbm(),
            [smem(), hbm(), hbm()],
            16 << 20,
            [whole, part, whole, pltpu.SemaphoreType.DMA((3 * CHUNKS,))],
        )(ctl, state, bed)
        more = step + 1 < STEPS
        extra = (f32(8 * devices, TILE), f32(8, TILE)) if more else (tile_shape,)
        outs = call(
            functools.partial(update, step),
            (shape,) + extra,
            (hbm(), vmem(), vmem()) if more else (hbm(), hbm()),
            [smem(), vmem(), vmem(), vmem(), hbm(), hbm(), hbm()],
            8 << 20,
            [whole, part, whole, whole, pltpu.SemaphoreType.DMA((17,))],
        )(ctl, got, ground, columns, state, manning, rate)
        state = outs[0]
        if more:
            _, out, columns = outs
    arrived = shifted(outs[1], "xb", 1)
    leaving = call(
        second_leaving, tile_shape, anywhere(), [smem(), anywhere(), anywhere()], 1 << 20, sem
    )(ctl, state, arrived)
    arrived_next = shifted(leaving, "xb", 1)
    final = call(
        keep_rest, shape, anywhere(), [smem(), anywhere(), anywhere()], 1 << 20, sem
    )(ctl, state, arrived)
    return call(
        keep_last, shape, anywhere(), [smem(), anywhere(), anywhere()], 1 << 20, sem, {2: 0}
    )(ctl, arrived_next, final)


def solution(mesh):
    placed = (
        P(("runs", "xb", "yb"), None, None, None),
        P(("runs", "xb", "yb"), None, None),
        P(("runs", "xb", "yb"), None, None),
        P("runs", None),
        P(None, "runs"),
        P(None, "runs"),
    )
    return jax.shard_map(
        body,
        mesh=mesh,
        in_specs=placed,
        out_specs=P(("runs", "xb", "yb"), None, None, None),
        check_vma=False,
    )
```

```python
import functools

import jax
import jax.numpy as jnp
from jax import lax
from jax.experimental import pallas as pl
from jax.experimental.pallas import tpu as pltpu
from jax.sharding import PartitionSpec as P

STEPS = 3
GRAVITY = 9.81
ROOT_G = GRAVITY**0.5
SPACING = 5.0
COURANT = 0.2
ROWS = 32
LANES = 128
TILE = 256
VMEM_BYTES = 60 * 1024 * 1024
SLOT_LOW, WALL_WEST, WALL_EAST, WALL_OUTER, WET, MOVE = 0, 1, 3, 5, 7, 13
CONTROLS = 16
CHUNKS = 4
TOP = 6
SCALE = 0.5 / SPACING
SLOPE = GRAVITY / (2.0 * SPACING)


def shifted(value, axis, steps, around=True):
    count = lax.axis_size(axis)
    pairs = [(source, (source + steps) % count) for source in range(count)]
    if not around:
        pairs = [pair for pair in pairs if abs(pair[0] - pair[1]) == abs(steps)]
    return lax.ppermute(value, axis, pairs)


def cell(h, hu, hv):
    root = lax.rsqrt(h)
    inverse = root * root
    u = hu * inverse
    v = hv * inverse
    celerity = ROOT_G * (h * root)
    pressure = (0.5 * GRAVITY) * (h * h)
    cross = hu * v
    speed_x = jnp.abs(u) + celerity
    speed_y = jnp.abs(v) + celerity
    along_x = (h, hu, hv, hu * u + pressure, cross, speed_x)
    along_y = (h, hv, hu, hv * v + pressure, cross, speed_y)
    return along_x, along_y


def face(left, right):
    wave = jnp.maximum(left[5], right[5])
    return (
        (left[1] + right[1]) - wave * (right[0] - left[0]),
        (left[3] + right[3]) - wave * (right[1] - left[1]),
        (left[4] + right[4]) - wave * (right[2] - left[2]),
    )


def slot_of(ctl, position):
    low = ctl[SLOT_LOW]
    return low if position == 0 else 1 - low


def flag(ctl, index):
    return ctl[index] > 0


def start_all(pairs, sems, first=0):
    copies = [
        pltpu.make_async_copy(src, dst, sems.at[first + k]) for k, (src, dst) in enumerate(pairs)
    ]
    for copy in copies:
        copy.start()
    return copies


def wait_all(copies):
    for copy in copies:
        copy.wait()


def sublanes(width=TILE):
    return lax.broadcasted_iota(jnp.int32, (8, width), 0)


def stacked(lines, base):
    row = sublanes()
    for index, line in enumerate(lines):
        base = jnp.where(row == index, jnp.broadcast_to(line, (8, TILE)), base)
    return base


def messages(ctl, state, bed, fastest, out, columns):
    upper = lax.axis_index("yb")
    column = lax.axis_index("xb")
    last = lax.axis_size("xb") - 1
    devices = 2 * (last + 1)
    block = out.shape[0] // devices
    device = column * 2 + upper
    top = jnp.broadcast_to(fastest, (8, TILE))
    for peer in range(devices):
        out[peer * block : peer * block + 8, :] = top
    row = sublanes()

    def edge(line):
        rows = slice(line, line + 1)
        slots = [slot_of(ctl, position) for position in range(2)]
        fields = [state[slot, field, rows, :] for slot in slots for field in range(3)]
        return stacked(fields, top), [bed[slot, rows, :] for slot in slots] if bed is not None else None

    for inside, peer, line in (
        (column > 0, device - 2, 0),
        (column < last, device + 2, TILE - 1),
    ):

        @pl.when(inside)
        def _(peer=peer, line=line):
            lines, ground = edge(line)
            start = pl.multiple_of(peer * block, 8)
            out[pl.ds(start, 8), :] = lines
            if ground:
                out[pl.ds(pl.multiple_of(start + 8, 8), 8), :] = stacked(ground, top)

    slot = jnp.where(upper > 0, ctl[SLOT_LOW], 1 - ctl[SLOT_LOW])
    begin = pl.multiple_of((1 - upper) * LANES, LANES)
    lane = lax.broadcasted_iota(jnp.int32, (TILE, LANES), 1)
    packed = None
    for field in range(4 if bed is not None else 3):
        if field < 3:
            part = state[slot, field, :, pl.ds(begin, LANES)]
        else:
            part = bed[slot, :, pl.ds(begin, LANES)]
        turned = pltpu.roll(part, field + 1 - upper, 1)
        packed = turned if field == 0 else jnp.where(lane == field, turned, packed)
    lines = jnp.transpose(packed)[:8]
    columns[...] = lines
    start = pl.multiple_of((device + 1 - 2 * upper) * block, 8)
    out[pl.ds(start, 8), :] = jnp.where(row == TOP, top, lines)


def opening(
    state_in, bed_in, neighbours_in, wet_in, moves_in,
    out, columns, ctl,
    state, bed, neighbours, wet, moves, sems,
):
    copies = start_all(
        (
            (neighbours_in, neighbours),
            (wet_in, wet),
            (moves_in, moves),
            (state_in.at[0], state.at[0]),
            (state_in.at[1], state.at[1]),
            (bed_in, bed),
        ),
        sems,
    )
    device = lax.axis_index("xb") * 2 + lax.axis_index("yb")
    wait_all(copies[:3])
    first = device * 2
    low = jnp.where(neighbours[3, first] == first + 1, 0, 1)
    ctl[SLOT_LOW] = low
    for position in range(2):
        slot = low if position == 0 else 1 - low
        tile = first + slot
        ctl[WALL_WEST + position] = (neighbours[0, tile] < 0).astype(jnp.int32)
        ctl[WALL_EAST + position] = (neighbours[1, tile] < 0).astype(jnp.int32)
        ctl[WALL_OUTER + position] = (neighbours[2 + position, tile] < 0).astype(jnp.int32)
    for step in range(STEPS):
        for slot in range(2):
            ctl[WET + 2 * step + slot] = wet[step, first + slot]
        ctl[MOVE + step] = moves[step, device]

    total = jnp.zeros((ROWS, TILE), jnp.float32)
    for slot in range(2):
        copies[3 + slot].wait()

        def group(index, best, slot=slot):
            rows = pl.ds(pl.multiple_of(index * ROWS, ROWS), ROWS)
            along_x, along_y = cell(*(state[slot, field, rows, :] for field in range(3)))
            return jnp.maximum(best, jnp.maximum(along_x[5], along_y[5]))

        best = lax.fori_loop(0, TILE // ROWS, group, jnp.zeros((ROWS, TILE), jnp.float32))
        total = jnp.maximum(total, jnp.where(wet[0, first + slot] > 0, best, 0.0))
    copies[5].wait()
    messages(ctl, state, bed, jnp.max(total, keepdims=True), out, columns)


def rates(ctl, state_in, bed_in, rate_out, state, bed, rate, sems):
    row_ids = lax.broadcasted_iota(jnp.int32, (ROWS, TILE), 0)
    lane = lax.broadcasted_iota(jnp.int32, (ROWS, LANES), 1)
    row8 = sublanes()
    last = TILE // ROWS - 1
    chunk = TILE // CHUNKS
    incoming = []
    for part in range(CHUNKS):
        rows = slice(part * chunk, (part + 1) * chunk)
        incoming.append(
            start_all(
                (
                    (state_in.at[:, :, rows], state.at[:, :, rows]),
                    (bed_in.at[:, rows], bed.at[:, rows]),
                ),
                sems,
                2 * part,
            )
        )
    wait_all(incoming[0])
    outgoing = []

    def field_ref(which, field):
        return bed.at[which] if field == 3 else state.at[which, field]

    def opening_faces(position):
        slot = slot_of(ctl, position)
        keep = jnp.where(flag(ctl, WALL_WEST + position), 1.0, 0.0)
        first = [field_ref(slot, field)[0:8, :] for field in range(4)]
        right, _ = cell(*first[:3])
        left, _ = cell(first[0], -first[1], first[2])
        return tuple(keep * part[0:1, :] for part in face(left, right)) + (keep * first[3][0:1, :],)

    def group_of(position):
        slot = slot_of(ctl, position)
        other = 1 - slot
        keep_outer = jnp.where(flag(ctl, WALL_OUTER + position), 1.0, 0.0)
        keep_east = jnp.where(flag(ctl, WALL_EAST + position), 1.0, 0.0)
        inner_lane = LANES - 1 if position == 0 else 0
        outer_lane = LANES - 1 - inner_lane
        inner_cols = slice(0, LANES) if position == 0 else slice(LANES, TILE)
        inner_turn = LANES - 1 if position == 0 else 1

        def group(index, carry):
            base = pl.multiple_of(index * ROWS, ROWS)
            rows = pl.ds(base, ROWS)
            after = pl.ds(pl.multiple_of(jnp.minimum(base + ROWS, TILE - 8), 8), 8)
            at_end = index == last
            fields = []
            for field in range(4):
                ref = field_ref(slot, field)
                block = ref[rows, :]
                mirrored = jnp.broadcast_to(block[ROWS - 1 : ROWS], (8, TILE))
                if field == 1:
                    mirrored = -mirrored
                if field == 3:
                    mirrored = keep_east * mirrored
                fields.append(
                    jnp.concatenate([block, jnp.where(at_end, mirrored, ref[after, :])], 0)
                )
            cells_x, cells_y = cell(*fields[:3])

            def down(value):
                return pltpu.roll(value, ROWS + 7, 0)[:ROWS]

            here = tuple(value[:ROWS] for value in cells_x)
            keep = jnp.where(row8 == 7, jnp.where(at_end, keep_east, 1.0), 1.0)
            faces = tuple(
                jnp.concatenate([value[: ROWS - 8], value[ROWS - 8 :] * keep], 0)
                for value in face(here, tuple(down(value) for value in cells_x))
            )
            turned = tuple(pltpu.roll(value, 1, 0) for value in faces)
            change_x = tuple(
                value - jnp.where(row_ids == 0, before, moved)
                for value, before, moved in zip(faces, carry[:3], turned)
            )
            ground = fields[3][:ROWS]
            ground_up = pltpu.roll(ground, 1, 0)
            slope_x = down(fields[3]) - jnp.where(row_ids == 0, carry[3], ground_up)
            carried = tuple(value[0:1, :] for value in turned) + (ground_up[0:1, :],)

            ghosts = []
            for field in range(4):
                inner = pltpu.roll(field_ref(other, field)[rows, inner_cols], inner_turn, 1)
                own = fields[field][:ROWS, inner_cols]
                if field == 2:
                    own = -own
                if field == 3:
                    own = keep_outer * own
                ghosts.append(jnp.where(lane == inner_lane, inner, own))
            _, ghost_y = cell(*ghosts[:3])
            low = tuple(value[:ROWS, :LANES] for value in cells_y)
            high = tuple(value[:ROWS, LANES:] for value in cells_y)

            def right_of(low_part, high_part, ghost_part):
                turned_low = pltpu.roll(low_part, LANES - 1, 1)
                turned_high = pltpu.roll(high_part, LANES - 1, 1)
                return (
                    jnp.where(lane == LANES - 1, turned_high, turned_low),
                    jnp.where(lane == LANES - 1, ghost_part, turned_high),
                )

            pairs = [right_of(a, b, c) for a, b, c in zip(low, high, ghost_y)]
            faces_low = face(low, tuple(pair[0] for pair in pairs))
            faces_high = face(high, tuple(pair[1] for pair in pairs))
            faces_edge = face(ghost_y, low)
            if position == 0:
                faces_edge = tuple(keep_outer * value for value in faces_edge)
            else:
                keep_lane = jnp.where(lane == outer_lane, keep_outer, 1.0)
                faces_high = tuple(keep_lane * value for value in faces_high)
            change_y = []
            for a, b, c in zip(faces_low, faces_high, faces_edge):
                turned_a = pltpu.roll(a, 1, 1)
                turned_b = pltpu.roll(b, 1, 1)
                change_y.append(
                    jnp.concatenate(
                        [
                            a - jnp.where(lane == 0, c, turned_a),
                            b - jnp.where(lane == 0, turned_a, turned_b),
                        ],
                        1,
                    )
                )
            ground_low = ground[:, :LANES]
            ground_high = ground[:, LANES:]
            north = right_of(ground_low, ground_high, ghosts[3])
            turned_low = pltpu.roll(ground_low, 1, 1)
            turned_high = pltpu.roll(ground_high, 1, 1)
            slope_y = jnp.concatenate(
                [
                    north[0] - jnp.where(lane == 0, ghosts[3], turned_low),
                    north[1] - jnp.where(lane == 0, turned_low, turned_high),
                ],
                1,
            )
            weight = SLOPE * fields[0][:ROWS]
            rate[slot, 0, rows, :] = SCALE * (change_x[0] + change_y[0])
            rate[slot, 1, rows, :] = SCALE * (change_x[1] + change_y[2]) + weight * slope_x
            rate[slot, 2, rows, :] = SCALE * (change_x[2] + change_y[1]) + weight * slope_y
            return carried

        return group

    carries = [opening_faces(position) for position in range(2)]
    groups = [group_of(position) for position in range(2)]
    per_chunk = chunk // ROWS
    for part in range(CHUNKS):
        if part + 1 < CHUNKS:
            wait_all(incoming[part + 1])
        for position in range(2):
            carries[position] = lax.fori_loop(
                part * per_chunk, (part + 1) * per_chunk, groups[position], carries[position]
            )
        rows = slice(part * chunk, (part + 1) * chunk)
        outgoing += start_all(
            ((rate.at[:, :, rows], rate_out.at[:, :, rows]),), sems, 2 * CHUNKS + part
        )
    wait_all(outgoing)


def correct_rows(ctl, slot, got, ground, block, state, rate, bottom):
    position = jnp.where(ctl[SLOT_LOW] == slot, 0, 1)
    device = lax.axis_index("xb") * 2 + lax.axis_index("yb")
    wall = WALL_WEST if bottom else WALL_EAST

    @pl.when(jnp.logical_not(flag(ctl, wall + position)))
    def _():
        peer = device - 2 if bottom else device + 2
        lines = got[pl.ds(pl.multiple_of(peer * block, 8), 8), :]
        grounds = ground[pl.ds(pl.multiple_of(peer * 16 + 8, 8), 8), :]

        def line(value, offset):
            picked = jnp.where(
                position == 0, value[offset : offset + 1, :], value[offset + 3 : offset + 4, :]
            )
            return jnp.broadcast_to(picked, (8, TILE))

        ghost, _ = cell(*(line(lines, field) for field in range(3)))
        ghost_ground = jnp.where(position == 0, grounds[0:1, :], grounds[1:2, :])
        rows = slice(0, 8) if bottom else slice(TILE - 8, TILE)
        own = [state[slot, field, rows, :] for field in range(3)]
        here, _ = cell(*own)
        fluxes = face(ghost, here) if bottom else face(here, ghost)
        push = SCALE * fluxes[1] + (SLOPE * own[0]) * ghost_ground
        row = sublanes()
        sign = -1.0 if bottom else 1.0
        chosen = row == (0 if bottom else 7)
        for field, value in enumerate((SCALE * fluxes[0], push, SCALE * fluxes[2])):
            rate[slot, field, rows, :] += jnp.where(chosen, sign * value, 0.0)


def column_fix(got, ground, block, columns, bed_columns):
    upper = lax.axis_index("yb")
    device = lax.axis_index("xb") * 2 + upper
    peer = device + 1 - 2 * upper
    lines = got[pl.ds(pl.multiple_of(peer * block, 8), 8), :]
    ghost_ground = ground[pl.ds(pl.multiple_of(peer * 16, 8), 8), :][3:4]
    del bed_columns
    mine = columns[...]
    _, ghost = cell(lines[0:1], lines[1:2], lines[2:3])
    _, own = cell(mine[0:1], mine[1:2], mine[2:3])
    low = upper == 0
    left = tuple(jnp.where(low, a, b) for a, b in zip(own, ghost))
    right = tuple(jnp.where(low, b, a) for a, b in zip(own, ghost))
    fluxes = face(left, right)
    sign = jnp.where(low, 1.0, -1.0)
    push = SCALE * fluxes[1] + (SLOPE * mine[0:1]) * ghost_ground
    block8 = stacked(
        [sign * SCALE * fluxes[0], sign * SCALE * fluxes[2], sign * push],
        jnp.zeros((8, TILE), jnp.float32),
    )
    return jnp.transpose(
        jnp.concatenate([block8, jnp.zeros((LANES - 8, TILE), jnp.float32)], 0)
    )


def update(step, ctl, got, ground, columns, state_in, manning_in, rate_in, *rest):
    more = step + 1 < STEPS
    if more:
        fresh_out, out, columns_out = rest[:3]
        rest = rest[3:]
    else:
        fresh_out, leaving = rest[:2]
        rest = rest[2:]
    state, manning, rate, fresh, sems = rest
    half = TILE // 2
    parts = [(slot, slice(k * half, (k + 1) * half)) for slot in range(2) for k in range(2)]
    incoming = []
    for index, (slot, rows) in enumerate(parts):
        incoming.append(
            start_all(
                (
                    (rate_in.at[slot, :, rows], rate.at[slot, :, rows]),
                    (state_in.at[slot, :, rows], state.at[slot, :, rows]),
                    (manning_in.at[slot, rows], manning.at[slot, rows]),
                ),
                sems,
                3 * index,
            )
        )
    upper = lax.axis_index("yb")
    devices = 2 * lax.axis_size("xb")
    block = got.shape[0] // devices
    tops = got[0:8, :]
    for peer in range(1, devices):
        tops = jnp.maximum(tops, got[peer * block : peer * block + 8, :])
    delta = (COURANT * SPACING) / tops[TOP : TOP + 1, :]
    fix = column_fix(got, ground, block, columns, None)
    facing = jnp.where(upper > 0, ctl[SLOT_LOW], 1 - ctl[SLOT_LOW])
    begin = pl.multiple_of((1 - upper) * LANES, LANES)
    target = (1 - upper) * (LANES - 1)
    lane = lax.broadcasted_iota(jnp.int32, (half, LANES), 1)
    total = jnp.zeros((ROWS, TILE), jnp.float32)
    outgoing = []
    for index, (slot, part_rows) in enumerate(parts):
        wait_all(incoming[index])
        bottom = index % 2 == 0
        correct_rows(ctl, slot, got, ground, block, state, rate, bottom)

        @pl.when(facing == slot)
        def _(slot=slot, part_rows=part_rows):
            for field in range(3):
                turned = pltpu.roll(
                    fix[part_rows], lax.rem(target + LANES - field, LANES), 1
                )
                rate[slot, field, part_rows, pl.ds(begin, LANES)] += jnp.where(
                    lane == target, turned, 0.0
                )

        wet_now = flag(ctl, WET + 2 * step + slot)

        def group(index, best, slot=slot, wet_now=wet_now):
            rows = pl.ds(pl.multiple_of(index * ROWS, ROWS), ROWS)
            h0, hu0, hv0 = (state[slot, field, rows, :] for field in range(3))
            h = h0 - delta * rate[slot, 0, rows, :]
            hu = hu0 - delta * rate[slot, 1, rows, :]
            hv = hv0 - delta * rate[slot, 2, rows, :]
            rough = manning[slot, rows, :]
            inverse = 1.0 / h
            u = hu * inverse
            v = hv * inverse
            speed = jnp.sqrt(u * u + v * v)
            power = jnp.exp((-4.0 / 3.0) * jnp.log(jnp.abs(h)))
            drag = (GRAVITY * delta) * (rough * rough) * (speed * power)
            factor = 1.0 / (1.0 + drag)
            hu = hu * factor
            hv = hv * factor
            h = jnp.where(wet_now, h, h0)
            hu = jnp.where(wet_now, hu, hu0)
            hv = jnp.where(wet_now, hv, hv0)
            fresh[slot, 0, rows, :] = h
            fresh[slot, 1, rows, :] = hu
            fresh[slot, 2, rows, :] = hv
            if more:
                along_x, along_y = cell(h, hu, hv)
                best = jnp.maximum(best, jnp.maximum(along_x[5], along_y[5]))
            return best

        best = lax.fori_loop(
            part_rows.start // ROWS,
            part_rows.stop // ROWS,
            group,
            jnp.zeros((ROWS, TILE), jnp.float32),
        )
        if more:
            best = jnp.where(flag(ctl, WET + 2 * step + 2 + slot), best, 0.0)
            total = jnp.maximum(total, best)
        outgoing += start_all(
            ((fresh.at[slot, :, part_rows], fresh_out.at[slot, :, part_rows]),), sems, 12 + index
        )
    if more:
        messages(ctl, fresh, None, jnp.max(total, keepdims=True), out, columns_out)
    else:
        outgoing += start_all(((fresh.at[ctl[MOVE]], leaving),), sems, 16)
    wait_all(outgoing)


def second_leaving(ctl, state, arrived, leaving, sems):
    again = ctl[MOVE] == ctl[MOVE + 1]

    @pl.when(again)
    def _():
        pltpu.make_async_copy(arrived, leaving, sems.at[0]).start()

    @pl.when(jnp.logical_not(again))
    def _():
        pltpu.make_async_copy(state.at[1 - ctl[MOVE]], leaving, sems.at[0]).start()

    pltpu.make_async_copy(arrived, leaving, sems.at[0]).wait()


def keep_rest(ctl, state, arrived, out, sems):
    rest = out.at[1 - ctl[MOVE + 1]]
    again = ctl[MOVE] == ctl[MOVE + 1]

    @pl.when(again)
    def _():
        pltpu.make_async_copy(state.at[1 - ctl[MOVE]], rest, sems.at[0]).start()

    @pl.when(jnp.logical_not(again))
    def _():
        pltpu.make_async_copy(arrived, rest, sems.at[0]).start()

    pltpu.make_async_copy(arrived, rest, sems.at[0]).wait()


def keep_last(ctl, arrived, before, out, sems):
    del before
    copy = pltpu.make_async_copy(arrived, out.at[ctl[MOVE + 1]], sems.at[0])
    copy.start()
    copy.wait()


def vmem():
    return pl.BlockSpec(memory_space=pltpu.VMEM)


def smem():
    return pl.BlockSpec(memory_space=pltpu.SMEM)


def hbm():
    return pl.BlockSpec(memory_space=pltpu.HBM)


def anywhere():
    return pl.BlockSpec(memory_space=pl.ANY)


def call(kernel, outs, out_specs, in_specs, flops, scratch=(), aliases=None, room=VMEM_BYTES):
    return pl.pallas_call(
        kernel,
        scratch_shapes=scratch,
        input_output_aliases=aliases or {},
        out_shape=outs,
        in_specs=in_specs,
        out_specs=out_specs,
        compiler_params=pltpu.CompilerParams(vmem_limit_bytes=room),
        cost_estimate=pl.CostEstimate(flops=flops, bytes_accessed=4 << 20, transcendentals=0),
    )


def f32(*shape):
    return jax.ShapeDtypeStruct(shape, jnp.float32)


def spread(fast):
    return lax.all_to_all(fast, ("xb", "yb"), split_axis=0, concat_axis=0, tiled=True)


def body(state, bed, manning, neighbours, wet, moves):
    shape = f32(*state.shape)
    tile_shape = f32(*state.shape[1:])
    devices = lax.axis_size("xb") * lax.axis_size("yb")
    sem = [pltpu.SemaphoreType.DMA((1,))]
    whole = pltpu.VMEM(state.shape, jnp.float32)
    part = pltpu.VMEM(bed.shape, jnp.float32)
    out, columns, ctl = call(
        opening,
        (
            f32(16 * devices, TILE),
            f32(8, TILE),
            jax.ShapeDtypeStruct((CONTROLS,), jnp.int32),
        ),
        (vmem(), vmem(), smem()),
        [hbm()] * 5,
        4 << 20,
        [
            whole,
            part,
            pltpu.SMEM(neighbours.shape[::-1], jnp.int32),
            pltpu.SMEM(wet.shape, jnp.int32),
            pltpu.SMEM(moves.shape, jnp.int32),
            pltpu.SemaphoreType.DMA((6,)),
        ],
    )(state, bed, neighbours.T, wet, moves)
    ground = None
    for step in range(STEPS):
        got = spread(out)
        ground = got if step == 0 else ground
        rate = call(
            rates,
            shape,
            hbm(),
            [smem(), hbm(), hbm()],
            16 << 20,
            [whole, part, whole, pltpu.SemaphoreType.DMA((3 * CHUNKS,))],
        )(ctl, state, bed)
        more = step + 1 < STEPS
        extra = (f32(8 * devices, TILE), f32(8, TILE)) if more else (tile_shape,)
        outs = call(
            functools.partial(update, step),
            (shape,) + extra,
            (hbm(), vmem(), vmem()) if more else (hbm(), hbm()),
            [smem(), vmem(), vmem(), vmem(), hbm(), hbm(), hbm()],
            8 << 20,
            [whole, part, whole, whole, pltpu.SemaphoreType.DMA((17,))],
        )(ctl, got, ground, columns, state, manning, rate)
        state = outs[0]
        if more:
            _, out, columns = outs
    arrived = shifted(outs[1], "xb", 1)
    leaving = call(
        second_leaving, tile_shape, anywhere(), [smem(), anywhere(), anywhere()], 1 << 20, sem, room=1 << 20
    )(ctl, state, arrived)
    arrived_next = shifted(leaving, "xb", 1)
    final = call(
        keep_rest, shape, anywhere(), [smem(), anywhere(), anywhere()], 1 << 20, sem, room=1 << 20
    )(ctl, state, arrived)
    return call(
        keep_last, shape, anywhere(), [smem(), anywhere(), anywhere()], 1 << 20, sem, {2: 0}, 1 << 20
    )(ctl, arrived_next, final)


def solution(mesh):
    placed = (
        P(("runs", "xb", "yb"), None, None, None),
        P(("runs", "xb", "yb"), None, None),
        P(("runs", "xb", "yb"), None, None),
        P("runs", None),
        P(None, "runs"),
        P(None, "runs"),
    )
    return jax.shard_map(
        body,
        mesh=mesh,
        in_specs=placed,
        out_specs=P(("runs", "xb", "yb"), None, None, None),
        check_vma=False,
    )
```

```python
import functools

import jax
import jax.numpy as jnp
from jax import lax
from jax.experimental import pallas as pl
from jax.experimental.pallas import tpu as pltpu
from jax.sharding import PartitionSpec as P

STEPS = 3
GRAVITY = 9.81
ROOT_G = GRAVITY**0.5
SPACING = 5.0
COURANT = 0.2
ROWS = 32
LANES = 128
TILE = 256
VMEM_BYTES = 60 * 1024 * 1024
SLOT_LOW, WALL_WEST, WALL_EAST, WALL_OUTER, WET, MOVE = 0, 1, 3, 5, 7, 13
WET_FIRST, WET_SECOND = 16, 19
CONTROLS = 24
EARLY = 192
LATE = TILE - EARLY + 16
CHUNKS = 4
TOP = 6
SCALE = 0.5 / SPACING
SLOPE = GRAVITY / (2.0 * SPACING)


def shifted(value, axis, steps, around=True):
    count = lax.axis_size(axis)
    pairs = [(source, (source + steps) % count) for source in range(count)]
    if not around:
        pairs = [pair for pair in pairs if abs(pair[0] - pair[1]) == abs(steps)]
    return lax.ppermute(value, axis, pairs)


def cell(h, hu, hv):
    root = lax.rsqrt(h)
    inverse = root * root
    u = hu * inverse
    v = hv * inverse
    celerity = ROOT_G * (h * root)
    pressure = (0.5 * GRAVITY) * (h * h)
    cross = hu * v
    speed_x = jnp.abs(u) + celerity
    speed_y = jnp.abs(v) + celerity
    along_x = (h, hu, hv, hu * u + pressure, cross, speed_x)
    along_y = (h, hv, hu, hv * v + pressure, cross, speed_y)
    return along_x, along_y


def face(left, right):
    wave = jnp.maximum(left[5], right[5])
    return (
        (left[1] + right[1]) - wave * (right[0] - left[0]),
        (left[3] + right[3]) - wave * (right[1] - left[1]),
        (left[4] + right[4]) - wave * (right[2] - left[2]),
    )


def slot_of(ctl, position):
    low = ctl[SLOT_LOW]
    return low if position == 0 else 1 - low


def flag(ctl, index):
    return ctl[index] > 0


def start_all(pairs, sems, first=0):
    copies = [
        pltpu.make_async_copy(src, dst, sems.at[first + k]) for k, (src, dst) in enumerate(pairs)
    ]
    for copy in copies:
        copy.start()
    return copies


def wait_all(copies):
    for copy in copies:
        copy.wait()


def sublanes(width=TILE):
    return lax.broadcasted_iota(jnp.int32, (8, width), 0)


def stacked(lines, base):
    row = sublanes()
    for index, line in enumerate(lines):
        base = jnp.where(row == index, jnp.broadcast_to(line, (8, TILE)), base)
    return base


def messages(ctl, state, bed, fastest, out, columns):
    upper = lax.axis_index("yb")
    column = lax.axis_index("xb")
    last = lax.axis_size("xb") - 1
    devices = 2 * (last + 1)
    block = out.shape[0] // devices
    device = column * 2 + upper
    top = jnp.broadcast_to(fastest, (8, TILE))
    for peer in range(devices):
        out[peer * block : peer * block + 8, :] = top
    row = sublanes()

    def edge(line):
        rows = slice(line, line + 1)
        slots = [slot_of(ctl, position) for position in range(2)]
        fields = [state[slot, field, rows, :] for slot in slots for field in range(3)]
        return stacked(fields, top), [bed[slot, rows, :] for slot in slots] if bed is not None else None

    for inside, peer, line in (
        (column > 0, device - 2, 0),
        (column < last, device + 2, TILE - 1),
    ):

        @pl.when(inside)
        def _(peer=peer, line=line):
            lines, ground = edge(line)
            start = pl.multiple_of(peer * block, 8)
            out[pl.ds(start, 8), :] = lines
            if ground:
                out[pl.ds(pl.multiple_of(start + 8, 8), 8), :] = stacked(ground, top)

    slot = jnp.where(upper > 0, ctl[SLOT_LOW], 1 - ctl[SLOT_LOW])
    begin = pl.multiple_of((1 - upper) * LANES, LANES)
    lane = lax.broadcasted_iota(jnp.int32, (TILE, LANES), 1)
    packed = None
    for field in range(4 if bed is not None else 3):
        if field < 3:
            part = state[slot, field, :, pl.ds(begin, LANES)]
        else:
            part = bed[slot, :, pl.ds(begin, LANES)]
        turned = pltpu.roll(part, field + 1 - upper, 1)
        packed = turned if field == 0 else jnp.where(lane == field, turned, packed)
    lines = jnp.transpose(packed)[:8]
    columns[...] = lines
    start = pl.multiple_of((device + 1 - 2 * upper) * block, 8)
    out[pl.ds(start, 8), :] = jnp.where(row == TOP, top, lines)


def opening(
    state_in, bed_in, manning_in, neighbours_in, wet_in, moves_in,
    out, columns, ctl, leaving,
    state, bed, neighbours, wet, moves, sems,
):
    copies = start_all(
        (
            (neighbours_in, neighbours),
            (wet_in, wet),
            (moves_in, moves),
            (state_in.at[0], state.at[0]),
            (state_in.at[1], state.at[1]),
            (bed_in, bed),
        ),
        sems,
    )
    device = lax.axis_index("xb") * 2 + lax.axis_index("yb")
    wait_all(copies[:3])
    first = device * 2
    low = jnp.where(neighbours[3, first] == first + 1, 0, 1)
    ctl[SLOT_LOW] = low
    for position in range(2):
        slot = low if position == 0 else 1 - low
        tile = first + slot
        ctl[WALL_WEST + position] = (neighbours[0, tile] < 0).astype(jnp.int32)
        ctl[WALL_EAST + position] = (neighbours[1, tile] < 0).astype(jnp.int32)
        ctl[WALL_OUTER + position] = (neighbours[2 + position, tile] < 0).astype(jnp.int32)
    for step in range(STEPS):
        for slot in range(2):
            ctl[WET + 2 * step + slot] = wet[step, first + slot]
        ctl[MOVE + step] = moves[step, device]
    early = early_copies(moves[0, device], state_in, bed_in, manning_in, leaving, sems, 6)
    for copy in early:
        copy.start()
    count = lax.axis_size("xb")
    upper = lax.axis_index("yb")
    column = lax.axis_index("xb")
    source = lax.rem(column + count - 1, count) * 2 + upper
    before = lax.rem(column + count - 2, count) * 2 + upper
    again = moves[0, source] == moves[1, source]
    tile_first = source * 2 + moves[0, source]
    tile_second = jnp.where(
        again, before * 2 + moves[0, before], source * 2 + 1 - moves[0, source]
    )
    for step in range(STEPS):
        ctl[WET_FIRST + step] = wet[step, tile_first]
        ctl[WET_SECOND + step] = wet[step, tile_second]

    total = jnp.zeros((ROWS, TILE), jnp.float32)
    for slot in range(2):
        copies[3 + slot].wait()

        def group(index, best, slot=slot):
            rows = pl.ds(pl.multiple_of(index * ROWS, ROWS), ROWS)
            along_x, along_y = cell(*(state[slot, field, rows, :] for field in range(3)))
            return jnp.maximum(best, jnp.maximum(along_x[5], along_y[5]))

        best = lax.fori_loop(0, TILE // ROWS, group, jnp.zeros((ROWS, TILE), jnp.float32))
        total = jnp.maximum(total, jnp.where(wet[0, first + slot] > 0, best, 0.0))
    copies[5].wait()
    messages(ctl, state, bed, jnp.max(total, keepdims=True), out, columns)
    wait_all(early)


def early_copies(slot, state_in, bed_in, manning_in, leaving, sems, first):
    rows = slice(0, EARLY)
    pairs = (
        (state_in.at[slot, :, rows], leaving.at[0:3]),
        (bed_in.at[slot, rows], leaving.at[3]),
        (manning_in.at[slot, rows], leaving.at[4]),
    )
    return [
        pltpu.make_async_copy(src, dst, sems.at[first + k]) for k, (src, dst) in enumerate(pairs)
    ]


def rates_and_leaving(
    ctl, state_in, bed_in, state_first, manning_in, arrived, rate_out, leaving,
    state, bed, rate, sems, moving,
):
    again = ctl[MOVE] == ctl[MOVE + 1]
    passed = pltpu.make_async_copy(arrived, leaving, moving.at[0])
    own = early_copies(1 - ctl[MOVE], state_first, bed_in, manning_in, leaving, moving, 1)

    @pl.when(again)
    def _():
        passed.start()

    @pl.when(jnp.logical_not(again))
    def _():
        for copy in own:
            copy.start()

    rates(ctl, state_in, bed_in, rate_out, state, bed, rate, sems)

    @pl.when(again)
    def _():
        passed.wait()

    @pl.when(jnp.logical_not(again))
    def _():
        wait_all(own)


def rates(ctl, state_in, bed_in, rate_out, state, bed, rate, sems):
    row_ids = lax.broadcasted_iota(jnp.int32, (ROWS, TILE), 0)
    lane = lax.broadcasted_iota(jnp.int32, (ROWS, LANES), 1)
    row8 = sublanes()
    last = TILE // ROWS - 1
    chunk = TILE // CHUNKS
    incoming = []
    for part in range(CHUNKS):
        rows = slice(part * chunk, (part + 1) * chunk)
        incoming.append(
            start_all(
                (
                    (state_in.at[:, :, rows], state.at[:, :, rows]),
                    (bed_in.at[:, rows], bed.at[:, rows]),
                ),
                sems,
                2 * part,
            )
        )
    wait_all(incoming[0])
    outgoing = []

    def field_ref(which, field):
        return bed.at[which] if field == 3 else state.at[which, field]

    def opening_faces(position):
        slot = slot_of(ctl, position)
        keep = jnp.where(flag(ctl, WALL_WEST + position), 1.0, 0.0)
        first = [field_ref(slot, field)[0:8, :] for field in range(4)]
        right, _ = cell(*first[:3])
        left, _ = cell(first[0], -first[1], first[2])
        return tuple(keep * part[0:1, :] for part in face(left, right)) + (keep * first[3][0:1, :],)

    def group_of(position):
        slot = slot_of(ctl, position)
        other = 1 - slot
        keep_outer = jnp.where(flag(ctl, WALL_OUTER + position), 1.0, 0.0)
        keep_east = jnp.where(flag(ctl, WALL_EAST + position), 1.0, 0.0)
        inner_lane = LANES - 1 if position == 0 else 0
        outer_lane = LANES - 1 - inner_lane
        inner_cols = slice(0, LANES) if position == 0 else slice(LANES, TILE)
        inner_turn = LANES - 1 if position == 0 else 1

        def group(index, carry):
            base = pl.multiple_of(index * ROWS, ROWS)
            rows = pl.ds(base, ROWS)
            after = pl.ds(pl.multiple_of(jnp.minimum(base + ROWS, TILE - 8), 8), 8)
            at_end = index == last
            fields = []
            for field in range(4):
                ref = field_ref(slot, field)
                block = ref[rows, :]
                mirrored = jnp.broadcast_to(block[ROWS - 1 : ROWS], (8, TILE))
                if field == 1:
                    mirrored = -mirrored
                if field == 3:
                    mirrored = keep_east * mirrored
                fields.append(
                    jnp.concatenate([block, jnp.where(at_end, mirrored, ref[after, :])], 0)
                )
            cells_x, cells_y = cell(*fields[:3])

            def down(value):
                return pltpu.roll(value, ROWS + 7, 0)[:ROWS]

            here = tuple(value[:ROWS] for value in cells_x)
            keep = jnp.where(row8 == 7, jnp.where(at_end, keep_east, 1.0), 1.0)
            faces = tuple(
                jnp.concatenate([value[: ROWS - 8], value[ROWS - 8 :] * keep], 0)
                for value in face(here, tuple(down(value) for value in cells_x))
            )
            turned = tuple(pltpu.roll(value, 1, 0) for value in faces)
            change_x = tuple(
                value - jnp.where(row_ids == 0, before, moved)
                for value, before, moved in zip(faces, carry[:3], turned)
            )
            ground = fields[3][:ROWS]
            ground_up = pltpu.roll(ground, 1, 0)
            slope_x = down(fields[3]) - jnp.where(row_ids == 0, carry[3], ground_up)
            carried = tuple(value[0:1, :] for value in turned) + (ground_up[0:1, :],)

            ghosts = []
            for field in range(4):
                inner = pltpu.roll(field_ref(other, field)[rows, inner_cols], inner_turn, 1)
                own = fields[field][:ROWS, inner_cols]
                if field == 2:
                    own = -own
                if field == 3:
                    own = keep_outer * own
                ghosts.append(jnp.where(lane == inner_lane, inner, own))
            _, ghost_y = cell(*ghosts[:3])
            low = tuple(value[:ROWS, :LANES] for value in cells_y)
            high = tuple(value[:ROWS, LANES:] for value in cells_y)

            def right_of(low_part, high_part, ghost_part):
                turned_low = pltpu.roll(low_part, LANES - 1, 1)
                turned_high = pltpu.roll(high_part, LANES - 1, 1)
                return (
                    jnp.where(lane == LANES - 1, turned_high, turned_low),
                    jnp.where(lane == LANES - 1, ghost_part, turned_high),
                )

            pairs = [right_of(a, b, c) for a, b, c in zip(low, high, ghost_y)]
            faces_low = face(low, tuple(pair[0] for pair in pairs))
            faces_high = face(high, tuple(pair[1] for pair in pairs))
            faces_edge = face(ghost_y, low)
            if position == 0:
                faces_edge = tuple(keep_outer * value for value in faces_edge)
            else:
                keep_lane = jnp.where(lane == outer_lane, keep_outer, 1.0)
                faces_high = tuple(keep_lane * value for value in faces_high)
            change_y = []
            for a, b, c in zip(faces_low, faces_high, faces_edge):
                turned_a = pltpu.roll(a, 1, 1)
                turned_b = pltpu.roll(b, 1, 1)
                change_y.append(
                    jnp.concatenate(
                        [
                            a - jnp.where(lane == 0, c, turned_a),
                            b - jnp.where(lane == 0, turned_a, turned_b),
                        ],
                        1,
                    )
                )
            ground_low = ground[:, :LANES]
            ground_high = ground[:, LANES:]
            north = right_of(ground_low, ground_high, ghosts[3])
            turned_low = pltpu.roll(ground_low, 1, 1)
            turned_high = pltpu.roll(ground_high, 1, 1)
            slope_y = jnp.concatenate(
                [
                    north[0] - jnp.where(lane == 0, ghosts[3], turned_low),
                    north[1] - jnp.where(lane == 0, turned_low, turned_high),
                ],
                1,
            )
            weight = SLOPE * fields[0][:ROWS]
            rate[slot, 0, rows, :] = SCALE * (change_x[0] + change_y[0])
            rate[slot, 1, rows, :] = SCALE * (change_x[1] + change_y[2]) + weight * slope_x
            rate[slot, 2, rows, :] = SCALE * (change_x[2] + change_y[1]) + weight * slope_y
            return carried

        return group

    carries = [opening_faces(position) for position in range(2)]
    groups = [group_of(position) for position in range(2)]
    per_chunk = chunk // ROWS
    for part in range(CHUNKS):
        if part + 1 < CHUNKS:
            wait_all(incoming[part + 1])
        for position in range(2):
            carries[position] = lax.fori_loop(
                part * per_chunk, (part + 1) * per_chunk, groups[position], carries[position]
            )
        rows = slice(part * chunk, (part + 1) * chunk)
        outgoing += start_all(
            ((rate.at[:, :, rows], rate_out.at[:, :, rows]),), sems, 2 * CHUNKS + part
        )
    wait_all(outgoing)


def moved_on(old, slopes, rough, delta, wet_now):
    h, hu, hv = (value - delta * slope for value, slope in zip(old, slopes))
    inverse = 1.0 / h
    u = hu * inverse
    v = hv * inverse
    speed = jnp.sqrt(u * u + v * v)
    power = jnp.exp((-4.0 / 3.0) * jnp.log(jnp.abs(h)))
    drag = (GRAVITY * delta) * (rough * rough) * (speed * power)
    factor = 1.0 / (1.0 + drag)
    fresh = (h, hu * factor, hv * factor)
    return tuple(jnp.where(wet_now, new, value) for new, value in zip(fresh, old))


def repeat_steps(ctl, wet_from, deltas, early, work, other, sems):
    chunk = EARLY // 3
    incoming = []
    for part in range(3):
        rows = slice(part * chunk, (part + 1) * chunk)
        incoming += start_all(((early.at[:, rows], work.at[:, rows]),), sems, part)
    row_ids = lax.broadcasted_iota(jnp.int32, (ROWS, TILE), 0)
    lane = lax.broadcasted_iota(jnp.int32, (ROWS, LANES), 1)
    start = tuple(jnp.zeros((1, TILE), jnp.float32) for _ in range(4))

    def halves(value):
        return value[:, :LANES], value[:, LANES:]

    def right_of(value):
        low, high = (pltpu.roll(part, LANES - 1, 1) for part in halves(value))
        return jnp.concatenate([jnp.where(lane == LANES - 1, high, low), high], 1)

    def left_of(value):
        low, high = (pltpu.roll(part, 1, 1) for part in halves(value))
        return jnp.concatenate([low, jnp.where(lane == 0, low, high)], 1)

    def down(value):
        return pltpu.roll(value, ROWS + 7, 0)[:ROWS]

    for step in range(STEPS):
        source, target = (work, other) if step % 2 == 0 else (other, work)
        delta = deltas[step][0:1, :]
        wet_now = flag(ctl, wet_from + step)

        def group(index, carry, source=source, target=target, delta=delta, wet_now=wet_now):
            base = pl.multiple_of(index * ROWS, ROWS)
            rows = pl.ds(base, ROWS)
            after = pl.ds(pl.multiple_of(jnp.minimum(base + ROWS, EARLY - 8), 8), 8)
            refs = [source.at[field] for field in range(3)] + [work.at[3]]
            fields = [jnp.concatenate([ref[rows, :], ref[after, :]], 0) for ref in refs]
            cells_x, cells_y = cell(*fields[:3])
            here_x = tuple(value[:ROWS] for value in cells_x)
            here_y = tuple(value[:ROWS] for value in cells_y)
            faces_x = face(here_x, tuple(down(value) for value in cells_x))
            turned = tuple(pltpu.roll(value, 1, 0) for value in faces_x)
            change_x = tuple(
                value - jnp.where(row_ids == 0, before, moved)
                for value, before, moved in zip(faces_x, carry[:3], turned)
            )
            ground = fields[3][:ROWS]
            ground_up = pltpu.roll(ground, 1, 0)
            slope_x = down(fields[3]) - jnp.where(row_ids == 0, carry[3], ground_up)
            carried = tuple(value[0:1, :] for value in turned) + (ground_up[0:1, :],)
            faces_y = face(here_y, tuple(right_of(value) for value in here_y))
            change_y = tuple(value - left_of(value) for value in faces_y)
            slope_y = right_of(ground) - left_of(ground)
            old = tuple(value[:ROWS] for value in fields[:3])
            weight = SLOPE * old[0]
            slopes = (
                SCALE * (change_x[0] + change_y[0]),
                SCALE * (change_x[1] + change_y[2]) + weight * slope_x,
                SCALE * (change_x[2] + change_y[1]) + weight * slope_y,
            )
            for field, value in enumerate(
                moved_on(old, slopes, work[4, rows, :], delta, wet_now)
            ):
                target[field, rows, :] = value
            return carried

        per_chunk = chunk // ROWS
        if step == 0:
            carry = start
            incoming[0].wait()
            for part in range(3):
                if part < 2:
                    incoming[part + 1].wait()
                carry = lax.fori_loop(part * per_chunk, (part + 1) * per_chunk, group, carry)
        else:
            lax.fori_loop(0, EARLY // ROWS, group, start)


def late_rows(tile, late):
    row = sublanes()
    kept = EARLY - 8
    lane = lax.broadcasted_iota(jnp.int32, (8, LANES), 1)
    for field in range(3):
        late[field, 0:8, :] = jnp.where(
            row < 3, tile[field, 0:8, :], tile[field, kept : kept + 8, :]
        )
        late[field, 8 : TILE - kept, :] = tile[field, kept + 8 :, :]
        packed = [None, None]
        for block in range(EARLY // 8):
            rows = slice(8 * block, 8 * block + 8)
            sides = jnp.where(lane < 64, tile[field, rows, :LANES], tile[field, rows, LANES:])
            turned = pltpu.roll(sides, (3 + 8 * block) % LANES, 1)
            which = block // 16
            packed[which] = (
                turned
                if packed[which] is None
                else jnp.where(lane // 8 == block % 16, turned, packed[which])
            )
        late[field, TILE - kept :, :] = jnp.concatenate(packed, 1)


def merge(late, early, tile):
    row = sublanes()
    kept = EARLY - 8
    lane = lax.broadcasted_iota(jnp.int32, (8, LANES), 1)
    for field in range(3):
        first = late[field, 0:8, :]
        for block in range(EARLY // 8):
            rows = slice(8 * block, 8 * block + 8)
            which = block // 16
            packed = late[field, TILE - kept :, which * LANES : (which + 1) * LANES]
            sides = pltpu.roll(packed, (-3 - 8 * block) % LANES, 1)
            value = early[field, rows, :]
            value = jnp.concatenate(
                [
                    jnp.where(lane < 3, sides, value[:, :LANES]),
                    jnp.where(lane >= LANES - 3, sides, value[:, LANES:]),
                ],
                1,
            )
            if block == 0:
                value = jnp.where(row < 3, first, value)
            if block == EARLY // 8 - 1:
                value = jnp.where(row < 5, value, first)
            tile[field, rows, :] = value
        tile[field, EARLY:, :] = late[field, 8 : TILE - kept, :]


def repeat_second(ctl, delta0, delta1, delta2, early, tile, work, sems):
    repeat_steps(ctl, WET_SECOND, (delta0, delta1, delta2), early, work, tile, sems)


def repeat_first(
    ctl, delta0, delta1, delta2, early, late, staying, out, work, other, tile, sems
):
    rest = out.at[1 - ctl[MOVE + 1]]
    again = ctl[MOVE] == ctl[MOVE + 1]

    @pl.when(again)
    def _():
        copy = pltpu.make_async_copy(staying, rest, sems.at[3])
        copy.start()
        copy.wait()

    @pl.when(jnp.logical_not(again))
    def _():
        repeat_steps(ctl, WET_FIRST, (delta0, delta1, delta2), early, work, other, sems)
        merge(late, other, tile)
        copy = pltpu.make_async_copy(tile, rest, sems.at[3])
        copy.start()
        copy.wait()


def finish(ctl, late, early, before, out, tile, sems):
    del before
    merge(late, early, tile)
    copy = pltpu.make_async_copy(tile, out.at[ctl[MOVE + 1]], sems.at[0])
    copy.start()
    copy.wait()


def second_late(ctl, arrived, own, leaving, sems):
    again = ctl[MOVE] == ctl[MOVE + 1]

    @pl.when(again)
    def _():
        pltpu.make_async_copy(arrived, leaving, sems.at[0]).start()

    @pl.when(jnp.logical_not(again))
    def _():
        pltpu.make_async_copy(own, leaving, sems.at[0]).start()

    pltpu.make_async_copy(arrived, leaving, sems.at[0]).wait()


def correct_rows(ctl, slot, got, ground, block, state, rate, bottom):
    position = jnp.where(ctl[SLOT_LOW] == slot, 0, 1)
    device = lax.axis_index("xb") * 2 + lax.axis_index("yb")
    wall = WALL_WEST if bottom else WALL_EAST

    @pl.when(jnp.logical_not(flag(ctl, wall + position)))
    def _():
        peer = device - 2 if bottom else device + 2
        lines = got[pl.ds(pl.multiple_of(peer * block, 8), 8), :]
        grounds = ground[pl.ds(pl.multiple_of(peer * 16 + 8, 8), 8), :]

        def line(value, offset):
            picked = jnp.where(
                position == 0, value[offset : offset + 1, :], value[offset + 3 : offset + 4, :]
            )
            return jnp.broadcast_to(picked, (8, TILE))

        ghost, _ = cell(*(line(lines, field) for field in range(3)))
        ghost_ground = jnp.where(position == 0, grounds[0:1, :], grounds[1:2, :])
        rows = slice(0, 8) if bottom else slice(TILE - 8, TILE)
        own = [state[slot, field, rows, :] for field in range(3)]
        here, _ = cell(*own)
        fluxes = face(ghost, here) if bottom else face(here, ghost)
        push = SCALE * fluxes[1] + (SLOPE * own[0]) * ghost_ground
        row = sublanes()
        sign = -1.0 if bottom else 1.0
        chosen = row == (0 if bottom else 7)
        for field, value in enumerate((SCALE * fluxes[0], push, SCALE * fluxes[2])):
            rate[slot, field, rows, :] += jnp.where(chosen, sign * value, 0.0)


def column_fix(got, ground, block, columns, bed_columns):
    upper = lax.axis_index("yb")
    device = lax.axis_index("xb") * 2 + upper
    peer = device + 1 - 2 * upper
    lines = got[pl.ds(pl.multiple_of(peer * block, 8), 8), :]
    ghost_ground = ground[pl.ds(pl.multiple_of(peer * 16, 8), 8), :][3:4]
    del bed_columns
    mine = columns[...]
    _, ghost = cell(lines[0:1], lines[1:2], lines[2:3])
    _, own = cell(mine[0:1], mine[1:2], mine[2:3])
    low = upper == 0
    left = tuple(jnp.where(low, a, b) for a, b in zip(own, ghost))
    right = tuple(jnp.where(low, b, a) for a, b in zip(own, ghost))
    fluxes = face(left, right)
    sign = jnp.where(low, 1.0, -1.0)
    push = SCALE * fluxes[1] + (SLOPE * mine[0:1]) * ghost_ground
    block8 = stacked(
        [sign * SCALE * fluxes[0], sign * SCALE * fluxes[2], sign * push],
        jnp.zeros((8, TILE), jnp.float32),
    )
    return jnp.transpose(
        jnp.concatenate([block8, jnp.zeros((LANES - 8, TILE), jnp.float32)], 0)
    )


def update(step, ctl, got, ground, columns, state_in, manning_in, rate_in, *rest):
    more = step + 1 < STEPS
    if more:
        fresh_out, out, columns_out, delta_out = rest[:4]
        rest = rest[4:]
    else:
        staying, late_first, late_second, delta_out = rest[:4]
        rest = rest[4:]
    state, manning, rate, fresh, sems = rest
    half = TILE // 2
    parts = [(slot, slice(k * half, (k + 1) * half)) for slot in range(2) for k in range(2)]
    incoming = []
    for index, (slot, rows) in enumerate(parts):
        incoming.append(
            start_all(
                (
                    (rate_in.at[slot, :, rows], rate.at[slot, :, rows]),
                    (state_in.at[slot, :, rows], state.at[slot, :, rows]),
                    (manning_in.at[slot, rows], manning.at[slot, rows]),
                ),
                sems,
                3 * index,
            )
        )
    upper = lax.axis_index("yb")
    devices = 2 * lax.axis_size("xb")
    block = got.shape[0] // devices
    tops = got[0:8, :]
    for peer in range(1, devices):
        tops = jnp.maximum(tops, got[peer * block : peer * block + 8, :])
    delta = (COURANT * SPACING) / tops[TOP : TOP + 1, :]
    delta_out[...] = jnp.broadcast_to(delta, (8, TILE))
    fix = column_fix(got, ground, block, columns, None)
    facing = jnp.where(upper > 0, ctl[SLOT_LOW], 1 - ctl[SLOT_LOW])
    begin = pl.multiple_of((1 - upper) * LANES, LANES)
    target = (1 - upper) * (LANES - 1)
    lane = lax.broadcasted_iota(jnp.int32, (half, LANES), 1)
    total = jnp.zeros((ROWS, TILE), jnp.float32)
    outgoing = []
    for index, (slot, part_rows) in enumerate(parts):
        wait_all(incoming[index])
        bottom = index % 2 == 0
        correct_rows(ctl, slot, got, ground, block, state, rate, bottom)

        @pl.when(facing == slot)
        def _(slot=slot, part_rows=part_rows):
            for field in range(3):
                turned = pltpu.roll(
                    fix[part_rows], lax.rem(target + LANES - field, LANES), 1
                )
                rate[slot, field, part_rows, pl.ds(begin, LANES)] += jnp.where(
                    lane == target, turned, 0.0
                )

        wet_now = flag(ctl, WET + 2 * step + slot)

        def group(index, best, slot=slot, wet_now=wet_now):
            rows = pl.ds(pl.multiple_of(index * ROWS, ROWS), ROWS)
            old = tuple(state[slot, field, rows, :] for field in range(3))
            slopes = tuple(rate[slot, field, rows, :] for field in range(3))
            h, hu, hv = moved_on(old, slopes, manning[slot, rows, :], delta, wet_now)
            fresh[slot, 0, rows, :] = h
            fresh[slot, 1, rows, :] = hu
            fresh[slot, 2, rows, :] = hv
            if more:
                along_x, along_y = cell(h, hu, hv)
                best = jnp.maximum(best, jnp.maximum(along_x[5], along_y[5]))
            return best

        best = lax.fori_loop(
            part_rows.start // ROWS,
            part_rows.stop // ROWS,
            group,
            jnp.zeros((ROWS, TILE), jnp.float32),
        )
        if more:
            best = jnp.where(flag(ctl, WET + 2 * step + 2 + slot), best, 0.0)
            total = jnp.maximum(total, best)
        if more:
            outgoing += start_all(
                ((fresh.at[slot, :, part_rows], fresh_out.at[slot, :, part_rows]),),
                sems,
                12 + index,
            )
    if more:
        messages(ctl, fresh, None, jnp.max(total, keepdims=True), out, columns_out)
    else:
        outgoing += start_all(((fresh.at[1 - ctl[MOVE]], staying),), sems, 16)
        late_rows(fresh.at[ctl[MOVE]], late_first)
        late_rows(fresh.at[1 - ctl[MOVE]], late_second)
    wait_all(outgoing)


def vmem():
    return pl.BlockSpec(memory_space=pltpu.VMEM)


def smem():
    return pl.BlockSpec(memory_space=pltpu.SMEM)


def hbm():
    return pl.BlockSpec(memory_space=pltpu.HBM)


def anywhere():
    return pl.BlockSpec(memory_space=pl.ANY)


def call(kernel, outs, out_specs, in_specs, flops, scratch=(), aliases=None, room=VMEM_BYTES):
    return pl.pallas_call(
        kernel,
        scratch_shapes=scratch,
        input_output_aliases=aliases or {},
        out_shape=outs,
        in_specs=in_specs,
        out_specs=out_specs,
        compiler_params=pltpu.CompilerParams(vmem_limit_bytes=room),
        cost_estimate=pl.CostEstimate(flops=flops, bytes_accessed=4 << 20, transcendentals=0),
    )


def f32(*shape):
    return jax.ShapeDtypeStruct(shape, jnp.float32)


def spread(fast):
    return lax.all_to_all(fast, ("xb", "yb"), split_axis=0, concat_axis=0, tiled=True)


def body(state, bed, manning, neighbours, wet, moves):
    shape = f32(*state.shape)
    tile_shape = f32(*state.shape[1:])
    devices = lax.axis_size("xb") * lax.axis_size("yb")
    sem = [pltpu.SemaphoreType.DMA((1,))]
    whole = pltpu.VMEM(state.shape, jnp.float32)
    part = pltpu.VMEM(bed.shape, jnp.float32)
    early_shape = f32(5, EARLY, TILE)
    late_shape = f32(3, LATE, TILE)
    delta_shape = f32(8, TILE)
    out, columns, ctl, leaving = call(
        opening,
        (
            f32(16 * devices, TILE),
            f32(8, TILE),
            jax.ShapeDtypeStruct((CONTROLS,), jnp.int32),
            early_shape,
        ),
        (vmem(), vmem(), smem(), hbm()),
        [hbm()] * 6,
        4 << 20,
        [
            whole,
            part,
            pltpu.SMEM(neighbours.shape[::-1], jnp.int32),
            pltpu.SMEM(wet.shape, jnp.int32),
            pltpu.SMEM(moves.shape, jnp.int32),
            pltpu.SemaphoreType.DMA((9,)),
        ],
    )(state, bed, manning, neighbours.T, wet, moves)
    early_first = shifted(leaving, "xb", 1)
    state_first = state
    ground = None
    deltas = []
    for step in range(STEPS):
        got = spread(out)
        ground = got if step == 0 else ground
        scratch = [whole, part, whole, pltpu.SemaphoreType.DMA((3 * CHUNKS,))]
        if step == 1:
            rate, leaving = call(
                rates_and_leaving,
                (shape, early_shape),
                (hbm(), hbm()),
                [smem()] + [hbm()] * 5,
                16 << 20,
                scratch + [pltpu.SemaphoreType.DMA((4,))],
            )(ctl, state, bed, state_first, manning, early_first)
            early_second = shifted(leaving, "xb", 1)
        else:
            rate = call(rates, shape, hbm(), [smem(), hbm(), hbm()], 16 << 20, scratch)(
                ctl, state, bed
            )
        if step + 1 < STEPS:
            shapes = (shape, f32(8 * devices, TILE), f32(8, TILE), delta_shape)
            places = (hbm(), vmem(), vmem(), vmem())
        else:
            shapes = (tile_shape, late_shape, late_shape, delta_shape)
            places = (hbm(), vmem(), vmem(), vmem())
        outs = call(
            functools.partial(update, step),
            shapes,
            places,
            [smem(), vmem(), vmem(), vmem(), hbm(), hbm(), hbm()],
            8 << 20,
            [whole, part, whole, whole, pltpu.SemaphoreType.DMA((17,))],
        )(ctl, got, ground, columns, state, manning, rate)
        deltas.append(outs[3])
        if step + 1 < STEPS:
            state, out, columns, _ = outs
    staying, late_first, late_second, _ = outs
    late_arrived = shifted(late_first, "xb", 1)
    small = 8 << 20
    early_work = pltpu.VMEM(early_shape.shape, jnp.float32)
    early_state = f32(3, EARLY, TILE)
    second = call(
        repeat_second,
        early_state,
        vmem(),
        [smem()] + [vmem()] * 3 + [hbm()],
        8 << 20,
        [early_work, pltpu.SemaphoreType.DMA((3,))],
        room=small,
    )(ctl, *deltas, early_second)
    leaving = call(
        second_late, late_shape, anywhere(), [smem(), anywhere(), anywhere()], 1 << 20, sem,
        room=1 << 20,
    )(ctl, late_arrived, late_second)
    late_next = shifted(leaving, "xb", 1)
    final = call(
        repeat_first,
        shape,
        hbm(),
        [smem()] + [vmem()] * 3 + [hbm(), vmem(), hbm()],
        8 << 20,
        [
            early_work,
            pltpu.VMEM(early_state.shape, jnp.float32),
            pltpu.VMEM(tile_shape.shape, jnp.float32),
            pltpu.SemaphoreType.DMA((4,)),
        ],
        room=small,
    )(ctl, *deltas, early_first, late_arrived, staying)
    return call(
        finish,
        shape,
        hbm(),
        [smem(), vmem(), vmem(), hbm()],
        1 << 20,
        [pltpu.VMEM(tile_shape.shape, jnp.float32)] + sem,
        {3: 0},
        room=small,
    )(ctl, late_next, second, final)


def solution(mesh):
    placed = (
        P(("runs", "xb", "yb"), None, None, None),
        P(("runs", "xb", "yb"), None, None),
        P(("runs", "xb", "yb"), None, None),
        P("runs", None),
        P(None, "runs"),
        P(None, "runs"),
    )
    return jax.shard_map(
        body,
        mesh=mesh,
        in_specs=placed,
        out_specs=P(("runs", "xb", "yb"), None, None, None),
        check_vma=False,
    )
```

```python
import functools

import jax
import jax.numpy as jnp
from jax import lax
from jax.experimental import pallas as pl
from jax.experimental.pallas import tpu as pltpu
from jax.sharding import PartitionSpec as P

STEPS = 3
GRAVITY = 9.81
ROOT_G = GRAVITY**0.5
SPACING = 5.0
COURANT = 0.2
ROWS = 32
LANES = 128
TILE = 256
VMEM_BYTES = 60 * 1024 * 1024
SLOT_LOW, WALL_WEST, WALL_EAST, WALL_OUTER, WET, MOVE = 0, 1, 3, 5, 7, 13
WET_FIRST, WET_SECOND = 16, 19
CONTROLS = 24
EARLY = 192
LATE = TILE - EARLY + 16
CHUNKS = 4
TOP = 6
SCALE = 0.5 / SPACING
SLOPE = GRAVITY / (2.0 * SPACING)


def shifted(value, axis, steps, around=True):
    count = lax.axis_size(axis)
    pairs = [(source, (source + steps) % count) for source in range(count)]
    if not around:
        pairs = [pair for pair in pairs if abs(pair[0] - pair[1]) == abs(steps)]
    return lax.ppermute(value, axis, pairs)


def cell(h, hu, hv):
    root = lax.rsqrt(h)
    inverse = root * root
    u = hu * inverse
    v = hv * inverse
    celerity = ROOT_G * (h * root)
    pressure = (0.5 * GRAVITY) * (h * h)
    cross = hu * v
    speed_x = jnp.abs(u) + celerity
    speed_y = jnp.abs(v) + celerity
    along_x = (h, hu, hv, hu * u + pressure, cross, speed_x)
    along_y = (h, hv, hu, hv * v + pressure, cross, speed_y)
    return along_x, along_y


def face(left, right):
    wave = jnp.maximum(left[5], right[5])
    return (
        (left[1] + right[1]) - wave * (right[0] - left[0]),
        (left[3] + right[3]) - wave * (right[1] - left[1]),
        (left[4] + right[4]) - wave * (right[2] - left[2]),
    )


def slot_of(ctl, position):
    low = ctl[SLOT_LOW]
    return low if position == 0 else 1 - low


def flag(ctl, index):
    return ctl[index] > 0


def start_all(pairs, sems, first=0):
    copies = [
        pltpu.make_async_copy(src, dst, sems.at[first + k]) for k, (src, dst) in enumerate(pairs)
    ]
    for copy in copies:
        copy.start()
    return copies


def wait_all(copies):
    for copy in copies:
        copy.wait()


def sublanes(width=TILE):
    return lax.broadcasted_iota(jnp.int32, (8, width), 0)


def stacked(lines, base):
    row = sublanes()
    for index, line in enumerate(lines):
        base = jnp.where(row == index, jnp.broadcast_to(line, (8, TILE)), base)
    return base


def messages(ctl, state, bed, fastest, out, columns):
    upper = lax.axis_index("yb")
    column = lax.axis_index("xb")
    last = lax.axis_size("xb") - 1
    devices = 2 * (last + 1)
    block = out.shape[0] // devices
    device = column * 2 + upper
    top = jnp.broadcast_to(fastest, (8, TILE))
    for peer in range(devices):
        out[peer * block : peer * block + 8, :] = top
    row = sublanes()

    def edge(line):
        rows = slice(line, line + 1)
        slots = [slot_of(ctl, position) for position in range(2)]
        fields = [state[slot, field, rows, :] for slot in slots for field in range(3)]
        return stacked(fields, top), [bed[slot, rows, :] for slot in slots] if bed is not None else None

    for inside, peer, line in (
        (column > 0, device - 2, 0),
        (column < last, device + 2, TILE - 1),
    ):

        @pl.when(inside)
        def _(peer=peer, line=line):
            lines, ground = edge(line)
            start = pl.multiple_of(peer * block, 8)
            out[pl.ds(start, 8), :] = lines
            if ground:
                out[pl.ds(pl.multiple_of(start + 8, 8), 8), :] = stacked(ground, top)

    slot = jnp.where(upper > 0, ctl[SLOT_LOW], 1 - ctl[SLOT_LOW])
    begin = pl.multiple_of((1 - upper) * LANES, LANES)
    lane = lax.broadcasted_iota(jnp.int32, (TILE, LANES), 1)
    packed = None
    for field in range(4 if bed is not None else 3):
        if field < 3:
            part = state[slot, field, :, pl.ds(begin, LANES)]
        else:
            part = bed[slot, :, pl.ds(begin, LANES)]
        turned = pltpu.roll(part, field + 1 - upper, 1)
        packed = turned if field == 0 else jnp.where(lane == field, turned, packed)
    lines = jnp.transpose(packed)[:8]
    columns[...] = lines
    start = pl.multiple_of((device + 1 - 2 * upper) * block, 8)
    out[pl.ds(start, 8), :] = jnp.where(row == TOP, top, lines)


def opening(
    state_in, bed_in, manning_in, neighbours_in, wet_in, moves_in,
    out, columns, ctl, leaving,
    state, bed, manning, neighbours, wet, moves, sems,
):
    copies = start_all(
        (
            (neighbours_in, neighbours),
            (wet_in, wet),
            (moves_in, moves),
            (state_in.at[0], state.at[0]),
            (state_in.at[1], state.at[1]),
            (bed_in, bed),
        ),
        sems,
    )
    device = lax.axis_index("xb") * 2 + lax.axis_index("yb")
    wait_all(copies[:3])
    first = device * 2
    low = jnp.where(neighbours[3, first] == first + 1, 0, 1)
    ctl[SLOT_LOW] = low
    for position in range(2):
        slot = low if position == 0 else 1 - low
        tile = first + slot
        ctl[WALL_WEST + position] = (neighbours[0, tile] < 0).astype(jnp.int32)
        ctl[WALL_EAST + position] = (neighbours[1, tile] < 0).astype(jnp.int32)
        ctl[WALL_OUTER + position] = (neighbours[2 + position, tile] < 0).astype(jnp.int32)
    for step in range(STEPS):
        for slot in range(2):
            ctl[WET + 2 * step + slot] = wet[step, first + slot]
        ctl[MOVE + step] = moves[step, device]
    moving = moves[0, device]
    rough = start_all(((manning_in.at[moving, 0:EARLY], manning),), sems, 6)
    count = lax.axis_size("xb")
    upper = lax.axis_index("yb")
    column = lax.axis_index("xb")
    source = lax.rem(column + count - 1, count) * 2 + upper
    before = lax.rem(column + count - 2, count) * 2 + upper
    again = moves[0, source] == moves[1, source]
    tile_first = source * 2 + moves[0, source]
    tile_second = jnp.where(
        again, before * 2 + moves[0, before], source * 2 + 1 - moves[0, source]
    )
    for step in range(STEPS):
        ctl[WET_FIRST + step] = wet[step, tile_first]
        ctl[WET_SECOND + step] = wet[step, tile_second]

    total = jnp.zeros((ROWS, TILE), jnp.float32)
    for slot in range(2):
        copies[3 + slot].wait()

        def group(index, best, slot=slot):
            rows = pl.ds(pl.multiple_of(index * ROWS, ROWS), ROWS)
            along_x, along_y = cell(*(state[slot, field, rows, :] for field in range(3)))
            return jnp.maximum(best, jnp.maximum(along_x[5], along_y[5]))

        best = lax.fori_loop(0, TILE // ROWS, group, jnp.zeros((ROWS, TILE), jnp.float32))
        total = jnp.maximum(total, jnp.where(wet[0, first + slot] > 0, best, 0.0))
    copies[5].wait()
    wait_all(rough)
    early = start_all(
        (
            (state.at[moving, :, 0:EARLY], leaving.at[0:3]),
            (bed.at[moving, 0:EARLY], leaving.at[3]),
            (manning, leaving.at[4]),
        ),
        sems,
        7,
    )
    messages(ctl, state, bed, jnp.max(total, keepdims=True), out, columns)
    wait_all(early)


def pass_on(ctl_in, leaving, ctl, same):
    del leaving, same
    for index in range(CONTROLS):
        ctl[index] = ctl_in[index]


def second_early(
    ctl_in, order, state_in, bed_in, manning_in, arrived, ctl, leaving, buffer, sems
):
    del order
    for index in range(CONTROLS):
        ctl[index] = ctl_in[index]
    again = ctl_in[MOVE] == ctl_in[MOVE + 1]
    other = 1 - ctl_in[MOVE]
    parts = 3
    size = EARLY // parts
    chunks = [slice(part * size, (part + 1) * size) for part in range(parts)]
    for part, rows in enumerate(chunks):

        @pl.when(again)
        def _(part=part, rows=rows):
            pltpu.make_async_copy(arrived.at[:, rows], buffer.at[:, rows], sems.at[part]).start()

        @pl.when(jnp.logical_not(again))
        def _(part=part, rows=rows):
            sem = sems.at[part]
            pltpu.make_async_copy(
                state_in.at[other, :, rows], buffer.at[0:3, rows], sem
            ).start()
            pltpu.make_async_copy(bed_in.at[other, rows], buffer.at[3, rows], sem).start()
            pltpu.make_async_copy(manning_in.at[other, rows], buffer.at[4, rows], sem).start()

    outgoing = []
    for part, rows in enumerate(chunks):
        pltpu.make_async_copy(arrived.at[:, rows], buffer.at[:, rows], sems.at[part]).wait()
        outgoing += start_all(
            ((buffer.at[:, rows], leaving.at[:, rows]),), sems, parts + part
        )
    wait_all(outgoing)


def rates(ctl, state_in, bed_in, rate_out, state, bed, rate, sems):
    row_ids = lax.broadcasted_iota(jnp.int32, (ROWS, TILE), 0)
    lane = lax.broadcasted_iota(jnp.int32, (ROWS, LANES), 1)
    row8 = sublanes()
    last = TILE // ROWS - 1
    chunk = TILE // CHUNKS
    incoming = []
    for part in range(CHUNKS):
        rows = slice(part * chunk, (part + 1) * chunk)
        incoming.append(
            start_all(
                (
                    (state_in.at[:, :, rows], state.at[:, :, rows]),
                    (bed_in.at[:, rows], bed.at[:, rows]),
                ),
                sems,
                2 * part,
            )
        )
    wait_all(incoming[0])
    outgoing = []

    def field_ref(which, field):
        return bed.at[which] if field == 3 else state.at[which, field]

    def opening_faces(position):
        slot = slot_of(ctl, position)
        keep = jnp.where(flag(ctl, WALL_WEST + position), 1.0, 0.0)
        first = [field_ref(slot, field)[0:8, :] for field in range(4)]
        right, _ = cell(*first[:3])
        left, _ = cell(first[0], -first[1], first[2])
        return tuple(keep * part[0:1, :] for part in face(left, right)) + (keep * first[3][0:1, :],)

    def group_of(position):
        slot = slot_of(ctl, position)
        other = 1 - slot
        keep_outer = jnp.where(flag(ctl, WALL_OUTER + position), 1.0, 0.0)
        keep_east = jnp.where(flag(ctl, WALL_EAST + position), 1.0, 0.0)
        inner_lane = LANES - 1 if position == 0 else 0
        outer_lane = LANES - 1 - inner_lane
        inner_cols = slice(0, LANES) if position == 0 else slice(LANES, TILE)
        inner_turn = LANES - 1 if position == 0 else 1

        def group(index, carry):
            base = pl.multiple_of(index * ROWS, ROWS)
            rows = pl.ds(base, ROWS)
            after = pl.ds(pl.multiple_of(jnp.minimum(base + ROWS, TILE - 8), 8), 8)
            at_end = index == last
            fields = []
            for field in range(4):
                ref = field_ref(slot, field)
                block = ref[rows, :]
                mirrored = jnp.broadcast_to(block[ROWS - 1 : ROWS], (8, TILE))
                if field == 1:
                    mirrored = -mirrored
                if field == 3:
                    mirrored = keep_east * mirrored
                fields.append(
                    jnp.concatenate([block, jnp.where(at_end, mirrored, ref[after, :])], 0)
                )
            cells_x, cells_y = cell(*fields[:3])

            def down(value):
                return pltpu.roll(value, ROWS + 7, 0)[:ROWS]

            here = tuple(value[:ROWS] for value in cells_x)
            keep = jnp.where(row8 == 7, jnp.where(at_end, keep_east, 1.0), 1.0)
            faces = tuple(
                jnp.concatenate([value[: ROWS - 8], value[ROWS - 8 :] * keep], 0)
                for value in face(here, tuple(down(value) for value in cells_x))
            )
            turned = tuple(pltpu.roll(value, 1, 0) for value in faces)
            change_x = tuple(
                value - jnp.where(row_ids == 0, before, moved)
                for value, before, moved in zip(faces, carry[:3], turned)
            )
            ground = fields[3][:ROWS]
            ground_up = pltpu.roll(ground, 1, 0)
            slope_x = down(fields[3]) - jnp.where(row_ids == 0, carry[3], ground_up)
            carried = tuple(value[0:1, :] for value in turned) + (ground_up[0:1, :],)

            ghosts = []
            for field in range(4):
                inner = pltpu.roll(field_ref(other, field)[rows, inner_cols], inner_turn, 1)
                own = fields[field][:ROWS, inner_cols]
                if field == 2:
                    own = -own
                if field == 3:
                    own = keep_outer * own
                ghosts.append(jnp.where(lane == inner_lane, inner, own))
            _, ghost_y = cell(*ghosts[:3])
            low = tuple(value[:ROWS, :LANES] for value in cells_y)
            high = tuple(value[:ROWS, LANES:] for value in cells_y)

            def right_of(low_part, high_part, ghost_part):
                turned_low = pltpu.roll(low_part, LANES - 1, 1)
                turned_high = pltpu.roll(high_part, LANES - 1, 1)
                return (
                    jnp.where(lane == LANES - 1, turned_high, turned_low),
                    jnp.where(lane == LANES - 1, ghost_part, turned_high),
                )

            pairs = [right_of(a, b, c) for a, b, c in zip(low, high, ghost_y)]
            faces_low = face(low, tuple(pair[0] for pair in pairs))
            faces_high = face(high, tuple(pair[1] for pair in pairs))
            faces_edge = face(ghost_y, low)
            if position == 0:
                faces_edge = tuple(keep_outer * value for value in faces_edge)
            else:
                keep_lane = jnp.where(lane == outer_lane, keep_outer, 1.0)
                faces_high = tuple(keep_lane * value for value in faces_high)
            change_y = []
            for a, b, c in zip(faces_low, faces_high, faces_edge):
                turned_a = pltpu.roll(a, 1, 1)
                turned_b = pltpu.roll(b, 1, 1)
                change_y.append(
                    jnp.concatenate(
                        [
                            a - jnp.where(lane == 0, c, turned_a),
                            b - jnp.where(lane == 0, turned_a, turned_b),
                        ],
                        1,
                    )
                )
            ground_low = ground[:, :LANES]
            ground_high = ground[:, LANES:]
            north = right_of(ground_low, ground_high, ghosts[3])
            turned_low = pltpu.roll(ground_low, 1, 1)
            turned_high = pltpu.roll(ground_high, 1, 1)
            slope_y = jnp.concatenate(
                [
                    north[0] - jnp.where(lane == 0, ghosts[3], turned_low),
                    north[1] - jnp.where(lane == 0, turned_low, turned_high),
                ],
                1,
            )
            weight = SLOPE * fields[0][:ROWS]
            rate[slot, 0, rows, :] = SCALE * (change_x[0] + change_y[0])
            rate[slot, 1, rows, :] = SCALE * (change_x[1] + change_y[2]) + weight * slope_x
            rate[slot, 2, rows, :] = SCALE * (change_x[2] + change_y[1]) + weight * slope_y
            return carried

        return group

    carries = [opening_faces(position) for position in range(2)]
    groups = [group_of(position) for position in range(2)]
    per_chunk = chunk // ROWS
    for part in range(CHUNKS):
        if part + 1 < CHUNKS:
            wait_all(incoming[part + 1])
        for position in range(2):
            carries[position] = lax.fori_loop(
                part * per_chunk, (part + 1) * per_chunk, groups[position], carries[position]
            )
        rows = slice(part * chunk, (part + 1) * chunk)
        outgoing += start_all(
            ((rate.at[:, :, rows], rate_out.at[:, :, rows]),), sems, 2 * CHUNKS + part
        )
    wait_all(outgoing)


def moved_on(old, slopes, rough, delta, wet_now):
    h, hu, hv = (value - delta * slope for value, slope in zip(old, slopes))
    inverse = 1.0 / h
    u = hu * inverse
    v = hv * inverse
    speed = jnp.sqrt(u * u + v * v)
    power = jnp.exp((-4.0 / 3.0) * jnp.log(jnp.abs(h)))
    drag = (GRAVITY * delta) * (rough * rough) * (speed * power)
    factor = 1.0 / (1.0 + drag)
    fresh = (h, hu * factor, hv * factor)
    return tuple(jnp.where(wet_now, new, value) for new, value in zip(fresh, old))


def repeat_steps(ctl, wet_from, deltas, early, work, other, sems):
    chunk = EARLY // 3
    incoming = []
    for part in range(3):
        rows = slice(part * chunk, (part + 1) * chunk)
        incoming += start_all(((early.at[:, rows], work.at[:, rows]),), sems, part)
    row_ids = lax.broadcasted_iota(jnp.int32, (ROWS, TILE), 0)
    lane = lax.broadcasted_iota(jnp.int32, (ROWS, LANES), 1)
    start = tuple(jnp.zeros((1, TILE), jnp.float32) for _ in range(4))

    def halves(value):
        return value[:, :LANES], value[:, LANES:]

    def right_of(value):
        low, high = (pltpu.roll(part, LANES - 1, 1) for part in halves(value))
        return jnp.concatenate([jnp.where(lane == LANES - 1, high, low), high], 1)

    def left_of(value):
        low, high = (pltpu.roll(part, 1, 1) for part in halves(value))
        return jnp.concatenate([low, jnp.where(lane == 0, low, high)], 1)

    def down(value):
        return pltpu.roll(value, ROWS + 7, 0)[:ROWS]

    for step in range(STEPS):
        source, target = (work, other) if step % 2 == 0 else (other, work)
        delta = deltas[step][0:1, :]
        wet_now = flag(ctl, wet_from + step)

        def group(index, carry, source=source, target=target, delta=delta, wet_now=wet_now):
            base = pl.multiple_of(index * ROWS, ROWS)
            rows = pl.ds(base, ROWS)
            after = pl.ds(pl.multiple_of(jnp.minimum(base + ROWS, EARLY - 8), 8), 8)
            refs = [source.at[field] for field in range(3)] + [work.at[3]]
            fields = [jnp.concatenate([ref[rows, :], ref[after, :]], 0) for ref in refs]
            cells_x, cells_y = cell(*fields[:3])
            here_x = tuple(value[:ROWS] for value in cells_x)
            here_y = tuple(value[:ROWS] for value in cells_y)
            faces_x = face(here_x, tuple(down(value) for value in cells_x))
            turned = tuple(pltpu.roll(value, 1, 0) for value in faces_x)
            change_x = tuple(
                value - jnp.where(row_ids == 0, before, moved)
                for value, before, moved in zip(faces_x, carry[:3], turned)
            )
            ground = fields[3][:ROWS]
            ground_up = pltpu.roll(ground, 1, 0)
            slope_x = down(fields[3]) - jnp.where(row_ids == 0, carry[3], ground_up)
            carried = tuple(value[0:1, :] for value in turned) + (ground_up[0:1, :],)
            faces_y = face(here_y, tuple(right_of(value) for value in here_y))
            change_y = tuple(value - left_of(value) for value in faces_y)
            slope_y = right_of(ground) - left_of(ground)
            old = tuple(value[:ROWS] for value in fields[:3])
            weight = SLOPE * old[0]
            slopes = (
                SCALE * (change_x[0] + change_y[0]),
                SCALE * (change_x[1] + change_y[2]) + weight * slope_x,
                SCALE * (change_x[2] + change_y[1]) + weight * slope_y,
            )
            for field, value in enumerate(
                moved_on(old, slopes, work[4, rows, :], delta, wet_now)
            ):
                target[field, rows, :] = value
            return carried

        per_chunk = chunk // ROWS
        if step == 0:
            carry = start
            incoming[0].wait()
            for part in range(3):
                if part < 2:
                    incoming[part + 1].wait()
                carry = lax.fori_loop(part * per_chunk, (part + 1) * per_chunk, group, carry)
        else:
            lax.fori_loop(0, EARLY // ROWS, group, start)


def late_rows(tile, late):
    row = sublanes()
    kept = EARLY - 8
    lane = lax.broadcasted_iota(jnp.int32, (8, LANES), 1)
    for field in range(3):
        late[field, 0:8, :] = jnp.where(
            row < 3, tile[field, 0:8, :], tile[field, kept : kept + 8, :]
        )
        late[field, 8 : TILE - kept, :] = tile[field, kept + 8 :, :]
        packed = [None, None]
        for block in range(EARLY // 8):
            rows = slice(8 * block, 8 * block + 8)
            sides = jnp.where(lane < 64, tile[field, rows, :LANES], tile[field, rows, LANES:])
            turned = pltpu.roll(sides, (3 + 8 * block) % LANES, 1)
            which = block // 16
            packed[which] = (
                turned
                if packed[which] is None
                else jnp.where(lane // 8 == block % 16, turned, packed[which])
            )
        late[field, TILE - kept :, :] = jnp.concatenate(packed, 1)


def merge(late, early, tile):
    row = sublanes()
    kept = EARLY - 8
    lane = lax.broadcasted_iota(jnp.int32, (8, LANES), 1)
    for field in range(3):
        first = late[field, 0:8, :]
        for block in range(EARLY // 8):
            rows = slice(8 * block, 8 * block + 8)
            which = block // 16
            packed = late[field, TILE - kept :, which * LANES : (which + 1) * LANES]
            sides = pltpu.roll(packed, (-3 - 8 * block) % LANES, 1)
            value = early[field, rows, :]
            value = jnp.concatenate(
                [
                    jnp.where(lane < 3, sides, value[:, :LANES]),
                    jnp.where(lane >= LANES - 3, sides, value[:, LANES:]),
                ],
                1,
            )
            if block == 0:
                value = jnp.where(row < 3, first, value)
            if block == EARLY // 8 - 1:
                value = jnp.where(row < 5, value, first)
            tile[field, rows, :] = value
        tile[field, EARLY:, :] = late[field, 8 : TILE - kept, :]


def repeat_second(ctl, delta0, delta1, delta2, early, out, work, tile, sems):
    repeat_steps(ctl, WET_SECOND, (delta0, delta1, delta2), early, work, tile, sems)
    copy = pltpu.make_async_copy(tile, out, sems.at[0])
    copy.start()
    copy.wait()


def repeat_first(
    ctl, delta0, delta1, delta2, early, late, staying, out, work, other, tile, sems
):
    rest = out.at[1 - ctl[MOVE + 1]]
    again = ctl[MOVE] == ctl[MOVE + 1]

    @pl.when(again)
    def _():
        copy = pltpu.make_async_copy(staying, rest, sems.at[3])
        copy.start()
        copy.wait()

    @pl.when(jnp.logical_not(again))
    def _():
        repeat_steps(ctl, WET_FIRST, (delta0, delta1, delta2), early, work, other, sems)
        merge(late, other, tile)
        copy = pltpu.make_async_copy(tile, rest, sems.at[3])
        copy.start()
        copy.wait()


def finish(ctl, late, early, before, out, tile, sems):
    del before
    merge(late, early, tile)
    copy = pltpu.make_async_copy(tile, out.at[ctl[MOVE + 1]], sems.at[0])
    copy.start()
    copy.wait()


def second_late(ctl, arrived, own, order, leaving, buffer, sems):
    del order
    again = ctl[MOVE] == ctl[MOVE + 1]

    @pl.when(again)
    def _():
        pltpu.make_async_copy(arrived, buffer, sems.at[0]).start()

    @pl.when(jnp.logical_not(again))
    def _():
        pltpu.make_async_copy(own, buffer, sems.at[0]).start()

    pltpu.make_async_copy(arrived, buffer, sems.at[0]).wait()
    copy = pltpu.make_async_copy(buffer, leaving, sems.at[0])
    copy.start()
    copy.wait()


def correct_rows(ctl, slot, got, ground, block, state, rate, bottom):
    position = jnp.where(ctl[SLOT_LOW] == slot, 0, 1)
    device = lax.axis_index("xb") * 2 + lax.axis_index("yb")
    wall = WALL_WEST if bottom else WALL_EAST

    @pl.when(jnp.logical_not(flag(ctl, wall + position)))
    def _():
        peer = device - 2 if bottom else device + 2
        lines = got[pl.ds(pl.multiple_of(peer * block, 8), 8), :]
        grounds = ground[pl.ds(pl.multiple_of(peer * 16 + 8, 8), 8), :]

        def line(value, offset):
            picked = jnp.where(
                position == 0, value[offset : offset + 1, :], value[offset + 3 : offset + 4, :]
            )
            return jnp.broadcast_to(picked, (8, TILE))

        ghost, _ = cell(*(line(lines, field) for field in range(3)))
        ghost_ground = jnp.where(position == 0, grounds[0:1, :], grounds[1:2, :])
        rows = slice(0, 8) if bottom else slice(TILE - 8, TILE)
        own = [state[slot, field, rows, :] for field in range(3)]
        here, _ = cell(*own)
        fluxes = face(ghost, here) if bottom else face(here, ghost)
        push = SCALE * fluxes[1] + (SLOPE * own[0]) * ghost_ground
        row = sublanes()
        sign = -1.0 if bottom else 1.0
        chosen = row == (0 if bottom else 7)
        for field, value in enumerate((SCALE * fluxes[0], push, SCALE * fluxes[2])):
            rate[slot, field, rows, :] += jnp.where(chosen, sign * value, 0.0)


def column_fix(got, ground, block, columns, bed_columns):
    upper = lax.axis_index("yb")
    device = lax.axis_index("xb") * 2 + upper
    peer = device + 1 - 2 * upper
    lines = got[pl.ds(pl.multiple_of(peer * block, 8), 8), :]
    ghost_ground = ground[pl.ds(pl.multiple_of(peer * 16, 8), 8), :][3:4]
    del bed_columns
    mine = columns[...]
    _, ghost = cell(lines[0:1], lines[1:2], lines[2:3])
    _, own = cell(mine[0:1], mine[1:2], mine[2:3])
    low = upper == 0
    left = tuple(jnp.where(low, a, b) for a, b in zip(own, ghost))
    right = tuple(jnp.where(low, b, a) for a, b in zip(own, ghost))
    fluxes = face(left, right)
    sign = jnp.where(low, 1.0, -1.0)
    push = SCALE * fluxes[1] + (SLOPE * mine[0:1]) * ghost_ground
    block8 = stacked(
        [sign * SCALE * fluxes[0], sign * SCALE * fluxes[2], sign * push],
        jnp.zeros((8, TILE), jnp.float32),
    )
    return jnp.transpose(
        jnp.concatenate([block8, jnp.zeros((LANES - 8, TILE), jnp.float32)], 0)
    )


def update(step, ctl, got, ground, columns, state_in, manning_in, rate_in, *rest):
    more = step + 1 < STEPS
    if more:
        fresh_out, out, columns_out, delta_out = rest[:4]
        rest = rest[4:]
    else:
        staying, late_first, late_second, delta_out = rest[:4]
        rest = rest[4:]
    state, manning, rate, fresh, sems = rest
    half = TILE // 2
    parts = [(slot, slice(k * half, (k + 1) * half)) for slot in range(2) for k in range(2)]
    incoming = []
    for index, (slot, rows) in enumerate(parts):
        incoming.append(
            start_all(
                (
                    (rate_in.at[slot, :, rows], rate.at[slot, :, rows]),
                    (state_in.at[slot, :, rows], state.at[slot, :, rows]),
                    (manning_in.at[slot, rows], manning.at[slot, rows]),
                ),
                sems,
                3 * index,
            )
        )
    upper = lax.axis_index("yb")
    devices = 2 * lax.axis_size("xb")
    block = got.shape[0] // devices
    tops = got[0:8, :]
    for peer in range(1, devices):
        tops = jnp.maximum(tops, got[peer * block : peer * block + 8, :])
    delta = (COURANT * SPACING) / tops[TOP : TOP + 1, :]
    delta_out[...] = jnp.broadcast_to(delta, (8, TILE))
    fix = column_fix(got, ground, block, columns, None)
    facing = jnp.where(upper > 0, ctl[SLOT_LOW], 1 - ctl[SLOT_LOW])
    begin = pl.multiple_of((1 - upper) * LANES, LANES)
    target = (1 - upper) * (LANES - 1)
    lane = lax.broadcasted_iota(jnp.int32, (half, LANES), 1)
    total = jnp.zeros((ROWS, TILE), jnp.float32)
    outgoing = []
    for index, (slot, part_rows) in enumerate(parts):
        wait_all(incoming[index])
        bottom = index % 2 == 0
        correct_rows(ctl, slot, got, ground, block, state, rate, bottom)

        @pl.when(facing == slot)
        def _(slot=slot, part_rows=part_rows):
            for field in range(3):
                turned = pltpu.roll(
                    fix[part_rows], lax.rem(target + LANES - field, LANES), 1
                )
                rate[slot, field, part_rows, pl.ds(begin, LANES)] += jnp.where(
                    lane == target, turned, 0.0
                )

        wet_now = flag(ctl, WET + 2 * step + slot)

        def group(index, best, slot=slot, wet_now=wet_now):
            rows = pl.ds(pl.multiple_of(index * ROWS, ROWS), ROWS)
            old = tuple(state[slot, field, rows, :] for field in range(3))
            slopes = tuple(rate[slot, field, rows, :] for field in range(3))
            h, hu, hv = moved_on(old, slopes, manning[slot, rows, :], delta, wet_now)
            fresh[slot, 0, rows, :] = h
            fresh[slot, 1, rows, :] = hu
            fresh[slot, 2, rows, :] = hv
            if more:
                along_x, along_y = cell(h, hu, hv)
                best = jnp.maximum(best, jnp.maximum(along_x[5], along_y[5]))
            return best

        best = lax.fori_loop(
            part_rows.start // ROWS,
            part_rows.stop // ROWS,
            group,
            jnp.zeros((ROWS, TILE), jnp.float32),
        )
        if more:
            best = jnp.where(flag(ctl, WET + 2 * step + 2 + slot), best, 0.0)
            total = jnp.maximum(total, best)
        if more:
            outgoing += start_all(
                ((fresh.at[slot, :, part_rows], fresh_out.at[slot, :, part_rows]),),
                sems,
                12 + index,
            )
    if more:
        messages(ctl, fresh, None, jnp.max(total, keepdims=True), out, columns_out)
    else:
        outgoing += start_all(((fresh.at[1 - ctl[MOVE]], staying),), sems, 16)
        late_rows(fresh.at[ctl[MOVE]], late_first)
        late_rows(fresh.at[1 - ctl[MOVE]], late_second)
    wait_all(outgoing)


def vmem():
    return pl.BlockSpec(memory_space=pltpu.VMEM)


def smem():
    return pl.BlockSpec(memory_space=pltpu.SMEM)


def hbm():
    return pl.BlockSpec(memory_space=pltpu.HBM)


def anywhere():
    return pl.BlockSpec(memory_space=pl.ANY)


def call(kernel, outs, out_specs, in_specs, flops, scratch=(), aliases=None, room=VMEM_BYTES):
    return pl.pallas_call(
        kernel,
        scratch_shapes=scratch,
        input_output_aliases=aliases or {},
        out_shape=outs,
        in_specs=in_specs,
        out_specs=out_specs,
        compiler_params=pltpu.CompilerParams(vmem_limit_bytes=room),
        cost_estimate=pl.CostEstimate(flops=flops, bytes_accessed=4 << 20, transcendentals=0),
    )


def f32(*shape):
    return jax.ShapeDtypeStruct(shape, jnp.float32)


def spread(fast):
    return lax.all_to_all(fast, ("xb", "yb"), split_axis=0, concat_axis=0, tiled=True)


def body(state, bed, manning, neighbours, wet, moves):
    shape = f32(*state.shape)
    tile_shape = f32(*state.shape[1:])
    devices = lax.axis_size("xb") * lax.axis_size("yb")
    sem = [pltpu.SemaphoreType.DMA((1,))]
    whole = pltpu.VMEM(state.shape, jnp.float32)
    part = pltpu.VMEM(bed.shape, jnp.float32)
    early_shape = f32(5, EARLY, TILE)
    late_shape = f32(3, LATE, TILE)
    delta_shape = f32(8, TILE)
    out, columns, ctl, leaving = call(
        opening,
        (
            f32(16 * devices, TILE),
            f32(8, TILE),
            jax.ShapeDtypeStruct((CONTROLS,), jnp.int32),
            early_shape,
        ),
        (vmem(), vmem(), smem(), hbm()),
        [hbm()] * 6,
        4 << 20,
        [
            whole,
            part,
            pltpu.VMEM((EARLY, TILE), jnp.float32),
            pltpu.SMEM(neighbours.shape[::-1], jnp.int32),
            pltpu.SMEM(wet.shape, jnp.int32),
            pltpu.SMEM(moves.shape, jnp.int32),
            pltpu.SemaphoreType.DMA((10,)),
        ],
    )(state, bed, manning, neighbours.T, wet, moves)
    controls = jax.ShapeDtypeStruct((CONTROLS,), jnp.int32)
    early_work = pltpu.VMEM(early_shape.shape, jnp.float32)
    state_first = state
    ground = None
    deltas = []
    for step in range(STEPS):
        got = spread(out)
        ground = got if step == 0 else ground
        if step == 0:
            ctl, leaving = call(
                pass_on, (controls, early_shape), (smem(), hbm()), [smem(), hbm()], 1 << 10,
                aliases={1: 1},
            )(ctl, leaving)
            early_first = shifted(leaving, "xb", 1)
        elif step == 1:
            ctl, leaving = call(
                second_early,
                (controls, early_shape),
                (smem(), hbm()),
                [smem()] + [hbm()] * 5,
                1 << 10,
                [early_work, pltpu.SemaphoreType.DMA((6,))],
            )(ctl, deltas[0], state_first, bed, manning, early_first)
            early_second = shifted(leaving, "xb", 1)
        rate = call(
            rates,
            shape,
            hbm(),
            [smem(), hbm(), hbm()],
            16 << 20,
            [whole, part, whole, pltpu.SemaphoreType.DMA((3 * CHUNKS,))],
        )(ctl, state, bed)
        if step + 1 < STEPS:
            shapes = (shape, f32(8 * devices, TILE), f32(8, TILE), delta_shape)
            places = (hbm(), vmem(), vmem(), vmem())
        else:
            shapes = (tile_shape, late_shape, late_shape, delta_shape)
            places = (hbm(), vmem(), vmem(), vmem())
        outs = call(
            functools.partial(update, step),
            shapes,
            places,
            [smem(), vmem(), vmem(), vmem(), hbm(), hbm(), hbm()],
            8 << 20,
            [whole, part, whole, whole, pltpu.SemaphoreType.DMA((17,))],
        )(ctl, got, ground, columns, state, manning, rate)
        deltas.append(outs[3])
        if step + 1 < STEPS:
            state, out, columns, _ = outs
    staying, late_first, late_second, _ = outs
    late_arrived = shifted(late_first, "xb", 1)
    early_state = f32(3, EARLY, TILE)
    second = call(
        repeat_second,
        early_state,
        hbm(),
        [smem()] + [vmem()] * 3 + [hbm()],
        8 << 20,
        [early_work, pltpu.VMEM(early_state.shape, jnp.float32), pltpu.SemaphoreType.DMA((3,))],
    )(ctl, *deltas, early_second)
    leaving = call(
        second_late,
        late_shape,
        hbm(),
        [smem(), hbm(), hbm(), hbm()],
        1 << 10,
        [pltpu.VMEM(late_shape.shape, jnp.float32)] + sem,
    )(ctl, late_arrived, late_second, second)
    late_next = shifted(leaving, "xb", 1)
    final = call(
        repeat_first,
        shape,
        hbm(),
        [smem()] + [vmem()] * 3 + [hbm(), vmem(), hbm()],
        8 << 20,
        [
            early_work,
            pltpu.VMEM(early_state.shape, jnp.float32),
            pltpu.VMEM(tile_shape.shape, jnp.float32),
            pltpu.SemaphoreType.DMA((4,)),
        ],
    )(ctl, *deltas, early_first, late_arrived, staying)
    return call(
        finish,
        shape,
        hbm(),
        [smem(), vmem(), vmem(), hbm()],
        1 << 20,
        [pltpu.VMEM(tile_shape.shape, jnp.float32)] + sem,
        {3: 0},
    )(ctl, late_next, second, final)


def solution(mesh):
    placed = (
        P(("runs", "xb", "yb"), None, None, None),
        P(("runs", "xb", "yb"), None, None),
        P(("runs", "xb", "yb"), None, None),
        P("runs", None),
        P(None, "runs"),
        P(None, "runs"),
    )
    return jax.shard_map(
        body,
        mesh=mesh,
        in_specs=placed,
        out_specs=P(("runs", "xb", "yb"), None, None, None),
        check_vma=False,
    )
```

```python
import functools

import jax
import jax.numpy as jnp
from jax import lax
from jax.experimental import pallas as pl
from jax.experimental.pallas import tpu as pltpu
from jax.sharding import PartitionSpec as P

STEPS = 3
GRAVITY = 9.81
ROOT_G = GRAVITY**0.5
SPACING = 5.0
COURANT = 0.2
ROWS = 32
LANES = 128
TILE = 256
VMEM_BYTES = 60 * 1024 * 1024
SLOT_LOW, WALL_WEST, WALL_EAST, WALL_OUTER, WET, MOVE = 0, 1, 3, 5, 7, 13
CONTROLS = 16
CHUNKS = 8
PARTS = 8
HALF = TILE // 2
STRIP = 16
TOP = 6
SCALE = 0.5 / SPACING
SLOPE = GRAVITY / (2.0 * SPACING)


def shifted(value, axis, steps, around=True):
    count = lax.axis_size(axis)
    pairs = [(source, (source + steps) % count) for source in range(count)]
    if not around:
        pairs = [pair for pair in pairs if abs(pair[0] - pair[1]) == abs(steps)]
    return lax.ppermute(value, axis, pairs)


def cell(h, hu, hv):
    root = lax.rsqrt(h)
    inverse = root * root
    u = hu * inverse
    v = hv * inverse
    celerity = ROOT_G * (h * root)
    pressure = (0.5 * GRAVITY) * (h * h)
    cross = hu * v
    speed_x = jnp.abs(u) + celerity
    speed_y = jnp.abs(v) + celerity
    along_x = (h, hu, hv, hu * u + pressure, cross, speed_x)
    along_y = (h, hv, hu, hv * v + pressure, cross, speed_y)
    return along_x, along_y


def face(left, right):
    wave = jnp.maximum(left[5], right[5])
    return (
        (left[1] + right[1]) - wave * (right[0] - left[0]),
        (left[3] + right[3]) - wave * (right[1] - left[1]),
        (left[4] + right[4]) - wave * (right[2] - left[2]),
    )


def slot_of(ctl, position):
    low = ctl[SLOT_LOW]
    return low if position == 0 else 1 - low


def flag(ctl, index):
    return ctl[index] > 0


def start_all(pairs, sems, first=0):
    copies = [
        pltpu.make_async_copy(src, dst, sems.at[first + k]) for k, (src, dst) in enumerate(pairs)
    ]
    for copy in copies:
        copy.start()
    return copies


def wait_all(copies):
    for copy in copies:
        copy.wait()


def sublanes(width=TILE):
    return lax.broadcasted_iota(jnp.int32, (8, width), 0)


def stacked(lines, base):
    row = sublanes()
    for index, line in enumerate(lines):
        base = jnp.where(row == index, jnp.broadcast_to(line, (8, TILE)), base)
    return base


def messages(ctl, state, bed, fastest, out, columns):
    upper = lax.axis_index("yb")
    column = lax.axis_index("xb")
    last = lax.axis_size("xb") - 1
    devices = 2 * (last + 1)
    block = out.shape[0] // devices
    device = column * 2 + upper
    top = jnp.broadcast_to(fastest, (8, TILE))
    for peer in range(devices):
        out[peer * block : peer * block + 8, :] = top
    row = sublanes()

    def edge(line):
        rows = slice(line, line + 1)
        slots = [slot_of(ctl, position) for position in range(2)]
        fields = [state[slot, field, rows, :] for slot in slots for field in range(3)]
        return stacked(fields, top), [bed[slot, rows, :] for slot in slots] if bed is not None else None

    for inside, peer, line in (
        (column > 0, device - 2, 0),
        (column < last, device + 2, TILE - 1),
    ):

        @pl.when(inside)
        def _(peer=peer, line=line):
            lines, ground = edge(line)
            start = pl.multiple_of(peer * block, 8)
            out[pl.ds(start, 8), :] = lines
            if ground:
                out[pl.ds(pl.multiple_of(start + 8, 8), 8), :] = stacked(ground, top)

    slot = jnp.where(upper > 0, ctl[SLOT_LOW], 1 - ctl[SLOT_LOW])
    begin = pl.multiple_of((1 - upper) * LANES, LANES)
    lane = lax.broadcasted_iota(jnp.int32, (TILE, LANES), 1)
    packed = None
    for field in range(4 if bed is not None else 3):
        if field < 3:
            part = state[slot, field, :, pl.ds(begin, LANES)]
        else:
            part = bed[slot, :, pl.ds(begin, LANES)]
        turned = pltpu.roll(part, field + 1 - upper, 1)
        packed = turned if field == 0 else jnp.where(lane == field, turned, packed)
    lines = jnp.transpose(packed)[:8]
    columns[...] = lines
    start = pl.multiple_of((device + 1 - 2 * upper) * block, 8)
    out[pl.ds(start, 8), :] = jnp.where(row == TOP, top, lines)


def opening(
    state_in, bed_in, neighbours_in, wet_in, moves_in,
    out, columns, ctl,
    state, bed, neighbours, wet, moves, sems,
):
    copies = start_all(
        (
            (neighbours_in, neighbours),
            (wet_in, wet),
            (moves_in, moves),
            (state_in.at[0], state.at[0]),
            (state_in.at[1], state.at[1]),
            (bed_in, bed),
        ),
        sems,
    )
    device = lax.axis_index("xb") * 2 + lax.axis_index("yb")
    wait_all(copies[:3])
    first = device * 2
    low = jnp.where(neighbours[3, first] == first + 1, 0, 1)
    ctl[SLOT_LOW] = low
    for position in range(2):
        slot = low if position == 0 else 1 - low
        tile = first + slot
        ctl[WALL_WEST + position] = (neighbours[0, tile] < 0).astype(jnp.int32)
        ctl[WALL_EAST + position] = (neighbours[1, tile] < 0).astype(jnp.int32)
        ctl[WALL_OUTER + position] = (neighbours[2 + position, tile] < 0).astype(jnp.int32)
    for step in range(STEPS):
        for slot in range(2):
            ctl[WET + 2 * step + slot] = wet[step, first + slot]
        ctl[MOVE + step] = moves[step, device]

    total = jnp.zeros((ROWS, TILE), jnp.float32)
    for slot in range(2):
        copies[3 + slot].wait()

        def group(index, best, slot=slot):
            rows = pl.ds(pl.multiple_of(index * ROWS, ROWS), ROWS)
            along_x, along_y = cell(*(state[slot, field, rows, :] for field in range(3)))
            return jnp.maximum(best, jnp.maximum(along_x[5], along_y[5]))

        best = lax.fori_loop(0, TILE // ROWS, group, jnp.zeros((ROWS, TILE), jnp.float32))
        total = jnp.maximum(total, jnp.where(wet[0, first + slot] > 0, best, 0.0))
    copies[5].wait()
    messages(ctl, state, bed, jnp.max(total, keepdims=True), out, columns)


def rates(ctl, state_in, bed_in, rate_out, state, bed, rate, sems):
    width = 2 * TILE
    row_ids = lax.broadcasted_iota(jnp.int32, (STRIP, width), 0)
    row8 = sublanes(width)
    lane = lax.broadcasted_iota(jnp.int32, (STRIP, LANES), 1)
    last = TILE // STRIP - 1
    chunk = TILE // CHUNKS
    slots = [slot_of(ctl, position) for position in range(2)]
    incoming = []
    for part in range(CHUNKS):
        rows = slice(part * chunk, (part + 1) * chunk)
        incoming.append(
            start_all(
                (
                    (state_in.at[:, :, rows], state.at[:, :, rows]),
                    (bed_in.at[:, rows], bed.at[:, rows]),
                ),
                sems,
                2 * part,
            )
        )
    keep_west, keep_east, keep_south, keep_north = (
        jnp.where(flag(ctl, index), 1.0, 0.0)
        for index in (WALL_WEST, WALL_EAST, WALL_OUTER, WALL_OUTER + 1)
    )

    def strip(field, rows):
        if field == 3:
            return jnp.concatenate([bed[slot, rows, :] for slot in slots], 1)
        return jnp.concatenate([state[slot, field, rows, :] for slot in slots], 1)

    def blocks(value):
        return [value[:, k * LANES : (k + 1) * LANES] for k in range(4)]

    def right_of(value, end=None):
        turned = [pltpu.roll(part, LANES - 1, 1) for part in blocks(value)]
        after = turned[1:] + [turned[3] if end is None else end]
        return jnp.concatenate(
            [
                jnp.where(lane == LANES - 1, following, part)
                if following is not part
                else part
                for part, following in zip(turned, after)
            ],
            1,
        )

    def left_of(value, end):
        turned = [pltpu.roll(part, 1, 1) for part in blocks(value)]
        before = [end] + turned[:3]
        return jnp.concatenate(
            [jnp.where(lane == 0, previous, part) for part, previous in zip(turned, before)], 1
        )

    def down(value):
        return pltpu.roll(value, STRIP + 7, 0)[:STRIP]

    def group(index, carry):
        base = pl.multiple_of(index * STRIP, STRIP)
        rows = pl.ds(base, STRIP)
        after = pl.ds(pl.multiple_of(jnp.minimum(base + STRIP, TILE - 8), 8), 8)
        at_end = index == last
        fields = [
            jnp.concatenate([strip(field, rows), strip(field, after)], 0) for field in range(3)
        ]
        cells_x, cells_y = cell(*fields)
        here_x = tuple(value[:STRIP] for value in cells_x)
        here_y = tuple(value[:STRIP] for value in cells_y)

        ending = jnp.logical_and(row8 == 7, at_end)
        faces = list(face(here_x, tuple(down(value) for value in cells_x)))
        wall = keep_east * (2.0 * (here_x[3] + here_x[5] * here_x[1])[STRIP - 8 :])
        for component, value in enumerate((0.0, wall, 0.0)):
            upper = faces[component]
            faces[component] = jnp.concatenate(
                [upper[: STRIP - 8], jnp.where(ending, value, upper[STRIP - 8 :])], 0
            )
        turned = tuple(pltpu.roll(value, 1, 0) for value in faces)
        change_x = tuple(
            value - jnp.where(row_ids == 0, before, moved)
            for value, before, moved in zip(faces, carry[:3], turned)
        )
        ground = strip(3, rows)
        ground_after = jnp.where(
            at_end,
            jnp.broadcast_to(keep_east * ground[STRIP - 1 :], (8, width)),
            strip(3, after),
        )
        ground_up = pltpu.roll(ground, 1, 0)
        slope_x = down(jnp.concatenate([ground, ground_after], 0)) - jnp.where(
            row_ids == 0, carry[3], ground_up
        )
        carried = tuple(value[0:1, :] for value in turned) + (ground_up[0:1, :],)

        faces_y = list(face(here_y, tuple(right_of(value) for value in here_y)))
        normal = here_y[3]
        spread_y = here_y[5] * here_y[1]
        north = keep_north * (2.0 * (normal + spread_y)[:, width - LANES :])
        south = keep_south * (2.0 * (normal - spread_y)[:, :LANES])
        change_y = []
        for component, (high, low) in enumerate(((0.0, 0.0), (north, south), (0.0, 0.0))):
            parts = blocks(faces_y[component])
            parts[3] = jnp.where(lane == LANES - 1, high, parts[3])
            value = jnp.concatenate(parts, 1)
            change_y.append(value - left_of(value, low))
        slope_y = right_of(ground, keep_north * ground[:, width - LANES :]) - left_of(
            ground, keep_south * ground[:, :LANES]
        )
        weight = SLOPE * here_x[0]
        results = (
            SCALE * (change_x[0] + change_y[0]),
            SCALE * (change_x[1] + change_y[2]) + weight * slope_x,
            SCALE * (change_x[2] + change_y[1]) + weight * slope_y,
        )
        for field, value in enumerate(results):
            for position, slot in enumerate(slots):
                rate[slot, field, rows, :] = value[:, position * TILE : (position + 1) * TILE]
        return carried

    wait_all(incoming[0])
    top, _ = cell(*(strip(field, slice(0, 8)) for field in range(3)))
    nothing = jnp.zeros((1, width), jnp.float32)
    carry = (
        nothing,
        keep_west * (2.0 * (top[3] - top[5] * top[1])[0:1]),
        nothing,
        keep_west * strip(3, slice(0, 8))[0:1],
    )
    per_chunk = chunk // STRIP
    outgoing = []
    for part in range(CHUNKS):
        if part + 1 < CHUNKS:
            wait_all(incoming[part + 1])
        carry = lax.fori_loop(part * per_chunk, (part + 1) * per_chunk, group, carry)
        rows = slice(part * chunk, (part + 1) * chunk)
        outgoing += start_all(
            ((rate.at[:, :, rows], rate_out.at[:, :, rows]),), sems, 2 * CHUNKS + part
        )
    wait_all(outgoing)


def correct_rows(ctl, slot, got, ground, block, state, rate, bottom):
    position = jnp.where(ctl[SLOT_LOW] == slot, 0, 1)
    device = lax.axis_index("xb") * 2 + lax.axis_index("yb")
    wall = WALL_WEST if bottom else WALL_EAST

    @pl.when(jnp.logical_not(flag(ctl, wall + position)))
    def _():
        peer = device - 2 if bottom else device + 2
        lines = got[pl.ds(pl.multiple_of(peer * block, 8), 8), :]
        grounds = ground[pl.ds(pl.multiple_of(peer * 16 + 8, 8), 8), :]

        def line(value, offset):
            picked = jnp.where(
                position == 0, value[offset : offset + 1, :], value[offset + 3 : offset + 4, :]
            )
            return jnp.broadcast_to(picked, (8, TILE))

        ghost, _ = cell(*(line(lines, field) for field in range(3)))
        ghost_ground = jnp.where(position == 0, grounds[0:1, :], grounds[1:2, :])
        rows = slice(0, 8) if bottom else slice(TILE - 8, TILE)
        own = [state[slot, field, rows, :] for field in range(3)]
        here, _ = cell(*own)
        fluxes = face(ghost, here) if bottom else face(here, ghost)
        push = SCALE * fluxes[1] + (SLOPE * own[0]) * ghost_ground
        row = sublanes()
        sign = -1.0 if bottom else 1.0
        chosen = row == (0 if bottom else 7)
        for field, value in enumerate((SCALE * fluxes[0], push, SCALE * fluxes[2])):
            rate[slot, field, rows, :] += jnp.where(chosen, sign * value, 0.0)


def column_fix(got, ground, block, columns, bed_columns):
    upper = lax.axis_index("yb")
    device = lax.axis_index("xb") * 2 + upper
    peer = device + 1 - 2 * upper
    lines = got[pl.ds(pl.multiple_of(peer * block, 8), 8), :]
    ghost_ground = ground[pl.ds(pl.multiple_of(peer * 16, 8), 8), :][3:4]
    del bed_columns
    mine = columns[...]
    _, ghost = cell(lines[0:1], lines[1:2], lines[2:3])
    _, own = cell(mine[0:1], mine[1:2], mine[2:3])
    low = upper == 0
    left = tuple(jnp.where(low, a, b) for a, b in zip(own, ghost))
    right = tuple(jnp.where(low, b, a) for a, b in zip(own, ghost))
    fluxes = face(left, right)
    sign = jnp.where(low, 1.0, -1.0)
    push = SCALE * fluxes[1] + (SLOPE * mine[0:1]) * ghost_ground
    block8 = stacked(
        [sign * SCALE * fluxes[0], sign * SCALE * fluxes[2], sign * push],
        jnp.zeros((8, TILE), jnp.float32),
    )
    return jnp.transpose(
        jnp.concatenate([block8, jnp.zeros((LANES - 8, TILE), jnp.float32)], 0)
    )


def update(step, ctl, got_in, ground_in, columns_in, state_in, manning_in, rate_in, *rest):
    more = step + 1 < STEPS
    if more:
        fresh_out, out_to, columns_to = rest[:3]
        rest = rest[3:]
    else:
        fresh_out, leaving_low, leaving_high = rest[:3]
        rest = rest[3:]
    state, manning, rate, fresh, got, ground, columns, out, columns_out, sems = rest
    small = start_all(
        ((got_in, got), (ground_in, ground), (columns_in, columns)), sems, 5 * PARTS
    )
    size = 2 * TILE // PARTS
    parts = [
        (slot, slice(k * size, (k + 1) * size)) for slot in range(2) for k in range(PARTS // 2)
    ]
    incoming = []
    for index, (slot, rows) in enumerate(parts):
        incoming.append(
            start_all(
                (
                    (rate_in.at[slot, :, rows], rate.at[slot, :, rows]),
                    (state_in.at[slot, :, rows], state.at[slot, :, rows]),
                    (manning_in.at[slot, rows], manning.at[slot, rows]),
                ),
                sems,
                3 * index,
            )
        )
    wait_all(small)
    upper = lax.axis_index("yb")
    devices = 2 * lax.axis_size("xb")
    block = got.shape[0] // devices
    tops = got[0:8, :]
    for peer in range(1, devices):
        tops = jnp.maximum(tops, got[peer * block : peer * block + 8, :])
    delta = (COURANT * SPACING) / tops[TOP : TOP + 1, :]
    fix = column_fix(got, ground, block, columns, None)
    facing = jnp.where(upper > 0, ctl[SLOT_LOW], 1 - ctl[SLOT_LOW])
    begin = pl.multiple_of((1 - upper) * LANES, LANES)
    target = (1 - upper) * (LANES - 1)
    lane = lax.broadcasted_iota(jnp.int32, (size, LANES), 1)
    total = jnp.zeros((ROWS, TILE), jnp.float32)
    outgoing = []
    for index, (slot, part_rows) in enumerate(parts):
        wait_all(incoming[index])
        if part_rows.start == 0:
            correct_rows(ctl, slot, got, ground, block, state, rate, True)
        if part_rows.stop == TILE:
            correct_rows(ctl, slot, got, ground, block, state, rate, False)

        @pl.when(facing == slot)
        def _(slot=slot, part_rows=part_rows):
            for field in range(3):
                turned = pltpu.roll(
                    fix[part_rows], lax.rem(target + LANES - field, LANES), 1
                )
                rate[slot, field, part_rows, pl.ds(begin, LANES)] += jnp.where(
                    lane == target, turned, 0.0
                )

        wet_now = flag(ctl, WET + 2 * step + slot)

        def group(index, best, slot=slot, wet_now=wet_now):
            rows = pl.ds(pl.multiple_of(index * ROWS, ROWS), ROWS)
            h0, hu0, hv0 = (state[slot, field, rows, :] for field in range(3))
            h = h0 - delta * rate[slot, 0, rows, :]
            hu = hu0 - delta * rate[slot, 1, rows, :]
            hv = hv0 - delta * rate[slot, 2, rows, :]
            rough = manning[slot, rows, :]
            inverse = 1.0 / h
            u = hu * inverse
            v = hv * inverse
            speed = jnp.sqrt(u * u + v * v)
            power = jnp.exp((-4.0 / 3.0) * jnp.log(jnp.abs(h)))
            drag = (GRAVITY * delta) * (rough * rough) * (speed * power)
            factor = 1.0 / (1.0 + drag)
            hu = hu * factor
            hv = hv * factor
            h = jnp.where(wet_now, h, h0)
            hu = jnp.where(wet_now, hu, hu0)
            hv = jnp.where(wet_now, hv, hv0)
            fresh[slot, 0, rows, :] = h
            fresh[slot, 1, rows, :] = hu
            fresh[slot, 2, rows, :] = hv
            if more:
                along_x, along_y = cell(h, hu, hv)
                best = jnp.maximum(best, jnp.maximum(along_x[5], along_y[5]))
            return best

        best = lax.fori_loop(
            part_rows.start // ROWS,
            part_rows.stop // ROWS,
            group,
            jnp.zeros((ROWS, TILE), jnp.float32),
        )
        if more:
            best = jnp.where(flag(ctl, WET + 2 * step + 2 + slot), best, 0.0)
            total = jnp.maximum(total, best)
        outgoing += start_all(
            ((fresh.at[slot, :, part_rows], fresh_out.at[slot, :, part_rows]),),
            sems,
            3 * PARTS + index,
        )
    if more:
        messages(ctl, fresh, None, jnp.max(total, keepdims=True), out, columns_out)
        outgoing += start_all(((out, out_to), (columns_out, columns_to)), sems, 4 * PARTS)
    else:
        tile = fresh.at[ctl[MOVE]]
        outgoing += start_all(
            ((tile.at[:, :HALF], leaving_low), (tile.at[:, HALF:], leaving_high)),
            sems,
            4 * PARTS,
        )
    wait_all(outgoing)


def second_leaving(rows, ctl, state, arrived, leaving, sems):
    again = ctl[MOVE] == ctl[MOVE + 1]

    @pl.when(again)
    def _():
        pltpu.make_async_copy(arrived, leaving, sems.at[0]).start()

    @pl.when(jnp.logical_not(again))
    def _():
        other = state.at[1 - ctl[MOVE], :, rows]
        pltpu.make_async_copy(other, leaving, sems.at[0]).start()

    pltpu.make_async_copy(arrived, leaving, sems.at[0]).wait()


def keep_rest(ctl, state, arrived_low, arrived_high, out, sems):
    rest = out.at[1 - ctl[MOVE + 1]]
    again = ctl[MOVE] == ctl[MOVE + 1]
    halves = ((slice(0, HALF), arrived_low), (slice(HALF, TILE), arrived_high))
    for index, (rows, arrived) in enumerate(halves):

        @pl.when(again)
        def _(index=index, rows=rows):
            kept = state.at[1 - ctl[MOVE], :, rows]
            pltpu.make_async_copy(kept, rest.at[:, rows], sems.at[index]).start()

        @pl.when(jnp.logical_not(again))
        def _(index=index, rows=rows, arrived=arrived):
            pltpu.make_async_copy(arrived, rest.at[:, rows], sems.at[index]).start()

    for index, (rows, arrived) in enumerate(halves):
        pltpu.make_async_copy(arrived, rest.at[:, rows], sems.at[index]).wait()


def keep_last(rows, ctl, arrived, before, out, sems):
    del before
    copy = pltpu.make_async_copy(arrived, out.at[ctl[MOVE + 1], :, rows], sems.at[0])
    copy.start()
    copy.wait()


def vmem():
    return pl.BlockSpec(memory_space=pltpu.VMEM)


def smem():
    return pl.BlockSpec(memory_space=pltpu.SMEM)


def hbm():
    return pl.BlockSpec(memory_space=pltpu.HBM)


def anywhere():
    return pl.BlockSpec(memory_space=pl.ANY)


def call(kernel, outs, out_specs, in_specs, flops, scratch=(), aliases=None, room=VMEM_BYTES):
    return pl.pallas_call(
        kernel,
        scratch_shapes=scratch,
        input_output_aliases=aliases or {},
        out_shape=outs,
        in_specs=in_specs,
        out_specs=out_specs,
        compiler_params=pltpu.CompilerParams(vmem_limit_bytes=room),
        cost_estimate=pl.CostEstimate(flops=flops, bytes_accessed=4 << 20, transcendentals=0),
    )


def f32(*shape):
    return jax.ShapeDtypeStruct(shape, jnp.float32)


def spread(fast):
    return lax.all_to_all(fast, ("xb", "yb"), split_axis=0, concat_axis=0, tiled=True)


def body(state, bed, manning, neighbours, wet, moves):
    shape = f32(*state.shape)
    half_shape = f32(3, HALF, TILE)
    devices = lax.axis_size("xb") * lax.axis_size("yb")
    sem = [pltpu.SemaphoreType.DMA((1,))]
    whole = pltpu.VMEM(state.shape, jnp.float32)
    part = pltpu.VMEM(bed.shape, jnp.float32)
    out, columns, ctl = call(
        opening,
        (
            f32(16 * devices, TILE),
            f32(8, TILE),
            jax.ShapeDtypeStruct((CONTROLS,), jnp.int32),
        ),
        (vmem(), vmem(), smem()),
        [hbm()] * 5,
        4 << 20,
        [
            whole,
            part,
            pltpu.SMEM(neighbours.shape[::-1], jnp.int32),
            pltpu.SMEM(wet.shape, jnp.int32),
            pltpu.SMEM(moves.shape, jnp.int32),
            pltpu.SemaphoreType.DMA((6,)),
        ],
    )(state, bed, neighbours.T, wet, moves)
    ground = None
    for step in range(STEPS):
        got = spread(out)
        ground = got if step == 0 else ground
        rate = call(
            rates,
            shape,
            hbm(),
            [smem(), hbm(), hbm()],
            16 << 20,
            [whole, part, whole, pltpu.SemaphoreType.DMA((3 * CHUNKS,))],
        )(ctl, state, bed)
        more = step + 1 < STEPS
        extra = (f32(8 * devices, TILE), f32(8, TILE)) if more else (half_shape, half_shape)
        outs = call(
            functools.partial(update, step),
            (shape,) + extra,
            (hbm(),) * 3,
            [smem()] + [hbm()] * 6,
            8 << 20,
            [
                whole,
                part,
                whole,
                whole,
                pltpu.VMEM(got.shape, jnp.float32),
                pltpu.VMEM(ground.shape, jnp.float32),
                pltpu.VMEM((8, TILE), jnp.float32),
                pltpu.VMEM((8 * devices, TILE), jnp.float32),
                pltpu.VMEM((8, TILE), jnp.float32),
                pltpu.SemaphoreType.DMA((5 * PARTS + 3,)),
            ],
        )(ctl, got, ground, columns, state, manning, rate)
        state = outs[0]
        if more:
            _, out, columns = outs
    halves = (slice(0, HALF), slice(HALF, TILE))
    room = 1 << 20
    arrived = [shifted(leaving, "xb", 1) for leaving in outs[1:]]
    arrived_next = []
    for rows, got in zip(halves, arrived):
        leaving = call(
            functools.partial(second_leaving, rows),
            half_shape,
            anywhere(),
            [smem(), anywhere(), anywhere()],
            1 << 20,
            sem,
            room=room,
        )(ctl, state, got)
        arrived_next.append(shifted(leaving, "xb", 1))
    final = call(
        keep_rest,
        shape,
        hbm(),
        [smem(), anywhere(), anywhere(), anywhere()],
        1 << 20,
        [pltpu.SemaphoreType.DMA((2,))],
        room=room,
    )(ctl, state, *arrived)
    for rows, got in zip(halves, arrived_next):
        final = call(
            functools.partial(keep_last, rows),
            shape,
            hbm(),
            [smem(), anywhere(), hbm()],
            1 << 20,
            sem,
            {2: 0},
            room=room,
        )(ctl, got, final)
    return final


def solution(mesh):
    placed = (
        P(("runs", "xb", "yb"), None, None, None),
        P(("runs", "xb", "yb"), None, None),
        P(("runs", "xb", "yb"), None, None),
        P("runs", None),
        P(None, "runs"),
        P(None, "runs"),
    )
    return jax.shard_map(
        body,
        mesh=mesh,
        in_specs=placed,
        out_specs=P(("runs", "xb", "yb"), None, None, None),
        check_vma=False,
    )
```

```python
import functools

import jax
import jax.numpy as jnp
from jax import lax
from jax.experimental import pallas as pl
from jax.experimental.pallas import tpu as pltpu
from jax.sharding import PartitionSpec as P

STEPS = 3
GRAVITY = 9.81
ROOT_G = GRAVITY**0.5
SPACING = 5.0
COURANT = 0.2
ROWS = 32
LANES = 128
TILE = 256
VMEM_BYTES = 60 * 1024 * 1024
SLOT_LOW, WALL_WEST, WALL_EAST, WALL_OUTER, WET, MOVE = 0, 1, 3, 5, 7, 13
WET_FIRST, WET_SECOND = 16, 19
CONTROLS = 24
EARLY = 96
LATE = (TILE - EARLY + 16) // 2
CUT = TILE - LATE
CHUNKS = 8
PARTS = 8
STRIP = 16
TOP = 6
SCALE = 0.5 / SPACING
SLOPE = GRAVITY / (2.0 * SPACING)


def shifted(value, axis, steps, around=True):
    count = lax.axis_size(axis)
    pairs = [(source, (source + steps) % count) for source in range(count)]
    if not around:
        pairs = [pair for pair in pairs if abs(pair[0] - pair[1]) == abs(steps)]
    return lax.ppermute(value, axis, pairs)


def cell(h, hu, hv):
    root = lax.rsqrt(h)
    inverse = root * root
    u = hu * inverse
    v = hv * inverse
    celerity = ROOT_G * (h * root)
    pressure = (0.5 * GRAVITY) * (h * h)
    cross = hu * v
    speed_x = jnp.abs(u) + celerity
    speed_y = jnp.abs(v) + celerity
    along_x = (h, hu, hv, hu * u + pressure, cross, speed_x)
    along_y = (h, hv, hu, hv * v + pressure, cross, speed_y)
    return along_x, along_y


def face(left, right):
    wave = jnp.maximum(left[5], right[5])
    return (
        (left[1] + right[1]) - wave * (right[0] - left[0]),
        (left[3] + right[3]) - wave * (right[1] - left[1]),
        (left[4] + right[4]) - wave * (right[2] - left[2]),
    )


def slot_of(ctl, position):
    low = ctl[SLOT_LOW]
    return low if position == 0 else 1 - low


def flag(ctl, index):
    return ctl[index] > 0


def start_all(pairs, sems, first=0):
    copies = [
        pltpu.make_async_copy(src, dst, sems.at[first + k]) for k, (src, dst) in enumerate(pairs)
    ]
    for copy in copies:
        copy.start()
    return copies


def wait_all(copies):
    for copy in copies:
        copy.wait()


def sublanes(width=TILE):
    return lax.broadcasted_iota(jnp.int32, (8, width), 0)


def stacked(lines, base):
    row = sublanes()
    for index, line in enumerate(lines):
        base = jnp.where(row == index, jnp.broadcast_to(line, (8, TILE)), base)
    return base


def messages(ctl, state, bed, fastest, out, columns):
    upper = lax.axis_index("yb")
    column = lax.axis_index("xb")
    last = lax.axis_size("xb") - 1
    devices = 2 * (last + 1)
    block = out.shape[0] // devices
    device = column * 2 + upper
    top = jnp.broadcast_to(fastest, (8, TILE))
    for peer in range(devices):
        out[peer * block : peer * block + 8, :] = top
    row = sublanes()

    def edge(line):
        rows = slice(line, line + 1)
        slots = [slot_of(ctl, position) for position in range(2)]
        fields = [state[slot, field, rows, :] for slot in slots for field in range(3)]
        return stacked(fields, top), [bed[slot, rows, :] for slot in slots] if bed is not None else None

    for inside, peer, line in (
        (column > 0, device - 2, 0),
        (column < last, device + 2, TILE - 1),
    ):

        @pl.when(inside)
        def _(peer=peer, line=line):
            lines, ground = edge(line)
            start = pl.multiple_of(peer * block, 8)
            out[pl.ds(start, 8), :] = lines
            if ground:
                out[pl.ds(pl.multiple_of(start + 8, 8), 8), :] = stacked(ground, top)

    slot = jnp.where(upper > 0, ctl[SLOT_LOW], 1 - ctl[SLOT_LOW])
    begin = pl.multiple_of((1 - upper) * LANES, LANES)
    lane = lax.broadcasted_iota(jnp.int32, (TILE, LANES), 1)
    packed = None
    for field in range(4 if bed is not None else 3):
        if field < 3:
            part = state[slot, field, :, pl.ds(begin, LANES)]
        else:
            part = bed[slot, :, pl.ds(begin, LANES)]
        turned = pltpu.roll(part, field + 1 - upper, 1)
        packed = turned if field == 0 else jnp.where(lane == field, turned, packed)
    lines = jnp.transpose(packed)[:8]
    columns[...] = lines
    start = pl.multiple_of((device + 1 - 2 * upper) * block, 8)
    out[pl.ds(start, 8), :] = jnp.where(row == TOP, top, lines)


def opening(
    state_in, bed_in, manning_in, neighbours_in, wet_in, moves_in,
    out, columns, ctl, leaving,
    state, bed, manning, neighbours, wet, moves, sems,
):
    copies = start_all(
        (
            (neighbours_in, neighbours),
            (wet_in, wet),
            (moves_in, moves),
            (state_in.at[0], state.at[0]),
            (state_in.at[1], state.at[1]),
            (bed_in, bed),
        ),
        sems,
    )
    device = lax.axis_index("xb") * 2 + lax.axis_index("yb")
    wait_all(copies[:3])
    first = device * 2
    low = jnp.where(neighbours[3, first] == first + 1, 0, 1)
    ctl[SLOT_LOW] = low
    for position in range(2):
        slot = low if position == 0 else 1 - low
        tile = first + slot
        ctl[WALL_WEST + position] = (neighbours[0, tile] < 0).astype(jnp.int32)
        ctl[WALL_EAST + position] = (neighbours[1, tile] < 0).astype(jnp.int32)
        ctl[WALL_OUTER + position] = (neighbours[2 + position, tile] < 0).astype(jnp.int32)
    for step in range(STEPS):
        for slot in range(2):
            ctl[WET + 2 * step + slot] = wet[step, first + slot]
        ctl[MOVE + step] = moves[step, device]
    moving = moves[0, device]
    rough = start_all(((manning_in.at[moving, 0:EARLY], manning),), sems, 6)
    count = lax.axis_size("xb")
    upper = lax.axis_index("yb")
    column = lax.axis_index("xb")
    source = lax.rem(column + count - 1, count) * 2 + upper
    before = lax.rem(column + count - 2, count) * 2 + upper
    again = moves[0, source] == moves[1, source]
    tile_first = source * 2 + moves[0, source]
    tile_second = jnp.where(
        again, before * 2 + moves[0, before], source * 2 + 1 - moves[0, source]
    )
    for step in range(STEPS):
        ctl[WET_FIRST + step] = wet[step, tile_first]
        ctl[WET_SECOND + step] = wet[step, tile_second]

    total = jnp.zeros((ROWS, TILE), jnp.float32)
    for slot in range(2):
        copies[3 + slot].wait()

        def group(index, best, slot=slot):
            rows = pl.ds(pl.multiple_of(index * ROWS, ROWS), ROWS)
            along_x, along_y = cell(*(state[slot, field, rows, :] for field in range(3)))
            return jnp.maximum(best, jnp.maximum(along_x[5], along_y[5]))

        best = lax.fori_loop(0, TILE // ROWS, group, jnp.zeros((ROWS, TILE), jnp.float32))
        total = jnp.maximum(total, jnp.where(wet[0, first + slot] > 0, best, 0.0))
    copies[5].wait()
    wait_all(rough)
    early = start_all(
        (
            (state.at[moving, :, 0:EARLY], leaving.at[0:3]),
            (bed.at[moving, 0:EARLY], leaving.at[3]),
            (manning, leaving.at[4]),
        ),
        sems,
        7,
    )
    messages(ctl, state, bed, jnp.max(total, keepdims=True), out, columns)
    wait_all(early)


def hold(order, leaving, same):
    del order, leaving, same


class Passing:
    def __init__(self, ctl, state_in, bed_in, manning_in, arrived, leaving, buffer, sems):
        self.again = ctl[MOVE] == ctl[MOVE + 1]
        self.other = 1 - ctl[MOVE]
        self.refs = state_in, bed_in, manning_in, arrived, leaving, buffer, sems

    def start(self):
        state_in, bed_in, manning_in, arrived, _, buffer, sems = self.refs
        rows = slice(0, EARLY)
        sem = sems.at[0]

        @pl.when(self.again)
        def _():
            pltpu.make_async_copy(arrived, buffer, sem).start()

        @pl.when(jnp.logical_not(self.again))
        def _():
            pltpu.make_async_copy(state_in.at[self.other, :, rows], buffer.at[0:3], sem).start()
            pltpu.make_async_copy(bed_in.at[self.other, rows], buffer.at[3], sem).start()
            pltpu.make_async_copy(manning_in.at[self.other, rows], buffer.at[4], sem).start()

    def middle(self):
        _, _, _, arrived, leaving, buffer, sems = self.refs
        pltpu.make_async_copy(arrived, buffer, sems.at[0]).wait()
        pltpu.make_async_copy(buffer, leaving, sems.at[1]).start()

    def end(self):
        _, _, _, _, leaving, buffer, sems = self.refs
        pltpu.make_async_copy(buffer, leaving, sems.at[1]).wait()


def rates_and_leaving(
    ctl, state_in, bed_in, state_first, manning_in, arrived, rate_out, leaving,
    state, bed, rate, sems, buffer, moving,
):
    passing = Passing(ctl, state_first, bed_in, manning_in, arrived, leaving, buffer, moving)
    rates(ctl, state_in, bed_in, rate_out, state, bed, rate, sems, passing)


def rates(ctl, state_in, bed_in, rate_out, state, bed, rate, sems, passing=None):
    width = 2 * TILE
    row_ids = lax.broadcasted_iota(jnp.int32, (STRIP, width), 0)
    row8 = sublanes(width)
    lane = lax.broadcasted_iota(jnp.int32, (STRIP, LANES), 1)
    last = TILE // STRIP - 1
    chunk = TILE // CHUNKS
    slots = [slot_of(ctl, position) for position in range(2)]
    incoming = []
    for part in range(CHUNKS):
        rows = slice(part * chunk, (part + 1) * chunk)
        incoming.append(
            start_all(
                (
                    (state_in.at[:, :, rows], state.at[:, :, rows]),
                    (bed_in.at[:, rows], bed.at[:, rows]),
                ),
                sems,
                2 * part,
            )
        )
    if passing:
        passing.start()
    keep_west, keep_east, keep_south, keep_north = (
        jnp.where(flag(ctl, index), 1.0, 0.0)
        for index in (WALL_WEST, WALL_EAST, WALL_OUTER, WALL_OUTER + 1)
    )

    def strip(field, rows):
        if field == 3:
            return jnp.concatenate([bed[slot, rows, :] for slot in slots], 1)
        return jnp.concatenate([state[slot, field, rows, :] for slot in slots], 1)

    def blocks(value):
        return [value[:, k * LANES : (k + 1) * LANES] for k in range(4)]

    def right_of(value, end=None):
        turned = [pltpu.roll(part, LANES - 1, 1) for part in blocks(value)]
        after = turned[1:] + [turned[3] if end is None else end]
        return jnp.concatenate(
            [
                jnp.where(lane == LANES - 1, following, part)
                if following is not part
                else part
                for part, following in zip(turned, after)
            ],
            1,
        )

    def left_of(value, end):
        turned = [pltpu.roll(part, 1, 1) for part in blocks(value)]
        before = [end] + turned[:3]
        return jnp.concatenate(
            [jnp.where(lane == 0, previous, part) for part, previous in zip(turned, before)], 1
        )

    def down(value):
        return pltpu.roll(value, STRIP + 7, 0)[:STRIP]

    def group(index, carry):
        base = pl.multiple_of(index * STRIP, STRIP)
        rows = pl.ds(base, STRIP)
        after = pl.ds(pl.multiple_of(jnp.minimum(base + STRIP, TILE - 8), 8), 8)
        at_end = index == last
        fields = [
            jnp.concatenate([strip(field, rows), strip(field, after)], 0) for field in range(3)
        ]
        cells_x, cells_y = cell(*fields)
        here_x = tuple(value[:STRIP] for value in cells_x)
        here_y = tuple(value[:STRIP] for value in cells_y)

        ending = jnp.logical_and(row8 == 7, at_end)
        faces = list(face(here_x, tuple(down(value) for value in cells_x)))
        wall = keep_east * (2.0 * (here_x[3] + here_x[5] * here_x[1])[STRIP - 8 :])
        for component, value in enumerate((0.0, wall, 0.0)):
            upper = faces[component]
            faces[component] = jnp.concatenate(
                [upper[: STRIP - 8], jnp.where(ending, value, upper[STRIP - 8 :])], 0
            )
        turned = tuple(pltpu.roll(value, 1, 0) for value in faces)
        change_x = tuple(
            value - jnp.where(row_ids == 0, before, moved)
            for value, before, moved in zip(faces, carry[:3], turned)
        )
        ground = strip(3, rows)
        ground_after = jnp.where(
            at_end,
            jnp.broadcast_to(keep_east * ground[STRIP - 1 :], (8, width)),
            strip(3, after),
        )
        ground_up = pltpu.roll(ground, 1, 0)
        slope_x = down(jnp.concatenate([ground, ground_after], 0)) - jnp.where(
            row_ids == 0, carry[3], ground_up
        )
        carried = tuple(value[0:1, :] for value in turned) + (ground_up[0:1, :],)

        faces_y = list(face(here_y, tuple(right_of(value) for value in here_y)))
        normal = here_y[3]
        spread_y = here_y[5] * here_y[1]
        north = keep_north * (2.0 * (normal + spread_y)[:, width - LANES :])
        south = keep_south * (2.0 * (normal - spread_y)[:, :LANES])
        change_y = []
        for component, (high, low) in enumerate(((0.0, 0.0), (north, south), (0.0, 0.0))):
            parts = blocks(faces_y[component])
            parts[3] = jnp.where(lane == LANES - 1, high, parts[3])
            value = jnp.concatenate(parts, 1)
            change_y.append(value - left_of(value, low))
        slope_y = right_of(ground, keep_north * ground[:, width - LANES :]) - left_of(
            ground, keep_south * ground[:, :LANES]
        )
        weight = SLOPE * here_x[0]
        results = (
            SCALE * (change_x[0] + change_y[0]),
            SCALE * (change_x[1] + change_y[2]) + weight * slope_x,
            SCALE * (change_x[2] + change_y[1]) + weight * slope_y,
        )
        for field, value in enumerate(results):
            for position, slot in enumerate(slots):
                rate[slot, field, rows, :] = value[:, position * TILE : (position + 1) * TILE]
        return carried

    wait_all(incoming[0])
    top, _ = cell(*(strip(field, slice(0, 8)) for field in range(3)))
    nothing = jnp.zeros((1, width), jnp.float32)
    carry = (
        nothing,
        keep_west * (2.0 * (top[3] - top[5] * top[1])[0:1]),
        nothing,
        keep_west * strip(3, slice(0, 8))[0:1],
    )
    per_chunk = chunk // STRIP
    outgoing = []
    for part in range(CHUNKS):
        if part + 1 < CHUNKS:
            wait_all(incoming[part + 1])
        carry = lax.fori_loop(part * per_chunk, (part + 1) * per_chunk, group, carry)
        rows = slice(part * chunk, (part + 1) * chunk)
        outgoing += start_all(
            ((rate.at[:, :, rows], rate_out.at[:, :, rows]),), sems, 2 * CHUNKS + part
        )
        if passing and part == CHUNKS // 2:
            passing.middle()
    wait_all(outgoing)
    if passing:
        passing.end()


def moved_on(old, slopes, rough, delta, wet_now):
    h, hu, hv = (value - delta * slope for value, slope in zip(old, slopes))
    inverse = 1.0 / h
    u = hu * inverse
    v = hv * inverse
    speed = jnp.sqrt(u * u + v * v)
    power = jnp.exp((-4.0 / 3.0) * jnp.log(jnp.abs(h)))
    drag = (GRAVITY * delta) * (rough * rough) * (speed * power)
    factor = 1.0 / (1.0 + drag)
    fresh = (h, hu * factor, hv * factor)
    return tuple(jnp.where(wet_now, new, value) for new, value in zip(fresh, old))


def repeat_steps(ctl, wet_from, deltas, early, work, other, sems):
    chunk = EARLY // 3
    incoming = []
    for part in range(3):
        rows = slice(part * chunk, (part + 1) * chunk)
        incoming += start_all(((early.at[:, rows], work.at[:, rows]),), sems, part)
    row_ids = lax.broadcasted_iota(jnp.int32, (ROWS, TILE), 0)
    lane = lax.broadcasted_iota(jnp.int32, (ROWS, LANES), 1)
    start = tuple(jnp.zeros((1, TILE), jnp.float32) for _ in range(4))

    def halves(value):
        return value[:, :LANES], value[:, LANES:]

    def right_of(value):
        low, high = (pltpu.roll(part, LANES - 1, 1) for part in halves(value))
        return jnp.concatenate([jnp.where(lane == LANES - 1, high, low), high], 1)

    def left_of(value):
        low, high = (pltpu.roll(part, 1, 1) for part in halves(value))
        return jnp.concatenate([low, jnp.where(lane == 0, low, high)], 1)

    def down(value):
        return pltpu.roll(value, ROWS + 7, 0)[:ROWS]

    for step in range(STEPS):
        source, target = (work, other) if step % 2 == 0 else (other, work)
        delta = deltas[step][0:1, :]
        wet_now = flag(ctl, wet_from + step)

        def group(index, carry, source=source, target=target, delta=delta, wet_now=wet_now):
            base = pl.multiple_of(index * ROWS, ROWS)
            rows = pl.ds(base, ROWS)
            after = pl.ds(pl.multiple_of(jnp.minimum(base + ROWS, EARLY - 8), 8), 8)
            refs = [source.at[field] for field in range(3)] + [work.at[3]]
            fields = [jnp.concatenate([ref[rows, :], ref[after, :]], 0) for ref in refs]
            cells_x, cells_y = cell(*fields[:3])
            here_x = tuple(value[:ROWS] for value in cells_x)
            here_y = tuple(value[:ROWS] for value in cells_y)
            faces_x = face(here_x, tuple(down(value) for value in cells_x))
            turned = tuple(pltpu.roll(value, 1, 0) for value in faces_x)
            change_x = tuple(
                value - jnp.where(row_ids == 0, before, moved)
                for value, before, moved in zip(faces_x, carry[:3], turned)
            )
            ground = fields[3][:ROWS]
            ground_up = pltpu.roll(ground, 1, 0)
            slope_x = down(fields[3]) - jnp.where(row_ids == 0, carry[3], ground_up)
            carried = tuple(value[0:1, :] for value in turned) + (ground_up[0:1, :],)
            faces_y = face(here_y, tuple(right_of(value) for value in here_y))
            change_y = tuple(value - left_of(value) for value in faces_y)
            slope_y = right_of(ground) - left_of(ground)
            old = tuple(value[:ROWS] for value in fields[:3])
            weight = SLOPE * old[0]
            slopes = (
                SCALE * (change_x[0] + change_y[0]),
                SCALE * (change_x[1] + change_y[2]) + weight * slope_x,
                SCALE * (change_x[2] + change_y[1]) + weight * slope_y,
            )
            for field, value in enumerate(
                moved_on(old, slopes, work[4, rows, :], delta, wet_now)
            ):
                target[field, rows, :] = value
            return carried

        per_chunk = chunk // ROWS
        if step == 0:
            carry = start
            incoming[0].wait()
            for part in range(3):
                if part < 2:
                    incoming[part + 1].wait()
                carry = lax.fori_loop(part * per_chunk, (part + 1) * per_chunk, group, carry)
        else:
            lax.fori_loop(0, EARLY // ROWS, group, start)


def late_rows(tile, late):
    row = sublanes()
    kept = EARLY - 8
    lane = lax.broadcasted_iota(jnp.int32, (8, LANES), 1)
    for field in range(3):
        late[field, 0:8, :] = jnp.where(
            row < 3, tile[field, 0:8, :], tile[field, kept : kept + 8, :]
        )
        packed = [jnp.zeros((8, LANES), jnp.float32)] * 2
        for block in range(EARLY // 8):
            rows = slice(8 * block, 8 * block + 8)
            sides = jnp.where(lane < 64, tile[field, rows, :LANES], tile[field, rows, LANES:])
            turned = pltpu.roll(sides, (3 + 8 * block) % LANES, 1)
            which = block // 16
            packed[which] = jnp.where(lane // 8 == block % 16, turned, packed[which])
        late[field, 8:16, :] = jnp.concatenate(packed, 1)
        late[field, 16:, :] = tile[field, EARLY:CUT, :]


def merge(late, early, tile):
    row = sublanes()
    lane = lax.broadcasted_iota(jnp.int32, (8, LANES), 1)
    for field in range(3):
        first = late[field, 0:8, :]
        for block in range(EARLY // 8):
            rows = slice(8 * block, 8 * block + 8)
            which = block // 16
            packed = late[field, 8:16, which * LANES : (which + 1) * LANES]
            sides = pltpu.roll(packed, (-3 - 8 * block) % LANES, 1)
            value = early[field, rows, :]
            value = jnp.concatenate(
                [
                    jnp.where(lane < 3, sides, value[:, :LANES]),
                    jnp.where(lane >= LANES - 3, sides, value[:, LANES:]),
                ],
                1,
            )
            if block == 0:
                value = jnp.where(row < 3, first, value)
            if block == EARLY // 8 - 1:
                value = jnp.where(row < 5, value, first)
            tile[field, rows, :] = value
        tile[field, EARLY:, :] = late[field, 16:, :]


def repeat_second(ctl, delta0, delta1, delta2, early, out, work, tile, sems):
    repeat_steps(ctl, WET_SECOND, (delta0, delta1, delta2), early, work, tile, sems)
    copy = pltpu.make_async_copy(tile, out, sems.at[0])
    copy.start()
    copy.wait()


def repeat_first(
    ctl, delta0, delta1, delta2, early, late_in, plain_in, staying, out,
    work, other, tile, late, sems,
):
    rest = out.at[1 - ctl[MOVE + 1]]
    again = ctl[MOVE] == ctl[MOVE + 1]
    low, high = tile.at[:, :CUT], tile.at[:, CUT:]

    @pl.when(again)
    def _():
        copy = pltpu.make_async_copy(staying, tile, sems.at[3])
        copy.start()
        copy.wait()

    @pl.when(jnp.logical_not(again))
    def _():
        copies = start_all(((late_in, late), (plain_in, high)), sems, 3)
        repeat_steps(ctl, WET_FIRST, (delta0, delta1, delta2), early, work, other, sems)
        wait_all(copies)
        merge(late, other, low)

    copy = pltpu.make_async_copy(tile, rest, sems.at[3])
    copy.start()
    copy.wait()


def finish_low(ctl, late_in, early_in, before, out, late, early, tile, sems):
    del before
    wait_all(start_all(((late_in, late), (early_in, early)), sems))
    merge(late, early, tile)
    wait_all(start_all(((tile, out.at[ctl[MOVE + 1], :, 0:CUT]),), sems))


def finish_high(ctl, plain_in, before, out, plain, sems):
    del before
    wait_all(start_all(((plain_in, plain),), sems))
    wait_all(start_all(((plain, out.at[ctl[MOVE + 1], :, CUT:]),), sems))


def second_late(is_low, ctl, arrived, own, order, leaving, buffer, sems):
    del order
    again = ctl[MOVE] == ctl[MOVE + 1]

    @pl.when(again)
    def _():
        pltpu.make_async_copy(arrived, buffer, sems.at[0]).start()

    @pl.when(jnp.logical_not(again))
    def _():
        source = own if is_low else own.at[:, CUT:]
        pltpu.make_async_copy(source, buffer, sems.at[0]).start()

    pltpu.make_async_copy(arrived, buffer, sems.at[0]).wait()
    wait_all(start_all(((buffer, leaving),), sems))


def correct_rows(ctl, slot, got, ground, block, state, rate, bottom):
    position = jnp.where(ctl[SLOT_LOW] == slot, 0, 1)
    device = lax.axis_index("xb") * 2 + lax.axis_index("yb")
    wall = WALL_WEST if bottom else WALL_EAST

    @pl.when(jnp.logical_not(flag(ctl, wall + position)))
    def _():
        peer = device - 2 if bottom else device + 2
        lines = got[pl.ds(pl.multiple_of(peer * block, 8), 8), :]
        grounds = ground[pl.ds(pl.multiple_of(peer * 16 + 8, 8), 8), :]

        def line(value, offset):
            picked = jnp.where(
                position == 0, value[offset : offset + 1, :], value[offset + 3 : offset + 4, :]
            )
            return jnp.broadcast_to(picked, (8, TILE))

        ghost, _ = cell(*(line(lines, field) for field in range(3)))
        ghost_ground = jnp.where(position == 0, grounds[0:1, :], grounds[1:2, :])
        rows = slice(0, 8) if bottom else slice(TILE - 8, TILE)
        own = [state[slot, field, rows, :] for field in range(3)]
        here, _ = cell(*own)
        fluxes = face(ghost, here) if bottom else face(here, ghost)
        push = SCALE * fluxes[1] + (SLOPE * own[0]) * ghost_ground
        row = sublanes()
        sign = -1.0 if bottom else 1.0
        chosen = row == (0 if bottom else 7)
        for field, value in enumerate((SCALE * fluxes[0], push, SCALE * fluxes[2])):
            rate[slot, field, rows, :] += jnp.where(chosen, sign * value, 0.0)


def column_fix(got, ground, block, columns, bed_columns):
    upper = lax.axis_index("yb")
    device = lax.axis_index("xb") * 2 + upper
    peer = device + 1 - 2 * upper
    lines = got[pl.ds(pl.multiple_of(peer * block, 8), 8), :]
    ghost_ground = ground[pl.ds(pl.multiple_of(peer * 16, 8), 8), :][3:4]
    del bed_columns
    mine = columns[...]
    _, ghost = cell(lines[0:1], lines[1:2], lines[2:3])
    _, own = cell(mine[0:1], mine[1:2], mine[2:3])
    low = upper == 0
    left = tuple(jnp.where(low, a, b) for a, b in zip(own, ghost))
    right = tuple(jnp.where(low, b, a) for a, b in zip(own, ghost))
    fluxes = face(left, right)
    sign = jnp.where(low, 1.0, -1.0)
    push = SCALE * fluxes[1] + (SLOPE * mine[0:1]) * ghost_ground
    block8 = stacked(
        [sign * SCALE * fluxes[0], sign * SCALE * fluxes[2], sign * push],
        jnp.zeros((8, TILE), jnp.float32),
    )
    return jnp.transpose(
        jnp.concatenate([block8, jnp.zeros((LANES - 8, TILE), jnp.float32)], 0)
    )


def update(step, ctl, got_in, ground_in, columns_in, state_in, manning_in, rate_in, *rest):
    more = step + 1 < STEPS
    if more:
        fresh_out, out_to, columns_to, delta_out = rest[:4]
    else:
        staying, late_first, late_second, plain_first, delta_out = rest[:5]
    rest = rest[4 if more else 5 :]
    state, manning, rate, fresh, got, ground, columns, out, columns_out, sems = rest
    small = start_all(
        ((got_in, got), (ground_in, ground), (columns_in, columns)), sems, 5 * PARTS
    )
    size = 2 * TILE // PARTS
    parts = [
        (slot, slice(k * size, (k + 1) * size)) for slot in range(2) for k in range(PARTS // 2)
    ]
    incoming = []
    for index, (slot, rows) in enumerate(parts):
        incoming.append(
            start_all(
                (
                    (rate_in.at[slot, :, rows], rate.at[slot, :, rows]),
                    (state_in.at[slot, :, rows], state.at[slot, :, rows]),
                    (manning_in.at[slot, rows], manning.at[slot, rows]),
                ),
                sems,
                3 * index,
            )
        )
    wait_all(small)
    upper = lax.axis_index("yb")
    devices = 2 * lax.axis_size("xb")
    block = got.shape[0] // devices
    tops = got[0:8, :]
    for peer in range(1, devices):
        tops = jnp.maximum(tops, got[peer * block : peer * block + 8, :])
    delta = (COURANT * SPACING) / tops[TOP : TOP + 1, :]
    delta_out[...] = jnp.broadcast_to(delta, (8, TILE))
    fix = column_fix(got, ground, block, columns, None)
    facing = jnp.where(upper > 0, ctl[SLOT_LOW], 1 - ctl[SLOT_LOW])
    begin = pl.multiple_of((1 - upper) * LANES, LANES)
    target = (1 - upper) * (LANES - 1)
    lane = lax.broadcasted_iota(jnp.int32, (size, LANES), 1)
    total = jnp.zeros((ROWS, TILE), jnp.float32)
    outgoing = []
    for index, (slot, part_rows) in enumerate(parts):
        wait_all(incoming[index])
        if part_rows.start == 0:
            correct_rows(ctl, slot, got, ground, block, state, rate, True)
        if part_rows.stop == TILE:
            correct_rows(ctl, slot, got, ground, block, state, rate, False)

        @pl.when(facing == slot)
        def _(slot=slot, part_rows=part_rows):
            for field in range(3):
                turned = pltpu.roll(
                    fix[part_rows], lax.rem(target + LANES - field, LANES), 1
                )
                rate[slot, field, part_rows, pl.ds(begin, LANES)] += jnp.where(
                    lane == target, turned, 0.0
                )

        wet_now = flag(ctl, WET + 2 * step + slot)

        def group(index, best, slot=slot, wet_now=wet_now):
            rows = pl.ds(pl.multiple_of(index * ROWS, ROWS), ROWS)
            old = tuple(state[slot, field, rows, :] for field in range(3))
            slopes = tuple(rate[slot, field, rows, :] for field in range(3))
            h, hu, hv = moved_on(old, slopes, manning[slot, rows, :], delta, wet_now)
            fresh[slot, 0, rows, :] = h
            fresh[slot, 1, rows, :] = hu
            fresh[slot, 2, rows, :] = hv
            if more:
                along_x, along_y = cell(h, hu, hv)
                best = jnp.maximum(best, jnp.maximum(along_x[5], along_y[5]))
            return best

        best = lax.fori_loop(
            part_rows.start // ROWS,
            part_rows.stop // ROWS,
            group,
            jnp.zeros((ROWS, TILE), jnp.float32),
        )
        if more:
            best = jnp.where(flag(ctl, WET + 2 * step + 2 + slot), best, 0.0)
            total = jnp.maximum(total, best)
        if more:
            outgoing += start_all(
                ((fresh.at[slot, :, part_rows], fresh_out.at[slot, :, part_rows]),),
                sems,
                3 * PARTS + index,
            )
    if more:
        messages(ctl, fresh, None, jnp.max(total, keepdims=True), out, columns_out)
        outgoing += start_all(((out, out_to), (columns_out, columns_to)), sems, 4 * PARTS)
    else:
        first, second = fresh.at[ctl[MOVE]], fresh.at[1 - ctl[MOVE]]
        outgoing += start_all(
            ((first.at[:, CUT:], plain_first), (second, staying)), sems, 4 * PARTS
        )
        late_rows(first, late_first)
        late_rows(second, late_second)
    wait_all(outgoing)


def vmem():
    return pl.BlockSpec(memory_space=pltpu.VMEM)


def smem():
    return pl.BlockSpec(memory_space=pltpu.SMEM)


def hbm():
    return pl.BlockSpec(memory_space=pltpu.HBM)


def anywhere():
    return pl.BlockSpec(memory_space=pl.ANY)


def call(kernel, outs, out_specs, in_specs, flops, scratch=(), aliases=None, room=VMEM_BYTES):
    return pl.pallas_call(
        kernel,
        scratch_shapes=scratch,
        input_output_aliases=aliases or {},
        out_shape=outs,
        in_specs=in_specs,
        out_specs=out_specs,
        compiler_params=pltpu.CompilerParams(vmem_limit_bytes=room),
        cost_estimate=pl.CostEstimate(flops=flops, bytes_accessed=4 << 20, transcendentals=0),
    )


def f32(*shape):
    return jax.ShapeDtypeStruct(shape, jnp.float32)


def spread(fast):
    return lax.all_to_all(fast, ("xb", "yb"), split_axis=0, concat_axis=0, tiled=True)


def body(state, bed, manning, neighbours, wet, moves):
    shape = f32(*state.shape)
    devices = lax.axis_size("xb") * lax.axis_size("yb")
    sem = [pltpu.SemaphoreType.DMA((1,))]
    whole = pltpu.VMEM(state.shape, jnp.float32)
    part = pltpu.VMEM(bed.shape, jnp.float32)
    tile_shape = f32(*state.shape[1:])
    early_shape = f32(5, EARLY, TILE)
    early_state = f32(3, EARLY, TILE)
    late_shape = f32(3, LATE, TILE)
    delta_shape = f32(8, TILE)

    def buffer(like):
        return pltpu.VMEM(like.shape, jnp.float32)

    out, columns, ctl, leaving = call(
        opening,
        (
            f32(16 * devices, TILE),
            f32(8, TILE),
            jax.ShapeDtypeStruct((CONTROLS,), jnp.int32),
            early_shape,
        ),
        (vmem(), vmem(), smem(), hbm()),
        [hbm()] * 6,
        4 << 20,
        [
            whole,
            part,
            pltpu.VMEM((EARLY, TILE), jnp.float32),
            pltpu.SMEM(neighbours.shape[::-1], jnp.int32),
            pltpu.SMEM(wet.shape, jnp.int32),
            pltpu.SMEM(moves.shape, jnp.int32),
            pltpu.SemaphoreType.DMA((10,)),
        ],
    )(state, bed, manning, neighbours.T, wet, moves)
    state_first = state
    ground = None
    deltas = []
    early = []
    for step in range(STEPS):
        got = spread(out)
        ground = got if step == 0 else ground
        scratch = [whole, part, whole, pltpu.SemaphoreType.DMA((3 * CHUNKS,))]
        if step == 1:
            rate, leaving = call(
                rates_and_leaving,
                (shape, early_shape),
                (hbm(), hbm()),
                [smem()] + [hbm()] * 5,
                16 << 20,
                scratch + [buffer(early_shape), pltpu.SemaphoreType.DMA((2,))],
            )(ctl, state, bed, state_first, manning, early[0])
        else:
            rate = call(rates, shape, hbm(), [smem(), hbm(), hbm()], 16 << 20, scratch)(
                ctl, state, bed
            )
        more = step + 1 < STEPS
        if more:
            leaving = call(
                hold, early_shape, hbm(), [hbm(), hbm()], 1 << 10, aliases={1: 0}
            )(got, leaving)
            early.append(shifted(leaving, "xb", 1))
            shapes = (shape, f32(8 * devices, TILE), f32(8, TILE), delta_shape)
            places = (hbm(), hbm(), hbm(), vmem())
        else:
            shapes = (tile_shape, late_shape, late_shape, late_shape, delta_shape)
            places = (hbm(), vmem(), vmem(), hbm(), vmem())
        outs = call(
            functools.partial(update, step),
            shapes,
            places,
            [smem()] + [hbm()] * 6,
            8 << 20,
            [
                whole,
                part,
                whole,
                whole,
                pltpu.VMEM(got.shape, jnp.float32),
                pltpu.VMEM(ground.shape, jnp.float32),
                pltpu.VMEM((8, TILE), jnp.float32),
                pltpu.VMEM((8 * devices, TILE), jnp.float32),
                pltpu.VMEM((8, TILE), jnp.float32),
                pltpu.SemaphoreType.DMA((5 * PARTS + 3,)),
            ],
        )(ctl, got, ground, columns, state, manning, rate)
        deltas.append(outs[-1])
        if more:
            state, out, columns, _ = outs
    staying, late_first, late_second, plain_first, _ = outs
    room = 16 << 20
    late_arrived = shifted(late_first, "xb", 1)
    plain_arrived = shifted(plain_first, "xb", 1)
    second = call(
        repeat_second,
        early_state,
        anywhere(),
        [smem()] + [vmem()] * 3 + [anywhere()],
        8 << 20,
        [buffer(early_shape), buffer(early_state), pltpu.SemaphoreType.DMA((3,))],
        room=room,
    )(ctl, *deltas, early[1])

    def pass_late(is_low, arrived, own):
        leaving = call(
            functools.partial(second_late, is_low),
            late_shape,
            anywhere(),
            [smem(), anywhere(), anywhere(), anywhere()],
            1 << 20,
            [buffer(late_shape)] + sem,
            room=room,
        )(ctl, arrived, own, second)
        return shifted(leaving, "xb", 1)

    late_next = pass_late(True, late_arrived, late_second)
    plain_next = pass_late(False, plain_arrived, staying)
    final = call(
        repeat_first,
        shape,
        hbm(),
        [smem()] + [vmem()] * 3 + [anywhere()] * 4,
        8 << 20,
        [
            buffer(early_shape),
            buffer(early_state),
            buffer(tile_shape),
            buffer(late_shape),
            pltpu.SemaphoreType.DMA((5,)),
        ],
        room=room,
    )(ctl, *deltas, early[0], late_arrived, plain_arrived, staying)
    final = call(
        finish_low,
        shape,
        hbm(),
        [smem(), anywhere(), anywhere(), hbm()],
        1 << 20,
        [
            buffer(late_shape),
            buffer(early_state),
            pltpu.VMEM((3, CUT, TILE), jnp.float32),
            pltpu.SemaphoreType.DMA((2,)),
        ],
        {3: 0},
        room=room,
    )(ctl, late_next, second, final)
    return call(
        finish_high,
        shape,
        hbm(),
        [smem(), anywhere(), hbm()],
        1 << 20,
        [buffer(late_shape)] + sem,
        {2: 0},
        room=room,
    )(ctl, plain_next, final)


def solution(mesh):
    placed = (
        P(("runs", "xb", "yb"), None, None, None),
        P(("runs", "xb", "yb"), None, None),
        P(("runs", "xb", "yb"), None, None),
        P("runs", None),
        P(None, "runs"),
        P(None, "runs"),
    )
    return jax.shard_map(
        body,
        mesh=mesh,
        in_specs=placed,
        out_specs=P(("runs", "xb", "yb"), None, None, None),
        check_vma=False,
    )
```

```python
import functools

import jax
import jax.numpy as jnp
from jax import lax
from jax.experimental import pallas as pl
from jax.experimental.pallas import tpu as pltpu
from jax.sharding import PartitionSpec as P

STEPS = 3
GRAVITY = 9.81
ROOT_G = GRAVITY**0.5
SPACING = 5.0
COURANT = 0.2
ROWS = 32
LANES = 128
TILE = 256
VMEM_BYTES = 60 * 1024 * 1024
SLOT_LOW, WALL_WEST, WALL_EAST, WALL_OUTER, WET, MOVE = 0, 1, 3, 5, 7, 13
WET_FIRST, WET_SECOND = 16, 19
CONTROLS = 24
EARLY = 160
PIECES = ((0, 80), (80, 160))
LATE = TILE - EARLY + 16
CHUNKS = 8
PARTS = 8
STRIP = 16
TOP = 6
SCALE = 0.5 / SPACING
SLOPE = GRAVITY / (2.0 * SPACING)


def shifted(value, axis, steps, around=True):
    count = lax.axis_size(axis)
    pairs = [(source, (source + steps) % count) for source in range(count)]
    if not around:
        pairs = [pair for pair in pairs if abs(pair[0] - pair[1]) == abs(steps)]
    return lax.ppermute(value, axis, pairs)


def cell(h, hu, hv):
    root = lax.rsqrt(h)
    inverse = root * root
    u = hu * inverse
    v = hv * inverse
    celerity = ROOT_G * (h * root)
    pressure = (0.5 * GRAVITY) * (h * h)
    cross = hu * v
    speed_x = jnp.abs(u) + celerity
    speed_y = jnp.abs(v) + celerity
    along_x = (h, hu, hv, hu * u + pressure, cross, speed_x)
    along_y = (h, hv, hu, hv * v + pressure, cross, speed_y)
    return along_x, along_y


def face(left, right):
    wave = jnp.maximum(left[5], right[5])
    return (
        (left[1] + right[1]) - wave * (right[0] - left[0]),
        (left[3] + right[3]) - wave * (right[1] - left[1]),
        (left[4] + right[4]) - wave * (right[2] - left[2]),
    )


def slot_of(ctl, position):
    low = ctl[SLOT_LOW]
    return low if position == 0 else 1 - low


def flag(ctl, index):
    return ctl[index] > 0


def start_all(pairs, sems, first=0):
    copies = [
        pltpu.make_async_copy(src, dst, sems.at[first + k]) for k, (src, dst) in enumerate(pairs)
    ]
    for copy in copies:
        copy.start()
    return copies


def wait_all(copies):
    for copy in copies:
        copy.wait()


def sublanes(width=TILE):
    return lax.broadcasted_iota(jnp.int32, (8, width), 0)


def stacked(lines, base):
    row = sublanes()
    for index, line in enumerate(lines):
        base = jnp.where(row == index, jnp.broadcast_to(line, (8, TILE)), base)
    return base


def messages(ctl, state, bed, fastest, out, columns):
    upper = lax.axis_index("yb")
    column = lax.axis_index("xb")
    last = lax.axis_size("xb") - 1
    devices = 2 * (last + 1)
    block = out.shape[0] // devices
    device = column * 2 + upper
    top = jnp.broadcast_to(fastest, (8, TILE))
    for peer in range(devices):
        out[peer * block : peer * block + 8, :] = top
    row = sublanes()

    def edge(line):
        rows = slice(line, line + 1)
        slots = [slot_of(ctl, position) for position in range(2)]
        fields = [state[slot, field, rows, :] for slot in slots for field in range(3)]
        return stacked(fields, top), [bed[slot, rows, :] for slot in slots] if bed is not None else None

    for inside, peer, line in (
        (column > 0, device - 2, 0),
        (column < last, device + 2, TILE - 1),
    ):

        @pl.when(inside)
        def _(peer=peer, line=line):
            lines, ground = edge(line)
            start = pl.multiple_of(peer * block, 8)
            out[pl.ds(start, 8), :] = lines
            if ground:
                out[pl.ds(pl.multiple_of(start + 8, 8), 8), :] = stacked(ground, top)

    slot = jnp.where(upper > 0, ctl[SLOT_LOW], 1 - ctl[SLOT_LOW])
    begin = pl.multiple_of((1 - upper) * LANES, LANES)
    lane = lax.broadcasted_iota(jnp.int32, (TILE, LANES), 1)
    packed = None
    for field in range(4 if bed is not None else 3):
        if field < 3:
            part = state[slot, field, :, pl.ds(begin, LANES)]
        else:
            part = bed[slot, :, pl.ds(begin, LANES)]
        turned = pltpu.roll(part, field + 1 - upper, 1)
        packed = turned if field == 0 else jnp.where(lane == field, turned, packed)
    lines = jnp.transpose(packed)[:8]
    columns[...] = lines
    start = pl.multiple_of((device + 1 - 2 * upper) * block, 8)
    out[pl.ds(start, 8), :] = jnp.where(row == TOP, top, lines)


def opening(
    state_in, bed_in, manning_in, neighbours_in, wet_in, moves_in,
    out, columns, ctl, leaving,
    state, bed, manning, neighbours, wet, moves, sems,
):
    copies = start_all(
        (
            (neighbours_in, neighbours),
            (wet_in, wet),
            (moves_in, moves),
            (state_in.at[0], state.at[0]),
            (state_in.at[1], state.at[1]),
            (bed_in, bed),
        ),
        sems,
    )
    device = lax.axis_index("xb") * 2 + lax.axis_index("yb")
    wait_all(copies[:3])
    first = device * 2
    low = jnp.where(neighbours[3, first] == first + 1, 0, 1)
    ctl[SLOT_LOW] = low
    for position in range(2):
        slot = low if position == 0 else 1 - low
        tile = first + slot
        ctl[WALL_WEST + position] = (neighbours[0, tile] < 0).astype(jnp.int32)
        ctl[WALL_EAST + position] = (neighbours[1, tile] < 0).astype(jnp.int32)
        ctl[WALL_OUTER + position] = (neighbours[2 + position, tile] < 0).astype(jnp.int32)
    for step in range(STEPS):
        for slot in range(2):
            ctl[WET + 2 * step + slot] = wet[step, first + slot]
        ctl[MOVE + step] = moves[step, device]
    moving = moves[0, device]
    rough = start_all(((manning_in.at[moving, 0:EARLY], manning),), sems, 6)
    count = lax.axis_size("xb")
    upper = lax.axis_index("yb")
    column = lax.axis_index("xb")
    source = lax.rem(column + count - 1, count) * 2 + upper
    before = lax.rem(column + count - 2, count) * 2 + upper
    again = moves[0, source] == moves[1, source]
    tile_first = source * 2 + moves[0, source]
    tile_second = jnp.where(
        again, before * 2 + moves[0, before], source * 2 + 1 - moves[0, source]
    )
    for step in range(STEPS):
        ctl[WET_FIRST + step] = wet[step, tile_first]
        ctl[WET_SECOND + step] = wet[step, tile_second]

    total = jnp.zeros((ROWS, TILE), jnp.float32)
    for slot in range(2):
        copies[3 + slot].wait()

        def group(index, best, slot=slot):
            rows = pl.ds(pl.multiple_of(index * ROWS, ROWS), ROWS)
            along_x, along_y = cell(*(state[slot, field, rows, :] for field in range(3)))
            return jnp.maximum(best, jnp.maximum(along_x[5], along_y[5]))

        best = lax.fori_loop(0, TILE // ROWS, group, jnp.zeros((ROWS, TILE), jnp.float32))
        total = jnp.maximum(total, jnp.where(wet[0, first + slot] > 0, best, 0.0))
    copies[5].wait()
    wait_all(rough)
    early = start_all(
        (
            (state.at[moving, :, 0:EARLY], leaving.at[0:3]),
            (bed.at[moving, 0:EARLY], leaving.at[3]),
            (manning, leaving.at[4]),
        ),
        sems,
        7,
    )
    messages(ctl, state, bed, jnp.max(total, keepdims=True), out, columns)
    wait_all(early)


class Passing:
    def __init__(self, ctl, state_in, bed_in, manning_in, arrived, leaving, buffer, sems):
        self.again = ctl[MOVE] == ctl[MOVE + 1]
        self.other = 1 - ctl[MOVE]
        self.refs = state_in, bed_in, manning_in, arrived, buffer, sems
        self.outgoing = [
            pltpu.make_async_copy(buffer.at[:, begin:end], piece, sems.at[1 + index])
            for index, ((begin, end), piece) in enumerate(zip(PIECES, leaving))
        ]

    def start(self):
        state_in, bed_in, manning_in, arrived, buffer, sems = self.refs
        rows = slice(0, EARLY)
        sem = sems.at[0]

        @pl.when(self.again)
        def _():
            pltpu.make_async_copy(arrived, buffer, sem).start()

        @pl.when(jnp.logical_not(self.again))
        def _():
            pltpu.make_async_copy(state_in.at[self.other, :, rows], buffer.at[0:3], sem).start()
            pltpu.make_async_copy(bed_in.at[self.other, rows], buffer.at[3], sem).start()
            pltpu.make_async_copy(manning_in.at[self.other, rows], buffer.at[4], sem).start()

    def middle(self):
        _, _, _, arrived, buffer, sems = self.refs
        pltpu.make_async_copy(arrived, buffer, sems.at[0]).wait()
        for copy in self.outgoing:
            copy.start()

    def end(self):
        wait_all(self.outgoing)


def rates_and_leaving(
    ctl, state_in, bed_in, state_first, manning_in, arrived, rate_out, leaving_low, leaving_high,
    state, bed, rate, sems, buffer, moving,
):
    passing = Passing(
        ctl, state_first, bed_in, manning_in, arrived, (leaving_low, leaving_high), buffer, moving
    )
    rates(ctl, state_in, bed_in, rate_out, state, bed, rate, sems, passing)


def rates_after(ctl, state_in, bed_in, order, *rest):
    del order
    rates(ctl, state_in, bed_in, *rest)


def rates(ctl, state_in, bed_in, rate_out, state, bed, rate, sems, passing=None):
    width = 2 * TILE
    row_ids = lax.broadcasted_iota(jnp.int32, (STRIP, width), 0)
    row8 = sublanes(width)
    lane = lax.broadcasted_iota(jnp.int32, (STRIP, LANES), 1)
    last = TILE // STRIP - 1
    chunk = TILE // CHUNKS
    slots = [slot_of(ctl, position) for position in range(2)]
    incoming = []
    for part in range(CHUNKS):
        rows = slice(part * chunk, (part + 1) * chunk)
        incoming.append(
            start_all(
                (
                    (state_in.at[:, :, rows], state.at[:, :, rows]),
                    (bed_in.at[:, rows], bed.at[:, rows]),
                ),
                sems,
                2 * part,
            )
        )
    if passing:
        passing.start()
    keep_west, keep_east, keep_south, keep_north = (
        jnp.where(flag(ctl, index), 1.0, 0.0)
        for index in (WALL_WEST, WALL_EAST, WALL_OUTER, WALL_OUTER + 1)
    )

    def strip(field, rows):
        if field == 3:
            return jnp.concatenate([bed[slot, rows, :] for slot in slots], 1)
        return jnp.concatenate([state[slot, field, rows, :] for slot in slots], 1)

    def blocks(value):
        return [value[:, k * LANES : (k + 1) * LANES] for k in range(4)]

    def right_of(value, end=None):
        turned = [pltpu.roll(part, LANES - 1, 1) for part in blocks(value)]
        after = turned[1:] + [turned[3] if end is None else end]
        return jnp.concatenate(
            [
                jnp.where(lane == LANES - 1, following, part)
                if following is not part
                else part
                for part, following in zip(turned, after)
            ],
            1,
        )

    def left_of(value, end):
        turned = [pltpu.roll(part, 1, 1) for part in blocks(value)]
        before = [end] + turned[:3]
        return jnp.concatenate(
            [jnp.where(lane == 0, previous, part) for part, previous in zip(turned, before)], 1
        )

    def down(value):
        return pltpu.roll(value, STRIP + 7, 0)[:STRIP]

    def group(index, carry):
        base = pl.multiple_of(index * STRIP, STRIP)
        rows = pl.ds(base, STRIP)
        after = pl.ds(pl.multiple_of(jnp.minimum(base + STRIP, TILE - 8), 8), 8)
        at_end = index == last
        fields = [
            jnp.concatenate([strip(field, rows), strip(field, after)], 0) for field in range(3)
        ]
        cells_x, cells_y = cell(*fields)
        here_x = tuple(value[:STRIP] for value in cells_x)
        here_y = tuple(value[:STRIP] for value in cells_y)

        ending = jnp.logical_and(row8 == 7, at_end)
        faces = list(face(here_x, tuple(down(value) for value in cells_x)))
        wall = keep_east * (2.0 * (here_x[3] + here_x[5] * here_x[1])[STRIP - 8 :])
        for component, value in enumerate((0.0, wall, 0.0)):
            upper = faces[component]
            faces[component] = jnp.concatenate(
                [upper[: STRIP - 8], jnp.where(ending, value, upper[STRIP - 8 :])], 0
            )
        turned = tuple(pltpu.roll(value, 1, 0) for value in faces)
        change_x = tuple(
            value - jnp.where(row_ids == 0, before, moved)
            for value, before, moved in zip(faces, carry[:3], turned)
        )
        ground = strip(3, rows)
        ground_after = jnp.where(
            at_end,
            jnp.broadcast_to(keep_east * ground[STRIP - 1 :], (8, width)),
            strip(3, after),
        )
        ground_up = pltpu.roll(ground, 1, 0)
        slope_x = down(jnp.concatenate([ground, ground_after], 0)) - jnp.where(
            row_ids == 0, carry[3], ground_up
        )
        carried = tuple(value[0:1, :] for value in turned) + (ground_up[0:1, :],)

        faces_y = list(face(here_y, tuple(right_of(value) for value in here_y)))
        normal = here_y[3]
        spread_y = here_y[5] * here_y[1]
        north = keep_north * (2.0 * (normal + spread_y)[:, width - LANES :])
        south = keep_south * (2.0 * (normal - spread_y)[:, :LANES])
        change_y = []
        for component, (high, low) in enumerate(((0.0, 0.0), (north, south), (0.0, 0.0))):
            parts = blocks(faces_y[component])
            parts[3] = jnp.where(lane == LANES - 1, high, parts[3])
            value = jnp.concatenate(parts, 1)
            change_y.append(value - left_of(value, low))
        slope_y = right_of(ground, keep_north * ground[:, width - LANES :]) - left_of(
            ground, keep_south * ground[:, :LANES]
        )
        weight = SLOPE * here_x[0]
        results = (
            SCALE * (change_x[0] + change_y[0]),
            SCALE * (change_x[1] + change_y[2]) + weight * slope_x,
            SCALE * (change_x[2] + change_y[1]) + weight * slope_y,
        )
        for field, value in enumerate(results):
            for position, slot in enumerate(slots):
                rate[slot, field, rows, :] = value[:, position * TILE : (position + 1) * TILE]
        return carried

    wait_all(incoming[0])
    top, _ = cell(*(strip(field, slice(0, 8)) for field in range(3)))
    nothing = jnp.zeros((1, width), jnp.float32)
    carry = (
        nothing,
        keep_west * (2.0 * (top[3] - top[5] * top[1])[0:1]),
        nothing,
        keep_west * strip(3, slice(0, 8))[0:1],
    )
    per_chunk = chunk // STRIP
    outgoing = []
    for part in range(CHUNKS):
        if part + 1 < CHUNKS:
            wait_all(incoming[part + 1])
        carry = lax.fori_loop(part * per_chunk, (part + 1) * per_chunk, group, carry)
        rows = slice(part * chunk, (part + 1) * chunk)
        outgoing += start_all(
            ((rate.at[:, :, rows], rate_out.at[:, :, rows]),), sems, 2 * CHUNKS + part
        )
        if passing and part == CHUNKS // 2:
            passing.middle()
    wait_all(outgoing)
    if passing:
        passing.end()


def moved_on(old, slopes, rough, delta, wet_now):
    h, hu, hv = (value - delta * slope for value, slope in zip(old, slopes))
    inverse = 1.0 / h
    u = hu * inverse
    v = hv * inverse
    speed = jnp.sqrt(u * u + v * v)
    power = jnp.exp((-4.0 / 3.0) * jnp.log(jnp.abs(h)))
    drag = (GRAVITY * delta) * (rough * rough) * (speed * power)
    factor = 1.0 / (1.0 + drag)
    fresh = (h, hu * factor, hv * factor)
    return tuple(jnp.where(wet_now, new, value) for new, value in zip(fresh, old))


def repeat_steps(ctl, wet_from, deltas, early, work, other, sems):
    incoming = []
    for ref in early:
        begin = 0 if ref is early[0] else early[0].shape[1]
        incoming += start_all(
            ((ref, work.at[:, begin : begin + ref.shape[1]]),), sems, len(incoming)
        )
    row_ids = lax.broadcasted_iota(jnp.int32, (ROWS, TILE), 0)
    lane = lax.broadcasted_iota(jnp.int32, (ROWS, LANES), 1)
    start = tuple(jnp.zeros((1, TILE), jnp.float32) for _ in range(4))

    def halves(value):
        return value[:, :LANES], value[:, LANES:]

    def right_of(value):
        low, high = (pltpu.roll(part, LANES - 1, 1) for part in halves(value))
        return jnp.concatenate([jnp.where(lane == LANES - 1, high, low), high], 1)

    def left_of(value):
        low, high = (pltpu.roll(part, 1, 1) for part in halves(value))
        return jnp.concatenate([low, jnp.where(lane == 0, low, high)], 1)

    def down(value):
        return pltpu.roll(value, ROWS + 7, 0)[:ROWS]

    for step in range(STEPS):
        source, target = (work, other) if step % 2 == 0 else (other, work)
        delta = deltas[step][0:1, :]
        wet_now = flag(ctl, wet_from + step)

        def group(index, carry, source=source, target=target, delta=delta, wet_now=wet_now):
            base = pl.multiple_of(index * ROWS, ROWS)
            rows = pl.ds(base, ROWS)
            after = pl.ds(pl.multiple_of(jnp.minimum(base + ROWS, EARLY - 8), 8), 8)
            refs = [source.at[field] for field in range(3)] + [work.at[3]]
            fields = [jnp.concatenate([ref[rows, :], ref[after, :]], 0) for ref in refs]
            cells_x, cells_y = cell(*fields[:3])
            here_x = tuple(value[:ROWS] for value in cells_x)
            here_y = tuple(value[:ROWS] for value in cells_y)
            faces_x = face(here_x, tuple(down(value) for value in cells_x))
            turned = tuple(pltpu.roll(value, 1, 0) for value in faces_x)
            change_x = tuple(
                value - jnp.where(row_ids == 0, before, moved)
                for value, before, moved in zip(faces_x, carry[:3], turned)
            )
            ground = fields[3][:ROWS]
            ground_up = pltpu.roll(ground, 1, 0)
            slope_x = down(fields[3]) - jnp.where(row_ids == 0, carry[3], ground_up)
            carried = tuple(value[0:1, :] for value in turned) + (ground_up[0:1, :],)
            faces_y = face(here_y, tuple(right_of(value) for value in here_y))
            change_y = tuple(value - left_of(value) for value in faces_y)
            slope_y = right_of(ground) - left_of(ground)
            old = tuple(value[:ROWS] for value in fields[:3])
            weight = SLOPE * old[0]
            slopes = (
                SCALE * (change_x[0] + change_y[0]),
                SCALE * (change_x[1] + change_y[2]) + weight * slope_x,
                SCALE * (change_x[2] + change_y[1]) + weight * slope_y,
            )
            for field, value in enumerate(
                moved_on(old, slopes, work[4, rows, :], delta, wet_now)
            ):
                target[field, rows, :] = value
            return carried

        if step == 0:
            wait_all(incoming)
        lax.fori_loop(0, EARLY // ROWS, group, start)


def late_rows(tile, late):
    row = sublanes()
    kept = EARLY - 8
    lane = lax.broadcasted_iota(jnp.int32, (8, LANES), 1)
    for field in range(3):
        late[field, 0:8, :] = jnp.where(
            row < 3, tile[field, 0:8, :], tile[field, kept : kept + 8, :]
        )
        packed = [jnp.zeros((8, LANES), jnp.float32)] * 2
        for block in range(EARLY // 8):
            rows = slice(8 * block, 8 * block + 8)
            sides = jnp.where(lane < 64, tile[field, rows, :LANES], tile[field, rows, LANES:])
            turned = pltpu.roll(sides, (3 + 8 * block) % LANES, 1)
            which = block // 16
            packed[which] = jnp.where(lane // 8 == block % 16, turned, packed[which])
        late[field, 8:16, :] = jnp.concatenate(packed, 1)
        late[field, 16:, :] = tile[field, EARLY:, :]


def merge(late, early, tile):
    row = sublanes()
    lane = lax.broadcasted_iota(jnp.int32, (8, LANES), 1)
    for field in range(3):
        first = late[field, 0:8, :]
        for block in range(EARLY // 8):
            rows = slice(8 * block, 8 * block + 8)
            which = block // 16
            packed = late[field, 8:16, which * LANES : (which + 1) * LANES]
            sides = pltpu.roll(packed, (-3 - 8 * block) % LANES, 1)
            value = early[field, rows, :]
            value = jnp.concatenate(
                [
                    jnp.where(lane < 3, sides, value[:, :LANES]),
                    jnp.where(lane >= LANES - 3, sides, value[:, LANES:]),
                ],
                1,
            )
            if block == 0:
                value = jnp.where(row < 3, first, value)
            if block == EARLY // 8 - 1:
                value = jnp.where(row < 5, value, first)
            tile[field, rows, :] = value
        tile[field, EARLY:, :] = late[field, 16:, :]


def repeat_second(ctl, delta0, delta1, delta2, low, high, out, work, tile, sems):
    repeat_steps(ctl, WET_SECOND, (delta0, delta1, delta2), (low, high), work, tile, sems)
    wait_all(start_all(((tile, out),), sems))


def repeat_first(
    ctl, delta0, delta1, delta2, early, late_in, staying, out, work, other, tile, late, sems
):
    rest = out.at[1 - ctl[MOVE + 1]]
    again = ctl[MOVE] == ctl[MOVE + 1]

    @pl.when(again)
    def _():
        wait_all(start_all(((staying, tile),), sems))

    @pl.when(jnp.logical_not(again))
    def _():
        copies = start_all(((late_in, late),), sems, 1)
        repeat_steps(ctl, WET_FIRST, (delta0, delta1, delta2), (early,), work, other, sems)
        wait_all(copies)
        merge(late, other, tile)

    wait_all(start_all(((tile, rest),), sems))


def finish(ctl, late_in, early_in, before, out, late, early, tile, sems):
    del before
    wait_all(start_all(((late_in, late), (early_in, early)), sems))
    merge(late, early, tile)
    wait_all(start_all(((tile, out.at[ctl[MOVE + 1]]),), sems))


def second_late(ctl, arrived, own, order, leaving, buffer, sems):
    del order
    again = ctl[MOVE] == ctl[MOVE + 1]

    @pl.when(again)
    def _():
        pltpu.make_async_copy(arrived, buffer, sems.at[0]).start()

    @pl.when(jnp.logical_not(again))
    def _():
        pltpu.make_async_copy(own, buffer, sems.at[0]).start()

    pltpu.make_async_copy(arrived, buffer, sems.at[0]).wait()
    wait_all(start_all(((buffer, leaving),), sems))


def correct_rows(ctl, slot, got, ground, block, state, rate, bottom):
    position = jnp.where(ctl[SLOT_LOW] == slot, 0, 1)
    device = lax.axis_index("xb") * 2 + lax.axis_index("yb")
    wall = WALL_WEST if bottom else WALL_EAST

    @pl.when(jnp.logical_not(flag(ctl, wall + position)))
    def _():
        peer = device - 2 if bottom else device + 2
        lines = got[pl.ds(pl.multiple_of(peer * block, 8), 8), :]
        grounds = ground[pl.ds(pl.multiple_of(peer * 16 + 8, 8), 8), :]

        def line(value, offset):
            picked = jnp.where(
                position == 0, value[offset : offset + 1, :], value[offset + 3 : offset + 4, :]
            )
            return jnp.broadcast_to(picked, (8, TILE))

        ghost, _ = cell(*(line(lines, field) for field in range(3)))
        ghost_ground = jnp.where(position == 0, grounds[0:1, :], grounds[1:2, :])
        rows = slice(0, 8) if bottom else slice(TILE - 8, TILE)
        own = [state[slot, field, rows, :] for field in range(3)]
        here, _ = cell(*own)
        fluxes = face(ghost, here) if bottom else face(here, ghost)
        push = SCALE * fluxes[1] + (SLOPE * own[0]) * ghost_ground
        row = sublanes()
        sign = -1.0 if bottom else 1.0
        chosen = row == (0 if bottom else 7)
        for field, value in enumerate((SCALE * fluxes[0], push, SCALE * fluxes[2])):
            rate[slot, field, rows, :] += jnp.where(chosen, sign * value, 0.0)


def column_fix(got, ground, block, columns, bed_columns):
    upper = lax.axis_index("yb")
    device = lax.axis_index("xb") * 2 + upper
    peer = device + 1 - 2 * upper
    lines = got[pl.ds(pl.multiple_of(peer * block, 8), 8), :]
    ghost_ground = ground[pl.ds(pl.multiple_of(peer * 16, 8), 8), :][3:4]
    del bed_columns
    mine = columns[...]
    _, ghost = cell(lines[0:1], lines[1:2], lines[2:3])
    _, own = cell(mine[0:1], mine[1:2], mine[2:3])
    low = upper == 0
    left = tuple(jnp.where(low, a, b) for a, b in zip(own, ghost))
    right = tuple(jnp.where(low, b, a) for a, b in zip(own, ghost))
    fluxes = face(left, right)
    sign = jnp.where(low, 1.0, -1.0)
    push = SCALE * fluxes[1] + (SLOPE * mine[0:1]) * ghost_ground
    block8 = stacked(
        [sign * SCALE * fluxes[0], sign * SCALE * fluxes[2], sign * push],
        jnp.zeros((8, TILE), jnp.float32),
    )
    return jnp.transpose(
        jnp.concatenate([block8, jnp.zeros((LANES - 8, TILE), jnp.float32)], 0)
    )


def update(step, ctl, got_in, ground_in, columns_in, state_in, manning_in, rate_in, *rest):
    more = step + 1 < STEPS
    if more:
        fresh_out, out_to, columns_to, delta_out = rest[:4]
    else:
        staying, late_first, late_second, delta_out = rest[:4]
    rest = rest[4:]
    state, manning, rate, fresh, got, ground, columns, out, columns_out, delta_keep, sems = rest
    small = start_all(
        ((got_in, got), (ground_in, ground), (columns_in, columns)), sems, 5 * PARTS
    )
    size = 2 * TILE // PARTS
    parts = [
        (slot, slice(k * size, (k + 1) * size)) for slot in range(2) for k in range(PARTS // 2)
    ]
    incoming = []
    for index, (slot, rows) in enumerate(parts):
        incoming.append(
            start_all(
                (
                    (rate_in.at[slot, :, rows], rate.at[slot, :, rows]),
                    (state_in.at[slot, :, rows], state.at[slot, :, rows]),
                    (manning_in.at[slot, rows], manning.at[slot, rows]),
                ),
                sems,
                3 * index,
            )
        )
    wait_all(small)
    upper = lax.axis_index("yb")
    devices = 2 * lax.axis_size("xb")
    block = got.shape[0] // devices
    tops = got[0:8, :]
    for peer in range(1, devices):
        tops = jnp.maximum(tops, got[peer * block : peer * block + 8, :])
    delta = (COURANT * SPACING) / tops[TOP : TOP + 1, :]
    delta_keep[...] = jnp.broadcast_to(delta, (8, TILE))
    outgoing = start_all(((delta_keep, delta_out),), sems, 5 * PARTS + 3)
    fix = column_fix(got, ground, block, columns, None)
    facing = jnp.where(upper > 0, ctl[SLOT_LOW], 1 - ctl[SLOT_LOW])
    begin = pl.multiple_of((1 - upper) * LANES, LANES)
    target = (1 - upper) * (LANES - 1)
    lane = lax.broadcasted_iota(jnp.int32, (size, LANES), 1)
    total = jnp.zeros((ROWS, TILE), jnp.float32)
    for index, (slot, part_rows) in enumerate(parts):
        wait_all(incoming[index])
        if part_rows.start == 0:
            correct_rows(ctl, slot, got, ground, block, state, rate, True)
        if part_rows.stop == TILE:
            correct_rows(ctl, slot, got, ground, block, state, rate, False)

        @pl.when(facing == slot)
        def _(slot=slot, part_rows=part_rows):
            for field in range(3):
                turned = pltpu.roll(
                    fix[part_rows], lax.rem(target + LANES - field, LANES), 1
                )
                rate[slot, field, part_rows, pl.ds(begin, LANES)] += jnp.where(
                    lane == target, turned, 0.0
                )

        wet_now = flag(ctl, WET + 2 * step + slot)

        def group(index, best, slot=slot, wet_now=wet_now):
            rows = pl.ds(pl.multiple_of(index * ROWS, ROWS), ROWS)
            old = tuple(state[slot, field, rows, :] for field in range(3))
            slopes = tuple(rate[slot, field, rows, :] for field in range(3))
            h, hu, hv = moved_on(old, slopes, manning[slot, rows, :], delta, wet_now)
            fresh[slot, 0, rows, :] = h
            fresh[slot, 1, rows, :] = hu
            fresh[slot, 2, rows, :] = hv
            if more:
                along_x, along_y = cell(h, hu, hv)
                best = jnp.maximum(best, jnp.maximum(along_x[5], along_y[5]))
            return best

        best = lax.fori_loop(
            part_rows.start // ROWS,
            part_rows.stop // ROWS,
            group,
            jnp.zeros((ROWS, TILE), jnp.float32),
        )
        if more:
            best = jnp.where(flag(ctl, WET + 2 * step + 2 + slot), best, 0.0)
            total = jnp.maximum(total, best)
        if more:
            outgoing += start_all(
                ((fresh.at[slot, :, part_rows], fresh_out.at[slot, :, part_rows]),),
                sems,
                3 * PARTS + index,
            )
    if more:
        messages(ctl, fresh, None, jnp.max(total, keepdims=True), out, columns_out)
        outgoing += start_all(((out, out_to), (columns_out, columns_to)), sems, 4 * PARTS)
    else:
        first, second = fresh.at[ctl[MOVE]], fresh.at[1 - ctl[MOVE]]
        outgoing += start_all(((second, staying),), sems, 4 * PARTS)
        late_rows(first, late_first)
        late_rows(second, late_second)
    wait_all(outgoing)


def vmem():
    return pl.BlockSpec(memory_space=pltpu.VMEM)


def smem():
    return pl.BlockSpec(memory_space=pltpu.SMEM)


def hbm():
    return pl.BlockSpec(memory_space=pltpu.HBM)


def anywhere():
    return pl.BlockSpec(memory_space=pl.ANY)


def call(
    kernel, outs, out_specs, in_specs, flops, scratch=(), aliases=None, room=VMEM_BYTES, moved=4
):
    return pl.pallas_call(
        kernel,
        scratch_shapes=scratch,
        input_output_aliases=aliases or {},
        out_shape=outs,
        in_specs=in_specs,
        out_specs=out_specs,
        compiler_params=pltpu.CompilerParams(vmem_limit_bytes=room),
        cost_estimate=pl.CostEstimate(flops=flops, bytes_accessed=moved << 20, transcendentals=0),
    )


def f32(*shape):
    return jax.ShapeDtypeStruct(shape, jnp.float32)


def spread(fast):
    return lax.all_to_all(fast, ("xb", "yb"), split_axis=0, concat_axis=0, tiled=True)


def body(state, bed, manning, neighbours, wet, moves):
    shape = f32(*state.shape)
    devices = lax.axis_size("xb") * lax.axis_size("yb")
    sem = [pltpu.SemaphoreType.DMA((1,))]
    whole = pltpu.VMEM(state.shape, jnp.float32)
    part = pltpu.VMEM(bed.shape, jnp.float32)
    tile_shape = f32(*state.shape[1:])
    early_shape = f32(5, EARLY, TILE)
    early_state = f32(3, EARLY, TILE)
    late_shape = f32(3, LATE, TILE)
    delta_shape = f32(8, TILE)

    def buffer(like):
        return pltpu.VMEM(like.shape, jnp.float32)

    out, columns, ctl, leaving = call(
        opening,
        (
            f32(16 * devices, TILE),
            f32(8, TILE),
            jax.ShapeDtypeStruct((CONTROLS,), jnp.int32),
            early_shape,
        ),
        (vmem(), vmem(), smem(), hbm()),
        [hbm()] * 6,
        4 << 20,
        [
            whole,
            part,
            pltpu.VMEM((EARLY, TILE), jnp.float32),
            pltpu.SMEM(neighbours.shape[::-1], jnp.int32),
            pltpu.SMEM(wet.shape, jnp.int32),
            pltpu.SMEM(moves.shape, jnp.int32),
            pltpu.SemaphoreType.DMA((10,)),
        ],
    )(state, bed, manning, neighbours.T, wet, moves)
    state_first = state
    ground = None
    deltas = []
    for step in range(STEPS):
        got = spread(out)
        ground = got if step == 0 else ground
        scratch = [whole, part, whole, pltpu.SemaphoreType.DMA((3 * CHUNKS,))]
        if step == 0:
            early_first = shifted(leaving, "xb", 1)
            rate = call(rates, shape, hbm(), [smem(), hbm(), hbm()], 16 << 20, scratch)(
                ctl, state, bed
            )
        elif step == 1:
            rate, *leaving = call(
                rates_and_leaving,
                (shape,) + tuple(f32(5, end - begin, TILE) for begin, end in PIECES),
                (hbm(),) * 3,
                [smem()] + [hbm()] * 5,
                16 << 20,
                scratch + [buffer(early_shape), pltpu.SemaphoreType.DMA((3,))],
            )(ctl, state, bed, state_first, manning, early_first)
            early_second = [shifted(piece, "xb", 1) for piece in leaving]
        else:
            rate = call(rates_after, shape, hbm(), [smem()] + [hbm()] * 3, 16 << 20, scratch)(
                ctl, state, bed, early_second[0]
            )
        more = step + 1 < STEPS
        if more:
            shapes = (shape, f32(8 * devices, TILE), f32(8, TILE), delta_shape)
            places = (hbm(),) * 4
        else:
            shapes = (tile_shape, late_shape, late_shape, delta_shape)
            places = (hbm(), vmem(), vmem(), hbm())
        outs = call(
            functools.partial(update, step),
            shapes,
            places,
            [smem()] + [hbm()] * 6,
            8 << 20,
            [
                whole,
                part,
                whole,
                whole,
                pltpu.VMEM(got.shape, jnp.float32),
                pltpu.VMEM(ground.shape, jnp.float32),
                pltpu.VMEM((8, TILE), jnp.float32),
                pltpu.VMEM((8 * devices, TILE), jnp.float32),
                pltpu.VMEM((8, TILE), jnp.float32),
                buffer(delta_shape),
                pltpu.SemaphoreType.DMA((5 * PARTS + 4,)),
            ],
            moved=9 if step == 0 else 4,
        )(ctl, got, ground, columns, state, manning, rate)
        deltas.append(outs[-1])
        if more:
            state, out, columns, _ = outs
    staying, late_first, late_second, _ = outs
    room = 16 << 20
    late_arrived = shifted(late_first, "xb", 1)
    second = call(
        repeat_second,
        early_state,
        anywhere(),
        [smem()] + [vmem()] * 3 + [anywhere()] * 2,
        8 << 20,
        [buffer(early_shape), buffer(early_state), pltpu.SemaphoreType.DMA((2,))],
        room=room,
    )(ctl, *deltas, *early_second)
    leaving = call(
        second_late,
        late_shape,
        anywhere(),
        [smem(), anywhere(), anywhere(), anywhere()],
        1 << 20,
        [buffer(late_shape)] + sem,
        room=room,
    )(ctl, late_arrived, late_second, second)
    late_next = shifted(leaving, "xb", 1)
    final = call(
        repeat_first,
        shape,
        hbm(),
        [smem()] + [vmem()] * 3 + [anywhere()] * 3,
        8 << 20,
        [
            buffer(early_shape),
            buffer(early_state),
            buffer(tile_shape),
            buffer(late_shape),
            pltpu.SemaphoreType.DMA((2,)),
        ],
        room=room,
    )(ctl, *deltas, early_first, late_arrived, staying)
    return call(
        finish,
        shape,
        hbm(),
        [smem(), anywhere(), anywhere(), hbm()],
        1 << 20,
        [
            buffer(late_shape),
            buffer(early_state),
            buffer(tile_shape),
            pltpu.SemaphoreType.DMA((2,)),
        ],
        {3: 0},
        room=room,
    )(ctl, late_next, second, final)


def solution(mesh):
    placed = (
        P(("runs", "xb", "yb"), None, None, None),
        P(("runs", "xb", "yb"), None, None),
        P(("runs", "xb", "yb"), None, None),
        P("runs", None),
        P(None, "runs"),
        P(None, "runs"),
    )
    return jax.shard_map(
        body,
        mesh=mesh,
        in_specs=placed,
        out_specs=P(("runs", "xb", "yb"), None, None, None),
        check_vma=False,
    )
```

```python
import functools

import jax
import jax.numpy as jnp
from jax import lax
from jax.experimental import pallas as pl
from jax.experimental.pallas import tpu as pltpu
from jax.sharding import PartitionSpec as P

STEPS = 3
GRAVITY = 9.81
ROOT_G = GRAVITY**0.5
SPACING = 5.0
COURANT = 0.2
ROWS = 32
LANES = 128
TILE = 256
VMEM_BYTES = 60 * 1024 * 1024
SLOT_LOW, WALL_WEST, WALL_EAST, WALL_OUTER, WET, MOVE = 0, 1, 3, 5, 7, 13
WET_FIRST, WET_SECOND = 16, 19
CONTROLS = 24
EARLY = 192
PIECES = ((0, 96), (96, 192))
LATE = TILE - EARLY + 16
CHUNKS = 8
PARTS = 8
STRIP = 16
TOP = 6
SCALE = 0.5 / SPACING
SLOPE = GRAVITY / (2.0 * SPACING)


def shifted(value, axis, steps, around=True):
    count = lax.axis_size(axis)
    pairs = [(source, (source + steps) % count) for source in range(count)]
    if not around:
        pairs = [pair for pair in pairs if abs(pair[0] - pair[1]) == abs(steps)]
    return lax.ppermute(value, axis, pairs)


def cell(h, hu, hv):
    root = lax.rsqrt(h)
    inverse = root * root
    u = hu * inverse
    v = hv * inverse
    celerity = ROOT_G * (h * root)
    pressure = (0.5 * GRAVITY) * (h * h)
    cross = hu * v
    speed_x = jnp.abs(u) + celerity
    speed_y = jnp.abs(v) + celerity
    along_x = (h, hu, hv, hu * u + pressure, cross, speed_x)
    along_y = (h, hv, hu, hv * v + pressure, cross, speed_y)
    return along_x, along_y


def face(left, right):
    wave = jnp.maximum(left[5], right[5])
    return (
        (left[1] + right[1]) - wave * (right[0] - left[0]),
        (left[3] + right[3]) - wave * (right[1] - left[1]),
        (left[4] + right[4]) - wave * (right[2] - left[2]),
    )


def slot_of(ctl, position):
    low = ctl[SLOT_LOW]
    return low if position == 0 else 1 - low


def flag(ctl, index):
    return ctl[index] > 0


def start_all(pairs, sems, first=0):
    copies = [
        pltpu.make_async_copy(src, dst, sems.at[first + k]) for k, (src, dst) in enumerate(pairs)
    ]
    for copy in copies:
        copy.start()
    return copies


def wait_all(copies):
    for copy in copies:
        copy.wait()


def sublanes(width=TILE):
    return lax.broadcasted_iota(jnp.int32, (8, width), 0)


def stacked(lines, base):
    row = sublanes()
    for index, line in enumerate(lines):
        base = jnp.where(row == index, jnp.broadcast_to(line, (8, TILE)), base)
    return base


def messages(ctl, state, bed, fastest, out, columns):
    upper = lax.axis_index("yb")
    column = lax.axis_index("xb")
    last = lax.axis_size("xb") - 1
    devices = 2 * (last + 1)
    block = out.shape[0] // devices
    device = column * 2 + upper
    top = jnp.broadcast_to(fastest, (8, TILE))
    for peer in range(devices):
        out[peer * block : peer * block + 8, :] = top
    row = sublanes()

    def edge(line):
        rows = slice(line, line + 1)
        slots = [slot_of(ctl, position) for position in range(2)]
        fields = [state[slot, field, rows, :] for slot in slots for field in range(3)]
        return stacked(fields, top), [bed[slot, rows, :] for slot in slots] if bed is not None else None

    for inside, peer, line in (
        (column > 0, device - 2, 0),
        (column < last, device + 2, TILE - 1),
    ):

        @pl.when(inside)
        def _(peer=peer, line=line):
            lines, ground = edge(line)
            start = pl.multiple_of(peer * block, 8)
            out[pl.ds(start, 8), :] = lines
            if ground:
                out[pl.ds(pl.multiple_of(start + 8, 8), 8), :] = stacked(ground, top)

    slot = jnp.where(upper > 0, ctl[SLOT_LOW], 1 - ctl[SLOT_LOW])
    begin = pl.multiple_of((1 - upper) * LANES, LANES)
    lane = lax.broadcasted_iota(jnp.int32, (TILE, LANES), 1)
    packed = None
    for field in range(4 if bed is not None else 3):
        if field < 3:
            part = state[slot, field, :, pl.ds(begin, LANES)]
        else:
            part = bed[slot, :, pl.ds(begin, LANES)]
        turned = pltpu.roll(part, field + 1 - upper, 1)
        packed = turned if field == 0 else jnp.where(lane == field, turned, packed)
    lines = jnp.transpose(packed)[:8]
    columns[...] = lines
    start = pl.multiple_of((device + 1 - 2 * upper) * block, 8)
    out[pl.ds(start, 8), :] = jnp.where(row == TOP, top, lines)


def opening(
    state_in, bed_in, manning_in, neighbours_in, wet_in, moves_in,
    out, columns, ctl, leaving,
    state, bed, manning, neighbours, wet, moves, sems,
):
    copies = start_all(
        (
            (neighbours_in, neighbours),
            (wet_in, wet),
            (moves_in, moves),
            (state_in.at[0], state.at[0]),
            (state_in.at[1], state.at[1]),
            (bed_in, bed),
        ),
        sems,
    )
    device = lax.axis_index("xb") * 2 + lax.axis_index("yb")
    wait_all(copies[:3])
    first = device * 2
    low = jnp.where(neighbours[3, first] == first + 1, 0, 1)
    ctl[SLOT_LOW] = low
    for position in range(2):
        slot = low if position == 0 else 1 - low
        tile = first + slot
        ctl[WALL_WEST + position] = (neighbours[0, tile] < 0).astype(jnp.int32)
        ctl[WALL_EAST + position] = (neighbours[1, tile] < 0).astype(jnp.int32)
        ctl[WALL_OUTER + position] = (neighbours[2 + position, tile] < 0).astype(jnp.int32)
    for step in range(STEPS):
        for slot in range(2):
            ctl[WET + 2 * step + slot] = wet[step, first + slot]
        ctl[MOVE + step] = moves[step, device]
    moving = moves[0, device]
    rough = start_all(((manning_in.at[moving, 0:EARLY], manning),), sems, 6)
    count = lax.axis_size("xb")
    upper = lax.axis_index("yb")
    column = lax.axis_index("xb")
    source = lax.rem(column + count - 1, count) * 2 + upper
    before = lax.rem(column + count - 2, count) * 2 + upper
    again = moves[0, source] == moves[1, source]
    tile_first = source * 2 + moves[0, source]
    tile_second = jnp.where(
        again, before * 2 + moves[0, before], source * 2 + 1 - moves[0, source]
    )
    for step in range(STEPS):
        ctl[WET_FIRST + step] = wet[step, tile_first]
        ctl[WET_SECOND + step] = wet[step, tile_second]

    wait_all(copies[3:] + rough)
    early = start_all(
        (
            (state.at[moving, :, 0:EARLY], leaving.at[0:3]),
            (bed.at[moving, 0:EARLY], leaving.at[3]),
            (manning, leaving.at[4]),
        ),
        sems,
        7,
    )
    total = jnp.zeros((ROWS, TILE), jnp.float32)
    for slot in range(2):

        def group(index, best, slot=slot):
            rows = pl.ds(pl.multiple_of(index * ROWS, ROWS), ROWS)
            along_x, along_y = cell(*(state[slot, field, rows, :] for field in range(3)))
            return jnp.maximum(best, jnp.maximum(along_x[5], along_y[5]))

        best = lax.fori_loop(0, TILE // ROWS, group, jnp.zeros((ROWS, TILE), jnp.float32))
        total = jnp.maximum(total, jnp.where(wet[0, first + slot] > 0, best, 0.0))
    messages(ctl, state, bed, jnp.max(total, keepdims=True), out, columns)
    wait_all(early)


class Passing:
    def __init__(self, ctl, state_in, bed_in, manning_in, arrived, leaving, buffer, sems):
        self.again = ctl[MOVE] == ctl[MOVE + 1]
        self.other = 1 - ctl[MOVE]
        self.refs = state_in, bed_in, manning_in, arrived, buffer, sems
        self.outgoing = [
            pltpu.make_async_copy(buffer.at[:, begin:end], piece, sems.at[1 + index])
            for index, ((begin, end), piece) in enumerate(zip(PIECES, leaving))
        ]

    def start(self):
        state_in, bed_in, manning_in, arrived, buffer, sems = self.refs
        rows = slice(0, EARLY)
        sem = sems.at[0]

        @pl.when(self.again)
        def _():
            pltpu.make_async_copy(arrived, buffer, sem).start()

        @pl.when(jnp.logical_not(self.again))
        def _():
            pltpu.make_async_copy(state_in.at[self.other, :, rows], buffer.at[0:3], sem).start()
            pltpu.make_async_copy(bed_in.at[self.other, rows], buffer.at[3], sem).start()
            pltpu.make_async_copy(manning_in.at[self.other, rows], buffer.at[4], sem).start()

    def middle(self):
        _, _, _, arrived, buffer, sems = self.refs
        pltpu.make_async_copy(arrived, buffer, sems.at[0]).wait()
        for copy in self.outgoing:
            copy.start()

    def end(self):
        wait_all(self.outgoing)


def rates_and_leaving(
    ctl, state_in, bed_in, state_first, manning_in, arrived, rate_out, leaving_low, leaving_high,
    state, bed, rate, sems, buffer, moving,
):
    passing = Passing(
        ctl, state_first, bed_in, manning_in, arrived, (leaving_low, leaving_high), buffer, moving
    )
    rates(ctl, state_in, bed_in, rate_out, state, bed, rate, sems, passing)


def rates_after(ctl, state_in, bed_in, order, *rest):
    del order
    rates(ctl, state_in, bed_in, *rest)


def rates(ctl, state_in, bed_in, rate_out, state, bed, rate, sems, passing=None):
    width = 2 * TILE
    row_ids = lax.broadcasted_iota(jnp.int32, (STRIP, width), 0)
    row8 = sublanes(width)
    lane = lax.broadcasted_iota(jnp.int32, (STRIP, LANES), 1)
    last = TILE // STRIP - 1
    chunk = TILE // CHUNKS
    slots = [slot_of(ctl, position) for position in range(2)]
    incoming = []
    for part in range(CHUNKS):
        rows = slice(part * chunk, (part + 1) * chunk)
        incoming.append(
            start_all(
                (
                    (state_in.at[:, :, rows], state.at[:, :, rows]),
                    (bed_in.at[:, rows], bed.at[:, rows]),
                ),
                sems,
                2 * part,
            )
        )
    if passing:
        passing.start()
    keep_west, keep_east, keep_south, keep_north = (
        jnp.where(flag(ctl, index), 1.0, 0.0)
        for index in (WALL_WEST, WALL_EAST, WALL_OUTER, WALL_OUTER + 1)
    )

    def strip(field, rows):
        if field == 3:
            return jnp.concatenate([bed[slot, rows, :] for slot in slots], 1)
        return jnp.concatenate([state[slot, field, rows, :] for slot in slots], 1)

    def blocks(value):
        return [value[:, k * LANES : (k + 1) * LANES] for k in range(4)]

    def right_of(value, end=None):
        turned = [pltpu.roll(part, LANES - 1, 1) for part in blocks(value)]
        after = turned[1:] + [turned[3] if end is None else end]
        return jnp.concatenate(
            [
                jnp.where(lane == LANES - 1, following, part)
                if following is not part
                else part
                for part, following in zip(turned, after)
            ],
            1,
        )

    def left_of(value, end):
        turned = [pltpu.roll(part, 1, 1) for part in blocks(value)]
        before = [end] + turned[:3]
        return jnp.concatenate(
            [jnp.where(lane == 0, previous, part) for part, previous in zip(turned, before)], 1
        )

    def down(value):
        return pltpu.roll(value, STRIP + 7, 0)[:STRIP]

    def group(index, carry):
        base = pl.multiple_of(index * STRIP, STRIP)
        rows = pl.ds(base, STRIP)
        after = pl.ds(pl.multiple_of(jnp.minimum(base + STRIP, TILE - 8), 8), 8)
        at_end = index == last
        fields = [
            jnp.concatenate([strip(field, rows), strip(field, after)], 0) for field in range(3)
        ]
        cells_x, cells_y = cell(*fields)
        here_x = tuple(value[:STRIP] for value in cells_x)
        here_y = tuple(value[:STRIP] for value in cells_y)

        ending = jnp.logical_and(row8 == 7, at_end)
        faces = list(face(here_x, tuple(down(value) for value in cells_x)))
        wall = keep_east * (2.0 * (here_x[3] + here_x[5] * here_x[1])[STRIP - 8 :])
        for component, value in enumerate((0.0, wall, 0.0)):
            upper = faces[component]
            faces[component] = jnp.concatenate(
                [upper[: STRIP - 8], jnp.where(ending, value, upper[STRIP - 8 :])], 0
            )
        turned = tuple(pltpu.roll(value, 1, 0) for value in faces)
        change_x = tuple(
            value - jnp.where(row_ids == 0, before, moved)
            for value, before, moved in zip(faces, carry[:3], turned)
        )
        ground = strip(3, rows)
        ground_after = jnp.where(
            at_end,
            jnp.broadcast_to(keep_east * ground[STRIP - 1 :], (8, width)),
            strip(3, after),
        )
        ground_up = pltpu.roll(ground, 1, 0)
        slope_x = down(jnp.concatenate([ground, ground_after], 0)) - jnp.where(
            row_ids == 0, carry[3], ground_up
        )
        carried = tuple(value[0:1, :] for value in turned) + (ground_up[0:1, :],)

        faces_y = list(face(here_y, tuple(right_of(value) for value in here_y)))
        normal = here_y[3]
        spread_y = here_y[5] * here_y[1]
        north = keep_north * (2.0 * (normal + spread_y)[:, width - LANES :])
        south = keep_south * (2.0 * (normal - spread_y)[:, :LANES])
        change_y = []
        for component, (high, low) in enumerate(((0.0, 0.0), (north, south), (0.0, 0.0))):
            parts = blocks(faces_y[component])
            parts[3] = jnp.where(lane == LANES - 1, high, parts[3])
            value = jnp.concatenate(parts, 1)
            change_y.append(value - left_of(value, low))
        slope_y = right_of(ground, keep_north * ground[:, width - LANES :]) - left_of(
            ground, keep_south * ground[:, :LANES]
        )
        weight = SLOPE * here_x[0]
        results = (
            SCALE * (change_x[0] + change_y[0]),
            SCALE * (change_x[1] + change_y[2]) + weight * slope_x,
            SCALE * (change_x[2] + change_y[1]) + weight * slope_y,
        )
        for field, value in enumerate(results):
            for position, slot in enumerate(slots):
                rate[slot, field, rows, :] = value[:, position * TILE : (position + 1) * TILE]
        return carried

    wait_all(incoming[0])
    top, _ = cell(*(strip(field, slice(0, 8)) for field in range(3)))
    nothing = jnp.zeros((1, width), jnp.float32)
    carry = (
        nothing,
        keep_west * (2.0 * (top[3] - top[5] * top[1])[0:1]),
        nothing,
        keep_west * strip(3, slice(0, 8))[0:1],
    )
    per_chunk = chunk // STRIP
    outgoing = []
    for part in range(CHUNKS):
        if part + 1 < CHUNKS:
            wait_all(incoming[part + 1])
        carry = lax.fori_loop(part * per_chunk, (part + 1) * per_chunk, group, carry)
        rows = slice(part * chunk, (part + 1) * chunk)
        outgoing += start_all(
            ((rate.at[:, :, rows], rate_out.at[:, :, rows]),), sems, 2 * CHUNKS + part
        )
        if passing and part == CHUNKS // 2:
            passing.middle()
    wait_all(outgoing)
    if passing:
        passing.end()


def moved_on(old, slopes, rough, delta, wet_now):
    h, hu, hv = (value - delta * slope for value, slope in zip(old, slopes))
    inverse = 1.0 / h
    u = hu * inverse
    v = hv * inverse
    speed = jnp.sqrt(u * u + v * v)
    power = jnp.exp((-4.0 / 3.0) * jnp.log(jnp.abs(h)))
    drag = (GRAVITY * delta) * (rough * rough) * (speed * power)
    factor = 1.0 / (1.0 + drag)
    fresh = (h, hu * factor, hv * factor)
    return tuple(jnp.where(wet_now, new, value) for new, value in zip(fresh, old))


def repeat_steps(ctl, wet_from, deltas, early, work, other, sems):
    incoming = []
    for ref in early:
        begin = 0 if ref is early[0] else early[0].shape[1]
        incoming += start_all(
            ((ref, work.at[:, begin : begin + ref.shape[1]]),), sems, len(incoming)
        )
    row_ids = lax.broadcasted_iota(jnp.int32, (ROWS, TILE), 0)
    lane = lax.broadcasted_iota(jnp.int32, (ROWS, LANES), 1)
    start = tuple(jnp.zeros((1, TILE), jnp.float32) for _ in range(4))

    def halves(value):
        return value[:, :LANES], value[:, LANES:]

    def right_of(value):
        low, high = (pltpu.roll(part, LANES - 1, 1) for part in halves(value))
        return jnp.concatenate([jnp.where(lane == LANES - 1, high, low), high], 1)

    def left_of(value):
        low, high = (pltpu.roll(part, 1, 1) for part in halves(value))
        return jnp.concatenate([low, jnp.where(lane == 0, low, high)], 1)

    def down(value):
        return pltpu.roll(value, ROWS + 7, 0)[:ROWS]

    for step in range(STEPS):
        source, target = (work, other) if step % 2 == 0 else (other, work)
        delta = deltas[step][0:1, :]
        wet_now = flag(ctl, wet_from + step)

        def group(index, carry, source=source, target=target, delta=delta, wet_now=wet_now):
            base = pl.multiple_of(index * ROWS, ROWS)
            rows = pl.ds(base, ROWS)
            after = pl.ds(pl.multiple_of(jnp.minimum(base + ROWS, EARLY - 8), 8), 8)
            refs = [source.at[field] for field in range(3)] + [work.at[3]]
            fields = [jnp.concatenate([ref[rows, :], ref[after, :]], 0) for ref in refs]
            cells_x, cells_y = cell(*fields[:3])
            here_x = tuple(value[:ROWS] for value in cells_x)
            here_y = tuple(value[:ROWS] for value in cells_y)
            faces_x = face(here_x, tuple(down(value) for value in cells_x))
            turned = tuple(pltpu.roll(value, 1, 0) for value in faces_x)
            change_x = tuple(
                value - jnp.where(row_ids == 0, before, moved)
                for value, before, moved in zip(faces_x, carry[:3], turned)
            )
            ground = fields[3][:ROWS]
            ground_up = pltpu.roll(ground, 1, 0)
            slope_x = down(fields[3]) - jnp.where(row_ids == 0, carry[3], ground_up)
            carried = tuple(value[0:1, :] for value in turned) + (ground_up[0:1, :],)
            faces_y = face(here_y, tuple(right_of(value) for value in here_y))
            change_y = tuple(value - left_of(value) for value in faces_y)
            slope_y = right_of(ground) - left_of(ground)
            old = tuple(value[:ROWS] for value in fields[:3])
            weight = SLOPE * old[0]
            slopes = (
                SCALE * (change_x[0] + change_y[0]),
                SCALE * (change_x[1] + change_y[2]) + weight * slope_x,
                SCALE * (change_x[2] + change_y[1]) + weight * slope_y,
            )
            for field, value in enumerate(
                moved_on(old, slopes, work[4, rows, :], delta, wet_now)
            ):
                target[field, rows, :] = value
            return carried

        if step == 0:
            wait_all(incoming)
        lax.fori_loop(0, EARLY // ROWS, group, start)


def late_rows(tile, late):
    row = sublanes()
    kept = EARLY - 8
    lane = lax.broadcasted_iota(jnp.int32, (8, LANES), 1)
    for field in range(3):
        late[field, 0:8, :] = jnp.where(
            row < 3, tile[field, 0:8, :], tile[field, kept : kept + 8, :]
        )
        packed = [jnp.zeros((8, LANES), jnp.float32)] * 2
        for block in range(EARLY // 8):
            rows = slice(8 * block, 8 * block + 8)
            sides = jnp.where(lane < 64, tile[field, rows, :LANES], tile[field, rows, LANES:])
            turned = pltpu.roll(sides, (3 + 8 * block) % LANES, 1)
            which = block // 16
            packed[which] = jnp.where(lane // 8 == block % 16, turned, packed[which])
        late[field, 8:16, :] = jnp.concatenate(packed, 1)
        late[field, 16:, :] = tile[field, EARLY:, :]


def merge(late, early, tile):
    row = sublanes()
    lane = lax.broadcasted_iota(jnp.int32, (8, LANES), 1)
    for field in range(3):
        first = late[field, 0:8, :]
        for block in range(EARLY // 8):
            rows = slice(8 * block, 8 * block + 8)
            which = block // 16
            packed = late[field, 8:16, which * LANES : (which + 1) * LANES]
            sides = pltpu.roll(packed, (-3 - 8 * block) % LANES, 1)
            value = early[field, rows, :]
            value = jnp.concatenate(
                [
                    jnp.where(lane < 3, sides, value[:, :LANES]),
                    jnp.where(lane >= LANES - 3, sides, value[:, LANES:]),
                ],
                1,
            )
            if block == 0:
                value = jnp.where(row < 3, first, value)
            if block == EARLY // 8 - 1:
                value = jnp.where(row < 5, value, first)
            tile[field, rows, :] = value
        tile[field, EARLY:, :] = late[field, 16:, :]


def repeat_second(ctl, delta0, delta1, delta2, low, high, late, out, late_out, work, tile, sems):
    near = start_all(((late, late_out),), sems, 2)
    repeat_steps(ctl, WET_SECOND, (delta0, delta1, delta2), (low, high), work, tile, sems)
    wait_all(start_all(((tile, out),), sems) + near)


def repeat_first(
    ctl, delta0, delta1, delta2, early, late_in, state, out, work, other, tile, late, sems
):
    rest = out.at[1 - ctl[MOVE + 1]]
    again = ctl[MOVE] == ctl[MOVE + 1]

    @pl.when(again)
    def _():
        wait_all(start_all(((state.at[1 - ctl[MOVE]], tile),), sems))

    @pl.when(jnp.logical_not(again))
    def _():
        copies = start_all(((late_in, late),), sems, 1)
        repeat_steps(ctl, WET_FIRST, (delta0, delta1, delta2), (early,), work, other, sems)
        wait_all(copies)
        merge(late, other, tile)

    wait_all(start_all(((tile, rest),), sems))


def finish(ctl, late_in, early_in, before, out, late, early, tile, sems):
    del before
    wait_all(start_all(((late_in, late), (early_in, early)), sems))
    merge(late, early, tile)
    wait_all(start_all(((tile, out.at[ctl[MOVE + 1]]),), sems))


def second_late(ctl, arrived, own, order, leaving, buffer, sems):
    del order
    again = ctl[MOVE] == ctl[MOVE + 1]

    @pl.when(again)
    def _():
        pltpu.make_async_copy(arrived, buffer, sems.at[0]).start()

    @pl.when(jnp.logical_not(again))
    def _():
        pltpu.make_async_copy(own, buffer, sems.at[0]).start()

    pltpu.make_async_copy(arrived, buffer, sems.at[0]).wait()
    wait_all(start_all(((buffer, leaving),), sems))


def correct_rows(ctl, slot, got, ground, block, state, rate, bottom):
    position = jnp.where(ctl[SLOT_LOW] == slot, 0, 1)
    device = lax.axis_index("xb") * 2 + lax.axis_index("yb")
    wall = WALL_WEST if bottom else WALL_EAST

    @pl.when(jnp.logical_not(flag(ctl, wall + position)))
    def _():
        peer = device - 2 if bottom else device + 2
        lines = got[pl.ds(pl.multiple_of(peer * block, 8), 8), :]
        grounds = ground[pl.ds(pl.multiple_of(peer * 16 + 8, 8), 8), :]

        def line(value, offset):
            picked = jnp.where(
                position == 0, value[offset : offset + 1, :], value[offset + 3 : offset + 4, :]
            )
            return jnp.broadcast_to(picked, (8, TILE))

        ghost, _ = cell(*(line(lines, field) for field in range(3)))
        ghost_ground = jnp.where(position == 0, grounds[0:1, :], grounds[1:2, :])
        rows = slice(0, 8) if bottom else slice(TILE - 8, TILE)
        own = [state[slot, field, rows, :] for field in range(3)]
        here, _ = cell(*own)
        fluxes = face(ghost, here) if bottom else face(here, ghost)
        push = SCALE * fluxes[1] + (SLOPE * own[0]) * ghost_ground
        row = sublanes()
        sign = -1.0 if bottom else 1.0
        chosen = row == (0 if bottom else 7)
        for field, value in enumerate((SCALE * fluxes[0], push, SCALE * fluxes[2])):
            rate[slot, field, rows, :] += jnp.where(chosen, sign * value, 0.0)


def column_fix(got, ground, block, columns, bed_columns):
    upper = lax.axis_index("yb")
    device = lax.axis_index("xb") * 2 + upper
    peer = device + 1 - 2 * upper
    lines = got[pl.ds(pl.multiple_of(peer * block, 8), 8), :]
    ghost_ground = ground[pl.ds(pl.multiple_of(peer * 16, 8), 8), :][3:4]
    del bed_columns
    mine = columns[...]
    _, ghost = cell(lines[0:1], lines[1:2], lines[2:3])
    _, own = cell(mine[0:1], mine[1:2], mine[2:3])
    low = upper == 0
    left = tuple(jnp.where(low, a, b) for a, b in zip(own, ghost))
    right = tuple(jnp.where(low, b, a) for a, b in zip(own, ghost))
    fluxes = face(left, right)
    sign = jnp.where(low, 1.0, -1.0)
    push = SCALE * fluxes[1] + (SLOPE * mine[0:1]) * ghost_ground
    block8 = stacked(
        [sign * SCALE * fluxes[0], sign * SCALE * fluxes[2], sign * push],
        jnp.zeros((8, TILE), jnp.float32),
    )
    return jnp.transpose(
        jnp.concatenate([block8, jnp.zeros((LANES - 8, TILE), jnp.float32)], 0)
    )


def update(step, ctl, got_in, ground_in, columns_in, state_in, manning_in, rate_in, *rest):
    more = step + 1 < STEPS
    fresh_out, first_out, second_out, delta_out = rest[:4]
    rest = rest[4:]
    state, manning, rate, fresh, got, ground, columns, first, second, delta_keep, sems = rest
    out, columns_out = late_first, late_second = first, second
    small = start_all(
        ((got_in, got), (ground_in, ground), (columns_in, columns)), sems, 5 * PARTS
    )
    size = 2 * TILE // PARTS
    parts = [
        (slot, slice(k * size, (k + 1) * size)) for slot in range(2) for k in range(PARTS // 2)
    ]
    incoming = []
    for index, (slot, rows) in enumerate(parts):
        incoming.append(
            start_all(
                (
                    (rate_in.at[slot, :, rows], rate.at[slot, :, rows]),
                    (state_in.at[slot, :, rows], state.at[slot, :, rows]),
                    (manning_in.at[slot, rows], manning.at[slot, rows]),
                ),
                sems,
                3 * index,
            )
        )
    wait_all(small)
    upper = lax.axis_index("yb")
    devices = 2 * lax.axis_size("xb")
    block = got.shape[0] // devices
    tops = got[0:8, :]
    for peer in range(1, devices):
        tops = jnp.maximum(tops, got[peer * block : peer * block + 8, :])
    delta = (COURANT * SPACING) / tops[TOP : TOP + 1, :]
    delta_keep[...] = jnp.broadcast_to(delta, (8, TILE))
    outgoing = start_all(((delta_keep, delta_out),), sems, 5 * PARTS + 3)
    fix = column_fix(got, ground, block, columns, None)
    facing = jnp.where(upper > 0, ctl[SLOT_LOW], 1 - ctl[SLOT_LOW])
    begin = pl.multiple_of((1 - upper) * LANES, LANES)
    target = (1 - upper) * (LANES - 1)
    lane = lax.broadcasted_iota(jnp.int32, (size, LANES), 1)
    total = jnp.zeros((ROWS, TILE), jnp.float32)
    for index, (slot, part_rows) in enumerate(parts):
        wait_all(incoming[index])
        if part_rows.start == 0:
            correct_rows(ctl, slot, got, ground, block, state, rate, True)
        if part_rows.stop == TILE:
            correct_rows(ctl, slot, got, ground, block, state, rate, False)

        @pl.when(facing == slot)
        def _(slot=slot, part_rows=part_rows):
            for field in range(3):
                turned = pltpu.roll(
                    fix[part_rows], lax.rem(target + LANES - field, LANES), 1
                )
                rate[slot, field, part_rows, pl.ds(begin, LANES)] += jnp.where(
                    lane == target, turned, 0.0
                )

        wet_now = flag(ctl, WET + 2 * step + slot)

        def group(index, best, slot=slot, wet_now=wet_now):
            rows = pl.ds(pl.multiple_of(index * ROWS, ROWS), ROWS)
            old = tuple(state[slot, field, rows, :] for field in range(3))
            slopes = tuple(rate[slot, field, rows, :] for field in range(3))
            h, hu, hv = moved_on(old, slopes, manning[slot, rows, :], delta, wet_now)
            fresh[slot, 0, rows, :] = h
            fresh[slot, 1, rows, :] = hu
            fresh[slot, 2, rows, :] = hv
            if more:
                along_x, along_y = cell(h, hu, hv)
                best = jnp.maximum(best, jnp.maximum(along_x[5], along_y[5]))
            return best

        best = lax.fori_loop(
            part_rows.start // ROWS,
            part_rows.stop // ROWS,
            group,
            jnp.zeros((ROWS, TILE), jnp.float32),
        )
        if more:
            best = jnp.where(flag(ctl, WET + 2 * step + 2 + slot), best, 0.0)
            total = jnp.maximum(total, best)
        outgoing += start_all(
            ((fresh.at[slot, :, part_rows], fresh_out.at[slot, :, part_rows]),),
            sems,
            3 * PARTS + index,
        )
    if more:
        messages(ctl, fresh, None, jnp.max(total, keepdims=True), out, columns_out)
        outgoing += start_all(((out, first_out), (columns_out, second_out)), sems, 4 * PARTS)
    else:
        late_rows(fresh.at[ctl[MOVE]], late_first)
        outgoing += start_all(((late_first, first_out),), sems, 4 * PARTS)
        late_rows(fresh.at[1 - ctl[MOVE]], late_second)
        outgoing += start_all(((late_second, second_out),), sems, 4 * PARTS + 1)
    wait_all(outgoing)


def vmem():
    return pl.BlockSpec(memory_space=pltpu.VMEM)


def smem():
    return pl.BlockSpec(memory_space=pltpu.SMEM)


def hbm():
    return pl.BlockSpec(memory_space=pltpu.HBM)


def anywhere():
    return pl.BlockSpec(memory_space=pl.ANY)


def call(
    kernel, outs, out_specs, in_specs, flops, scratch=(), aliases=None, room=VMEM_BYTES, moved=4
):
    return pl.pallas_call(
        kernel,
        scratch_shapes=scratch,
        input_output_aliases=aliases or {},
        out_shape=outs,
        in_specs=in_specs,
        out_specs=out_specs,
        compiler_params=pltpu.CompilerParams(vmem_limit_bytes=room),
        cost_estimate=pl.CostEstimate(flops=flops, bytes_accessed=moved << 20, transcendentals=0),
    )


def f32(*shape):
    return jax.ShapeDtypeStruct(shape, jnp.float32)


def spread(fast):
    return lax.all_to_all(fast, ("xb", "yb"), split_axis=0, concat_axis=0, tiled=True)


def body(state, bed, manning, neighbours, wet, moves):
    shape = f32(*state.shape)
    devices = lax.axis_size("xb") * lax.axis_size("yb")
    sem = [pltpu.SemaphoreType.DMA((1,))]
    whole = pltpu.VMEM(state.shape, jnp.float32)
    part = pltpu.VMEM(bed.shape, jnp.float32)
    tile_shape = f32(*state.shape[1:])
    early_shape = f32(5, EARLY, TILE)
    early_state = f32(3, EARLY, TILE)
    late_shape = f32(3, LATE, TILE)
    delta_shape = f32(8, TILE)

    def buffer(like):
        return pltpu.VMEM(like.shape, jnp.float32)

    out, columns, ctl, leaving = call(
        opening,
        (
            f32(16 * devices, TILE),
            f32(8, TILE),
            jax.ShapeDtypeStruct((CONTROLS,), jnp.int32),
            early_shape,
        ),
        (vmem(), vmem(), smem(), hbm()),
        [hbm()] * 6,
        4 << 20,
        [
            whole,
            part,
            pltpu.VMEM((EARLY, TILE), jnp.float32),
            pltpu.SMEM(neighbours.shape[::-1], jnp.int32),
            pltpu.SMEM(wet.shape, jnp.int32),
            pltpu.SMEM(moves.shape, jnp.int32),
            pltpu.SemaphoreType.DMA((10,)),
        ],
    )(state, bed, manning, neighbours.T, wet, moves)
    state_first = state
    ground = None
    deltas = []
    for step in range(STEPS):
        got = spread(out)
        ground = got if step == 0 else ground
        scratch = [whole, part, whole, pltpu.SemaphoreType.DMA((3 * CHUNKS,))]
        if step == 0:
            early_first = shifted(leaving, "xb", 1)
            rate = call(rates, shape, hbm(), [smem(), hbm(), hbm()], 16 << 20, scratch)(
                ctl, state, bed
            )
        elif step == 1:
            rate, *leaving = call(
                rates_and_leaving,
                (shape,) + tuple(f32(5, end - begin, TILE) for begin, end in PIECES),
                (hbm(),) * 3,
                [smem()] + [hbm()] * 5,
                16 << 20,
                scratch + [buffer(early_shape), pltpu.SemaphoreType.DMA((3,))],
            )(ctl, state, bed, state_first, manning, early_first)
            early_second = [shifted(piece, "xb", 1) for piece in leaving]
        else:
            rate = call(rates_after, shape, hbm(), [smem()] + [hbm()] * 3, 16 << 20, scratch)(
                ctl, state, bed, early_second[0]
            )
        more = step + 1 < STEPS
        if more:
            shapes = f32(8 * devices, TILE), f32(8, TILE)
        else:
            shapes = late_shape, late_shape
        outs = call(
            functools.partial(update, step),
            (shape,) + shapes + (delta_shape,),
            (hbm(),) * 4,
            [smem()] + [hbm()] * 6,
            8 << 20,
            [
                whole,
                part,
                whole,
                whole,
                pltpu.VMEM(got.shape, jnp.float32),
                pltpu.VMEM(ground.shape, jnp.float32),
                pltpu.VMEM((8, TILE), jnp.float32),
                buffer(shapes[0]),
                buffer(shapes[1]),
                buffer(delta_shape),
                pltpu.SemaphoreType.DMA((5 * PARTS + 4,)),
            ],
            moved=16 if step == 0 else 4,
        )(ctl, got, ground, columns, state, manning, rate)
        deltas.append(outs[-1])
        state, out, columns, _ = outs
    late_first, late_second = out, columns
    room = 16 << 20
    late_arrived = shifted(late_first, "xb", 1)
    second, late_second = call(
        repeat_second,
        (early_state, late_shape),
        (anywhere(), vmem()),
        [smem()] + [vmem()] * 3 + [anywhere()] * 3,
        8 << 20,
        [buffer(early_shape), buffer(early_state), pltpu.SemaphoreType.DMA((3,))],
        room=room,
    )(ctl, *deltas, *early_second, late_second)
    leaving = call(
        second_late,
        late_shape,
        anywhere(),
        [smem(), anywhere(), anywhere(), anywhere()],
        1 << 20,
        [buffer(late_shape)] + sem,
        room=room,
    )(ctl, late_arrived, late_second, second)
    late_next = shifted(leaving, "xb", 1)
    final = call(
        repeat_first,
        shape,
        hbm(),
        [smem()] + [vmem()] * 3 + [anywhere()] * 3,
        8 << 20,
        [
            buffer(early_shape),
            buffer(early_state),
            buffer(tile_shape),
            buffer(late_shape),
            pltpu.SemaphoreType.DMA((2,)),
        ],
        room=room,
    )(ctl, *deltas, early_first, late_arrived, state)
    return call(
        finish,
        shape,
        hbm(),
        [smem(), anywhere(), anywhere(), hbm()],
        1 << 20,
        [
            buffer(late_shape),
            buffer(early_state),
            buffer(tile_shape),
            pltpu.SemaphoreType.DMA((2,)),
        ],
        {3: 0},
        room=room,
    )(ctl, late_next, second, final)


def solution(mesh):
    placed = (
        P(("runs", "xb", "yb"), None, None, None),
        P(("runs", "xb", "yb"), None, None),
        P(("runs", "xb", "yb"), None, None),
        P("runs", None),
        P(None, "runs"),
        P(None, "runs"),
    )
    return jax.shard_map(
        body,
        mesh=mesh,
        in_specs=placed,
        out_specs=P(("runs", "xb", "yb"), None, None, None),
        check_vma=False,
    )
```

```python
import functools

import jax
import jax.numpy as jnp
from jax import lax
from jax.experimental import pallas as pl
from jax.experimental.pallas import tpu as pltpu
from jax.sharding import PartitionSpec as P

STEPS = 3
GRAVITY = 9.81
ROOT_G = GRAVITY**0.5
SPACING = 5.0
COURANT = 0.2
ROWS = 32
LANES = 128
TILE = 256
VMEM_BYTES = 60 * 1024 * 1024
SLOT_LOW, WALL_WEST, WALL_EAST, WALL_OUTER, WET, MOVE = 0, 1, 3, 5, 7, 13
WET_FIRST, WET_SECOND = 16, 19
CONTROLS = 24
EARLY = 160
PIECES = ((0, 80), (80, 160))
LATE = TILE - EARLY + 16
CHUNKS = 8
PARTS = 8
STRIP = 16
TOP = 6
SCALE = 0.5 / SPACING
SLOPE = GRAVITY / (2.0 * SPACING)


def shifted(value, axis, steps, around=True):
    count = lax.axis_size(axis)
    pairs = [(source, (source + steps) % count) for source in range(count)]
    if not around:
        pairs = [pair for pair in pairs if abs(pair[0] - pair[1]) == abs(steps)]
    return lax.ppermute(value, axis, pairs)


def cell(h, hu, hv):
    root = lax.rsqrt(h)
    inverse = root * root
    u = hu * inverse
    v = hv * inverse
    celerity = ROOT_G * (h * root)
    pressure = (0.5 * GRAVITY) * (h * h)
    cross = hu * v
    speed_x = jnp.abs(u) + celerity
    speed_y = jnp.abs(v) + celerity
    along_x = (h, hu, hv, hu * u + pressure, cross, speed_x)
    along_y = (h, hv, hu, hv * v + pressure, cross, speed_y)
    return along_x, along_y


def face(left, right):
    wave = jnp.maximum(left[5], right[5])
    return (
        (left[1] + right[1]) - wave * (right[0] - left[0]),
        (left[3] + right[3]) - wave * (right[1] - left[1]),
        (left[4] + right[4]) - wave * (right[2] - left[2]),
    )


def slot_of(ctl, position):
    low = ctl[SLOT_LOW]
    return low if position == 0 else 1 - low


def flag(ctl, index):
    return ctl[index] > 0


def start_all(pairs, sems, first=0):
    copies = [
        pltpu.make_async_copy(src, dst, sems.at[first + k]) for k, (src, dst) in enumerate(pairs)
    ]
    for copy in copies:
        copy.start()
    return copies


def wait_all(copies):
    for copy in copies:
        copy.wait()


def sublanes(width=TILE):
    return lax.broadcasted_iota(jnp.int32, (8, width), 0)


def stacked(lines, base):
    row = sublanes()
    for index, line in enumerate(lines):
        base = jnp.where(row == index, jnp.broadcast_to(line, (8, TILE)), base)
    return base


def messages(ctl, state, bed, fastest, out, columns):
    upper = lax.axis_index("yb")
    column = lax.axis_index("xb")
    last = lax.axis_size("xb") - 1
    devices = 2 * (last + 1)
    block = out.shape[0] // devices
    device = column * 2 + upper
    top = jnp.broadcast_to(fastest, (8, TILE))
    for peer in range(devices):
        out[peer * block : peer * block + 8, :] = top
    row = sublanes()

    def edge(line):
        rows = slice(line, line + 1)
        slots = [slot_of(ctl, position) for position in range(2)]
        fields = [state[slot, field, rows, :] for slot in slots for field in range(3)]
        return stacked(fields, top), [bed[slot, rows, :] for slot in slots] if bed is not None else None

    for inside, peer, line in (
        (column > 0, device - 2, 0),
        (column < last, device + 2, TILE - 1),
    ):

        @pl.when(inside)
        def _(peer=peer, line=line):
            lines, ground = edge(line)
            start = pl.multiple_of(peer * block, 8)
            out[pl.ds(start, 8), :] = lines
            if ground:
                out[pl.ds(pl.multiple_of(start + 8, 8), 8), :] = stacked(ground, top)

    slot = jnp.where(upper > 0, ctl[SLOT_LOW], 1 - ctl[SLOT_LOW])
    begin = pl.multiple_of((1 - upper) * LANES, LANES)
    lane = lax.broadcasted_iota(jnp.int32, (TILE, LANES), 1)
    packed = None
    for field in range(4 if bed is not None else 3):
        if field < 3:
            part = state[slot, field, :, pl.ds(begin, LANES)]
        else:
            part = bed[slot, :, pl.ds(begin, LANES)]
        turned = pltpu.roll(part, field + 1 - upper, 1)
        packed = turned if field == 0 else jnp.where(lane == field, turned, packed)
    lines = jnp.transpose(packed)[:8]
    columns[...] = lines
    start = pl.multiple_of((device + 1 - 2 * upper) * block, 8)
    out[pl.ds(start, 8), :] = jnp.where(row == TOP, top, lines)


def opening(
    state_in, bed_in, manning_in, neighbours_in, wet_in, moves_in,
    out, columns, ctl, leaving_low, leaving_high,
    state, bed, manning, neighbours, wet, moves, sems,
):
    copies = start_all(
        (
            (neighbours_in, neighbours),
            (wet_in, wet),
            (moves_in, moves),
            (state_in.at[0], state.at[0]),
            (state_in.at[1], state.at[1]),
            (bed_in, bed),
        ),
        sems,
    )
    device = lax.axis_index("xb") * 2 + lax.axis_index("yb")
    wait_all(copies[:3])
    first = device * 2
    low = jnp.where(neighbours[3, first] == first + 1, 0, 1)
    ctl[SLOT_LOW] = low
    for position in range(2):
        slot = low if position == 0 else 1 - low
        tile = first + slot
        ctl[WALL_WEST + position] = (neighbours[0, tile] < 0).astype(jnp.int32)
        ctl[WALL_EAST + position] = (neighbours[1, tile] < 0).astype(jnp.int32)
        ctl[WALL_OUTER + position] = (neighbours[2 + position, tile] < 0).astype(jnp.int32)
    for step in range(STEPS):
        for slot in range(2):
            ctl[WET + 2 * step + slot] = wet[step, first + slot]
        ctl[MOVE + step] = moves[step, device]
    moving = moves[0, device]
    rough = start_all(((manning_in.at[moving, 0:EARLY], manning),), sems, 6)
    count = lax.axis_size("xb")
    upper = lax.axis_index("yb")
    column = lax.axis_index("xb")
    source = lax.rem(column + count - 1, count) * 2 + upper
    before = lax.rem(column + count - 2, count) * 2 + upper
    again = moves[0, source] == moves[1, source]
    tile_first = source * 2 + moves[0, source]
    tile_second = jnp.where(
        again, before * 2 + moves[0, before], source * 2 + 1 - moves[0, source]
    )
    for step in range(STEPS):
        ctl[WET_FIRST + step] = wet[step, tile_first]
        ctl[WET_SECOND + step] = wet[step, tile_second]

    wait_all(copies[3:] + rough)
    early = []
    for (begin, end), leaving in zip(PIECES, (leaving_low, leaving_high)):
        early += start_all(
            (
                (state.at[moving, :, begin:end], leaving.at[0:3]),
                (bed.at[moving, begin:end], leaving.at[3]),
                (manning.at[begin:end], leaving.at[4]),
            ),
            sems,
            7 + len(early),
        )
    total = jnp.zeros((ROWS, TILE), jnp.float32)
    for slot in range(2):

        def group(index, best, slot=slot):
            rows = pl.ds(pl.multiple_of(index * ROWS, ROWS), ROWS)
            along_x, along_y = cell(*(state[slot, field, rows, :] for field in range(3)))
            return jnp.maximum(best, jnp.maximum(along_x[5], along_y[5]))

        best = lax.fori_loop(0, TILE // ROWS, group, jnp.zeros((ROWS, TILE), jnp.float32))
        total = jnp.maximum(total, jnp.where(wet[0, first + slot] > 0, best, 0.0))
    messages(ctl, state, bed, jnp.max(total, keepdims=True), out, columns)
    wait_all(early)


class Passing:
    def __init__(self, ctl, state_in, bed_in, manning_in, arrived, leaving, buffer, sems):
        self.again = ctl[MOVE] == ctl[MOVE + 1]
        self.other = 1 - ctl[MOVE]
        self.refs = state_in, bed_in, manning_in, arrived, buffer, sems
        self.outgoing = [
            pltpu.make_async_copy(buffer.at[:, begin:end], piece, sems.at[1 + index])
            for index, ((begin, end), piece) in enumerate(zip(PIECES, leaving))
        ]

    def start(self):
        state_in, bed_in, manning_in, arrived, buffer, sems = self.refs
        rows = slice(0, EARLY)
        sem = sems.at[0]

        @pl.when(self.again)
        def _():
            for (begin, end), piece in zip(PIECES, arrived):
                pltpu.make_async_copy(piece, buffer.at[:, begin:end], sem).start()

        @pl.when(jnp.logical_not(self.again))
        def _():
            pltpu.make_async_copy(state_in.at[self.other, :, rows], buffer.at[0:3], sem).start()
            pltpu.make_async_copy(bed_in.at[self.other, rows], buffer.at[3], sem).start()
            pltpu.make_async_copy(manning_in.at[self.other, rows], buffer.at[4], sem).start()

    def middle(self):
        _, _, _, arrived, buffer, sems = self.refs
        for (begin, end), piece in zip(PIECES, arrived):
            pltpu.make_async_copy(piece, buffer.at[:, begin:end], sems.at[0]).wait()
        for copy in self.outgoing:
            copy.start()

    def end(self):
        wait_all(self.outgoing)


def rates_and_leaving(
    ctl, state_in, bed_in, state_first, manning_in, arrived_low, arrived_high,
    rate_out, leaving_low, leaving_high,
    state, bed, rate, sems, buffer, moving,
):
    arrived = arrived_low, arrived_high
    passing = Passing(
        ctl, state_first, bed_in, manning_in, arrived, (leaving_low, leaving_high), buffer, moving
    )
    rates(ctl, state_in, bed_in, rate_out, state, bed, rate, sems, passing)


def rates_after(ctl, state_in, bed_in, order, *rest):
    del order
    rates(ctl, state_in, bed_in, *rest)


def rates(ctl, state_in, bed_in, rate_out, state, bed, rate, sems, passing=None):
    width = 2 * TILE
    row_ids = lax.broadcasted_iota(jnp.int32, (STRIP, width), 0)
    row8 = sublanes(width)
    lane = lax.broadcasted_iota(jnp.int32, (STRIP, LANES), 1)
    last = TILE // STRIP - 1
    chunk = TILE // CHUNKS
    slots = [slot_of(ctl, position) for position in range(2)]
    incoming = []
    for part in range(CHUNKS):
        rows = slice(part * chunk, (part + 1) * chunk)
        incoming.append(
            start_all(
                (
                    (state_in.at[:, :, rows], state.at[:, :, rows]),
                    (bed_in.at[:, rows], bed.at[:, rows]),
                ),
                sems,
                2 * part,
            )
        )
    if passing:
        passing.start()
    keep_west, keep_east, keep_south, keep_north = (
        jnp.where(flag(ctl, index), 1.0, 0.0)
        for index in (WALL_WEST, WALL_EAST, WALL_OUTER, WALL_OUTER + 1)
    )

    def strip(field, rows):
        if field == 3:
            return jnp.concatenate([bed[slot, rows, :] for slot in slots], 1)
        return jnp.concatenate([state[slot, field, rows, :] for slot in slots], 1)

    def blocks(value):
        return [value[:, k * LANES : (k + 1) * LANES] for k in range(4)]

    def right_of(value, end=None):
        turned = [pltpu.roll(part, LANES - 1, 1) for part in blocks(value)]
        after = turned[1:] + [turned[3] if end is None else end]
        return jnp.concatenate(
            [
                jnp.where(lane == LANES - 1, following, part)
                if following is not part
                else part
                for part, following in zip(turned, after)
            ],
            1,
        )

    def left_of(value, end):
        turned = [pltpu.roll(part, 1, 1) for part in blocks(value)]
        before = [end] + turned[:3]
        return jnp.concatenate(
            [jnp.where(lane == 0, previous, part) for part, previous in zip(turned, before)], 1
        )

    def down(value):
        return pltpu.roll(value, STRIP + 7, 0)[:STRIP]

    def group(index, carry):
        base = pl.multiple_of(index * STRIP, STRIP)
        rows = pl.ds(base, STRIP)
        after = pl.ds(pl.multiple_of(jnp.minimum(base + STRIP, TILE - 8), 8), 8)
        at_end = index == last
        fields = [
            jnp.concatenate([strip(field, rows), strip(field, after)], 0) for field in range(3)
        ]
        cells_x, cells_y = cell(*fields)
        here_x = tuple(value[:STRIP] for value in cells_x)
        here_y = tuple(value[:STRIP] for value in cells_y)

        ending = jnp.logical_and(row8 == 7, at_end)
        faces = list(face(here_x, tuple(down(value) for value in cells_x)))
        wall = keep_east * (2.0 * (here_x[3] + here_x[5] * here_x[1])[STRIP - 8 :])
        for component, value in enumerate((0.0, wall, 0.0)):
            upper = faces[component]
            faces[component] = jnp.concatenate(
                [upper[: STRIP - 8], jnp.where(ending, value, upper[STRIP - 8 :])], 0
            )
        turned = tuple(pltpu.roll(value, 1, 0) for value in faces)
        change_x = tuple(
            value - jnp.where(row_ids == 0, before, moved)
            for value, before, moved in zip(faces, carry[:3], turned)
        )
        ground = strip(3, rows)
        ground_after = jnp.where(
            at_end,
            jnp.broadcast_to(keep_east * ground[STRIP - 1 :], (8, width)),
            strip(3, after),
        )
        ground_up = pltpu.roll(ground, 1, 0)
        slope_x = down(jnp.concatenate([ground, ground_after], 0)) - jnp.where(
            row_ids == 0, carry[3], ground_up
        )
        carried = tuple(value[0:1, :] for value in turned) + (ground_up[0:1, :],)

        faces_y = list(face(here_y, tuple(right_of(value) for value in here_y)))
        normal = here_y[3]
        spread_y = here_y[5] * here_y[1]
        north = keep_north * (2.0 * (normal + spread_y)[:, width - LANES :])
        south = keep_south * (2.0 * (normal - spread_y)[:, :LANES])
        change_y = []
        for component, (high, low) in enumerate(((0.0, 0.0), (north, south), (0.0, 0.0))):
            parts = blocks(faces_y[component])
            parts[3] = jnp.where(lane == LANES - 1, high, parts[3])
            value = jnp.concatenate(parts, 1)
            change_y.append(value - left_of(value, low))
        slope_y = right_of(ground, keep_north * ground[:, width - LANES :]) - left_of(
            ground, keep_south * ground[:, :LANES]
        )
        weight = SLOPE * here_x[0]
        results = (
            SCALE * (change_x[0] + change_y[0]),
            SCALE * (change_x[1] + change_y[2]) + weight * slope_x,
            SCALE * (change_x[2] + change_y[1]) + weight * slope_y,
        )
        for field, value in enumerate(results):
            for position, slot in enumerate(slots):
                rate[slot, field, rows, :] = value[:, position * TILE : (position + 1) * TILE]
        return carried

    wait_all(incoming[0])
    top, _ = cell(*(strip(field, slice(0, 8)) for field in range(3)))
    nothing = jnp.zeros((1, width), jnp.float32)
    carry = (
        nothing,
        keep_west * (2.0 * (top[3] - top[5] * top[1])[0:1]),
        nothing,
        keep_west * strip(3, slice(0, 8))[0:1],
    )
    per_chunk = chunk // STRIP
    outgoing = []
    for part in range(CHUNKS):
        if part + 1 < CHUNKS:
            wait_all(incoming[part + 1])
        carry = lax.fori_loop(part * per_chunk, (part + 1) * per_chunk, group, carry)
        rows = slice(part * chunk, (part + 1) * chunk)
        outgoing += start_all(
            ((rate.at[:, :, rows], rate_out.at[:, :, rows]),), sems, 2 * CHUNKS + part
        )
        if passing and part == CHUNKS // 2:
            passing.middle()
    wait_all(outgoing)
    if passing:
        passing.end()


def moved_on(old, slopes, rough, delta, wet_now):
    h, hu, hv = (value - delta * slope for value, slope in zip(old, slopes))
    inverse = 1.0 / h
    u = hu * inverse
    v = hv * inverse
    speed = jnp.sqrt(u * u + v * v)
    power = jnp.exp((-4.0 / 3.0) * jnp.log(jnp.abs(h)))
    drag = (GRAVITY * delta) * (rough * rough) * (speed * power)
    factor = 1.0 / (1.0 + drag)
    fresh = (h, hu * factor, hv * factor)
    return tuple(jnp.where(wet_now, new, value) for new, value in zip(fresh, old))


def repeat_steps(ctl, wet_from, deltas, early, work, other, sems):
    incoming = []
    for ref in early:
        begin = 0 if ref is early[0] else early[0].shape[1]
        incoming += start_all(
            ((ref, work.at[:, begin : begin + ref.shape[1]]),), sems, len(incoming)
        )
    row_ids = lax.broadcasted_iota(jnp.int32, (ROWS, TILE), 0)
    lane = lax.broadcasted_iota(jnp.int32, (ROWS, LANES), 1)
    start = tuple(jnp.zeros((1, TILE), jnp.float32) for _ in range(4))

    def halves(value):
        return value[:, :LANES], value[:, LANES:]

    def right_of(value):
        low, high = (pltpu.roll(part, LANES - 1, 1) for part in halves(value))
        return jnp.concatenate([jnp.where(lane == LANES - 1, high, low), high], 1)

    def left_of(value):
        low, high = (pltpu.roll(part, 1, 1) for part in halves(value))
        return jnp.concatenate([low, jnp.where(lane == 0, low, high)], 1)

    def down(value):
        return pltpu.roll(value, ROWS + 7, 0)[:ROWS]

    for step in range(STEPS):
        source, target = (work, other) if step % 2 == 0 else (other, work)
        delta = deltas[step][0:1, :]
        wet_now = flag(ctl, wet_from + step)

        def group(index, carry, source=source, target=target, delta=delta, wet_now=wet_now):
            base = pl.multiple_of(index * ROWS, ROWS)
            rows = pl.ds(base, ROWS)
            after = pl.ds(pl.multiple_of(jnp.minimum(base + ROWS, EARLY - 8), 8), 8)
            refs = [source.at[field] for field in range(3)] + [work.at[3]]
            fields = [jnp.concatenate([ref[rows, :], ref[after, :]], 0) for ref in refs]
            cells_x, cells_y = cell(*fields[:3])
            here_x = tuple(value[:ROWS] for value in cells_x)
            here_y = tuple(value[:ROWS] for value in cells_y)
            faces_x = face(here_x, tuple(down(value) for value in cells_x))
            turned = tuple(pltpu.roll(value, 1, 0) for value in faces_x)
            change_x = tuple(
                value - jnp.where(row_ids == 0, before, moved)
                for value, before, moved in zip(faces_x, carry[:3], turned)
            )
            ground = fields[3][:ROWS]
            ground_up = pltpu.roll(ground, 1, 0)
            slope_x = down(fields[3]) - jnp.where(row_ids == 0, carry[3], ground_up)
            carried = tuple(value[0:1, :] for value in turned) + (ground_up[0:1, :],)
            faces_y = face(here_y, tuple(right_of(value) for value in here_y))
            change_y = tuple(value - left_of(value) for value in faces_y)
            slope_y = right_of(ground) - left_of(ground)
            old = tuple(value[:ROWS] for value in fields[:3])
            weight = SLOPE * old[0]
            slopes = (
                SCALE * (change_x[0] + change_y[0]),
                SCALE * (change_x[1] + change_y[2]) + weight * slope_x,
                SCALE * (change_x[2] + change_y[1]) + weight * slope_y,
            )
            for field, value in enumerate(
                moved_on(old, slopes, work[4, rows, :], delta, wet_now)
            ):
                target[field, rows, :] = value
            return carried

        if step == 0:
            wait_all(incoming)
        lax.fori_loop(0, EARLY // ROWS, group, start)


def late_rows(tile, late):
    row = sublanes()
    kept = EARLY - 8
    lane = lax.broadcasted_iota(jnp.int32, (8, LANES), 1)
    for field in range(3):
        late[field, 0:8, :] = jnp.where(
            row < 3, tile[field, 0:8, :], tile[field, kept : kept + 8, :]
        )
        packed = [jnp.zeros((8, LANES), jnp.float32)] * 2
        for block in range(EARLY // 8):
            rows = slice(8 * block, 8 * block + 8)
            sides = jnp.where(lane < 64, tile[field, rows, :LANES], tile[field, rows, LANES:])
            turned = pltpu.roll(sides, (3 + 8 * block) % LANES, 1)
            which = block // 16
            packed[which] = jnp.where(lane // 8 == block % 16, turned, packed[which])
        late[field, 8:16, :] = jnp.concatenate(packed, 1)
        late[field, 16:, :] = tile[field, EARLY:, :]


def merge(late, early, tile):
    row = sublanes()
    lane = lax.broadcasted_iota(jnp.int32, (8, LANES), 1)
    for field in range(3):
        first = late[field, 0:8, :]
        for block in range(EARLY // 8):
            rows = slice(8 * block, 8 * block + 8)
            which = block // 16
            packed = late[field, 8:16, which * LANES : (which + 1) * LANES]
            sides = pltpu.roll(packed, (-3 - 8 * block) % LANES, 1)
            value = early[field, rows, :]
            value = jnp.concatenate(
                [
                    jnp.where(lane < 3, sides, value[:, :LANES]),
                    jnp.where(lane >= LANES - 3, sides, value[:, LANES:]),
                ],
                1,
            )
            if block == 0:
                value = jnp.where(row < 3, first, value)
            if block == EARLY // 8 - 1:
                value = jnp.where(row < 5, value, first)
            tile[field, rows, :] = value
        tile[field, EARLY:, :] = late[field, 16:, :]


def repeat_second(ctl, delta0, delta1, delta2, low, high, late, out, late_out, work, tile, sems):
    near = start_all(((late, late_out),), sems, 2)
    repeat_steps(ctl, WET_SECOND, (delta0, delta1, delta2), (low, high), work, tile, sems)
    wait_all(start_all(((tile, out),), sems) + near)


def repeat_first(
    ctl, delta0, delta1, delta2, low, high, late_in, state, out, work, other, tile, late, sems
):
    rest = out.at[1 - ctl[MOVE + 1]]
    again = ctl[MOVE] == ctl[MOVE + 1]

    @pl.when(again)
    def _():
        wait_all(start_all(((state.at[1 - ctl[MOVE]], tile),), sems))

    @pl.when(jnp.logical_not(again))
    def _():
        copies = start_all(((late_in, late),), sems, 2)
        repeat_steps(ctl, WET_FIRST, (delta0, delta1, delta2), (low, high), work, other, sems)
        wait_all(copies)
        merge(late, other, tile)

    wait_all(start_all(((tile, rest),), sems))


def finish(ctl, late_in, early_in, before, out, late, early, tile, sems):
    del before
    wait_all(start_all(((late_in, late), (early_in, early)), sems))
    merge(late, early, tile)
    wait_all(start_all(((tile, out.at[ctl[MOVE + 1]]),), sems))


def second_late(ctl, arrived, own, order, leaving, buffer, sems):
    del order
    again = ctl[MOVE] == ctl[MOVE + 1]

    @pl.when(again)
    def _():
        pltpu.make_async_copy(arrived, buffer, sems.at[0]).start()

    @pl.when(jnp.logical_not(again))
    def _():
        pltpu.make_async_copy(own, buffer, sems.at[0]).start()

    pltpu.make_async_copy(arrived, buffer, sems.at[0]).wait()
    wait_all(start_all(((buffer, leaving),), sems))


def correct_rows(ctl, slot, got, ground, block, state, rate, bottom):
    position = jnp.where(ctl[SLOT_LOW] == slot, 0, 1)
    device = lax.axis_index("xb") * 2 + lax.axis_index("yb")
    wall = WALL_WEST if bottom else WALL_EAST

    @pl.when(jnp.logical_not(flag(ctl, wall + position)))
    def _():
        peer = device - 2 if bottom else device + 2
        lines = got[pl.ds(pl.multiple_of(peer * block, 8), 8), :]
        grounds = ground[pl.ds(pl.multiple_of(peer * 16 + 8, 8), 8), :]

        def line(value, offset):
            picked = jnp.where(
                position == 0, value[offset : offset + 1, :], value[offset + 3 : offset + 4, :]
            )
            return jnp.broadcast_to(picked, (8, TILE))

        ghost, _ = cell(*(line(lines, field) for field in range(3)))
        ghost_ground = jnp.where(position == 0, grounds[0:1, :], grounds[1:2, :])
        rows = slice(0, 8) if bottom else slice(TILE - 8, TILE)
        own = [state[slot, field, rows, :] for field in range(3)]
        here, _ = cell(*own)
        fluxes = face(ghost, here) if bottom else face(here, ghost)
        push = SCALE * fluxes[1] + (SLOPE * own[0]) * ghost_ground
        row = sublanes()
        sign = -1.0 if bottom else 1.0
        chosen = row == (0 if bottom else 7)
        for field, value in enumerate((SCALE * fluxes[0], push, SCALE * fluxes[2])):
            rate[slot, field, rows, :] += jnp.where(chosen, sign * value, 0.0)


def column_fix(got, ground, block, columns, bed_columns):
    upper = lax.axis_index("yb")
    device = lax.axis_index("xb") * 2 + upper
    peer = device + 1 - 2 * upper
    lines = got[pl.ds(pl.multiple_of(peer * block, 8), 8), :]
    ghost_ground = ground[pl.ds(pl.multiple_of(peer * 16, 8), 8), :][3:4]
    del bed_columns
    mine = columns[...]
    _, ghost = cell(lines[0:1], lines[1:2], lines[2:3])
    _, own = cell(mine[0:1], mine[1:2], mine[2:3])
    low = upper == 0
    left = tuple(jnp.where(low, a, b) for a, b in zip(own, ghost))
    right = tuple(jnp.where(low, b, a) for a, b in zip(own, ghost))
    fluxes = face(left, right)
    sign = jnp.where(low, 1.0, -1.0)
    push = SCALE * fluxes[1] + (SLOPE * mine[0:1]) * ghost_ground
    block8 = stacked(
        [sign * SCALE * fluxes[0], sign * SCALE * fluxes[2], sign * push],
        jnp.zeros((8, TILE), jnp.float32),
    )
    return jnp.transpose(
        jnp.concatenate([block8, jnp.zeros((LANES - 8, TILE), jnp.float32)], 0)
    )


def update(step, ctl, got_in, ground_in, columns_in, state_in, manning_in, rate_in, *rest):
    more = step + 1 < STEPS
    fresh_out, first_out, second_out, delta_out = rest[:4]
    rest = rest[4:]
    state, manning, rate, fresh, got, ground, columns, first, second, delta_keep, sems = rest
    out, columns_out = late_first, late_second = first, second
    small = start_all(
        ((got_in, got), (ground_in, ground), (columns_in, columns)), sems, 5 * PARTS
    )
    size = 2 * TILE // PARTS
    parts = [
        (slot, slice(k * size, (k + 1) * size)) for slot in range(2) for k in range(PARTS // 2)
    ]
    incoming = []
    for index, (slot, rows) in enumerate(parts):
        incoming.append(
            start_all(
                (
                    (rate_in.at[slot, :, rows], rate.at[slot, :, rows]),
                    (state_in.at[slot, :, rows], state.at[slot, :, rows]),
                    (manning_in.at[slot, rows], manning.at[slot, rows]),
                ),
                sems,
                3 * index,
            )
        )
    wait_all(small)
    upper = lax.axis_index("yb")
    devices = 2 * lax.axis_size("xb")
    block = got.shape[0] // devices
    tops = got[0:8, :]
    for peer in range(1, devices):
        tops = jnp.maximum(tops, got[peer * block : peer * block + 8, :])
    delta = (COURANT * SPACING) / tops[TOP : TOP + 1, :]
    delta_keep[...] = jnp.broadcast_to(delta, (8, TILE))
    outgoing = start_all(((delta_keep, delta_out),), sems, 5 * PARTS + 3)
    fix = column_fix(got, ground, block, columns, None)
    facing = jnp.where(upper > 0, ctl[SLOT_LOW], 1 - ctl[SLOT_LOW])
    begin = pl.multiple_of((1 - upper) * LANES, LANES)
    target = (1 - upper) * (LANES - 1)
    lane = lax.broadcasted_iota(jnp.int32, (size, LANES), 1)
    total = jnp.zeros((ROWS, TILE), jnp.float32)
    for index, (slot, part_rows) in enumerate(parts):
        wait_all(incoming[index])
        if part_rows.start == 0:
            correct_rows(ctl, slot, got, ground, block, state, rate, True)
        if part_rows.stop == TILE:
            correct_rows(ctl, slot, got, ground, block, state, rate, False)

        @pl.when(facing == slot)
        def _(slot=slot, part_rows=part_rows):
            for field in range(3):
                turned = pltpu.roll(
                    fix[part_rows], lax.rem(target + LANES - field, LANES), 1
                )
                rate[slot, field, part_rows, pl.ds(begin, LANES)] += jnp.where(
                    lane == target, turned, 0.0
                )

        wet_now = flag(ctl, WET + 2 * step + slot)

        def group(index, best, slot=slot, wet_now=wet_now):
            rows = pl.ds(pl.multiple_of(index * ROWS, ROWS), ROWS)
            old = tuple(state[slot, field, rows, :] for field in range(3))
            slopes = tuple(rate[slot, field, rows, :] for field in range(3))
            h, hu, hv = moved_on(old, slopes, manning[slot, rows, :], delta, wet_now)
            fresh[slot, 0, rows, :] = h
            fresh[slot, 1, rows, :] = hu
            fresh[slot, 2, rows, :] = hv
            if more:
                along_x, along_y = cell(h, hu, hv)
                best = jnp.maximum(best, jnp.maximum(along_x[5], along_y[5]))
            return best

        best = lax.fori_loop(
            part_rows.start // ROWS,
            part_rows.stop // ROWS,
            group,
            jnp.zeros((ROWS, TILE), jnp.float32),
        )
        if more:
            best = jnp.where(flag(ctl, WET + 2 * step + 2 + slot), best, 0.0)
            total = jnp.maximum(total, best)
        outgoing += start_all(
            ((fresh.at[slot, :, part_rows], fresh_out.at[slot, :, part_rows]),),
            sems,
            3 * PARTS + index,
        )
    if more:
        messages(ctl, fresh, None, jnp.max(total, keepdims=True), out, columns_out)
        outgoing += start_all(((out, first_out), (columns_out, second_out)), sems, 4 * PARTS)
    else:
        late_rows(fresh.at[ctl[MOVE]], late_first)
        outgoing += start_all(((late_first, first_out),), sems, 4 * PARTS)
        late_rows(fresh.at[1 - ctl[MOVE]], late_second)
        outgoing += start_all(((late_second, second_out),), sems, 4 * PARTS + 1)
    wait_all(outgoing)


def vmem():
    return pl.BlockSpec(memory_space=pltpu.VMEM)


def smem():
    return pl.BlockSpec(memory_space=pltpu.SMEM)


def hbm():
    return pl.BlockSpec(memory_space=pltpu.HBM)


def anywhere():
    return pl.BlockSpec(memory_space=pl.ANY)


def call(
    kernel, outs, out_specs, in_specs, flops, scratch=(), aliases=None, room=VMEM_BYTES, moved=4
):
    return pl.pallas_call(
        kernel,
        scratch_shapes=scratch,
        input_output_aliases=aliases or {},
        out_shape=outs,
        in_specs=in_specs,
        out_specs=out_specs,
        compiler_params=pltpu.CompilerParams(vmem_limit_bytes=room),
        cost_estimate=pl.CostEstimate(flops=flops, bytes_accessed=moved << 20, transcendentals=0),
    )


def f32(*shape):
    return jax.ShapeDtypeStruct(shape, jnp.float32)


def spread(fast):
    return lax.all_to_all(fast, ("xb", "yb"), split_axis=0, concat_axis=0, tiled=True)


def body(state, bed, manning, neighbours, wet, moves):
    shape = f32(*state.shape)
    devices = lax.axis_size("xb") * lax.axis_size("yb")
    sem = [pltpu.SemaphoreType.DMA((1,))]
    whole = pltpu.VMEM(state.shape, jnp.float32)
    part = pltpu.VMEM(bed.shape, jnp.float32)
    tile_shape = f32(*state.shape[1:])
    early_shape = f32(5, EARLY, TILE)
    early_state = f32(3, EARLY, TILE)
    late_shape = f32(3, LATE, TILE)
    delta_shape = f32(8, TILE)

    def buffer(like):
        return pltpu.VMEM(like.shape, jnp.float32)

    piece_shapes = tuple(f32(5, end - begin, TILE) for begin, end in PIECES)
    out, columns, ctl, *leaving = call(
        opening,
        (
            f32(16 * devices, TILE),
            f32(8, TILE),
            jax.ShapeDtypeStruct((CONTROLS,), jnp.int32),
        )
        + piece_shapes,
        (vmem(), vmem(), smem(), hbm(), hbm()),
        [hbm()] * 6,
        4 << 20,
        [
            whole,
            part,
            pltpu.VMEM((EARLY, TILE), jnp.float32),
            pltpu.SMEM(neighbours.shape[::-1], jnp.int32),
            pltpu.SMEM(wet.shape, jnp.int32),
            pltpu.SMEM(moves.shape, jnp.int32),
            pltpu.SemaphoreType.DMA((13,)),
        ],
    )(state, bed, manning, neighbours.T, wet, moves)
    state_first = state
    ground = None
    deltas = []
    for step in range(STEPS):
        got = spread(out)
        ground = got if step == 0 else ground
        scratch = [whole, part, whole, pltpu.SemaphoreType.DMA((3 * CHUNKS,))]
        if step == 0:
            early_first = [shifted(piece, "xb", 1) for piece in leaving]
            rate = call(rates, shape, hbm(), [smem(), hbm(), hbm()], 16 << 20, scratch)(
                ctl, state, bed
            )
        elif step == 1:
            rate, *leaving = call(
                rates_and_leaving,
                (shape,) + piece_shapes,
                (hbm(),) * 3,
                [smem()] + [hbm()] * 6,
                16 << 20,
                scratch + [buffer(early_shape), pltpu.SemaphoreType.DMA((3,))],
            )(ctl, state, bed, state_first, manning, *early_first)
            early_second = [shifted(piece, "xb", 1) for piece in leaving]
        else:
            rate = call(rates_after, shape, hbm(), [smem()] + [hbm()] * 3, 16 << 20, scratch)(
                ctl, state, bed, early_second[0]
            )
        more = step + 1 < STEPS
        if more:
            shapes = f32(8 * devices, TILE), f32(8, TILE)
        else:
            shapes = late_shape, late_shape
        outs = call(
            functools.partial(update, step),
            (shape,) + shapes + (delta_shape,),
            (hbm(),) * 4,
            [smem()] + [hbm()] * 6,
            8 << 20,
            [
                whole,
                part,
                whole,
                whole,
                pltpu.VMEM(got.shape, jnp.float32),
                pltpu.VMEM(ground.shape, jnp.float32),
                pltpu.VMEM((8, TILE), jnp.float32),
                buffer(shapes[0]),
                buffer(shapes[1]),
                buffer(delta_shape),
                pltpu.SemaphoreType.DMA((5 * PARTS + 4,)),
            ],
            moved=4,
        )(ctl, got, ground, columns, state, manning, rate)
        deltas.append(outs[-1])
        state, out, columns, _ = outs
    late_first, late_second = out, columns
    room = 16 << 20
    late_arrived = shifted(late_first, "xb", 1)
    second, late_second = call(
        repeat_second,
        (early_state, late_shape),
        (anywhere(), vmem()),
        [smem()] + [vmem()] * 3 + [anywhere()] * 3,
        8 << 20,
        [buffer(early_shape), buffer(early_state), pltpu.SemaphoreType.DMA((3,))],
        room=room,
    )(ctl, *deltas, *early_second, late_second)
    leaving = call(
        second_late,
        late_shape,
        anywhere(),
        [smem(), anywhere(), anywhere(), anywhere()],
        1 << 20,
        [buffer(late_shape)] + sem,
        room=room,
    )(ctl, late_arrived, late_second, second)
    late_next = shifted(leaving, "xb", 1)
    final = call(
        repeat_first,
        shape,
        hbm(),
        [smem()] + [vmem()] * 3 + [anywhere()] * 4,
        8 << 20,
        [
            buffer(early_shape),
            buffer(early_state),
            buffer(tile_shape),
            buffer(late_shape),
            pltpu.SemaphoreType.DMA((3,)),
        ],
        room=room,
    )(ctl, *deltas, *early_first, late_arrived, state)
    return call(
        finish,
        shape,
        hbm(),
        [smem(), anywhere(), anywhere(), hbm()],
        1 << 20,
        [
            buffer(late_shape),
            buffer(early_state),
            buffer(tile_shape),
            pltpu.SemaphoreType.DMA((2,)),
        ],
        {3: 0},
        room=room,
    )(ctl, late_next, second, final)


def solution(mesh):
    placed = (
        P(("runs", "xb", "yb"), None, None, None),
        P(("runs", "xb", "yb"), None, None),
        P(("runs", "xb", "yb"), None, None),
        P("runs", None),
        P(None, "runs"),
        P(None, "runs"),
    )
    return jax.shard_map(
        body,
        mesh=mesh,
        in_specs=placed,
        out_specs=P(("runs", "xb", "yb"), None, None, None),
        check_vma=False,
    )
```

```python
import functools

import jax
import jax.numpy as jnp
from jax import lax
from jax.experimental import pallas as pl
from jax.experimental.pallas import tpu as pltpu
from jax.sharding import PartitionSpec as P

STEPS = 3
GRAVITY = 9.81
ROOT_G = GRAVITY**0.5
SPACING = 5.0
COURANT = 0.2
ROWS = 32
LANES = 128
TILE = 256
VMEM_BYTES = 60 * 1024 * 1024
SLOT_LOW, WALL_WEST, WALL_EAST, WALL_OUTER, WET, MOVE = 0, 1, 3, 5, 7, 13
WET_FIRST, WET_SECOND = 16, 19
CONTROLS = 24
EARLY = 192
PIECES = ((0, 96), (96, 192))
LATE = TILE - EARLY + 16
CHUNKS = 8
PARTS = 8
STRIP = 16
TOP = 6
SCALE = 0.5 / SPACING
SLOPE = GRAVITY / (2.0 * SPACING)


def shifted(value, axis, steps, around=True):
    count = lax.axis_size(axis)
    pairs = [(source, (source + steps) % count) for source in range(count)]
    if not around:
        pairs = [pair for pair in pairs if abs(pair[0] - pair[1]) == abs(steps)]
    return lax.ppermute(value, axis, pairs)


def cell(h, hu, hv):
    root = lax.rsqrt(h)
    inverse = root * root
    u = hu * inverse
    v = hv * inverse
    celerity = ROOT_G * (h * root)
    pressure = (0.5 * GRAVITY) * (h * h)
    cross = hu * v
    speed_x = jnp.abs(u) + celerity
    speed_y = jnp.abs(v) + celerity
    along_x = (h, hu, hv, hu * u + pressure, cross, speed_x)
    along_y = (h, hv, hu, hv * v + pressure, cross, speed_y)
    return along_x, along_y


def face(left, right):
    wave = jnp.maximum(left[5], right[5])
    return (
        (left[1] + right[1]) - wave * (right[0] - left[0]),
        (left[3] + right[3]) - wave * (right[1] - left[1]),
        (left[4] + right[4]) - wave * (right[2] - left[2]),
    )


def slot_of(ctl, position):
    low = ctl[SLOT_LOW]
    return low if position == 0 else 1 - low


def flag(ctl, index):
    return ctl[index] > 0


def start_all(pairs, sems, first=0):
    copies = [
        pltpu.make_async_copy(src, dst, sems.at[first + k]) for k, (src, dst) in enumerate(pairs)
    ]
    for copy in copies:
        copy.start()
    return copies


def wait_all(copies):
    for copy in copies:
        copy.wait()


def sublanes(width=TILE):
    return lax.broadcasted_iota(jnp.int32, (8, width), 0)


def stacked(lines, base):
    row = sublanes()
    for index, line in enumerate(lines):
        base = jnp.where(row == index, jnp.broadcast_to(line, (8, TILE)), base)
    return base


def messages(ctl, state, bed, fastest, out, columns):
    upper = lax.axis_index("yb")
    column = lax.axis_index("xb")
    last = lax.axis_size("xb") - 1
    devices = 2 * (last + 1)
    device = column * 2 + upper
    top = jnp.broadcast_to(fastest, (8, TILE))
    for peer in range(devices):
        out[peer * 8 : peer * 8 + 8, :TILE] = top
        if bed is not None:
            out[peer * 8 : peer * 8 + 8, TILE:] = top[:, :LANES]
    row = sublanes()

    def edge(line):
        rows = slice(line, line + 1)
        lines = []
        for position in range(2):
            slot = slot_of(ctl, position)
            lines += [state[slot, field, rows, :] for field in range(3)]
            if bed is not None:
                lines.append(bed[slot, rows, :])
        return stacked(lines, top)

    for inside, peer, line in (
        (column > 0, device - 2, 0),
        (column < last, device + 2, TILE - 1),
    ):

        @pl.when(inside)
        def _(peer=peer, line=line):
            out[pl.ds(pl.multiple_of(peer * 8, 8), 8), :TILE] = edge(line)

    slot = jnp.where(upper > 0, ctl[SLOT_LOW], 1 - ctl[SLOT_LOW])
    begin = pl.multiple_of((1 - upper) * LANES, LANES)
    lane = lax.broadcasted_iota(jnp.int32, (TILE, LANES), 1)
    packed = None
    for field in range(4 if bed is not None else 3):
        if field < 3:
            part = state[slot, field, :, pl.ds(begin, LANES)]
        else:
            part = bed[slot, :, pl.ds(begin, LANES)]
        turned = pltpu.roll(part, field + 1 - upper, 1)
        packed = turned if field == 0 else jnp.where(lane == field, turned, packed)
    lines = jnp.transpose(packed)[:8]
    columns[...] = lines
    start = pl.multiple_of((device + 1 - 2 * upper) * 8, 8)
    out[pl.ds(start, 8), :TILE] = jnp.where(row == TOP, top, lines)


def opening(
    state_in, bed_in, manning_in, neighbours_in, wet_in, moves_in,
    out, columns, ctl, leaving_low, leaving_high,
    state, bed, manning, neighbours, wet, moves, sems,
):
    copies = start_all(
        (
            (neighbours_in, neighbours),
            (wet_in, wet),
            (moves_in, moves),
            (state_in.at[0], state.at[0]),
            (state_in.at[1], state.at[1]),
            (bed_in, bed),
        ),
        sems,
    )
    device = lax.axis_index("xb") * 2 + lax.axis_index("yb")
    wait_all(copies[:3])
    first = device * 2
    low = jnp.where(neighbours[3, first] == first + 1, 0, 1)
    ctl[SLOT_LOW] = low
    for position in range(2):
        slot = low if position == 0 else 1 - low
        tile = first + slot
        ctl[WALL_WEST + position] = (neighbours[0, tile] < 0).astype(jnp.int32)
        ctl[WALL_EAST + position] = (neighbours[1, tile] < 0).astype(jnp.int32)
        ctl[WALL_OUTER + position] = (neighbours[2 + position, tile] < 0).astype(jnp.int32)
    for step in range(STEPS):
        for slot in range(2):
            ctl[WET + 2 * step + slot] = wet[step, first + slot]
        ctl[MOVE + step] = moves[step, device]
    moving = moves[0, device]
    rough = start_all(((manning_in.at[moving, 0:EARLY], manning),), sems, 6)
    count = lax.axis_size("xb")
    upper = lax.axis_index("yb")
    column = lax.axis_index("xb")
    source = lax.rem(column + count - 1, count) * 2 + upper
    before = lax.rem(column + count - 2, count) * 2 + upper
    again = moves[0, source] == moves[1, source]
    tile_first = source * 2 + moves[0, source]
    tile_second = jnp.where(
        again, before * 2 + moves[0, before], source * 2 + 1 - moves[0, source]
    )
    for step in range(STEPS):
        ctl[WET_FIRST + step] = wet[step, tile_first]
        ctl[WET_SECOND + step] = wet[step, tile_second]

    wait_all(copies[3:] + rough)
    early = []
    for (begin, end), leaving in zip(PIECES, (leaving_low, leaving_high)):
        early += start_all(
            (
                (state.at[moving, :, begin:end], leaving.at[0:3]),
                (bed.at[moving, begin:end], leaving.at[3]),
                (manning.at[begin:end], leaving.at[4]),
            ),
            sems,
            7 + len(early),
        )
    total = jnp.zeros((ROWS, TILE), jnp.float32)
    for slot in range(2):

        def group(index, best, slot=slot):
            rows = pl.ds(pl.multiple_of(index * ROWS, ROWS), ROWS)
            along_x, along_y = cell(*(state[slot, field, rows, :] for field in range(3)))
            return jnp.maximum(best, jnp.maximum(along_x[5], along_y[5]))

        best = lax.fori_loop(0, TILE // ROWS, group, jnp.zeros((ROWS, TILE), jnp.float32))
        total = jnp.maximum(total, jnp.where(wet[0, first + slot] > 0, best, 0.0))
    messages(ctl, state, bed, jnp.max(total, keepdims=True), out, columns)
    wait_all(early)


def hold(order, leaving, same):
    del order, leaving, same


class Passing:
    def __init__(self, ctl, state_in, bed_in, manning_in, arrived, leaving, buffer, sems):
        self.again = ctl[MOVE] == ctl[MOVE + 1]
        self.other = 1 - ctl[MOVE]
        self.refs = state_in, bed_in, manning_in, arrived, buffer, sems
        self.outgoing = [
            pltpu.make_async_copy(buffer.at[:, begin:end], piece, sems.at[1 + index])
            for index, ((begin, end), piece) in enumerate(zip(PIECES, leaving))
        ]

    def start(self):
        state_in, bed_in, manning_in, arrived, buffer, sems = self.refs
        rows = slice(0, EARLY)
        sem = sems.at[0]

        @pl.when(self.again)
        def _():
            for (begin, end), piece in zip(PIECES, arrived):
                pltpu.make_async_copy(piece, buffer.at[:, begin:end], sem).start()

        @pl.when(jnp.logical_not(self.again))
        def _():
            pltpu.make_async_copy(state_in.at[self.other, :, rows], buffer.at[0:3], sem).start()
            pltpu.make_async_copy(bed_in.at[self.other, rows], buffer.at[3], sem).start()
            pltpu.make_async_copy(manning_in.at[self.other, rows], buffer.at[4], sem).start()

    def middle(self):
        _, _, _, arrived, buffer, sems = self.refs
        for (begin, end), piece in zip(PIECES, arrived):
            pltpu.make_async_copy(piece, buffer.at[:, begin:end], sems.at[0]).wait()
        for copy in self.outgoing:
            copy.start()

    def end(self):
        wait_all(self.outgoing)


def rates_and_leaving(
    ctl, state_in, bed_in, state_first, manning_in, arrived_low, arrived_high,
    rate_out, leaving_low, leaving_high,
    state, bed, rate, sems, buffer, moving,
):
    arrived = arrived_low, arrived_high
    passing = Passing(
        ctl, state_first, bed_in, manning_in, arrived, (leaving_low, leaving_high), buffer, moving
    )
    rates(ctl, state_in, bed_in, rate_out, state, bed, rate, sems, passing)


def rates_after(ctl, state_in, bed_in, order, *rest):
    del order
    rates(ctl, state_in, bed_in, *rest)


def rates(ctl, state_in, bed_in, rate_out, state, bed, rate, sems, passing=None):
    width = 2 * TILE
    row_ids = lax.broadcasted_iota(jnp.int32, (STRIP, width), 0)
    row8 = sublanes(width)
    lane = lax.broadcasted_iota(jnp.int32, (STRIP, LANES), 1)
    last = TILE // STRIP - 1
    chunk = TILE // CHUNKS
    slots = [slot_of(ctl, position) for position in range(2)]
    incoming = []
    for part in range(CHUNKS):
        rows = slice(part * chunk, (part + 1) * chunk)
        incoming.append(
            start_all(
                (
                    (state_in.at[:, :, rows], state.at[:, :, rows]),
                    (bed_in.at[:, rows], bed.at[:, rows]),
                ),
                sems,
                2 * part,
            )
        )
    if passing:
        passing.start()
    keep_west, keep_east, keep_south, keep_north = (
        jnp.where(flag(ctl, index), 1.0, 0.0)
        for index in (WALL_WEST, WALL_EAST, WALL_OUTER, WALL_OUTER + 1)
    )

    def strip(field, rows):
        if field == 3:
            return jnp.concatenate([bed[slot, rows, :] for slot in slots], 1)
        return jnp.concatenate([state[slot, field, rows, :] for slot in slots], 1)

    def blocks(value):
        return [value[:, k * LANES : (k + 1) * LANES] for k in range(4)]

    def right_of(value, end=None):
        turned = [pltpu.roll(part, LANES - 1, 1) for part in blocks(value)]
        after = turned[1:] + [turned[3] if end is None else end]
        return jnp.concatenate(
            [
                jnp.where(lane == LANES - 1, following, part)
                if following is not part
                else part
                for part, following in zip(turned, after)
            ],
            1,
        )

    def left_of(value, end):
        turned = [pltpu.roll(part, 1, 1) for part in blocks(value)]
        before = [end] + turned[:3]
        return jnp.concatenate(
            [jnp.where(lane == 0, previous, part) for part, previous in zip(turned, before)], 1
        )

    def down(value):
        return pltpu.roll(value, STRIP + 7, 0)[:STRIP]

    def group(index, carry):
        base = pl.multiple_of(index * STRIP, STRIP)
        rows = pl.ds(base, STRIP)
        after = pl.ds(pl.multiple_of(jnp.minimum(base + STRIP, TILE - 8), 8), 8)
        at_end = index == last
        fields = [
            jnp.concatenate([strip(field, rows), strip(field, after)], 0) for field in range(3)
        ]
        cells_x, cells_y = cell(*fields)
        here_x = tuple(value[:STRIP] for value in cells_x)
        here_y = tuple(value[:STRIP] for value in cells_y)

        ending = jnp.logical_and(row8 == 7, at_end)
        faces = list(face(here_x, tuple(down(value) for value in cells_x)))
        wall = keep_east * (2.0 * (here_x[3] + here_x[5] * here_x[1])[STRIP - 8 :])
        for component, value in enumerate((0.0, wall, 0.0)):
            upper = faces[component]
            faces[component] = jnp.concatenate(
                [upper[: STRIP - 8], jnp.where(ending, value, upper[STRIP - 8 :])], 0
            )
        turned = tuple(pltpu.roll(value, 1, 0) for value in faces)
        change_x = tuple(
            value - jnp.where(row_ids == 0, before, moved)
            for value, before, moved in zip(faces, carry[:3], turned)
        )
        ground = strip(3, rows)
        ground_after = jnp.where(
            at_end,
            jnp.broadcast_to(keep_east * ground[STRIP - 1 :], (8, width)),
            strip(3, after),
        )
        ground_up = pltpu.roll(ground, 1, 0)
        slope_x = down(jnp.concatenate([ground, ground_after], 0)) - jnp.where(
            row_ids == 0, carry[3], ground_up
        )
        carried = tuple(value[0:1, :] for value in turned) + (ground_up[0:1, :],)

        faces_y = list(face(here_y, tuple(right_of(value) for value in here_y)))
        normal = here_y[3]
        spread_y = here_y[5] * here_y[1]
        north = keep_north * (2.0 * (normal + spread_y)[:, width - LANES :])
        south = keep_south * (2.0 * (normal - spread_y)[:, :LANES])
        change_y = []
        for component, (high, low) in enumerate(((0.0, 0.0), (north, south), (0.0, 0.0))):
            parts = blocks(faces_y[component])
            parts[3] = jnp.where(lane == LANES - 1, high, parts[3])
            value = jnp.concatenate(parts, 1)
            change_y.append(value - left_of(value, low))
        slope_y = right_of(ground, keep_north * ground[:, width - LANES :]) - left_of(
            ground, keep_south * ground[:, :LANES]
        )
        weight = SLOPE * here_x[0]
        results = (
            SCALE * (change_x[0] + change_y[0]),
            SCALE * (change_x[1] + change_y[2]) + weight * slope_x,
            SCALE * (change_x[2] + change_y[1]) + weight * slope_y,
        )
        for field, value in enumerate(results):
            for position, slot in enumerate(slots):
                rate[slot, field, rows, :] = value[:, position * TILE : (position + 1) * TILE]
        return carried

    wait_all(incoming[0])
    top, _ = cell(*(strip(field, slice(0, 8)) for field in range(3)))
    nothing = jnp.zeros((1, width), jnp.float32)
    carry = (
        nothing,
        keep_west * (2.0 * (top[3] - top[5] * top[1])[0:1]),
        nothing,
        keep_west * strip(3, slice(0, 8))[0:1],
    )
    per_chunk = chunk // STRIP
    outgoing = []
    for part in range(CHUNKS):
        if part + 1 < CHUNKS:
            wait_all(incoming[part + 1])
        carry = lax.fori_loop(part * per_chunk, (part + 1) * per_chunk, group, carry)
        rows = slice(part * chunk, (part + 1) * chunk)
        outgoing += start_all(
            ((rate.at[:, :, rows], rate_out.at[:, :, rows]),), sems, 2 * CHUNKS + part
        )
        if passing and part == CHUNKS // 2:
            passing.middle()
    wait_all(outgoing)
    if passing:
        passing.end()


def moved_on(old, slopes, rough, delta, wet_now):
    h, hu, hv = (value - delta * slope for value, slope in zip(old, slopes))
    inverse = 1.0 / h
    u = hu * inverse
    v = hv * inverse
    speed = jnp.sqrt(u * u + v * v)
    power = jnp.exp((-4.0 / 3.0) * jnp.log(jnp.abs(h)))
    drag = (GRAVITY * delta) * (rough * rough) * (speed * power)
    factor = 1.0 / (1.0 + drag)
    fresh = (h, hu * factor, hv * factor)
    return tuple(jnp.where(wet_now, new, value) for new, value in zip(fresh, old))


def repeat_steps(ctl, wet_from, deltas, early, work, other, sems):
    incoming = []
    for ref in early:
        begin = 0 if ref is early[0] else early[0].shape[1]
        incoming += start_all(
            ((ref, work.at[:, begin : begin + ref.shape[1]]),), sems, len(incoming)
        )
    row_ids = lax.broadcasted_iota(jnp.int32, (ROWS, TILE), 0)
    lane = lax.broadcasted_iota(jnp.int32, (ROWS, LANES), 1)
    start = tuple(jnp.zeros((1, TILE), jnp.float32) for _ in range(4))

    def halves(value):
        return value[:, :LANES], value[:, LANES:]

    def right_of(value):
        low, high = (pltpu.roll(part, LANES - 1, 1) for part in halves(value))
        return jnp.concatenate([jnp.where(lane == LANES - 1, high, low), high], 1)

    def left_of(value):
        low, high = (pltpu.roll(part, 1, 1) for part in halves(value))
        return jnp.concatenate([low, jnp.where(lane == 0, low, high)], 1)

    def down(value):
        return pltpu.roll(value, ROWS + 7, 0)[:ROWS]

    for step in range(STEPS):
        source, target = (work, other) if step % 2 == 0 else (other, work)
        delta = deltas[step][0:1, :]
        wet_now = flag(ctl, wet_from + step)

        def group(index, carry, source=source, target=target, delta=delta, wet_now=wet_now):
            base = pl.multiple_of(index * ROWS, ROWS)
            rows = pl.ds(base, ROWS)
            after = pl.ds(pl.multiple_of(jnp.minimum(base + ROWS, EARLY - 8), 8), 8)
            refs = [source.at[field] for field in range(3)] + [work.at[3]]
            fields = [jnp.concatenate([ref[rows, :], ref[after, :]], 0) for ref in refs]
            cells_x, cells_y = cell(*fields[:3])
            here_x = tuple(value[:ROWS] for value in cells_x)
            here_y = tuple(value[:ROWS] for value in cells_y)
            faces_x = face(here_x, tuple(down(value) for value in cells_x))
            turned = tuple(pltpu.roll(value, 1, 0) for value in faces_x)
            change_x = tuple(
                value - jnp.where(row_ids == 0, before, moved)
                for value, before, moved in zip(faces_x, carry[:3], turned)
            )
            ground = fields[3][:ROWS]
            ground_up = pltpu.roll(ground, 1, 0)
            slope_x = down(fields[3]) - jnp.where(row_ids == 0, carry[3], ground_up)
            carried = tuple(value[0:1, :] for value in turned) + (ground_up[0:1, :],)
            faces_y = face(here_y, tuple(right_of(value) for value in here_y))
            change_y = tuple(value - left_of(value) for value in faces_y)
            slope_y = right_of(ground) - left_of(ground)
            old = tuple(value[:ROWS] for value in fields[:3])
            weight = SLOPE * old[0]
            slopes = (
                SCALE * (change_x[0] + change_y[0]),
                SCALE * (change_x[1] + change_y[2]) + weight * slope_x,
                SCALE * (change_x[2] + change_y[1]) + weight * slope_y,
            )
            for field, value in enumerate(
                moved_on(old, slopes, work[4, rows, :], delta, wet_now)
            ):
                target[field, rows, :] = value
            return carried

        if step == 0:
            wait_all(incoming)
        lax.fori_loop(0, EARLY // ROWS, group, start)


def late_rows(tile, late):
    row = sublanes()
    kept = EARLY - 8
    lane = lax.broadcasted_iota(jnp.int32, (8, LANES), 1)
    for field in range(3):
        late[field, 0:8, :] = jnp.where(
            row < 3, tile[field, 0:8, :], tile[field, kept : kept + 8, :]
        )
        packed = [jnp.zeros((8, LANES), jnp.float32)] * 2
        for block in range(EARLY // 8):
            rows = slice(8 * block, 8 * block + 8)
            sides = jnp.where(lane < 64, tile[field, rows, :LANES], tile[field, rows, LANES:])
            turned = pltpu.roll(sides, (3 + 8 * block) % LANES, 1)
            which = block // 16
            packed[which] = jnp.where(lane // 8 == block % 16, turned, packed[which])
        late[field, 8:16, :] = jnp.concatenate(packed, 1)
        late[field, 16:, :] = tile[field, EARLY:, :]


def merge(late, early, tile):
    row = sublanes()
    lane = lax.broadcasted_iota(jnp.int32, (8, LANES), 1)
    for field in range(3):
        first = late[field, 0:8, :]
        for block in range(EARLY // 8):
            rows = slice(8 * block, 8 * block + 8)
            which = block // 16
            packed = late[field, 8:16, which * LANES : (which + 1) * LANES]
            sides = pltpu.roll(packed, (-3 - 8 * block) % LANES, 1)
            value = early[field, rows, :]
            value = jnp.concatenate(
                [
                    jnp.where(lane < 3, sides, value[:, :LANES]),
                    jnp.where(lane >= LANES - 3, sides, value[:, LANES:]),
                ],
                1,
            )
            if block == 0:
                value = jnp.where(row < 3, first, value)
            if block == EARLY // 8 - 1:
                value = jnp.where(row < 5, value, first)
            tile[field, rows, :] = value
        tile[field, EARLY:, :] = late[field, 16:, :]


def repeat_second(ctl, delta0, delta1, delta2, low, high, late, out, late_out, work, tile, sems):
    near = start_all(((late, late_out),), sems, 2)
    repeat_steps(ctl, WET_SECOND, (delta0, delta1, delta2), (low, high), work, tile, sems)
    wait_all(start_all(((tile, out),), sems) + near)


def repeat_first(
    ctl, delta0, delta1, delta2, low, high, late_in, state, out, work, other, tile, late, sems
):
    rest = out.at[1 - ctl[MOVE + 1]]
    again = ctl[MOVE] == ctl[MOVE + 1]

    @pl.when(again)
    def _():
        wait_all(start_all(((state.at[1 - ctl[MOVE]], tile),), sems))

    @pl.when(jnp.logical_not(again))
    def _():
        copies = start_all(((late_in, late),), sems, 2)
        repeat_steps(ctl, WET_FIRST, (delta0, delta1, delta2), (low, high), work, other, sems)
        wait_all(copies)
        merge(late, other, tile)

    wait_all(start_all(((tile, rest),), sems))


def finish(ctl, late_in, early_in, before, out, late, early, tile, sems):
    del before
    wait_all(start_all(((late_in, late), (early_in, early)), sems))
    merge(late, early, tile)
    wait_all(start_all(((tile, out.at[ctl[MOVE + 1]]),), sems))


def second_late(ctl, arrived, own, order, leaving, buffer, sems):
    del order
    again = ctl[MOVE] == ctl[MOVE + 1]

    @pl.when(again)
    def _():
        pltpu.make_async_copy(arrived, buffer, sems.at[0]).start()

    @pl.when(jnp.logical_not(again))
    def _():
        pltpu.make_async_copy(own, buffer, sems.at[0]).start()

    pltpu.make_async_copy(arrived, buffer, sems.at[0]).wait()
    wait_all(start_all(((buffer, leaving),), sems))


def correct_rows(ctl, slot, got, ground, state, rate, bottom):
    position = jnp.where(ctl[SLOT_LOW] == slot, 0, 1)
    device = lax.axis_index("xb") * 2 + lax.axis_index("yb")
    wall = WALL_WEST if bottom else WALL_EAST

    @pl.when(jnp.logical_not(flag(ctl, wall + position)))
    def _():
        peer = device - 2 if bottom else device + 2
        block = pl.ds(pl.multiple_of(peer * 8, 8), 8)
        lines = got[block, :TILE]
        grounds = ground[block, :TILE]
        stride = 4 if got.shape[1] > TILE else 3

        def line(offset):
            other = offset + stride
            picked = jnp.where(
                position == 0, lines[offset : offset + 1, :], lines[other : other + 1, :]
            )
            return jnp.broadcast_to(picked, (8, TILE))

        ghost, _ = cell(*(line(field) for field in range(3)))
        ghost_ground = jnp.where(position == 0, grounds[3:4, :], grounds[7:8, :])
        rows = slice(0, 8) if bottom else slice(TILE - 8, TILE)
        own = [state[slot, field, rows, :] for field in range(3)]
        here, _ = cell(*own)
        fluxes = face(ghost, here) if bottom else face(here, ghost)
        push = SCALE * fluxes[1] + (SLOPE * own[0]) * ghost_ground
        row = sublanes()
        sign = -1.0 if bottom else 1.0
        chosen = row == (0 if bottom else 7)
        for field, value in enumerate((SCALE * fluxes[0], push, SCALE * fluxes[2])):
            rate[slot, field, rows, :] += jnp.where(chosen, sign * value, 0.0)


def column_fix(got, ground, columns):
    upper = lax.axis_index("yb")
    device = lax.axis_index("xb") * 2 + upper
    peer = device + 1 - 2 * upper
    block = pl.ds(pl.multiple_of(peer * 8, 8), 8)
    lines = got[block, :TILE]
    ghost_ground = ground[block, :TILE][3:4]
    mine = columns[...]
    _, ghost = cell(lines[0:1], lines[1:2], lines[2:3])
    _, own = cell(mine[0:1], mine[1:2], mine[2:3])
    low = upper == 0
    left = tuple(jnp.where(low, a, b) for a, b in zip(own, ghost))
    right = tuple(jnp.where(low, b, a) for a, b in zip(own, ghost))
    fluxes = face(left, right)
    sign = jnp.where(low, 1.0, -1.0)
    push = SCALE * fluxes[1] + (SLOPE * mine[0:1]) * ghost_ground
    block8 = stacked(
        [sign * SCALE * fluxes[0], sign * SCALE * fluxes[2], sign * push],
        jnp.zeros((8, TILE), jnp.float32),
    )
    return jnp.transpose(
        jnp.concatenate([block8, jnp.zeros((LANES - 8, TILE), jnp.float32)], 0)
    )


def update(step, ctl, got_in, ground_in, columns_in, state_in, manning_in, rate_in, *rest):
    more = step + 1 < STEPS
    fresh_out, first_out, second_out, delta_out = rest[:4]
    rest = rest[4:]
    state, manning, rate, fresh, got, ground, columns, first, second, delta_keep, sems = rest
    out, columns_out = late_first, late_second = first, second
    small = start_all(
        ((got_in, got), (ground_in, ground), (columns_in, columns)), sems, 5 * PARTS
    )
    size = 2 * TILE // PARTS
    parts = [
        (slot, slice(k * size, (k + 1) * size)) for slot in range(2) for k in range(PARTS // 2)
    ]
    incoming = []
    for index, (slot, rows) in enumerate(parts):
        incoming.append(
            start_all(
                (
                    (rate_in.at[slot, :, rows], rate.at[slot, :, rows]),
                    (state_in.at[slot, :, rows], state.at[slot, :, rows]),
                    (manning_in.at[slot, rows], manning.at[slot, rows]),
                ),
                sems,
                3 * index,
            )
        )
    wait_all(small)
    upper = lax.axis_index("yb")
    devices = 2 * lax.axis_size("xb")
    begin = TILE if got.shape[1] > TILE else 0
    tops = got[0:8, begin : begin + LANES]
    for peer in range(1, devices):
        tops = jnp.maximum(tops, got[peer * 8 : peer * 8 + 8, begin : begin + LANES])
    delta = (COURANT * SPACING) / tops[TOP : TOP + 1, :]
    delta = jnp.concatenate([delta, delta], 1)
    delta_keep[...] = jnp.broadcast_to(delta, (8, TILE))
    outgoing = start_all(((delta_keep, delta_out),), sems, 5 * PARTS + 3)
    fix = column_fix(got, ground, columns)
    facing = jnp.where(upper > 0, ctl[SLOT_LOW], 1 - ctl[SLOT_LOW])
    begin = pl.multiple_of((1 - upper) * LANES, LANES)
    target = (1 - upper) * (LANES - 1)
    lane = lax.broadcasted_iota(jnp.int32, (size, LANES), 1)
    total = jnp.zeros((ROWS, TILE), jnp.float32)
    for index, (slot, part_rows) in enumerate(parts):
        wait_all(incoming[index])
        if part_rows.start == 0:
            correct_rows(ctl, slot, got, ground, state, rate, True)
        if part_rows.stop == TILE:
            correct_rows(ctl, slot, got, ground, state, rate, False)

        @pl.when(facing == slot)
        def _(slot=slot, part_rows=part_rows):
            for field in range(3):
                turned = pltpu.roll(
                    fix[part_rows], lax.rem(target + LANES - field, LANES), 1
                )
                rate[slot, field, part_rows, pl.ds(begin, LANES)] += jnp.where(
                    lane == target, turned, 0.0
                )

        wet_now = flag(ctl, WET + 2 * step + slot)

        def group(index, best, slot=slot, wet_now=wet_now):
            rows = pl.ds(pl.multiple_of(index * ROWS, ROWS), ROWS)
            old = tuple(state[slot, field, rows, :] for field in range(3))
            slopes = tuple(rate[slot, field, rows, :] for field in range(3))
            h, hu, hv = moved_on(old, slopes, manning[slot, rows, :], delta, wet_now)
            fresh[slot, 0, rows, :] = h
            fresh[slot, 1, rows, :] = hu
            fresh[slot, 2, rows, :] = hv
            if more:
                along_x, along_y = cell(h, hu, hv)
                best = jnp.maximum(best, jnp.maximum(along_x[5], along_y[5]))
            return best

        best = lax.fori_loop(
            part_rows.start // ROWS,
            part_rows.stop // ROWS,
            group,
            jnp.zeros((ROWS, TILE), jnp.float32),
        )
        if more:
            best = jnp.where(flag(ctl, WET + 2 * step + 2 + slot), best, 0.0)
            total = jnp.maximum(total, best)
        outgoing += start_all(
            ((fresh.at[slot, :, part_rows], fresh_out.at[slot, :, part_rows]),),
            sems,
            3 * PARTS + index,
        )
    if more:
        messages(ctl, fresh, None, jnp.max(total, keepdims=True), out, columns_out)
        outgoing += start_all(((out, first_out), (columns_out, second_out)), sems, 4 * PARTS)
    else:
        late_rows(fresh.at[ctl[MOVE]], late_first)
        outgoing += start_all(((late_first, first_out),), sems, 4 * PARTS)
        late_rows(fresh.at[1 - ctl[MOVE]], late_second)
        outgoing += start_all(((late_second, second_out),), sems, 4 * PARTS + 1)
    wait_all(outgoing)


def vmem():
    return pl.BlockSpec(memory_space=pltpu.VMEM)


def smem():
    return pl.BlockSpec(memory_space=pltpu.SMEM)


def hbm():
    return pl.BlockSpec(memory_space=pltpu.HBM)


def anywhere():
    return pl.BlockSpec(memory_space=pl.ANY)


def call(
    kernel, outs, out_specs, in_specs, flops, scratch=(), aliases=None, room=VMEM_BYTES, moved=4
):
    return pl.pallas_call(
        kernel,
        scratch_shapes=scratch,
        input_output_aliases=aliases or {},
        out_shape=outs,
        in_specs=in_specs,
        out_specs=out_specs,
        compiler_params=pltpu.CompilerParams(vmem_limit_bytes=room),
        cost_estimate=pl.CostEstimate(flops=flops, bytes_accessed=moved << 20, transcendentals=0),
    )


def f32(*shape):
    return jax.ShapeDtypeStruct(shape, jnp.float32)


def spread(fast):
    return lax.all_to_all(fast, ("xb", "yb"), split_axis=0, concat_axis=0, tiled=True)


def body(state, bed, manning, neighbours, wet, moves):
    shape = f32(*state.shape)
    devices = lax.axis_size("xb") * lax.axis_size("yb")
    sem = [pltpu.SemaphoreType.DMA((1,))]
    whole = pltpu.VMEM(state.shape, jnp.float32)
    part = pltpu.VMEM(bed.shape, jnp.float32)
    tile_shape = f32(*state.shape[1:])
    early_shape = f32(5, EARLY, TILE)
    early_state = f32(3, EARLY, TILE)
    late_shape = f32(3, LATE, TILE)
    delta_shape = f32(8, TILE)

    def buffer(like):
        return pltpu.VMEM(like.shape, jnp.float32)

    piece_shapes = tuple(f32(5, end - begin, TILE) for begin, end in PIECES)
    out, columns, ctl, *leaving = call(
        opening,
        (
            f32(8 * devices, TILE + LANES),
            f32(8, TILE),
            jax.ShapeDtypeStruct((CONTROLS,), jnp.int32),
        )
        + piece_shapes,
        (vmem(), vmem(), smem(), hbm(), hbm()),
        [hbm()] * 6,
        4 << 20,
        [
            whole,
            part,
            pltpu.VMEM((EARLY, TILE), jnp.float32),
            pltpu.SMEM(neighbours.shape[::-1], jnp.int32),
            pltpu.SMEM(wet.shape, jnp.int32),
            pltpu.SMEM(moves.shape, jnp.int32),
            pltpu.SemaphoreType.DMA((13,)),
        ],
    )(state, bed, manning, neighbours.T, wet, moves)
    state_first = state
    ground = None
    deltas = []
    for step in range(STEPS):
        got = spread(out)
        ground = got if step == 0 else ground
        scratch = [whole, part, whole, pltpu.SemaphoreType.DMA((3 * CHUNKS,))]
        if step == 0:
            rate = call(rates, shape, hbm(), [smem(), hbm(), hbm()], 16 << 20, scratch)(
                ctl, state, bed
            )
            leaving[1] = call(
                hold, piece_shapes[1], hbm(), [hbm(), hbm()], 1 << 10, aliases={1: 0}
            )(rate, leaving[1])
            early_first = [shifted(piece, "xb", 1) for piece in leaving]
        elif step == 1:
            rate, *leaving = call(
                rates_and_leaving,
                (shape,) + piece_shapes,
                (hbm(),) * 3,
                [smem()] + [hbm()] * 6,
                16 << 20,
                scratch + [buffer(early_shape), pltpu.SemaphoreType.DMA((3,))],
            )(ctl, state, bed, state_first, manning, *early_first)
            early_second = [shifted(piece, "xb", 1) for piece in leaving]
        else:
            rate = call(rates_after, shape, hbm(), [smem()] + [hbm()] * 3, 16 << 20, scratch)(
                ctl, state, bed, early_second[0]
            )
        more = step + 1 < STEPS
        if more:
            shapes = f32(8 * devices, TILE), f32(8, TILE)
        else:
            shapes = late_shape, late_shape
        outs = call(
            functools.partial(update, step),
            (shape,) + shapes + (delta_shape,),
            (hbm(),) * 4,
            [smem()] + [hbm()] * 6,
            8 << 20,
            [
                whole,
                part,
                whole,
                whole,
                pltpu.VMEM(got.shape, jnp.float32),
                pltpu.VMEM(ground.shape, jnp.float32),
                pltpu.VMEM((8, TILE), jnp.float32),
                buffer(shapes[0]),
                buffer(shapes[1]),
                buffer(delta_shape),
                pltpu.SemaphoreType.DMA((5 * PARTS + 4,)),
            ],
            moved=6,
        )(ctl, got, ground, columns, state, manning, rate)
        deltas.append(outs[-1])
        state, out, columns, _ = outs
    late_first, late_second = out, columns
    room = 16 << 20
    late_arrived = shifted(late_first, "xb", 1)
    second, late_second = call(
        repeat_second,
        (early_state, late_shape),
        (anywhere(), vmem()),
        [smem()] + [vmem()] * 3 + [anywhere()] * 3,
        8 << 20,
        [buffer(early_shape), buffer(early_state), pltpu.SemaphoreType.DMA((3,))],
        room=room,
    )(ctl, *deltas, *early_second, late_second)
    leaving = call(
        second_late,
        late_shape,
        anywhere(),
        [smem(), anywhere(), anywhere(), anywhere()],
        1 << 20,
        [buffer(late_shape)] + sem,
        room=room,
    )(ctl, late_arrived, late_second, second)
    late_next = shifted(leaving, "xb", 1)
    final = call(
        repeat_first,
        shape,
        hbm(),
        [smem()] + [vmem()] * 3 + [anywhere()] * 4,
        8 << 20,
        [
            buffer(early_shape),
            buffer(early_state),
            buffer(tile_shape),
            buffer(late_shape),
            pltpu.SemaphoreType.DMA((3,)),
        ],
        room=room,
    )(ctl, *deltas, *early_first, late_arrived, state)
    return call(
        finish,
        shape,
        hbm(),
        [smem(), anywhere(), anywhere(), hbm()],
        1 << 20,
        [
            buffer(late_shape),
            buffer(early_state),
            buffer(tile_shape),
            pltpu.SemaphoreType.DMA((2,)),
        ],
        {3: 0},
        room=room,
    )(ctl, late_next, second, final)


def solution(mesh):
    placed = (
        P(("runs", "xb", "yb"), None, None, None),
        P(("runs", "xb", "yb"), None, None),
        P(("runs", "xb", "yb"), None, None),
        P("runs", None),
        P(None, "runs"),
        P(None, "runs"),
    )
    return jax.shard_map(
        body,
        mesh=mesh,
        in_specs=placed,
        out_specs=P(("runs", "xb", "yb"), None, None, None),
        check_vma=False,
    )
```

```python
import functools

import jax
import jax.numpy as jnp
from jax import lax
from jax.experimental import pallas as pl
from jax.experimental.pallas import tpu as pltpu
from jax.sharding import PartitionSpec as P

STEPS = 3
GRAVITY = 9.81
ROOT_G = GRAVITY**0.5
SPACING = 5.0
COURANT = 0.2
ROWS = 32
LANES = 128
TILE = 256
VMEM_BYTES = 60 * 1024 * 1024
SLOT_LOW, WALL_WEST, WALL_EAST, WALL_OUTER, WET, MOVE = 0, 1, 3, 5, 7, 13
WET_FIRST, WET_SECOND = 16, 19
CONTROLS = 24
EARLY = 160
PIECES = ((0, 88), (88, 160))
LATE = TILE - EARLY + 16
CHUNKS = 8
PARTS = 8
STRIP = 16
TOP = 6
SCALE = 0.5 / SPACING
SLOPE = GRAVITY / (2.0 * SPACING)


def shifted(value, axis, steps, around=True):
    count = lax.axis_size(axis)
    pairs = [(source, (source + steps) % count) for source in range(count)]
    if not around:
        pairs = [pair for pair in pairs if abs(pair[0] - pair[1]) == abs(steps)]
    return lax.ppermute(value, axis, pairs)


def cell(h, hu, hv):
    root = lax.rsqrt(h)
    inverse = root * root
    u = hu * inverse
    v = hv * inverse
    celerity = ROOT_G * (h * root)
    pressure = (0.5 * GRAVITY) * (h * h)
    cross = hu * v
    speed_x = jnp.abs(u) + celerity
    speed_y = jnp.abs(v) + celerity
    along_x = (h, hu, hv, hu * u + pressure, cross, speed_x)
    along_y = (h, hv, hu, hv * v + pressure, cross, speed_y)
    return along_x, along_y


def face(left, right):
    wave = jnp.maximum(left[5], right[5])
    return (
        (left[1] + right[1]) - wave * (right[0] - left[0]),
        (left[3] + right[3]) - wave * (right[1] - left[1]),
        (left[4] + right[4]) - wave * (right[2] - left[2]),
    )


def slot_of(ctl, position):
    low = ctl[SLOT_LOW]
    return low if position == 0 else 1 - low


def flag(ctl, index):
    return ctl[index] > 0


def start_all(pairs, sems, first=0):
    copies = [
        pltpu.make_async_copy(src, dst, sems.at[first + k]) for k, (src, dst) in enumerate(pairs)
    ]
    for copy in copies:
        copy.start()
    return copies


def wait_all(copies):
    for copy in copies:
        copy.wait()


def sublanes(width=TILE):
    return lax.broadcasted_iota(jnp.int32, (8, width), 0)


def stacked(lines, base):
    row = sublanes()
    for index, line in enumerate(lines):
        base = jnp.where(row == index, jnp.broadcast_to(line, (8, TILE)), base)
    return base


def messages(ctl, state, bed, fastest, out, columns):
    upper = lax.axis_index("yb")
    column = lax.axis_index("xb")
    last = lax.axis_size("xb") - 1
    devices = 2 * (last + 1)
    device = column * 2 + upper
    top = jnp.broadcast_to(fastest, (8, TILE))
    for peer in range(devices):
        out[peer * 8 : peer * 8 + 8, :TILE] = top
        if bed is not None:
            out[peer * 8 : peer * 8 + 8, TILE:] = top[:, :LANES]
    row = sublanes()

    def edge(line):
        rows = slice(line, line + 1)
        lines = []
        for position in range(2):
            slot = slot_of(ctl, position)
            lines += [state[slot, field, rows, :] for field in range(3)]
            if bed is not None:
                lines.append(bed[slot, rows, :])
        return stacked(lines, top)

    for inside, peer, line in (
        (column > 0, device - 2, 0),
        (column < last, device + 2, TILE - 1),
    ):

        @pl.when(inside)
        def _(peer=peer, line=line):
            out[pl.ds(pl.multiple_of(peer * 8, 8), 8), :TILE] = edge(line)

    slot = jnp.where(upper > 0, ctl[SLOT_LOW], 1 - ctl[SLOT_LOW])
    begin = pl.multiple_of((1 - upper) * LANES, LANES)
    lane = lax.broadcasted_iota(jnp.int32, (TILE, LANES), 1)
    packed = None
    for field in range(4 if bed is not None else 3):
        if field < 3:
            part = state[slot, field, :, pl.ds(begin, LANES)]
        else:
            part = bed[slot, :, pl.ds(begin, LANES)]
        turned = pltpu.roll(part, field + 1 - upper, 1)
        packed = turned if field == 0 else jnp.where(lane == field, turned, packed)
    lines = jnp.transpose(packed)[:8]
    columns[...] = lines
    start = pl.multiple_of((device + 1 - 2 * upper) * 8, 8)
    out[pl.ds(start, 8), :TILE] = jnp.where(row == TOP, top, lines)


def opening(
    state_in, bed_in, manning_in, neighbours_in, wet_in, moves_in,
    out, columns, ctl, leaving_low, leaving_high,
    state, bed, manning, neighbours, wet, moves, sems,
):
    copies = start_all(
        (
            (neighbours_in, neighbours),
            (wet_in, wet),
            (moves_in, moves),
            (state_in.at[0], state.at[0]),
            (state_in.at[1], state.at[1]),
            (bed_in, bed),
        ),
        sems,
    )
    device = lax.axis_index("xb") * 2 + lax.axis_index("yb")
    wait_all(copies[:3])
    first = device * 2
    low = jnp.where(neighbours[3, first] == first + 1, 0, 1)
    ctl[SLOT_LOW] = low
    for position in range(2):
        slot = low if position == 0 else 1 - low
        tile = first + slot
        ctl[WALL_WEST + position] = (neighbours[0, tile] < 0).astype(jnp.int32)
        ctl[WALL_EAST + position] = (neighbours[1, tile] < 0).astype(jnp.int32)
        ctl[WALL_OUTER + position] = (neighbours[2 + position, tile] < 0).astype(jnp.int32)
    for step in range(STEPS):
        for slot in range(2):
            ctl[WET + 2 * step + slot] = wet[step, first + slot]
        ctl[MOVE + step] = moves[step, device]
    moving = moves[0, device]
    rough = start_all(((manning_in.at[moving, 0:EARLY], manning),), sems, 6)
    count = lax.axis_size("xb")
    upper = lax.axis_index("yb")
    column = lax.axis_index("xb")
    source = lax.rem(column + count - 1, count) * 2 + upper
    before = lax.rem(column + count - 2, count) * 2 + upper
    again = moves[0, source] == moves[1, source]
    tile_first = source * 2 + moves[0, source]
    tile_second = jnp.where(
        again, before * 2 + moves[0, before], source * 2 + 1 - moves[0, source]
    )
    for step in range(STEPS):
        ctl[WET_FIRST + step] = wet[step, tile_first]
        ctl[WET_SECOND + step] = wet[step, tile_second]

    wait_all(copies[3:] + rough)
    early = []
    for (begin, end), leaving in zip(PIECES, (leaving_low, leaving_high)):
        early += start_all(
            (
                (state.at[moving, :, begin:end], leaving.at[0:3]),
                (bed.at[moving, begin:end], leaving.at[3]),
                (manning.at[begin:end], leaving.at[4]),
            ),
            sems,
            7 + len(early),
        )
    total = jnp.zeros((ROWS, TILE), jnp.float32)
    for slot in range(2):

        def group(index, best, slot=slot):
            rows = pl.ds(pl.multiple_of(index * ROWS, ROWS), ROWS)
            along_x, along_y = cell(*(state[slot, field, rows, :] for field in range(3)))
            return jnp.maximum(best, jnp.maximum(along_x[5], along_y[5]))

        best = lax.fori_loop(0, TILE // ROWS, group, jnp.zeros((ROWS, TILE), jnp.float32))
        total = jnp.maximum(total, jnp.where(wet[0, first + slot] > 0, best, 0.0))
    messages(ctl, state, bed, jnp.max(total, keepdims=True), out, columns)
    wait_all(early)


def hold(order, leaving, same):
    del order, leaving, same


class Passing:
    def __init__(self, ctl, state_in, bed_in, manning_in, arrived, leaving, buffer, sems):
        self.again = ctl[MOVE] == ctl[MOVE + 1]
        self.other = 1 - ctl[MOVE]
        self.refs = state_in, bed_in, manning_in, arrived, buffer, sems
        self.outgoing = [
            pltpu.make_async_copy(buffer.at[:, begin:end], piece, sems.at[1 + index])
            for index, ((begin, end), piece) in enumerate(zip(PIECES, leaving))
        ]

    def start(self):
        state_in, bed_in, manning_in, arrived, buffer, sems = self.refs
        rows = slice(0, EARLY)
        sem = sems.at[0]

        @pl.when(self.again)
        def _():
            for (begin, end), piece in zip(PIECES, arrived):
                pltpu.make_async_copy(piece, buffer.at[:, begin:end], sem).start()

        @pl.when(jnp.logical_not(self.again))
        def _():
            pltpu.make_async_copy(state_in.at[self.other, :, rows], buffer.at[0:3], sem).start()
            pltpu.make_async_copy(bed_in.at[self.other, rows], buffer.at[3], sem).start()
            pltpu.make_async_copy(manning_in.at[self.other, rows], buffer.at[4], sem).start()

    def middle(self):
        _, _, _, arrived, buffer, sems = self.refs
        for (begin, end), piece in zip(PIECES, arrived):
            pltpu.make_async_copy(piece, buffer.at[:, begin:end], sems.at[0]).wait()
        for copy in self.outgoing:
            copy.start()

    def end(self):
        wait_all(self.outgoing)


def rates_and_leaving(
    ctl, state_in, bed_in, state_first, manning_in, arrived_low, arrived_high,
    rate_out, leaving_low, leaving_high,
    state, bed, rate, sems, buffer, moving,
):
    arrived = arrived_low, arrived_high
    passing = Passing(
        ctl, state_first, bed_in, manning_in, arrived, (leaving_low, leaving_high), buffer, moving
    )
    rates(ctl, state_in, bed_in, rate_out, state, bed, rate, sems, passing)


def rates_after(ctl, state_in, bed_in, order, *rest):
    del order
    rates(ctl, state_in, bed_in, *rest)


def rates(ctl, state_in, bed_in, rate_out, state, bed, rate, sems, passing=None):
    width = 2 * TILE
    row_ids = lax.broadcasted_iota(jnp.int32, (STRIP, width), 0)
    row8 = sublanes(width)
    lane = lax.broadcasted_iota(jnp.int32, (STRIP, LANES), 1)
    last = TILE // STRIP - 1
    chunk = TILE // CHUNKS
    slots = [slot_of(ctl, position) for position in range(2)]
    incoming = []
    for part in range(CHUNKS):
        rows = slice(part * chunk, (part + 1) * chunk)
        incoming.append(
            start_all(
                (
                    (state_in.at[:, :, rows], state.at[:, :, rows]),
                    (bed_in.at[:, rows], bed.at[:, rows]),
                ),
                sems,
                2 * part,
            )
        )
    if passing:
        passing.start()
    keep_west, keep_east, keep_south, keep_north = (
        jnp.where(flag(ctl, index), 1.0, 0.0)
        for index in (WALL_WEST, WALL_EAST, WALL_OUTER, WALL_OUTER + 1)
    )

    def strip(field, rows):
        if field == 3:
            return jnp.concatenate([bed[slot, rows, :] for slot in slots], 1)
        return jnp.concatenate([state[slot, field, rows, :] for slot in slots], 1)

    def blocks(value):
        return [value[:, k * LANES : (k + 1) * LANES] for k in range(4)]

    def right_of(value, end=None):
        turned = [pltpu.roll(part, LANES - 1, 1) for part in blocks(value)]
        after = turned[1:] + [turned[3] if end is None else end]
        return jnp.concatenate(
            [
                jnp.where(lane == LANES - 1, following, part)
                if following is not part
                else part
                for part, following in zip(turned, after)
            ],
            1,
        )

    def left_of(value, end):
        turned = [pltpu.roll(part, 1, 1) for part in blocks(value)]
        before = [end] + turned[:3]
        return jnp.concatenate(
            [jnp.where(lane == 0, previous, part) for part, previous in zip(turned, before)], 1
        )

    def down(value):
        return pltpu.roll(value, STRIP + 7, 0)[:STRIP]

    def group(index, carry):
        base = pl.multiple_of(index * STRIP, STRIP)
        rows = pl.ds(base, STRIP)
        after = pl.ds(pl.multiple_of(jnp.minimum(base + STRIP, TILE - 8), 8), 8)
        at_end = index == last
        fields = [
            jnp.concatenate([strip(field, rows), strip(field, after)], 0) for field in range(3)
        ]
        cells_x, cells_y = cell(*fields)
        here_x = tuple(value[:STRIP] for value in cells_x)
        here_y = tuple(value[:STRIP] for value in cells_y)

        ending = jnp.logical_and(row8 == 7, at_end)
        faces = list(face(here_x, tuple(down(value) for value in cells_x)))
        wall = keep_east * (2.0 * (here_x[3] + here_x[5] * here_x[1])[STRIP - 8 :])
        for component, value in enumerate((0.0, wall, 0.0)):
            upper = faces[component]
            faces[component] = jnp.concatenate(
                [upper[: STRIP - 8], jnp.where(ending, value, upper[STRIP - 8 :])], 0
            )
        turned = tuple(pltpu.roll(value, 1, 0) for value in faces)
        change_x = tuple(
            value - jnp.where(row_ids == 0, before, moved)
            for value, before, moved in zip(faces, carry[:3], turned)
        )
        ground = strip(3, rows)
        ground_after = jnp.where(
            at_end,
            jnp.broadcast_to(keep_east * ground[STRIP - 1 :], (8, width)),
            strip(3, after),
        )
        ground_up = pltpu.roll(ground, 1, 0)
        slope_x = down(jnp.concatenate([ground, ground_after], 0)) - jnp.where(
            row_ids == 0, carry[3], ground_up
        )
        carried = tuple(value[0:1, :] for value in turned) + (ground_up[0:1, :],)

        faces_y = list(face(here_y, tuple(right_of(value) for value in here_y)))
        normal = here_y[3]
        spread_y = here_y[5] * here_y[1]
        north = keep_north * (2.0 * (normal + spread_y)[:, width - LANES :])
        south = keep_south * (2.0 * (normal - spread_y)[:, :LANES])
        change_y = []
        for component, (high, low) in enumerate(((0.0, 0.0), (north, south), (0.0, 0.0))):
            parts = blocks(faces_y[component])
            parts[3] = jnp.where(lane == LANES - 1, high, parts[3])
            value = jnp.concatenate(parts, 1)
            change_y.append(value - left_of(value, low))
        slope_y = right_of(ground, keep_north * ground[:, width - LANES :]) - left_of(
            ground, keep_south * ground[:, :LANES]
        )
        weight = SLOPE * here_x[0]
        results = (
            SCALE * (change_x[0] + change_y[0]),
            SCALE * (change_x[1] + change_y[2]) + weight * slope_x,
            SCALE * (change_x[2] + change_y[1]) + weight * slope_y,
        )
        for field, value in enumerate(results):
            for position, slot in enumerate(slots):
                rate[slot, field, rows, :] = value[:, position * TILE : (position + 1) * TILE]
        return carried

    wait_all(incoming[0])
    top, _ = cell(*(strip(field, slice(0, 8)) for field in range(3)))
    nothing = jnp.zeros((1, width), jnp.float32)
    carry = (
        nothing,
        keep_west * (2.0 * (top[3] - top[5] * top[1])[0:1]),
        nothing,
        keep_west * strip(3, slice(0, 8))[0:1],
    )
    per_chunk = chunk // STRIP
    outgoing = []
    for part in range(CHUNKS):
        if part + 1 < CHUNKS:
            wait_all(incoming[part + 1])
        carry = lax.fori_loop(part * per_chunk, (part + 1) * per_chunk, group, carry)
        rows = slice(part * chunk, (part + 1) * chunk)
        outgoing += start_all(
            ((rate.at[:, :, rows], rate_out.at[:, :, rows]),), sems, 2 * CHUNKS + part
        )
        if passing and part == CHUNKS // 2:
            passing.middle()
    wait_all(outgoing)
    if passing:
        passing.end()


def moved_on(old, slopes, rough, delta, wet_now):
    h, hu, hv = (value - delta * slope for value, slope in zip(old, slopes))
    inverse = 1.0 / h
    u = hu * inverse
    v = hv * inverse
    speed = jnp.sqrt(u * u + v * v)
    power = jnp.exp((-4.0 / 3.0) * jnp.log(jnp.abs(h)))
    drag = (GRAVITY * delta) * (rough * rough) * (speed * power)
    factor = 1.0 / (1.0 + drag)
    fresh = (h, hu * factor, hv * factor)
    return tuple(jnp.where(wet_now, new, value) for new, value in zip(fresh, old))


def repeat_steps(ctl, wet_from, deltas, early, work, other, sems):
    incoming = []
    for ref in early:
        begin = 0 if ref is early[0] else early[0].shape[1]
        incoming += start_all(
            ((ref, work.at[:, begin : begin + ref.shape[1]]),), sems, len(incoming)
        )
    row_ids = lax.broadcasted_iota(jnp.int32, (ROWS, TILE), 0)
    lane = lax.broadcasted_iota(jnp.int32, (ROWS, LANES), 1)
    start = tuple(jnp.zeros((1, TILE), jnp.float32) for _ in range(4))

    def halves(value):
        return value[:, :LANES], value[:, LANES:]

    def right_of(value):
        low, high = (pltpu.roll(part, LANES - 1, 1) for part in halves(value))
        return jnp.concatenate([jnp.where(lane == LANES - 1, high, low), high], 1)

    def left_of(value):
        low, high = (pltpu.roll(part, 1, 1) for part in halves(value))
        return jnp.concatenate([low, jnp.where(lane == 0, low, high)], 1)

    def down(value):
        return pltpu.roll(value, ROWS + 7, 0)[:ROWS]

    for step in range(STEPS):
        source, target = (work, other) if step % 2 == 0 else (other, work)
        delta = deltas[step][0:1, :]
        wet_now = flag(ctl, wet_from + step)

        def group(index, carry, source=source, target=target, delta=delta, wet_now=wet_now):
            base = pl.multiple_of(index * ROWS, ROWS)
            rows = pl.ds(base, ROWS)
            after = pl.ds(pl.multiple_of(jnp.minimum(base + ROWS, EARLY - 8), 8), 8)
            refs = [source.at[field] for field in range(3)] + [work.at[3]]
            fields = [jnp.concatenate([ref[rows, :], ref[after, :]], 0) for ref in refs]
            cells_x, cells_y = cell(*fields[:3])
            here_x = tuple(value[:ROWS] for value in cells_x)
            here_y = tuple(value[:ROWS] for value in cells_y)
            faces_x = face(here_x, tuple(down(value) for value in cells_x))
            turned = tuple(pltpu.roll(value, 1, 0) for value in faces_x)
            change_x = tuple(
                value - jnp.where(row_ids == 0, before, moved)
                for value, before, moved in zip(faces_x, carry[:3], turned)
            )
            ground = fields[3][:ROWS]
            ground_up = pltpu.roll(ground, 1, 0)
            slope_x = down(fields[3]) - jnp.where(row_ids == 0, carry[3], ground_up)
            carried = tuple(value[0:1, :] for value in turned) + (ground_up[0:1, :],)
            faces_y = face(here_y, tuple(right_of(value) for value in here_y))
            change_y = tuple(value - left_of(value) for value in faces_y)
            slope_y = right_of(ground) - left_of(ground)
            old = tuple(value[:ROWS] for value in fields[:3])
            weight = SLOPE * old[0]
            slopes = (
                SCALE * (change_x[0] + change_y[0]),
                SCALE * (change_x[1] + change_y[2]) + weight * slope_x,
                SCALE * (change_x[2] + change_y[1]) + weight * slope_y,
            )
            for field, value in enumerate(
                moved_on(old, slopes, work[4, rows, :], delta, wet_now)
            ):
                target[field, rows, :] = value
            return carried

        if step == 0:
            wait_all(incoming)
        lax.fori_loop(0, EARLY // ROWS, group, start)


def late_rows(tile, late):
    row = sublanes()
    kept = EARLY - 8
    lane = lax.broadcasted_iota(jnp.int32, (8, LANES), 1)
    for field in range(3):
        late[field, 0:8, :] = jnp.where(
            row < 3, tile[field, 0:8, :], tile[field, kept : kept + 8, :]
        )
        packed = [jnp.zeros((8, LANES), jnp.float32)] * 2
        for block in range(EARLY // 8):
            rows = slice(8 * block, 8 * block + 8)
            sides = jnp.where(lane < 64, tile[field, rows, :LANES], tile[field, rows, LANES:])
            turned = pltpu.roll(sides, (3 + 8 * block) % LANES, 1)
            which = block // 16
            packed[which] = jnp.where(lane // 8 == block % 16, turned, packed[which])
        late[field, 8:16, :] = jnp.concatenate(packed, 1)
        late[field, 16:, :] = tile[field, EARLY:, :]


def merge(late, early, tile):
    row = sublanes()
    lane = lax.broadcasted_iota(jnp.int32, (8, LANES), 1)
    for field in range(3):
        first = late[field, 0:8, :]
        for block in range(EARLY // 8):
            rows = slice(8 * block, 8 * block + 8)
            which = block // 16
            packed = late[field, 8:16, which * LANES : (which + 1) * LANES]
            sides = pltpu.roll(packed, (-3 - 8 * block) % LANES, 1)
            value = early[field, rows, :]
            value = jnp.concatenate(
                [
                    jnp.where(lane < 3, sides, value[:, :LANES]),
                    jnp.where(lane >= LANES - 3, sides, value[:, LANES:]),
                ],
                1,
            )
            if block == 0:
                value = jnp.where(row < 3, first, value)
            if block == EARLY // 8 - 1:
                value = jnp.where(row < 5, value, first)
            tile[field, rows, :] = value
        tile[field, EARLY:, :] = late[field, 16:, :]


def repeat_second(ctl, delta0, delta1, delta2, low, high, late, out, late_out, work, tile, sems):
    near = start_all(((late, late_out),), sems, 2)
    repeat_steps(ctl, WET_SECOND, (delta0, delta1, delta2), (low, high), work, tile, sems)
    wait_all(start_all(((tile, out),), sems) + near)


def repeat_first(
    ctl, delta0, delta1, delta2, low, high, late_in, state, out, work, other, tile, late, sems
):
    rest = out.at[1 - ctl[MOVE + 1]]
    again = ctl[MOVE] == ctl[MOVE + 1]

    @pl.when(again)
    def _():
        wait_all(start_all(((state.at[1 - ctl[MOVE]], tile),), sems))

    @pl.when(jnp.logical_not(again))
    def _():
        copies = start_all(((late_in, late),), sems, 2)
        repeat_steps(ctl, WET_FIRST, (delta0, delta1, delta2), (low, high), work, other, sems)
        wait_all(copies)
        merge(late, other, tile)

    wait_all(start_all(((tile, rest),), sems))


def finish(ctl, late_in, early_in, before, out, late, early, tile, sems):
    del before
    wait_all(start_all(((late_in, late), (early_in, early)), sems))
    merge(late, early, tile)
    wait_all(start_all(((tile, out.at[ctl[MOVE + 1]]),), sems))


def second_late(ctl, arrived, own, order, leaving, buffer, sems):
    del order
    again = ctl[MOVE] == ctl[MOVE + 1]

    @pl.when(again)
    def _():
        pltpu.make_async_copy(arrived, buffer, sems.at[0]).start()

    @pl.when(jnp.logical_not(again))
    def _():
        pltpu.make_async_copy(own, buffer, sems.at[0]).start()

    pltpu.make_async_copy(arrived, buffer, sems.at[0]).wait()
    wait_all(start_all(((buffer, leaving),), sems))


def correct_rows(ctl, slot, got, ground, state, rate, bottom):
    position = jnp.where(ctl[SLOT_LOW] == slot, 0, 1)
    device = lax.axis_index("xb") * 2 + lax.axis_index("yb")
    wall = WALL_WEST if bottom else WALL_EAST

    @pl.when(jnp.logical_not(flag(ctl, wall + position)))
    def _():
        peer = device - 2 if bottom else device + 2
        block = pl.ds(pl.multiple_of(peer * 8, 8), 8)
        lines = got[block, :TILE]
        grounds = ground[block, :TILE]
        stride = 4 if got.shape[1] > TILE else 3

        def line(offset):
            other = offset + stride
            picked = jnp.where(
                position == 0, lines[offset : offset + 1, :], lines[other : other + 1, :]
            )
            return jnp.broadcast_to(picked, (8, TILE))

        ghost, _ = cell(*(line(field) for field in range(3)))
        ghost_ground = jnp.where(position == 0, grounds[3:4, :], grounds[7:8, :])
        rows = slice(0, 8) if bottom else slice(TILE - 8, TILE)
        own = [state[slot, field, rows, :] for field in range(3)]
        here, _ = cell(*own)
        fluxes = face(ghost, here) if bottom else face(here, ghost)
        push = SCALE * fluxes[1] + (SLOPE * own[0]) * ghost_ground
        row = sublanes()
        sign = -1.0 if bottom else 1.0
        chosen = row == (0 if bottom else 7)
        for field, value in enumerate((SCALE * fluxes[0], push, SCALE * fluxes[2])):
            rate[slot, field, rows, :] += jnp.where(chosen, sign * value, 0.0)


def column_fix(got, ground, columns):
    upper = lax.axis_index("yb")
    device = lax.axis_index("xb") * 2 + upper
    peer = device + 1 - 2 * upper
    block = pl.ds(pl.multiple_of(peer * 8, 8), 8)
    lines = got[block, :TILE]
    ghost_ground = ground[block, :TILE][3:4]
    mine = columns[...]
    _, ghost = cell(lines[0:1], lines[1:2], lines[2:3])
    _, own = cell(mine[0:1], mine[1:2], mine[2:3])
    low = upper == 0
    left = tuple(jnp.where(low, a, b) for a, b in zip(own, ghost))
    right = tuple(jnp.where(low, b, a) for a, b in zip(own, ghost))
    fluxes = face(left, right)
    sign = jnp.where(low, 1.0, -1.0)
    push = SCALE * fluxes[1] + (SLOPE * mine[0:1]) * ghost_ground
    block8 = stacked(
        [sign * SCALE * fluxes[0], sign * SCALE * fluxes[2], sign * push],
        jnp.zeros((8, TILE), jnp.float32),
    )
    return jnp.transpose(
        jnp.concatenate([block8, jnp.zeros((LANES - 8, TILE), jnp.float32)], 0)
    )


def update(step, ctl, got_in, ground_in, columns_in, state_in, manning_in, rate_in, *rest):
    more = step + 1 < STEPS
    fresh_out, first_out, second_out, delta_out = rest[:4]
    rest = rest[4:]
    state, manning, rate, fresh, got, ground, columns, first, second, delta_keep, sems = rest
    out, columns_out = late_first, late_second = first, second
    small = start_all(
        ((got_in, got), (ground_in, ground), (columns_in, columns)), sems, 5 * PARTS
    )
    size = 2 * TILE // PARTS
    parts = [
        (slot, slice(k * size, (k + 1) * size)) for slot in range(2) for k in range(PARTS // 2)
    ]
    incoming = []
    for index, (slot, rows) in enumerate(parts):
        incoming.append(
            start_all(
                (
                    (rate_in.at[slot, :, rows], rate.at[slot, :, rows]),
                    (state_in.at[slot, :, rows], state.at[slot, :, rows]),
                    (manning_in.at[slot, rows], manning.at[slot, rows]),
                ),
                sems,
                3 * index,
            )
        )
    wait_all(small)
    upper = lax.axis_index("yb")
    devices = 2 * lax.axis_size("xb")
    begin = TILE if got.shape[1] > TILE else 0
    tops = got[0:8, begin : begin + LANES]
    for peer in range(1, devices):
        tops = jnp.maximum(tops, got[peer * 8 : peer * 8 + 8, begin : begin + LANES])
    delta = (COURANT * SPACING) / tops[TOP : TOP + 1, :]
    delta = jnp.concatenate([delta, delta], 1)
    delta_keep[...] = jnp.broadcast_to(delta, (8, TILE))
    outgoing = start_all(((delta_keep, delta_out),), sems, 5 * PARTS + 3)
    fix = column_fix(got, ground, columns)
    facing = jnp.where(upper > 0, ctl[SLOT_LOW], 1 - ctl[SLOT_LOW])
    begin = pl.multiple_of((1 - upper) * LANES, LANES)
    target = (1 - upper) * (LANES - 1)
    lane = lax.broadcasted_iota(jnp.int32, (size, LANES), 1)
    total = jnp.zeros((ROWS, TILE), jnp.float32)
    for index, (slot, part_rows) in enumerate(parts):
        wait_all(incoming[index])
        if part_rows.start == 0:
            correct_rows(ctl, slot, got, ground, state, rate, True)
        if part_rows.stop == TILE:
            correct_rows(ctl, slot, got, ground, state, rate, False)

        @pl.when(facing == slot)
        def _(slot=slot, part_rows=part_rows):
            for field in range(3):
                turned = pltpu.roll(
                    fix[part_rows], lax.rem(target + LANES - field, LANES), 1
                )
                rate[slot, field, part_rows, pl.ds(begin, LANES)] += jnp.where(
                    lane == target, turned, 0.0
                )

        wet_now = flag(ctl, WET + 2 * step + slot)

        def group(index, best, slot=slot, wet_now=wet_now):
            rows = pl.ds(pl.multiple_of(index * ROWS, ROWS), ROWS)
            old = tuple(state[slot, field, rows, :] for field in range(3))
            slopes = tuple(rate[slot, field, rows, :] for field in range(3))
            h, hu, hv = moved_on(old, slopes, manning[slot, rows, :], delta, wet_now)
            fresh[slot, 0, rows, :] = h
            fresh[slot, 1, rows, :] = hu
            fresh[slot, 2, rows, :] = hv
            if more:
                along_x, along_y = cell(h, hu, hv)
                best = jnp.maximum(best, jnp.maximum(along_x[5], along_y[5]))
            return best

        best = lax.fori_loop(
            part_rows.start // ROWS,
            part_rows.stop // ROWS,
            group,
            jnp.zeros((ROWS, TILE), jnp.float32),
        )
        if more:
            best = jnp.where(flag(ctl, WET + 2 * step + 2 + slot), best, 0.0)
            total = jnp.maximum(total, best)
        outgoing += start_all(
            ((fresh.at[slot, :, part_rows], fresh_out.at[slot, :, part_rows]),),
            sems,
            3 * PARTS + index,
        )
    if more:
        messages(ctl, fresh, None, jnp.max(total, keepdims=True), out, columns_out)
        outgoing += start_all(((out, first_out), (columns_out, second_out)), sems, 4 * PARTS)
    else:
        late_rows(fresh.at[ctl[MOVE]], late_first)
        outgoing += start_all(((late_first, first_out),), sems, 4 * PARTS)
        late_rows(fresh.at[1 - ctl[MOVE]], late_second)
        outgoing += start_all(((late_second, second_out),), sems, 4 * PARTS + 1)
    wait_all(outgoing)


def vmem():
    return pl.BlockSpec(memory_space=pltpu.VMEM)


def smem():
    return pl.BlockSpec(memory_space=pltpu.SMEM)


def hbm():
    return pl.BlockSpec(memory_space=pltpu.HBM)


def anywhere():
    return pl.BlockSpec(memory_space=pl.ANY)


def call(
    kernel, outs, out_specs, in_specs, flops, scratch=(), aliases=None, room=VMEM_BYTES, moved=4
):
    return pl.pallas_call(
        kernel,
        scratch_shapes=scratch,
        input_output_aliases=aliases or {},
        out_shape=outs,
        in_specs=in_specs,
        out_specs=out_specs,
        compiler_params=pltpu.CompilerParams(vmem_limit_bytes=room),
        cost_estimate=pl.CostEstimate(flops=flops, bytes_accessed=moved << 20, transcendentals=0),
    )


def f32(*shape):
    return jax.ShapeDtypeStruct(shape, jnp.float32)


def spread(fast):
    return lax.all_to_all(fast, ("xb", "yb"), split_axis=0, concat_axis=0, tiled=True)


def body(state, bed, manning, neighbours, wet, moves):
    shape = f32(*state.shape)
    devices = lax.axis_size("xb") * lax.axis_size("yb")
    sem = [pltpu.SemaphoreType.DMA((1,))]
    whole = pltpu.VMEM(state.shape, jnp.float32)
    part = pltpu.VMEM(bed.shape, jnp.float32)
    tile_shape = f32(*state.shape[1:])
    early_shape = f32(5, EARLY, TILE)
    early_state = f32(3, EARLY, TILE)
    late_shape = f32(3, LATE, TILE)
    delta_shape = f32(8, TILE)

    def buffer(like):
        return pltpu.VMEM(like.shape, jnp.float32)

    piece_shapes = tuple(f32(5, end - begin, TILE) for begin, end in PIECES)
    out, columns, ctl, *leaving = call(
        opening,
        (
            f32(8 * devices, TILE + LANES),
            f32(8, TILE),
            jax.ShapeDtypeStruct((CONTROLS,), jnp.int32),
        )
        + piece_shapes,
        (vmem(), vmem(), smem(), hbm(), hbm()),
        [hbm()] * 6,
        4 << 20,
        [
            whole,
            part,
            pltpu.VMEM((EARLY, TILE), jnp.float32),
            pltpu.SMEM(neighbours.shape[::-1], jnp.int32),
            pltpu.SMEM(wet.shape, jnp.int32),
            pltpu.SMEM(moves.shape, jnp.int32),
            pltpu.SemaphoreType.DMA((13,)),
        ],
    )(state, bed, manning, neighbours.T, wet, moves)
    state_first = state
    ground = None
    deltas = []
    for step in range(STEPS):
        got = spread(out)
        ground = got if step == 0 else ground
        scratch = [whole, part, whole, pltpu.SemaphoreType.DMA((3 * CHUNKS,))]
        if step == 0:
            rate = call(rates, shape, hbm(), [smem(), hbm(), hbm()], 16 << 20, scratch)(
                ctl, state, bed
            )
            leaving[1] = call(
                hold, piece_shapes[1], hbm(), [hbm(), hbm()], 1 << 10, aliases={1: 0}
            )(rate, leaving[1])
            early_first = [shifted(piece, "xb", 1) for piece in leaving]
        elif step == 1:
            rate, *leaving = call(
                rates_and_leaving,
                (shape,) + piece_shapes,
                (hbm(),) * 3,
                [smem()] + [hbm()] * 6,
                16 << 20,
                scratch + [buffer(early_shape), pltpu.SemaphoreType.DMA((3,))],
            )(ctl, state, bed, state_first, manning, *early_first)
            early_second = [shifted(piece, "xb", 1) for piece in leaving]
        else:
            rate = call(rates_after, shape, hbm(), [smem()] + [hbm()] * 3, 16 << 20, scratch)(
                ctl, state, bed, early_second[0]
            )
        more = step + 1 < STEPS
        if more:
            shapes = f32(8 * devices, TILE), f32(8, TILE)
        else:
            shapes = late_shape, late_shape
        outs = call(
            functools.partial(update, step),
            (shape,) + shapes + (delta_shape,),
            (hbm(),) * 4,
            [smem()] + [hbm()] * 6,
            8 << 20,
            [
                whole,
                part,
                whole,
                whole,
                pltpu.VMEM(got.shape, jnp.float32),
                pltpu.VMEM(ground.shape, jnp.float32),
                pltpu.VMEM((8, TILE), jnp.float32),
                buffer(shapes[0]),
                buffer(shapes[1]),
                buffer(delta_shape),
                pltpu.SemaphoreType.DMA((5 * PARTS + 4,)),
            ],
            moved=10,
        )(ctl, got, ground, columns, state, manning, rate)
        deltas.append(outs[-1])
        state, out, columns, _ = outs
    late_first, late_second = out, columns
    room = 16 << 20
    late_arrived = shifted(late_first, "xb", 1)
    second, late_second = call(
        repeat_second,
        (early_state, late_shape),
        (anywhere(), vmem()),
        [smem()] + [vmem()] * 3 + [anywhere()] * 3,
        8 << 20,
        [buffer(early_shape), buffer(early_state), pltpu.SemaphoreType.DMA((3,))],
        room=room,
    )(ctl, *deltas, *early_second, late_second)
    leaving = call(
        second_late,
        late_shape,
        anywhere(),
        [smem(), anywhere(), anywhere(), anywhere()],
        1 << 20,
        [buffer(late_shape)] + sem,
        room=room,
    )(ctl, late_arrived, late_second, second)
    late_next = shifted(leaving, "xb", 1)
    final = call(
        repeat_first,
        shape,
        hbm(),
        [smem()] + [vmem()] * 3 + [anywhere()] * 4,
        8 << 20,
        [
            buffer(early_shape),
            buffer(early_state),
            buffer(tile_shape),
            buffer(late_shape),
            pltpu.SemaphoreType.DMA((3,)),
        ],
        room=room,
    )(ctl, *deltas, *early_first, late_arrived, state)
    return call(
        finish,
        shape,
        hbm(),
        [smem(), anywhere(), anywhere(), hbm()],
        1 << 20,
        [
            buffer(late_shape),
            buffer(early_state),
            buffer(tile_shape),
            pltpu.SemaphoreType.DMA((2,)),
        ],
        {3: 0},
        room=room,
    )(ctl, late_next, second, final)


def solution(mesh):
    placed = (
        P(("runs", "xb", "yb"), None, None, None),
        P(("runs", "xb", "yb"), None, None),
        P(("runs", "xb", "yb"), None, None),
        P("runs", None),
        P(None, "runs"),
        P(None, "runs"),
    )
    return jax.shard_map(
        body,
        mesh=mesh,
        in_specs=placed,
        out_specs=P(("runs", "xb", "yb"), None, None, None),
        check_vma=False,
    )
```

```python
import functools

import jax
import jax.numpy as jnp
from jax import lax
from jax.experimental import pallas as pl
from jax.experimental.pallas import tpu as pltpu
from jax.sharding import PartitionSpec as P

STEPS = 3
GRAVITY = 9.81
ROOT_G = GRAVITY**0.5
SPACING = 5.0
COURANT = 0.2
ROWS = 32
LANES = 128
TILE = 256
VMEM_BYTES = 60 * 1024 * 1024
SLOT_LOW, WALL_WEST, WALL_EAST, WALL_OUTER, WET, MOVE = 0, 1, 3, 5, 7, 13
WET_FIRST, WET_SECOND = 16, 19
CONTROLS = 24
EARLY = 160
PIECES = ((0, 88), (88, 160))
LATE = TILE - EARLY + 16
CHUNKS = 8
PARTS = 8
STRIP = 16
TOP = 6
SCALE = 0.5 / SPACING
SLOPE = GRAVITY / (2.0 * SPACING)


def shifted(value, axis, steps, around=True):
    count = lax.axis_size(axis)
    pairs = [(source, (source + steps) % count) for source in range(count)]
    if not around:
        pairs = [pair for pair in pairs if abs(pair[0] - pair[1]) == abs(steps)]
    return lax.ppermute(value, axis, pairs)


def cell(h, hu, hv):
    root = lax.rsqrt(h)
    inverse = root * root
    u = hu * inverse
    v = hv * inverse
    celerity = ROOT_G * (h * root)
    pressure = (0.5 * GRAVITY) * (h * h)
    cross = hu * v
    speed_x = jnp.abs(u) + celerity
    speed_y = jnp.abs(v) + celerity
    along_x = (h, hu, hv, hu * u + pressure, cross, speed_x)
    along_y = (h, hv, hu, hv * v + pressure, cross, speed_y)
    return along_x, along_y


def face(left, right):
    wave = jnp.maximum(left[5], right[5])
    return (
        (left[1] + right[1]) - wave * (right[0] - left[0]),
        (left[3] + right[3]) - wave * (right[1] - left[1]),
        (left[4] + right[4]) - wave * (right[2] - left[2]),
    )


def slot_of(ctl, position):
    low = ctl[SLOT_LOW]
    return low if position == 0 else 1 - low


def flag(ctl, index):
    return ctl[index] > 0


def start_all(pairs, sems, first=0):
    copies = [
        pltpu.make_async_copy(src, dst, sems.at[first + k]) for k, (src, dst) in enumerate(pairs)
    ]
    for copy in copies:
        copy.start()
    return copies


def wait_all(copies):
    for copy in copies:
        copy.wait()


def sublanes(width=TILE):
    return lax.broadcasted_iota(jnp.int32, (8, width), 0)


def stacked(lines, base):
    row = sublanes()
    for index, line in enumerate(lines):
        base = jnp.where(row == index, jnp.broadcast_to(line, (8, TILE)), base)
    return base


def messages(ctl, state, bed, fastest, out, columns):
    upper = lax.axis_index("yb")
    column = lax.axis_index("xb")
    last = lax.axis_size("xb") - 1
    devices = 2 * (last + 1)
    device = column * 2 + upper
    top = jnp.broadcast_to(fastest, (8, TILE))
    for peer in range(devices):
        out[peer * 8 : peer * 8 + 8, :TILE] = top
        if bed is not None:
            out[peer * 8 : peer * 8 + 8, TILE:] = top[:, :LANES]
    row = sublanes()

    def edge(line):
        rows = slice(line, line + 1)
        lines = []
        for position in range(2):
            slot = slot_of(ctl, position)
            lines += [state[slot, field, rows, :] for field in range(3)]
            if bed is not None:
                lines.append(bed[slot, rows, :])
        return stacked(lines, top)

    for inside, peer, line in (
        (column > 0, device - 2, 0),
        (column < last, device + 2, TILE - 1),
    ):

        @pl.when(inside)
        def _(peer=peer, line=line):
            out[pl.ds(pl.multiple_of(peer * 8, 8), 8), :TILE] = edge(line)

    slot = jnp.where(upper > 0, ctl[SLOT_LOW], 1 - ctl[SLOT_LOW])
    begin = pl.multiple_of((1 - upper) * LANES, LANES)
    lane = lax.broadcasted_iota(jnp.int32, (TILE, LANES), 1)
    packed = None
    for field in range(4 if bed is not None else 3):
        if field < 3:
            part = state[slot, field, :, pl.ds(begin, LANES)]
        else:
            part = bed[slot, :, pl.ds(begin, LANES)]
        turned = pltpu.roll(part, field + 1 - upper, 1)
        packed = turned if field == 0 else jnp.where(lane == field, turned, packed)
    lines = jnp.transpose(packed)[:8]
    columns[...] = lines
    start = pl.multiple_of((device + 1 - 2 * upper) * 8, 8)
    out[pl.ds(start, 8), :TILE] = jnp.where(row == TOP, top, lines)


def opening(
    state_in, bed_in, manning_in, neighbours_in, wet_in, moves_in,
    out, columns, ctl, leaving_low, leaving_high,
    state, bed, manning, neighbours, wet, moves, sems,
):
    copies = start_all(
        (
            (neighbours_in, neighbours),
            (wet_in, wet),
            (moves_in, moves),
            (state_in.at[0], state.at[0]),
            (state_in.at[1], state.at[1]),
            (bed_in, bed),
        ),
        sems,
    )
    device = lax.axis_index("xb") * 2 + lax.axis_index("yb")
    wait_all(copies[:3])
    first = device * 2
    low = jnp.where(neighbours[3, first] == first + 1, 0, 1)
    ctl[SLOT_LOW] = low
    for position in range(2):
        slot = low if position == 0 else 1 - low
        tile = first + slot
        ctl[WALL_WEST + position] = (neighbours[0, tile] < 0).astype(jnp.int32)
        ctl[WALL_EAST + position] = (neighbours[1, tile] < 0).astype(jnp.int32)
        ctl[WALL_OUTER + position] = (neighbours[2 + position, tile] < 0).astype(jnp.int32)
    for step in range(STEPS):
        for slot in range(2):
            ctl[WET + 2 * step + slot] = wet[step, first + slot]
        ctl[MOVE + step] = moves[step, device]
    moving = moves[0, device]
    rough = start_all(((manning_in.at[moving, 0:EARLY], manning),), sems, 6)
    count = lax.axis_size("xb")
    upper = lax.axis_index("yb")
    column = lax.axis_index("xb")
    source = lax.rem(column + count - 1, count) * 2 + upper
    before = lax.rem(column + count - 2, count) * 2 + upper
    again = moves[0, source] == moves[1, source]
    tile_first = source * 2 + moves[0, source]
    tile_second = jnp.where(
        again, before * 2 + moves[0, before], source * 2 + 1 - moves[0, source]
    )
    for step in range(STEPS):
        ctl[WET_FIRST + step] = wet[step, tile_first]
        ctl[WET_SECOND + step] = wet[step, tile_second]

    wait_all(copies[3:] + rough)
    early = []
    for (begin, end), leaving in zip(PIECES, (leaving_low, leaving_high)):
        early += start_all(
            (
                (state.at[moving, :, begin:end], leaving.at[0:3]),
                (bed.at[moving, begin:end], leaving.at[3]),
                (manning.at[begin:end], leaving.at[4]),
            ),
            sems,
            7 + len(early),
        )
    total = jnp.zeros((ROWS, TILE), jnp.float32)
    for slot in range(2):

        def group(index, best, slot=slot):
            rows = pl.ds(pl.multiple_of(index * ROWS, ROWS), ROWS)
            along_x, along_y = cell(*(state[slot, field, rows, :] for field in range(3)))
            return jnp.maximum(best, jnp.maximum(along_x[5], along_y[5]))

        best = lax.fori_loop(0, TILE // ROWS, group, jnp.zeros((ROWS, TILE), jnp.float32))
        total = jnp.maximum(total, jnp.where(wet[0, first + slot] > 0, best, 0.0))
    messages(ctl, state, bed, jnp.max(total, keepdims=True), out, columns)
    wait_all(early)


def hold(order, leaving, same):
    del order, leaving, same


class Passing:
    def __init__(self, ctl, state_in, bed_in, manning_in, arrived, leaving, buffer, sems):
        self.again = ctl[MOVE] == ctl[MOVE + 1]
        self.other = 1 - ctl[MOVE]
        self.refs = state_in, bed_in, manning_in, arrived, buffer, sems
        self.outgoing = [
            pltpu.make_async_copy(buffer.at[:, begin:end], piece, sems.at[1 + index])
            for index, ((begin, end), piece) in enumerate(zip(PIECES, leaving))
        ]

    def start(self):
        state_in, bed_in, manning_in, arrived, buffer, sems = self.refs
        rows = slice(0, EARLY)
        sem = sems.at[0]

        @pl.when(self.again)
        def _():
            for (begin, end), piece in zip(PIECES, arrived):
                pltpu.make_async_copy(piece, buffer.at[:, begin:end], sem).start()

        @pl.when(jnp.logical_not(self.again))
        def _():
            pltpu.make_async_copy(state_in.at[self.other, :, rows], buffer.at[0:3], sem).start()
            pltpu.make_async_copy(bed_in.at[self.other, rows], buffer.at[3], sem).start()
            pltpu.make_async_copy(manning_in.at[self.other, rows], buffer.at[4], sem).start()

    def middle(self):
        _, _, _, arrived, buffer, sems = self.refs
        for (begin, end), piece in zip(PIECES, arrived):
            pltpu.make_async_copy(piece, buffer.at[:, begin:end], sems.at[0]).wait()
        for copy in self.outgoing:
            copy.start()

    def end(self):
        wait_all(self.outgoing)


def rates_and_leaving(
    ctl, state_in, bed_in, state_first, manning_in, arrived_low, arrived_high,
    rate_out, leaving_low, leaving_high,
    state, bed, rate, sems, buffer, moving,
):
    arrived = arrived_low, arrived_high
    passing = Passing(
        ctl, state_first, bed_in, manning_in, arrived, (leaving_low, leaving_high), buffer, moving
    )
    rates(ctl, state_in, bed_in, rate_out, state, bed, rate, sems, passing)


def rates_after(ctl, state_in, bed_in, order, *rest):
    del order
    rates(ctl, state_in, bed_in, *rest)


def rates(ctl, state_in, bed_in, rate_out, state, bed, rate, sems, passing=None):
    width = 2 * TILE
    row_ids = lax.broadcasted_iota(jnp.int32, (STRIP, width), 0)
    row8 = sublanes(width)
    lane = lax.broadcasted_iota(jnp.int32, (STRIP, LANES), 1)
    last = TILE // STRIP - 1
    chunk = TILE // CHUNKS
    slots = [slot_of(ctl, position) for position in range(2)]
    incoming = []
    for part in range(CHUNKS):
        rows = slice(part * chunk, (part + 1) * chunk)
        incoming.append(
            start_all(
                (
                    (state_in.at[:, :, rows], state.at[:, :, rows]),
                    (bed_in.at[:, rows], bed.at[:, rows]),
                ),
                sems,
                2 * part,
            )
        )
    if passing:
        passing.start()
    keep_west, keep_east, keep_south, keep_north = (
        jnp.where(flag(ctl, index), 1.0, 0.0)
        for index in (WALL_WEST, WALL_EAST, WALL_OUTER, WALL_OUTER + 1)
    )

    def strip(field, rows):
        if field == 3:
            return jnp.concatenate([bed[slot, rows, :] for slot in slots], 1)
        return jnp.concatenate([state[slot, field, rows, :] for slot in slots], 1)

    def blocks(value):
        return [value[:, k * LANES : (k + 1) * LANES] for k in range(4)]

    def right_of(value, end=None):
        turned = [pltpu.roll(part, LANES - 1, 1) for part in blocks(value)]
        after = turned[1:] + [turned[3] if end is None else end]
        return jnp.concatenate(
            [
                jnp.where(lane == LANES - 1, following, part)
                if following is not part
                else part
                for part, following in zip(turned, after)
            ],
            1,
        )

    def left_of(value, end):
        turned = [pltpu.roll(part, 1, 1) for part in blocks(value)]
        before = [end] + turned[:3]
        return jnp.concatenate(
            [jnp.where(lane == 0, previous, part) for part, previous in zip(turned, before)], 1
        )

    def down(value):
        return pltpu.roll(value, STRIP + 7, 0)[:STRIP]

    def group(index, carry):
        base = pl.multiple_of(index * STRIP, STRIP)
        rows = pl.ds(base, STRIP)
        after = pl.ds(pl.multiple_of(jnp.minimum(base + STRIP, TILE - 8), 8), 8)
        at_end = index == last
        fields = [
            jnp.concatenate([strip(field, rows), strip(field, after)], 0) for field in range(3)
        ]
        cells_x, cells_y = cell(*fields)
        here_x = tuple(value[:STRIP] for value in cells_x)
        here_y = tuple(value[:STRIP] for value in cells_y)

        ending = jnp.logical_and(row8 == 7, at_end)
        faces = list(face(here_x, tuple(down(value) for value in cells_x)))
        wall = keep_east * (2.0 * (here_x[3] + here_x[5] * here_x[1])[STRIP - 8 :])
        for component, value in enumerate((0.0, wall, 0.0)):
            upper = faces[component]
            faces[component] = jnp.concatenate(
                [upper[: STRIP - 8], jnp.where(ending, value, upper[STRIP - 8 :])], 0
            )
        turned = tuple(pltpu.roll(value, 1, 0) for value in faces)
        change_x = tuple(
            value - jnp.where(row_ids == 0, before, moved)
            for value, before, moved in zip(faces, carry[:3], turned)
        )
        ground = strip(3, rows)
        ground_after = jnp.where(
            at_end,
            jnp.broadcast_to(keep_east * ground[STRIP - 1 :], (8, width)),
            strip(3, after),
        )
        ground_up = pltpu.roll(ground, 1, 0)
        slope_x = down(jnp.concatenate([ground, ground_after], 0)) - jnp.where(
            row_ids == 0, carry[3], ground_up
        )
        carried = tuple(value[0:1, :] for value in turned) + (ground_up[0:1, :],)

        faces_y = list(face(here_y, tuple(right_of(value) for value in here_y)))
        normal = here_y[3]
        spread_y = here_y[5] * here_y[1]
        north = keep_north * (2.0 * (normal + spread_y)[:, width - LANES :])
        south = keep_south * (2.0 * (normal - spread_y)[:, :LANES])
        change_y = []
        for component, (high, low) in enumerate(((0.0, 0.0), (north, south), (0.0, 0.0))):
            parts = blocks(faces_y[component])
            parts[3] = jnp.where(lane == LANES - 1, high, parts[3])
            value = jnp.concatenate(parts, 1)
            change_y.append(value - left_of(value, low))
        slope_y = right_of(ground, keep_north * ground[:, width - LANES :]) - left_of(
            ground, keep_south * ground[:, :LANES]
        )
        weight = SLOPE * here_x[0]
        results = (
            SCALE * (change_x[0] + change_y[0]),
            SCALE * (change_x[1] + change_y[2]) + weight * slope_x,
            SCALE * (change_x[2] + change_y[1]) + weight * slope_y,
        )
        for field, value in enumerate(results):
            for position, slot in enumerate(slots):
                rate[slot, field, rows, :] = value[:, position * TILE : (position + 1) * TILE]
        return carried

    wait_all(incoming[0])
    top, _ = cell(*(strip(field, slice(0, 8)) for field in range(3)))
    nothing = jnp.zeros((1, width), jnp.float32)
    carry = (
        nothing,
        keep_west * (2.0 * (top[3] - top[5] * top[1])[0:1]),
        nothing,
        keep_west * strip(3, slice(0, 8))[0:1],
    )
    per_chunk = chunk // STRIP
    outgoing = []
    for part in range(CHUNKS):
        if part + 1 < CHUNKS:
            wait_all(incoming[part + 1])
        carry = lax.fori_loop(part * per_chunk, (part + 1) * per_chunk, group, carry)
        rows = slice(part * chunk, (part + 1) * chunk)
        outgoing += start_all(
            ((rate.at[:, :, rows], rate_out.at[:, :, rows]),), sems, 2 * CHUNKS + part
        )
        if passing and part == CHUNKS // 2:
            passing.middle()
    wait_all(outgoing)
    if passing:
        passing.end()


def moved_on(old, slopes, rough, delta, wet_now):
    h, hu, hv = (value - delta * slope for value, slope in zip(old, slopes))
    inverse = 1.0 / h
    u = hu * inverse
    v = hv * inverse
    speed = jnp.sqrt(u * u + v * v)
    power = jnp.exp((-4.0 / 3.0) * jnp.log(jnp.abs(h)))
    drag = (GRAVITY * delta) * (rough * rough) * (speed * power)
    factor = 1.0 / (1.0 + drag)
    fresh = (h, hu * factor, hv * factor)
    return tuple(jnp.where(wet_now, new, value) for new, value in zip(fresh, old))


def repeat_steps(ctl, wet_from, deltas, early, work, other, sems):
    incoming = []
    for ref in early:
        begin = 0 if ref is early[0] else early[0].shape[1]
        incoming += start_all(
            ((ref, work.at[:, begin : begin + ref.shape[1]]),), sems, len(incoming)
        )
    row_ids = lax.broadcasted_iota(jnp.int32, (ROWS, TILE), 0)
    lane = lax.broadcasted_iota(jnp.int32, (ROWS, LANES), 1)
    start = tuple(jnp.zeros((1, TILE), jnp.float32) for _ in range(4))

    def halves(value):
        return value[:, :LANES], value[:, LANES:]

    def right_of(value):
        low, high = (pltpu.roll(part, LANES - 1, 1) for part in halves(value))
        return jnp.concatenate([jnp.where(lane == LANES - 1, high, low), high], 1)

    def left_of(value):
        low, high = (pltpu.roll(part, 1, 1) for part in halves(value))
        return jnp.concatenate([low, jnp.where(lane == 0, low, high)], 1)

    def down(value):
        return pltpu.roll(value, ROWS + 7, 0)[:ROWS]

    for step in range(STEPS):
        source, target = (work, other) if step % 2 == 0 else (other, work)
        delta = deltas[step][0:1, :]
        wet_now = flag(ctl, wet_from + step)

        def group(index, carry, source=source, target=target, delta=delta, wet_now=wet_now):
            base = pl.multiple_of(index * ROWS, ROWS)
            rows = pl.ds(base, ROWS)
            after = pl.ds(pl.multiple_of(jnp.minimum(base + ROWS, EARLY - 8), 8), 8)
            refs = [source.at[field] for field in range(3)] + [work.at[3]]
            fields = [jnp.concatenate([ref[rows, :], ref[after, :]], 0) for ref in refs]
            cells_x, cells_y = cell(*fields[:3])
            here_x = tuple(value[:ROWS] for value in cells_x)
            here_y = tuple(value[:ROWS] for value in cells_y)
            faces_x = face(here_x, tuple(down(value) for value in cells_x))
            turned = tuple(pltpu.roll(value, 1, 0) for value in faces_x)
            change_x = tuple(
                value - jnp.where(row_ids == 0, before, moved)
                for value, before, moved in zip(faces_x, carry[:3], turned)
            )
            ground = fields[3][:ROWS]
            ground_up = pltpu.roll(ground, 1, 0)
            slope_x = down(fields[3]) - jnp.where(row_ids == 0, carry[3], ground_up)
            carried = tuple(value[0:1, :] for value in turned) + (ground_up[0:1, :],)
            faces_y = face(here_y, tuple(right_of(value) for value in here_y))
            change_y = tuple(value - left_of(value) for value in faces_y)
            slope_y = right_of(ground) - left_of(ground)
            old = tuple(value[:ROWS] for value in fields[:3])
            weight = SLOPE * old[0]
            slopes = (
                SCALE * (change_x[0] + change_y[0]),
                SCALE * (change_x[1] + change_y[2]) + weight * slope_x,
                SCALE * (change_x[2] + change_y[1]) + weight * slope_y,
            )
            for field, value in enumerate(
                moved_on(old, slopes, work[4, rows, :], delta, wet_now)
            ):
                target[field, rows, :] = value
            return carried

        if step == 0:
            wait_all(incoming)
        lax.fori_loop(0, EARLY // ROWS, group, start)


def late_rows(tile, late):
    row = sublanes()
    kept = EARLY - 8
    lane = lax.broadcasted_iota(jnp.int32, (8, LANES), 1)
    for field in range(3):
        late[field, 0:8, :] = jnp.where(
            row < 3, tile[field, 0:8, :], tile[field, kept : kept + 8, :]
        )
        packed = [jnp.zeros((8, LANES), jnp.float32)] * 2
        for block in range(EARLY // 8):
            rows = slice(8 * block, 8 * block + 8)
            sides = jnp.where(lane < 64, tile[field, rows, :LANES], tile[field, rows, LANES:])
            turned = pltpu.roll(sides, (3 + 8 * block) % LANES, 1)
            which = block // 16
            packed[which] = jnp.where(lane // 8 == block % 16, turned, packed[which])
        late[field, 8:16, :] = jnp.concatenate(packed, 1)
        late[field, 16:, :] = tile[field, EARLY:, :]


def merge(late, early, tile):
    row = sublanes()
    lane = lax.broadcasted_iota(jnp.int32, (8, LANES), 1)
    for field in range(3):
        first = late[field, 0:8, :]
        for block in range(EARLY // 8):
            rows = slice(8 * block, 8 * block + 8)
            which = block // 16
            packed = late[field, 8:16, which * LANES : (which + 1) * LANES]
            sides = pltpu.roll(packed, (-3 - 8 * block) % LANES, 1)
            value = early[field, rows, :]
            value = jnp.concatenate(
                [
                    jnp.where(lane < 3, sides, value[:, :LANES]),
                    jnp.where(lane >= LANES - 3, sides, value[:, LANES:]),
                ],
                1,
            )
            if block == 0:
                value = jnp.where(row < 3, first, value)
            if block == EARLY // 8 - 1:
                value = jnp.where(row < 5, value, first)
            tile[field, rows, :] = value
        tile[field, EARLY:, :] = late[field, 16:, :]


def repeat_second(ctl, delta0, delta1, delta2, low, high, late, out, late_out, work, tile, sems):
    near = start_all(((late, late_out),), sems, 2)
    repeat_steps(ctl, WET_SECOND, (delta0, delta1, delta2), (low, high), work, tile, sems)
    wait_all(start_all(((tile, out),), sems) + near)


def repeat_first(
    ctl, delta0, delta1, delta2, low, high, late_in, state, out, work, other, tile, late, sems
):
    rest = out.at[1 - ctl[MOVE + 1]]
    again = ctl[MOVE] == ctl[MOVE + 1]

    @pl.when(again)
    def _():
        wait_all(start_all(((state.at[1 - ctl[MOVE]], tile),), sems))

    @pl.when(jnp.logical_not(again))
    def _():
        copies = start_all(((late_in, late),), sems, 2)
        repeat_steps(ctl, WET_FIRST, (delta0, delta1, delta2), (low, high), work, other, sems)
        wait_all(copies)
        merge(late, other, tile)

    wait_all(start_all(((tile, rest),), sems))


def finish(ctl, late_in, early_in, before, out, late, early, tile, sems):
    del before
    wait_all(start_all(((late_in, late), (early_in, early)), sems))
    merge(late, early, tile)
    wait_all(start_all(((tile, out.at[ctl[MOVE + 1]]),), sems))


def second_late(ctl, arrived, own, order, leaving, buffer, sems):
    del order
    again = ctl[MOVE] == ctl[MOVE + 1]

    @pl.when(again)
    def _():
        pltpu.make_async_copy(arrived, buffer, sems.at[0]).start()

    @pl.when(jnp.logical_not(again))
    def _():
        pltpu.make_async_copy(own, buffer, sems.at[0]).start()

    pltpu.make_async_copy(arrived, buffer, sems.at[0]).wait()
    wait_all(start_all(((buffer, leaving),), sems))


def correct_rows(ctl, slot, got, ground, state, rate, bottom):
    position = jnp.where(ctl[SLOT_LOW] == slot, 0, 1)
    device = lax.axis_index("xb") * 2 + lax.axis_index("yb")
    wall = WALL_WEST if bottom else WALL_EAST

    @pl.when(jnp.logical_not(flag(ctl, wall + position)))
    def _():
        peer = device - 2 if bottom else device + 2
        block = pl.ds(pl.multiple_of(peer * 8, 8), 8)
        lines = got[block, :TILE]
        grounds = ground[block, :TILE]
        stride = 4 if got.shape[1] > TILE else 3

        def line(offset):
            other = offset + stride
            picked = jnp.where(
                position == 0, lines[offset : offset + 1, :], lines[other : other + 1, :]
            )
            return jnp.broadcast_to(picked, (8, TILE))

        ghost, _ = cell(*(line(field) for field in range(3)))
        ghost_ground = jnp.where(position == 0, grounds[3:4, :], grounds[7:8, :])
        rows = slice(0, 8) if bottom else slice(TILE - 8, TILE)
        own = [state[slot, field, rows, :] for field in range(3)]
        here, _ = cell(*own)
        fluxes = face(ghost, here) if bottom else face(here, ghost)
        push = SCALE * fluxes[1] + (SLOPE * own[0]) * ghost_ground
        row = sublanes()
        sign = -1.0 if bottom else 1.0
        chosen = row == (0 if bottom else 7)
        for field, value in enumerate((SCALE * fluxes[0], push, SCALE * fluxes[2])):
            rate[slot, field, rows, :] += jnp.where(chosen, sign * value, 0.0)


def column_fix(got, ground, columns):
    upper = lax.axis_index("yb")
    device = lax.axis_index("xb") * 2 + upper
    peer = device + 1 - 2 * upper
    block = pl.ds(pl.multiple_of(peer * 8, 8), 8)
    lines = got[block, :TILE]
    ghost_ground = ground[block, :TILE][3:4]
    mine = columns[...]
    _, ghost = cell(lines[0:1], lines[1:2], lines[2:3])
    _, own = cell(mine[0:1], mine[1:2], mine[2:3])
    low = upper == 0
    left = tuple(jnp.where(low, a, b) for a, b in zip(own, ghost))
    right = tuple(jnp.where(low, b, a) for a, b in zip(own, ghost))
    fluxes = face(left, right)
    sign = jnp.where(low, 1.0, -1.0)
    push = SCALE * fluxes[1] + (SLOPE * mine[0:1]) * ghost_ground
    block8 = stacked(
        [sign * SCALE * fluxes[0], sign * SCALE * fluxes[2], sign * push],
        jnp.zeros((8, TILE), jnp.float32),
    )
    return jnp.transpose(
        jnp.concatenate([block8, jnp.zeros((LANES - 8, TILE), jnp.float32)], 0)
    )


def update(step, ctl, got_in, ground_in, columns_in, state_in, manning_in, rate_in, *rest):
    more = step + 1 < STEPS
    fresh_out, first_out, second_out, delta_out = rest[:4]
    rest = rest[4:]
    state, manning, rate, fresh, got, ground, columns, first, second, delta_keep, sems = rest
    out, columns_out = late_first, late_second = first, second
    small = start_all(
        ((got_in, got), (ground_in, ground), (columns_in, columns)), sems, 5 * PARTS
    )
    size = 2 * TILE // PARTS
    parts = [
        (slot, slice(k * size, (k + 1) * size)) for slot in range(2) for k in range(PARTS // 2)
    ]
    incoming = []
    for index, (slot, rows) in enumerate(parts):
        incoming.append(
            start_all(
                (
                    (rate_in.at[slot, :, rows], rate.at[slot, :, rows]),
                    (state_in.at[slot, :, rows], state.at[slot, :, rows]),
                    (manning_in.at[slot, rows], manning.at[slot, rows]),
                ),
                sems,
                3 * index,
            )
        )
    wait_all(small)
    upper = lax.axis_index("yb")
    devices = 2 * lax.axis_size("xb")
    begin = TILE if got.shape[1] > TILE else 0
    tops = got[0:8, begin : begin + LANES]
    for peer in range(1, devices):
        tops = jnp.maximum(tops, got[peer * 8 : peer * 8 + 8, begin : begin + LANES])
    delta = (COURANT * SPACING) / tops[TOP : TOP + 1, :]
    delta = jnp.concatenate([delta, delta], 1)
    delta_keep[...] = jnp.broadcast_to(delta, (8, TILE))
    outgoing = start_all(((delta_keep, delta_out),), sems, 5 * PARTS + 3)
    fix = column_fix(got, ground, columns)
    facing = jnp.where(upper > 0, ctl[SLOT_LOW], 1 - ctl[SLOT_LOW])
    begin = pl.multiple_of((1 - upper) * LANES, LANES)
    target = (1 - upper) * (LANES - 1)
    lane = lax.broadcasted_iota(jnp.int32, (size, LANES), 1)
    total = jnp.zeros((ROWS, TILE), jnp.float32)
    for index, (slot, part_rows) in enumerate(parts):
        wait_all(incoming[index])
        if part_rows.start == 0:
            correct_rows(ctl, slot, got, ground, state, rate, True)
        if part_rows.stop == TILE:
            correct_rows(ctl, slot, got, ground, state, rate, False)

        @pl.when(facing == slot)
        def _(slot=slot, part_rows=part_rows):
            for field in range(3):
                turned = pltpu.roll(
                    fix[part_rows], lax.rem(target + LANES - field, LANES), 1
                )
                rate[slot, field, part_rows, pl.ds(begin, LANES)] += jnp.where(
                    lane == target, turned, 0.0
                )

        wet_now = flag(ctl, WET + 2 * step + slot)

        def group(index, best, slot=slot, wet_now=wet_now):
            rows = pl.ds(pl.multiple_of(index * ROWS, ROWS), ROWS)
            old = tuple(state[slot, field, rows, :] for field in range(3))
            slopes = tuple(rate[slot, field, rows, :] for field in range(3))
            h, hu, hv = moved_on(old, slopes, manning[slot, rows, :], delta, wet_now)
            fresh[slot, 0, rows, :] = h
            fresh[slot, 1, rows, :] = hu
            fresh[slot, 2, rows, :] = hv
            if more:
                along_x, along_y = cell(h, hu, hv)
                best = jnp.maximum(best, jnp.maximum(along_x[5], along_y[5]))
            return best

        best = lax.fori_loop(
            part_rows.start // ROWS,
            part_rows.stop // ROWS,
            group,
            jnp.zeros((ROWS, TILE), jnp.float32),
        )
        if more:
            best = jnp.where(flag(ctl, WET + 2 * step + 2 + slot), best, 0.0)
            total = jnp.maximum(total, best)
        outgoing += start_all(
            ((fresh.at[slot, :, part_rows], fresh_out.at[slot, :, part_rows]),),
            sems,
            3 * PARTS + index,
        )
    if more:
        messages(ctl, fresh, None, jnp.max(total, keepdims=True), out, columns_out)
        outgoing += start_all(((out, first_out), (columns_out, second_out)), sems, 4 * PARTS)
    else:
        late_rows(fresh.at[ctl[MOVE]], late_first)
        outgoing += start_all(((late_first, first_out),), sems, 4 * PARTS)
        late_rows(fresh.at[1 - ctl[MOVE]], late_second)
        outgoing += start_all(((late_second, second_out),), sems, 4 * PARTS + 1)
    wait_all(outgoing)


def vmem():
    return pl.BlockSpec(memory_space=pltpu.VMEM)


def smem():
    return pl.BlockSpec(memory_space=pltpu.SMEM)


def hbm():
    return pl.BlockSpec(memory_space=pltpu.HBM)


def anywhere():
    return pl.BlockSpec(memory_space=pl.ANY)


def call(
    kernel, outs, out_specs, in_specs, flops, scratch=(), aliases=None, room=VMEM_BYTES, moved=4
):
    return pl.pallas_call(
        kernel,
        scratch_shapes=scratch,
        input_output_aliases=aliases or {},
        out_shape=outs,
        in_specs=in_specs,
        out_specs=out_specs,
        compiler_params=pltpu.CompilerParams(vmem_limit_bytes=room),
        cost_estimate=pl.CostEstimate(flops=flops, bytes_accessed=moved << 20, transcendentals=0),
    )


def f32(*shape):
    return jax.ShapeDtypeStruct(shape, jnp.float32)


def spread(fast):
    return lax.all_to_all(fast, ("xb", "yb"), split_axis=0, concat_axis=0, tiled=True)


def body(state, bed, manning, neighbours, wet, moves):
    shape = f32(*state.shape)
    devices = lax.axis_size("xb") * lax.axis_size("yb")
    sem = [pltpu.SemaphoreType.DMA((1,))]
    whole = pltpu.VMEM(state.shape, jnp.float32)
    part = pltpu.VMEM(bed.shape, jnp.float32)
    tile_shape = f32(*state.shape[1:])
    early_shape = f32(5, EARLY, TILE)
    early_state = f32(3, EARLY, TILE)
    late_shape = f32(3, LATE, TILE)
    delta_shape = f32(8, TILE)

    def buffer(like):
        return pltpu.VMEM(like.shape, jnp.float32)

    piece_shapes = tuple(f32(5, end - begin, TILE) for begin, end in PIECES)
    out, columns, ctl, *leaving = call(
        opening,
        (
            f32(8 * devices, TILE + LANES),
            f32(8, TILE),
            jax.ShapeDtypeStruct((CONTROLS,), jnp.int32),
        )
        + piece_shapes,
        (vmem(), vmem(), smem(), hbm(), hbm()),
        [hbm()] * 6,
        4 << 20,
        [
            whole,
            part,
            pltpu.VMEM((EARLY, TILE), jnp.float32),
            pltpu.SMEM(neighbours.shape[::-1], jnp.int32),
            pltpu.SMEM(wet.shape, jnp.int32),
            pltpu.SMEM(moves.shape, jnp.int32),
            pltpu.SemaphoreType.DMA((13,)),
        ],
    )(state, bed, manning, neighbours.T, wet, moves)
    state_first = state
    ground = None
    deltas = []
    for step in range(STEPS):
        got = spread(out)
        ground = got if step == 0 else ground
        scratch = [whole, part, whole, pltpu.SemaphoreType.DMA((3 * CHUNKS,))]
        if step == 0:
            rate = call(rates, shape, hbm(), [smem(), hbm(), hbm()], 0, scratch, moved=0)(
                ctl, state, bed
            )
            leaving[1] = call(
                hold, piece_shapes[1], hbm(), [hbm(), hbm()], 1 << 10, aliases={1: 0}
            )(rate, leaving[1])
            early_first = [shifted(piece, "xb", 1) for piece in leaving]
        elif step == 1:
            rate, *leaving = call(
                rates_and_leaving,
                (shape,) + piece_shapes,
                (hbm(),) * 3,
                [smem()] + [hbm()] * 6,
                16 << 20,
                scratch + [buffer(early_shape), pltpu.SemaphoreType.DMA((3,))],
            )(ctl, state, bed, state_first, manning, *early_first)
            early_second = [shifted(piece, "xb", 1) for piece in leaving]
        else:
            rate = call(rates_after, shape, hbm(), [smem()] + [hbm()] * 3, 16 << 20, scratch)(
                ctl, state, bed, early_second[0]
            )
        more = step + 1 < STEPS
        if more:
            shapes = f32(8 * devices, TILE), f32(8, TILE)
        else:
            shapes = late_shape, late_shape
        outs = call(
            functools.partial(update, step),
            (shape,) + shapes + (delta_shape,),
            (hbm(),) * 4,
            [smem()] + [hbm()] * 6,
            8 << 20,
            [
                whole,
                part,
                whole,
                whole,
                pltpu.VMEM(got.shape, jnp.float32),
                pltpu.VMEM(ground.shape, jnp.float32),
                pltpu.VMEM((8, TILE), jnp.float32),
                buffer(shapes[0]),
                buffer(shapes[1]),
                buffer(delta_shape),
                pltpu.SemaphoreType.DMA((5 * PARTS + 4,)),
            ],
            moved=10,
        )(ctl, got, ground, columns, state, manning, rate)
        deltas.append(outs[-1])
        state, out, columns, _ = outs
    late_first, late_second = out, columns
    room = 16 << 20
    late_arrived = shifted(late_first, "xb", 1)
    second, late_second = call(
        repeat_second,
        (early_state, late_shape),
        (anywhere(), vmem()),
        [smem()] + [vmem()] * 3 + [anywhere()] * 3,
        8 << 20,
        [buffer(early_shape), buffer(early_state), pltpu.SemaphoreType.DMA((3,))],
        room=room,
    )(ctl, *deltas, *early_second, late_second)
    leaving = call(
        second_late,
        late_shape,
        anywhere(),
        [smem(), anywhere(), anywhere(), anywhere()],
        1 << 20,
        [buffer(late_shape)] + sem,
        room=room,
    )(ctl, late_arrived, late_second, second)
    late_next = shifted(leaving, "xb", 1)
    final = call(
        repeat_first,
        shape,
        hbm(),
        [smem()] + [vmem()] * 3 + [anywhere()] * 4,
        8 << 20,
        [
            buffer(early_shape),
            buffer(early_state),
            buffer(tile_shape),
            buffer(late_shape),
            pltpu.SemaphoreType.DMA((3,)),
        ],
        room=room,
    )(ctl, *deltas, *early_first, late_arrived, state)
    return call(
        finish,
        shape,
        hbm(),
        [smem(), anywhere(), anywhere(), hbm()],
        1 << 20,
        [
            buffer(late_shape),
            buffer(early_state),
            buffer(tile_shape),
            pltpu.SemaphoreType.DMA((2,)),
        ],
        {3: 0},
        room=room,
    )(ctl, late_next, second, final)


def solution(mesh):
    placed = (
        P(("runs", "xb", "yb"), None, None, None),
        P(("runs", "xb", "yb"), None, None),
        P(("runs", "xb", "yb"), None, None),
        P("runs", None),
        P(None, "runs"),
        P(None, "runs"),
    )
    return jax.shard_map(
        body,
        mesh=mesh,
        in_specs=placed,
        out_specs=P(("runs", "xb", "yb"), None, None, None),
        check_vma=False,
    )
```

```python
import functools

import jax
import jax.numpy as jnp
from jax import lax
from jax.experimental import pallas as pl
from jax.experimental.pallas import tpu as pltpu
from jax.sharding import PartitionSpec as P

STEPS = 3
GRAVITY = 9.81
ROOT_G = GRAVITY**0.5
SPACING = 5.0
COURANT = 0.2
ROWS = 32
LANES = 128
TILE = 256
VMEM_BYTES = 60 * 1024 * 1024
SLOT_LOW, WALL_WEST, WALL_EAST, WALL_OUTER, WET, MOVE = 0, 1, 3, 5, 7, 13
WET_FIRST, WET_SECOND = 16, 19
CONTROLS = 24
EARLY = 160
PIECES = ((0, 88), (88, 160))
LATE = TILE - EARLY + 16
CHUNKS = 8
PARTS = 8
STRIP = 16
TOP = 6
SCALE = 0.5 / SPACING
SLOPE = GRAVITY / (2.0 * SPACING)


def shifted(value, axis, steps, around=True):
    count = lax.axis_size(axis)
    pairs = [(source, (source + steps) % count) for source in range(count)]
    if not around:
        pairs = [pair for pair in pairs if abs(pair[0] - pair[1]) == abs(steps)]
    return lax.ppermute(value, axis, pairs)


def cell(h, hu, hv):
    root = lax.rsqrt(h)
    inverse = root * root
    u = hu * inverse
    v = hv * inverse
    celerity = ROOT_G * (h * root)
    pressure = (0.5 * GRAVITY) * (h * h)
    cross = hu * v
    speed_x = jnp.abs(u) + celerity
    speed_y = jnp.abs(v) + celerity
    along_x = (h, hu, hv, hu * u + pressure, cross, speed_x)
    along_y = (h, hv, hu, hv * v + pressure, cross, speed_y)
    return along_x, along_y


def face(left, right):
    wave = jnp.maximum(left[5], right[5])
    return (
        (left[1] + right[1]) - wave * (right[0] - left[0]),
        (left[3] + right[3]) - wave * (right[1] - left[1]),
        (left[4] + right[4]) - wave * (right[2] - left[2]),
    )


def slot_of(ctl, position):
    low = ctl[SLOT_LOW]
    return low if position == 0 else 1 - low


def flag(ctl, index):
    return ctl[index] > 0


def start_all(pairs, sems, first=0):
    copies = [
        pltpu.make_async_copy(src, dst, sems.at[first + k]) for k, (src, dst) in enumerate(pairs)
    ]
    for copy in copies:
        copy.start()
    return copies


def wait_all(copies):
    for copy in copies:
        copy.wait()


def sublanes(width=TILE):
    return lax.broadcasted_iota(jnp.int32, (8, width), 0)


def stacked(lines, base):
    row = sublanes()
    for index, line in enumerate(lines):
        base = jnp.where(row == index, jnp.broadcast_to(line, (8, TILE)), base)
    return base


def messages(ctl, state, bed, fastest, out, columns):
    upper = lax.axis_index("yb")
    column = lax.axis_index("xb")
    last = lax.axis_size("xb") - 1
    devices = 2 * (last + 1)
    device = column * 2 + upper
    top = jnp.broadcast_to(fastest, (8, TILE))
    for peer in range(devices):
        out[peer * 8 : peer * 8 + 8, :TILE] = top
        if bed is not None:
            out[peer * 8 : peer * 8 + 8, TILE:] = top[:, :LANES]
    row = sublanes()

    def edge(line):
        rows = slice(line, line + 1)
        lines = []
        for position in range(2):
            slot = slot_of(ctl, position)
            lines += [state[slot, field, rows, :] for field in range(3)]
            if bed is not None:
                lines.append(bed[slot, rows, :])
        return stacked(lines, top)

    for inside, peer, line in (
        (column > 0, device - 2, 0),
        (column < last, device + 2, TILE - 1),
    ):

        @pl.when(inside)
        def _(peer=peer, line=line):
            out[pl.ds(pl.multiple_of(peer * 8, 8), 8), :TILE] = edge(line)

    slot = jnp.where(upper > 0, ctl[SLOT_LOW], 1 - ctl[SLOT_LOW])
    begin = pl.multiple_of((1 - upper) * LANES, LANES)
    lane = lax.broadcasted_iota(jnp.int32, (TILE, LANES), 1)
    packed = None
    for field in range(4 if bed is not None else 3):
        if field < 3:
            part = state[slot, field, :, pl.ds(begin, LANES)]
        else:
            part = bed[slot, :, pl.ds(begin, LANES)]
        turned = pltpu.roll(part, field + 1 - upper, 1)
        packed = turned if field == 0 else jnp.where(lane == field, turned, packed)
    lines = jnp.transpose(packed)[:8]
    columns[...] = lines
    start = pl.multiple_of((device + 1 - 2 * upper) * 8, 8)
    out[pl.ds(start, 8), :TILE] = jnp.where(row == TOP, top, lines)


def opening(
    state_in, bed_in, manning_in, neighbours_in, wet_in, moves_in,
    out, columns, ctl, leaving_low, leaving_high,
    state, bed, manning, neighbours, wet, moves, sems,
):
    copies = start_all(
        (
            (neighbours_in, neighbours),
            (wet_in, wet),
            (moves_in, moves),
            (state_in.at[0], state.at[0]),
            (state_in.at[1], state.at[1]),
            (bed_in, bed),
        ),
        sems,
    )
    device = lax.axis_index("xb") * 2 + lax.axis_index("yb")
    wait_all(copies[:3])
    first = device * 2
    low = jnp.where(neighbours[3, first] == first + 1, 0, 1)
    ctl[SLOT_LOW] = low
    for position in range(2):
        slot = low if position == 0 else 1 - low
        tile = first + slot
        ctl[WALL_WEST + position] = (neighbours[0, tile] < 0).astype(jnp.int32)
        ctl[WALL_EAST + position] = (neighbours[1, tile] < 0).astype(jnp.int32)
        ctl[WALL_OUTER + position] = (neighbours[2 + position, tile] < 0).astype(jnp.int32)
    for step in range(STEPS):
        for slot in range(2):
            ctl[WET + 2 * step + slot] = wet[step, first + slot]
        ctl[MOVE + step] = moves[step, device]
    moving = moves[0, device]
    rough = start_all(((manning_in.at[moving, 0:EARLY], manning),), sems, 6)
    count = lax.axis_size("xb")
    upper = lax.axis_index("yb")
    column = lax.axis_index("xb")
    source = lax.rem(column + count - 1, count) * 2 + upper
    before = lax.rem(column + count - 2, count) * 2 + upper
    again = moves[0, source] == moves[1, source]
    tile_first = source * 2 + moves[0, source]
    tile_second = jnp.where(
        again, before * 2 + moves[0, before], source * 2 + 1 - moves[0, source]
    )
    for step in range(STEPS):
        ctl[WET_FIRST + step] = wet[step, tile_first]
        ctl[WET_SECOND + step] = wet[step, tile_second]

    wait_all(copies[3:] + rough)
    early = []
    for (begin, end), leaving in zip(PIECES, (leaving_low, leaving_high)):
        early += start_all(
            (
                (state.at[moving, :, begin:end], leaving.at[0:3]),
                (bed.at[moving, begin:end], leaving.at[3]),
                (manning.at[begin:end], leaving.at[4]),
            ),
            sems,
            7 + len(early),
        )
    total = jnp.zeros((ROWS, TILE), jnp.float32)
    for slot in range(2):

        def group(index, best, slot=slot):
            rows = pl.ds(pl.multiple_of(index * ROWS, ROWS), ROWS)
            along_x, along_y = cell(*(state[slot, field, rows, :] for field in range(3)))
            return jnp.maximum(best, jnp.maximum(along_x[5], along_y[5]))

        best = lax.fori_loop(0, TILE // ROWS, group, jnp.zeros((ROWS, TILE), jnp.float32))
        total = jnp.maximum(total, jnp.where(wet[0, first + slot] > 0, best, 0.0))
    messages(ctl, state, bed, jnp.max(total, keepdims=True), out, columns)
    wait_all(early)


def hold(order, leaving, same):
    del order, leaving, same


class Passing:
    def __init__(self, ctl, state_in, bed_in, manning_in, arrived, leaving, buffer, sems):
        self.again = ctl[MOVE] == ctl[MOVE + 1]
        self.other = 1 - ctl[MOVE]
        self.refs = state_in, bed_in, manning_in, arrived, buffer, sems
        self.outgoing = [
            pltpu.make_async_copy(buffer.at[:, begin:end], piece, sems.at[1 + index])
            for index, ((begin, end), piece) in enumerate(zip(PIECES, leaving))
        ]

    def start(self):
        state_in, bed_in, manning_in, arrived, buffer, sems = self.refs
        rows = slice(0, EARLY)
        sem = sems.at[0]

        @pl.when(self.again)
        def _():
            for (begin, end), piece in zip(PIECES, arrived):
                pltpu.make_async_copy(piece, buffer.at[:, begin:end], sem).start()

        @pl.when(jnp.logical_not(self.again))
        def _():
            pltpu.make_async_copy(state_in.at[self.other, :, rows], buffer.at[0:3], sem).start()
            pltpu.make_async_copy(bed_in.at[self.other, rows], buffer.at[3], sem).start()
            pltpu.make_async_copy(manning_in.at[self.other, rows], buffer.at[4], sem).start()

    def middle(self):
        _, _, _, arrived, buffer, sems = self.refs
        for (begin, end), piece in zip(PIECES, arrived):
            pltpu.make_async_copy(piece, buffer.at[:, begin:end], sems.at[0]).wait()
        for copy in self.outgoing:
            copy.start()

    def end(self):
        wait_all(self.outgoing)


def rates_and_leaving(
    ctl, state_in, bed_in, state_first, manning_in, arrived_low, arrived_high,
    rate_out, leaving_low, leaving_high,
    state, bed, rate, sems, buffer, moving,
):
    arrived = arrived_low, arrived_high
    passing = Passing(
        ctl, state_first, bed_in, manning_in, arrived, (leaving_low, leaving_high), buffer, moving
    )
    rates(ctl, state_in, bed_in, rate_out, state, bed, rate, sems, passing)


def rates_after(ctl, state_in, bed_in, order, *rest):
    del order
    rates(ctl, state_in, bed_in, *rest)


def rates(ctl, state_in, bed_in, rate_out, state, bed, rate, sems, passing=None):
    width = 2 * TILE
    row_ids = lax.broadcasted_iota(jnp.int32, (STRIP, width), 0)
    row8 = sublanes(width)
    lane = lax.broadcasted_iota(jnp.int32, (STRIP, LANES), 1)
    last = TILE // STRIP - 1
    chunk = TILE // CHUNKS
    slots = [slot_of(ctl, position) for position in range(2)]
    incoming = []
    for part in range(CHUNKS):
        rows = slice(part * chunk, (part + 1) * chunk)
        incoming.append(
            start_all(
                (
                    (state_in.at[:, :, rows], state.at[:, :, rows]),
                    (bed_in.at[:, rows], bed.at[:, rows]),
                ),
                sems,
                2 * part,
            )
        )
    if passing:
        passing.start()
    keep_west, keep_east, keep_south, keep_north = (
        jnp.where(flag(ctl, index), 1.0, 0.0)
        for index in (WALL_WEST, WALL_EAST, WALL_OUTER, WALL_OUTER + 1)
    )

    def strip(field, rows):
        if field == 3:
            return jnp.concatenate([bed[slot, rows, :] for slot in slots], 1)
        return jnp.concatenate([state[slot, field, rows, :] for slot in slots], 1)

    def blocks(value):
        return [value[:, k * LANES : (k + 1) * LANES] for k in range(4)]

    def right_of(value, end=None):
        turned = [pltpu.roll(part, LANES - 1, 1) for part in blocks(value)]
        after = turned[1:] + [turned[3] if end is None else end]
        return jnp.concatenate(
            [
                jnp.where(lane == LANES - 1, following, part)
                if following is not part
                else part
                for part, following in zip(turned, after)
            ],
            1,
        )

    def left_of(value, end):
        turned = [pltpu.roll(part, 1, 1) for part in blocks(value)]
        before = [end] + turned[:3]
        return jnp.concatenate(
            [jnp.where(lane == 0, previous, part) for part, previous in zip(turned, before)], 1
        )

    def down(value):
        return pltpu.roll(value, STRIP + 7, 0)[:STRIP]

    def group(index, carry):
        base = pl.multiple_of(index * STRIP, STRIP)
        rows = pl.ds(base, STRIP)
        after = pl.ds(pl.multiple_of(jnp.minimum(base + STRIP, TILE - 8), 8), 8)
        at_end = index == last
        fields = [
            jnp.concatenate([strip(field, rows), strip(field, after)], 0) for field in range(3)
        ]
        cells_x, cells_y = cell(*fields)
        here_x = tuple(value[:STRIP] for value in cells_x)
        here_y = tuple(value[:STRIP] for value in cells_y)

        ending = jnp.logical_and(row8 == 7, at_end)
        faces = list(face(here_x, tuple(down(value) for value in cells_x)))
        wall = keep_east * (2.0 * (here_x[3] + here_x[5] * here_x[1])[STRIP - 8 :])
        for component, value in enumerate((0.0, wall, 0.0)):
            upper = faces[component]
            faces[component] = jnp.concatenate(
                [upper[: STRIP - 8], jnp.where(ending, value, upper[STRIP - 8 :])], 0
            )
        turned = tuple(pltpu.roll(value, 1, 0) for value in faces)
        change_x = tuple(
            value - jnp.where(row_ids == 0, before, moved)
            for value, before, moved in zip(faces, carry[:3], turned)
        )
        ground = strip(3, rows)
        ground_after = jnp.where(
            at_end,
            jnp.broadcast_to(keep_east * ground[STRIP - 1 :], (8, width)),
            strip(3, after),
        )
        ground_up = pltpu.roll(ground, 1, 0)
        slope_x = down(jnp.concatenate([ground, ground_after], 0)) - jnp.where(
            row_ids == 0, carry[3], ground_up
        )
        carried = tuple(value[0:1, :] for value in turned) + (ground_up[0:1, :],)

        faces_y = list(face(here_y, tuple(right_of(value) for value in here_y)))
        normal = here_y[3]
        spread_y = here_y[5] * here_y[1]
        north = keep_north * (2.0 * (normal + spread_y)[:, width - LANES :])
        south = keep_south * (2.0 * (normal - spread_y)[:, :LANES])
        change_y = []
        for component, (high, low) in enumerate(((0.0, 0.0), (north, south), (0.0, 0.0))):
            parts = blocks(faces_y[component])
            parts[3] = jnp.where(lane == LANES - 1, high, parts[3])
            value = jnp.concatenate(parts, 1)
            change_y.append(value - left_of(value, low))
        slope_y = right_of(ground, keep_north * ground[:, width - LANES :]) - left_of(
            ground, keep_south * ground[:, :LANES]
        )
        weight = SLOPE * here_x[0]
        results = (
            SCALE * (change_x[0] + change_y[0]),
            SCALE * (change_x[1] + change_y[2]) + weight * slope_x,
            SCALE * (change_x[2] + change_y[1]) + weight * slope_y,
        )
        for field, value in enumerate(results):
            for position, slot in enumerate(slots):
                rate[slot, field, rows, :] = value[:, position * TILE : (position + 1) * TILE]
        return carried

    wait_all(incoming[0])
    top, _ = cell(*(strip(field, slice(0, 8)) for field in range(3)))
    nothing = jnp.zeros((1, width), jnp.float32)
    carry = (
        nothing,
        keep_west * (2.0 * (top[3] - top[5] * top[1])[0:1]),
        nothing,
        keep_west * strip(3, slice(0, 8))[0:1],
    )
    per_chunk = chunk // STRIP
    outgoing = []
    for part in range(CHUNKS):
        if part + 1 < CHUNKS:
            wait_all(incoming[part + 1])
        carry = lax.fori_loop(part * per_chunk, (part + 1) * per_chunk, group, carry)
        rows = slice(part * chunk, (part + 1) * chunk)
        outgoing += start_all(
            ((rate.at[:, :, rows], rate_out.at[:, :, rows]),), sems, 2 * CHUNKS + part
        )
        if passing and part == CHUNKS // 2:
            passing.middle()
    wait_all(outgoing)
    if passing:
        passing.end()


def moved_on(old, slopes, rough, delta, wet_now):
    h, hu, hv = (value - delta * slope for value, slope in zip(old, slopes))
    inverse = 1.0 / h
    u = hu * inverse
    v = hv * inverse
    speed = jnp.sqrt(u * u + v * v)
    power = jnp.exp((-4.0 / 3.0) * jnp.log(jnp.abs(h)))
    drag = (GRAVITY * delta) * (rough * rough) * (speed * power)
    factor = 1.0 / (1.0 + drag)
    fresh = (h, hu * factor, hv * factor)
    return tuple(jnp.where(wet_now, new, value) for new, value in zip(fresh, old))


def repeat_steps(ctl, wet_from, deltas, early, work, other, sems):
    incoming = []
    for ref in early:
        begin = 0 if ref is early[0] else early[0].shape[1]
        incoming += start_all(
            ((ref, work.at[:, begin : begin + ref.shape[1]]),), sems, len(incoming)
        )
    row_ids = lax.broadcasted_iota(jnp.int32, (ROWS, TILE), 0)
    lane = lax.broadcasted_iota(jnp.int32, (ROWS, LANES), 1)
    start = tuple(jnp.zeros((1, TILE), jnp.float32) for _ in range(4))

    def halves(value):
        return value[:, :LANES], value[:, LANES:]

    def right_of(value):
        low, high = (pltpu.roll(part, LANES - 1, 1) for part in halves(value))
        return jnp.concatenate([jnp.where(lane == LANES - 1, high, low), high], 1)

    def left_of(value):
        low, high = (pltpu.roll(part, 1, 1) for part in halves(value))
        return jnp.concatenate([low, jnp.where(lane == 0, low, high)], 1)

    def down(value):
        return pltpu.roll(value, ROWS + 7, 0)[:ROWS]

    for step in range(STEPS):
        source, target = (work, other) if step % 2 == 0 else (other, work)
        delta = deltas[step][0:1, :]
        wet_now = flag(ctl, wet_from + step)

        def group(index, carry, source=source, target=target, delta=delta, wet_now=wet_now):
            base = pl.multiple_of(index * ROWS, ROWS)
            rows = pl.ds(base, ROWS)
            after = pl.ds(pl.multiple_of(jnp.minimum(base + ROWS, EARLY - 8), 8), 8)
            refs = [source.at[field] for field in range(3)] + [work.at[3]]
            fields = [jnp.concatenate([ref[rows, :], ref[after, :]], 0) for ref in refs]
            cells_x, cells_y = cell(*fields[:3])
            here_x = tuple(value[:ROWS] for value in cells_x)
            here_y = tuple(value[:ROWS] for value in cells_y)
            faces_x = face(here_x, tuple(down(value) for value in cells_x))
            turned = tuple(pltpu.roll(value, 1, 0) for value in faces_x)
            change_x = tuple(
                value - jnp.where(row_ids == 0, before, moved)
                for value, before, moved in zip(faces_x, carry[:3], turned)
            )
            ground = fields[3][:ROWS]
            ground_up = pltpu.roll(ground, 1, 0)
            slope_x = down(fields[3]) - jnp.where(row_ids == 0, carry[3], ground_up)
            carried = tuple(value[0:1, :] for value in turned) + (ground_up[0:1, :],)
            faces_y = face(here_y, tuple(right_of(value) for value in here_y))
            change_y = tuple(value - left_of(value) for value in faces_y)
            slope_y = right_of(ground) - left_of(ground)
            old = tuple(value[:ROWS] for value in fields[:3])
            weight = SLOPE * old[0]
            slopes = (
                SCALE * (change_x[0] + change_y[0]),
                SCALE * (change_x[1] + change_y[2]) + weight * slope_x,
                SCALE * (change_x[2] + change_y[1]) + weight * slope_y,
            )
            for field, value in enumerate(
                moved_on(old, slopes, work[4, rows, :], delta, wet_now)
            ):
                target[field, rows, :] = value
            return carried

        if step == 0:
            wait_all(incoming)
        lax.fori_loop(0, EARLY // ROWS, group, start)


def late_rows(tile, late):
    row = sublanes()
    kept = EARLY - 8
    lane = lax.broadcasted_iota(jnp.int32, (8, LANES), 1)
    for field in range(3):
        late[field, 0:8, :] = jnp.where(
            row < 3, tile[field, 0:8, :], tile[field, kept : kept + 8, :]
        )
        packed = [jnp.zeros((8, LANES), jnp.float32)] * 2
        for block in range(EARLY // 8):
            rows = slice(8 * block, 8 * block + 8)
            sides = jnp.where(lane < 64, tile[field, rows, :LANES], tile[field, rows, LANES:])
            turned = pltpu.roll(sides, (3 + 8 * block) % LANES, 1)
            which = block // 16
            packed[which] = jnp.where(lane // 8 == block % 16, turned, packed[which])
        late[field, 8:16, :] = jnp.concatenate(packed, 1)
        late[field, 16:, :] = tile[field, EARLY:, :]


def merge(late, early, tile):
    for field in range(3):
        merge_field(field, late, early, tile)


def merge_field(field, late, early, tile):
    row = sublanes()
    lane = lax.broadcasted_iota(jnp.int32, (8, LANES), 1)
    first = late[field, 0:8, :]
    for block in range(EARLY // 8):
        rows = slice(8 * block, 8 * block + 8)
        which = block // 16
        packed = late[field, 8:16, which * LANES : (which + 1) * LANES]
        sides = pltpu.roll(packed, (-3 - 8 * block) % LANES, 1)
        value = early[field, rows, :]
        value = jnp.concatenate(
            [
                jnp.where(lane < 3, sides, value[:, :LANES]),
                jnp.where(lane >= LANES - 3, sides, value[:, LANES:]),
            ],
            1,
        )
        if block == 0:
            value = jnp.where(row < 3, first, value)
        if block == EARLY // 8 - 1:
            value = jnp.where(row < 5, value, first)
        tile[field, rows, :] = value
    tile[field, EARLY:, :] = late[field, 16:, :]


def repeat_second(ctl, delta0, delta1, delta2, low, high, late, out, late_out, work, tile, sems):
    near = start_all(((late, late_out),), sems, 2)
    repeat_steps(ctl, WET_SECOND, (delta0, delta1, delta2), (low, high), work, tile, sems)
    wait_all(start_all(((tile, out),), sems) + near)


def repeat_first(
    ctl, delta0, delta1, delta2, low, high, late_in, state, out, work, other, tile, late, sems
):
    rest = out.at[1 - ctl[MOVE + 1]]
    again = ctl[MOVE] == ctl[MOVE + 1]

    @pl.when(again)
    def _():
        wait_all(start_all(((state.at[1 - ctl[MOVE]], tile),), sems))

    @pl.when(jnp.logical_not(again))
    def _():
        copies = start_all(((late_in, late),), sems, 2)
        repeat_steps(ctl, WET_FIRST, (delta0, delta1, delta2), (low, high), work, other, sems)
        wait_all(copies)
        merge(late, other, tile)

    wait_all(start_all(((tile, rest),), sems))


def finish(ctl, late, early, before, out, tile, sems):
    del before
    copies = []
    for field in range(3):
        merge_field(field, late, early, tile)
        copies += start_all(
            ((tile.at[field], out.at[ctl[MOVE + 1], field]),), sems, field
        )
    wait_all(copies)


def second_late(ctl, arrived, own, order, leaving):
    del order
    again = ctl[MOVE] == ctl[MOVE + 1]
    for field in range(3):
        leaving[field] = jnp.where(again, arrived[field], own[field])


def correct_rows(ctl, slot, got, ground, state, rate, bottom):
    position = jnp.where(ctl[SLOT_LOW] == slot, 0, 1)
    device = lax.axis_index("xb") * 2 + lax.axis_index("yb")
    wall = WALL_WEST if bottom else WALL_EAST

    @pl.when(jnp.logical_not(flag(ctl, wall + position)))
    def _():
        peer = device - 2 if bottom else device + 2
        block = pl.ds(pl.multiple_of(peer * 8, 8), 8)
        lines = got[block, :TILE]
        grounds = ground[block, :TILE]
        stride = 4 if got.shape[1] > TILE else 3

        def line(offset):
            other = offset + stride
            picked = jnp.where(
                position == 0, lines[offset : offset + 1, :], lines[other : other + 1, :]
            )
            return jnp.broadcast_to(picked, (8, TILE))

        ghost, _ = cell(*(line(field) for field in range(3)))
        ghost_ground = jnp.where(position == 0, grounds[3:4, :], grounds[7:8, :])
        rows = slice(0, 8) if bottom else slice(TILE - 8, TILE)
        own = [state[slot, field, rows, :] for field in range(3)]
        here, _ = cell(*own)
        fluxes = face(ghost, here) if bottom else face(here, ghost)
        push = SCALE * fluxes[1] + (SLOPE * own[0]) * ghost_ground
        row = sublanes()
        sign = -1.0 if bottom else 1.0
        chosen = row == (0 if bottom else 7)
        for field, value in enumerate((SCALE * fluxes[0], push, SCALE * fluxes[2])):
            rate[slot, field, rows, :] += jnp.where(chosen, sign * value, 0.0)


def column_fix(got, ground, columns):
    upper = lax.axis_index("yb")
    device = lax.axis_index("xb") * 2 + upper
    peer = device + 1 - 2 * upper
    block = pl.ds(pl.multiple_of(peer * 8, 8), 8)
    lines = got[block, :TILE]
    ghost_ground = ground[block, :TILE][3:4]
    mine = columns[...]
    _, ghost = cell(lines[0:1], lines[1:2], lines[2:3])
    _, own = cell(mine[0:1], mine[1:2], mine[2:3])
    low = upper == 0
    left = tuple(jnp.where(low, a, b) for a, b in zip(own, ghost))
    right = tuple(jnp.where(low, b, a) for a, b in zip(own, ghost))
    fluxes = face(left, right)
    sign = jnp.where(low, 1.0, -1.0)
    push = SCALE * fluxes[1] + (SLOPE * mine[0:1]) * ghost_ground
    block8 = stacked(
        [sign * SCALE * fluxes[0], sign * SCALE * fluxes[2], sign * push],
        jnp.zeros((8, TILE), jnp.float32),
    )
    return jnp.transpose(
        jnp.concatenate([block8, jnp.zeros((LANES - 8, TILE), jnp.float32)], 0)
    )


def update(step, ctl, got_in, ground_in, columns_in, state_in, manning_in, rate_in, *rest):
    more = step + 1 < STEPS
    fresh_out, first_out, second_out, delta_out = rest[:4]
    rest = rest[4:]
    state, manning, rate, fresh, got, ground, columns, first, second, delta_keep, sems = rest
    out, columns_out = late_first, late_second = first, second
    small = start_all(
        ((got_in, got), (ground_in, ground), (columns_in, columns)), sems, 5 * PARTS
    )
    size = 2 * TILE // PARTS
    parts = [
        (slot, slice(k * size, (k + 1) * size)) for slot in range(2) for k in range(PARTS // 2)
    ]
    incoming = []
    for index, (slot, rows) in enumerate(parts):
        incoming.append(
            start_all(
                (
                    (rate_in.at[slot, :, rows], rate.at[slot, :, rows]),
                    (state_in.at[slot, :, rows], state.at[slot, :, rows]),
                    (manning_in.at[slot, rows], manning.at[slot, rows]),
                ),
                sems,
                3 * index,
            )
        )
    wait_all(small)
    upper = lax.axis_index("yb")
    devices = 2 * lax.axis_size("xb")
    begin = TILE if got.shape[1] > TILE else 0
    tops = got[0:8, begin : begin + LANES]
    for peer in range(1, devices):
        tops = jnp.maximum(tops, got[peer * 8 : peer * 8 + 8, begin : begin + LANES])
    delta = (COURANT * SPACING) / tops[TOP : TOP + 1, :]
    delta = jnp.concatenate([delta, delta], 1)
    delta_keep[...] = jnp.broadcast_to(delta, (8, TILE))
    outgoing = start_all(((delta_keep, delta_out),), sems, 5 * PARTS + 3)
    fix = column_fix(got, ground, columns)
    facing = jnp.where(upper > 0, ctl[SLOT_LOW], 1 - ctl[SLOT_LOW])
    begin = pl.multiple_of((1 - upper) * LANES, LANES)
    target = (1 - upper) * (LANES - 1)
    lane = lax.broadcasted_iota(jnp.int32, (size, LANES), 1)
    total = jnp.zeros((ROWS, TILE), jnp.float32)
    for index, (slot, part_rows) in enumerate(parts):
        wait_all(incoming[index])
        if part_rows.start == 0:
            correct_rows(ctl, slot, got, ground, state, rate, True)
        if part_rows.stop == TILE:
            correct_rows(ctl, slot, got, ground, state, rate, False)

        @pl.when(facing == slot)
        def _(slot=slot, part_rows=part_rows):
            for field in range(3):
                turned = pltpu.roll(
                    fix[part_rows], lax.rem(target + LANES - field, LANES), 1
                )
                rate[slot, field, part_rows, pl.ds(begin, LANES)] += jnp.where(
                    lane == target, turned, 0.0
                )

        wet_now = flag(ctl, WET + 2 * step + slot)

        def group(index, best, slot=slot, wet_now=wet_now):
            rows = pl.ds(pl.multiple_of(index * ROWS, ROWS), ROWS)
            old = tuple(state[slot, field, rows, :] for field in range(3))
            slopes = tuple(rate[slot, field, rows, :] for field in range(3))
            h, hu, hv = moved_on(old, slopes, manning[slot, rows, :], delta, wet_now)
            fresh[slot, 0, rows, :] = h
            fresh[slot, 1, rows, :] = hu
            fresh[slot, 2, rows, :] = hv
            if more:
                along_x, along_y = cell(h, hu, hv)
                best = jnp.maximum(best, jnp.maximum(along_x[5], along_y[5]))
            return best

        best = lax.fori_loop(
            part_rows.start // ROWS,
            part_rows.stop // ROWS,
            group,
            jnp.zeros((ROWS, TILE), jnp.float32),
        )
        if more:
            best = jnp.where(flag(ctl, WET + 2 * step + 2 + slot), best, 0.0)
            total = jnp.maximum(total, best)
        outgoing += start_all(
            ((fresh.at[slot, :, part_rows], fresh_out.at[slot, :, part_rows]),),
            sems,
            3 * PARTS + index,
        )
    if more:
        messages(ctl, fresh, None, jnp.max(total, keepdims=True), out, columns_out)
        outgoing += start_all(((out, first_out), (columns_out, second_out)), sems, 4 * PARTS)
    else:
        late_rows(fresh.at[ctl[MOVE]], late_first)
        outgoing += start_all(((late_first, first_out),), sems, 4 * PARTS)
        late_rows(fresh.at[1 - ctl[MOVE]], late_second)
        outgoing += start_all(((late_second, second_out),), sems, 4 * PARTS + 1)
    wait_all(outgoing)


def vmem():
    return pl.BlockSpec(memory_space=pltpu.VMEM)


def smem():
    return pl.BlockSpec(memory_space=pltpu.SMEM)


def hbm():
    return pl.BlockSpec(memory_space=pltpu.HBM)


def anywhere():
    return pl.BlockSpec(memory_space=pl.ANY)


def call(
    kernel, outs, out_specs, in_specs, flops, scratch=(), aliases=None, room=VMEM_BYTES, moved=4
):
    return pl.pallas_call(
        kernel,
        scratch_shapes=scratch,
        input_output_aliases=aliases or {},
        out_shape=outs,
        in_specs=in_specs,
        out_specs=out_specs,
        compiler_params=pltpu.CompilerParams(vmem_limit_bytes=room),
        cost_estimate=pl.CostEstimate(flops=flops, bytes_accessed=moved << 20, transcendentals=0),
    )


def f32(*shape):
    return jax.ShapeDtypeStruct(shape, jnp.float32)


def spread(fast):
    return lax.all_to_all(fast, ("xb", "yb"), split_axis=0, concat_axis=0, tiled=True)


def body(state, bed, manning, neighbours, wet, moves):
    shape = f32(*state.shape)
    devices = lax.axis_size("xb") * lax.axis_size("yb")
    whole = pltpu.VMEM(state.shape, jnp.float32)
    part = pltpu.VMEM(bed.shape, jnp.float32)
    tile_shape = f32(*state.shape[1:])
    early_shape = f32(5, EARLY, TILE)
    early_state = f32(3, EARLY, TILE)
    late_shape = f32(3, LATE, TILE)
    delta_shape = f32(8, TILE)

    def buffer(like):
        return pltpu.VMEM(like.shape, jnp.float32)

    piece_shapes = tuple(f32(5, end - begin, TILE) for begin, end in PIECES)
    out, columns, ctl, *leaving = call(
        opening,
        (
            f32(8 * devices, TILE + LANES),
            f32(8, TILE),
            jax.ShapeDtypeStruct((CONTROLS,), jnp.int32),
        )
        + piece_shapes,
        (vmem(), vmem(), smem(), hbm(), hbm()),
        [hbm()] * 6,
        4 << 20,
        [
            whole,
            part,
            pltpu.VMEM((EARLY, TILE), jnp.float32),
            pltpu.SMEM(neighbours.shape[::-1], jnp.int32),
            pltpu.SMEM(wet.shape, jnp.int32),
            pltpu.SMEM(moves.shape, jnp.int32),
            pltpu.SemaphoreType.DMA((13,)),
        ],
    )(state, bed, manning, neighbours.T, wet, moves)
    state_first = state
    ground = None
    deltas = []
    for step in range(STEPS):
        got = spread(out)
        ground = got if step == 0 else ground
        scratch = [whole, part, whole, pltpu.SemaphoreType.DMA((3 * CHUNKS,))]
        if step == 0:
            rate = call(rates, shape, hbm(), [smem(), hbm(), hbm()], 0, scratch, moved=0)(
                ctl, state, bed
            )
            leaving[1] = call(
                hold, piece_shapes[1], hbm(), [hbm(), hbm()], 1 << 10, aliases={1: 0}
            )(rate, leaving[1])
            early_first = [shifted(piece, "xb", 1) for piece in leaving]
        elif step == 1:
            rate, *leaving = call(
                rates_and_leaving,
                (shape,) + piece_shapes,
                (hbm(),) * 3,
                [smem()] + [hbm()] * 6,
                16 << 20,
                scratch + [buffer(early_shape), pltpu.SemaphoreType.DMA((3,))],
            )(ctl, state, bed, state_first, manning, *early_first)
            early_second = [shifted(piece, "xb", 1) for piece in leaving]
        else:
            rate = call(rates_after, shape, hbm(), [smem()] + [hbm()] * 3, 16 << 20, scratch)(
                ctl, state, bed, early_second[0]
            )
        more = step + 1 < STEPS
        if more:
            shapes = f32(8 * devices, TILE), f32(8, TILE)
        else:
            shapes = late_shape, late_shape
        outs = call(
            functools.partial(update, step),
            (shape,) + shapes + (delta_shape,),
            (hbm(),) * 4,
            [smem()] + [hbm()] * 6,
            8 << 20,
            [
                whole,
                part,
                whole,
                whole,
                pltpu.VMEM(got.shape, jnp.float32),
                pltpu.VMEM(ground.shape, jnp.float32),
                pltpu.VMEM((8, TILE), jnp.float32),
                buffer(shapes[0]),
                buffer(shapes[1]),
                buffer(delta_shape),
                pltpu.SemaphoreType.DMA((5 * PARTS + 4,)),
            ],
            moved=14 if step == 0 else 10,
        )(ctl, got, ground, columns, state, manning, rate)
        deltas.append(outs[-1])
        state, out, columns, _ = outs
    late_first, late_second = out, columns
    room = 16 << 20
    late_arrived = shifted(late_first, "xb", 1)
    second, late_second = call(
        repeat_second,
        (early_state, late_shape),
        (anywhere(), vmem()),
        [smem()] + [vmem()] * 3 + [anywhere()] * 3,
        8 << 20,
        [buffer(early_shape), buffer(early_state), pltpu.SemaphoreType.DMA((3,))],
        room=room,
    )(ctl, *deltas, *early_second, late_second)
    leaving = call(
        second_late,
        late_shape,
        vmem(),
        [smem(), vmem(), vmem(), anywhere()],
        1 << 10,
        room=room,
    )(ctl, late_arrived, late_second, second)
    late_next = shifted(leaving, "xb", 1)
    final = call(
        repeat_first,
        shape,
        hbm(),
        [smem()] + [vmem()] * 3 + [anywhere()] * 4,
        8 << 20,
        [
            buffer(early_shape),
            buffer(early_state),
            buffer(tile_shape),
            buffer(late_shape),
            pltpu.SemaphoreType.DMA((3,)),
        ],
        room=room,
    )(ctl, *deltas, *early_first, late_arrived, state)
    return call(
        finish,
        shape,
        hbm(),
        [smem(), vmem(), vmem(), hbm()],
        1 << 20,
        [buffer(tile_shape), pltpu.SemaphoreType.DMA((3,))],
        {3: 0},
        room=room,
    )(ctl, late_next, second, final)


def solution(mesh):
    placed = (
        P(("runs", "xb", "yb"), None, None, None),
        P(("runs", "xb", "yb"), None, None),
        P(("runs", "xb", "yb"), None, None),
        P("runs", None),
        P(None, "runs"),
        P(None, "runs"),
    )
    return jax.shard_map(
        body,
        mesh=mesh,
        in_specs=placed,
        out_specs=P(("runs", "xb", "yb"), None, None, None),
        check_vma=False,
    )
```

```python
import functools

import jax
import jax.numpy as jnp
from jax import lax
from jax.experimental import pallas as pl
from jax.experimental.pallas import tpu as pltpu
from jax.sharding import PartitionSpec as P

STEPS = 3
GRAVITY = 9.81
ROOT_G = GRAVITY**0.5
SPACING = 5.0
COURANT = 0.2
ROWS = 32
LANES = 128
TILE = 256
VMEM_BYTES = 60 * 1024 * 1024
SLOT_LOW, WALL_WEST, WALL_EAST, WALL_OUTER, WET, MOVE = 0, 1, 3, 5, 7, 13
WET_FIRST, WET_SECOND = 16, 19
CONTROLS = 24
EARLY = 144
PIECES = ((0, 80), (80, 144))
AGAIN = 16
LATE = TILE - EARLY + 16
CHUNKS = 8
PARTS = 8
STRIP = 16
TOP = 6
SCALE = 0.5 / SPACING
SLOPE = GRAVITY / (2.0 * SPACING)


def shifted(value, axis, steps, around=True):
    count = lax.axis_size(axis)
    pairs = [(source, (source + steps) % count) for source in range(count)]
    if not around:
        pairs = [pair for pair in pairs if abs(pair[0] - pair[1]) == abs(steps)]
    return lax.ppermute(value, axis, pairs)


def cell(h, hu, hv):
    root = lax.rsqrt(h)
    inverse = root * root
    u = hu * inverse
    v = hv * inverse
    celerity = ROOT_G * (h * root)
    pressure = (0.5 * GRAVITY) * (h * h)
    cross = hu * v
    speed_x = jnp.abs(u) + celerity
    speed_y = jnp.abs(v) + celerity
    along_x = (h, hu, hv, hu * u + pressure, cross, speed_x)
    along_y = (h, hv, hu, hv * v + pressure, cross, speed_y)
    return along_x, along_y


def face(left, right):
    wave = jnp.maximum(left[5], right[5])
    return (
        (left[1] + right[1]) - wave * (right[0] - left[0]),
        (left[3] + right[3]) - wave * (right[1] - left[1]),
        (left[4] + right[4]) - wave * (right[2] - left[2]),
    )


def slot_of(ctl, position):
    low = ctl[SLOT_LOW]
    return low if position == 0 else 1 - low


def flag(ctl, index):
    return ctl[index] > 0


def start_all(pairs, sems, first=0):
    copies = [
        pltpu.make_async_copy(src, dst, sems.at[first + k]) for k, (src, dst) in enumerate(pairs)
    ]
    for copy in copies:
        copy.start()
    return copies


def wait_all(copies):
    for copy in copies:
        copy.wait()


def sublanes(width=TILE):
    return lax.broadcasted_iota(jnp.int32, (8, width), 0)


def stacked(lines, base):
    row = sublanes()
    for index, line in enumerate(lines):
        base = jnp.where(row == index, jnp.broadcast_to(line, (8, TILE)), base)
    return base


def messages(ctl, state, bed, fastest, out, columns):
    upper = lax.axis_index("yb")
    column = lax.axis_index("xb")
    last = lax.axis_size("xb") - 1
    devices = 2 * (last + 1)
    device = column * 2 + upper
    top = jnp.broadcast_to(fastest, (8, TILE))
    for peer in range(devices):
        out[peer * 8 : peer * 8 + 8, :TILE] = top
        if bed is not None:
            out[peer * 8 : peer * 8 + 8, TILE:] = top[:, :LANES]
    row = sublanes()

    def edge(line):
        rows = slice(line, line + 1)
        lines = []
        for position in range(2):
            slot = slot_of(ctl, position)
            lines += [state[slot, field, rows, :] for field in range(3)]
            if bed is not None:
                lines.append(bed[slot, rows, :])
        return stacked(lines, top)

    for inside, peer, line in (
        (column > 0, device - 2, 0),
        (column < last, device + 2, TILE - 1),
    ):

        @pl.when(inside)
        def _(peer=peer, line=line):
            out[pl.ds(pl.multiple_of(peer * 8, 8), 8), :TILE] = edge(line)

    slot = jnp.where(upper > 0, ctl[SLOT_LOW], 1 - ctl[SLOT_LOW])
    begin = pl.multiple_of((1 - upper) * LANES, LANES)
    lane = lax.broadcasted_iota(jnp.int32, (TILE, LANES), 1)
    packed = None
    for field in range(4 if bed is not None else 3):
        if field < 3:
            part = state[slot, field, :, pl.ds(begin, LANES)]
        else:
            part = bed[slot, :, pl.ds(begin, LANES)]
        turned = pltpu.roll(part, field + 1 - upper, 1)
        packed = turned if field == 0 else jnp.where(lane == field, turned, packed)
    lines = jnp.transpose(packed)[:8]
    columns[...] = lines
    start = pl.multiple_of((device + 1 - 2 * upper) * 8, 8)
    out[pl.ds(start, 8), :TILE] = jnp.where(row == TOP, top, lines)


def opening(
    state_in, bed_in, manning_in, neighbours_in, wet_in, moves_in,
    out, columns, ctl, leaving_low, leaving_high,
    state, bed, manning, neighbours, wet, moves, sems,
):
    copies = start_all(
        (
            (neighbours_in, neighbours),
            (wet_in, wet),
            (moves_in, moves),
            (state_in.at[0], state.at[0]),
            (state_in.at[1], state.at[1]),
            (bed_in, bed),
        ),
        sems,
    )
    device = lax.axis_index("xb") * 2 + lax.axis_index("yb")
    wait_all(copies[:3])
    first = device * 2
    low = jnp.where(neighbours[3, first] == first + 1, 0, 1)
    ctl[SLOT_LOW] = low
    for position in range(2):
        slot = low if position == 0 else 1 - low
        tile = first + slot
        ctl[WALL_WEST + position] = (neighbours[0, tile] < 0).astype(jnp.int32)
        ctl[WALL_EAST + position] = (neighbours[1, tile] < 0).astype(jnp.int32)
        ctl[WALL_OUTER + position] = (neighbours[2 + position, tile] < 0).astype(jnp.int32)
    for step in range(STEPS):
        for slot in range(2):
            ctl[WET + 2 * step + slot] = wet[step, first + slot]
        ctl[MOVE + step] = moves[step, device]
    moving = moves[0, device]
    rough = start_all(((manning_in.at[moving, 0:EARLY], manning),), sems, 6)
    count = lax.axis_size("xb")
    upper = lax.axis_index("yb")
    column = lax.axis_index("xb")
    source = lax.rem(column + count - 1, count) * 2 + upper
    before = lax.rem(column + count - 2, count) * 2 + upper
    again = moves[0, source] == moves[1, source]
    tile_first = source * 2 + moves[0, source]
    tile_second = jnp.where(
        again, before * 2 + moves[0, before], source * 2 + 1 - moves[0, source]
    )
    for step in range(STEPS):
        ctl[WET_FIRST + step] = wet[step, tile_first]
        ctl[WET_SECOND + step] = wet[step, tile_second]

    wait_all(copies[3:] + rough)
    early = []
    for (begin, end), leaving in zip(PIECES, (leaving_low, leaving_high)):
        early += start_all(
            (
                (state.at[moving, :, begin:end], leaving.at[0:3]),
                (bed.at[moving, begin:end], leaving.at[3]),
                (manning.at[begin:end], leaving.at[4]),
            ),
            sems,
            7 + len(early),
        )
    total = jnp.zeros((ROWS, TILE), jnp.float32)
    for slot in range(2):

        def group(index, best, slot=slot):
            rows = pl.ds(pl.multiple_of(index * ROWS, ROWS), ROWS)
            along_x, along_y = cell(*(state[slot, field, rows, :] for field in range(3)))
            return jnp.maximum(best, jnp.maximum(along_x[5], along_y[5]))

        best = lax.fori_loop(0, TILE // ROWS, group, jnp.zeros((ROWS, TILE), jnp.float32))
        total = jnp.maximum(total, jnp.where(wet[0, first + slot] > 0, best, 0.0))
    messages(ctl, state, bed, jnp.max(total, keepdims=True), out, columns)
    wait_all(early)


def hold(order, leaving, same):
    del order, leaving, same


class Passing:
    def __init__(self, ctl, state_in, bed_in, manning_in, arrived, leaving, buffer, sems):
        self.again = ctl[MOVE] == ctl[MOVE + 1]
        self.other = 1 - ctl[MOVE]
        self.refs = state_in, bed_in, manning_in, arrived, buffer, sems
        self.outgoing = [
            pltpu.make_async_copy(buffer.at[:, begin:end], piece, sems.at[1 + index])
            for index, ((begin, end), piece) in enumerate(zip(PIECES, leaving))
        ]

    def start(self):
        state_in, bed_in, manning_in, arrived, buffer, sems = self.refs
        rows = slice(0, EARLY)
        sem = sems.at[0]

        @pl.when(self.again)
        def _():
            for (begin, end), piece in zip(PIECES, arrived):
                pltpu.make_async_copy(piece, buffer.at[:, begin:end], sem).start()

        @pl.when(jnp.logical_not(self.again))
        def _():
            pltpu.make_async_copy(state_in.at[self.other, :, rows], buffer.at[0:3], sem).start()
            pltpu.make_async_copy(bed_in.at[self.other, rows], buffer.at[3], sem).start()
            pltpu.make_async_copy(manning_in.at[self.other, rows], buffer.at[4], sem).start()

    def middle(self):
        _, _, _, arrived, buffer, sems = self.refs
        for (begin, end), piece in zip(PIECES, arrived):
            pltpu.make_async_copy(piece, buffer.at[:, begin:end], sems.at[0]).wait()
        for copy in self.outgoing:
            copy.start()

    def end(self):
        wait_all(self.outgoing)


def rates_and_leaving(
    ctl, state_in, bed_in, state_first, manning_in, arrived_low, arrived_high,
    rate_out, leaving_low, leaving_high,
    state, bed, rate, sems, buffer, moving,
):
    arrived = arrived_low, arrived_high
    passing = Passing(
        ctl, state_first, bed_in, manning_in, arrived, (leaving_low, leaving_high), buffer, moving
    )
    rates(ctl, state_in, bed_in, rate_out, state, bed, rate, sems, passing)


def rates_after(ctl, state_in, bed_in, order, *rest):
    del order
    rates(ctl, state_in, bed_in, *rest)


def rates(ctl, state_in, bed_in, rate_out, state, bed, rate, sems, passing=None):
    width = 2 * TILE
    row_ids = lax.broadcasted_iota(jnp.int32, (STRIP, width), 0)
    row8 = sublanes(width)
    lane = lax.broadcasted_iota(jnp.int32, (STRIP, LANES), 1)
    last = TILE // STRIP - 1
    chunk = TILE // CHUNKS
    slots = [slot_of(ctl, position) for position in range(2)]
    incoming = []
    for part in range(CHUNKS):
        rows = slice(part * chunk, (part + 1) * chunk)
        incoming.append(
            start_all(
                (
                    (state_in.at[:, :, rows], state.at[:, :, rows]),
                    (bed_in.at[:, rows], bed.at[:, rows]),
                ),
                sems,
                2 * part,
            )
        )
    if passing:
        passing.start()
    keep_west, keep_east, keep_south, keep_north = (
        jnp.where(flag(ctl, index), 1.0, 0.0)
        for index in (WALL_WEST, WALL_EAST, WALL_OUTER, WALL_OUTER + 1)
    )

    def strip(field, rows):
        if field == 3:
            return jnp.concatenate([bed[slot, rows, :] for slot in slots], 1)
        return jnp.concatenate([state[slot, field, rows, :] for slot in slots], 1)

    def blocks(value):
        return [value[:, k * LANES : (k + 1) * LANES] for k in range(4)]

    def right_of(value, end=None):
        turned = [pltpu.roll(part, LANES - 1, 1) for part in blocks(value)]
        after = turned[1:] + [turned[3] if end is None else end]
        return jnp.concatenate(
            [
                jnp.where(lane == LANES - 1, following, part)
                if following is not part
                else part
                for part, following in zip(turned, after)
            ],
            1,
        )

    def left_of(value, end):
        turned = [pltpu.roll(part, 1, 1) for part in blocks(value)]
        before = [end] + turned[:3]
        return jnp.concatenate(
            [jnp.where(lane == 0, previous, part) for part, previous in zip(turned, before)], 1
        )

    def down(value):
        return pltpu.roll(value, STRIP + 7, 0)[:STRIP]

    def group(index, carry):
        base = pl.multiple_of(index * STRIP, STRIP)
        rows = pl.ds(base, STRIP)
        after = pl.ds(pl.multiple_of(jnp.minimum(base + STRIP, TILE - 8), 8), 8)
        at_end = index == last
        fields = [
            jnp.concatenate([strip(field, rows), strip(field, after)], 0) for field in range(3)
        ]
        cells_x, cells_y = cell(*fields)
        here_x = tuple(value[:STRIP] for value in cells_x)
        here_y = tuple(value[:STRIP] for value in cells_y)

        ending = jnp.logical_and(row8 == 7, at_end)
        faces = list(face(here_x, tuple(down(value) for value in cells_x)))
        wall = keep_east * (2.0 * (here_x[3] + here_x[5] * here_x[1])[STRIP - 8 :])
        for component, value in enumerate((0.0, wall, 0.0)):
            upper = faces[component]
            faces[component] = jnp.concatenate(
                [upper[: STRIP - 8], jnp.where(ending, value, upper[STRIP - 8 :])], 0
            )
        turned = tuple(pltpu.roll(value, 1, 0) for value in faces)
        change_x = tuple(
            value - jnp.where(row_ids == 0, before, moved)
            for value, before, moved in zip(faces, carry[:3], turned)
        )
        ground = strip(3, rows)
        ground_after = jnp.where(
            at_end,
            jnp.broadcast_to(keep_east * ground[STRIP - 1 :], (8, width)),
            strip(3, after),
        )
        ground_up = pltpu.roll(ground, 1, 0)
        slope_x = down(jnp.concatenate([ground, ground_after], 0)) - jnp.where(
            row_ids == 0, carry[3], ground_up
        )
        carried = tuple(value[0:1, :] for value in turned) + (ground_up[0:1, :],)

        faces_y = list(face(here_y, tuple(right_of(value) for value in here_y)))
        normal = here_y[3]
        spread_y = here_y[5] * here_y[1]
        north = keep_north * (2.0 * (normal + spread_y)[:, width - LANES :])
        south = keep_south * (2.0 * (normal - spread_y)[:, :LANES])
        change_y = []
        for component, (high, low) in enumerate(((0.0, 0.0), (north, south), (0.0, 0.0))):
            parts = blocks(faces_y[component])
            parts[3] = jnp.where(lane == LANES - 1, high, parts[3])
            value = jnp.concatenate(parts, 1)
            change_y.append(value - left_of(value, low))
        slope_y = right_of(ground, keep_north * ground[:, width - LANES :]) - left_of(
            ground, keep_south * ground[:, :LANES]
        )
        weight = SLOPE * here_x[0]
        results = (
            SCALE * (change_x[0] + change_y[0]),
            SCALE * (change_x[1] + change_y[2]) + weight * slope_x,
            SCALE * (change_x[2] + change_y[1]) + weight * slope_y,
        )
        for field, value in enumerate(results):
            for position, slot in enumerate(slots):
                rate[slot, field, rows, :] = value[:, position * TILE : (position + 1) * TILE]
        return carried

    wait_all(incoming[0])
    top, _ = cell(*(strip(field, slice(0, 8)) for field in range(3)))
    nothing = jnp.zeros((1, width), jnp.float32)
    carry = (
        nothing,
        keep_west * (2.0 * (top[3] - top[5] * top[1])[0:1]),
        nothing,
        keep_west * strip(3, slice(0, 8))[0:1],
    )
    per_chunk = chunk // STRIP
    outgoing = []
    for part in range(CHUNKS):
        if part + 1 < CHUNKS:
            wait_all(incoming[part + 1])
        carry = lax.fori_loop(part * per_chunk, (part + 1) * per_chunk, group, carry)
        rows = slice(part * chunk, (part + 1) * chunk)
        outgoing += start_all(
            ((rate.at[:, :, rows], rate_out.at[:, :, rows]),), sems, 2 * CHUNKS + part
        )
        if passing and part == CHUNKS // 2:
            passing.middle()
    wait_all(outgoing)
    if passing:
        passing.end()


def moved_on(old, slopes, rough, delta, wet_now):
    h, hu, hv = (value - delta * slope for value, slope in zip(old, slopes))
    inverse = 1.0 / h
    u = hu * inverse
    v = hv * inverse
    speed = jnp.sqrt(u * u + v * v)
    power = jnp.exp((-4.0 / 3.0) * jnp.log(jnp.abs(h)))
    drag = (GRAVITY * delta) * (rough * rough) * (speed * power)
    factor = 1.0 / (1.0 + drag)
    fresh = (h, hu * factor, hv * factor)
    return tuple(jnp.where(wet_now, new, value) for new, value in zip(fresh, old))


def repeat_steps(ctl, wet_from, deltas, early, work, other, sems):
    incoming = []
    for ref in early:
        begin = 0 if ref is early[0] else early[0].shape[1]
        incoming += start_all(
            ((ref, work.at[:, begin : begin + ref.shape[1]]),), sems, len(incoming)
        )
    row_ids = lax.broadcasted_iota(jnp.int32, (AGAIN, TILE), 0)
    lane = lax.broadcasted_iota(jnp.int32, (AGAIN, LANES), 1)
    start = tuple(jnp.zeros((1, TILE), jnp.float32) for _ in range(4))

    def halves(value):
        return value[:, :LANES], value[:, LANES:]

    def right_of(value):
        low, high = (pltpu.roll(part, LANES - 1, 1) for part in halves(value))
        return jnp.concatenate([jnp.where(lane == LANES - 1, high, low), high], 1)

    def left_of(value):
        low, high = (pltpu.roll(part, 1, 1) for part in halves(value))
        return jnp.concatenate([low, jnp.where(lane == 0, low, high)], 1)

    def down(value):
        return pltpu.roll(value, AGAIN + 7, 0)[:AGAIN]

    for step in range(STEPS):
        source, target = (work, other) if step % 2 == 0 else (other, work)
        delta = deltas[step][0:1, :]
        wet_now = flag(ctl, wet_from + step)

        def group(index, carry, source=source, target=target, delta=delta, wet_now=wet_now):
            base = pl.multiple_of(index * AGAIN, AGAIN)
            rows = pl.ds(base, AGAIN)
            after = pl.ds(pl.multiple_of(jnp.minimum(base + AGAIN, EARLY - 8), 8), 8)
            refs = [source.at[field] for field in range(3)] + [work.at[3]]
            fields = [jnp.concatenate([ref[rows, :], ref[after, :]], 0) for ref in refs]
            cells_x, cells_y = cell(*fields[:3])
            here_x = tuple(value[:AGAIN] for value in cells_x)
            here_y = tuple(value[:AGAIN] for value in cells_y)
            faces_x = face(here_x, tuple(down(value) for value in cells_x))
            turned = tuple(pltpu.roll(value, 1, 0) for value in faces_x)
            change_x = tuple(
                value - jnp.where(row_ids == 0, before, moved)
                for value, before, moved in zip(faces_x, carry[:3], turned)
            )
            ground = fields[3][:AGAIN]
            ground_up = pltpu.roll(ground, 1, 0)
            slope_x = down(fields[3]) - jnp.where(row_ids == 0, carry[3], ground_up)
            carried = tuple(value[0:1, :] for value in turned) + (ground_up[0:1, :],)
            faces_y = face(here_y, tuple(right_of(value) for value in here_y))
            change_y = tuple(value - left_of(value) for value in faces_y)
            slope_y = right_of(ground) - left_of(ground)
            old = tuple(value[:AGAIN] for value in fields[:3])
            weight = SLOPE * old[0]
            slopes = (
                SCALE * (change_x[0] + change_y[0]),
                SCALE * (change_x[1] + change_y[2]) + weight * slope_x,
                SCALE * (change_x[2] + change_y[1]) + weight * slope_y,
            )
            for field, value in enumerate(
                moved_on(old, slopes, work[4, rows, :], delta, wet_now)
            ):
                target[field, rows, :] = value
            return carried

        if step == 0:
            wait_all(incoming)
        lax.fori_loop(0, EARLY // AGAIN, group, start)


def late_rows(tile, late):
    row = sublanes()
    kept = EARLY - 8
    lane = lax.broadcasted_iota(jnp.int32, (8, LANES), 1)
    for field in range(3):
        late[field, 0:8, :] = jnp.where(
            row < 3, tile[field, 0:8, :], tile[field, kept : kept + 8, :]
        )
        packed = [jnp.zeros((8, LANES), jnp.float32)] * 2
        for block in range(EARLY // 8):
            rows = slice(8 * block, 8 * block + 8)
            sides = jnp.where(lane < 64, tile[field, rows, :LANES], tile[field, rows, LANES:])
            turned = pltpu.roll(sides, (3 + 8 * block) % LANES, 1)
            which = block // 16
            packed[which] = jnp.where(lane // 8 == block % 16, turned, packed[which])
        late[field, 8:16, :] = jnp.concatenate(packed, 1)
        late[field, 16:, :] = tile[field, EARLY:, :]


def merge(late, early, tile):
    for field in range(3):
        merge_field(field, late, early, tile)


def merge_field(field, late, early, tile):
    row = sublanes()
    lane = lax.broadcasted_iota(jnp.int32, (8, LANES), 1)
    first = late[field, 0:8, :]
    for block in range(EARLY // 8):
        rows = slice(8 * block, 8 * block + 8)
        which = block // 16
        packed = late[field, 8:16, which * LANES : (which + 1) * LANES]
        sides = pltpu.roll(packed, (-3 - 8 * block) % LANES, 1)
        value = early[field, rows, :]
        value = jnp.concatenate(
            [
                jnp.where(lane < 3, sides, value[:, :LANES]),
                jnp.where(lane >= LANES - 3, sides, value[:, LANES:]),
            ],
            1,
        )
        if block == 0:
            value = jnp.where(row < 3, first, value)
        if block == EARLY // 8 - 1:
            value = jnp.where(row < 5, value, first)
        tile[field, rows, :] = value
    tile[field, EARLY:, :] = late[field, 16:, :]


def repeat_second(ctl, delta0, delta1, delta2, low, high, late, out, late_out, work, tile, sems):
    near = start_all(((late, late_out),), sems, 2)
    repeat_steps(ctl, WET_SECOND, (delta0, delta1, delta2), (low, high), work, tile, sems)
    wait_all(start_all(((tile, out),), sems) + near)


def repeat_first(
    ctl, delta0, delta1, delta2, low, high, late_in, state, out, work, other, tile, late, sems
):
    rest = out.at[1 - ctl[MOVE + 1]]
    again = ctl[MOVE] == ctl[MOVE + 1]

    @pl.when(again)
    def _():
        wait_all(start_all(((state.at[1 - ctl[MOVE]], tile),), sems))

    @pl.when(jnp.logical_not(again))
    def _():
        copies = start_all(((late_in, late),), sems, 2)
        repeat_steps(ctl, WET_FIRST, (delta0, delta1, delta2), (low, high), work, other, sems)
        wait_all(copies)
        merge(late, other, tile)

    wait_all(start_all(((tile, rest),), sems))


def finish(ctl, late, early, before, out, tile, sems):
    del before
    copies = []
    for field in range(3):
        merge_field(field, late, early, tile)
        copies += start_all(
            ((tile.at[field], out.at[ctl[MOVE + 1], field]),), sems, field
        )
    wait_all(copies)


def second_late(ctl, arrived, own, order, leaving):
    del order
    again = ctl[MOVE] == ctl[MOVE + 1]
    for field in range(3):
        leaving[field] = jnp.where(again, arrived[field], own[field])


def correct_rows(ctl, slot, got, ground, state, rate, bottom):
    position = jnp.where(ctl[SLOT_LOW] == slot, 0, 1)
    device = lax.axis_index("xb") * 2 + lax.axis_index("yb")
    wall = WALL_WEST if bottom else WALL_EAST

    @pl.when(jnp.logical_not(flag(ctl, wall + position)))
    def _():
        peer = device - 2 if bottom else device + 2
        block = pl.ds(pl.multiple_of(peer * 8, 8), 8)
        lines = got[block, :TILE]
        grounds = ground[block, :TILE]
        stride = 4 if got.shape[1] > TILE else 3

        def line(offset):
            other = offset + stride
            picked = jnp.where(
                position == 0, lines[offset : offset + 1, :], lines[other : other + 1, :]
            )
            return jnp.broadcast_to(picked, (8, TILE))

        ghost, _ = cell(*(line(field) for field in range(3)))
        ghost_ground = jnp.where(position == 0, grounds[3:4, :], grounds[7:8, :])
        rows = slice(0, 8) if bottom else slice(TILE - 8, TILE)
        own = [state[slot, field, rows, :] for field in range(3)]
        here, _ = cell(*own)
        fluxes = face(ghost, here) if bottom else face(here, ghost)
        push = SCALE * fluxes[1] + (SLOPE * own[0]) * ghost_ground
        row = sublanes()
        sign = -1.0 if bottom else 1.0
        chosen = row == (0 if bottom else 7)
        for field, value in enumerate((SCALE * fluxes[0], push, SCALE * fluxes[2])):
            rate[slot, field, rows, :] += jnp.where(chosen, sign * value, 0.0)


def column_fix(got, ground, columns):
    upper = lax.axis_index("yb")
    device = lax.axis_index("xb") * 2 + upper
    peer = device + 1 - 2 * upper
    block = pl.ds(pl.multiple_of(peer * 8, 8), 8)
    lines = got[block, :TILE]
    ghost_ground = ground[block, :TILE][3:4]
    mine = columns[...]
    _, ghost = cell(lines[0:1], lines[1:2], lines[2:3])
    _, own = cell(mine[0:1], mine[1:2], mine[2:3])
    low = upper == 0
    left = tuple(jnp.where(low, a, b) for a, b in zip(own, ghost))
    right = tuple(jnp.where(low, b, a) for a, b in zip(own, ghost))
    fluxes = face(left, right)
    sign = jnp.where(low, 1.0, -1.0)
    push = SCALE * fluxes[1] + (SLOPE * mine[0:1]) * ghost_ground
    block8 = stacked(
        [sign * SCALE * fluxes[0], sign * SCALE * fluxes[2], sign * push],
        jnp.zeros((8, TILE), jnp.float32),
    )
    return jnp.transpose(
        jnp.concatenate([block8, jnp.zeros((LANES - 8, TILE), jnp.float32)], 0)
    )


def update(step, ctl, got_in, ground_in, columns_in, state_in, manning_in, rate_in, *rest):
    more = step + 1 < STEPS
    fresh_out, first_out, second_out, delta_out = rest[:4]
    rest = rest[4:]
    state, manning, rate, fresh, got, ground, columns, first, second, delta_keep, sems = rest
    out, columns_out = late_first, late_second = first, second
    small = start_all(
        ((got_in, got), (ground_in, ground), (columns_in, columns)), sems, 5 * PARTS
    )
    size = 2 * TILE // PARTS
    parts = [
        (slot, slice(k * size, (k + 1) * size)) for slot in range(2) for k in range(PARTS // 2)
    ]
    incoming = []
    for index, (slot, rows) in enumerate(parts):
        incoming.append(
            start_all(
                (
                    (rate_in.at[slot, :, rows], rate.at[slot, :, rows]),
                    (state_in.at[slot, :, rows], state.at[slot, :, rows]),
                    (manning_in.at[slot, rows], manning.at[slot, rows]),
                ),
                sems,
                3 * index,
            )
        )
    wait_all(small)
    upper = lax.axis_index("yb")
    devices = 2 * lax.axis_size("xb")
    begin = TILE if got.shape[1] > TILE else 0
    tops = got[0:8, begin : begin + LANES]
    for peer in range(1, devices):
        tops = jnp.maximum(tops, got[peer * 8 : peer * 8 + 8, begin : begin + LANES])
    delta = (COURANT * SPACING) / tops[TOP : TOP + 1, :]
    delta = jnp.concatenate([delta, delta], 1)
    delta_keep[...] = jnp.broadcast_to(delta, (8, TILE))
    outgoing = start_all(((delta_keep, delta_out),), sems, 5 * PARTS + 3)
    fix = column_fix(got, ground, columns)
    facing = jnp.where(upper > 0, ctl[SLOT_LOW], 1 - ctl[SLOT_LOW])
    begin = pl.multiple_of((1 - upper) * LANES, LANES)
    target = (1 - upper) * (LANES - 1)
    lane = lax.broadcasted_iota(jnp.int32, (size, LANES), 1)
    total = jnp.zeros((ROWS, TILE), jnp.float32)
    for index, (slot, part_rows) in enumerate(parts):
        wait_all(incoming[index])
        if part_rows.start == 0:
            correct_rows(ctl, slot, got, ground, state, rate, True)
        if part_rows.stop == TILE:
            correct_rows(ctl, slot, got, ground, state, rate, False)

        @pl.when(facing == slot)
        def _(slot=slot, part_rows=part_rows):
            for field in range(3):
                turned = pltpu.roll(
                    fix[part_rows], lax.rem(target + LANES - field, LANES), 1
                )
                rate[slot, field, part_rows, pl.ds(begin, LANES)] += jnp.where(
                    lane == target, turned, 0.0
                )

        wet_now = flag(ctl, WET + 2 * step + slot)

        def group(index, best, slot=slot, wet_now=wet_now):
            rows = pl.ds(pl.multiple_of(index * ROWS, ROWS), ROWS)
            old = tuple(state[slot, field, rows, :] for field in range(3))
            slopes = tuple(rate[slot, field, rows, :] for field in range(3))
            h, hu, hv = moved_on(old, slopes, manning[slot, rows, :], delta, wet_now)
            fresh[slot, 0, rows, :] = h
            fresh[slot, 1, rows, :] = hu
            fresh[slot, 2, rows, :] = hv
            if more:
                along_x, along_y = cell(h, hu, hv)
                best = jnp.maximum(best, jnp.maximum(along_x[5], along_y[5]))
            return best

        best = lax.fori_loop(
            part_rows.start // ROWS,
            part_rows.stop // ROWS,
            group,
            jnp.zeros((ROWS, TILE), jnp.float32),
        )
        if more:
            best = jnp.where(flag(ctl, WET + 2 * step + 2 + slot), best, 0.0)
            total = jnp.maximum(total, best)
        outgoing += start_all(
            ((fresh.at[slot, :, part_rows], fresh_out.at[slot, :, part_rows]),),
            sems,
            3 * PARTS + index,
        )
    if more:
        messages(ctl, fresh, None, jnp.max(total, keepdims=True), out, columns_out)
        outgoing += start_all(((out, first_out), (columns_out, second_out)), sems, 4 * PARTS)
    else:
        late_rows(fresh.at[ctl[MOVE]], late_first)
        outgoing += start_all(((late_first, first_out),), sems, 4 * PARTS)
        late_rows(fresh.at[1 - ctl[MOVE]], late_second)
        outgoing += start_all(((late_second, second_out),), sems, 4 * PARTS + 1)
    wait_all(outgoing)


def vmem():
    return pl.BlockSpec(memory_space=pltpu.VMEM)


def smem():
    return pl.BlockSpec(memory_space=pltpu.SMEM)


def hbm():
    return pl.BlockSpec(memory_space=pltpu.HBM)


def anywhere():
    return pl.BlockSpec(memory_space=pl.ANY)


def call(
    kernel, outs, out_specs, in_specs, flops, scratch=(), aliases=None, room=VMEM_BYTES, moved=4
):
    return pl.pallas_call(
        kernel,
        scratch_shapes=scratch,
        input_output_aliases=aliases or {},
        out_shape=outs,
        in_specs=in_specs,
        out_specs=out_specs,
        compiler_params=pltpu.CompilerParams(vmem_limit_bytes=room),
        cost_estimate=pl.CostEstimate(flops=flops, bytes_accessed=moved << 20, transcendentals=0),
    )


def f32(*shape):
    return jax.ShapeDtypeStruct(shape, jnp.float32)


def spread(fast):
    return lax.all_to_all(fast, ("xb", "yb"), split_axis=0, concat_axis=0, tiled=True)


def body(state, bed, manning, neighbours, wet, moves):
    shape = f32(*state.shape)
    devices = lax.axis_size("xb") * lax.axis_size("yb")
    whole = pltpu.VMEM(state.shape, jnp.float32)
    part = pltpu.VMEM(bed.shape, jnp.float32)
    tile_shape = f32(*state.shape[1:])
    early_shape = f32(5, EARLY, TILE)
    early_state = f32(3, EARLY, TILE)
    late_shape = f32(3, LATE, TILE)
    delta_shape = f32(8, TILE)

    def buffer(like):
        return pltpu.VMEM(like.shape, jnp.float32)

    piece_shapes = tuple(f32(5, end - begin, TILE) for begin, end in PIECES)
    out, columns, ctl, *leaving = call(
        opening,
        (
            f32(8 * devices, TILE + LANES),
            f32(8, TILE),
            jax.ShapeDtypeStruct((CONTROLS,), jnp.int32),
        )
        + piece_shapes,
        (vmem(), vmem(), smem(), hbm(), hbm()),
        [hbm()] * 6,
        4 << 20,
        [
            whole,
            part,
            pltpu.VMEM((EARLY, TILE), jnp.float32),
            pltpu.SMEM(neighbours.shape[::-1], jnp.int32),
            pltpu.SMEM(wet.shape, jnp.int32),
            pltpu.SMEM(moves.shape, jnp.int32),
            pltpu.SemaphoreType.DMA((13,)),
        ],
    )(state, bed, manning, neighbours.T, wet, moves)
    state_first = state
    ground = None
    deltas = []
    for step in range(STEPS):
        got = spread(out)
        ground = got if step == 0 else ground
        scratch = [whole, part, whole, pltpu.SemaphoreType.DMA((3 * CHUNKS,))]
        if step == 0:
            rate = call(rates, shape, hbm(), [smem(), hbm(), hbm()], 0, scratch, moved=0)(
                ctl, state, bed
            )
            leaving[1] = call(
                hold, piece_shapes[1], hbm(), [hbm(), hbm()], 1 << 10, aliases={1: 0}
            )(rate, leaving[1])
            early_first = [shifted(piece, "xb", 1) for piece in leaving]
        elif step == 1:
            rate, *leaving = call(
                rates_and_leaving,
                (shape,) + piece_shapes,
                (hbm(),) * 3,
                [smem()] + [hbm()] * 6,
                16 << 20,
                scratch + [buffer(early_shape), pltpu.SemaphoreType.DMA((3,))],
            )(ctl, state, bed, state_first, manning, *early_first)
            early_second = [shifted(piece, "xb", 1) for piece in leaving]
        else:
            rate = call(rates_after, shape, hbm(), [smem()] + [hbm()] * 3, 16 << 20, scratch)(
                ctl, state, bed, early_second[0]
            )
        more = step + 1 < STEPS
        if more:
            shapes = f32(8 * devices, TILE), f32(8, TILE)
        else:
            shapes = late_shape, late_shape
        outs = call(
            functools.partial(update, step),
            (shape,) + shapes + (delta_shape,),
            (hbm(),) * 4,
            [smem()] + [hbm()] * 6,
            8 << 20,
            [
                whole,
                part,
                whole,
                whole,
                pltpu.VMEM(got.shape, jnp.float32),
                pltpu.VMEM(ground.shape, jnp.float32),
                pltpu.VMEM((8, TILE), jnp.float32),
                buffer(shapes[0]),
                buffer(shapes[1]),
                buffer(delta_shape),
                pltpu.SemaphoreType.DMA((5 * PARTS + 4,)),
            ],
            moved=14 if step == 0 else 10,
        )(ctl, got, ground, columns, state, manning, rate)
        deltas.append(outs[-1])
        state, out, columns, _ = outs
    late_first, late_second = out, columns
    room = 16 << 20
    late_arrived = shifted(late_first, "xb", 1)
    second, late_second = call(
        repeat_second,
        (early_state, late_shape),
        (anywhere(), vmem()),
        [smem()] + [vmem()] * 3 + [anywhere()] * 3,
        8 << 20,
        [buffer(early_shape), buffer(early_state), pltpu.SemaphoreType.DMA((3,))],
        room=room,
    )(ctl, *deltas, *early_second, late_second)
    leaving = call(
        second_late,
        late_shape,
        vmem(),
        [smem(), vmem(), vmem(), anywhere()],
        1 << 10,
        room=room,
    )(ctl, late_arrived, late_second, second)
    late_next = shifted(leaving, "xb", 1)
    final = call(
        repeat_first,
        shape,
        hbm(),
        [smem()] + [vmem()] * 3 + [anywhere()] * 4,
        8 << 20,
        [
            buffer(early_shape),
            buffer(early_state),
            buffer(tile_shape),
            buffer(late_shape),
            pltpu.SemaphoreType.DMA((3,)),
        ],
        room=room,
    )(ctl, *deltas, *early_first, late_arrived, state)
    return call(
        finish,
        shape,
        hbm(),
        [smem(), vmem(), vmem(), hbm()],
        1 << 20,
        [buffer(tile_shape), pltpu.SemaphoreType.DMA((3,))],
        {3: 0},
        room=room,
    )(ctl, late_next, second, final)


def solution(mesh):
    placed = (
        P(("runs", "xb", "yb"), None, None, None),
        P(("runs", "xb", "yb"), None, None),
        P(("runs", "xb", "yb"), None, None),
        P("runs", None),
        P(None, "runs"),
        P(None, "runs"),
    )
    return jax.shard_map(
        body,
        mesh=mesh,
        in_specs=placed,
        out_specs=P(("runs", "xb", "yb"), None, None, None),
        check_vma=False,
    )
```

```python
import functools

import jax
import jax.numpy as jnp
from jax import lax
from jax.experimental import pallas as pl
from jax.experimental.pallas import tpu as pltpu
from jax.sharding import PartitionSpec as P

STEPS = 3
GRAVITY = 9.81
ROOT_G = GRAVITY**0.5
SPACING = 5.0
COURANT = 0.2
ROWS = 32
LANES = 128
TILE = 256
VMEM_BYTES = 60 * 1024 * 1024
SLOT_LOW, WALL_WEST, WALL_EAST, WALL_OUTER, WET, MOVE = 0, 1, 3, 5, 7, 13
WET_FIRST, WET_SECOND = 16, 19
CONTROLS = 24
EARLY = 160
PIECES = ((0, 88), (88, 160))
LATE = TILE - EARLY + 16
CHUNKS = 8
PARTS = 8
STRIP = 16
TOP = 6
SCALE = 0.5 / SPACING
SLOPE = GRAVITY / (2.0 * SPACING)


def shifted(value, axis, steps, around=True):
    count = lax.axis_size(axis)
    pairs = [(source, (source + steps) % count) for source in range(count)]
    if not around:
        pairs = [pair for pair in pairs if abs(pair[0] - pair[1]) == abs(steps)]
    return lax.ppermute(value, axis, pairs)


def cell(h, hu, hv):
    root = lax.rsqrt(h)
    inverse = root * root
    u = hu * inverse
    v = hv * inverse
    celerity = ROOT_G * (h * root)
    pressure = (0.5 * GRAVITY) * (h * h)
    cross = hu * v
    speed_x = jnp.abs(u) + celerity
    speed_y = jnp.abs(v) + celerity
    along_x = (h, hu, hv, hu * u + pressure, cross, speed_x)
    along_y = (h, hv, hu, hv * v + pressure, cross, speed_y)
    return along_x, along_y


def face(left, right):
    wave = jnp.maximum(left[5], right[5])
    return (
        (left[1] + right[1]) - wave * (right[0] - left[0]),
        (left[3] + right[3]) - wave * (right[1] - left[1]),
        (left[4] + right[4]) - wave * (right[2] - left[2]),
    )


def slot_of(ctl, position):
    low = ctl[SLOT_LOW]
    return low if position == 0 else 1 - low


def flag(ctl, index):
    return ctl[index] > 0


def start_all(pairs, sems, first=0):
    copies = [
        pltpu.make_async_copy(src, dst, sems.at[first + k]) for k, (src, dst) in enumerate(pairs)
    ]
    for copy in copies:
        copy.start()
    return copies


def wait_all(copies):
    for copy in copies:
        copy.wait()


def sublanes(width=TILE):
    return lax.broadcasted_iota(jnp.int32, (8, width), 0)


def stacked(lines, base):
    row = sublanes()
    for index, line in enumerate(lines):
        base = jnp.where(row == index, jnp.broadcast_to(line, (8, TILE)), base)
    return base


def messages(ctl, state, bed, fastest, out, columns):
    upper = lax.axis_index("yb")
    column = lax.axis_index("xb")
    last = lax.axis_size("xb") - 1
    devices = 2 * (last + 1)
    device = column * 2 + upper
    top = jnp.broadcast_to(fastest, (8, TILE))
    for peer in range(devices):
        out[peer * 8 : peer * 8 + 8, :TILE] = top
        if bed is not None:
            out[peer * 8 : peer * 8 + 8, TILE:] = top[:, :LANES]
    row = sublanes()

    def edge(line):
        rows = slice(line, line + 1)
        lines = []
        for position in range(2):
            slot = slot_of(ctl, position)
            lines += [state[slot, field, rows, :] for field in range(3)]
            if bed is not None:
                lines.append(bed[slot, rows, :])
        return stacked(lines, top)

    for inside, peer, line in (
        (column > 0, device - 2, 0),
        (column < last, device + 2, TILE - 1),
    ):

        @pl.when(inside)
        def _(peer=peer, line=line):
            out[pl.ds(pl.multiple_of(peer * 8, 8), 8), :TILE] = edge(line)

    slot = jnp.where(upper > 0, ctl[SLOT_LOW], 1 - ctl[SLOT_LOW])
    begin = pl.multiple_of((1 - upper) * LANES, LANES)
    lane = lax.broadcasted_iota(jnp.int32, (TILE, LANES), 1)
    packed = None
    for field in range(4 if bed is not None else 3):
        if field < 3:
            part = state[slot, field, :, pl.ds(begin, LANES)]
        else:
            part = bed[slot, :, pl.ds(begin, LANES)]
        turned = pltpu.roll(part, field + 1 - upper, 1)
        packed = turned if field == 0 else jnp.where(lane == field, turned, packed)
    lines = jnp.transpose(packed)[:8]
    columns[...] = lines
    start = pl.multiple_of((device + 1 - 2 * upper) * 8, 8)
    out[pl.ds(start, 8), :TILE] = jnp.where(row == TOP, top, lines)


def opening(
    state_in, bed_in, manning_in, neighbours_in, wet_in, moves_in,
    out, columns, ctl, leaving_low, leaving_high,
    state, bed, manning, neighbours, wet, moves, sems,
):
    copies = start_all(
        (
            (neighbours_in, neighbours),
            (wet_in, wet),
            (moves_in, moves),
            (state_in.at[0], state.at[0]),
            (state_in.at[1], state.at[1]),
            (bed_in, bed),
        ),
        sems,
    )
    device = lax.axis_index("xb") * 2 + lax.axis_index("yb")
    wait_all(copies[:3])
    first = device * 2
    low = jnp.where(neighbours[3, first] == first + 1, 0, 1)
    ctl[SLOT_LOW] = low
    for position in range(2):
        slot = low if position == 0 else 1 - low
        tile = first + slot
        ctl[WALL_WEST + position] = (neighbours[0, tile] < 0).astype(jnp.int32)
        ctl[WALL_EAST + position] = (neighbours[1, tile] < 0).astype(jnp.int32)
        ctl[WALL_OUTER + position] = (neighbours[2 + position, tile] < 0).astype(jnp.int32)
    for step in range(STEPS):
        for slot in range(2):
            ctl[WET + 2 * step + slot] = wet[step, first + slot]
        ctl[MOVE + step] = moves[step, device]
    moving = moves[0, device]
    rough = start_all(((manning_in.at[moving, 0:EARLY], manning),), sems, 6)
    count = lax.axis_size("xb")
    upper = lax.axis_index("yb")
    column = lax.axis_index("xb")
    source = lax.rem(column + count - 1, count) * 2 + upper
    before = lax.rem(column + count - 2, count) * 2 + upper
    again = moves[0, source] == moves[1, source]
    tile_first = source * 2 + moves[0, source]
    tile_second = jnp.where(
        again, before * 2 + moves[0, before], source * 2 + 1 - moves[0, source]
    )
    for step in range(STEPS):
        ctl[WET_FIRST + step] = wet[step, tile_first]
        ctl[WET_SECOND + step] = wet[step, tile_second]

    wait_all(copies[3:] + rough)
    early = []
    for (begin, end), leaving in zip(PIECES, (leaving_low, leaving_high)):
        early += start_all(
            (
                (state.at[moving, :, begin:end], leaving.at[0:3]),
                (bed.at[moving, begin:end], leaving.at[3]),
                (manning.at[begin:end], leaving.at[4]),
            ),
            sems,
            7 + len(early),
        )
    total = jnp.zeros((ROWS, TILE), jnp.float32)
    for slot in range(2):

        def group(index, best, slot=slot):
            rows = pl.ds(pl.multiple_of(index * ROWS, ROWS), ROWS)
            along_x, along_y = cell(*(state[slot, field, rows, :] for field in range(3)))
            return jnp.maximum(best, jnp.maximum(along_x[5], along_y[5]))

        best = lax.fori_loop(0, TILE // ROWS, group, jnp.zeros((ROWS, TILE), jnp.float32))
        total = jnp.maximum(total, jnp.where(wet[0, first + slot] > 0, best, 0.0))
    messages(ctl, state, bed, jnp.max(total, keepdims=True), out, columns)
    wait_all(early)


def hold(first, second, leaving, same):
    del first, second, leaving, same


class Passing:
    def __init__(self, ctl, state_in, bed_in, manning_in, arrived, leaving, buffer, sems):
        self.again = ctl[MOVE] == ctl[MOVE + 1]
        self.other = 1 - ctl[MOVE]
        self.refs = state_in, bed_in, manning_in, arrived, buffer, sems
        self.outgoing = [
            pltpu.make_async_copy(buffer.at[:, begin:end], piece, sems.at[1 + index])
            for index, ((begin, end), piece) in enumerate(zip(PIECES, leaving))
        ]

    def start(self):
        state_in, bed_in, manning_in, arrived, buffer, sems = self.refs
        rows = slice(0, EARLY)
        sem = sems.at[0]

        @pl.when(self.again)
        def _():
            for (begin, end), piece in zip(PIECES, arrived):
                pltpu.make_async_copy(piece, buffer.at[:, begin:end], sem).start()

        @pl.when(jnp.logical_not(self.again))
        def _():
            pltpu.make_async_copy(state_in.at[self.other, :, rows], buffer.at[0:3], sem).start()
            pltpu.make_async_copy(bed_in.at[self.other, rows], buffer.at[3], sem).start()
            pltpu.make_async_copy(manning_in.at[self.other, rows], buffer.at[4], sem).start()

    def middle(self):
        _, _, _, arrived, buffer, sems = self.refs
        for (begin, end), piece in zip(PIECES, arrived):
            pltpu.make_async_copy(piece, buffer.at[:, begin:end], sems.at[0]).wait()
        for copy in self.outgoing:
            copy.start()

    def end(self):
        wait_all(self.outgoing)


def rates_and_leaving(
    ctl, state_in, bed_in, state_first, manning_in, arrived_low, arrived_high,
    rate_out, leaving_low, leaving_high,
    state, bed, rate, sems, buffer, moving,
):
    arrived = arrived_low, arrived_high
    passing = Passing(
        ctl, state_first, bed_in, manning_in, arrived, (leaving_low, leaving_high), buffer, moving
    )
    rates(ctl, state_in, bed_in, rate_out, state, bed, rate, sems, passing)


def rates_after(ctl, state_in, bed_in, order, *rest):
    del order
    rates(ctl, state_in, bed_in, *rest)


def rates(ctl, state_in, bed_in, rate_out, state, bed, rate, sems, passing=None):
    width = 2 * TILE
    row_ids = lax.broadcasted_iota(jnp.int32, (STRIP, width), 0)
    row8 = sublanes(width)
    lane = lax.broadcasted_iota(jnp.int32, (STRIP, LANES), 1)
    last = TILE // STRIP - 1
    chunk = TILE // CHUNKS
    slots = [slot_of(ctl, position) for position in range(2)]
    incoming = []
    for part in range(CHUNKS):
        rows = slice(part * chunk, (part + 1) * chunk)
        incoming.append(
            start_all(
                (
                    (state_in.at[:, :, rows], state.at[:, :, rows]),
                    (bed_in.at[:, rows], bed.at[:, rows]),
                ),
                sems,
                2 * part,
            )
        )
    if passing:
        passing.start()
    keep_west, keep_east, keep_south, keep_north = (
        jnp.where(flag(ctl, index), 1.0, 0.0)
        for index in (WALL_WEST, WALL_EAST, WALL_OUTER, WALL_OUTER + 1)
    )

    def strip(field, rows):
        if field == 3:
            return jnp.concatenate([bed[slot, rows, :] for slot in slots], 1)
        return jnp.concatenate([state[slot, field, rows, :] for slot in slots], 1)

    def blocks(value):
        return [value[:, k * LANES : (k + 1) * LANES] for k in range(4)]

    def right_of(value, end=None):
        turned = [pltpu.roll(part, LANES - 1, 1) for part in blocks(value)]
        after = turned[1:] + [turned[3] if end is None else end]
        return jnp.concatenate(
            [
                jnp.where(lane == LANES - 1, following, part)
                if following is not part
                else part
                for part, following in zip(turned, after)
            ],
            1,
        )

    def left_of(value, end):
        turned = [pltpu.roll(part, 1, 1) for part in blocks(value)]
        before = [end] + turned[:3]
        return jnp.concatenate(
            [jnp.where(lane == 0, previous, part) for part, previous in zip(turned, before)], 1
        )

    def down(value):
        return pltpu.roll(value, STRIP + 7, 0)[:STRIP]

    def group(index, carry):
        base = pl.multiple_of(index * STRIP, STRIP)
        rows = pl.ds(base, STRIP)
        after = pl.ds(pl.multiple_of(jnp.minimum(base + STRIP, TILE - 8), 8), 8)
        at_end = index == last
        fields = [
            jnp.concatenate([strip(field, rows), strip(field, after)], 0) for field in range(3)
        ]
        cells_x, cells_y = cell(*fields)
        here_x = tuple(value[:STRIP] for value in cells_x)
        here_y = tuple(value[:STRIP] for value in cells_y)

        ending = jnp.logical_and(row8 == 7, at_end)
        faces = list(face(here_x, tuple(down(value) for value in cells_x)))
        wall = keep_east * (2.0 * (here_x[3] + here_x[5] * here_x[1])[STRIP - 8 :])
        for component, value in enumerate((0.0, wall, 0.0)):
            upper = faces[component]
            faces[component] = jnp.concatenate(
                [upper[: STRIP - 8], jnp.where(ending, value, upper[STRIP - 8 :])], 0
            )
        turned = tuple(pltpu.roll(value, 1, 0) for value in faces)
        change_x = tuple(
            value - jnp.where(row_ids == 0, before, moved)
            for value, before, moved in zip(faces, carry[:3], turned)
        )
        ground = strip(3, rows)
        ground_after = jnp.where(
            at_end,
            jnp.broadcast_to(keep_east * ground[STRIP - 1 :], (8, width)),
            strip(3, after),
        )
        ground_up = pltpu.roll(ground, 1, 0)
        slope_x = down(jnp.concatenate([ground, ground_after], 0)) - jnp.where(
            row_ids == 0, carry[3], ground_up
        )
        carried = tuple(value[0:1, :] for value in turned) + (ground_up[0:1, :],)

        faces_y = list(face(here_y, tuple(right_of(value) for value in here_y)))
        normal = here_y[3]
        spread_y = here_y[5] * here_y[1]
        north = keep_north * (2.0 * (normal + spread_y)[:, width - LANES :])
        south = keep_south * (2.0 * (normal - spread_y)[:, :LANES])
        change_y = []
        for component, (high, low) in enumerate(((0.0, 0.0), (north, south), (0.0, 0.0))):
            parts = blocks(faces_y[component])
            parts[3] = jnp.where(lane == LANES - 1, high, parts[3])
            value = jnp.concatenate(parts, 1)
            change_y.append(value - left_of(value, low))
        slope_y = right_of(ground, keep_north * ground[:, width - LANES :]) - left_of(
            ground, keep_south * ground[:, :LANES]
        )
        weight = SLOPE * here_x[0]
        results = (
            SCALE * (change_x[0] + change_y[0]),
            SCALE * (change_x[1] + change_y[2]) + weight * slope_x,
            SCALE * (change_x[2] + change_y[1]) + weight * slope_y,
        )
        for field, value in enumerate(results):
            for position, slot in enumerate(slots):
                rate[slot, field, rows, :] = value[:, position * TILE : (position + 1) * TILE]
        return carried

    wait_all(incoming[0])
    top, _ = cell(*(strip(field, slice(0, 8)) for field in range(3)))
    nothing = jnp.zeros((1, width), jnp.float32)
    carry = (
        nothing,
        keep_west * (2.0 * (top[3] - top[5] * top[1])[0:1]),
        nothing,
        keep_west * strip(3, slice(0, 8))[0:1],
    )
    per_chunk = chunk // STRIP
    outgoing = []
    for part in range(CHUNKS):
        if part + 1 < CHUNKS:
            wait_all(incoming[part + 1])
        carry = lax.fori_loop(part * per_chunk, (part + 1) * per_chunk, group, carry)
        rows = slice(part * chunk, (part + 1) * chunk)
        outgoing += start_all(
            ((rate.at[:, :, rows], rate_out.at[:, :, rows]),), sems, 2 * CHUNKS + part
        )
        if passing and part == CHUNKS // 2:
            passing.middle()
    wait_all(outgoing)
    if passing:
        passing.end()


def moved_on(old, slopes, rough, delta, wet_now):
    h, hu, hv = (value - delta * slope for value, slope in zip(old, slopes))
    inverse = 1.0 / h
    u = hu * inverse
    v = hv * inverse
    speed = jnp.sqrt(u * u + v * v)
    power = jnp.exp((-4.0 / 3.0) * jnp.log(jnp.abs(h)))
    drag = (GRAVITY * delta) * (rough * rough) * (speed * power)
    factor = 1.0 / (1.0 + drag)
    fresh = (h, hu * factor, hv * factor)
    return tuple(jnp.where(wet_now, new, value) for new, value in zip(fresh, old))


def repeat_steps(ctl, wet_from, deltas, early, work, other, sems):
    incoming = []
    for ref in early:
        begin = 0 if ref is early[0] else early[0].shape[1]
        incoming += start_all(
            ((ref, work.at[:, begin : begin + ref.shape[1]]),), sems, len(incoming)
        )
    row_ids = lax.broadcasted_iota(jnp.int32, (ROWS, TILE), 0)
    lane = lax.broadcasted_iota(jnp.int32, (ROWS, LANES), 1)
    start = tuple(jnp.zeros((1, TILE), jnp.float32) for _ in range(4))

    def halves(value):
        return value[:, :LANES], value[:, LANES:]

    def right_of(value):
        low, high = (pltpu.roll(part, LANES - 1, 1) for part in halves(value))
        return jnp.concatenate([jnp.where(lane == LANES - 1, high, low), high], 1)

    def left_of(value):
        low, high = (pltpu.roll(part, 1, 1) for part in halves(value))
        return jnp.concatenate([low, jnp.where(lane == 0, low, high)], 1)

    def down(value):
        return pltpu.roll(value, ROWS + 7, 0)[:ROWS]

    for step in range(STEPS):
        source, target = (work, other) if step % 2 == 0 else (other, work)
        delta = deltas[step][0:1, :]
        wet_now = flag(ctl, wet_from + step)

        def group(index, carry, source=source, target=target, delta=delta, wet_now=wet_now):
            base = pl.multiple_of(index * ROWS, ROWS)
            rows = pl.ds(base, ROWS)
            after = pl.ds(pl.multiple_of(jnp.minimum(base + ROWS, EARLY - 8), 8), 8)
            refs = [source.at[field] for field in range(3)] + [work.at[3]]
            fields = [jnp.concatenate([ref[rows, :], ref[after, :]], 0) for ref in refs]
            cells_x, cells_y = cell(*fields[:3])
            here_x = tuple(value[:ROWS] for value in cells_x)
            here_y = tuple(value[:ROWS] for value in cells_y)
            faces_x = face(here_x, tuple(down(value) for value in cells_x))
            turned = tuple(pltpu.roll(value, 1, 0) for value in faces_x)
            change_x = tuple(
                value - jnp.where(row_ids == 0, before, moved)
                for value, before, moved in zip(faces_x, carry[:3], turned)
            )
            ground = fields[3][:ROWS]
            ground_up = pltpu.roll(ground, 1, 0)
            slope_x = down(fields[3]) - jnp.where(row_ids == 0, carry[3], ground_up)
            carried = tuple(value[0:1, :] for value in turned) + (ground_up[0:1, :],)
            faces_y = face(here_y, tuple(right_of(value) for value in here_y))
            change_y = tuple(value - left_of(value) for value in faces_y)
            slope_y = right_of(ground) - left_of(ground)
            old = tuple(value[:ROWS] for value in fields[:3])
            weight = SLOPE * old[0]
            slopes = (
                SCALE * (change_x[0] + change_y[0]),
                SCALE * (change_x[1] + change_y[2]) + weight * slope_x,
                SCALE * (change_x[2] + change_y[1]) + weight * slope_y,
            )
            for field, value in enumerate(
                moved_on(old, slopes, work[4, rows, :], delta, wet_now)
            ):
                target[field, rows, :] = value
            return carried

        if step == 0:
            wait_all(incoming)
        lax.fori_loop(0, EARLY // ROWS, group, start)


def late_rows(tile, late):
    row = sublanes()
    kept = EARLY - 8
    lane = lax.broadcasted_iota(jnp.int32, (8, LANES), 1)
    for field in range(3):
        late[field, 0:8, :] = jnp.where(
            row < 3, tile[field, 0:8, :], tile[field, kept : kept + 8, :]
        )
        packed = [jnp.zeros((8, LANES), jnp.float32)] * 2
        for block in range(EARLY // 8):
            rows = slice(8 * block, 8 * block + 8)
            sides = jnp.where(lane < 64, tile[field, rows, :LANES], tile[field, rows, LANES:])
            turned = pltpu.roll(sides, (3 + 8 * block) % LANES, 1)
            which = block // 16
            packed[which] = jnp.where(lane // 8 == block % 16, turned, packed[which])
        late[field, 8:16, :] = jnp.concatenate(packed, 1)
        late[field, 16:, :] = tile[field, EARLY:, :]


def merge(late, early, tile):
    for field in range(3):
        merge_field(field, late, early, tile)


def merge_field(field, late, early, tile):
    row = sublanes()
    lane = lax.broadcasted_iota(jnp.int32, (8, LANES), 1)
    first = late[field, 0:8, :]
    for block in range(EARLY // 8):
        rows = slice(8 * block, 8 * block + 8)
        which = block // 16
        packed = late[field, 8:16, which * LANES : (which + 1) * LANES]
        sides = pltpu.roll(packed, (-3 - 8 * block) % LANES, 1)
        value = early[field, rows, :]
        value = jnp.concatenate(
            [
                jnp.where(lane < 3, sides, value[:, :LANES]),
                jnp.where(lane >= LANES - 3, sides, value[:, LANES:]),
            ],
            1,
        )
        if block == 0:
            value = jnp.where(row < 3, first, value)
        if block == EARLY // 8 - 1:
            value = jnp.where(row < 5, value, first)
        tile[field, rows, :] = value
    tile[field, EARLY:, :] = late[field, 16:, :]


def repeat_second(ctl, delta0, delta1, delta2, low, high, late, out, late_out, work, tile, sems):
    near = start_all(((late, late_out),), sems, 2)
    repeat_steps(ctl, WET_SECOND, (delta0, delta1, delta2), (low, high), work, tile, sems)
    wait_all(start_all(((tile, out),), sems) + near)


def repeat_first(
    ctl, delta0, delta1, delta2, low, high, late_in, state, out, work, other, tile, late, sems
):
    rest = out.at[1 - ctl[MOVE + 1]]
    again = ctl[MOVE] == ctl[MOVE + 1]

    @pl.when(again)
    def _():
        wait_all(start_all(((state.at[1 - ctl[MOVE]], tile),), sems))

    @pl.when(jnp.logical_not(again))
    def _():
        copies = start_all(((late_in, late),), sems, 2)
        repeat_steps(ctl, WET_FIRST, (delta0, delta1, delta2), (low, high), work, other, sems)
        wait_all(copies)
        merge(late, other, tile)

    wait_all(start_all(((tile, rest),), sems))


def finish(ctl, late, early, before, out, tile, sems):
    del before
    copies = []
    for field in range(3):
        merge_field(field, late, early, tile)
        copies += start_all(
            ((tile.at[field], out.at[ctl[MOVE + 1], field]),), sems, field
        )
    wait_all(copies)


def second_late(ctl, arrived, own, order, leaving):
    del order
    again = ctl[MOVE] == ctl[MOVE + 1]
    for field in range(3):
        leaving[field] = jnp.where(again, arrived[field], own[field])


def correct_rows(ctl, slot, got, ground, state, rate, bottom):
    position = jnp.where(ctl[SLOT_LOW] == slot, 0, 1)
    device = lax.axis_index("xb") * 2 + lax.axis_index("yb")
    wall = WALL_WEST if bottom else WALL_EAST

    @pl.when(jnp.logical_not(flag(ctl, wall + position)))
    def _():
        peer = device - 2 if bottom else device + 2
        block = pl.ds(pl.multiple_of(peer * 8, 8), 8)
        lines = got[block, :TILE]
        grounds = ground[block, :TILE]
        stride = 4 if got.shape[1] > TILE else 3

        def line(offset):
            other = offset + stride
            picked = jnp.where(
                position == 0, lines[offset : offset + 1, :], lines[other : other + 1, :]
            )
            return jnp.broadcast_to(picked, (8, TILE))

        ghost, _ = cell(*(line(field) for field in range(3)))
        ghost_ground = jnp.where(position == 0, grounds[3:4, :], grounds[7:8, :])
        rows = slice(0, 8) if bottom else slice(TILE - 8, TILE)
        own = [state[slot, field, rows, :] for field in range(3)]
        here, _ = cell(*own)
        fluxes = face(ghost, here) if bottom else face(here, ghost)
        push = SCALE * fluxes[1] + (SLOPE * own[0]) * ghost_ground
        row = sublanes()
        sign = -1.0 if bottom else 1.0
        chosen = row == (0 if bottom else 7)
        for field, value in enumerate((SCALE * fluxes[0], push, SCALE * fluxes[2])):
            rate[slot, field, rows, :] += jnp.where(chosen, sign * value, 0.0)


def column_fix(got, ground, columns):
    upper = lax.axis_index("yb")
    device = lax.axis_index("xb") * 2 + upper
    peer = device + 1 - 2 * upper
    block = pl.ds(pl.multiple_of(peer * 8, 8), 8)
    lines = got[block, :TILE]
    ghost_ground = ground[block, :TILE][3:4]
    mine = columns[...]
    _, ghost = cell(lines[0:1], lines[1:2], lines[2:3])
    _, own = cell(mine[0:1], mine[1:2], mine[2:3])
    low = upper == 0
    left = tuple(jnp.where(low, a, b) for a, b in zip(own, ghost))
    right = tuple(jnp.where(low, b, a) for a, b in zip(own, ghost))
    fluxes = face(left, right)
    sign = jnp.where(low, 1.0, -1.0)
    push = SCALE * fluxes[1] + (SLOPE * mine[0:1]) * ghost_ground
    block8 = stacked(
        [sign * SCALE * fluxes[0], sign * SCALE * fluxes[2], sign * push],
        jnp.zeros((8, TILE), jnp.float32),
    )
    return jnp.transpose(
        jnp.concatenate([block8, jnp.zeros((LANES - 8, TILE), jnp.float32)], 0)
    )


def update(step, ctl, got_in, ground_in, columns_in, state_in, manning_in, rate_in, *rest):
    more = step + 1 < STEPS
    fresh_out, first_out, second_out, delta_out = rest[:4]
    rest = rest[4:]
    state, manning, rate, fresh, got, ground, columns, first, second, delta_keep, sems = rest
    out, columns_out = late_first, late_second = first, second
    small = start_all(
        ((got_in, got), (ground_in, ground), (columns_in, columns)), sems, 5 * PARTS
    )
    size = 2 * TILE // PARTS
    parts = [
        (slot, slice(k * size, (k + 1) * size)) for slot in range(2) for k in range(PARTS // 2)
    ]
    incoming = []
    for index, (slot, rows) in enumerate(parts):
        incoming.append(
            start_all(
                (
                    (rate_in.at[slot, :, rows], rate.at[slot, :, rows]),
                    (state_in.at[slot, :, rows], state.at[slot, :, rows]),
                    (manning_in.at[slot, rows], manning.at[slot, rows]),
                ),
                sems,
                3 * index,
            )
        )
    wait_all(small)
    upper = lax.axis_index("yb")
    devices = 2 * lax.axis_size("xb")
    begin = TILE if got.shape[1] > TILE else 0
    tops = got[0:8, begin : begin + LANES]
    for peer in range(1, devices):
        tops = jnp.maximum(tops, got[peer * 8 : peer * 8 + 8, begin : begin + LANES])
    delta = (COURANT * SPACING) / tops[TOP : TOP + 1, :]
    delta = jnp.concatenate([delta, delta], 1)
    delta_keep[...] = jnp.broadcast_to(delta, (8, TILE))
    outgoing = start_all(((delta_keep, delta_out),), sems, 5 * PARTS + 3)
    fix = column_fix(got, ground, columns)
    facing = jnp.where(upper > 0, ctl[SLOT_LOW], 1 - ctl[SLOT_LOW])
    begin = pl.multiple_of((1 - upper) * LANES, LANES)
    target = (1 - upper) * (LANES - 1)
    lane = lax.broadcasted_iota(jnp.int32, (size, LANES), 1)
    total = jnp.zeros((ROWS, TILE), jnp.float32)
    for index, (slot, part_rows) in enumerate(parts):
        wait_all(incoming[index])
        if part_rows.start == 0:
            correct_rows(ctl, slot, got, ground, state, rate, True)
        if part_rows.stop == TILE:
            correct_rows(ctl, slot, got, ground, state, rate, False)

        @pl.when(facing == slot)
        def _(slot=slot, part_rows=part_rows):
            for field in range(3):
                turned = pltpu.roll(
                    fix[part_rows], lax.rem(target + LANES - field, LANES), 1
                )
                rate[slot, field, part_rows, pl.ds(begin, LANES)] += jnp.where(
                    lane == target, turned, 0.0
                )

        wet_now = flag(ctl, WET + 2 * step + slot)

        def group(index, best, slot=slot, wet_now=wet_now):
            rows = pl.ds(pl.multiple_of(index * ROWS, ROWS), ROWS)
            old = tuple(state[slot, field, rows, :] for field in range(3))
            slopes = tuple(rate[slot, field, rows, :] for field in range(3))
            h, hu, hv = moved_on(old, slopes, manning[slot, rows, :], delta, wet_now)
            fresh[slot, 0, rows, :] = h
            fresh[slot, 1, rows, :] = hu
            fresh[slot, 2, rows, :] = hv
            if more:
                along_x, along_y = cell(h, hu, hv)
                best = jnp.maximum(best, jnp.maximum(along_x[5], along_y[5]))
            return best

        best = lax.fori_loop(
            part_rows.start // ROWS,
            part_rows.stop // ROWS,
            group,
            jnp.zeros((ROWS, TILE), jnp.float32),
        )
        if more:
            best = jnp.where(flag(ctl, WET + 2 * step + 2 + slot), best, 0.0)
            total = jnp.maximum(total, best)
        outgoing += start_all(
            ((fresh.at[slot, :, part_rows], fresh_out.at[slot, :, part_rows]),),
            sems,
            3 * PARTS + index,
        )
    if more:
        messages(ctl, fresh, None, jnp.max(total, keepdims=True), out, columns_out)
        outgoing += start_all(((out, first_out), (columns_out, second_out)), sems, 4 * PARTS)
    else:
        late_rows(fresh.at[ctl[MOVE]], late_first)
        outgoing += start_all(((late_first, first_out),), sems, 4 * PARTS)
        late_rows(fresh.at[1 - ctl[MOVE]], late_second)
        outgoing += start_all(((late_second, second_out),), sems, 4 * PARTS + 1)
    wait_all(outgoing)


def vmem():
    return pl.BlockSpec(memory_space=pltpu.VMEM)


def smem():
    return pl.BlockSpec(memory_space=pltpu.SMEM)


def hbm():
    return pl.BlockSpec(memory_space=pltpu.HBM)


def anywhere():
    return pl.BlockSpec(memory_space=pl.ANY)


def call(
    kernel, outs, out_specs, in_specs, flops, scratch=(), aliases=None, room=VMEM_BYTES, moved=4
):
    return pl.pallas_call(
        kernel,
        scratch_shapes=scratch,
        input_output_aliases=aliases or {},
        out_shape=outs,
        in_specs=in_specs,
        out_specs=out_specs,
        compiler_params=pltpu.CompilerParams(vmem_limit_bytes=room),
        cost_estimate=pl.CostEstimate(flops=flops, bytes_accessed=moved << 20, transcendentals=0),
    )


def f32(*shape):
    return jax.ShapeDtypeStruct(shape, jnp.float32)


def spread(fast):
    return lax.all_to_all(fast, ("xb", "yb"), split_axis=0, concat_axis=0, tiled=True)


def body(state, bed, manning, neighbours, wet, moves):
    shape = f32(*state.shape)
    devices = lax.axis_size("xb") * lax.axis_size("yb")
    whole = pltpu.VMEM(state.shape, jnp.float32)
    part = pltpu.VMEM(bed.shape, jnp.float32)
    tile_shape = f32(*state.shape[1:])
    early_shape = f32(5, EARLY, TILE)
    early_state = f32(3, EARLY, TILE)
    late_shape = f32(3, LATE, TILE)
    delta_shape = f32(8, TILE)

    def buffer(like):
        return pltpu.VMEM(like.shape, jnp.float32)

    piece_shapes = tuple(f32(5, end - begin, TILE) for begin, end in PIECES)
    out, columns, ctl, *leaving = call(
        opening,
        (
            f32(8 * devices, TILE + LANES),
            f32(8, TILE),
            jax.ShapeDtypeStruct((CONTROLS,), jnp.int32),
        )
        + piece_shapes,
        (vmem(), vmem(), smem(), hbm(), hbm()),
        [hbm()] * 6,
        4 << 20,
        [
            whole,
            part,
            pltpu.VMEM((EARLY, TILE), jnp.float32),
            pltpu.SMEM(neighbours.shape[::-1], jnp.int32),
            pltpu.SMEM(wet.shape, jnp.int32),
            pltpu.SMEM(moves.shape, jnp.int32),
            pltpu.SemaphoreType.DMA((13,)),
        ],
    )(state, bed, manning, neighbours.T, wet, moves)
    state_first = state
    ground = None
    deltas = []
    for step in range(STEPS):
        got = spread(out)
        ground = got if step == 0 else ground
        scratch = [whole, part, whole, pltpu.SemaphoreType.DMA((3 * CHUNKS,))]
        if step == 0:
            rate = call(rates, shape, hbm(), [smem(), hbm(), hbm()], 0, scratch, moved=0)(
                ctl, state, bed
            )
            leaving[1] = call(
                hold, piece_shapes[1], hbm(), [hbm()] * 3, 1 << 10, aliases={2: 0}
            )(rate, got, leaving[1])
            early_first = [shifted(piece, "xb", 1) for piece in leaving]
        elif step == 1:
            rate, *leaving = call(
                rates_and_leaving,
                (shape,) + piece_shapes,
                (hbm(),) * 3,
                [smem()] + [hbm()] * 6,
                16 << 20,
                scratch + [buffer(early_shape), pltpu.SemaphoreType.DMA((3,))],
            )(ctl, state, bed, state_first, manning, *early_first)
            early_second = [shifted(piece, "xb", 1) for piece in leaving]
        else:
            rate = call(rates_after, shape, hbm(), [smem()] + [hbm()] * 3, 16 << 20, scratch)(
                ctl, state, bed, early_second[0]
            )
        more = step + 1 < STEPS
        if more:
            shapes = f32(8 * devices, TILE), f32(8, TILE)
        else:
            shapes = late_shape, late_shape
        outs = call(
            functools.partial(update, step),
            (shape,) + shapes + (delta_shape,),
            (hbm(),) * 4,
            [smem()] + [hbm()] * 6,
            8 << 20,
            [
                whole,
                part,
                whole,
                whole,
                pltpu.VMEM(got.shape, jnp.float32),
                pltpu.VMEM(ground.shape, jnp.float32),
                pltpu.VMEM((8, TILE), jnp.float32),
                buffer(shapes[0]),
                buffer(shapes[1]),
                buffer(delta_shape),
                pltpu.SemaphoreType.DMA((5 * PARTS + 4,)),
            ],
            moved=14 if step == 0 else 10,
        )(ctl, got, ground, columns, state, manning, rate)
        deltas.append(outs[-1])
        state, out, columns, _ = outs
    late_first, late_second = out, columns
    room = 16 << 20
    late_arrived = shifted(late_first, "xb", 1)
    second, late_second = call(
        repeat_second,
        (early_state, late_shape),
        (anywhere(), vmem()),
        [smem()] + [vmem()] * 3 + [anywhere()] * 3,
        8 << 20,
        [buffer(early_shape), buffer(early_state), pltpu.SemaphoreType.DMA((3,))],
        room=room,
    )(ctl, *deltas, *early_second, late_second)
    leaving = call(
        second_late,
        late_shape,
        vmem(),
        [smem(), vmem(), vmem(), anywhere()],
        1 << 10,
        room=room,
    )(ctl, late_arrived, late_second, second)
    late_next = shifted(leaving, "xb", 1)
    final = call(
        repeat_first,
        shape,
        hbm(),
        [smem()] + [vmem()] * 3 + [anywhere()] * 4,
        8 << 20,
        [
            buffer(early_shape),
            buffer(early_state),
            buffer(tile_shape),
            buffer(late_shape),
            pltpu.SemaphoreType.DMA((3,)),
        ],
        room=room,
    )(ctl, *deltas, *early_first, late_arrived, state)
    return call(
        finish,
        shape,
        hbm(),
        [smem(), vmem(), vmem(), hbm()],
        1 << 20,
        [buffer(tile_shape), pltpu.SemaphoreType.DMA((3,))],
        {3: 0},
        room=room,
    )(ctl, late_next, second, final)


def solution(mesh):
    placed = (
        P(("runs", "xb", "yb"), None, None, None),
        P(("runs", "xb", "yb"), None, None),
        P(("runs", "xb", "yb"), None, None),
        P("runs", None),
        P(None, "runs"),
        P(None, "runs"),
    )
    return jax.shard_map(
        body,
        mesh=mesh,
        in_specs=placed,
        out_specs=P(("runs", "xb", "yb"), None, None, None),
        check_vma=False,
    )
```

```python
import functools

import jax
import jax.numpy as jnp
from jax import lax
from jax.experimental import pallas as pl
from jax.experimental.pallas import tpu as pltpu
from jax.sharding import PartitionSpec as P

STEPS = 3
GRAVITY = 9.81
ROOT_G = GRAVITY**0.5
SPACING = 5.0
COURANT = 0.2
ROWS = 32
LANES = 128
TILE = 256
VMEM_BYTES = 60 * 1024 * 1024
SLOT_LOW, WALL_WEST, WALL_EAST, WALL_OUTER, WET, MOVE = 0, 1, 3, 5, 7, 13
WET_FIRST, WET_SECOND = 16, 19
CONTROLS = 24
EARLY = 144
PIECES = ((0, 72), (72, 144))
AGAIN = 16
LATE = TILE - EARLY + 16
CHUNKS = 8
PARTS = 8
STRIP = 16
TOP = 6
SCALE = 0.5 / SPACING
SLOPE = GRAVITY / (2.0 * SPACING)


def shifted(value, axis, steps, around=True):
    count = lax.axis_size(axis)
    pairs = [(source, (source + steps) % count) for source in range(count)]
    if not around:
        pairs = [pair for pair in pairs if abs(pair[0] - pair[1]) == abs(steps)]
    return lax.ppermute(value, axis, pairs)


def cell(h, hu, hv):
    root = lax.rsqrt(h)
    inverse = root * root
    u = hu * inverse
    v = hv * inverse
    celerity = ROOT_G * (h * root)
    pressure = (0.5 * GRAVITY) * (h * h)
    cross = hu * v
    speed_x = jnp.abs(u) + celerity
    speed_y = jnp.abs(v) + celerity
    along_x = (h, hu, hv, hu * u + pressure, cross, speed_x)
    along_y = (h, hv, hu, hv * v + pressure, cross, speed_y)
    return along_x, along_y


def face(left, right):
    wave = jnp.maximum(left[5], right[5])
    return (
        (left[1] + right[1]) - wave * (right[0] - left[0]),
        (left[3] + right[3]) - wave * (right[1] - left[1]),
        (left[4] + right[4]) - wave * (right[2] - left[2]),
    )


def slot_of(ctl, position):
    low = ctl[SLOT_LOW]
    return low if position == 0 else 1 - low


def flag(ctl, index):
    return ctl[index] > 0


def start_all(pairs, sems, first=0):
    copies = [
        pltpu.make_async_copy(src, dst, sems.at[first + k]) for k, (src, dst) in enumerate(pairs)
    ]
    for copy in copies:
        copy.start()
    return copies


def wait_all(copies):
    for copy in copies:
        copy.wait()


def sublanes(width=TILE):
    return lax.broadcasted_iota(jnp.int32, (8, width), 0)


def stacked(lines, base):
    row = sublanes()
    for index, line in enumerate(lines):
        base = jnp.where(row == index, jnp.broadcast_to(line, (8, TILE)), base)
    return base


def messages(ctl, state, bed, fastest, out, columns):
    upper = lax.axis_index("yb")
    column = lax.axis_index("xb")
    last = lax.axis_size("xb") - 1
    devices = 2 * (last + 1)
    device = column * 2 + upper
    top = jnp.broadcast_to(fastest, (8, TILE))
    for peer in range(devices):
        out[peer * 8 : peer * 8 + 8, :TILE] = top
        if bed is not None:
            out[peer * 8 : peer * 8 + 8, TILE:] = top[:, :LANES]
    row = sublanes()

    def edge(line):
        rows = slice(line, line + 1)
        lines = []
        for position in range(2):
            slot = slot_of(ctl, position)
            lines += [state[slot, field, rows, :] for field in range(3)]
            if bed is not None:
                lines.append(bed[slot, rows, :])
        return stacked(lines, top)

    for inside, peer, line in (
        (column > 0, device - 2, 0),
        (column < last, device + 2, TILE - 1),
    ):

        @pl.when(inside)
        def _(peer=peer, line=line):
            out[pl.ds(pl.multiple_of(peer * 8, 8), 8), :TILE] = edge(line)

    slot = jnp.where(upper > 0, ctl[SLOT_LOW], 1 - ctl[SLOT_LOW])
    begin = pl.multiple_of((1 - upper) * LANES, LANES)
    lane = lax.broadcasted_iota(jnp.int32, (TILE, LANES), 1)
    packed = None
    for field in range(4 if bed is not None else 3):
        if field < 3:
            part = state[slot, field, :, pl.ds(begin, LANES)]
        else:
            part = bed[slot, :, pl.ds(begin, LANES)]
        turned = pltpu.roll(part, field + 1 - upper, 1)
        packed = turned if field == 0 else jnp.where(lane == field, turned, packed)
    lines = jnp.transpose(packed)[:8]
    columns[...] = lines
    start = pl.multiple_of((device + 1 - 2 * upper) * 8, 8)
    out[pl.ds(start, 8), :TILE] = jnp.where(row == TOP, top, lines)


def opening(
    state_in, bed_in, manning_in, neighbours_in, wet_in, moves_in,
    out, columns, ctl, leaving_low, leaving_high,
    state, bed, manning, neighbours, wet, moves, sems,
):
    copies = start_all(
        (
            (neighbours_in, neighbours),
            (wet_in, wet),
            (moves_in, moves),
            (state_in.at[0], state.at[0]),
            (state_in.at[1], state.at[1]),
            (bed_in, bed),
        ),
        sems,
    )
    device = lax.axis_index("xb") * 2 + lax.axis_index("yb")
    wait_all(copies[:3])
    first = device * 2
    low = jnp.where(neighbours[3, first] == first + 1, 0, 1)
    ctl[SLOT_LOW] = low
    for position in range(2):
        slot = low if position == 0 else 1 - low
        tile = first + slot
        ctl[WALL_WEST + position] = (neighbours[0, tile] < 0).astype(jnp.int32)
        ctl[WALL_EAST + position] = (neighbours[1, tile] < 0).astype(jnp.int32)
        ctl[WALL_OUTER + position] = (neighbours[2 + position, tile] < 0).astype(jnp.int32)
    for step in range(STEPS):
        for slot in range(2):
            ctl[WET + 2 * step + slot] = wet[step, first + slot]
        ctl[MOVE + step] = moves[step, device]
    moving = moves[0, device]
    rough = start_all(((manning_in.at[moving, 0:EARLY], manning),), sems, 6)
    count = lax.axis_size("xb")
    upper = lax.axis_index("yb")
    column = lax.axis_index("xb")
    source = lax.rem(column + count - 1, count) * 2 + upper
    before = lax.rem(column + count - 2, count) * 2 + upper
    again = moves[0, source] == moves[1, source]
    tile_first = source * 2 + moves[0, source]
    tile_second = jnp.where(
        again, before * 2 + moves[0, before], source * 2 + 1 - moves[0, source]
    )
    for step in range(STEPS):
        ctl[WET_FIRST + step] = wet[step, tile_first]
        ctl[WET_SECOND + step] = wet[step, tile_second]

    wait_all(copies[3:] + rough)
    early = []
    for (begin, end), leaving in zip(PIECES, (leaving_low, leaving_high)):
        early += start_all(
            (
                (state.at[moving, :, begin:end], leaving.at[0:3]),
                (bed.at[moving, begin:end], leaving.at[3]),
                (manning.at[begin:end], leaving.at[4]),
            ),
            sems,
            7 + len(early),
        )
    total = jnp.zeros((ROWS, TILE), jnp.float32)
    for slot in range(2):

        def group(index, best, slot=slot):
            rows = pl.ds(pl.multiple_of(index * ROWS, ROWS), ROWS)
            along_x, along_y = cell(*(state[slot, field, rows, :] for field in range(3)))
            return jnp.maximum(best, jnp.maximum(along_x[5], along_y[5]))

        best = lax.fori_loop(0, TILE // ROWS, group, jnp.zeros((ROWS, TILE), jnp.float32))
        total = jnp.maximum(total, jnp.where(wet[0, first + slot] > 0, best, 0.0))
    messages(ctl, state, bed, jnp.max(total, keepdims=True), out, columns)
    wait_all(early)


def hold(first, second, leaving, same):
    del first, second, leaving, same


class Passing:
    def __init__(self, ctl, piece, state_in, bed_in, manning_in, arrived, leaving, buffer, sems):
        self.again = ctl[MOVE] == ctl[MOVE + 1]
        self.other = 1 - ctl[MOVE]
        self.rows = slice(*piece)
        self.refs = state_in, bed_in, manning_in
        self.incoming = pltpu.make_async_copy(arrived, buffer, sems.at[0])
        self.outgoing = pltpu.make_async_copy(buffer, leaving, sems.at[1])
        self.buffer = buffer
        self.sem = sems.at[0]

    def start(self):
        state_in, bed_in, manning_in = self.refs
        buffer, sem, rows = self.buffer, self.sem, self.rows

        @pl.when(self.again)
        def _():
            self.incoming.start()

        @pl.when(jnp.logical_not(self.again))
        def _():
            pltpu.make_async_copy(state_in.at[self.other, :, rows], buffer.at[0:3], sem).start()
            pltpu.make_async_copy(bed_in.at[self.other, rows], buffer.at[3], sem).start()
            pltpu.make_async_copy(manning_in.at[self.other, rows], buffer.at[4], sem).start()

    def middle(self):
        self.incoming.wait()
        self.outgoing.start()

    def end(self):
        self.outgoing.wait()


def rates_and_leaving(
    ctl, state_in, bed_in, state_first, manning_in, arrived, rate_out, leaving,
    state, bed, rate, sems, buffer, moving,
):
    passing = Passing(
        ctl, PIECES[0], state_first, bed_in, manning_in, arrived, leaving, buffer, moving
    )
    rates(ctl, state_in, bed_in, rate_out, state, bed, rate, sems, passing)


def update_and_leaving(
    step, ctl, got_in, ground_in, columns_in, state_in, manning_in, rate_in,
    state_first, bed_in, arrived, fresh_out, first_out, second_out, delta_out, leaving, *rest
):
    *rest, buffer, moving = rest
    passing = Passing(
        ctl, PIECES[1], state_first, bed_in, manning_in, arrived, leaving, buffer, moving
    )
    passing.start()
    update(
        step, ctl, got_in, ground_in, columns_in, state_in, manning_in, rate_in,
        fresh_out, first_out, second_out, delta_out, *rest, passing=passing,
    )
    passing.end()


def rates_after(ctl, state_in, bed_in, order, *rest):
    del order
    rates(ctl, state_in, bed_in, *rest)


def rates(ctl, state_in, bed_in, rate_out, state, bed, rate, sems, passing=None):
    width = 2 * TILE
    row_ids = lax.broadcasted_iota(jnp.int32, (STRIP, width), 0)
    row8 = sublanes(width)
    lane = lax.broadcasted_iota(jnp.int32, (STRIP, LANES), 1)
    last = TILE // STRIP - 1
    chunk = TILE // CHUNKS
    slots = [slot_of(ctl, position) for position in range(2)]
    incoming = []
    for part in range(CHUNKS):
        rows = slice(part * chunk, (part + 1) * chunk)
        incoming.append(
            start_all(
                (
                    (state_in.at[:, :, rows], state.at[:, :, rows]),
                    (bed_in.at[:, rows], bed.at[:, rows]),
                ),
                sems,
                2 * part,
            )
        )
    if passing:
        passing.start()
    keep_west, keep_east, keep_south, keep_north = (
        jnp.where(flag(ctl, index), 1.0, 0.0)
        for index in (WALL_WEST, WALL_EAST, WALL_OUTER, WALL_OUTER + 1)
    )

    def strip(field, rows):
        if field == 3:
            return jnp.concatenate([bed[slot, rows, :] for slot in slots], 1)
        return jnp.concatenate([state[slot, field, rows, :] for slot in slots], 1)

    def blocks(value):
        return [value[:, k * LANES : (k + 1) * LANES] for k in range(4)]

    def right_of(value, end=None):
        turned = [pltpu.roll(part, LANES - 1, 1) for part in blocks(value)]
        after = turned[1:] + [turned[3] if end is None else end]
        return jnp.concatenate(
            [
                jnp.where(lane == LANES - 1, following, part)
                if following is not part
                else part
                for part, following in zip(turned, after)
            ],
            1,
        )

    def left_of(value, end):
        turned = [pltpu.roll(part, 1, 1) for part in blocks(value)]
        before = [end] + turned[:3]
        return jnp.concatenate(
            [jnp.where(lane == 0, previous, part) for part, previous in zip(turned, before)], 1
        )

    def down(value):
        return pltpu.roll(value, STRIP + 7, 0)[:STRIP]

    def group(index, carry):
        base = pl.multiple_of(index * STRIP, STRIP)
        rows = pl.ds(base, STRIP)
        after = pl.ds(pl.multiple_of(jnp.minimum(base + STRIP, TILE - 8), 8), 8)
        at_end = index == last
        fields = [
            jnp.concatenate([strip(field, rows), strip(field, after)], 0) for field in range(3)
        ]
        cells_x, cells_y = cell(*fields)
        here_x = tuple(value[:STRIP] for value in cells_x)
        here_y = tuple(value[:STRIP] for value in cells_y)

        ending = jnp.logical_and(row8 == 7, at_end)
        faces = list(face(here_x, tuple(down(value) for value in cells_x)))
        wall = keep_east * (2.0 * (here_x[3] + here_x[5] * here_x[1])[STRIP - 8 :])
        for component, value in enumerate((0.0, wall, 0.0)):
            upper = faces[component]
            faces[component] = jnp.concatenate(
                [upper[: STRIP - 8], jnp.where(ending, value, upper[STRIP - 8 :])], 0
            )
        turned = tuple(pltpu.roll(value, 1, 0) for value in faces)
        change_x = tuple(
            value - jnp.where(row_ids == 0, before, moved)
            for value, before, moved in zip(faces, carry[:3], turned)
        )
        ground = strip(3, rows)
        ground_after = jnp.where(
            at_end,
            jnp.broadcast_to(keep_east * ground[STRIP - 1 :], (8, width)),
            strip(3, after),
        )
        ground_up = pltpu.roll(ground, 1, 0)
        slope_x = down(jnp.concatenate([ground, ground_after], 0)) - jnp.where(
            row_ids == 0, carry[3], ground_up
        )
        carried = tuple(value[0:1, :] for value in turned) + (ground_up[0:1, :],)

        faces_y = list(face(here_y, tuple(right_of(value) for value in here_y)))
        normal = here_y[3]
        spread_y = here_y[5] * here_y[1]
        north = keep_north * (2.0 * (normal + spread_y)[:, width - LANES :])
        south = keep_south * (2.0 * (normal - spread_y)[:, :LANES])
        change_y = []
        for component, (high, low) in enumerate(((0.0, 0.0), (north, south), (0.0, 0.0))):
            parts = blocks(faces_y[component])
            parts[3] = jnp.where(lane == LANES - 1, high, parts[3])
            value = jnp.concatenate(parts, 1)
            change_y.append(value - left_of(value, low))
        slope_y = right_of(ground, keep_north * ground[:, width - LANES :]) - left_of(
            ground, keep_south * ground[:, :LANES]
        )
        weight = SLOPE * here_x[0]
        results = (
            SCALE * (change_x[0] + change_y[0]),
            SCALE * (change_x[1] + change_y[2]) + weight * slope_x,
            SCALE * (change_x[2] + change_y[1]) + weight * slope_y,
        )
        for field, value in enumerate(results):
            for position, slot in enumerate(slots):
                rate[slot, field, rows, :] = value[:, position * TILE : (position + 1) * TILE]
        return carried

    wait_all(incoming[0])
    top, _ = cell(*(strip(field, slice(0, 8)) for field in range(3)))
    nothing = jnp.zeros((1, width), jnp.float32)
    carry = (
        nothing,
        keep_west * (2.0 * (top[3] - top[5] * top[1])[0:1]),
        nothing,
        keep_west * strip(3, slice(0, 8))[0:1],
    )
    per_chunk = chunk // STRIP
    outgoing = []
    for part in range(CHUNKS):
        if part + 1 < CHUNKS:
            wait_all(incoming[part + 1])
        carry = lax.fori_loop(part * per_chunk, (part + 1) * per_chunk, group, carry)
        rows = slice(part * chunk, (part + 1) * chunk)
        outgoing += start_all(
            ((rate.at[:, :, rows], rate_out.at[:, :, rows]),), sems, 2 * CHUNKS + part
        )
        if passing and part == CHUNKS // 2:
            passing.middle()
    wait_all(outgoing)
    if passing:
        passing.end()


def moved_on(old, slopes, rough, delta, wet_now):
    h, hu, hv = (value - delta * slope for value, slope in zip(old, slopes))
    inverse = 1.0 / h
    u = hu * inverse
    v = hv * inverse
    speed = jnp.sqrt(u * u + v * v)
    power = jnp.exp((-4.0 / 3.0) * jnp.log(jnp.abs(h)))
    drag = (GRAVITY * delta) * (rough * rough) * (speed * power)
    factor = 1.0 / (1.0 + drag)
    fresh = (h, hu * factor, hv * factor)
    return tuple(jnp.where(wet_now, new, value) for new, value in zip(fresh, old))


def repeat_steps(ctl, wet_from, deltas, early, work, other, sems):
    incoming = []
    for ref in early:
        begin = 0 if ref is early[0] else early[0].shape[1]
        incoming += start_all(
            ((ref, work.at[:, begin : begin + ref.shape[1]]),), sems, len(incoming)
        )
    row_ids = lax.broadcasted_iota(jnp.int32, (AGAIN, TILE), 0)
    lane = lax.broadcasted_iota(jnp.int32, (AGAIN, LANES), 1)
    start = tuple(jnp.zeros((1, TILE), jnp.float32) for _ in range(4))

    def halves(value):
        return value[:, :LANES], value[:, LANES:]

    def right_of(value):
        low, high = (pltpu.roll(part, LANES - 1, 1) for part in halves(value))
        return jnp.concatenate([jnp.where(lane == LANES - 1, high, low), high], 1)

    def left_of(value):
        low, high = (pltpu.roll(part, 1, 1) for part in halves(value))
        return jnp.concatenate([low, jnp.where(lane == 0, low, high)], 1)

    def down(value):
        return pltpu.roll(value, AGAIN + 7, 0)[:AGAIN]

    for step in range(STEPS):
        source, target = (work, other) if step % 2 == 0 else (other, work)
        delta = deltas[step][0:1, :]
        wet_now = flag(ctl, wet_from + step)

        def group(index, carry, source=source, target=target, delta=delta, wet_now=wet_now):
            base = pl.multiple_of(index * AGAIN, AGAIN)
            rows = pl.ds(base, AGAIN)
            after = pl.ds(pl.multiple_of(jnp.minimum(base + AGAIN, EARLY - 8), 8), 8)
            refs = [source.at[field] for field in range(3)] + [work.at[3]]
            fields = [jnp.concatenate([ref[rows, :], ref[after, :]], 0) for ref in refs]
            cells_x, cells_y = cell(*fields[:3])
            here_x = tuple(value[:AGAIN] for value in cells_x)
            here_y = tuple(value[:AGAIN] for value in cells_y)
            faces_x = face(here_x, tuple(down(value) for value in cells_x))
            turned = tuple(pltpu.roll(value, 1, 0) for value in faces_x)
            change_x = tuple(
                value - jnp.where(row_ids == 0, before, moved)
                for value, before, moved in zip(faces_x, carry[:3], turned)
            )
            ground = fields[3][:AGAIN]
            ground_up = pltpu.roll(ground, 1, 0)
            slope_x = down(fields[3]) - jnp.where(row_ids == 0, carry[3], ground_up)
            carried = tuple(value[0:1, :] for value in turned) + (ground_up[0:1, :],)
            faces_y = face(here_y, tuple(right_of(value) for value in here_y))
            change_y = tuple(value - left_of(value) for value in faces_y)
            slope_y = right_of(ground) - left_of(ground)
            old = tuple(value[:AGAIN] for value in fields[:3])
            weight = SLOPE * old[0]
            slopes = (
                SCALE * (change_x[0] + change_y[0]),
                SCALE * (change_x[1] + change_y[2]) + weight * slope_x,
                SCALE * (change_x[2] + change_y[1]) + weight * slope_y,
            )
            for field, value in enumerate(
                moved_on(old, slopes, work[4, rows, :], delta, wet_now)
            ):
                target[field, rows, :] = value
            return carried

        if step == 0:
            wait_all(incoming)
        lax.fori_loop(0, EARLY // AGAIN, group, start)


def late_rows(tile, late):
    row = sublanes()
    kept = EARLY - 8
    lane = lax.broadcasted_iota(jnp.int32, (8, LANES), 1)
    for field in range(3):
        late[field, 0:8, :] = jnp.where(
            row < 3, tile[field, 0:8, :], tile[field, kept : kept + 8, :]
        )
        packed = [jnp.zeros((8, LANES), jnp.float32)] * 2
        for block in range(EARLY // 8):
            rows = slice(8 * block, 8 * block + 8)
            sides = jnp.where(lane < 64, tile[field, rows, :LANES], tile[field, rows, LANES:])
            turned = pltpu.roll(sides, (3 + 8 * block) % LANES, 1)
            which = block // 16
            packed[which] = jnp.where(lane // 8 == block % 16, turned, packed[which])
        late[field, 8:16, :] = jnp.concatenate(packed, 1)
        late[field, 16:, :] = tile[field, EARLY:, :]


def merge(late, early, tile):
    for field in range(3):
        merge_field(field, late, early, tile)


def merge_field(field, late, early, tile):
    row = sublanes()
    lane = lax.broadcasted_iota(jnp.int32, (8, LANES), 1)
    first = late[field, 0:8, :]
    for block in range(EARLY // 8):
        rows = slice(8 * block, 8 * block + 8)
        which = block // 16
        packed = late[field, 8:16, which * LANES : (which + 1) * LANES]
        sides = pltpu.roll(packed, (-3 - 8 * block) % LANES, 1)
        value = early[field, rows, :]
        value = jnp.concatenate(
            [
                jnp.where(lane < 3, sides, value[:, :LANES]),
                jnp.where(lane >= LANES - 3, sides, value[:, LANES:]),
            ],
            1,
        )
        if block == 0:
            value = jnp.where(row < 3, first, value)
        if block == EARLY // 8 - 1:
            value = jnp.where(row < 5, value, first)
        tile[field, rows, :] = value
    tile[field, EARLY:, :] = late[field, 16:, :]


def repeat_second(ctl, delta0, delta1, delta2, low, high, late, out, late_out, work, tile, sems):
    near = start_all(((late, late_out),), sems, 2)
    repeat_steps(ctl, WET_SECOND, (delta0, delta1, delta2), (low, high), work, tile, sems)
    wait_all(start_all(((tile, out),), sems) + near)


def repeat_first(
    ctl, delta0, delta1, delta2, low, high, late_in, state, out, work, other, tile, late, sems
):
    rest = out.at[1 - ctl[MOVE + 1]]
    again = ctl[MOVE] == ctl[MOVE + 1]

    @pl.when(again)
    def _():
        wait_all(start_all(((state.at[1 - ctl[MOVE]], tile),), sems))

    @pl.when(jnp.logical_not(again))
    def _():
        copies = start_all(((late_in, late),), sems, 2)
        repeat_steps(ctl, WET_FIRST, (delta0, delta1, delta2), (low, high), work, other, sems)
        wait_all(copies)
        merge(late, other, tile)

    wait_all(start_all(((tile, rest),), sems))


def finish(ctl, late, early, before, out, tile, sems):
    del before
    copies = []
    for field in range(3):
        merge_field(field, late, early, tile)
        copies += start_all(
            ((tile.at[field], out.at[ctl[MOVE + 1], field]),), sems, field
        )
    wait_all(copies)


def second_late(ctl, arrived, own, order, leaving):
    del order
    again = ctl[MOVE] == ctl[MOVE + 1]
    for field in range(3):
        leaving[field] = jnp.where(again, arrived[field], own[field])


def correct_rows(ctl, slot, got, ground, state, rate, bottom):
    position = jnp.where(ctl[SLOT_LOW] == slot, 0, 1)
    device = lax.axis_index("xb") * 2 + lax.axis_index("yb")
    wall = WALL_WEST if bottom else WALL_EAST

    @pl.when(jnp.logical_not(flag(ctl, wall + position)))
    def _():
        peer = device - 2 if bottom else device + 2
        block = pl.ds(pl.multiple_of(peer * 8, 8), 8)
        lines = got[block, :TILE]
        grounds = ground[block, :TILE]
        stride = 4 if got.shape[1] > TILE else 3

        def line(offset):
            other = offset + stride
            picked = jnp.where(
                position == 0, lines[offset : offset + 1, :], lines[other : other + 1, :]
            )
            return jnp.broadcast_to(picked, (8, TILE))

        ghost, _ = cell(*(line(field) for field in range(3)))
        ghost_ground = jnp.where(position == 0, grounds[3:4, :], grounds[7:8, :])
        rows = slice(0, 8) if bottom else slice(TILE - 8, TILE)
        own = [state[slot, field, rows, :] for field in range(3)]
        here, _ = cell(*own)
        fluxes = face(ghost, here) if bottom else face(here, ghost)
        push = SCALE * fluxes[1] + (SLOPE * own[0]) * ghost_ground
        row = sublanes()
        sign = -1.0 if bottom else 1.0
        chosen = row == (0 if bottom else 7)
        for field, value in enumerate((SCALE * fluxes[0], push, SCALE * fluxes[2])):
            rate[slot, field, rows, :] += jnp.where(chosen, sign * value, 0.0)


def column_fix(got, ground, columns):
    upper = lax.axis_index("yb")
    device = lax.axis_index("xb") * 2 + upper
    peer = device + 1 - 2 * upper
    block = pl.ds(pl.multiple_of(peer * 8, 8), 8)
    lines = got[block, :TILE]
    ghost_ground = ground[block, :TILE][3:4]
    mine = columns[...]
    _, ghost = cell(lines[0:1], lines[1:2], lines[2:3])
    _, own = cell(mine[0:1], mine[1:2], mine[2:3])
    low = upper == 0
    left = tuple(jnp.where(low, a, b) for a, b in zip(own, ghost))
    right = tuple(jnp.where(low, b, a) for a, b in zip(own, ghost))
    fluxes = face(left, right)
    sign = jnp.where(low, 1.0, -1.0)
    push = SCALE * fluxes[1] + (SLOPE * mine[0:1]) * ghost_ground
    block8 = stacked(
        [sign * SCALE * fluxes[0], sign * SCALE * fluxes[2], sign * push],
        jnp.zeros((8, TILE), jnp.float32),
    )
    return jnp.transpose(
        jnp.concatenate([block8, jnp.zeros((LANES - 8, TILE), jnp.float32)], 0)
    )


def update(
    step, ctl, got_in, ground_in, columns_in, state_in, manning_in, rate_in, *rest, passing=None
):
    more = step + 1 < STEPS
    fresh_out, first_out, second_out, delta_out = rest[:4]
    rest = rest[4:]
    state, manning, rate, fresh, got, ground, columns, first, second, delta_keep, sems = rest
    out, columns_out = late_first, late_second = first, second
    small = start_all(
        ((got_in, got), (ground_in, ground), (columns_in, columns)), sems, 5 * PARTS
    )
    size = 2 * TILE // PARTS
    parts = [
        (slot, slice(k * size, (k + 1) * size)) for slot in range(2) for k in range(PARTS // 2)
    ]
    incoming = []
    for index, (slot, rows) in enumerate(parts):
        incoming.append(
            start_all(
                (
                    (rate_in.at[slot, :, rows], rate.at[slot, :, rows]),
                    (state_in.at[slot, :, rows], state.at[slot, :, rows]),
                    (manning_in.at[slot, rows], manning.at[slot, rows]),
                ),
                sems,
                3 * index,
            )
        )
    wait_all(small)
    upper = lax.axis_index("yb")
    devices = 2 * lax.axis_size("xb")
    begin = TILE if got.shape[1] > TILE else 0
    tops = got[0:8, begin : begin + LANES]
    for peer in range(1, devices):
        tops = jnp.maximum(tops, got[peer * 8 : peer * 8 + 8, begin : begin + LANES])
    delta = (COURANT * SPACING) / tops[TOP : TOP + 1, :]
    delta = jnp.concatenate([delta, delta], 1)
    delta_keep[...] = jnp.broadcast_to(delta, (8, TILE))
    outgoing = start_all(((delta_keep, delta_out),), sems, 5 * PARTS + 3)
    fix = column_fix(got, ground, columns)
    facing = jnp.where(upper > 0, ctl[SLOT_LOW], 1 - ctl[SLOT_LOW])
    begin = pl.multiple_of((1 - upper) * LANES, LANES)
    target = (1 - upper) * (LANES - 1)
    lane = lax.broadcasted_iota(jnp.int32, (size, LANES), 1)
    total = jnp.zeros((ROWS, TILE), jnp.float32)
    for index, (slot, part_rows) in enumerate(parts):
        wait_all(incoming[index])
        if part_rows.start == 0:
            correct_rows(ctl, slot, got, ground, state, rate, True)
        if part_rows.stop == TILE:
            correct_rows(ctl, slot, got, ground, state, rate, False)

        @pl.when(facing == slot)
        def _(slot=slot, part_rows=part_rows):
            for field in range(3):
                turned = pltpu.roll(
                    fix[part_rows], lax.rem(target + LANES - field, LANES), 1
                )
                rate[slot, field, part_rows, pl.ds(begin, LANES)] += jnp.where(
                    lane == target, turned, 0.0
                )

        wet_now = flag(ctl, WET + 2 * step + slot)

        def group(index, best, slot=slot, wet_now=wet_now):
            rows = pl.ds(pl.multiple_of(index * ROWS, ROWS), ROWS)
            old = tuple(state[slot, field, rows, :] for field in range(3))
            slopes = tuple(rate[slot, field, rows, :] for field in range(3))
            h, hu, hv = moved_on(old, slopes, manning[slot, rows, :], delta, wet_now)
            fresh[slot, 0, rows, :] = h
            fresh[slot, 1, rows, :] = hu
            fresh[slot, 2, rows, :] = hv
            if more:
                along_x, along_y = cell(h, hu, hv)
                best = jnp.maximum(best, jnp.maximum(along_x[5], along_y[5]))
            return best

        best = lax.fori_loop(
            part_rows.start // ROWS,
            part_rows.stop // ROWS,
            group,
            jnp.zeros((ROWS, TILE), jnp.float32),
        )
        if more:
            best = jnp.where(flag(ctl, WET + 2 * step + 2 + slot), best, 0.0)
            total = jnp.maximum(total, best)
        outgoing += start_all(
            ((fresh.at[slot, :, part_rows], fresh_out.at[slot, :, part_rows]),),
            sems,
            3 * PARTS + index,
        )
        if passing and index == PARTS // 2:
            passing.middle()
    if more:
        messages(ctl, fresh, None, jnp.max(total, keepdims=True), out, columns_out)
        outgoing += start_all(((out, first_out), (columns_out, second_out)), sems, 4 * PARTS)
    else:
        late_rows(fresh.at[ctl[MOVE]], late_first)
        outgoing += start_all(((late_first, first_out),), sems, 4 * PARTS)
        late_rows(fresh.at[1 - ctl[MOVE]], late_second)
        outgoing += start_all(((late_second, second_out),), sems, 4 * PARTS + 1)
    wait_all(outgoing)


def vmem():
    return pl.BlockSpec(memory_space=pltpu.VMEM)


def smem():
    return pl.BlockSpec(memory_space=pltpu.SMEM)


def hbm():
    return pl.BlockSpec(memory_space=pltpu.HBM)


def anywhere():
    return pl.BlockSpec(memory_space=pl.ANY)


def call(
    kernel, outs, out_specs, in_specs, flops, scratch=(), aliases=None, room=VMEM_BYTES, moved=4
):
    return pl.pallas_call(
        kernel,
        scratch_shapes=scratch,
        input_output_aliases=aliases or {},
        out_shape=outs,
        in_specs=in_specs,
        out_specs=out_specs,
        compiler_params=pltpu.CompilerParams(vmem_limit_bytes=room),
        cost_estimate=pl.CostEstimate(flops=flops, bytes_accessed=moved << 20, transcendentals=0),
    )


def f32(*shape):
    return jax.ShapeDtypeStruct(shape, jnp.float32)


def spread(fast):
    return lax.all_to_all(fast, ("xb", "yb"), split_axis=0, concat_axis=0, tiled=True)


def body(state, bed, manning, neighbours, wet, moves):
    shape = f32(*state.shape)
    devices = lax.axis_size("xb") * lax.axis_size("yb")
    whole = pltpu.VMEM(state.shape, jnp.float32)
    part = pltpu.VMEM(bed.shape, jnp.float32)
    tile_shape = f32(*state.shape[1:])
    early_shape = f32(5, EARLY, TILE)
    early_state = f32(3, EARLY, TILE)
    late_shape = f32(3, LATE, TILE)
    delta_shape = f32(8, TILE)

    def buffer(like):
        return pltpu.VMEM(like.shape, jnp.float32)

    piece_shapes = tuple(f32(5, end - begin, TILE) for begin, end in PIECES)
    out, columns, ctl, *leaving = call(
        opening,
        (
            f32(8 * devices, TILE + LANES),
            f32(8, TILE),
            jax.ShapeDtypeStruct((CONTROLS,), jnp.int32),
        )
        + piece_shapes,
        (vmem(), vmem(), smem(), hbm(), hbm()),
        [hbm()] * 6,
        4 << 20,
        [
            whole,
            part,
            pltpu.VMEM((EARLY, TILE), jnp.float32),
            pltpu.SMEM(neighbours.shape[::-1], jnp.int32),
            pltpu.SMEM(wet.shape, jnp.int32),
            pltpu.SMEM(moves.shape, jnp.int32),
            pltpu.SemaphoreType.DMA((13,)),
        ],
    )(state, bed, manning, neighbours.T, wet, moves)
    state_first = state
    ground = None
    deltas = []
    for step in range(STEPS):
        got = spread(out)
        ground = got if step == 0 else ground
        scratch = [whole, part, whole, pltpu.SemaphoreType.DMA((3 * CHUNKS,))]
        piece_scratch = [buffer(piece_shapes[0]), pltpu.SemaphoreType.DMA((2,))]
        if step == 1:
            rate, leaving = call(
                rates_and_leaving,
                (shape, piece_shapes[0]),
                (hbm(),) * 2,
                [smem()] + [hbm()] * 5,
                16 << 20,
                scratch + piece_scratch,
            )(ctl, state, bed, state_first, manning, early_first[0])
            early_second = [shifted(leaving, "xb", 1)]
        elif step == 2:
            rate = call(rates_after, shape, hbm(), [smem()] + [hbm()] * 3, 16 << 20, scratch)(
                ctl, state, bed, early_second[0]
            )
        else:
            rate = call(rates, shape, hbm(), [smem(), hbm(), hbm()], 16 << 20, scratch)(
                ctl, state, bed
            )
            held = call(
                hold, piece_shapes[0], hbm(), [hbm()] * 3, 1 << 10, aliases={2: 0}
            )(rate, got, leaving[0])
            early_first = [shifted(held, "xb", 1)]
        more = step + 1 < STEPS
        if more:
            shapes = f32(8 * devices, TILE), f32(8, TILE)
        else:
            shapes = late_shape, late_shape
        passing = step == 1
        outs = call(
            functools.partial(update_and_leaving if passing else update, step),
            (shape,) + shapes + (delta_shape,) + ((piece_shapes[1],) if passing else ()),
            (hbm(),) * (5 if passing else 4),
            [smem()] + [hbm()] * (9 if passing else 6),
            8 << 20,
            [
                whole,
                part,
                whole,
                whole,
                pltpu.VMEM(got.shape, jnp.float32),
                pltpu.VMEM(ground.shape, jnp.float32),
                pltpu.VMEM((8, TILE), jnp.float32),
                buffer(shapes[0]),
                buffer(shapes[1]),
                buffer(delta_shape),
                pltpu.SemaphoreType.DMA((5 * PARTS + 4,)),
            ]
            + (piece_scratch if passing else []),
            moved=10,
        )(
            ctl, got, ground, columns, state, manning, rate,
            *((state_first, bed, early_first[1]) if passing else ())
        )
        state, out, columns, delta, *passed = outs
        deltas.append(delta)
        if step == 0:
            held = call(
                hold, piece_shapes[1], hbm(), [hbm()] * 3, 1 << 10, aliases={2: 0}
            )(delta, delta, leaving[1])
            early_first.append(shifted(held, "xb", 1))
        elif step == 1:
            early_second.append(shifted(passed[0], "xb", 1))
    late_first, late_second = out, columns
    room = 16 << 20
    late_arrived = shifted(late_first, "xb", 1)
    second, late_second = call(
        repeat_second,
        (early_state, late_shape),
        (anywhere(), vmem()),
        [smem()] + [vmem()] * 3 + [anywhere()] * 3,
        8 << 20,
        [buffer(early_shape), buffer(early_state), pltpu.SemaphoreType.DMA((3,))],
        room=room,
    )(ctl, *deltas, *early_second, late_second)
    leaving = call(
        second_late,
        late_shape,
        vmem(),
        [smem(), vmem(), vmem(), anywhere()],
        1 << 10,
        room=room,
    )(ctl, late_arrived, late_second, second)
    late_next = shifted(leaving, "xb", 1)
    final = call(
        repeat_first,
        shape,
        hbm(),
        [smem()] + [vmem()] * 3 + [anywhere()] * 4,
        8 << 20,
        [
            buffer(early_shape),
            buffer(early_state),
            buffer(tile_shape),
            buffer(late_shape),
            pltpu.SemaphoreType.DMA((3,)),
        ],
        room=room,
    )(ctl, *deltas, *early_first, late_arrived, state)
    return call(
        finish,
        shape,
        hbm(),
        [smem(), vmem(), vmem(), hbm()],
        1 << 20,
        [buffer(tile_shape), pltpu.SemaphoreType.DMA((3,))],
        {3: 0},
        room=room,
    )(ctl, late_next, second, final)


def solution(mesh):
    placed = (
        P(("runs", "xb", "yb"), None, None, None),
        P(("runs", "xb", "yb"), None, None),
        P(("runs", "xb", "yb"), None, None),
        P("runs", None),
        P(None, "runs"),
        P(None, "runs"),
    )
    return jax.shard_map(
        body,
        mesh=mesh,
        in_specs=placed,
        out_specs=P(("runs", "xb", "yb"), None, None, None),
        check_vma=False,
    )
```

```python
import functools

import jax
import jax.numpy as jnp
from jax import lax
from jax.experimental import pallas as pl
from jax.experimental.pallas import tpu as pltpu
from jax.sharding import PartitionSpec as P

STEPS = 3
GRAVITY = 9.81
ROOT_G = GRAVITY**0.5
SPACING = 5.0
COURANT = 0.2
ROWS = 32
LANES = 128
TILE = 256
VMEM_BYTES = 60 * 1024 * 1024
SLOT_LOW, WALL_WEST, WALL_EAST, WALL_OUTER, WET, MOVE = 0, 1, 3, 5, 7, 13
WET_FIRST, WET_SECOND = 16, 19
CONTROLS = 24
EARLY = 144
PIECES = ((0, 80), (80, 144))
AGAIN = 16
LATE = TILE - EARLY + 16
CHUNKS = 8
PARTS = 8
STRIP = 16
TOP = 6
SCALE = 0.5 / SPACING
SLOPE = GRAVITY / (2.0 * SPACING)


def shifted(value, axis, steps, around=True):
    count = lax.axis_size(axis)
    pairs = [(source, (source + steps) % count) for source in range(count)]
    if not around:
        pairs = [pair for pair in pairs if abs(pair[0] - pair[1]) == abs(steps)]
    return lax.ppermute(value, axis, pairs)


def cell(h, hu, hv):
    root = lax.rsqrt(h)
    inverse = root * root
    u = hu * inverse
    v = hv * inverse
    celerity = ROOT_G * (h * root)
    pressure = (0.5 * GRAVITY) * (h * h)
    cross = hu * v
    speed_x = jnp.abs(u) + celerity
    speed_y = jnp.abs(v) + celerity
    along_x = (h, hu, hv, hu * u + pressure, cross, speed_x)
    along_y = (h, hv, hu, hv * v + pressure, cross, speed_y)
    return along_x, along_y


def face(left, right):
    wave = jnp.maximum(left[5], right[5])
    return (
        (left[1] + right[1]) - wave * (right[0] - left[0]),
        (left[3] + right[3]) - wave * (right[1] - left[1]),
        (left[4] + right[4]) - wave * (right[2] - left[2]),
    )


def slot_of(ctl, position):
    low = ctl[SLOT_LOW]
    return low if position == 0 else 1 - low


def flag(ctl, index):
    return ctl[index] > 0


def start_all(pairs, sems, first=0):
    copies = [
        pltpu.make_async_copy(src, dst, sems.at[first + k]) for k, (src, dst) in enumerate(pairs)
    ]
    for copy in copies:
        copy.start()
    return copies


def wait_all(copies):
    for copy in copies:
        copy.wait()


def sublanes(width=TILE):
    return lax.broadcasted_iota(jnp.int32, (8, width), 0)


def stacked(lines, base):
    row = sublanes()
    for index, line in enumerate(lines):
        base = jnp.where(row == index, jnp.broadcast_to(line, (8, TILE)), base)
    return base


def messages(ctl, state, bed, fastest, out, columns):
    upper = lax.axis_index("yb")
    column = lax.axis_index("xb")
    last = lax.axis_size("xb") - 1
    devices = 2 * (last + 1)
    device = column * 2 + upper
    top = jnp.broadcast_to(fastest, (8, TILE))
    for peer in range(devices):
        out[peer * 8 : peer * 8 + 8, :TILE] = top
        if bed is not None:
            out[peer * 8 : peer * 8 + 8, TILE:] = top[:, :LANES]
    row = sublanes()

    def edge(line):
        rows = slice(line, line + 1)
        lines = []
        for position in range(2):
            slot = slot_of(ctl, position)
            lines += [state[slot, field, rows, :] for field in range(3)]
            if bed is not None:
                lines.append(bed[slot, rows, :])
        return stacked(lines, top)

    for inside, peer, line in (
        (column > 0, device - 2, 0),
        (column < last, device + 2, TILE - 1),
    ):

        @pl.when(inside)
        def _(peer=peer, line=line):
            out[pl.ds(pl.multiple_of(peer * 8, 8), 8), :TILE] = edge(line)

    slot = jnp.where(upper > 0, ctl[SLOT_LOW], 1 - ctl[SLOT_LOW])
    begin = pl.multiple_of((1 - upper) * LANES, LANES)
    lane = lax.broadcasted_iota(jnp.int32, (TILE, LANES), 1)
    packed = None
    for field in range(4 if bed is not None else 3):
        if field < 3:
            part = state[slot, field, :, pl.ds(begin, LANES)]
        else:
            part = bed[slot, :, pl.ds(begin, LANES)]
        turned = pltpu.roll(part, field + 1 - upper, 1)
        packed = turned if field == 0 else jnp.where(lane == field, turned, packed)
    lines = jnp.transpose(packed)[:8]
    columns[...] = lines
    start = pl.multiple_of((device + 1 - 2 * upper) * 8, 8)
    out[pl.ds(start, 8), :TILE] = jnp.where(row == TOP, top, lines)


def opening(
    state_in, bed_in, manning_in, neighbours_in, wet_in, moves_in,
    out, columns, ctl, leaving_low, leaving_high,
    state, bed, manning, neighbours, wet, moves, sems,
):
    copies = start_all(
        (
            (neighbours_in, neighbours),
            (wet_in, wet),
            (moves_in, moves),
            (state_in.at[0], state.at[0]),
            (state_in.at[1], state.at[1]),
            (bed_in, bed),
        ),
        sems,
    )
    device = lax.axis_index("xb") * 2 + lax.axis_index("yb")
    wait_all(copies[:3])
    first = device * 2
    low = jnp.where(neighbours[3, first] == first + 1, 0, 1)
    ctl[SLOT_LOW] = low
    for position in range(2):
        slot = low if position == 0 else 1 - low
        tile = first + slot
        ctl[WALL_WEST + position] = (neighbours[0, tile] < 0).astype(jnp.int32)
        ctl[WALL_EAST + position] = (neighbours[1, tile] < 0).astype(jnp.int32)
        ctl[WALL_OUTER + position] = (neighbours[2 + position, tile] < 0).astype(jnp.int32)
    for step in range(STEPS):
        for slot in range(2):
            ctl[WET + 2 * step + slot] = wet[step, first + slot]
        ctl[MOVE + step] = moves[step, device]
    moving = moves[0, device]
    rough = start_all(((manning_in.at[moving, 0:EARLY], manning),), sems, 6)
    count = lax.axis_size("xb")
    upper = lax.axis_index("yb")
    column = lax.axis_index("xb")
    source = lax.rem(column + count - 1, count) * 2 + upper
    before = lax.rem(column + count - 2, count) * 2 + upper
    again = moves[0, source] == moves[1, source]
    tile_first = source * 2 + moves[0, source]
    tile_second = jnp.where(
        again, before * 2 + moves[0, before], source * 2 + 1 - moves[0, source]
    )
    for step in range(STEPS):
        ctl[WET_FIRST + step] = wet[step, tile_first]
        ctl[WET_SECOND + step] = wet[step, tile_second]

    wait_all(copies[3:] + rough)
    early = []
    for (begin, end), leaving in zip(PIECES, (leaving_low, leaving_high)):
        early += start_all(
            (
                (state.at[moving, :, begin:end], leaving.at[0:3]),
                (bed.at[moving, begin:end], leaving.at[3]),
                (manning.at[begin:end], leaving.at[4]),
            ),
            sems,
            7 + len(early),
        )
    total = jnp.zeros((ROWS, TILE), jnp.float32)
    for slot in range(2):

        def group(index, best, slot=slot):
            rows = pl.ds(pl.multiple_of(index * ROWS, ROWS), ROWS)
            along_x, along_y = cell(*(state[slot, field, rows, :] for field in range(3)))
            return jnp.maximum(best, jnp.maximum(along_x[5], along_y[5]))

        best = lax.fori_loop(0, TILE // ROWS, group, jnp.zeros((ROWS, TILE), jnp.float32))
        total = jnp.maximum(total, jnp.where(wet[0, first + slot] > 0, best, 0.0))
    messages(ctl, state, bed, jnp.max(total, keepdims=True), out, columns)
    wait_all(early)


def hold(first, second, leaving, same):
    del first, second, leaving, same


class Passing:
    def __init__(self, ctl, piece, state_in, bed_in, manning_in, arrived, leaving, buffer, sems):
        self.again = ctl[MOVE] == ctl[MOVE + 1]
        self.other = 1 - ctl[MOVE]
        self.rows = slice(*piece)
        self.refs = state_in, bed_in, manning_in
        self.incoming = pltpu.make_async_copy(arrived, buffer, sems.at[0])
        self.outgoing = pltpu.make_async_copy(buffer, leaving, sems.at[1])
        self.buffer = buffer
        self.sem = sems.at[0]

    def start(self):
        state_in, bed_in, manning_in = self.refs
        buffer, sem, rows = self.buffer, self.sem, self.rows

        @pl.when(self.again)
        def _():
            self.incoming.start()

        @pl.when(jnp.logical_not(self.again))
        def _():
            pltpu.make_async_copy(state_in.at[self.other, :, rows], buffer.at[0:3], sem).start()
            pltpu.make_async_copy(bed_in.at[self.other, rows], buffer.at[3], sem).start()
            pltpu.make_async_copy(manning_in.at[self.other, rows], buffer.at[4], sem).start()

    def middle(self):
        self.incoming.wait()
        self.outgoing.start()

    def end(self):
        self.outgoing.wait()


def rates_and_leaving(
    ctl, state_in, bed_in, state_first, manning_in, arrived, rate_out, leaving,
    state, bed, rate, sems, buffer, moving,
):
    passing = Passing(
        ctl, PIECES[0], state_first, bed_in, manning_in, arrived, leaving, buffer, moving
    )
    rates(ctl, state_in, bed_in, rate_out, state, bed, rate, sems, passing)


def update_and_leaving(
    step, ctl, got_in, ground_in, columns_in, state_in, manning_in, rate_in,
    state_first, bed_in, arrived, fresh_out, first_out, second_out, delta_out, leaving, *rest
):
    *rest, buffer, moving = rest
    passing = Passing(
        ctl, PIECES[1], state_first, bed_in, manning_in, arrived, leaving, buffer, moving
    )
    passing.start()
    update(
        step, ctl, got_in, ground_in, columns_in, state_in, manning_in, rate_in,
        fresh_out, first_out, second_out, delta_out, *rest, passing=passing,
    )
    passing.end()


def rates_after(ctl, state_in, bed_in, order, *rest):
    del order
    rates(ctl, state_in, bed_in, *rest)


def rates(ctl, state_in, bed_in, rate_out, state, bed, rate, sems, passing=None):
    width = 2 * TILE
    row_ids = lax.broadcasted_iota(jnp.int32, (STRIP, width), 0)
    row8 = sublanes(width)
    lane = lax.broadcasted_iota(jnp.int32, (STRIP, LANES), 1)
    last = TILE // STRIP - 1
    chunk = TILE // CHUNKS
    slots = [slot_of(ctl, position) for position in range(2)]
    incoming = []
    for part in range(CHUNKS):
        rows = slice(part * chunk, (part + 1) * chunk)
        incoming.append(
            start_all(
                (
                    (state_in.at[:, :, rows], state.at[:, :, rows]),
                    (bed_in.at[:, rows], bed.at[:, rows]),
                ),
                sems,
                2 * part,
            )
        )
    if passing:
        passing.start()
    keep_west, keep_east, keep_south, keep_north = (
        jnp.where(flag(ctl, index), 1.0, 0.0)
        for index in (WALL_WEST, WALL_EAST, WALL_OUTER, WALL_OUTER + 1)
    )

    def strip(field, rows):
        if field == 3:
            return jnp.concatenate([bed[slot, rows, :] for slot in slots], 1)
        return jnp.concatenate([state[slot, field, rows, :] for slot in slots], 1)

    def blocks(value):
        return [value[:, k * LANES : (k + 1) * LANES] for k in range(4)]

    def right_of(value, end=None):
        turned = [pltpu.roll(part, LANES - 1, 1) for part in blocks(value)]
        after = turned[1:] + [turned[3] if end is None else end]
        return jnp.concatenate(
            [
                jnp.where(lane == LANES - 1, following, part)
                if following is not part
                else part
                for part, following in zip(turned, after)
            ],
            1,
        )

    def left_of(value, end):
        turned = [pltpu.roll(part, 1, 1) for part in blocks(value)]
        before = [end] + turned[:3]
        return jnp.concatenate(
            [jnp.where(lane == 0, previous, part) for part, previous in zip(turned, before)], 1
        )

    def down(value):
        return pltpu.roll(value, STRIP + 7, 0)[:STRIP]

    def group(index, carry):
        base = pl.multiple_of(index * STRIP, STRIP)
        rows = pl.ds(base, STRIP)
        after = pl.ds(pl.multiple_of(jnp.minimum(base + STRIP, TILE - 8), 8), 8)
        at_end = index == last
        fields = [
            jnp.concatenate([strip(field, rows), strip(field, after)], 0) for field in range(3)
        ]
        cells_x, cells_y = cell(*fields)
        here_x = tuple(value[:STRIP] for value in cells_x)
        here_y = tuple(value[:STRIP] for value in cells_y)

        ending = jnp.logical_and(row8 == 7, at_end)
        faces = list(face(here_x, tuple(down(value) for value in cells_x)))
        wall = keep_east * (2.0 * (here_x[3] + here_x[5] * here_x[1])[STRIP - 8 :])
        for component, value in enumerate((0.0, wall, 0.0)):
            upper = faces[component]
            faces[component] = jnp.concatenate(
                [upper[: STRIP - 8], jnp.where(ending, value, upper[STRIP - 8 :])], 0
            )
        turned = tuple(pltpu.roll(value, 1, 0) for value in faces)
        change_x = tuple(
            value - jnp.where(row_ids == 0, before, moved)
            for value, before, moved in zip(faces, carry[:3], turned)
        )
        ground = strip(3, rows)
        ground_after = jnp.where(
            at_end,
            jnp.broadcast_to(keep_east * ground[STRIP - 1 :], (8, width)),
            strip(3, after),
        )
        ground_up = pltpu.roll(ground, 1, 0)
        slope_x = down(jnp.concatenate([ground, ground_after], 0)) - jnp.where(
            row_ids == 0, carry[3], ground_up
        )
        carried = tuple(value[0:1, :] for value in turned) + (ground_up[0:1, :],)

        faces_y = list(face(here_y, tuple(right_of(value) for value in here_y)))
        normal = here_y[3]
        spread_y = here_y[5] * here_y[1]
        north = keep_north * (2.0 * (normal + spread_y)[:, width - LANES :])
        south = keep_south * (2.0 * (normal - spread_y)[:, :LANES])
        change_y = []
        for component, (high, low) in enumerate(((0.0, 0.0), (north, south), (0.0, 0.0))):
            parts = blocks(faces_y[component])
            parts[3] = jnp.where(lane == LANES - 1, high, parts[3])
            value = jnp.concatenate(parts, 1)
            change_y.append(value - left_of(value, low))
        slope_y = right_of(ground, keep_north * ground[:, width - LANES :]) - left_of(
            ground, keep_south * ground[:, :LANES]
        )
        weight = SLOPE * here_x[0]
        results = (
            SCALE * (change_x[0] + change_y[0]),
            SCALE * (change_x[1] + change_y[2]) + weight * slope_x,
            SCALE * (change_x[2] + change_y[1]) + weight * slope_y,
        )
        for field, value in enumerate(results):
            for position, slot in enumerate(slots):
                rate[slot, field, rows, :] = value[:, position * TILE : (position + 1) * TILE]
        return carried

    wait_all(incoming[0])
    top, _ = cell(*(strip(field, slice(0, 8)) for field in range(3)))
    nothing = jnp.zeros((1, width), jnp.float32)
    carry = (
        nothing,
        keep_west * (2.0 * (top[3] - top[5] * top[1])[0:1]),
        nothing,
        keep_west * strip(3, slice(0, 8))[0:1],
    )
    per_chunk = chunk // STRIP
    outgoing = []
    for part in range(CHUNKS):
        if part + 1 < CHUNKS:
            wait_all(incoming[part + 1])
        carry = lax.fori_loop(part * per_chunk, (part + 1) * per_chunk, group, carry)
        rows = slice(part * chunk, (part + 1) * chunk)
        outgoing += start_all(
            ((rate.at[:, :, rows], rate_out.at[:, :, rows]),), sems, 2 * CHUNKS + part
        )
        if passing and part == CHUNKS // 2:
            passing.middle()
    wait_all(outgoing)
    if passing:
        passing.end()


def moved_on(old, slopes, rough, delta, wet_now):
    h, hu, hv = (value - delta * slope for value, slope in zip(old, slopes))
    inverse = 1.0 / h
    u = hu * inverse
    v = hv * inverse
    speed = jnp.sqrt(u * u + v * v)
    power = jnp.exp((-4.0 / 3.0) * jnp.log(jnp.abs(h)))
    drag = (GRAVITY * delta) * (rough * rough) * (speed * power)
    factor = 1.0 / (1.0 + drag)
    fresh = (h, hu * factor, hv * factor)
    return tuple(jnp.where(wet_now, new, value) for new, value in zip(fresh, old))


def repeat_steps(ctl, wet_from, deltas, early, work, other, sems):
    incoming = []
    for ref in early:
        begin = 0 if ref is early[0] else early[0].shape[1]
        incoming += start_all(
            ((ref, work.at[:, begin : begin + ref.shape[1]]),), sems, len(incoming)
        )
    row_ids = lax.broadcasted_iota(jnp.int32, (AGAIN, TILE), 0)
    lane = lax.broadcasted_iota(jnp.int32, (AGAIN, LANES), 1)
    start = tuple(jnp.zeros((1, TILE), jnp.float32) for _ in range(4))

    def halves(value):
        return value[:, :LANES], value[:, LANES:]

    def right_of(value):
        low, high = (pltpu.roll(part, LANES - 1, 1) for part in halves(value))
        return jnp.concatenate([jnp.where(lane == LANES - 1, high, low), high], 1)

    def left_of(value):
        low, high = (pltpu.roll(part, 1, 1) for part in halves(value))
        return jnp.concatenate([low, jnp.where(lane == 0, low, high)], 1)

    def down(value):
        return pltpu.roll(value, AGAIN + 7, 0)[:AGAIN]

    for step in range(STEPS):
        source, target = (work, other) if step % 2 == 0 else (other, work)
        delta = deltas[step][0:1, :]
        wet_now = flag(ctl, wet_from + step)

        def group(index, carry, source=source, target=target, delta=delta, wet_now=wet_now):
            base = pl.multiple_of(index * AGAIN, AGAIN)
            rows = pl.ds(base, AGAIN)
            after = pl.ds(pl.multiple_of(jnp.minimum(base + AGAIN, EARLY - 8), 8), 8)
            refs = [source.at[field] for field in range(3)] + [work.at[3]]
            fields = [jnp.concatenate([ref[rows, :], ref[after, :]], 0) for ref in refs]
            cells_x, cells_y = cell(*fields[:3])
            here_x = tuple(value[:AGAIN] for value in cells_x)
            here_y = tuple(value[:AGAIN] for value in cells_y)
            faces_x = face(here_x, tuple(down(value) for value in cells_x))
            turned = tuple(pltpu.roll(value, 1, 0) for value in faces_x)
            change_x = tuple(
                value - jnp.where(row_ids == 0, before, moved)
                for value, before, moved in zip(faces_x, carry[:3], turned)
            )
            ground = fields[3][:AGAIN]
            ground_up = pltpu.roll(ground, 1, 0)
            slope_x = down(fields[3]) - jnp.where(row_ids == 0, carry[3], ground_up)
            carried = tuple(value[0:1, :] for value in turned) + (ground_up[0:1, :],)
            faces_y = face(here_y, tuple(right_of(value) for value in here_y))
            change_y = tuple(value - left_of(value) for value in faces_y)
            slope_y = right_of(ground) - left_of(ground)
            old = tuple(value[:AGAIN] for value in fields[:3])
            weight = SLOPE * old[0]
            slopes = (
                SCALE * (change_x[0] + change_y[0]),
                SCALE * (change_x[1] + change_y[2]) + weight * slope_x,
                SCALE * (change_x[2] + change_y[1]) + weight * slope_y,
            )
            for field, value in enumerate(
                moved_on(old, slopes, work[4, rows, :], delta, wet_now)
            ):
                target[field, rows, :] = value
            return carried

        if step == 0:
            wait_all(incoming)
        lax.fori_loop(0, EARLY // AGAIN, group, start)


def late_rows(tile, late):
    row = sublanes()
    kept = EARLY - 8
    lane = lax.broadcasted_iota(jnp.int32, (8, LANES), 1)
    for field in range(3):
        late[field, 0:8, :] = jnp.where(
            row < 3, tile[field, 0:8, :], tile[field, kept : kept + 8, :]
        )
        packed = [jnp.zeros((8, LANES), jnp.float32)] * 2
        for block in range(EARLY // 8):
            rows = slice(8 * block, 8 * block + 8)
            sides = jnp.where(lane < 64, tile[field, rows, :LANES], tile[field, rows, LANES:])
            turned = pltpu.roll(sides, (3 + 8 * block) % LANES, 1)
            which = block // 16
            packed[which] = jnp.where(lane // 8 == block % 16, turned, packed[which])
        late[field, 8:16, :] = jnp.concatenate(packed, 1)
        late[field, 16:, :] = tile[field, EARLY:, :]


def merge(late, early, tile):
    for field in range(3):
        merge_field(field, late, early, tile)


def merge_field(field, late, early, tile):
    row = sublanes()
    lane = lax.broadcasted_iota(jnp.int32, (8, LANES), 1)
    first = late[field, 0:8, :]
    for block in range(EARLY // 8):
        rows = slice(8 * block, 8 * block + 8)
        which = block // 16
        packed = late[field, 8:16, which * LANES : (which + 1) * LANES]
        sides = pltpu.roll(packed, (-3 - 8 * block) % LANES, 1)
        value = early[field, rows, :]
        value = jnp.concatenate(
            [
                jnp.where(lane < 3, sides, value[:, :LANES]),
                jnp.where(lane >= LANES - 3, sides, value[:, LANES:]),
            ],
            1,
        )
        if block == 0:
            value = jnp.where(row < 3, first, value)
        if block == EARLY // 8 - 1:
            value = jnp.where(row < 5, value, first)
        tile[field, rows, :] = value
    tile[field, EARLY:, :] = late[field, 16:, :]


def repeat_second(ctl, delta0, delta1, delta2, low, high, late, out, late_out, work, tile, sems):
    near = start_all(((late, late_out),), sems, 2)
    repeat_steps(ctl, WET_SECOND, (delta0, delta1, delta2), (low, high), work, tile, sems)
    wait_all(start_all(((tile, out),), sems) + near)


def repeat_first(
    ctl, delta0, delta1, delta2, low, high, late_in, staying, out, work, other, tile, late, sems
):
    rest = out.at[1 - ctl[MOVE + 1]]
    again = ctl[MOVE] == ctl[MOVE + 1]

    @pl.when(again)
    def _():
        wait_all(start_all(((staying, tile),), sems))

    @pl.when(jnp.logical_not(again))
    def _():
        copies = start_all(((late_in, late),), sems, 2)
        repeat_steps(ctl, WET_FIRST, (delta0, delta1, delta2), (low, high), work, other, sems)
        wait_all(copies)
        merge(late, other, tile)

    wait_all(start_all(((tile, rest),), sems))


def finish(ctl, late, early, before, out, tile, sems):
    del before
    copies = []
    for field in range(3):
        merge_field(field, late, early, tile)
        copies += start_all(
            ((tile.at[field], out.at[ctl[MOVE + 1], field]),), sems, field
        )
    wait_all(copies)


def second_late(ctl, arrived, own, order, leaving):
    del order
    again = ctl[MOVE] == ctl[MOVE + 1]
    for field in range(3):
        leaving[field] = jnp.where(again, arrived[field], own[field])


def correct_rows(ctl, slot, got, ground, state, rate, bottom):
    position = jnp.where(ctl[SLOT_LOW] == slot, 0, 1)
    device = lax.axis_index("xb") * 2 + lax.axis_index("yb")
    wall = WALL_WEST if bottom else WALL_EAST

    @pl.when(jnp.logical_not(flag(ctl, wall + position)))
    def _():
        peer = device - 2 if bottom else device + 2
        block = pl.ds(pl.multiple_of(peer * 8, 8), 8)
        lines = got[block, :TILE]
        grounds = ground[block, :TILE]
        stride = 4 if got.shape[1] > TILE else 3

        def line(offset):
            other = offset + stride
            picked = jnp.where(
                position == 0, lines[offset : offset + 1, :], lines[other : other + 1, :]
            )
            return jnp.broadcast_to(picked, (8, TILE))

        ghost, _ = cell(*(line(field) for field in range(3)))
        ghost_ground = jnp.where(position == 0, grounds[3:4, :], grounds[7:8, :])
        rows = slice(0, 8) if bottom else slice(TILE - 8, TILE)
        own = [state[slot, field, rows, :] for field in range(3)]
        here, _ = cell(*own)
        fluxes = face(ghost, here) if bottom else face(here, ghost)
        push = SCALE * fluxes[1] + (SLOPE * own[0]) * ghost_ground
        row = sublanes()
        sign = -1.0 if bottom else 1.0
        chosen = row == (0 if bottom else 7)
        for field, value in enumerate((SCALE * fluxes[0], push, SCALE * fluxes[2])):
            rate[slot, field, rows, :] += jnp.where(chosen, sign * value, 0.0)


def column_fix(got, ground, columns):
    upper = lax.axis_index("yb")
    device = lax.axis_index("xb") * 2 + upper
    peer = device + 1 - 2 * upper
    block = pl.ds(pl.multiple_of(peer * 8, 8), 8)
    lines = got[block, :TILE]
    ghost_ground = ground[block, :TILE][3:4]
    mine = columns[...]
    _, ghost = cell(lines[0:1], lines[1:2], lines[2:3])
    _, own = cell(mine[0:1], mine[1:2], mine[2:3])
    low = upper == 0
    left = tuple(jnp.where(low, a, b) for a, b in zip(own, ghost))
    right = tuple(jnp.where(low, b, a) for a, b in zip(own, ghost))
    fluxes = face(left, right)
    sign = jnp.where(low, 1.0, -1.0)
    push = SCALE * fluxes[1] + (SLOPE * mine[0:1]) * ghost_ground
    block8 = stacked(
        [sign * SCALE * fluxes[0], sign * SCALE * fluxes[2], sign * push],
        jnp.zeros((8, TILE), jnp.float32),
    )
    return jnp.transpose(
        jnp.concatenate([block8, jnp.zeros((LANES - 8, TILE), jnp.float32)], 0)
    )


def last_update(moving, ctl, got, ground, columns, state, manning, rate, order, *rest):
    del order
    slot = ctl[MOVE] if moving else 1 - ctl[MOVE]
    update(STEPS - 1, ctl, got, ground, columns, state, manning, rate, *rest, slots=(slot,))


def update(
    step, ctl, got_in, ground_in, columns_in, state_in, manning_in, rate_in, *rest,
    passing=None, slots=(0, 1),
):
    more = step + 1 < STEPS
    fresh_out, first_out, second_out, delta_out = rest[:4]
    rest = rest[4:]
    state, manning, rate, fresh, got, ground, columns, first, second, delta_keep, sems = rest
    out, columns_out = first, second
    small = start_all(
        ((got_in, got), (ground_in, ground), (columns_in, columns)), sems, 5 * PARTS
    )
    size = 2 * TILE // PARTS
    parts = [
        (slot, slice(k * size, (k + 1) * size)) for slot in slots for k in range(PARTS // 2)
    ]
    incoming = []
    for index, (slot, rows) in enumerate(parts):
        incoming.append(
            start_all(
                (
                    (rate_in.at[slot, :, rows], rate.at[slot, :, rows]),
                    (state_in.at[slot, :, rows], state.at[slot, :, rows]),
                    (manning_in.at[slot, rows], manning.at[slot, rows]),
                ),
                sems,
                3 * index,
            )
        )
    wait_all(small)
    upper = lax.axis_index("yb")
    devices = 2 * lax.axis_size("xb")
    begin = TILE if got.shape[1] > TILE else 0
    tops = got[0:8, begin : begin + LANES]
    for peer in range(1, devices):
        tops = jnp.maximum(tops, got[peer * 8 : peer * 8 + 8, begin : begin + LANES])
    delta = (COURANT * SPACING) / tops[TOP : TOP + 1, :]
    delta = jnp.concatenate([delta, delta], 1)
    delta_keep[...] = jnp.broadcast_to(delta, (8, TILE))
    outgoing = start_all(((delta_keep, delta_out),), sems, 5 * PARTS + 3)
    fix = column_fix(got, ground, columns)
    facing = jnp.where(upper > 0, ctl[SLOT_LOW], 1 - ctl[SLOT_LOW])
    begin = pl.multiple_of((1 - upper) * LANES, LANES)
    goal = (1 - upper) * (LANES - 1)
    lane = lax.broadcasted_iota(jnp.int32, (size, LANES), 1)
    total = jnp.zeros((ROWS, TILE), jnp.float32)
    for index, (slot, part_rows) in enumerate(parts):
        wait_all(incoming[index])
        if part_rows.start == 0:
            correct_rows(ctl, slot, got, ground, state, rate, True)
        if part_rows.stop == TILE:
            correct_rows(ctl, slot, got, ground, state, rate, False)

        @pl.when(facing == slot)
        def _(slot=slot, part_rows=part_rows):
            for field in range(3):
                turned = pltpu.roll(
                    fix[part_rows], lax.rem(goal + LANES - field, LANES), 1
                )
                rate[slot, field, part_rows, pl.ds(begin, LANES)] += jnp.where(
                    lane == goal, turned, 0.0
                )

        wet_now = flag(ctl, WET + 2 * step + slot)

        def group(index, best, slot=slot, wet_now=wet_now):
            rows = pl.ds(pl.multiple_of(index * ROWS, ROWS), ROWS)
            old = tuple(state[slot, field, rows, :] for field in range(3))
            slopes = tuple(rate[slot, field, rows, :] for field in range(3))
            h, hu, hv = moved_on(old, slopes, manning[slot, rows, :], delta, wet_now)
            fresh[slot, 0, rows, :] = h
            fresh[slot, 1, rows, :] = hu
            fresh[slot, 2, rows, :] = hv
            if more:
                along_x, along_y = cell(h, hu, hv)
                best = jnp.maximum(best, jnp.maximum(along_x[5], along_y[5]))
            return best

        best = lax.fori_loop(
            part_rows.start // ROWS,
            part_rows.stop // ROWS,
            group,
            jnp.zeros((ROWS, TILE), jnp.float32),
        )
        if more:
            best = jnp.where(flag(ctl, WET + 2 * step + 2 + slot), best, 0.0)
            total = jnp.maximum(total, best)
        target = fresh_out.at[slot, :, part_rows] if more else fresh_out.at[:, part_rows]
        outgoing += start_all(
            ((fresh.at[slot, :, part_rows], target),), sems, 3 * PARTS + index
        )
        if passing and index == PARTS // 2:
            passing.middle()
    if more:
        messages(ctl, fresh, None, jnp.max(total, keepdims=True), out, columns_out)
        outgoing += start_all(((out, first_out), (columns_out, second_out)), sems, 4 * PARTS)
    else:
        second[...] = jnp.zeros_like(second)
        late_rows(fresh.at[slots[0]], first)
        outgoing += start_all(((first, first_out), (second, second_out)), sems, 4 * PARTS)
    wait_all(outgoing)


def vmem():
    return pl.BlockSpec(memory_space=pltpu.VMEM)


def smem():
    return pl.BlockSpec(memory_space=pltpu.SMEM)


def hbm():
    return pl.BlockSpec(memory_space=pltpu.HBM)


def anywhere():
    return pl.BlockSpec(memory_space=pl.ANY)


def call(
    kernel, outs, out_specs, in_specs, flops, scratch=(), aliases=None, room=VMEM_BYTES, moved=4
):
    return pl.pallas_call(
        kernel,
        scratch_shapes=scratch,
        input_output_aliases=aliases or {},
        out_shape=outs,
        in_specs=in_specs,
        out_specs=out_specs,
        compiler_params=pltpu.CompilerParams(vmem_limit_bytes=room),
        cost_estimate=pl.CostEstimate(flops=flops, bytes_accessed=moved << 20, transcendentals=0),
    )


def f32(*shape):
    return jax.ShapeDtypeStruct(shape, jnp.float32)


def spread(fast):
    return lax.all_to_all(fast, ("xb", "yb"), split_axis=0, concat_axis=0, tiled=True)


def body(state, bed, manning, neighbours, wet, moves):
    shape = f32(*state.shape)
    devices = lax.axis_size("xb") * lax.axis_size("yb")
    whole = pltpu.VMEM(state.shape, jnp.float32)
    part = pltpu.VMEM(bed.shape, jnp.float32)
    tile_shape = f32(*state.shape[1:])
    early_shape = f32(5, EARLY, TILE)
    early_state = f32(3, EARLY, TILE)
    late_shape = f32(3, LATE, TILE)
    delta_shape = f32(8, TILE)

    def buffer(like):
        return pltpu.VMEM(like.shape, jnp.float32)

    piece_shapes = tuple(f32(5, end - begin, TILE) for begin, end in PIECES)
    out, columns, ctl, *leaving = call(
        opening,
        (
            f32(8 * devices, TILE + LANES),
            f32(8, TILE),
            jax.ShapeDtypeStruct((CONTROLS,), jnp.int32),
        )
        + piece_shapes,
        (vmem(), vmem(), smem(), hbm(), hbm()),
        [hbm()] * 6,
        4 << 20,
        [
            whole,
            part,
            pltpu.VMEM((EARLY, TILE), jnp.float32),
            pltpu.SMEM(neighbours.shape[::-1], jnp.int32),
            pltpu.SMEM(wet.shape, jnp.int32),
            pltpu.SMEM(moves.shape, jnp.int32),
            pltpu.SemaphoreType.DMA((13,)),
        ],
    )(state, bed, manning, neighbours.T, wet, moves)
    state_first = state
    ground = None
    deltas = []
    for step in range(STEPS):
        got = spread(out)
        ground = got if step == 0 else ground
        scratch = [whole, part, whole, pltpu.SemaphoreType.DMA((3 * CHUNKS,))]
        piece_scratch = [
            [buffer(piece), pltpu.SemaphoreType.DMA((2,))] for piece in piece_shapes
        ]
        if step == 1:
            rate, leaving = call(
                rates_and_leaving,
                (shape, piece_shapes[0]),
                (hbm(),) * 2,
                [smem()] + [hbm()] * 5,
                16 << 20,
                scratch + piece_scratch[0],
            )(ctl, state, bed, state_first, manning, early_first[0])
            early_second = [shifted(leaving, "xb", 1)]
        elif step == 2:
            rate = call(rates_after, shape, hbm(), [smem()] + [hbm()] * 3, 16 << 20, scratch)(
                ctl, state, bed, early_second[0]
            )
        else:
            rate = call(rates, shape, hbm(), [smem(), hbm(), hbm()], 16 << 20, scratch)(
                ctl, state, bed
            )
            held = call(
                hold, piece_shapes[0], hbm(), [hbm()] * 3, 1 << 10, aliases={2: 0}
            )(rate, got, leaving[0])
            early_first = [shifted(held, "xb", 1)]
        more = step + 1 < STEPS
        shapes = (f32(8 * devices, TILE) if more else late_shape), f32(8, TILE)
        passing = step == 1
        work = [
            whole,
            part,
            whole,
            whole,
            pltpu.VMEM(got.shape, jnp.float32),
            pltpu.VMEM(ground.shape, jnp.float32),
            pltpu.VMEM((8, TILE), jnp.float32),
            buffer(shapes[0]),
            buffer(shapes[1]),
            buffer(delta_shape),
            pltpu.SemaphoreType.DMA((5 * PARTS + 4,)),
        ]
        operands = ctl, got, ground, columns, state, manning, rate
        if not more:
            break
        outs = call(
            functools.partial(update_and_leaving if passing else update, step),
            (shape,) + shapes + (delta_shape,) + ((piece_shapes[1],) if passing else ()),
            (hbm(),) * (5 if passing else 4),
            [smem()] + [hbm()] * (9 if passing else 6),
            8 << 20,
            work + (piece_scratch[1] if passing else []),
            moved=10,
        )(*operands, *((state_first, bed, early_first[1]) if passing else ()))
        state, out, columns, delta, *passed = outs
        deltas.append(delta)
        if step == 0:
            held = call(
                hold, piece_shapes[1], hbm(), [hbm()] * 3, 1 << 10, aliases={2: 0}
            )(delta, delta, leaving[1])
            early_first.append(shifted(held, "xb", 1))
        elif step == 1:
            early_second.append(shifted(passed[0], "xb", 1))

    def finish_step(moving, order):
        return call(
            functools.partial(last_update, moving),
            (tile_shape,) + shapes + (delta_shape,),
            (hbm(),) * 4,
            [smem()] + [hbm()] * 7,
            8 << 20,
            work,
            moved=10,
        )(*operands, order)

    _, late_first, _, delta = finish_step(True, early_second[1])
    staying, late_second, _, _ = finish_step(False, delta)
    deltas.append(delta)
    room = 16 << 20
    late_arrived = shifted(late_first, "xb", 1)
    second, late_second = call(
        repeat_second,
        (early_state, late_shape),
        (anywhere(), vmem()),
        [smem()] + [vmem()] * 3 + [anywhere()] * 3,
        8 << 20,
        [buffer(early_shape), buffer(early_state), pltpu.SemaphoreType.DMA((3,))],
        room=room,
    )(ctl, *deltas, *early_second, late_second)
    leaving = call(
        second_late,
        late_shape,
        vmem(),
        [smem(), vmem(), vmem(), anywhere()],
        1 << 10,
        room=room,
    )(ctl, late_arrived, late_second, second)
    late_next = shifted(leaving, "xb", 1)
    final = call(
        repeat_first,
        shape,
        hbm(),
        [smem()] + [vmem()] * 3 + [anywhere()] * 4,
        8 << 20,
        [
            buffer(early_shape),
            buffer(early_state),
            buffer(tile_shape),
            buffer(late_shape),
            pltpu.SemaphoreType.DMA((3,)),
        ],
        room=room,
    )(ctl, *deltas, *early_first, late_arrived, staying)
    return call(
        finish,
        shape,
        hbm(),
        [smem(), vmem(), vmem(), hbm()],
        1 << 20,
        [buffer(tile_shape), pltpu.SemaphoreType.DMA((3,))],
        {3: 0},
        room=room,
    )(ctl, late_next, second, final)


def solution(mesh):
    placed = (
        P(("runs", "xb", "yb"), None, None, None),
        P(("runs", "xb", "yb"), None, None),
        P(("runs", "xb", "yb"), None, None),
        P("runs", None),
        P(None, "runs"),
        P(None, "runs"),
    )
    return jax.shard_map(
        body,
        mesh=mesh,
        in_specs=placed,
        out_specs=P(("runs", "xb", "yb"), None, None, None),
        check_vma=False,
    )
```

```python
import functools

import jax
import jax.numpy as jnp
from jax import lax
from jax.experimental import pallas as pl
from jax.experimental.pallas import tpu as pltpu
from jax.sharding import PartitionSpec as P

STEPS = 3
GRAVITY = 9.81
ROOT_G = GRAVITY**0.5
SPACING = 5.0
COURANT = 0.2
ROWS = 32
LANES = 128
TILE = 256
VMEM_BYTES = 60 * 1024 * 1024
SLOT_LOW, WALL_WEST, WALL_EAST, WALL_OUTER, WET, MOVE = 0, 1, 3, 5, 7, 13
WET_FIRST, WET_SECOND = 16, 19
CONTROLS = 24
EARLY = 160
PIECES = ((0, 72), (72, 160))
AGAIN = 32
LATE = TILE - EARLY + 16
CHUNKS = 8
PARTS = 8
STRIP = 16
TOP = 6
SCALE = 0.5 / SPACING
SLOPE = GRAVITY / (2.0 * SPACING)


def shifted(value, axis, steps, around=True):
    count = lax.axis_size(axis)
    pairs = [(source, (source + steps) % count) for source in range(count)]
    if not around:
        pairs = [pair for pair in pairs if abs(pair[0] - pair[1]) == abs(steps)]
    return lax.ppermute(value, axis, pairs)


def cell(h, hu, hv):
    root = lax.rsqrt(h)
    inverse = root * root
    u = hu * inverse
    v = hv * inverse
    celerity = ROOT_G * (h * root)
    pressure = (0.5 * GRAVITY) * (h * h)
    cross = hu * v
    speed_x = jnp.abs(u) + celerity
    speed_y = jnp.abs(v) + celerity
    along_x = (h, hu, hv, hu * u + pressure, cross, speed_x)
    along_y = (h, hv, hu, hv * v + pressure, cross, speed_y)
    return along_x, along_y


def face(left, right):
    wave = jnp.maximum(left[5], right[5])
    return (
        (left[1] + right[1]) - wave * (right[0] - left[0]),
        (left[3] + right[3]) - wave * (right[1] - left[1]),
        (left[4] + right[4]) - wave * (right[2] - left[2]),
    )


def slot_of(ctl, position):
    low = ctl[SLOT_LOW]
    return low if position == 0 else 1 - low


def flag(ctl, index):
    return ctl[index] > 0


def start_all(pairs, sems, first=0):
    copies = [
        pltpu.make_async_copy(src, dst, sems.at[first + k]) for k, (src, dst) in enumerate(pairs)
    ]
    for copy in copies:
        copy.start()
    return copies


def wait_all(copies):
    for copy in copies:
        copy.wait()


def sublanes(width=TILE):
    return lax.broadcasted_iota(jnp.int32, (8, width), 0)


def stacked(lines, base):
    row = sublanes()
    for index, line in enumerate(lines):
        base = jnp.where(row == index, jnp.broadcast_to(line, (8, TILE)), base)
    return base


def messages(ctl, state, bed, fastest, out, columns):
    upper = lax.axis_index("yb")
    column = lax.axis_index("xb")
    last = lax.axis_size("xb") - 1
    devices = 2 * (last + 1)
    device = column * 2 + upper
    top = jnp.broadcast_to(fastest, (8, TILE))
    for peer in range(devices):
        out[peer * 8 : peer * 8 + 8, :TILE] = top
        if bed is not None:
            out[peer * 8 : peer * 8 + 8, TILE:] = top[:, :LANES]
    row = sublanes()

    def edge(line):
        rows = slice(line, line + 1)
        lines = []
        for position in range(2):
            slot = slot_of(ctl, position)
            lines += [state[slot, field, rows, :] for field in range(3)]
            if bed is not None:
                lines.append(bed[slot, rows, :])
        return stacked(lines, top)

    for inside, peer, line in (
        (column > 0, device - 2, 0),
        (column < last, device + 2, TILE - 1),
    ):

        @pl.when(inside)
        def _(peer=peer, line=line):
            out[pl.ds(pl.multiple_of(peer * 8, 8), 8), :TILE] = edge(line)

    slot = jnp.where(upper > 0, ctl[SLOT_LOW], 1 - ctl[SLOT_LOW])
    begin = pl.multiple_of((1 - upper) * LANES, LANES)
    lane = lax.broadcasted_iota(jnp.int32, (TILE, LANES), 1)
    packed = None
    for field in range(4 if bed is not None else 3):
        if field < 3:
            part = state[slot, field, :, pl.ds(begin, LANES)]
        else:
            part = bed[slot, :, pl.ds(begin, LANES)]
        turned = pltpu.roll(part, field + 1 - upper, 1)
        packed = turned if field == 0 else jnp.where(lane == field, turned, packed)
    lines = jnp.transpose(packed)[:8]
    columns[...] = lines
    start = pl.multiple_of((device + 1 - 2 * upper) * 8, 8)
    out[pl.ds(start, 8), :TILE] = jnp.where(row == TOP, top, lines)


def opening(
    state_in, bed_in, neighbours_in, wet_in, moves_in,
    out, columns, ctl,
    state, bed, neighbours, wet, moves, sems,
):
    copies = start_all(
        (
            (neighbours_in, neighbours),
            (wet_in, wet),
            (moves_in, moves),
            (state_in.at[0], state.at[0]),
            (state_in.at[1], state.at[1]),
            (bed_in, bed),
        ),
        sems,
    )
    device = lax.axis_index("xb") * 2 + lax.axis_index("yb")
    wait_all(copies[:3])
    first = device * 2
    low = jnp.where(neighbours[3, first] == first + 1, 0, 1)
    ctl[SLOT_LOW] = low
    for position in range(2):
        slot = low if position == 0 else 1 - low
        tile = first + slot
        ctl[WALL_WEST + position] = (neighbours[0, tile] < 0).astype(jnp.int32)
        ctl[WALL_EAST + position] = (neighbours[1, tile] < 0).astype(jnp.int32)
        ctl[WALL_OUTER + position] = (neighbours[2 + position, tile] < 0).astype(jnp.int32)
    for step in range(STEPS):
        for slot in range(2):
            ctl[WET + 2 * step + slot] = wet[step, first + slot]
        ctl[MOVE + step] = moves[step, device]
    count = lax.axis_size("xb")
    upper = lax.axis_index("yb")
    column = lax.axis_index("xb")
    source = lax.rem(column + count - 1, count) * 2 + upper
    before = lax.rem(column + count - 2, count) * 2 + upper
    again = moves[0, source] == moves[1, source]
    tile_first = source * 2 + moves[0, source]
    tile_second = jnp.where(
        again, before * 2 + moves[0, before], source * 2 + 1 - moves[0, source]
    )
    for step in range(STEPS):
        ctl[WET_FIRST + step] = wet[step, tile_first]
        ctl[WET_SECOND + step] = wet[step, tile_second]

    total = jnp.zeros((ROWS, TILE), jnp.float32)
    for slot in range(2):
        copies[3 + slot].wait()

        def group(index, best, slot=slot):
            rows = pl.ds(pl.multiple_of(index * ROWS, ROWS), ROWS)
            along_x, along_y = cell(*(state[slot, field, rows, :] for field in range(3)))
            return jnp.maximum(best, jnp.maximum(along_x[5], along_y[5]))

        best = lax.fori_loop(0, TILE // ROWS, group, jnp.zeros((ROWS, TILE), jnp.float32))
        total = jnp.maximum(total, jnp.where(wet[0, first + slot] > 0, best, 0.0))
    copies[5].wait()
    messages(ctl, state, bed, jnp.max(total, keepdims=True), out, columns)


def hold(first, second, leaving, same):
    del first, second, leaving, same


class Splitting:
    def __init__(self, ctl, state_in, bed_in, manning_in, leaving, buffer, sems):
        slot = ctl[MOVE]
        rows = slice(0, EARLY)
        pairs = (
            (state_in.at[slot, :, rows], buffer.at[0:3]),
            (bed_in.at[slot, rows], buffer.at[3]),
            (manning_in.at[slot, rows], buffer.at[4]),
        )
        self.incoming = [
            pltpu.make_async_copy(src, dst, sems.at[k]) for k, (src, dst) in enumerate(pairs)
        ]
        self.outgoing = [
            pltpu.make_async_copy(buffer.at[:, begin:end], piece, sems.at[3 + k])
            for k, ((begin, end), piece) in enumerate(zip(PIECES, leaving))
        ]

    def start(self):
        for copy in self.incoming:
            copy.start()

    def middle(self):
        wait_all(self.incoming)
        for copy in self.outgoing:
            copy.start()

    def end(self):
        wait_all(self.outgoing)


class Passing:
    def __init__(self, ctl, piece, state_in, bed_in, manning_in, arrived, leaving, buffer, sems):
        self.again = ctl[MOVE] == ctl[MOVE + 1]
        self.other = 1 - ctl[MOVE]
        self.rows = slice(*piece)
        self.refs = state_in, bed_in, manning_in
        self.incoming = pltpu.make_async_copy(arrived, buffer, sems.at[0])
        self.outgoing = pltpu.make_async_copy(buffer, leaving, sems.at[1])
        self.buffer = buffer
        self.sem = sems.at[0]

    def start(self):
        state_in, bed_in, manning_in = self.refs
        buffer, sem, rows = self.buffer, self.sem, self.rows

        @pl.when(self.again)
        def _():
            self.incoming.start()

        @pl.when(jnp.logical_not(self.again))
        def _():
            pltpu.make_async_copy(state_in.at[self.other, :, rows], buffer.at[0:3], sem).start()
            pltpu.make_async_copy(bed_in.at[self.other, rows], buffer.at[3], sem).start()
            pltpu.make_async_copy(manning_in.at[self.other, rows], buffer.at[4], sem).start()

    def middle(self):
        self.incoming.wait()
        self.outgoing.start()

    def end(self):
        self.outgoing.wait()


def rates_and_splitting(
    ctl, state_in, bed_in, manning_in, rate_out, leaving_low, leaving_high,
    state, bed, rate, sems, buffer, moving,
):
    leaving = leaving_low, leaving_high
    splitting = Splitting(ctl, state_in, bed_in, manning_in, leaving, buffer, moving)
    rates(ctl, state_in, bed_in, rate_out, state, bed, rate, sems, splitting)


def rates_and_leaving(
    ctl, state_in, bed_in, state_first, manning_in, arrived, rate_out, leaving,
    state, bed, rate, sems, buffer, moving,
):
    passing = Passing(
        ctl, PIECES[0], state_first, bed_in, manning_in, arrived, leaving, buffer, moving
    )
    rates(ctl, state_in, bed_in, rate_out, state, bed, rate, sems, passing)


def update_and_leaving(
    step, ctl, got_in, ground_in, columns_in, state_in, manning_in, rate_in,
    state_first, bed_in, arrived, fresh_out, first_out, second_out, delta_out, leaving, *rest
):
    *rest, buffer, moving = rest
    passing = Passing(
        ctl, PIECES[1], state_first, bed_in, manning_in, arrived, leaving, buffer, moving
    )
    passing.start()
    update(
        step, ctl, got_in, ground_in, columns_in, state_in, manning_in, rate_in,
        fresh_out, first_out, second_out, delta_out, *rest, passing=passing,
    )
    passing.end()


def rates_after(ctl, state_in, bed_in, order, *rest):
    del order
    rates(ctl, state_in, bed_in, *rest)


def rates(ctl, state_in, bed_in, rate_out, state, bed, rate, sems, passing=None):
    width = 2 * TILE
    row_ids = lax.broadcasted_iota(jnp.int32, (STRIP, width), 0)
    row8 = sublanes(width)
    lane = lax.broadcasted_iota(jnp.int32, (STRIP, LANES), 1)
    last = TILE // STRIP - 1
    chunk = TILE // CHUNKS
    slots = [slot_of(ctl, position) for position in range(2)]
    incoming = []
    for part in range(CHUNKS):
        rows = slice(part * chunk, (part + 1) * chunk)
        incoming.append(
            start_all(
                (
                    (state_in.at[:, :, rows], state.at[:, :, rows]),
                    (bed_in.at[:, rows], bed.at[:, rows]),
                ),
                sems,
                2 * part,
            )
        )
    if passing:
        passing.start()
    keep_west, keep_east, keep_south, keep_north = (
        jnp.where(flag(ctl, index), 1.0, 0.0)
        for index in (WALL_WEST, WALL_EAST, WALL_OUTER, WALL_OUTER + 1)
    )

    def strip(field, rows):
        if field == 3:
            return jnp.concatenate([bed[slot, rows, :] for slot in slots], 1)
        return jnp.concatenate([state[slot, field, rows, :] for slot in slots], 1)

    def blocks(value):
        return [value[:, k * LANES : (k + 1) * LANES] for k in range(4)]

    def right_of(value, end=None):
        turned = [pltpu.roll(part, LANES - 1, 1) for part in blocks(value)]
        after = turned[1:] + [turned[3] if end is None else end]
        return jnp.concatenate(
            [
                jnp.where(lane == LANES - 1, following, part)
                if following is not part
                else part
                for part, following in zip(turned, after)
            ],
            1,
        )

    def left_of(value, end):
        turned = [pltpu.roll(part, 1, 1) for part in blocks(value)]
        before = [end] + turned[:3]
        return jnp.concatenate(
            [jnp.where(lane == 0, previous, part) for part, previous in zip(turned, before)], 1
        )

    def down(value):
        return pltpu.roll(value, STRIP + 7, 0)[:STRIP]

    def group(index, carry):
        base = pl.multiple_of(index * STRIP, STRIP)
        rows = pl.ds(base, STRIP)
        after = pl.ds(pl.multiple_of(jnp.minimum(base + STRIP, TILE - 8), 8), 8)
        at_end = index == last
        fields = [
            jnp.concatenate([strip(field, rows), strip(field, after)], 0) for field in range(3)
        ]
        cells_x, cells_y = cell(*fields)
        here_x = tuple(value[:STRIP] for value in cells_x)
        here_y = tuple(value[:STRIP] for value in cells_y)

        ending = jnp.logical_and(row8 == 7, at_end)
        faces = list(face(here_x, tuple(down(value) for value in cells_x)))
        wall = keep_east * (2.0 * (here_x[3] + here_x[5] * here_x[1])[STRIP - 8 :])
        for component, value in enumerate((0.0, wall, 0.0)):
            upper = faces[component]
            faces[component] = jnp.concatenate(
                [upper[: STRIP - 8], jnp.where(ending, value, upper[STRIP - 8 :])], 0
            )
        turned = tuple(pltpu.roll(value, 1, 0) for value in faces)
        change_x = tuple(
            value - jnp.where(row_ids == 0, before, moved)
            for value, before, moved in zip(faces, carry[:3], turned)
        )
        ground = strip(3, rows)
        ground_after = jnp.where(
            at_end,
            jnp.broadcast_to(keep_east * ground[STRIP - 1 :], (8, width)),
            strip(3, after),
        )
        ground_up = pltpu.roll(ground, 1, 0)
        slope_x = down(jnp.concatenate([ground, ground_after], 0)) - jnp.where(
            row_ids == 0, carry[3], ground_up
        )
        carried = tuple(value[0:1, :] for value in turned) + (ground_up[0:1, :],)

        faces_y = list(face(here_y, tuple(right_of(value) for value in here_y)))
        normal = here_y[3]
        spread_y = here_y[5] * here_y[1]
        north = keep_north * (2.0 * (normal + spread_y)[:, width - LANES :])
        south = keep_south * (2.0 * (normal - spread_y)[:, :LANES])
        change_y = []
        for component, (high, low) in enumerate(((0.0, 0.0), (north, south), (0.0, 0.0))):
            parts = blocks(faces_y[component])
            parts[3] = jnp.where(lane == LANES - 1, high, parts[3])
            value = jnp.concatenate(parts, 1)
            change_y.append(value - left_of(value, low))
        slope_y = right_of(ground, keep_north * ground[:, width - LANES :]) - left_of(
            ground, keep_south * ground[:, :LANES]
        )
        weight = SLOPE * here_x[0]
        results = (
            SCALE * (change_x[0] + change_y[0]),
            SCALE * (change_x[1] + change_y[2]) + weight * slope_x,
            SCALE * (change_x[2] + change_y[1]) + weight * slope_y,
        )
        for field, value in enumerate(results):
            for position, slot in enumerate(slots):
                rate[slot, field, rows, :] = value[:, position * TILE : (position + 1) * TILE]
        return carried

    wait_all(incoming[0])
    top, _ = cell(*(strip(field, slice(0, 8)) for field in range(3)))
    nothing = jnp.zeros((1, width), jnp.float32)
    carry = (
        nothing,
        keep_west * (2.0 * (top[3] - top[5] * top[1])[0:1]),
        nothing,
        keep_west * strip(3, slice(0, 8))[0:1],
    )
    per_chunk = chunk // STRIP
    outgoing = []
    for part in range(CHUNKS):
        if part + 1 < CHUNKS:
            wait_all(incoming[part + 1])
        carry = lax.fori_loop(part * per_chunk, (part + 1) * per_chunk, group, carry)
        rows = slice(part * chunk, (part + 1) * chunk)
        outgoing += start_all(
            ((rate.at[:, :, rows], rate_out.at[:, :, rows]),), sems, 2 * CHUNKS + part
        )
        if passing and part == CHUNKS // 2:
            passing.middle()
    wait_all(outgoing)
    if passing:
        passing.end()


def moved_on(old, slopes, rough, delta, wet_now):
    h, hu, hv = (value - delta * slope for value, slope in zip(old, slopes))
    inverse = 1.0 / h
    u = hu * inverse
    v = hv * inverse
    speed = jnp.sqrt(u * u + v * v)
    power = jnp.exp((-4.0 / 3.0) * jnp.log(jnp.abs(h)))
    drag = (GRAVITY * delta) * (rough * rough) * (speed * power)
    factor = 1.0 / (1.0 + drag)
    fresh = (h, hu * factor, hv * factor)
    return tuple(jnp.where(wet_now, new, value) for new, value in zip(fresh, old))


def repeat_steps(ctl, wet_from, deltas, early, work, other, sems):
    incoming = []
    for ref in early:
        begin = 0 if ref is early[0] else early[0].shape[1]
        incoming += start_all(
            ((ref, work.at[:, begin : begin + ref.shape[1]]),), sems, len(incoming)
        )
    row_ids = lax.broadcasted_iota(jnp.int32, (AGAIN, TILE), 0)
    lane = lax.broadcasted_iota(jnp.int32, (AGAIN, LANES), 1)
    start = tuple(jnp.zeros((1, TILE), jnp.float32) for _ in range(4))

    def halves(value):
        return value[:, :LANES], value[:, LANES:]

    def right_of(value):
        low, high = (pltpu.roll(part, LANES - 1, 1) for part in halves(value))
        return jnp.concatenate([jnp.where(lane == LANES - 1, high, low), high], 1)

    def left_of(value):
        low, high = (pltpu.roll(part, 1, 1) for part in halves(value))
        return jnp.concatenate([low, jnp.where(lane == 0, low, high)], 1)

    def down(value):
        return pltpu.roll(value, AGAIN + 7, 0)[:AGAIN]

    for step in range(STEPS):
        source, target = (work, other) if step % 2 == 0 else (other, work)
        delta = deltas[step][0:1, :]
        wet_now = flag(ctl, wet_from + step)

        def group(index, carry, source=source, target=target, delta=delta, wet_now=wet_now):
            base = pl.multiple_of(index * AGAIN, AGAIN)
            rows = pl.ds(base, AGAIN)
            after = pl.ds(pl.multiple_of(jnp.minimum(base + AGAIN, EARLY - 8), 8), 8)
            refs = [source.at[field] for field in range(3)] + [work.at[3]]
            fields = [jnp.concatenate([ref[rows, :], ref[after, :]], 0) for ref in refs]
            cells_x, cells_y = cell(*fields[:3])
            here_x = tuple(value[:AGAIN] for value in cells_x)
            here_y = tuple(value[:AGAIN] for value in cells_y)
            faces_x = face(here_x, tuple(down(value) for value in cells_x))
            turned = tuple(pltpu.roll(value, 1, 0) for value in faces_x)
            change_x = tuple(
                value - jnp.where(row_ids == 0, before, moved)
                for value, before, moved in zip(faces_x, carry[:3], turned)
            )
            ground = fields[3][:AGAIN]
            ground_up = pltpu.roll(ground, 1, 0)
            slope_x = down(fields[3]) - jnp.where(row_ids == 0, carry[3], ground_up)
            carried = tuple(value[0:1, :] for value in turned) + (ground_up[0:1, :],)
            faces_y = face(here_y, tuple(right_of(value) for value in here_y))
            change_y = tuple(value - left_of(value) for value in faces_y)
            slope_y = right_of(ground) - left_of(ground)
            old = tuple(value[:AGAIN] for value in fields[:3])
            weight = SLOPE * old[0]
            slopes = (
                SCALE * (change_x[0] + change_y[0]),
                SCALE * (change_x[1] + change_y[2]) + weight * slope_x,
                SCALE * (change_x[2] + change_y[1]) + weight * slope_y,
            )
            for field, value in enumerate(
                moved_on(old, slopes, work[4, rows, :], delta, wet_now)
            ):
                target[field, rows, :] = value
            return carried

        if step == 0:
            wait_all(incoming)
        lax.fori_loop(0, EARLY // AGAIN, group, start)


def late_rows(tile, late):
    row = sublanes()
    kept = EARLY - 8
    lane = lax.broadcasted_iota(jnp.int32, (8, LANES), 1)
    for field in range(3):
        late[field, 0:8, :] = jnp.where(
            row < 3, tile[field, 0:8, :], tile[field, kept : kept + 8, :]
        )
        packed = [jnp.zeros((8, LANES), jnp.float32)] * 2
        for block in range(EARLY // 8):
            rows = slice(8 * block, 8 * block + 8)
            sides = jnp.where(lane < 64, tile[field, rows, :LANES], tile[field, rows, LANES:])
            turned = pltpu.roll(sides, (3 + 8 * block) % LANES, 1)
            which = block // 16
            packed[which] = jnp.where(lane // 8 == block % 16, turned, packed[which])
        late[field, 8:16, :] = jnp.concatenate(packed, 1)
        late[field, 16:, :] = tile[field, EARLY:, :]


def merge(late, early, tile):
    for field in range(3):
        merge_field(field, late, early, tile)


def merge_field(field, late, early, tile):
    row = sublanes()
    lane = lax.broadcasted_iota(jnp.int32, (8, LANES), 1)
    first = late[field, 0:8, :]
    for block in range(EARLY // 8):
        rows = slice(8 * block, 8 * block + 8)
        which = block // 16
        packed = late[field, 8:16, which * LANES : (which + 1) * LANES]
        sides = pltpu.roll(packed, (-3 - 8 * block) % LANES, 1)
        value = early[field, rows, :]
        value = jnp.concatenate(
            [
                jnp.where(lane < 3, sides, value[:, :LANES]),
                jnp.where(lane >= LANES - 3, sides, value[:, LANES:]),
            ],
            1,
        )
        if block == 0:
            value = jnp.where(row < 3, first, value)
        if block == EARLY // 8 - 1:
            value = jnp.where(row < 5, value, first)
        tile[field, rows, :] = value
    tile[field, EARLY:, :] = late[field, 16:, :]


def repeat_second(ctl, delta0, delta1, delta2, low, high, late, out, late_out, work, tile, sems):
    near = start_all(((late, late_out),), sems, 2)
    repeat_steps(ctl, WET_SECOND, (delta0, delta1, delta2), (low, high), work, tile, sems)
    wait_all(start_all(((tile, out),), sems) + near)


def repeat_first(
    ctl, delta0, delta1, delta2, low, high, late_in, staying, out, work, other, tile, late, sems
):
    rest = out.at[1 - ctl[MOVE + 1]]
    again = ctl[MOVE] == ctl[MOVE + 1]

    @pl.when(again)
    def _():
        wait_all(start_all(((staying, tile),), sems))

    @pl.when(jnp.logical_not(again))
    def _():
        copies = start_all(((late_in, late),), sems, 2)
        repeat_steps(ctl, WET_FIRST, (delta0, delta1, delta2), (low, high), work, other, sems)
        wait_all(copies)
        merge(late, other, tile)

    wait_all(start_all(((tile, rest),), sems))


def finish(ctl, late, early, before, out, tile, sems):
    del before
    copies = []
    for field in range(3):
        merge_field(field, late, early, tile)
        copies += start_all(
            ((tile.at[field], out.at[ctl[MOVE + 1], field]),), sems, field
        )
    wait_all(copies)


def second_late(ctl, arrived, own, order, leaving):
    del order
    again = ctl[MOVE] == ctl[MOVE + 1]
    for field in range(3):
        leaving[field] = jnp.where(again, arrived[field], own[field])


def correct_rows(ctl, slot, got, ground, state, rate, bottom):
    position = jnp.where(ctl[SLOT_LOW] == slot, 0, 1)
    device = lax.axis_index("xb") * 2 + lax.axis_index("yb")
    wall = WALL_WEST if bottom else WALL_EAST

    @pl.when(jnp.logical_not(flag(ctl, wall + position)))
    def _():
        peer = device - 2 if bottom else device + 2
        block = pl.ds(pl.multiple_of(peer * 8, 8), 8)
        lines = got[block, :TILE]
        grounds = ground[block, :TILE]
        stride = 4 if got.shape[1] > TILE else 3

        def line(offset):
            other = offset + stride
            picked = jnp.where(
                position == 0, lines[offset : offset + 1, :], lines[other : other + 1, :]
            )
            return jnp.broadcast_to(picked, (8, TILE))

        ghost, _ = cell(*(line(field) for field in range(3)))
        ghost_ground = jnp.where(position == 0, grounds[3:4, :], grounds[7:8, :])
        rows = slice(0, 8) if bottom else slice(TILE - 8, TILE)
        own = [state[slot, field, rows, :] for field in range(3)]
        here, _ = cell(*own)
        fluxes = face(ghost, here) if bottom else face(here, ghost)
        push = SCALE * fluxes[1] + (SLOPE * own[0]) * ghost_ground
        row = sublanes()
        sign = -1.0 if bottom else 1.0
        chosen = row == (0 if bottom else 7)
        for field, value in enumerate((SCALE * fluxes[0], push, SCALE * fluxes[2])):
            rate[slot, field, rows, :] += jnp.where(chosen, sign * value, 0.0)


def column_fix(got, ground, columns):
    upper = lax.axis_index("yb")
    device = lax.axis_index("xb") * 2 + upper
    peer = device + 1 - 2 * upper
    block = pl.ds(pl.multiple_of(peer * 8, 8), 8)
    lines = got[block, :TILE]
    ghost_ground = ground[block, :TILE][3:4]
    mine = columns[...]
    _, ghost = cell(lines[0:1], lines[1:2], lines[2:3])
    _, own = cell(mine[0:1], mine[1:2], mine[2:3])
    low = upper == 0
    left = tuple(jnp.where(low, a, b) for a, b in zip(own, ghost))
    right = tuple(jnp.where(low, b, a) for a, b in zip(own, ghost))
    fluxes = face(left, right)
    sign = jnp.where(low, 1.0, -1.0)
    push = SCALE * fluxes[1] + (SLOPE * mine[0:1]) * ghost_ground
    block8 = stacked(
        [sign * SCALE * fluxes[0], sign * SCALE * fluxes[2], sign * push],
        jnp.zeros((8, TILE), jnp.float32),
    )
    return jnp.transpose(
        jnp.concatenate([block8, jnp.zeros((LANES - 8, TILE), jnp.float32)], 0)
    )


def last_update(moving, ctl, got, ground, columns, state, manning, rate, order, *rest):
    del order
    slot = ctl[MOVE] if moving else 1 - ctl[MOVE]
    update(STEPS - 1, ctl, got, ground, columns, state, manning, rate, *rest, slots=(slot,))


def update(
    step, ctl, got_in, ground_in, columns_in, state_in, manning_in, rate_in, *rest,
    passing=None, slots=(0, 1),
):
    more = step + 1 < STEPS
    fresh_out, first_out, second_out, delta_out = rest[:4]
    rest = rest[4:]
    state, manning, rate, fresh, got, ground, columns, first, second, delta_keep, sems = rest
    out, columns_out = first, second
    small = start_all(
        ((got_in, got), (ground_in, ground), (columns_in, columns)), sems, 5 * PARTS
    )
    size = 2 * TILE // PARTS
    parts = [
        (slot, slice(k * size, (k + 1) * size)) for slot in slots for k in range(PARTS // 2)
    ]
    incoming = []
    for index, (slot, rows) in enumerate(parts):
        incoming.append(
            start_all(
                (
                    (rate_in.at[slot, :, rows], rate.at[slot, :, rows]),
                    (state_in.at[slot, :, rows], state.at[slot, :, rows]),
                    (manning_in.at[slot, rows], manning.at[slot, rows]),
                ),
                sems,
                3 * index,
            )
        )
    wait_all(small)
    upper = lax.axis_index("yb")
    devices = 2 * lax.axis_size("xb")
    begin = TILE if got.shape[1] > TILE else 0
    tops = got[0:8, begin : begin + LANES]
    for peer in range(1, devices):
        tops = jnp.maximum(tops, got[peer * 8 : peer * 8 + 8, begin : begin + LANES])
    delta = (COURANT * SPACING) / tops[TOP : TOP + 1, :]
    delta = jnp.concatenate([delta, delta], 1)
    delta_keep[...] = jnp.broadcast_to(delta, (8, TILE))
    outgoing = start_all(((delta_keep, delta_out),), sems, 5 * PARTS + 3)
    fix = column_fix(got, ground, columns)
    facing = jnp.where(upper > 0, ctl[SLOT_LOW], 1 - ctl[SLOT_LOW])
    begin = pl.multiple_of((1 - upper) * LANES, LANES)
    goal = (1 - upper) * (LANES - 1)
    lane = lax.broadcasted_iota(jnp.int32, (size, LANES), 1)
    total = jnp.zeros((ROWS, TILE), jnp.float32)
    for index, (slot, part_rows) in enumerate(parts):
        wait_all(incoming[index])
        if part_rows.start == 0:
            correct_rows(ctl, slot, got, ground, state, rate, True)
        if part_rows.stop == TILE:
            correct_rows(ctl, slot, got, ground, state, rate, False)

        @pl.when(facing == slot)
        def _(slot=slot, part_rows=part_rows):
            for field in range(3):
                turned = pltpu.roll(
                    fix[part_rows], lax.rem(goal + LANES - field, LANES), 1
                )
                rate[slot, field, part_rows, pl.ds(begin, LANES)] += jnp.where(
                    lane == goal, turned, 0.0
                )

        wet_now = flag(ctl, WET + 2 * step + slot)

        def group(index, best, slot=slot, wet_now=wet_now):
            rows = pl.ds(pl.multiple_of(index * ROWS, ROWS), ROWS)
            old = tuple(state[slot, field, rows, :] for field in range(3))
            slopes = tuple(rate[slot, field, rows, :] for field in range(3))
            h, hu, hv = moved_on(old, slopes, manning[slot, rows, :], delta, wet_now)
            fresh[slot, 0, rows, :] = h
            fresh[slot, 1, rows, :] = hu
            fresh[slot, 2, rows, :] = hv
            if more:
                along_x, along_y = cell(h, hu, hv)
                best = jnp.maximum(best, jnp.maximum(along_x[5], along_y[5]))
            return best

        best = lax.fori_loop(
            part_rows.start // ROWS,
            part_rows.stop // ROWS,
            group,
            jnp.zeros((ROWS, TILE), jnp.float32),
        )
        if more:
            best = jnp.where(flag(ctl, WET + 2 * step + 2 + slot), best, 0.0)
            total = jnp.maximum(total, best)
        target = fresh_out.at[slot, :, part_rows] if more else fresh_out.at[:, part_rows]
        outgoing += start_all(
            ((fresh.at[slot, :, part_rows], target),), sems, 3 * PARTS + index
        )
        if passing and index == PARTS // 2:
            passing.middle()
    if more:
        messages(ctl, fresh, None, jnp.max(total, keepdims=True), out, columns_out)
        outgoing += start_all(((out, first_out), (columns_out, second_out)), sems, 4 * PARTS)
    else:
        second[...] = jnp.zeros_like(second)
        late_rows(fresh.at[slots[0]], first)
        outgoing += start_all(((first, first_out), (second, second_out)), sems, 4 * PARTS)
    wait_all(outgoing)


def vmem():
    return pl.BlockSpec(memory_space=pltpu.VMEM)


def smem():
    return pl.BlockSpec(memory_space=pltpu.SMEM)


def hbm():
    return pl.BlockSpec(memory_space=pltpu.HBM)


def anywhere():
    return pl.BlockSpec(memory_space=pl.ANY)


def call(
    kernel, outs, out_specs, in_specs, flops, scratch=(), aliases=None, room=VMEM_BYTES, moved=4
):
    return pl.pallas_call(
        kernel,
        scratch_shapes=scratch,
        input_output_aliases=aliases or {},
        out_shape=outs,
        in_specs=in_specs,
        out_specs=out_specs,
        compiler_params=pltpu.CompilerParams(vmem_limit_bytes=room),
        cost_estimate=pl.CostEstimate(flops=flops, bytes_accessed=moved << 20, transcendentals=0),
    )


def f32(*shape):
    return jax.ShapeDtypeStruct(shape, jnp.float32)


def spread(fast):
    return lax.all_to_all(fast, ("xb", "yb"), split_axis=0, concat_axis=0, tiled=True)


def body(state, bed, manning, neighbours, wet, moves):
    shape = f32(*state.shape)
    devices = lax.axis_size("xb") * lax.axis_size("yb")
    whole = pltpu.VMEM(state.shape, jnp.float32)
    part = pltpu.VMEM(bed.shape, jnp.float32)
    tile_shape = f32(*state.shape[1:])
    early_shape = f32(5, EARLY, TILE)
    early_state = f32(3, EARLY, TILE)
    late_shape = f32(3, LATE, TILE)
    delta_shape = f32(8, TILE)

    def buffer(like):
        return pltpu.VMEM(like.shape, jnp.float32)

    piece_shapes = tuple(f32(5, end - begin, TILE) for begin, end in PIECES)
    out, columns, ctl = call(
        opening,
        (
            f32(8 * devices, TILE + LANES),
            f32(8, TILE),
            jax.ShapeDtypeStruct((CONTROLS,), jnp.int32),
        ),
        (vmem(), vmem(), smem()),
        [hbm()] * 5,
        4 << 20,
        [
            whole,
            part,
            pltpu.SMEM(neighbours.shape[::-1], jnp.int32),
            pltpu.SMEM(wet.shape, jnp.int32),
            pltpu.SMEM(moves.shape, jnp.int32),
            pltpu.SemaphoreType.DMA((6,)),
        ],
    )(state, bed, neighbours.T, wet, moves)
    state_first = state
    ground = None
    deltas = []
    for step in range(STEPS):
        got = spread(out)
        ground = got if step == 0 else ground
        scratch = [whole, part, whole, pltpu.SemaphoreType.DMA((3 * CHUNKS,))]
        piece_scratch = [
            [buffer(piece), pltpu.SemaphoreType.DMA((2,))] for piece in piece_shapes
        ]
        if step == 1:
            rate, leaving = call(
                rates_and_leaving,
                (shape, piece_shapes[0]),
                (hbm(),) * 2,
                [smem()] + [hbm()] * 5,
                16 << 20,
                scratch + piece_scratch[0],
            )(ctl, state, bed, state_first, manning, early_first[0])
            early_second = [shifted(leaving, "xb", 1)]
        elif step == 2:
            rate = call(rates_after, shape, hbm(), [smem()] + [hbm()] * 3, 16 << 20, scratch)(
                ctl, state, bed, early_second[0]
            )
        else:
            rate, *leaving = call(
                rates_and_splitting,
                (shape,) + piece_shapes,
                (hbm(),) * 3,
                [smem()] + [hbm()] * 3,
                16 << 20,
                scratch + [buffer(early_shape), pltpu.SemaphoreType.DMA((5,))],
            )(ctl, state, bed, manning)
            held = call(
                hold, piece_shapes[0], hbm(), [hbm()] * 3, 1 << 10, aliases={2: 0}
            )(rate, got, leaving[0])
            early_first = [shifted(held, "xb", 1)]
        more = step + 1 < STEPS
        shapes = (f32(8 * devices, TILE) if more else late_shape), f32(8, TILE)
        passing = step == 1
        work = [
            whole,
            part,
            whole,
            whole,
            pltpu.VMEM(got.shape, jnp.float32),
            pltpu.VMEM(ground.shape, jnp.float32),
            pltpu.VMEM((8, TILE), jnp.float32),
            buffer(shapes[0]),
            buffer(shapes[1]),
            buffer(delta_shape),
            pltpu.SemaphoreType.DMA((5 * PARTS + 4,)),
        ]
        operands = ctl, got, ground, columns, state, manning, rate
        if not more:
            break
        outs = call(
            functools.partial(update_and_leaving if passing else update, step),
            (shape,) + shapes + (delta_shape,) + ((piece_shapes[1],) if passing else ()),
            (hbm(),) * (5 if passing else 4),
            [smem()] + [hbm()] * (9 if passing else 6),
            8 << 20,
            work + (piece_scratch[1] if passing else []),
            moved=10,
        )(*operands, *((state_first, bed, early_first[1]) if passing else ()))
        state, out, columns, delta, *passed = outs
        deltas.append(delta)
        if step == 0:
            held = call(
                hold, piece_shapes[1], hbm(), [hbm()] * 3, 1 << 10, aliases={2: 0}
            )(delta, delta, leaving[1])
            early_first.append(shifted(held, "xb", 1))
        elif step == 1:
            early_second.append(shifted(passed[0], "xb", 1))

    def finish_step(moving, order):
        return call(
            functools.partial(last_update, moving),
            (tile_shape,) + shapes + (delta_shape,),
            (hbm(),) * 4,
            [smem()] + [hbm()] * 7,
            8 << 20,
            work,
            moved=10,
        )(*operands, order)

    _, late_first, _, delta = finish_step(True, early_second[1])
    staying, late_second, _, _ = finish_step(False, delta)
    deltas.append(delta)
    room = 16 << 20
    late_arrived = shifted(late_first, "xb", 1)
    second, late_second = call(
        repeat_second,
        (early_state, late_shape),
        (anywhere(), vmem()),
        [smem()] + [vmem()] * 3 + [anywhere()] * 3,
        8 << 20,
        [buffer(early_shape), buffer(early_state), pltpu.SemaphoreType.DMA((3,))],
        room=room,
    )(ctl, *deltas, *early_second, late_second)
    leaving = call(
        second_late,
        late_shape,
        vmem(),
        [smem(), vmem(), vmem(), anywhere()],
        1 << 10,
        room=room,
    )(ctl, late_arrived, late_second, second)
    late_next = shifted(leaving, "xb", 1)
    final = call(
        repeat_first,
        shape,
        hbm(),
        [smem()] + [vmem()] * 3 + [anywhere()] * 4,
        8 << 20,
        [
            buffer(early_shape),
            buffer(early_state),
            buffer(tile_shape),
            buffer(late_shape),
            pltpu.SemaphoreType.DMA((3,)),
        ],
        room=room,
    )(ctl, *deltas, *early_first, late_arrived, staying)
    return call(
        finish,
        shape,
        hbm(),
        [smem(), vmem(), vmem(), hbm()],
        1 << 20,
        [buffer(tile_shape), pltpu.SemaphoreType.DMA((3,))],
        {3: 0},
        room=room,
    )(ctl, late_next, second, final)


def solution(mesh):
    placed = (
        P(("runs", "xb", "yb"), None, None, None),
        P(("runs", "xb", "yb"), None, None),
        P(("runs", "xb", "yb"), None, None),
        P("runs", None),
        P(None, "runs"),
        P(None, "runs"),
    )
    return jax.shard_map(
        body,
        mesh=mesh,
        in_specs=placed,
        out_specs=P(("runs", "xb", "yb"), None, None, None),
        check_vma=False,
    )
```

```python
import functools

import jax
import jax.numpy as jnp
from jax import lax
from jax.experimental import pallas as pl
from jax.experimental.pallas import tpu as pltpu
from jax.sharding import PartitionSpec as P

STEPS = 3
GRAVITY = 9.81
ROOT_G = GRAVITY**0.5
SPACING = 5.0
COURANT = 0.2
ROWS = 32
LANES = 128
TILE = 256
VMEM_BYTES = 60 * 1024 * 1024
SLOT_LOW, WALL_WEST, WALL_EAST, WALL_OUTER, WET, MOVE = 0, 1, 3, 5, 7, 13
WET_FIRST, WET_SECOND = 16, 19
CONTROLS = 24
EARLY = 160
PIECES = ((0, 80), (80, 160))
AGAIN = 32
LATE = TILE - EARLY + 16
CHUNKS = 8
PARTS = 8
STRIP = 16
TOP = 6
SCALE = 0.5 / SPACING
SLOPE = GRAVITY / (2.0 * SPACING)


def shifted(value, axis, steps, around=True):
    count = lax.axis_size(axis)
    pairs = [(source, (source + steps) % count) for source in range(count)]
    if not around:
        pairs = [pair for pair in pairs if abs(pair[0] - pair[1]) == abs(steps)]
    return lax.ppermute(value, axis, pairs)


def cell(h, hu, hv):
    root = lax.rsqrt(h)
    inverse = root * root
    u = hu * inverse
    v = hv * inverse
    celerity = ROOT_G * (h * root)
    pressure = (0.5 * GRAVITY) * (h * h)
    cross = hu * v
    speed_x = jnp.abs(u) + celerity
    speed_y = jnp.abs(v) + celerity
    along_x = (h, hu, hv, hu * u + pressure, cross, speed_x)
    along_y = (h, hv, hu, hv * v + pressure, cross, speed_y)
    return along_x, along_y


def face(left, right):
    wave = jnp.maximum(left[5], right[5])
    return (
        (left[1] + right[1]) - wave * (right[0] - left[0]),
        (left[3] + right[3]) - wave * (right[1] - left[1]),
        (left[4] + right[4]) - wave * (right[2] - left[2]),
    )


def slot_of(ctl, position):
    low = ctl[SLOT_LOW]
    return low if position == 0 else 1 - low


def flag(ctl, index):
    return ctl[index] > 0


def start_all(pairs, sems, first=0):
    copies = [
        pltpu.make_async_copy(src, dst, sems.at[first + k]) for k, (src, dst) in enumerate(pairs)
    ]
    for copy in copies:
        copy.start()
    return copies


def wait_all(copies):
    for copy in copies:
        copy.wait()


def sublanes(width=TILE):
    return lax.broadcasted_iota(jnp.int32, (8, width), 0)


def stacked(lines, base):
    row = sublanes()
    for index, line in enumerate(lines):
        base = jnp.where(row == index, jnp.broadcast_to(line, (8, TILE)), base)
    return base


def messages(ctl, state, bed, fastest, out, columns):
    upper = lax.axis_index("yb")
    column = lax.axis_index("xb")
    last = lax.axis_size("xb") - 1
    devices = 2 * (last + 1)
    device = column * 2 + upper
    top = jnp.broadcast_to(fastest, (8, TILE))
    for peer in range(devices):
        out[peer * 8 : peer * 8 + 8, :TILE] = top
        if bed is not None:
            out[peer * 8 : peer * 8 + 8, TILE:] = top[:, :LANES]
    row = sublanes()

    def edge(line):
        rows = slice(line, line + 1)
        lines = []
        for position in range(2):
            slot = slot_of(ctl, position)
            lines += [state[slot, field, rows, :] for field in range(3)]
            if bed is not None:
                lines.append(bed[slot, rows, :])
        return stacked(lines, top)

    for inside, peer, line in (
        (column > 0, device - 2, 0),
        (column < last, device + 2, TILE - 1),
    ):

        @pl.when(inside)
        def _(peer=peer, line=line):
            out[pl.ds(pl.multiple_of(peer * 8, 8), 8), :TILE] = edge(line)

    slot = jnp.where(upper > 0, ctl[SLOT_LOW], 1 - ctl[SLOT_LOW])
    begin = pl.multiple_of((1 - upper) * LANES, LANES)
    lane = lax.broadcasted_iota(jnp.int32, (TILE, LANES), 1)
    packed = None
    for field in range(4 if bed is not None else 3):
        if field < 3:
            part = state[slot, field, :, pl.ds(begin, LANES)]
        else:
            part = bed[slot, :, pl.ds(begin, LANES)]
        turned = pltpu.roll(part, field + 1 - upper, 1)
        packed = turned if field == 0 else jnp.where(lane == field, turned, packed)
    lines = jnp.transpose(packed)[:8]
    columns[...] = lines
    start = pl.multiple_of((device + 1 - 2 * upper) * 8, 8)
    out[pl.ds(start, 8), :TILE] = jnp.where(row == TOP, top, lines)


def opening(
    state_in, bed_in, neighbours_in, wet_in, moves_in,
    out, columns, ctl,
    state, bed, neighbours, wet, moves, sems,
):
    copies = start_all(
        (
            (neighbours_in, neighbours),
            (wet_in, wet),
            (moves_in, moves),
            (state_in.at[0], state.at[0]),
            (state_in.at[1], state.at[1]),
            (bed_in, bed),
        ),
        sems,
    )
    device = lax.axis_index("xb") * 2 + lax.axis_index("yb")
    wait_all(copies[:3])
    first = device * 2
    low = jnp.where(neighbours[3, first] == first + 1, 0, 1)
    ctl[SLOT_LOW] = low
    for position in range(2):
        slot = low if position == 0 else 1 - low
        tile = first + slot
        ctl[WALL_WEST + position] = (neighbours[0, tile] < 0).astype(jnp.int32)
        ctl[WALL_EAST + position] = (neighbours[1, tile] < 0).astype(jnp.int32)
        ctl[WALL_OUTER + position] = (neighbours[2 + position, tile] < 0).astype(jnp.int32)
    for step in range(STEPS):
        for slot in range(2):
            ctl[WET + 2 * step + slot] = wet[step, first + slot]
        ctl[MOVE + step] = moves[step, device]
    count = lax.axis_size("xb")
    upper = lax.axis_index("yb")
    column = lax.axis_index("xb")
    source = lax.rem(column + count - 1, count) * 2 + upper
    before = lax.rem(column + count - 2, count) * 2 + upper
    again = moves[0, source] == moves[1, source]
    tile_first = source * 2 + moves[0, source]
    tile_second = jnp.where(
        again, before * 2 + moves[0, before], source * 2 + 1 - moves[0, source]
    )
    for step in range(STEPS):
        ctl[WET_FIRST + step] = wet[step, tile_first]
        ctl[WET_SECOND + step] = wet[step, tile_second]

    total = jnp.zeros((ROWS, TILE), jnp.float32)
    for slot in range(2):
        copies[3 + slot].wait()

        def group(index, best, slot=slot):
            rows = pl.ds(pl.multiple_of(index * ROWS, ROWS), ROWS)
            along_x, along_y = cell(*(state[slot, field, rows, :] for field in range(3)))
            return jnp.maximum(best, jnp.maximum(along_x[5], along_y[5]))

        best = lax.fori_loop(0, TILE // ROWS, group, jnp.zeros((ROWS, TILE), jnp.float32))
        total = jnp.maximum(total, jnp.where(wet[0, first + slot] > 0, best, 0.0))
    copies[5].wait()
    messages(ctl, state, bed, jnp.max(total, keepdims=True), out, columns)


def hold(first, second, leaving, same):
    del first, second, leaving, same


class Splitting:
    def __init__(self, ctl, state_in, bed_in, manning_in, leaving, buffer, sems):
        slot = ctl[MOVE]
        rows = slice(0, EARLY)
        pairs = (
            (state_in.at[slot, :, rows], buffer.at[0:3]),
            (bed_in.at[slot, rows], buffer.at[3]),
            (manning_in.at[slot, rows], buffer.at[4]),
        )
        self.incoming = [
            pltpu.make_async_copy(src, dst, sems.at[k]) for k, (src, dst) in enumerate(pairs)
        ]
        self.outgoing = [
            pltpu.make_async_copy(buffer.at[:, begin:end], piece, sems.at[3 + k])
            for k, ((begin, end), piece) in enumerate(zip(PIECES, leaving))
        ]

    def start(self):
        for copy in self.incoming:
            copy.start()

    def middle(self):
        wait_all(self.incoming)
        for copy in self.outgoing:
            copy.start()

    def end(self):
        wait_all(self.outgoing)


class Passing:
    def __init__(self, ctl, piece, state_in, bed_in, manning_in, arrived, leaving, buffer, sems):
        self.again = ctl[MOVE] == ctl[MOVE + 1]
        self.other = 1 - ctl[MOVE]
        self.rows = slice(*piece)
        self.refs = state_in, bed_in, manning_in
        self.incoming = pltpu.make_async_copy(arrived, buffer, sems.at[0])
        self.outgoing = pltpu.make_async_copy(buffer, leaving, sems.at[1])
        self.buffer = buffer
        self.sem = sems.at[0]

    def start(self):
        state_in, bed_in, manning_in = self.refs
        buffer, sem, rows = self.buffer, self.sem, self.rows

        @pl.when(self.again)
        def _():
            self.incoming.start()

        @pl.when(jnp.logical_not(self.again))
        def _():
            pltpu.make_async_copy(state_in.at[self.other, :, rows], buffer.at[0:3], sem).start()
            pltpu.make_async_copy(bed_in.at[self.other, rows], buffer.at[3], sem).start()
            pltpu.make_async_copy(manning_in.at[self.other, rows], buffer.at[4], sem).start()

    def middle(self):
        self.incoming.wait()
        self.outgoing.start()

    def end(self):
        self.outgoing.wait()


def rates_and_splitting(
    ctl, state_in, bed_in, manning_in, rate_out, leaving_low, leaving_high,
    state, bed, rate, sems, buffer, moving,
):
    leaving = leaving_low, leaving_high
    splitting = Splitting(ctl, state_in, bed_in, manning_in, leaving, buffer, moving)
    rates(ctl, state_in, bed_in, rate_out, state, bed, rate, sems, splitting)


def rates_and_leaving(
    ctl, state_in, bed_in, state_first, manning_in, arrived, rate_out, leaving,
    state, bed, rate, sems, buffer, moving,
):
    passing = Passing(
        ctl, PIECES[0], state_first, bed_in, manning_in, arrived, leaving, buffer, moving
    )
    rates(ctl, state_in, bed_in, rate_out, state, bed, rate, sems, passing)


def update_and_leaving(
    step, ctl, got_in, ground_in, columns_in, state_in, manning_in, rate_in,
    state_first, bed_in, arrived, fresh_out, first_out, second_out, delta_out, leaving, *rest
):
    *rest, buffer, moving = rest
    passing = Passing(
        ctl, PIECES[1], state_first, bed_in, manning_in, arrived, leaving, buffer, moving
    )
    passing.start()
    update(
        step, ctl, got_in, ground_in, columns_in, state_in, manning_in, rate_in,
        fresh_out, first_out, second_out, delta_out, *rest, passing=passing,
    )
    passing.end()


def rates_after(ctl, state_in, bed_in, order, *rest):
    del order
    rates(ctl, state_in, bed_in, *rest)


def rates(ctl, state_in, bed_in, rate_out, state, bed, rate, sems, passing=None):
    width = 2 * TILE
    row_ids = lax.broadcasted_iota(jnp.int32, (STRIP, width), 0)
    row8 = sublanes(width)
    lane = lax.broadcasted_iota(jnp.int32, (STRIP, LANES), 1)
    last = TILE // STRIP - 1
    chunk = TILE // CHUNKS
    slots = [slot_of(ctl, position) for position in range(2)]
    incoming = []
    for part in range(CHUNKS):
        rows = slice(part * chunk, (part + 1) * chunk)
        incoming.append(
            start_all(
                (
                    (state_in.at[:, :, rows], state.at[:, :, rows]),
                    (bed_in.at[:, rows], bed.at[:, rows]),
                ),
                sems,
                2 * part,
            )
        )
    if passing:
        passing.start()
    keep_west, keep_east, keep_south, keep_north = (
        jnp.where(flag(ctl, index), 1.0, 0.0)
        for index in (WALL_WEST, WALL_EAST, WALL_OUTER, WALL_OUTER + 1)
    )

    def strip(field, rows):
        if field == 3:
            return jnp.concatenate([bed[slot, rows, :] for slot in slots], 1)
        return jnp.concatenate([state[slot, field, rows, :] for slot in slots], 1)

    def blocks(value):
        return [value[:, k * LANES : (k + 1) * LANES] for k in range(4)]

    def right_of(value, end=None):
        turned = [pltpu.roll(part, LANES - 1, 1) for part in blocks(value)]
        after = turned[1:] + [turned[3] if end is None else end]
        return jnp.concatenate(
            [
                jnp.where(lane == LANES - 1, following, part)
                if following is not part
                else part
                for part, following in zip(turned, after)
            ],
            1,
        )

    def left_of(value, end):
        turned = [pltpu.roll(part, 1, 1) for part in blocks(value)]
        before = [end] + turned[:3]
        return jnp.concatenate(
            [jnp.where(lane == 0, previous, part) for part, previous in zip(turned, before)], 1
        )

    def down(value):
        return pltpu.roll(value, STRIP + 7, 0)[:STRIP]

    def group(index, carry):
        base = pl.multiple_of(index * STRIP, STRIP)
        rows = pl.ds(base, STRIP)
        after = pl.ds(pl.multiple_of(jnp.minimum(base + STRIP, TILE - 8), 8), 8)
        at_end = index == last
        fields = [
            jnp.concatenate([strip(field, rows), strip(field, after)], 0) for field in range(3)
        ]
        cells_x, cells_y = cell(*fields)
        here_x = tuple(value[:STRIP] for value in cells_x)
        here_y = tuple(value[:STRIP] for value in cells_y)

        ending = jnp.logical_and(row8 == 7, at_end)
        faces = list(face(here_x, tuple(down(value) for value in cells_x)))
        wall = keep_east * (2.0 * (here_x[3] + here_x[5] * here_x[1])[STRIP - 8 :])
        for component, value in enumerate((0.0, wall, 0.0)):
            upper = faces[component]
            faces[component] = jnp.concatenate(
                [upper[: STRIP - 8], jnp.where(ending, value, upper[STRIP - 8 :])], 0
            )
        turned = tuple(pltpu.roll(value, 1, 0) for value in faces)
        change_x = tuple(
            value - jnp.where(row_ids == 0, before, moved)
            for value, before, moved in zip(faces, carry[:3], turned)
        )
        ground = strip(3, rows)
        ground_after = jnp.where(
            at_end,
            jnp.broadcast_to(keep_east * ground[STRIP - 1 :], (8, width)),
            strip(3, after),
        )
        ground_up = pltpu.roll(ground, 1, 0)
        slope_x = down(jnp.concatenate([ground, ground_after], 0)) - jnp.where(
            row_ids == 0, carry[3], ground_up
        )
        carried = tuple(value[0:1, :] for value in turned) + (ground_up[0:1, :],)

        faces_y = list(face(here_y, tuple(right_of(value) for value in here_y)))
        normal = here_y[3]
        spread_y = here_y[5] * here_y[1]
        north = keep_north * (2.0 * (normal + spread_y)[:, width - LANES :])
        south = keep_south * (2.0 * (normal - spread_y)[:, :LANES])
        change_y = []
        for component, (high, low) in enumerate(((0.0, 0.0), (north, south), (0.0, 0.0))):
            parts = blocks(faces_y[component])
            parts[3] = jnp.where(lane == LANES - 1, high, parts[3])
            value = jnp.concatenate(parts, 1)
            change_y.append(value - left_of(value, low))
        slope_y = right_of(ground, keep_north * ground[:, width - LANES :]) - left_of(
            ground, keep_south * ground[:, :LANES]
        )
        weight = SLOPE * here_x[0]
        results = (
            SCALE * (change_x[0] + change_y[0]),
            SCALE * (change_x[1] + change_y[2]) + weight * slope_x,
            SCALE * (change_x[2] + change_y[1]) + weight * slope_y,
        )
        for field, value in enumerate(results):
            for position, slot in enumerate(slots):
                rate[slot, field, rows, :] = value[:, position * TILE : (position + 1) * TILE]
        return carried

    wait_all(incoming[0])
    top, _ = cell(*(strip(field, slice(0, 8)) for field in range(3)))
    nothing = jnp.zeros((1, width), jnp.float32)
    carry = (
        nothing,
        keep_west * (2.0 * (top[3] - top[5] * top[1])[0:1]),
        nothing,
        keep_west * strip(3, slice(0, 8))[0:1],
    )
    per_chunk = chunk // STRIP
    outgoing = []
    for part in range(CHUNKS):
        if part + 1 < CHUNKS:
            wait_all(incoming[part + 1])
        carry = lax.fori_loop(part * per_chunk, (part + 1) * per_chunk, group, carry)
        rows = slice(part * chunk, (part + 1) * chunk)
        outgoing += start_all(
            ((rate.at[:, :, rows], rate_out.at[:, :, rows]),), sems, 2 * CHUNKS + part
        )
        if passing and part == CHUNKS // 2:
            passing.middle()
    wait_all(outgoing)
    if passing:
        passing.end()


def moved_on(old, slopes, rough, delta, wet_now):
    h, hu, hv = (value - delta * slope for value, slope in zip(old, slopes))
    inverse = 1.0 / h
    u = hu * inverse
    v = hv * inverse
    speed = jnp.sqrt(u * u + v * v)
    power = jnp.exp((-4.0 / 3.0) * jnp.log(jnp.abs(h)))
    drag = (GRAVITY * delta) * (rough * rough) * (speed * power)
    factor = 1.0 / (1.0 + drag)
    fresh = (h, hu * factor, hv * factor)
    return tuple(jnp.where(wet_now, new, value) for new, value in zip(fresh, old))


def repeat_steps(ctl, wet_from, deltas, early, work, other, sems):
    incoming = []
    for ref in early:
        begin = 0 if ref is early[0] else early[0].shape[1]
        incoming += start_all(
            ((ref, work.at[:, begin : begin + ref.shape[1]]),), sems, len(incoming)
        )
    row_ids = lax.broadcasted_iota(jnp.int32, (AGAIN, TILE), 0)
    lane = lax.broadcasted_iota(jnp.int32, (AGAIN, LANES), 1)
    start = tuple(jnp.zeros((1, TILE), jnp.float32) for _ in range(4))

    def halves(value):
        return value[:, :LANES], value[:, LANES:]

    def right_of(value):
        low, high = (pltpu.roll(part, LANES - 1, 1) for part in halves(value))
        return jnp.concatenate([jnp.where(lane == LANES - 1, high, low), high], 1)

    def left_of(value):
        low, high = (pltpu.roll(part, 1, 1) for part in halves(value))
        return jnp.concatenate([low, jnp.where(lane == 0, low, high)], 1)

    def down(value):
        return pltpu.roll(value, AGAIN + 7, 0)[:AGAIN]

    for step in range(STEPS):
        source, target = (work, other) if step % 2 == 0 else (other, work)
        delta = deltas[step][0:1, :]
        wet_now = flag(ctl, wet_from + step)

        def group(index, carry, source=source, target=target, delta=delta, wet_now=wet_now):
            base = pl.multiple_of(index * AGAIN, AGAIN)
            rows = pl.ds(base, AGAIN)
            after = pl.ds(pl.multiple_of(jnp.minimum(base + AGAIN, EARLY - 8), 8), 8)
            refs = [source.at[field] for field in range(3)] + [work.at[3]]
            fields = [jnp.concatenate([ref[rows, :], ref[after, :]], 0) for ref in refs]
            cells_x, cells_y = cell(*fields[:3])
            here_x = tuple(value[:AGAIN] for value in cells_x)
            here_y = tuple(value[:AGAIN] for value in cells_y)
            faces_x = face(here_x, tuple(down(value) for value in cells_x))
            turned = tuple(pltpu.roll(value, 1, 0) for value in faces_x)
            change_x = tuple(
                value - jnp.where(row_ids == 0, before, moved)
                for value, before, moved in zip(faces_x, carry[:3], turned)
            )
            ground = fields[3][:AGAIN]
            ground_up = pltpu.roll(ground, 1, 0)
            slope_x = down(fields[3]) - jnp.where(row_ids == 0, carry[3], ground_up)
            carried = tuple(value[0:1, :] for value in turned) + (ground_up[0:1, :],)
            faces_y = face(here_y, tuple(right_of(value) for value in here_y))
            change_y = tuple(value - left_of(value) for value in faces_y)
            slope_y = right_of(ground) - left_of(ground)
            old = tuple(value[:AGAIN] for value in fields[:3])
            weight = SLOPE * old[0]
            slopes = (
                SCALE * (change_x[0] + change_y[0]),
                SCALE * (change_x[1] + change_y[2]) + weight * slope_x,
                SCALE * (change_x[2] + change_y[1]) + weight * slope_y,
            )
            for field, value in enumerate(
                moved_on(old, slopes, work[4, rows, :], delta, wet_now)
            ):
                target[field, rows, :] = value
            return carried

        if step == 0:
            wait_all(incoming)
        lax.fori_loop(0, EARLY // AGAIN, group, start)


def late_rows(tile, late):
    row = sublanes()
    kept = EARLY - 8
    lane = lax.broadcasted_iota(jnp.int32, (8, LANES), 1)
    for field in range(3):
        late[field, 0:8, :] = jnp.where(
            row < 3, tile[field, 0:8, :], tile[field, kept : kept + 8, :]
        )
        packed = [jnp.zeros((8, LANES), jnp.float32)] * 2
        for block in range(EARLY // 8):
            rows = slice(8 * block, 8 * block + 8)
            sides = jnp.where(lane < 64, tile[field, rows, :LANES], tile[field, rows, LANES:])
            turned = pltpu.roll(sides, (3 + 8 * block) % LANES, 1)
            which = block // 16
            packed[which] = jnp.where(lane // 8 == block % 16, turned, packed[which])
        late[field, 8:16, :] = jnp.concatenate(packed, 1)
        late[field, 16:, :] = tile[field, EARLY:, :]


def merge(late, early, tile):
    for field in range(3):
        merge_field(field, late, early, tile)


def merge_field(field, late, early, tile):
    row = sublanes()
    lane = lax.broadcasted_iota(jnp.int32, (8, LANES), 1)
    first = late[field, 0:8, :]
    for block in range(EARLY // 8):
        rows = slice(8 * block, 8 * block + 8)
        which = block // 16
        packed = late[field, 8:16, which * LANES : (which + 1) * LANES]
        sides = pltpu.roll(packed, (-3 - 8 * block) % LANES, 1)
        value = early[field, rows, :]
        value = jnp.concatenate(
            [
                jnp.where(lane < 3, sides, value[:, :LANES]),
                jnp.where(lane >= LANES - 3, sides, value[:, LANES:]),
            ],
            1,
        )
        if block == 0:
            value = jnp.where(row < 3, first, value)
        if block == EARLY // 8 - 1:
            value = jnp.where(row < 5, value, first)
        tile[field, rows, :] = value
    tile[field, EARLY:, :] = late[field, 16:, :]


def repeat_second(ctl, delta0, delta1, delta2, low, high, late, out, late_out, work, tile, sems):
    near = start_all(((late, late_out),), sems, 2)
    repeat_steps(ctl, WET_SECOND, (delta0, delta1, delta2), (low, high), work, tile, sems)
    wait_all(start_all(((tile, out),), sems) + near)


def repeat_first(
    ctl, delta0, delta1, delta2, low, high, late_in, staying, out, work, other, tile, late, sems
):
    rest = out.at[1 - ctl[MOVE + 1]]
    again = ctl[MOVE] == ctl[MOVE + 1]

    @pl.when(again)
    def _():
        wait_all(start_all(((staying, tile),), sems))

    @pl.when(jnp.logical_not(again))
    def _():
        copies = start_all(((late_in, late),), sems, 2)
        repeat_steps(ctl, WET_FIRST, (delta0, delta1, delta2), (low, high), work, other, sems)
        wait_all(copies)
        merge(late, other, tile)

    wait_all(start_all(((tile, rest),), sems))


def finish(ctl, late, early, before, out, tile, sems):
    del before
    copies = []
    for field in range(3):
        merge_field(field, late, early, tile)
        copies += start_all(
            ((tile.at[field], out.at[ctl[MOVE + 1], field]),), sems, field
        )
    wait_all(copies)


def second_late(ctl, arrived, own, order, leaving):
    del order
    again = ctl[MOVE] == ctl[MOVE + 1]
    for field in range(3):
        leaving[field] = jnp.where(again, arrived[field], own[field])


def correct_rows(ctl, slot, got, ground, state, rate, bottom):
    position = jnp.where(ctl[SLOT_LOW] == slot, 0, 1)
    device = lax.axis_index("xb") * 2 + lax.axis_index("yb")
    wall = WALL_WEST if bottom else WALL_EAST

    @pl.when(jnp.logical_not(flag(ctl, wall + position)))
    def _():
        peer = device - 2 if bottom else device + 2
        block = pl.ds(pl.multiple_of(peer * 8, 8), 8)
        lines = got[block, :TILE]
        grounds = ground[block, :TILE]
        stride = 4 if got.shape[1] > TILE else 3

        def line(offset):
            other = offset + stride
            picked = jnp.where(
                position == 0, lines[offset : offset + 1, :], lines[other : other + 1, :]
            )
            return jnp.broadcast_to(picked, (8, TILE))

        ghost, _ = cell(*(line(field) for field in range(3)))
        ghost_ground = jnp.where(position == 0, grounds[3:4, :], grounds[7:8, :])
        rows = slice(0, 8) if bottom else slice(TILE - 8, TILE)
        own = [state[slot, field, rows, :] for field in range(3)]
        here, _ = cell(*own)
        fluxes = face(ghost, here) if bottom else face(here, ghost)
        push = SCALE * fluxes[1] + (SLOPE * own[0]) * ghost_ground
        row = sublanes()
        sign = -1.0 if bottom else 1.0
        chosen = row == (0 if bottom else 7)
        for field, value in enumerate((SCALE * fluxes[0], push, SCALE * fluxes[2])):
            rate[slot, field, rows, :] += jnp.where(chosen, sign * value, 0.0)


def column_fix(got, ground, columns):
    upper = lax.axis_index("yb")
    device = lax.axis_index("xb") * 2 + upper
    peer = device + 1 - 2 * upper
    block = pl.ds(pl.multiple_of(peer * 8, 8), 8)
    lines = got[block, :TILE]
    ghost_ground = ground[block, :TILE][3:4]
    mine = columns[...]
    _, ghost = cell(lines[0:1], lines[1:2], lines[2:3])
    _, own = cell(mine[0:1], mine[1:2], mine[2:3])
    low = upper == 0
    left = tuple(jnp.where(low, a, b) for a, b in zip(own, ghost))
    right = tuple(jnp.where(low, b, a) for a, b in zip(own, ghost))
    fluxes = face(left, right)
    sign = jnp.where(low, 1.0, -1.0)
    push = SCALE * fluxes[1] + (SLOPE * mine[0:1]) * ghost_ground
    block8 = stacked(
        [sign * SCALE * fluxes[0], sign * SCALE * fluxes[2], sign * push],
        jnp.zeros((8, TILE), jnp.float32),
    )
    return jnp.transpose(
        jnp.concatenate([block8, jnp.zeros((LANES - 8, TILE), jnp.float32)], 0)
    )


def last_update(moving, ctl, got, ground, columns, state, manning, rate, order, *rest):
    del order
    slot = ctl[MOVE] if moving else 1 - ctl[MOVE]
    update(STEPS - 1, ctl, got, ground, columns, state, manning, rate, *rest, slots=(slot,))


def update(
    step, ctl, got_in, ground_in, columns_in, state_in, manning_in, rate_in, *rest,
    passing=None, slots=(0, 1),
):
    more = step + 1 < STEPS
    fresh_out, first_out, second_out, delta_out = rest[:4]
    rest = rest[4:]
    state, manning, rate, fresh, got, ground, columns, first, second, delta_keep, sems = rest
    out, columns_out = first, second
    small = start_all(
        ((got_in, got), (ground_in, ground), (columns_in, columns)), sems, 5 * PARTS
    )
    size = 2 * TILE // PARTS
    parts = [
        (slot, slice(k * size, (k + 1) * size)) for slot in slots for k in range(PARTS // 2)
    ]
    incoming = []
    for index, (slot, rows) in enumerate(parts):
        incoming.append(
            start_all(
                (
                    (rate_in.at[slot, :, rows], rate.at[slot, :, rows]),
                    (state_in.at[slot, :, rows], state.at[slot, :, rows]),
                    (manning_in.at[slot, rows], manning.at[slot, rows]),
                ),
                sems,
                3 * index,
            )
        )
    wait_all(small)
    upper = lax.axis_index("yb")
    devices = 2 * lax.axis_size("xb")
    begin = TILE if got.shape[1] > TILE else 0
    tops = got[0:8, begin : begin + LANES]
    for peer in range(1, devices):
        tops = jnp.maximum(tops, got[peer * 8 : peer * 8 + 8, begin : begin + LANES])
    delta = (COURANT * SPACING) / tops[TOP : TOP + 1, :]
    delta = jnp.concatenate([delta, delta], 1)
    delta_keep[...] = jnp.broadcast_to(delta, (8, TILE))
    outgoing = start_all(((delta_keep, delta_out),), sems, 5 * PARTS + 3)
    fix = column_fix(got, ground, columns)
    facing = jnp.where(upper > 0, ctl[SLOT_LOW], 1 - ctl[SLOT_LOW])
    begin = pl.multiple_of((1 - upper) * LANES, LANES)
    goal = (1 - upper) * (LANES - 1)
    lane = lax.broadcasted_iota(jnp.int32, (size, LANES), 1)
    total = jnp.zeros((ROWS, TILE), jnp.float32)
    for index, (slot, part_rows) in enumerate(parts):
        wait_all(incoming[index])
        if part_rows.start == 0:
            correct_rows(ctl, slot, got, ground, state, rate, True)
        if part_rows.stop == TILE:
            correct_rows(ctl, slot, got, ground, state, rate, False)

        @pl.when(facing == slot)
        def _(slot=slot, part_rows=part_rows):
            for field in range(3):
                turned = pltpu.roll(
                    fix[part_rows], lax.rem(goal + LANES - field, LANES), 1
                )
                rate[slot, field, part_rows, pl.ds(begin, LANES)] += jnp.where(
                    lane == goal, turned, 0.0
                )

        wet_now = flag(ctl, WET + 2 * step + slot)

        def group(index, best, slot=slot, wet_now=wet_now):
            rows = pl.ds(pl.multiple_of(index * ROWS, ROWS), ROWS)
            old = tuple(state[slot, field, rows, :] for field in range(3))
            slopes = tuple(rate[slot, field, rows, :] for field in range(3))
            h, hu, hv = moved_on(old, slopes, manning[slot, rows, :], delta, wet_now)
            fresh[slot, 0, rows, :] = h
            fresh[slot, 1, rows, :] = hu
            fresh[slot, 2, rows, :] = hv
            if more:
                along_x, along_y = cell(h, hu, hv)
                best = jnp.maximum(best, jnp.maximum(along_x[5], along_y[5]))
            return best

        best = lax.fori_loop(
            part_rows.start // ROWS,
            part_rows.stop // ROWS,
            group,
            jnp.zeros((ROWS, TILE), jnp.float32),
        )
        if more:
            best = jnp.where(flag(ctl, WET + 2 * step + 2 + slot), best, 0.0)
            total = jnp.maximum(total, best)
        target = fresh_out.at[slot, :, part_rows] if more else fresh_out.at[:, part_rows]
        outgoing += start_all(
            ((fresh.at[slot, :, part_rows], target),), sems, 3 * PARTS + index
        )
        if passing and index == PARTS // 2:
            passing.middle()
    if more:
        messages(ctl, fresh, None, jnp.max(total, keepdims=True), out, columns_out)
        outgoing += start_all(((out, first_out), (columns_out, second_out)), sems, 4 * PARTS)
    else:
        second[...] = jnp.zeros_like(second)
        late_rows(fresh.at[slots[0]], first)
        outgoing += start_all(((first, first_out), (second, second_out)), sems, 4 * PARTS)
    wait_all(outgoing)


def vmem():
    return pl.BlockSpec(memory_space=pltpu.VMEM)


def smem():
    return pl.BlockSpec(memory_space=pltpu.SMEM)


def hbm():
    return pl.BlockSpec(memory_space=pltpu.HBM)


def anywhere():
    return pl.BlockSpec(memory_space=pl.ANY)


def call(
    kernel, outs, out_specs, in_specs, flops, scratch=(), aliases=None, room=VMEM_BYTES, moved=4
):
    return pl.pallas_call(
        kernel,
        scratch_shapes=scratch,
        input_output_aliases=aliases or {},
        out_shape=outs,
        in_specs=in_specs,
        out_specs=out_specs,
        compiler_params=pltpu.CompilerParams(vmem_limit_bytes=room),
        cost_estimate=pl.CostEstimate(flops=flops, bytes_accessed=moved << 20, transcendentals=0),
    )


def f32(*shape):
    return jax.ShapeDtypeStruct(shape, jnp.float32)


def spread(fast):
    return lax.all_to_all(fast, ("xb", "yb"), split_axis=0, concat_axis=0, tiled=True)


def body(state, bed, manning, neighbours, wet, moves):
    shape = f32(*state.shape)
    devices = lax.axis_size("xb") * lax.axis_size("yb")
    whole = pltpu.VMEM(state.shape, jnp.float32)
    part = pltpu.VMEM(bed.shape, jnp.float32)
    tile_shape = f32(*state.shape[1:])
    early_shape = f32(5, EARLY, TILE)
    early_state = f32(3, EARLY, TILE)
    late_shape = f32(3, LATE, TILE)
    delta_shape = f32(8, TILE)

    def buffer(like):
        return pltpu.VMEM(like.shape, jnp.float32)

    piece_shapes = tuple(f32(5, end - begin, TILE) for begin, end in PIECES)
    out, columns, ctl = call(
        opening,
        (
            f32(8 * devices, TILE + LANES),
            f32(8, TILE),
            jax.ShapeDtypeStruct((CONTROLS,), jnp.int32),
        ),
        (vmem(), vmem(), smem()),
        [hbm()] * 5,
        4 << 20,
        [
            whole,
            part,
            pltpu.SMEM(neighbours.shape[::-1], jnp.int32),
            pltpu.SMEM(wet.shape, jnp.int32),
            pltpu.SMEM(moves.shape, jnp.int32),
            pltpu.SemaphoreType.DMA((6,)),
        ],
    )(state, bed, neighbours.T, wet, moves)
    state_first = state
    ground = None
    deltas = []
    for step in range(STEPS):
        got = spread(out)
        ground = got if step == 0 else ground
        scratch = [whole, part, whole, pltpu.SemaphoreType.DMA((3 * CHUNKS,))]
        piece_scratch = [
            [buffer(piece), pltpu.SemaphoreType.DMA((2,))] for piece in piece_shapes
        ]
        if step == 1:
            rate, leaving = call(
                rates_and_leaving,
                (shape, piece_shapes[0]),
                (hbm(),) * 2,
                [smem()] + [hbm()] * 5,
                16 << 20,
                scratch + piece_scratch[0],
            )(ctl, state, bed, state_first, manning, early_first[0])
            early_second = [shifted(leaving, "xb", 1)]
        elif step == 2:
            rate = call(rates_after, shape, hbm(), [smem()] + [hbm()] * 3, 16 << 20, scratch)(
                ctl, state, bed, early_second[0]
            )
        else:
            rate, *leaving = call(
                rates_and_splitting,
                (shape,) + piece_shapes,
                (hbm(),) * 3,
                [smem()] + [hbm()] * 3,
                16 << 20,
                scratch + [buffer(early_shape), pltpu.SemaphoreType.DMA((5,))],
            )(ctl, state, bed, manning)
            held = call(
                hold, piece_shapes[0], hbm(), [hbm()] * 3, 1 << 10, aliases={2: 0}
            )(rate, got, leaving[0])
            early_first = [shifted(held, "xb", 1)]
        more = step + 1 < STEPS
        shapes = (f32(8 * devices, TILE) if more else late_shape), f32(8, TILE)
        passing = step == 1
        work = [
            whole,
            part,
            whole,
            whole,
            pltpu.VMEM(got.shape, jnp.float32),
            pltpu.VMEM(ground.shape, jnp.float32),
            pltpu.VMEM((8, TILE), jnp.float32),
            buffer(shapes[0]),
            buffer(shapes[1]),
            buffer(delta_shape),
            pltpu.SemaphoreType.DMA((5 * PARTS + 4,)),
        ]
        operands = ctl, got, ground, columns, state, manning, rate
        if not more:
            break
        outs = call(
            functools.partial(update_and_leaving if passing else update, step),
            (shape,) + shapes + (delta_shape,) + ((piece_shapes[1],) if passing else ()),
            (hbm(),) * (5 if passing else 4),
            [smem()] + [hbm()] * (9 if passing else 6),
            8 << 20,
            work + (piece_scratch[1] if passing else []),
            moved=10,
        )(*operands, *((state_first, bed, early_first[1]) if passing else ()))
        state, out, columns, delta, *passed = outs
        deltas.append(delta)
        if step == 0:
            held = call(
                hold, piece_shapes[1], hbm(), [hbm()] * 3, 1 << 10, aliases={2: 0}
            )(delta, delta, leaving[1])
            early_first.append(shifted(held, "xb", 1))
        elif step == 1:
            early_second.append(shifted(passed[0], "xb", 1))

    def finish_step(moving, order):
        return call(
            functools.partial(last_update, moving),
            (tile_shape,) + shapes + (delta_shape,),
            (hbm(),) * 4,
            [smem()] + [hbm()] * 7,
            8 << 20,
            work,
            moved=10,
        )(*operands, order)

    _, late_first, _, delta = finish_step(True, early_second[1])
    staying, late_second, _, _ = finish_step(False, delta)
    deltas.append(delta)
    room = 16 << 20
    late_arrived = shifted(late_first, "xb", 1)
    second, late_second = call(
        repeat_second,
        (early_state, late_shape),
        (anywhere(), vmem()),
        [smem()] + [vmem()] * 3 + [anywhere()] * 3,
        8 << 20,
        [buffer(early_shape), buffer(early_state), pltpu.SemaphoreType.DMA((3,))],
        room=room,
    )(ctl, *deltas, *early_second, late_second)
    leaving = call(
        second_late,
        late_shape,
        vmem(),
        [smem(), vmem(), vmem(), anywhere()],
        1 << 10,
        room=room,
    )(ctl, late_arrived, late_second, second)
    late_next = shifted(leaving, "xb", 1)
    final = call(
        repeat_first,
        shape,
        hbm(),
        [smem()] + [vmem()] * 3 + [anywhere()] * 4,
        8 << 20,
        [
            buffer(early_shape),
            buffer(early_state),
            buffer(tile_shape),
            buffer(late_shape),
            pltpu.SemaphoreType.DMA((3,)),
        ],
        room=room,
    )(ctl, *deltas, *early_first, late_arrived, staying)
    return call(
        finish,
        shape,
        hbm(),
        [smem(), vmem(), vmem(), hbm()],
        1 << 20,
        [buffer(tile_shape), pltpu.SemaphoreType.DMA((3,))],
        {3: 0},
        room=room,
    )(ctl, late_next, second, final)


def solution(mesh):
    placed = (
        P(("runs", "xb", "yb"), None, None, None),
        P(("runs", "xb", "yb"), None, None),
        P(("runs", "xb", "yb"), None, None),
        P("runs", None),
        P(None, "runs"),
        P(None, "runs"),
    )
    return jax.shard_map(
        body,
        mesh=mesh,
        in_specs=placed,
        out_specs=P(("runs", "xb", "yb"), None, None, None),
        check_vma=False,
    )
```

```python
import functools

import jax
import jax.numpy as jnp
from jax import lax
from jax.experimental import pallas as pl
from jax.experimental.pallas import tpu as pltpu
from jax.sharding import PartitionSpec as P

STEPS = 3
GRAVITY = 9.81
ROOT_G = GRAVITY**0.5
SPACING = 5.0
COURANT = 0.2
ROWS = 32
LANES = 128
TILE = 256
VMEM_BYTES = 60 * 1024 * 1024
SLOT_LOW, WALL_WEST, WALL_EAST, WALL_OUTER, WET, MOVE = 0, 1, 3, 5, 7, 13
WET_FIRST, WET_SECOND = 16, 19
CONTROLS = 24
EARLY = 128
PIECES = ((0, 64), (64, 128))
AGAIN = 32
LATE = TILE - EARLY + 16
CHUNKS = 8
PARTS = 8
STRIP = 16
TOP = 6
SCALE = 0.5 / SPACING
SLOPE = GRAVITY / (2.0 * SPACING)


def shifted(value, axis, steps, around=True):
    count = lax.axis_size(axis)
    pairs = [(source, (source + steps) % count) for source in range(count)]
    if not around:
        pairs = [pair for pair in pairs if abs(pair[0] - pair[1]) == abs(steps)]
    return lax.ppermute(value, axis, pairs)


def cell(h, hu, hv):
    root = lax.rsqrt(h)
    inverse = root * root
    u = hu * inverse
    v = hv * inverse
    celerity = ROOT_G * (h * root)
    pressure = (0.5 * GRAVITY) * (h * h)
    cross = hu * v
    speed_x = jnp.abs(u) + celerity
    speed_y = jnp.abs(v) + celerity
    along_x = (h, hu, hv, hu * u + pressure, cross, speed_x)
    along_y = (h, hv, hu, hv * v + pressure, cross, speed_y)
    return along_x, along_y


def face(left, right):
    wave = jnp.maximum(left[5], right[5])
    return (
        (left[1] + right[1]) - wave * (right[0] - left[0]),
        (left[3] + right[3]) - wave * (right[1] - left[1]),
        (left[4] + right[4]) - wave * (right[2] - left[2]),
    )


def slot_of(ctl, position):
    low = ctl[SLOT_LOW]
    return low if position == 0 else 1 - low


def flag(ctl, index):
    return ctl[index] > 0


def start_all(pairs, sems, first=0):
    copies = [
        pltpu.make_async_copy(src, dst, sems.at[first + k]) for k, (src, dst) in enumerate(pairs)
    ]
    for copy in copies:
        copy.start()
    return copies


def wait_all(copies):
    for copy in copies:
        copy.wait()


def sublanes(width=TILE):
    return lax.broadcasted_iota(jnp.int32, (8, width), 0)


def stacked(lines, base):
    row = sublanes()
    for index, line in enumerate(lines):
        base = jnp.where(row == index, jnp.broadcast_to(line, (8, TILE)), base)
    return base


def messages(ctl, state, bed, fastest, out, columns):
    upper = lax.axis_index("yb")
    column = lax.axis_index("xb")
    last = lax.axis_size("xb") - 1
    devices = 2 * (last + 1)
    device = column * 2 + upper
    top = jnp.broadcast_to(fastest, (8, TILE))
    for peer in range(devices):
        out[peer * 8 : peer * 8 + 8, :TILE] = top
        if bed is not None:
            out[peer * 8 : peer * 8 + 8, TILE:] = top[:, :LANES]
    row = sublanes()

    def edge(line):
        rows = slice(line, line + 1)
        lines = []
        for position in range(2):
            slot = slot_of(ctl, position)
            lines += [state[slot, field, rows, :] for field in range(3)]
            if bed is not None:
                lines.append(bed[slot, rows, :])
        return stacked(lines, top)

    for inside, peer, line in (
        (column > 0, device - 2, 0),
        (column < last, device + 2, TILE - 1),
    ):

        @pl.when(inside)
        def _(peer=peer, line=line):
            out[pl.ds(pl.multiple_of(peer * 8, 8), 8), :TILE] = edge(line)

    slot = jnp.where(upper > 0, ctl[SLOT_LOW], 1 - ctl[SLOT_LOW])
    begin = pl.multiple_of((1 - upper) * LANES, LANES)
    lane = lax.broadcasted_iota(jnp.int32, (TILE, LANES), 1)
    packed = None
    for field in range(4 if bed is not None else 3):
        if field < 3:
            part = state[slot, field, :, pl.ds(begin, LANES)]
        else:
            part = bed[slot, :, pl.ds(begin, LANES)]
        turned = pltpu.roll(part, field + 1 - upper, 1)
        packed = turned if field == 0 else jnp.where(lane == field, turned, packed)
    lines = jnp.transpose(packed)[:8]
    columns[...] = lines
    start = pl.multiple_of((device + 1 - 2 * upper) * 8, 8)
    out[pl.ds(start, 8), :TILE] = jnp.where(row == TOP, top, lines)


def opening(
    state_in, bed_in, neighbours_in, wet_in, moves_in,
    out, columns, ctl,
    state, bed, neighbours, wet, moves, sems,
):
    copies = start_all(
        (
            (neighbours_in, neighbours),
            (wet_in, wet),
            (moves_in, moves),
            (state_in.at[0], state.at[0]),
            (state_in.at[1], state.at[1]),
            (bed_in, bed),
        ),
        sems,
    )
    device = lax.axis_index("xb") * 2 + lax.axis_index("yb")
    wait_all(copies[:3])
    first = device * 2
    low = jnp.where(neighbours[3, first] == first + 1, 0, 1)
    ctl[SLOT_LOW] = low
    for position in range(2):
        slot = low if position == 0 else 1 - low
        tile = first + slot
        ctl[WALL_WEST + position] = (neighbours[0, tile] < 0).astype(jnp.int32)
        ctl[WALL_EAST + position] = (neighbours[1, tile] < 0).astype(jnp.int32)
        ctl[WALL_OUTER + position] = (neighbours[2 + position, tile] < 0).astype(jnp.int32)
    for step in range(STEPS):
        for slot in range(2):
            ctl[WET + 2 * step + slot] = wet[step, first + slot]
        ctl[MOVE + step] = moves[step, device]
    count = lax.axis_size("xb")
    upper = lax.axis_index("yb")
    column = lax.axis_index("xb")
    source = lax.rem(column + count - 1, count) * 2 + upper
    before = lax.rem(column + count - 2, count) * 2 + upper
    again = moves[0, source] == moves[1, source]
    tile_first = source * 2 + moves[0, source]
    tile_second = jnp.where(
        again, before * 2 + moves[0, before], source * 2 + 1 - moves[0, source]
    )
    for step in range(STEPS):
        ctl[WET_FIRST + step] = wet[step, tile_first]
        ctl[WET_SECOND + step] = wet[step, tile_second]

    total = jnp.zeros((ROWS, TILE), jnp.float32)
    for slot in range(2):
        copies[3 + slot].wait()

        def group(index, best, slot=slot):
            rows = pl.ds(pl.multiple_of(index * ROWS, ROWS), ROWS)
            along_x, along_y = cell(*(state[slot, field, rows, :] for field in range(3)))
            return jnp.maximum(best, jnp.maximum(along_x[5], along_y[5]))

        best = lax.fori_loop(0, TILE // ROWS, group, jnp.zeros((ROWS, TILE), jnp.float32))
        total = jnp.maximum(total, jnp.where(wet[0, first + slot] > 0, best, 0.0))
    copies[5].wait()
    messages(ctl, state, bed, jnp.max(total, keepdims=True), out, columns)


def hold(first, second, leaving, same):
    del first, second, leaving, same


class Splitting:
    def __init__(self, ctl, state_in, bed_in, manning_in, leaving, buffer, sems):
        slot = ctl[MOVE]
        rows = slice(0, EARLY)
        pairs = (
            (state_in.at[slot, :, rows], buffer.at[0:3]),
            (bed_in.at[slot, rows], buffer.at[3]),
            (manning_in.at[slot, rows], buffer.at[4]),
        )
        self.incoming = [
            pltpu.make_async_copy(src, dst, sems.at[k]) for k, (src, dst) in enumerate(pairs)
        ]
        self.outgoing = [
            pltpu.make_async_copy(buffer.at[:, begin:end], piece, sems.at[3 + k])
            for k, ((begin, end), piece) in enumerate(zip(PIECES, leaving))
        ]

    def start(self):
        for copy in self.incoming:
            copy.start()

    def middle(self):
        wait_all(self.incoming)
        for copy in self.outgoing:
            copy.start()

    def end(self):
        wait_all(self.outgoing)


class Passing:
    def __init__(self, ctl, piece, state_in, bed_in, manning_in, arrived, leaving, buffer, sems):
        self.again = ctl[MOVE] == ctl[MOVE + 1]
        self.other = 1 - ctl[MOVE]
        self.rows = slice(*piece)
        self.refs = state_in, bed_in, manning_in
        self.incoming = pltpu.make_async_copy(arrived, buffer, sems.at[0])
        self.outgoing = pltpu.make_async_copy(buffer, leaving, sems.at[1])
        self.buffer = buffer
        self.sem = sems.at[0]

    def start(self):
        state_in, bed_in, manning_in = self.refs
        buffer, sem, rows = self.buffer, self.sem, self.rows

        @pl.when(self.again)
        def _():
            self.incoming.start()

        @pl.when(jnp.logical_not(self.again))
        def _():
            pltpu.make_async_copy(state_in.at[self.other, :, rows], buffer.at[0:3], sem).start()
            pltpu.make_async_copy(bed_in.at[self.other, rows], buffer.at[3], sem).start()
            pltpu.make_async_copy(manning_in.at[self.other, rows], buffer.at[4], sem).start()

    def middle(self):
        self.incoming.wait()
        self.outgoing.start()

    def end(self):
        self.outgoing.wait()


def rates_and_splitting(
    ctl, state_in, bed_in, manning_in, rate_out, leaving_low, leaving_high,
    state, bed, rate, sems, buffer, moving,
):
    leaving = leaving_low, leaving_high
    splitting = Splitting(ctl, state_in, bed_in, manning_in, leaving, buffer, moving)
    rates(ctl, state_in, bed_in, rate_out, state, bed, rate, sems, splitting)


def rates_and_leaving(
    ctl, state_in, bed_in, state_first, manning_in, arrived, rate_out, leaving,
    state, bed, rate, sems, buffer, moving,
):
    passing = Passing(
        ctl, PIECES[0], state_first, bed_in, manning_in, arrived, leaving, buffer, moving
    )
    rates(ctl, state_in, bed_in, rate_out, state, bed, rate, sems, passing)


def update_and_leaving(
    step, ctl, got_in, ground_in, columns_in, state_in, manning_in, rate_in,
    state_first, bed_in, arrived, fresh_out, first_out, second_out, delta_out, leaving, *rest
):
    *rest, buffer, moving = rest
    passing = Passing(
        ctl, PIECES[1], state_first, bed_in, manning_in, arrived, leaving, buffer, moving
    )
    passing.start()
    update(
        step, ctl, got_in, ground_in, columns_in, state_in, manning_in, rate_in,
        fresh_out, first_out, second_out, delta_out, *rest, passing=passing,
    )
    passing.end()


def rates_after(ctl, state_in, bed_in, order, *rest):
    del order
    rates(ctl, state_in, bed_in, *rest)


def rates(ctl, state_in, bed_in, rate_out, state, bed, rate, sems, passing=None):
    width = 2 * TILE
    row_ids = lax.broadcasted_iota(jnp.int32, (STRIP, width), 0)
    row8 = sublanes(width)
    lane = lax.broadcasted_iota(jnp.int32, (STRIP, LANES), 1)
    last = TILE // STRIP - 1
    chunk = TILE // CHUNKS
    slots = [slot_of(ctl, position) for position in range(2)]
    incoming = []
    for part in range(CHUNKS):
        rows = slice(part * chunk, (part + 1) * chunk)
        incoming.append(
            start_all(
                (
                    (state_in.at[:, :, rows], state.at[:, :, rows]),
                    (bed_in.at[:, rows], bed.at[:, rows]),
                ),
                sems,
                2 * part,
            )
        )
    if passing:
        passing.start()
    keep_west, keep_east, keep_south, keep_north = (
        jnp.where(flag(ctl, index), 1.0, 0.0)
        for index in (WALL_WEST, WALL_EAST, WALL_OUTER, WALL_OUTER + 1)
    )

    def strip(field, rows):
        if field == 3:
            return jnp.concatenate([bed[slot, rows, :] for slot in slots], 1)
        return jnp.concatenate([state[slot, field, rows, :] for slot in slots], 1)

    def blocks(value):
        return [value[:, k * LANES : (k + 1) * LANES] for k in range(4)]

    def right_of(value, end=None):
        turned = [pltpu.roll(part, LANES - 1, 1) for part in blocks(value)]
        after = turned[1:] + [turned[3] if end is None else end]
        return jnp.concatenate(
            [
                jnp.where(lane == LANES - 1, following, part)
                if following is not part
                else part
                for part, following in zip(turned, after)
            ],
            1,
        )

    def left_of(value, end):
        turned = [pltpu.roll(part, 1, 1) for part in blocks(value)]
        before = [end] + turned[:3]
        return jnp.concatenate(
            [jnp.where(lane == 0, previous, part) for part, previous in zip(turned, before)], 1
        )

    def down(value):
        return pltpu.roll(value, STRIP + 7, 0)[:STRIP]

    def group(index, carry):
        base = pl.multiple_of(index * STRIP, STRIP)
        rows = pl.ds(base, STRIP)
        after = pl.ds(pl.multiple_of(jnp.minimum(base + STRIP, TILE - 8), 8), 8)
        at_end = index == last
        fields = [
            jnp.concatenate([strip(field, rows), strip(field, after)], 0) for field in range(3)
        ]
        cells_x, cells_y = cell(*fields)
        here_x = tuple(value[:STRIP] for value in cells_x)
        here_y = tuple(value[:STRIP] for value in cells_y)

        ending = jnp.logical_and(row8 == 7, at_end)
        faces = list(face(here_x, tuple(down(value) for value in cells_x)))
        wall = keep_east * (2.0 * (here_x[3] + here_x[5] * here_x[1])[STRIP - 8 :])
        for component, value in enumerate((0.0, wall, 0.0)):
            upper = faces[component]
            faces[component] = jnp.concatenate(
                [upper[: STRIP - 8], jnp.where(ending, value, upper[STRIP - 8 :])], 0
            )
        turned = tuple(pltpu.roll(value, 1, 0) for value in faces)
        change_x = tuple(
            value - jnp.where(row_ids == 0, before, moved)
            for value, before, moved in zip(faces, carry[:3], turned)
        )
        ground = strip(3, rows)
        ground_after = jnp.where(
            at_end,
            jnp.broadcast_to(keep_east * ground[STRIP - 1 :], (8, width)),
            strip(3, after),
        )
        ground_up = pltpu.roll(ground, 1, 0)
        slope_x = down(jnp.concatenate([ground, ground_after], 0)) - jnp.where(
            row_ids == 0, carry[3], ground_up
        )
        carried = tuple(value[0:1, :] for value in turned) + (ground_up[0:1, :],)

        faces_y = list(face(here_y, tuple(right_of(value) for value in here_y)))
        normal = here_y[3]
        spread_y = here_y[5] * here_y[1]
        north = keep_north * (2.0 * (normal + spread_y)[:, width - LANES :])
        south = keep_south * (2.0 * (normal - spread_y)[:, :LANES])
        change_y = []
        for component, (high, low) in enumerate(((0.0, 0.0), (north, south), (0.0, 0.0))):
            parts = blocks(faces_y[component])
            parts[3] = jnp.where(lane == LANES - 1, high, parts[3])
            value = jnp.concatenate(parts, 1)
            change_y.append(value - left_of(value, low))
        slope_y = right_of(ground, keep_north * ground[:, width - LANES :]) - left_of(
            ground, keep_south * ground[:, :LANES]
        )
        weight = SLOPE * here_x[0]
        results = (
            SCALE * (change_x[0] + change_y[0]),
            SCALE * (change_x[1] + change_y[2]) + weight * slope_x,
            SCALE * (change_x[2] + change_y[1]) + weight * slope_y,
        )
        for field, value in enumerate(results):
            for position, slot in enumerate(slots):
                rate[slot, field, rows, :] = value[:, position * TILE : (position + 1) * TILE]
        return carried

    wait_all(incoming[0])
    top, _ = cell(*(strip(field, slice(0, 8)) for field in range(3)))
    nothing = jnp.zeros((1, width), jnp.float32)
    carry = (
        nothing,
        keep_west * (2.0 * (top[3] - top[5] * top[1])[0:1]),
        nothing,
        keep_west * strip(3, slice(0, 8))[0:1],
    )
    per_chunk = chunk // STRIP
    outgoing = []
    for part in range(CHUNKS):
        if part + 1 < CHUNKS:
            wait_all(incoming[part + 1])
        carry = lax.fori_loop(part * per_chunk, (part + 1) * per_chunk, group, carry)
        rows = slice(part * chunk, (part + 1) * chunk)
        outgoing += start_all(
            ((rate.at[:, :, rows], rate_out.at[:, :, rows]),), sems, 2 * CHUNKS + part
        )
        if passing and part == CHUNKS // 2:
            passing.middle()
    wait_all(outgoing)
    if passing:
        passing.end()


def moved_on(old, slopes, rough, delta, wet_now):
    h, hu, hv = (value - delta * slope for value, slope in zip(old, slopes))
    inverse = 1.0 / h
    u = hu * inverse
    v = hv * inverse
    speed = jnp.sqrt(u * u + v * v)
    power = jnp.exp((-4.0 / 3.0) * jnp.log(jnp.abs(h)))
    drag = (GRAVITY * delta) * (rough * rough) * (speed * power)
    factor = 1.0 / (1.0 + drag)
    fresh = (h, hu * factor, hv * factor)
    return tuple(jnp.where(wet_now, new, value) for new, value in zip(fresh, old))


def repeat_steps(ctl, wet_from, deltas, early, work, other, sems):
    incoming = []
    for ref in early:
        begin = 0 if ref is early[0] else early[0].shape[1]
        incoming += start_all(
            ((ref, work.at[:, begin : begin + ref.shape[1]]),), sems, len(incoming)
        )
    row_ids = lax.broadcasted_iota(jnp.int32, (AGAIN, TILE), 0)
    lane = lax.broadcasted_iota(jnp.int32, (AGAIN, LANES), 1)
    start = tuple(jnp.zeros((1, TILE), jnp.float32) for _ in range(4))

    def halves(value):
        return value[:, :LANES], value[:, LANES:]

    def right_of(value):
        low, high = (pltpu.roll(part, LANES - 1, 1) for part in halves(value))
        return jnp.concatenate([jnp.where(lane == LANES - 1, high, low), high], 1)

    def left_of(value):
        low, high = (pltpu.roll(part, 1, 1) for part in halves(value))
        return jnp.concatenate([low, jnp.where(lane == 0, low, high)], 1)

    def down(value):
        return pltpu.roll(value, AGAIN + 7, 0)[:AGAIN]

    for step in range(STEPS):
        source, target = (work, other) if step % 2 == 0 else (other, work)
        delta = deltas[step][0:1, :]
        wet_now = flag(ctl, wet_from + step)

        def group(index, carry, source=source, target=target, delta=delta, wet_now=wet_now):
            base = pl.multiple_of(index * AGAIN, AGAIN)
            rows = pl.ds(base, AGAIN)
            after = pl.ds(pl.multiple_of(jnp.minimum(base + AGAIN, EARLY - 8), 8), 8)
            refs = [source.at[field] for field in range(3)] + [work.at[3]]
            fields = [jnp.concatenate([ref[rows, :], ref[after, :]], 0) for ref in refs]
            cells_x, cells_y = cell(*fields[:3])
            here_x = tuple(value[:AGAIN] for value in cells_x)
            here_y = tuple(value[:AGAIN] for value in cells_y)
            faces_x = face(here_x, tuple(down(value) for value in cells_x))
            turned = tuple(pltpu.roll(value, 1, 0) for value in faces_x)
            change_x = tuple(
                value - jnp.where(row_ids == 0, before, moved)
                for value, before, moved in zip(faces_x, carry[:3], turned)
            )
            ground = fields[3][:AGAIN]
            ground_up = pltpu.roll(ground, 1, 0)
            slope_x = down(fields[3]) - jnp.where(row_ids == 0, carry[3], ground_up)
            carried = tuple(value[0:1, :] for value in turned) + (ground_up[0:1, :],)
            faces_y = face(here_y, tuple(right_of(value) for value in here_y))
            change_y = tuple(value - left_of(value) for value in faces_y)
            slope_y = right_of(ground) - left_of(ground)
            old = tuple(value[:AGAIN] for value in fields[:3])
            weight = SLOPE * old[0]
            slopes = (
                SCALE * (change_x[0] + change_y[0]),
                SCALE * (change_x[1] + change_y[2]) + weight * slope_x,
                SCALE * (change_x[2] + change_y[1]) + weight * slope_y,
            )
            for field, value in enumerate(
                moved_on(old, slopes, work[4, rows, :], delta, wet_now)
            ):
                target[field, rows, :] = value
            return carried

        if step == 0:
            wait_all(incoming)
        lax.fori_loop(0, EARLY // AGAIN, group, start)


def late_rows(tile, late):
    row = sublanes()
    kept = EARLY - 8
    lane = lax.broadcasted_iota(jnp.int32, (8, LANES), 1)
    for field in range(3):
        late[field, 0:8, :] = jnp.where(
            row < 3, tile[field, 0:8, :], tile[field, kept : kept + 8, :]
        )
        packed = [jnp.zeros((8, LANES), jnp.float32)] * 2
        for block in range(EARLY // 8):
            rows = slice(8 * block, 8 * block + 8)
            sides = jnp.where(lane < 64, tile[field, rows, :LANES], tile[field, rows, LANES:])
            turned = pltpu.roll(sides, (3 + 8 * block) % LANES, 1)
            which = block // 16
            packed[which] = jnp.where(lane // 8 == block % 16, turned, packed[which])
        late[field, 8:16, :] = jnp.concatenate(packed, 1)
        late[field, 16:, :] = tile[field, EARLY:, :]


def merge(late, early, tile):
    for field in range(3):
        merge_field(field, late, early, tile)


def merge_field(field, late, early, tile):
    row = sublanes()
    lane = lax.broadcasted_iota(jnp.int32, (8, LANES), 1)
    first = late[field, 0:8, :]
    for block in range(EARLY // 8):
        rows = slice(8 * block, 8 * block + 8)
        which = block // 16
        packed = late[field, 8:16, which * LANES : (which + 1) * LANES]
        sides = pltpu.roll(packed, (-3 - 8 * block) % LANES, 1)
        value = early[field, rows, :]
        value = jnp.concatenate(
            [
                jnp.where(lane < 3, sides, value[:, :LANES]),
                jnp.where(lane >= LANES - 3, sides, value[:, LANES:]),
            ],
            1,
        )
        if block == 0:
            value = jnp.where(row < 3, first, value)
        if block == EARLY // 8 - 1:
            value = jnp.where(row < 5, value, first)
        tile[field, rows, :] = value
    tile[field, EARLY:, :] = late[field, 16:, :]


def repeat_second(ctl, delta0, delta1, delta2, low, high, late, out, late_out, work, tile, sems):
    near = start_all(((late, late_out),), sems, 2)
    repeat_steps(ctl, WET_SECOND, (delta0, delta1, delta2), (low, high), work, tile, sems)
    wait_all(start_all(((tile, out),), sems) + near)


def repeat_first(
    ctl, delta0, delta1, delta2, low, high, late_in, staying, out, work, other, tile, late, sems
):
    rest = out.at[1 - ctl[MOVE + 1]]
    again = ctl[MOVE] == ctl[MOVE + 1]

    @pl.when(again)
    def _():
        wait_all(start_all(((staying, tile),), sems))

    @pl.when(jnp.logical_not(again))
    def _():
        copies = start_all(((late_in, late),), sems, 2)
        repeat_steps(ctl, WET_FIRST, (delta0, delta1, delta2), (low, high), work, other, sems)
        wait_all(copies)
        merge(late, other, tile)

    wait_all(start_all(((tile, rest),), sems))


def finish(ctl, late, early, before, out, tile, sems):
    del before
    copies = []
    for field in range(3):
        merge_field(field, late, early, tile)
        copies += start_all(
            ((tile.at[field], out.at[ctl[MOVE + 1], field]),), sems, field
        )
    wait_all(copies)


def second_late(ctl, arrived, own, order, leaving):
    del order
    again = ctl[MOVE] == ctl[MOVE + 1]
    for field in range(3):
        leaving[field] = jnp.where(again, arrived[field], own[field])


def correct_rows(ctl, slot, got, ground, state, rate, bottom):
    position = jnp.where(ctl[SLOT_LOW] == slot, 0, 1)
    device = lax.axis_index("xb") * 2 + lax.axis_index("yb")
    wall = WALL_WEST if bottom else WALL_EAST

    @pl.when(jnp.logical_not(flag(ctl, wall + position)))
    def _():
        peer = device - 2 if bottom else device + 2
        block = pl.ds(pl.multiple_of(peer * 8, 8), 8)
        lines = got[block, :TILE]
        grounds = ground[block, :TILE]
        stride = 4 if got.shape[1] > TILE else 3

        def line(offset):
            other = offset + stride
            picked = jnp.where(
                position == 0, lines[offset : offset + 1, :], lines[other : other + 1, :]
            )
            return jnp.broadcast_to(picked, (8, TILE))

        ghost, _ = cell(*(line(field) for field in range(3)))
        ghost_ground = jnp.where(position == 0, grounds[3:4, :], grounds[7:8, :])
        rows = slice(0, 8) if bottom else slice(TILE - 8, TILE)
        own = [state[slot, field, rows, :] for field in range(3)]
        here, _ = cell(*own)
        fluxes = face(ghost, here) if bottom else face(here, ghost)
        push = SCALE * fluxes[1] + (SLOPE * own[0]) * ghost_ground
        row = sublanes()
        sign = -1.0 if bottom else 1.0
        chosen = row == (0 if bottom else 7)
        for field, value in enumerate((SCALE * fluxes[0], push, SCALE * fluxes[2])):
            rate[slot, field, rows, :] += jnp.where(chosen, sign * value, 0.0)


def column_fix(got, ground, columns):
    upper = lax.axis_index("yb")
    device = lax.axis_index("xb") * 2 + upper
    peer = device + 1 - 2 * upper
    block = pl.ds(pl.multiple_of(peer * 8, 8), 8)
    lines = got[block, :TILE]
    ghost_ground = ground[block, :TILE][3:4]
    mine = columns[...]
    _, ghost = cell(lines[0:1], lines[1:2], lines[2:3])
    _, own = cell(mine[0:1], mine[1:2], mine[2:3])
    low = upper == 0
    left = tuple(jnp.where(low, a, b) for a, b in zip(own, ghost))
    right = tuple(jnp.where(low, b, a) for a, b in zip(own, ghost))
    fluxes = face(left, right)
    sign = jnp.where(low, 1.0, -1.0)
    push = SCALE * fluxes[1] + (SLOPE * mine[0:1]) * ghost_ground
    block8 = stacked(
        [sign * SCALE * fluxes[0], sign * SCALE * fluxes[2], sign * push],
        jnp.zeros((8, TILE), jnp.float32),
    )
    return jnp.transpose(
        jnp.concatenate([block8, jnp.zeros((LANES - 8, TILE), jnp.float32)], 0)
    )


def last_update(moving, ctl, got, ground, columns, state, manning, rate, order, *rest):
    del order
    slot = ctl[MOVE] if moving else 1 - ctl[MOVE]
    update(STEPS - 1, ctl, got, ground, columns, state, manning, rate, *rest, slots=(slot,))


def update(
    step, ctl, got_in, ground_in, columns_in, state_in, manning_in, rate_in, *rest,
    passing=None, slots=(0, 1),
):
    more = step + 1 < STEPS
    fresh_out, first_out, second_out, delta_out = rest[:4]
    rest = rest[4:]
    state, manning, rate, fresh, got, ground, columns, first, second, delta_keep, sems = rest
    out, columns_out = first, second
    small = start_all(
        ((got_in, got), (ground_in, ground), (columns_in, columns)), sems, 5 * PARTS
    )
    size = 2 * TILE // PARTS
    parts = [
        (slot, slice(k * size, (k + 1) * size)) for slot in slots for k in range(PARTS // 2)
    ]
    incoming = []
    for index, (slot, rows) in enumerate(parts):
        incoming.append(
            start_all(
                (
                    (rate_in.at[slot, :, rows], rate.at[slot, :, rows]),
                    (state_in.at[slot, :, rows], state.at[slot, :, rows]),
                    (manning_in.at[slot, rows], manning.at[slot, rows]),
                ),
                sems,
                3 * index,
            )
        )
    wait_all(small)
    upper = lax.axis_index("yb")
    devices = 2 * lax.axis_size("xb")
    begin = TILE if got.shape[1] > TILE else 0
    tops = got[0:8, begin : begin + LANES]
    for peer in range(1, devices):
        tops = jnp.maximum(tops, got[peer * 8 : peer * 8 + 8, begin : begin + LANES])
    delta = (COURANT * SPACING) / tops[TOP : TOP + 1, :]
    delta = jnp.concatenate([delta, delta], 1)
    delta_keep[...] = jnp.broadcast_to(delta, (8, TILE))
    outgoing = start_all(((delta_keep, delta_out),), sems, 5 * PARTS + 3)
    fix = column_fix(got, ground, columns)
    facing = jnp.where(upper > 0, ctl[SLOT_LOW], 1 - ctl[SLOT_LOW])
    begin = pl.multiple_of((1 - upper) * LANES, LANES)
    goal = (1 - upper) * (LANES - 1)
    lane = lax.broadcasted_iota(jnp.int32, (size, LANES), 1)
    total = jnp.zeros((ROWS, TILE), jnp.float32)
    for index, (slot, part_rows) in enumerate(parts):
        wait_all(incoming[index])
        if part_rows.start == 0:
            correct_rows(ctl, slot, got, ground, state, rate, True)
        if part_rows.stop == TILE:
            correct_rows(ctl, slot, got, ground, state, rate, False)

        @pl.when(facing == slot)
        def _(slot=slot, part_rows=part_rows):
            for field in range(3):
                turned = pltpu.roll(
                    fix[part_rows], lax.rem(goal + LANES - field, LANES), 1
                )
                rate[slot, field, part_rows, pl.ds(begin, LANES)] += jnp.where(
                    lane == goal, turned, 0.0
                )

        wet_now = flag(ctl, WET + 2 * step + slot)

        def group(index, best, slot=slot, wet_now=wet_now):
            rows = pl.ds(pl.multiple_of(index * ROWS, ROWS), ROWS)
            old = tuple(state[slot, field, rows, :] for field in range(3))
            slopes = tuple(rate[slot, field, rows, :] for field in range(3))
            h, hu, hv = moved_on(old, slopes, manning[slot, rows, :], delta, wet_now)
            fresh[slot, 0, rows, :] = h
            fresh[slot, 1, rows, :] = hu
            fresh[slot, 2, rows, :] = hv
            if more:
                along_x, along_y = cell(h, hu, hv)
                best = jnp.maximum(best, jnp.maximum(along_x[5], along_y[5]))
            return best

        best = lax.fori_loop(
            part_rows.start // ROWS,
            part_rows.stop // ROWS,
            group,
            jnp.zeros((ROWS, TILE), jnp.float32),
        )
        if more:
            best = jnp.where(flag(ctl, WET + 2 * step + 2 + slot), best, 0.0)
            total = jnp.maximum(total, best)
        target = fresh_out.at[slot, :, part_rows] if more else fresh_out.at[:, part_rows]
        outgoing += start_all(
            ((fresh.at[slot, :, part_rows], target),), sems, 3 * PARTS + index
        )
        if passing and index == PARTS // 2:
            passing.middle()
    if more:
        messages(ctl, fresh, None, jnp.max(total, keepdims=True), out, columns_out)
        outgoing += start_all(((out, first_out), (columns_out, second_out)), sems, 4 * PARTS)
    else:
        second[...] = jnp.zeros_like(second)
        late_rows(fresh.at[slots[0]], first)
        outgoing += start_all(((first, first_out), (second, second_out)), sems, 4 * PARTS)
    wait_all(outgoing)


def vmem():
    return pl.BlockSpec(memory_space=pltpu.VMEM)


def smem():
    return pl.BlockSpec(memory_space=pltpu.SMEM)


def hbm():
    return pl.BlockSpec(memory_space=pltpu.HBM)


def anywhere():
    return pl.BlockSpec(memory_space=pl.ANY)


def call(
    kernel, outs, out_specs, in_specs, flops, scratch=(), aliases=None, room=VMEM_BYTES, moved=4
):
    return pl.pallas_call(
        kernel,
        scratch_shapes=scratch,
        input_output_aliases=aliases or {},
        out_shape=outs,
        in_specs=in_specs,
        out_specs=out_specs,
        compiler_params=pltpu.CompilerParams(vmem_limit_bytes=room),
        cost_estimate=pl.CostEstimate(flops=flops, bytes_accessed=moved << 20, transcendentals=0),
    )


def f32(*shape):
    return jax.ShapeDtypeStruct(shape, jnp.float32)


def spread(fast):
    return lax.all_to_all(fast, ("xb", "yb"), split_axis=0, concat_axis=0, tiled=True)


def body(state, bed, manning, neighbours, wet, moves):
    shape = f32(*state.shape)
    devices = lax.axis_size("xb") * lax.axis_size("yb")
    whole = pltpu.VMEM(state.shape, jnp.float32)
    part = pltpu.VMEM(bed.shape, jnp.float32)
    tile_shape = f32(*state.shape[1:])
    early_shape = f32(5, EARLY, TILE)
    early_state = f32(3, EARLY, TILE)
    late_shape = f32(3, LATE, TILE)
    delta_shape = f32(8, TILE)

    def buffer(like):
        return pltpu.VMEM(like.shape, jnp.float32)

    piece_shapes = tuple(f32(5, end - begin, TILE) for begin, end in PIECES)
    out, columns, ctl = call(
        opening,
        (
            f32(8 * devices, TILE + LANES),
            f32(8, TILE),
            jax.ShapeDtypeStruct((CONTROLS,), jnp.int32),
        ),
        (vmem(), vmem(), smem()),
        [hbm()] * 5,
        4 << 20,
        [
            whole,
            part,
            pltpu.SMEM(neighbours.shape[::-1], jnp.int32),
            pltpu.SMEM(wet.shape, jnp.int32),
            pltpu.SMEM(moves.shape, jnp.int32),
            pltpu.SemaphoreType.DMA((6,)),
        ],
    )(state, bed, neighbours.T, wet, moves)
    state_first = state
    ground = None
    deltas = []
    for step in range(STEPS):
        got = spread(out)
        ground = got if step == 0 else ground
        scratch = [whole, part, whole, pltpu.SemaphoreType.DMA((3 * CHUNKS,))]
        piece_scratch = [
            [buffer(piece), pltpu.SemaphoreType.DMA((2,))] for piece in piece_shapes
        ]
        if step == 1:
            rate, leaving = call(
                rates_and_leaving,
                (shape, piece_shapes[0]),
                (hbm(),) * 2,
                [smem()] + [hbm()] * 5,
                16 << 20,
                scratch + piece_scratch[0],
            )(ctl, state, bed, state_first, manning, early_first[0])
            early_second = [shifted(leaving, "xb", 1)]
        elif step == 2:
            rate = call(rates_after, shape, hbm(), [smem()] + [hbm()] * 3, 16 << 20, scratch)(
                ctl, state, bed, early_second[0]
            )
        else:
            rate, *leaving = call(
                rates_and_splitting,
                (shape,) + piece_shapes,
                (hbm(),) * 3,
                [smem()] + [hbm()] * 3,
                16 << 20,
                scratch + [buffer(early_shape), pltpu.SemaphoreType.DMA((5,))],
            )(ctl, state, bed, manning)
            held = call(
                hold, piece_shapes[0], hbm(), [hbm()] * 3, 1 << 10, aliases={2: 0}
            )(rate, got, leaving[0])
            early_first = [shifted(held, "xb", 1)]
        more = step + 1 < STEPS
        shapes = (f32(8 * devices, TILE) if more else late_shape), f32(8, TILE)
        passing = step == 1
        work = [
            whole,
            part,
            whole,
            whole,
            pltpu.VMEM(got.shape, jnp.float32),
            pltpu.VMEM(ground.shape, jnp.float32),
            pltpu.VMEM((8, TILE), jnp.float32),
            buffer(shapes[0]),
            buffer(shapes[1]),
            buffer(delta_shape),
            pltpu.SemaphoreType.DMA((5 * PARTS + 4,)),
        ]
        operands = ctl, got, ground, columns, state, manning, rate
        if not more:
            break
        outs = call(
            functools.partial(update_and_leaving if passing else update, step),
            (shape,) + shapes + (delta_shape,) + ((piece_shapes[1],) if passing else ()),
            (hbm(),) * (5 if passing else 4),
            [smem()] + [hbm()] * (9 if passing else 6),
            8 << 20,
            work + (piece_scratch[1] if passing else []),
            moved=10,
        )(*operands, *((state_first, bed, early_first[1]) if passing else ()))
        state, out, columns, delta, *passed = outs
        deltas.append(delta)
        if step == 0:
            held = call(
                hold, piece_shapes[1], hbm(), [hbm()] * 3, 1 << 10, aliases={2: 0}
            )(delta, delta, leaving[1])
            early_first.append(shifted(held, "xb", 1))
        elif step == 1:
            early_second.append(shifted(passed[0], "xb", 1))

    def finish_step(moving, order):
        return call(
            functools.partial(last_update, moving),
            (tile_shape,) + shapes + (delta_shape,),
            (hbm(),) * 4,
            [smem()] + [hbm()] * 7,
            8 << 20,
            work,
            moved=10,
        )(*operands, order)

    _, late_first, _, delta = finish_step(True, early_second[1])
    staying, late_second, _, _ = finish_step(False, delta)
    deltas.append(delta)
    room = 16 << 20
    late_arrived = shifted(late_first, "xb", 1)
    second, late_second = call(
        repeat_second,
        (early_state, late_shape),
        (anywhere(), vmem()),
        [smem()] + [vmem()] * 3 + [anywhere()] * 3,
        8 << 20,
        [buffer(early_shape), buffer(early_state), pltpu.SemaphoreType.DMA((3,))],
        room=room,
    )(ctl, *deltas, *early_second, late_second)
    leaving = call(
        second_late,
        late_shape,
        vmem(),
        [smem(), vmem(), vmem(), anywhere()],
        1 << 10,
        room=room,
    )(ctl, late_arrived, late_second, second)
    late_next = shifted(leaving, "xb", 1)
    final = call(
        repeat_first,
        shape,
        hbm(),
        [smem()] + [vmem()] * 3 + [anywhere()] * 4,
        8 << 20,
        [
            buffer(early_shape),
            buffer(early_state),
            buffer(tile_shape),
            buffer(late_shape),
            pltpu.SemaphoreType.DMA((3,)),
        ],
        room=room,
    )(ctl, *deltas, *early_first, late_arrived, staying)
    return call(
        finish,
        shape,
        hbm(),
        [smem(), vmem(), vmem(), hbm()],
        1 << 20,
        [buffer(tile_shape), pltpu.SemaphoreType.DMA((3,))],
        {3: 0},
        room=room,
    )(ctl, late_next, second, final)


def solution(mesh):
    placed = (
        P(("runs", "xb", "yb"), None, None, None),
        P(("runs", "xb", "yb"), None, None),
        P(("runs", "xb", "yb"), None, None),
        P("runs", None),
        P(None, "runs"),
        P(None, "runs"),
    )
    return jax.shard_map(
        body,
        mesh=mesh,
        in_specs=placed,
        out_specs=P(("runs", "xb", "yb"), None, None, None),
        check_vma=False,
    )
```

```python
import functools

import jax
import jax.numpy as jnp
from jax import lax
from jax.experimental import pallas as pl
from jax.experimental.pallas import tpu as pltpu
from jax.sharding import PartitionSpec as P

STEPS = 3
GRAVITY = 9.81
ROOT_G = GRAVITY**0.5
SPACING = 5.0
COURANT = 0.2
ROWS = 32
LANES = 128
TILE = 256
VMEM_BYTES = 60 * 1024 * 1024
SLOT_LOW, WALL_WEST, WALL_EAST, WALL_OUTER, WET, MOVE = 0, 1, 3, 5, 7, 13
WET_FIRST, WET_SECOND = 16, 19
CONTROLS = 24
EARLY = 144
PIECES = ((0, 80), (80, 144))
AGAIN = 48
LATE = TILE - EARLY + 16
CHUNKS = 8
PARTS = 8
STRIP = 32
TOP = 6
SCALE = 0.5 / SPACING
SLOPE = GRAVITY / (2.0 * SPACING)


def shifted(value, axis, steps, around=True):
    count = lax.axis_size(axis)
    pairs = [(source, (source + steps) % count) for source in range(count)]
    if not around:
        pairs = [pair for pair in pairs if abs(pair[0] - pair[1]) == abs(steps)]
    return lax.ppermute(value, axis, pairs)


def cell(h, hu, hv):
    root = lax.rsqrt(h)
    inverse = root * root
    u = hu * inverse
    v = hv * inverse
    celerity = ROOT_G * (h * root)
    pressure = (0.5 * GRAVITY) * (h * h)
    cross = hu * v
    speed_x = jnp.abs(u) + celerity
    speed_y = jnp.abs(v) + celerity
    along_x = (h, hu, hv, hu * u + pressure, cross, speed_x)
    along_y = (h, hv, hu, hv * v + pressure, cross, speed_y)
    return along_x, along_y


def face(left, right):
    wave = jnp.maximum(left[5], right[5])
    return (
        (left[1] + right[1]) - wave * (right[0] - left[0]),
        (left[3] + right[3]) - wave * (right[1] - left[1]),
        (left[4] + right[4]) - wave * (right[2] - left[2]),
    )


def slot_of(ctl, position):
    low = ctl[SLOT_LOW]
    return low if position == 0 else 1 - low


def flag(ctl, index):
    return ctl[index] > 0


def start_all(pairs, sems, first=0):
    copies = [
        pltpu.make_async_copy(src, dst, sems.at[first + k]) for k, (src, dst) in enumerate(pairs)
    ]
    for copy in copies:
        copy.start()
    return copies


def wait_all(copies):
    for copy in copies:
        copy.wait()


def sublanes(width=TILE):
    return lax.broadcasted_iota(jnp.int32, (8, width), 0)


def stacked(lines, base):
    row = sublanes()
    for index, line in enumerate(lines):
        base = jnp.where(row == index, jnp.broadcast_to(line, (8, TILE)), base)
    return base


def messages(ctl, state, bed, fastest, out, columns):
    upper = lax.axis_index("yb")
    column = lax.axis_index("xb")
    last = lax.axis_size("xb") - 1
    devices = 2 * (last + 1)
    device = column * 2 + upper
    top = jnp.broadcast_to(fastest, (8, TILE))
    for peer in range(devices):
        out[peer * 8 : peer * 8 + 8, :TILE] = top
        if bed is not None:
            out[peer * 8 : peer * 8 + 8, TILE:] = top[:, :LANES]
    row = sublanes()

    def edge(line):
        rows = slice(line, line + 1)
        lines = []
        for position in range(2):
            slot = slot_of(ctl, position)
            lines += [state[slot, field, rows, :] for field in range(3)]
            if bed is not None:
                lines.append(bed[slot, rows, :])
        return stacked(lines, top)

    for inside, peer, line in (
        (column > 0, device - 2, 0),
        (column < last, device + 2, TILE - 1),
    ):

        @pl.when(inside)
        def _(peer=peer, line=line):
            out[pl.ds(pl.multiple_of(peer * 8, 8), 8), :TILE] = edge(line)

    slot = jnp.where(upper > 0, ctl[SLOT_LOW], 1 - ctl[SLOT_LOW])
    begin = pl.multiple_of((1 - upper) * LANES, LANES)
    lane = lax.broadcasted_iota(jnp.int32, (TILE, LANES), 1)
    packed = None
    for field in range(4 if bed is not None else 3):
        if field < 3:
            part = state[slot, field, :, pl.ds(begin, LANES)]
        else:
            part = bed[slot, :, pl.ds(begin, LANES)]
        turned = pltpu.roll(part, field + 1 - upper, 1)
        packed = turned if field == 0 else jnp.where(lane == field, turned, packed)
    lines = jnp.transpose(packed)[:8]
    columns[...] = lines
    start = pl.multiple_of((device + 1 - 2 * upper) * 8, 8)
    out[pl.ds(start, 8), :TILE] = jnp.where(row == TOP, top, lines)


def opening(
    state_in, bed_in, neighbours_in, wet_in, moves_in,
    out, columns, ctl,
    state, bed, neighbours, wet, moves, sems,
):
    copies = start_all(
        (
            (neighbours_in, neighbours),
            (wet_in, wet),
            (moves_in, moves),
            (state_in.at[0], state.at[0]),
            (state_in.at[1], state.at[1]),
            (bed_in, bed),
        ),
        sems,
    )
    device = lax.axis_index("xb") * 2 + lax.axis_index("yb")
    wait_all(copies[:3])
    first = device * 2
    low = jnp.where(neighbours[3, first] == first + 1, 0, 1)
    ctl[SLOT_LOW] = low
    for position in range(2):
        slot = low if position == 0 else 1 - low
        tile = first + slot
        ctl[WALL_WEST + position] = (neighbours[0, tile] < 0).astype(jnp.int32)
        ctl[WALL_EAST + position] = (neighbours[1, tile] < 0).astype(jnp.int32)
        ctl[WALL_OUTER + position] = (neighbours[2 + position, tile] < 0).astype(jnp.int32)
    for step in range(STEPS):
        for slot in range(2):
            ctl[WET + 2 * step + slot] = wet[step, first + slot]
        ctl[MOVE + step] = moves[step, device]
    count = lax.axis_size("xb")
    upper = lax.axis_index("yb")
    column = lax.axis_index("xb")
    source = lax.rem(column + count - 1, count) * 2 + upper
    before = lax.rem(column + count - 2, count) * 2 + upper
    again = moves[0, source] == moves[1, source]
    tile_first = source * 2 + moves[0, source]
    tile_second = jnp.where(
        again, before * 2 + moves[0, before], source * 2 + 1 - moves[0, source]
    )
    for step in range(STEPS):
        ctl[WET_FIRST + step] = wet[step, tile_first]
        ctl[WET_SECOND + step] = wet[step, tile_second]

    total = jnp.zeros((ROWS, TILE), jnp.float32)
    for slot in range(2):
        copies[3 + slot].wait()

        def group(index, best, slot=slot):
            rows = pl.ds(pl.multiple_of(index * ROWS, ROWS), ROWS)
            along_x, along_y = cell(*(state[slot, field, rows, :] for field in range(3)))
            return jnp.maximum(best, jnp.maximum(along_x[5], along_y[5]))

        best = lax.fori_loop(0, TILE // ROWS, group, jnp.zeros((ROWS, TILE), jnp.float32))
        total = jnp.maximum(total, jnp.where(wet[0, first + slot] > 0, best, 0.0))
    copies[5].wait()
    messages(ctl, state, bed, jnp.max(total, keepdims=True), out, columns)


def hold(first, second, leaving, same):
    del first, second, leaving, same


class Splitting:
    def __init__(self, ctl, state_in, bed_in, manning_in, leaving, buffer, sems):
        slot = ctl[MOVE]
        rows = slice(0, EARLY)
        pairs = (
            (state_in.at[slot, :, rows], buffer.at[0:3]),
            (bed_in.at[slot, rows], buffer.at[3]),
            (manning_in.at[slot, rows], buffer.at[4]),
        )
        self.incoming = [
            pltpu.make_async_copy(src, dst, sems.at[k]) for k, (src, dst) in enumerate(pairs)
        ]
        self.outgoing = [
            pltpu.make_async_copy(buffer.at[:, begin:end], piece, sems.at[3 + k])
            for k, ((begin, end), piece) in enumerate(zip(PIECES, leaving))
        ]

    def start(self):
        for copy in self.incoming:
            copy.start()

    def middle(self):
        wait_all(self.incoming)
        for copy in self.outgoing:
            copy.start()

    def end(self):
        wait_all(self.outgoing)


class Passing:
    def __init__(self, ctl, piece, state_in, bed_in, manning_in, arrived, leaving, buffer, sems):
        self.again = ctl[MOVE] == ctl[MOVE + 1]
        self.other = 1 - ctl[MOVE]
        self.rows = slice(*piece)
        self.refs = state_in, bed_in, manning_in
        self.incoming = pltpu.make_async_copy(arrived, buffer, sems.at[0])
        self.outgoing = pltpu.make_async_copy(buffer, leaving, sems.at[1])
        self.buffer = buffer
        self.sem = sems.at[0]

    def start(self):
        state_in, bed_in, manning_in = self.refs
        buffer, sem, rows = self.buffer, self.sem, self.rows

        @pl.when(self.again)
        def _():
            self.incoming.start()

        @pl.when(jnp.logical_not(self.again))
        def _():
            pltpu.make_async_copy(state_in.at[self.other, :, rows], buffer.at[0:3], sem).start()
            pltpu.make_async_copy(bed_in.at[self.other, rows], buffer.at[3], sem).start()
            pltpu.make_async_copy(manning_in.at[self.other, rows], buffer.at[4], sem).start()

    def middle(self):
        self.incoming.wait()
        self.outgoing.start()

    def end(self):
        self.outgoing.wait()


def rates_and_splitting(
    ctl, state_in, bed_in, manning_in, rate_out, leaving_low, leaving_high,
    state, bed, rate, sems, buffer, moving,
):
    leaving = leaving_low, leaving_high
    splitting = Splitting(ctl, state_in, bed_in, manning_in, leaving, buffer, moving)
    rates(ctl, state_in, bed_in, rate_out, state, bed, rate, sems, splitting)


def rates_and_leaving(
    ctl, state_in, bed_in, state_first, manning_in, arrived, rate_out, leaving,
    state, bed, rate, sems, buffer, moving,
):
    passing = Passing(
        ctl, PIECES[0], state_first, bed_in, manning_in, arrived, leaving, buffer, moving
    )
    rates(ctl, state_in, bed_in, rate_out, state, bed, rate, sems, passing)


def update_and_leaving(
    step, ctl, got_in, ground_in, columns_in, state_in, manning_in, rate_in,
    state_first, bed_in, arrived, fresh_out, first_out, second_out, delta_out, leaving, *rest
):
    *rest, buffer, moving = rest
    passing = Passing(
        ctl, PIECES[1], state_first, bed_in, manning_in, arrived, leaving, buffer, moving
    )
    passing.start()
    update(
        step, ctl, got_in, ground_in, columns_in, state_in, manning_in, rate_in,
        fresh_out, first_out, second_out, delta_out, *rest, passing=passing,
    )
    passing.end()


def rates_after(ctl, state_in, bed_in, order, *rest):
    del order
    rates(ctl, state_in, bed_in, *rest)


def rates(ctl, state_in, bed_in, rate_out, state, bed, rate, sems, passing=None):
    width = 2 * TILE
    row_ids = lax.broadcasted_iota(jnp.int32, (STRIP, width), 0)
    row8 = sublanes(width)
    lane = lax.broadcasted_iota(jnp.int32, (STRIP, LANES), 1)
    last = TILE // STRIP - 1
    chunk = TILE // CHUNKS
    slots = [slot_of(ctl, position) for position in range(2)]
    incoming = []
    for part in range(CHUNKS):
        rows = slice(part * chunk, (part + 1) * chunk)
        incoming.append(
            start_all(
                (
                    (state_in.at[:, :, rows], state.at[:, :, rows]),
                    (bed_in.at[:, rows], bed.at[:, rows]),
                ),
                sems,
                2 * part,
            )
        )
    if passing:
        passing.start()
    keep_west, keep_east, keep_south, keep_north = (
        jnp.where(flag(ctl, index), 1.0, 0.0)
        for index in (WALL_WEST, WALL_EAST, WALL_OUTER, WALL_OUTER + 1)
    )

    def strip(field, rows):
        if field == 3:
            return jnp.concatenate([bed[slot, rows, :] for slot in slots], 1)
        return jnp.concatenate([state[slot, field, rows, :] for slot in slots], 1)

    def blocks(value):
        return [value[:, k * LANES : (k + 1) * LANES] for k in range(4)]

    def right_of(value, end=None):
        turned = [pltpu.roll(part, LANES - 1, 1) for part in blocks(value)]
        after = turned[1:] + [turned[3] if end is None else end]
        return jnp.concatenate(
            [
                jnp.where(lane == LANES - 1, following, part)
                if following is not part
                else part
                for part, following in zip(turned, after)
            ],
            1,
        )

    def left_of(value, end):
        turned = [pltpu.roll(part, 1, 1) for part in blocks(value)]
        before = [end] + turned[:3]
        return jnp.concatenate(
            [jnp.where(lane == 0, previous, part) for part, previous in zip(turned, before)], 1
        )

    def down(value):
        return pltpu.roll(value, STRIP + 7, 0)[:STRIP]

    def group(index, carry):
        base = pl.multiple_of(index * STRIP, STRIP)
        rows = pl.ds(base, STRIP)
        after = pl.ds(pl.multiple_of(jnp.minimum(base + STRIP, TILE - 8), 8), 8)
        at_end = index == last
        fields = [
            jnp.concatenate([strip(field, rows), strip(field, after)], 0) for field in range(3)
        ]
        cells_x, cells_y = cell(*fields)
        here_x = tuple(value[:STRIP] for value in cells_x)
        here_y = tuple(value[:STRIP] for value in cells_y)

        ending = jnp.logical_and(row8 == 7, at_end)
        faces = list(face(here_x, tuple(down(value) for value in cells_x)))
        wall = keep_east * (2.0 * (here_x[3] + here_x[5] * here_x[1])[STRIP - 8 :])
        for component, value in enumerate((0.0, wall, 0.0)):
            upper = faces[component]
            faces[component] = jnp.concatenate(
                [upper[: STRIP - 8], jnp.where(ending, value, upper[STRIP - 8 :])], 0
            )
        turned = tuple(pltpu.roll(value, 1, 0) for value in faces)
        change_x = tuple(
            value - jnp.where(row_ids == 0, before, moved)
            for value, before, moved in zip(faces, carry[:3], turned)
        )
        ground = strip(3, rows)
        ground_after = jnp.where(
            at_end,
            jnp.broadcast_to(keep_east * ground[STRIP - 1 :], (8, width)),
            strip(3, after),
        )
        ground_up = pltpu.roll(ground, 1, 0)
        slope_x = down(jnp.concatenate([ground, ground_after], 0)) - jnp.where(
            row_ids == 0, carry[3], ground_up
        )
        carried = tuple(value[0:1, :] for value in turned) + (ground_up[0:1, :],)

        faces_y = list(face(here_y, tuple(right_of(value) for value in here_y)))
        normal = here_y[3]
        spread_y = here_y[5] * here_y[1]
        north = keep_north * (2.0 * (normal + spread_y)[:, width - LANES :])
        south = keep_south * (2.0 * (normal - spread_y)[:, :LANES])
        change_y = []
        for component, (high, low) in enumerate(((0.0, 0.0), (north, south), (0.0, 0.0))):
            parts = blocks(faces_y[component])
            parts[3] = jnp.where(lane == LANES - 1, high, parts[3])
            value = jnp.concatenate(parts, 1)
            change_y.append(value - left_of(value, low))
        slope_y = right_of(ground, keep_north * ground[:, width - LANES :]) - left_of(
            ground, keep_south * ground[:, :LANES]
        )
        weight = SLOPE * here_x[0]
        results = (
            SCALE * (change_x[0] + change_y[0]),
            SCALE * (change_x[1] + change_y[2]) + weight * slope_x,
            SCALE * (change_x[2] + change_y[1]) + weight * slope_y,
        )
        for field, value in enumerate(results):
            for position, slot in enumerate(slots):
                rate[slot, field, rows, :] = value[:, position * TILE : (position + 1) * TILE]
        return carried

    wait_all(incoming[0])
    top, _ = cell(*(strip(field, slice(0, 8)) for field in range(3)))
    nothing = jnp.zeros((1, width), jnp.float32)
    carry = (
        nothing,
        keep_west * (2.0 * (top[3] - top[5] * top[1])[0:1]),
        nothing,
        keep_west * strip(3, slice(0, 8))[0:1],
    )
    per_chunk = chunk // STRIP
    outgoing = []
    for part in range(CHUNKS):
        if part + 1 < CHUNKS:
            wait_all(incoming[part + 1])
        carry = lax.fori_loop(part * per_chunk, (part + 1) * per_chunk, group, carry)
        rows = slice(part * chunk, (part + 1) * chunk)
        outgoing += start_all(
            ((rate.at[:, :, rows], rate_out.at[:, :, rows]),), sems, 2 * CHUNKS + part
        )
        if passing and part == CHUNKS // 2:
            passing.middle()
    wait_all(outgoing)
    if passing:
        passing.end()


def moved_on(old, slopes, rough, delta, wet_now):
    h, hu, hv = (value - delta * slope for value, slope in zip(old, slopes))
    inverse = 1.0 / h
    u = hu * inverse
    v = hv * inverse
    speed = jnp.sqrt(u * u + v * v)
    power = jnp.exp((-4.0 / 3.0) * jnp.log(jnp.abs(h)))
    drag = (GRAVITY * delta) * (rough * rough) * (speed * power)
    factor = 1.0 / (1.0 + drag)
    fresh = (h, hu * factor, hv * factor)
    return tuple(jnp.where(wet_now, new, value) for new, value in zip(fresh, old))


def repeat_steps(ctl, wet_from, deltas, early, work, other, sems):
    incoming = []
    for ref in early:
        begin = 0 if ref is early[0] else early[0].shape[1]
        incoming += start_all(
            ((ref, work.at[:, begin : begin + ref.shape[1]]),), sems, len(incoming)
        )
    row_ids = lax.broadcasted_iota(jnp.int32, (AGAIN, TILE), 0)
    lane = lax.broadcasted_iota(jnp.int32, (AGAIN, LANES), 1)
    start = tuple(jnp.zeros((1, TILE), jnp.float32) for _ in range(4))

    def halves(value):
        return value[:, :LANES], value[:, LANES:]

    def right_of(value):
        low, high = (pltpu.roll(part, LANES - 1, 1) for part in halves(value))
        return jnp.concatenate([jnp.where(lane == LANES - 1, high, low), high], 1)

    def left_of(value):
        low, high = (pltpu.roll(part, 1, 1) for part in halves(value))
        return jnp.concatenate([low, jnp.where(lane == 0, low, high)], 1)

    def down(value):
        return pltpu.roll(value, AGAIN + 7, 0)[:AGAIN]

    for step in range(STEPS):
        source, target = (work, other) if step % 2 == 0 else (other, work)
        delta = deltas[step][0:1, :]
        wet_now = flag(ctl, wet_from + step)

        def group(index, carry, source=source, target=target, delta=delta, wet_now=wet_now):
            base = pl.multiple_of(index * AGAIN, AGAIN)
            rows = pl.ds(base, AGAIN)
            after = pl.ds(pl.multiple_of(jnp.minimum(base + AGAIN, EARLY - 8), 8), 8)
            refs = [source.at[field] for field in range(3)] + [work.at[3]]
            fields = [jnp.concatenate([ref[rows, :], ref[after, :]], 0) for ref in refs]
            cells_x, cells_y = cell(*fields[:3])
            here_x = tuple(value[:AGAIN] for value in cells_x)
            here_y = tuple(value[:AGAIN] for value in cells_y)
            faces_x = face(here_x, tuple(down(value) for value in cells_x))
            turned = tuple(pltpu.roll(value, 1, 0) for value in faces_x)
            change_x = tuple(
                value - jnp.where(row_ids == 0, before, moved)
                for value, before, moved in zip(faces_x, carry[:3], turned)
            )
            ground = fields[3][:AGAIN]
            ground_up = pltpu.roll(ground, 1, 0)
            slope_x = down(fields[3]) - jnp.where(row_ids == 0, carry[3], ground_up)
            carried = tuple(value[0:1, :] for value in turned) + (ground_up[0:1, :],)
            faces_y = face(here_y, tuple(right_of(value) for value in here_y))
            change_y = tuple(value - left_of(value) for value in faces_y)
            slope_y = right_of(ground) - left_of(ground)
            old = tuple(value[:AGAIN] for value in fields[:3])
            weight = SLOPE * old[0]
            slopes = (
                SCALE * (change_x[0] + change_y[0]),
                SCALE * (change_x[1] + change_y[2]) + weight * slope_x,
                SCALE * (change_x[2] + change_y[1]) + weight * slope_y,
            )
            for field, value in enumerate(
                moved_on(old, slopes, work[4, rows, :], delta, wet_now)
            ):
                target[field, rows, :] = value
            return carried

        if step == 0:
            wait_all(incoming)
        lax.fori_loop(0, EARLY // AGAIN, group, start)


def late_rows(tile, late):
    row = sublanes()
    kept = EARLY - 8
    lane = lax.broadcasted_iota(jnp.int32, (8, LANES), 1)
    for field in range(3):
        late[field, 0:8, :] = jnp.where(
            row < 3, tile[field, 0:8, :], tile[field, kept : kept + 8, :]
        )
        packed = [jnp.zeros((8, LANES), jnp.float32)] * 2
        for block in range(EARLY // 8):
            rows = slice(8 * block, 8 * block + 8)
            sides = jnp.where(lane < 64, tile[field, rows, :LANES], tile[field, rows, LANES:])
            turned = pltpu.roll(sides, (3 + 8 * block) % LANES, 1)
            which = block // 16
            packed[which] = jnp.where(lane // 8 == block % 16, turned, packed[which])
        late[field, 8:16, :] = jnp.concatenate(packed, 1)
        late[field, 16:, :] = tile[field, EARLY:, :]


def merge(late, early, tile):
    for field in range(3):
        merge_field(field, late, early, tile)


def merge_field(field, late, early, tile):
    row = sublanes()
    lane = lax.broadcasted_iota(jnp.int32, (8, LANES), 1)
    first = late[field, 0:8, :]
    for block in range(EARLY // 8):
        rows = slice(8 * block, 8 * block + 8)
        which = block // 16
        packed = late[field, 8:16, which * LANES : (which + 1) * LANES]
        sides = pltpu.roll(packed, (-3 - 8 * block) % LANES, 1)
        value = early[field, rows, :]
        value = jnp.concatenate(
            [
                jnp.where(lane < 3, sides, value[:, :LANES]),
                jnp.where(lane >= LANES - 3, sides, value[:, LANES:]),
            ],
            1,
        )
        if block == 0:
            value = jnp.where(row < 3, first, value)
        if block == EARLY // 8 - 1:
            value = jnp.where(row < 5, value, first)
        tile[field, rows, :] = value
    tile[field, EARLY:, :] = late[field, 16:, :]


def repeat_second(ctl, delta0, delta1, delta2, low, high, late, out, late_out, work, tile, sems):
    near = start_all(((late, late_out),), sems, 2)
    repeat_steps(ctl, WET_SECOND, (delta0, delta1, delta2), (low, high), work, tile, sems)
    wait_all(start_all(((tile, out),), sems) + near)


def repeat_first(
    ctl, delta0, delta1, delta2, low, high, late_in, staying, out, work, other, tile, late, sems
):
    rest = out.at[1 - ctl[MOVE + 1]]
    again = ctl[MOVE] == ctl[MOVE + 1]

    @pl.when(again)
    def _():
        wait_all(start_all(((staying, tile),), sems))

    @pl.when(jnp.logical_not(again))
    def _():
        copies = start_all(((late_in, late),), sems, 2)
        repeat_steps(ctl, WET_FIRST, (delta0, delta1, delta2), (low, high), work, other, sems)
        wait_all(copies)
        merge(late, other, tile)

    wait_all(start_all(((tile, rest),), sems))


def finish(ctl, late, early, before, out, tile, sems):
    del before
    copies = []
    for field in range(3):
        merge_field(field, late, early, tile)
        copies += start_all(
            ((tile.at[field], out.at[ctl[MOVE + 1], field]),), sems, field
        )
    wait_all(copies)


def second_late(ctl, arrived, own, order, leaving):
    del order
    again = ctl[MOVE] == ctl[MOVE + 1]
    for field in range(3):
        leaving[field] = jnp.where(again, arrived[field], own[field])


def correct_rows(ctl, slot, got, ground, state, rate, bottom):
    position = jnp.where(ctl[SLOT_LOW] == slot, 0, 1)
    device = lax.axis_index("xb") * 2 + lax.axis_index("yb")
    wall = WALL_WEST if bottom else WALL_EAST

    @pl.when(jnp.logical_not(flag(ctl, wall + position)))
    def _():
        peer = device - 2 if bottom else device + 2
        block = pl.ds(pl.multiple_of(peer * 8, 8), 8)
        lines = got[block, :TILE]
        grounds = ground[block, :TILE]
        stride = 4 if got.shape[1] > TILE else 3

        def line(offset):
            other = offset + stride
            picked = jnp.where(
                position == 0, lines[offset : offset + 1, :], lines[other : other + 1, :]
            )
            return jnp.broadcast_to(picked, (8, TILE))

        ghost, _ = cell(*(line(field) for field in range(3)))
        ghost_ground = jnp.where(position == 0, grounds[3:4, :], grounds[7:8, :])
        rows = slice(0, 8) if bottom else slice(TILE - 8, TILE)
        own = [state[slot, field, rows, :] for field in range(3)]
        here, _ = cell(*own)
        fluxes = face(ghost, here) if bottom else face(here, ghost)
        push = SCALE * fluxes[1] + (SLOPE * own[0]) * ghost_ground
        row = sublanes()
        sign = -1.0 if bottom else 1.0
        chosen = row == (0 if bottom else 7)
        for field, value in enumerate((SCALE * fluxes[0], push, SCALE * fluxes[2])):
            rate[slot, field, rows, :] += jnp.where(chosen, sign * value, 0.0)


def column_fix(got, ground, columns):
    upper = lax.axis_index("yb")
    device = lax.axis_index("xb") * 2 + upper
    peer = device + 1 - 2 * upper
    block = pl.ds(pl.multiple_of(peer * 8, 8), 8)
    lines = got[block, :TILE]
    ghost_ground = ground[block, :TILE][3:4]
    mine = columns[...]
    _, ghost = cell(lines[0:1], lines[1:2], lines[2:3])
    _, own = cell(mine[0:1], mine[1:2], mine[2:3])
    low = upper == 0
    left = tuple(jnp.where(low, a, b) for a, b in zip(own, ghost))
    right = tuple(jnp.where(low, b, a) for a, b in zip(own, ghost))
    fluxes = face(left, right)
    sign = jnp.where(low, 1.0, -1.0)
    push = SCALE * fluxes[1] + (SLOPE * mine[0:1]) * ghost_ground
    block8 = stacked(
        [sign * SCALE * fluxes[0], sign * SCALE * fluxes[2], sign * push],
        jnp.zeros((8, TILE), jnp.float32),
    )
    return jnp.transpose(
        jnp.concatenate([block8, jnp.zeros((LANES - 8, TILE), jnp.float32)], 0)
    )


def last_update(moving, ctl, got, ground, columns, state, manning, rate, order, *rest):
    del order
    slot = ctl[MOVE] if moving else 1 - ctl[MOVE]
    update(STEPS - 1, ctl, got, ground, columns, state, manning, rate, *rest, slots=(slot,))


def update(
    step, ctl, got_in, ground_in, columns_in, state_in, manning_in, rate_in, *rest,
    passing=None, slots=(0, 1),
):
    more = step + 1 < STEPS
    fresh_out, first_out, second_out, delta_out = rest[:4]
    rest = rest[4:]
    state, manning, rate, fresh, got, ground, columns, first, second, delta_keep, sems = rest
    out, columns_out = first, second
    small = start_all(
        ((got_in, got), (ground_in, ground), (columns_in, columns)), sems, 5 * PARTS
    )
    size = 2 * TILE // PARTS
    parts = [
        (slot, slice(k * size, (k + 1) * size)) for slot in slots for k in range(PARTS // 2)
    ]
    incoming = []
    for index, (slot, rows) in enumerate(parts):
        incoming.append(
            start_all(
                (
                    (rate_in.at[slot, :, rows], rate.at[slot, :, rows]),
                    (state_in.at[slot, :, rows], state.at[slot, :, rows]),
                    (manning_in.at[slot, rows], manning.at[slot, rows]),
                ),
                sems,
                3 * index,
            )
        )
    wait_all(small)
    upper = lax.axis_index("yb")
    devices = 2 * lax.axis_size("xb")
    begin = TILE if got.shape[1] > TILE else 0
    tops = got[0:8, begin : begin + LANES]
    for peer in range(1, devices):
        tops = jnp.maximum(tops, got[peer * 8 : peer * 8 + 8, begin : begin + LANES])
    delta = (COURANT * SPACING) / tops[TOP : TOP + 1, :]
    delta = jnp.concatenate([delta, delta], 1)
    delta_keep[...] = jnp.broadcast_to(delta, (8, TILE))
    outgoing = start_all(((delta_keep, delta_out),), sems, 5 * PARTS + 3)
    fix = column_fix(got, ground, columns)
    facing = jnp.where(upper > 0, ctl[SLOT_LOW], 1 - ctl[SLOT_LOW])
    begin = pl.multiple_of((1 - upper) * LANES, LANES)
    goal = (1 - upper) * (LANES - 1)
    lane = lax.broadcasted_iota(jnp.int32, (size, LANES), 1)
    total = jnp.zeros((ROWS, TILE), jnp.float32)
    for index, (slot, part_rows) in enumerate(parts):
        wait_all(incoming[index])
        if part_rows.start == 0:
            correct_rows(ctl, slot, got, ground, state, rate, True)
        if part_rows.stop == TILE:
            correct_rows(ctl, slot, got, ground, state, rate, False)

        @pl.when(facing == slot)
        def _(slot=slot, part_rows=part_rows):
            for field in range(3):
                turned = pltpu.roll(
                    fix[part_rows], lax.rem(goal + LANES - field, LANES), 1
                )
                rate[slot, field, part_rows, pl.ds(begin, LANES)] += jnp.where(
                    lane == goal, turned, 0.0
                )

        wet_now = flag(ctl, WET + 2 * step + slot)

        def group(index, best, slot=slot, wet_now=wet_now):
            rows = pl.ds(pl.multiple_of(index * ROWS, ROWS), ROWS)
            old = tuple(state[slot, field, rows, :] for field in range(3))
            slopes = tuple(rate[slot, field, rows, :] for field in range(3))
            h, hu, hv = moved_on(old, slopes, manning[slot, rows, :], delta, wet_now)
            fresh[slot, 0, rows, :] = h
            fresh[slot, 1, rows, :] = hu
            fresh[slot, 2, rows, :] = hv
            if more:
                along_x, along_y = cell(h, hu, hv)
                best = jnp.maximum(best, jnp.maximum(along_x[5], along_y[5]))
            return best

        best = lax.fori_loop(
            part_rows.start // ROWS,
            part_rows.stop // ROWS,
            group,
            jnp.zeros((ROWS, TILE), jnp.float32),
        )
        if more:
            best = jnp.where(flag(ctl, WET + 2 * step + 2 + slot), best, 0.0)
            total = jnp.maximum(total, best)
        target = fresh_out.at[slot, :, part_rows] if more else fresh_out.at[:, part_rows]
        outgoing += start_all(
            ((fresh.at[slot, :, part_rows], target),), sems, 3 * PARTS + index
        )
        if passing and index == PARTS // 2:
            passing.middle()
    if more:
        messages(ctl, fresh, None, jnp.max(total, keepdims=True), out, columns_out)
        outgoing += start_all(((out, first_out), (columns_out, second_out)), sems, 4 * PARTS)
    else:
        second[...] = jnp.zeros_like(second)
        late_rows(fresh.at[slots[0]], first)
        outgoing += start_all(((first, first_out), (second, second_out)), sems, 4 * PARTS)
    wait_all(outgoing)


def vmem():
    return pl.BlockSpec(memory_space=pltpu.VMEM)


def smem():
    return pl.BlockSpec(memory_space=pltpu.SMEM)


def hbm():
    return pl.BlockSpec(memory_space=pltpu.HBM)


def anywhere():
    return pl.BlockSpec(memory_space=pl.ANY)


def call(
    kernel, outs, out_specs, in_specs, flops, scratch=(), aliases=None, room=VMEM_BYTES, moved=4
):
    return pl.pallas_call(
        kernel,
        scratch_shapes=scratch,
        input_output_aliases=aliases or {},
        out_shape=outs,
        in_specs=in_specs,
        out_specs=out_specs,
        compiler_params=pltpu.CompilerParams(vmem_limit_bytes=room),
        cost_estimate=pl.CostEstimate(flops=flops, bytes_accessed=moved << 20, transcendentals=0),
    )


def f32(*shape):
    return jax.ShapeDtypeStruct(shape, jnp.float32)


def spread(fast):
    return lax.all_to_all(fast, ("xb", "yb"), split_axis=0, concat_axis=0, tiled=True)


def body(state, bed, manning, neighbours, wet, moves):
    shape = f32(*state.shape)
    devices = lax.axis_size("xb") * lax.axis_size("yb")
    whole = pltpu.VMEM(state.shape, jnp.float32)
    part = pltpu.VMEM(bed.shape, jnp.float32)
    tile_shape = f32(*state.shape[1:])
    early_shape = f32(5, EARLY, TILE)
    early_state = f32(3, EARLY, TILE)
    late_shape = f32(3, LATE, TILE)
    delta_shape = f32(8, TILE)

    def buffer(like):
        return pltpu.VMEM(like.shape, jnp.float32)

    piece_shapes = tuple(f32(5, end - begin, TILE) for begin, end in PIECES)
    out, columns, ctl = call(
        opening,
        (
            f32(8 * devices, TILE + LANES),
            f32(8, TILE),
            jax.ShapeDtypeStruct((CONTROLS,), jnp.int32),
        ),
        (vmem(), vmem(), smem()),
        [hbm()] * 5,
        4 << 20,
        [
            whole,
            part,
            pltpu.SMEM(neighbours.shape[::-1], jnp.int32),
            pltpu.SMEM(wet.shape, jnp.int32),
            pltpu.SMEM(moves.shape, jnp.int32),
            pltpu.SemaphoreType.DMA((6,)),
        ],
    )(state, bed, neighbours.T, wet, moves)
    state_first = state
    ground = None
    deltas = []
    for step in range(STEPS):
        got = spread(out)
        ground = got if step == 0 else ground
        scratch = [whole, part, whole, pltpu.SemaphoreType.DMA((3 * CHUNKS,))]
        piece_scratch = [
            [buffer(piece), pltpu.SemaphoreType.DMA((2,))] for piece in piece_shapes
        ]
        if step == 1:
            rate, leaving = call(
                rates_and_leaving,
                (shape, piece_shapes[0]),
                (hbm(),) * 2,
                [smem()] + [hbm()] * 5,
                16 << 20,
                scratch + piece_scratch[0],
            )(ctl, state, bed, state_first, manning, early_first[0])
            early_second = [shifted(leaving, "xb", 1)]
        elif step == 2:
            rate = call(rates_after, shape, hbm(), [smem()] + [hbm()] * 3, 16 << 20, scratch)(
                ctl, state, bed, early_second[0]
            )
        else:
            rate, *leaving = call(
                rates_and_splitting,
                (shape,) + piece_shapes,
                (hbm(),) * 3,
                [smem()] + [hbm()] * 3,
                16 << 20,
                scratch + [buffer(early_shape), pltpu.SemaphoreType.DMA((5,))],
            )(ctl, state, bed, manning)
            held = call(
                hold, piece_shapes[0], hbm(), [hbm()] * 3, 1 << 10, aliases={2: 0}
            )(rate, got, leaving[0])
            early_first = [shifted(held, "xb", 1)]
        more = step + 1 < STEPS
        shapes = (f32(8 * devices, TILE) if more else late_shape), f32(8, TILE)
        passing = step == 1
        work = [
            whole,
            part,
            whole,
            whole,
            pltpu.VMEM(got.shape, jnp.float32),
            pltpu.VMEM(ground.shape, jnp.float32),
            pltpu.VMEM((8, TILE), jnp.float32),
            buffer(shapes[0]),
            buffer(shapes[1]),
            buffer(delta_shape),
            pltpu.SemaphoreType.DMA((5 * PARTS + 4,)),
        ]
        operands = ctl, got, ground, columns, state, manning, rate
        if not more:
            break
        outs = call(
            functools.partial(update_and_leaving if passing else update, step),
            (shape,) + shapes + (delta_shape,) + ((piece_shapes[1],) if passing else ()),
            (hbm(),) * (5 if passing else 4),
            [smem()] + [hbm()] * (9 if passing else 6),
            8 << 20,
            work + (piece_scratch[1] if passing else []),
            moved=10,
        )(*operands, *((state_first, bed, early_first[1]) if passing else ()))
        state, out, columns, delta, *passed = outs
        deltas.append(delta)
        if step == 0:
            held = call(
                hold, piece_shapes[1], hbm(), [hbm()] * 3, 1 << 10, aliases={2: 0}
            )(delta, delta, leaving[1])
            early_first.append(shifted(held, "xb", 1))
        elif step == 1:
            early_second.append(shifted(passed[0], "xb", 1))

    def finish_step(moving, order):
        return call(
            functools.partial(last_update, moving),
            (tile_shape,) + shapes + (delta_shape,),
            (hbm(),) * 4,
            [smem()] + [hbm()] * 7,
            8 << 20,
            work,
            moved=10,
        )(*operands, order)

    _, late_first, _, delta = finish_step(True, early_second[1])
    staying, late_second, _, _ = finish_step(False, delta)
    deltas.append(delta)
    room = 16 << 20
    late_arrived = shifted(late_first, "xb", 1)
    second, late_second = call(
        repeat_second,
        (early_state, late_shape),
        (anywhere(), vmem()),
        [smem()] + [vmem()] * 3 + [anywhere()] * 3,
        8 << 20,
        [buffer(early_shape), buffer(early_state), pltpu.SemaphoreType.DMA((3,))],
        room=room,
    )(ctl, *deltas, *early_second, late_second)
    leaving = call(
        second_late,
        late_shape,
        vmem(),
        [smem(), vmem(), vmem(), anywhere()],
        1 << 10,
        room=room,
    )(ctl, late_arrived, late_second, second)
    late_next = shifted(leaving, "xb", 1)
    final = call(
        repeat_first,
        shape,
        hbm(),
        [smem()] + [vmem()] * 3 + [anywhere()] * 4,
        8 << 20,
        [
            buffer(early_shape),
            buffer(early_state),
            buffer(tile_shape),
            buffer(late_shape),
            pltpu.SemaphoreType.DMA((3,)),
        ],
        room=room,
    )(ctl, *deltas, *early_first, late_arrived, staying)
    return call(
        finish,
        shape,
        hbm(),
        [smem(), vmem(), vmem(), hbm()],
        1 << 20,
        [buffer(tile_shape), pltpu.SemaphoreType.DMA((3,))],
        {3: 0},
        room=room,
    )(ctl, late_next, second, final)


def solution(mesh):
    placed = (
        P(("runs", "xb", "yb"), None, None, None),
        P(("runs", "xb", "yb"), None, None),
        P(("runs", "xb", "yb"), None, None),
        P("runs", None),
        P(None, "runs"),
        P(None, "runs"),
    )
    return jax.shard_map(
        body,
        mesh=mesh,
        in_specs=placed,
        out_specs=P(("runs", "xb", "yb"), None, None, None),
        check_vma=False,
    )
```

```python
import functools

import jax
import jax.numpy as jnp
from jax import lax
from jax.experimental import pallas as pl
from jax.experimental.pallas import tpu as pltpu
from jax.sharding import PartitionSpec as P

STEPS = 3
GRAVITY = 9.81
ROOT_G = GRAVITY**0.5
SPACING = 5.0
COURANT = 0.2
ROWS = 32
LANES = 128
TILE = 256
VMEM_BYTES = 60 * 1024 * 1024
SLOT_LOW, WALL_WEST, WALL_EAST, WALL_OUTER, WET, MOVE = 0, 1, 3, 5, 7, 13
WET_FIRST, WET_SECOND = 16, 19
CONTROLS = 24
EARLY = 144
PIECES = ((0, 80), (80, 144))
AGAIN = 48
LATE = TILE - EARLY + 16
HALF = LATE // 2
CHUNKS = 8
PARTS = 8
STRIP = 32
TOP = 6
SCALE = 0.5 / SPACING
SLOPE = GRAVITY / (2.0 * SPACING)


def shifted(value, axis, steps, around=True):
    count = lax.axis_size(axis)
    pairs = [(source, (source + steps) % count) for source in range(count)]
    if not around:
        pairs = [pair for pair in pairs if abs(pair[0] - pair[1]) == abs(steps)]
    return lax.ppermute(value, axis, pairs)


def cell(h, hu, hv):
    root = lax.rsqrt(h)
    inverse = root * root
    u = hu * inverse
    v = hv * inverse
    celerity = ROOT_G * (h * root)
    pressure = (0.5 * GRAVITY) * (h * h)
    cross = hu * v
    speed_x = jnp.abs(u) + celerity
    speed_y = jnp.abs(v) + celerity
    along_x = (h, hu, hv, hu * u + pressure, cross, speed_x)
    along_y = (h, hv, hu, hv * v + pressure, cross, speed_y)
    return along_x, along_y


def face(left, right):
    wave = jnp.maximum(left[5], right[5])
    return (
        (left[1] + right[1]) - wave * (right[0] - left[0]),
        (left[3] + right[3]) - wave * (right[1] - left[1]),
        (left[4] + right[4]) - wave * (right[2] - left[2]),
    )


def slot_of(ctl, position):
    low = ctl[SLOT_LOW]
    return low if position == 0 else 1 - low


def flag(ctl, index):
    return ctl[index] > 0


def start_all(pairs, sems, first=0):
    copies = [
        pltpu.make_async_copy(src, dst, sems.at[first + k]) for k, (src, dst) in enumerate(pairs)
    ]
    for copy in copies:
        copy.start()
    return copies


def wait_all(copies):
    for copy in copies:
        copy.wait()


def sublanes(width=TILE):
    return lax.broadcasted_iota(jnp.int32, (8, width), 0)


def stacked(lines, base):
    row = sublanes()
    for index, line in enumerate(lines):
        base = jnp.where(row == index, jnp.broadcast_to(line, (8, TILE)), base)
    return base


def messages(ctl, state, bed, fastest, out, columns):
    upper = lax.axis_index("yb")
    column = lax.axis_index("xb")
    last = lax.axis_size("xb") - 1
    devices = 2 * (last + 1)
    device = column * 2 + upper
    top = jnp.broadcast_to(fastest, (8, TILE))
    for peer in range(devices):
        out[peer * 8 : peer * 8 + 8, :TILE] = top
        if bed is not None:
            out[peer * 8 : peer * 8 + 8, TILE:] = top[:, :LANES]
    row = sublanes()

    def edge(line):
        rows = slice(line, line + 1)
        lines = []
        for position in range(2):
            slot = slot_of(ctl, position)
            lines += [state[slot, field, rows, :] for field in range(3)]
            if bed is not None:
                lines.append(bed[slot, rows, :])
        return stacked(lines, top)

    for inside, peer, line in (
        (column > 0, device - 2, 0),
        (column < last, device + 2, TILE - 1),
    ):

        @pl.when(inside)
        def _(peer=peer, line=line):
            out[pl.ds(pl.multiple_of(peer * 8, 8), 8), :TILE] = edge(line)

    slot = jnp.where(upper > 0, ctl[SLOT_LOW], 1 - ctl[SLOT_LOW])
    begin = pl.multiple_of((1 - upper) * LANES, LANES)
    lane = lax.broadcasted_iota(jnp.int32, (TILE, LANES), 1)
    packed = None
    for field in range(4 if bed is not None else 3):
        if field < 3:
            part = state[slot, field, :, pl.ds(begin, LANES)]
        else:
            part = bed[slot, :, pl.ds(begin, LANES)]
        turned = pltpu.roll(part, field + 1 - upper, 1)
        packed = turned if field == 0 else jnp.where(lane == field, turned, packed)
    lines = jnp.transpose(packed)[:8]
    columns[...] = lines
    start = pl.multiple_of((device + 1 - 2 * upper) * 8, 8)
    out[pl.ds(start, 8), :TILE] = jnp.where(row == TOP, top, lines)


def opening(
    state_in, bed_in, neighbours_in, wet_in, moves_in,
    out, columns, ctl,
    state, bed, neighbours, wet, moves, sems,
):
    copies = start_all(
        (
            (neighbours_in, neighbours),
            (wet_in, wet),
            (moves_in, moves),
            (state_in.at[0], state.at[0]),
            (state_in.at[1], state.at[1]),
            (bed_in, bed),
        ),
        sems,
    )
    device = lax.axis_index("xb") * 2 + lax.axis_index("yb")
    wait_all(copies[:3])
    first = device * 2
    low = jnp.where(neighbours[3, first] == first + 1, 0, 1)
    ctl[SLOT_LOW] = low
    for position in range(2):
        slot = low if position == 0 else 1 - low
        tile = first + slot
        ctl[WALL_WEST + position] = (neighbours[0, tile] < 0).astype(jnp.int32)
        ctl[WALL_EAST + position] = (neighbours[1, tile] < 0).astype(jnp.int32)
        ctl[WALL_OUTER + position] = (neighbours[2 + position, tile] < 0).astype(jnp.int32)
    for step in range(STEPS):
        for slot in range(2):
            ctl[WET + 2 * step + slot] = wet[step, first + slot]
        ctl[MOVE + step] = moves[step, device]
    count = lax.axis_size("xb")
    upper = lax.axis_index("yb")
    column = lax.axis_index("xb")
    source = lax.rem(column + count - 1, count) * 2 + upper
    before = lax.rem(column + count - 2, count) * 2 + upper
    again = moves[0, source] == moves[1, source]
    tile_first = source * 2 + moves[0, source]
    tile_second = jnp.where(
        again, before * 2 + moves[0, before], source * 2 + 1 - moves[0, source]
    )
    for step in range(STEPS):
        ctl[WET_FIRST + step] = wet[step, tile_first]
        ctl[WET_SECOND + step] = wet[step, tile_second]

    total = jnp.zeros((ROWS, TILE), jnp.float32)
    for slot in range(2):
        copies[3 + slot].wait()

        def group(index, best, slot=slot):
            rows = pl.ds(pl.multiple_of(index * ROWS, ROWS), ROWS)
            along_x, along_y = cell(*(state[slot, field, rows, :] for field in range(3)))
            return jnp.maximum(best, jnp.maximum(along_x[5], along_y[5]))

        best = lax.fori_loop(0, TILE // ROWS, group, jnp.zeros((ROWS, TILE), jnp.float32))
        total = jnp.maximum(total, jnp.where(wet[0, first + slot] > 0, best, 0.0))
    copies[5].wait()
    messages(ctl, state, bed, jnp.max(total, keepdims=True), out, columns)


def hold(first, second, leaving, same):
    del first, second, leaving, same


class Splitting:
    def __init__(self, ctl, state_in, bed_in, manning_in, leaving, buffer, sems):
        slot = ctl[MOVE]
        rows = slice(0, EARLY)
        pairs = (
            (state_in.at[slot, :, rows], buffer.at[0:3]),
            (bed_in.at[slot, rows], buffer.at[3]),
            (manning_in.at[slot, rows], buffer.at[4]),
        )
        self.incoming = [
            pltpu.make_async_copy(src, dst, sems.at[k]) for k, (src, dst) in enumerate(pairs)
        ]
        self.outgoing = [
            pltpu.make_async_copy(buffer.at[:, begin:end], piece, sems.at[3 + k])
            for k, ((begin, end), piece) in enumerate(zip(PIECES, leaving))
        ]

    def start(self):
        for copy in self.incoming:
            copy.start()

    def middle(self):
        wait_all(self.incoming)
        for copy in self.outgoing:
            copy.start()

    def end(self):
        wait_all(self.outgoing)


class Passing:
    def __init__(self, ctl, piece, state_in, bed_in, manning_in, arrived, leaving, buffer, sems):
        self.again = ctl[MOVE] == ctl[MOVE + 1]
        self.other = 1 - ctl[MOVE]
        self.rows = slice(*piece)
        self.refs = state_in, bed_in, manning_in
        self.incoming = pltpu.make_async_copy(arrived, buffer, sems.at[0])
        self.outgoing = pltpu.make_async_copy(buffer, leaving, sems.at[1])
        self.buffer = buffer
        self.sem = sems.at[0]

    def start(self):
        state_in, bed_in, manning_in = self.refs
        buffer, sem, rows = self.buffer, self.sem, self.rows

        @pl.when(self.again)
        def _():
            self.incoming.start()

        @pl.when(jnp.logical_not(self.again))
        def _():
            pltpu.make_async_copy(state_in.at[self.other, :, rows], buffer.at[0:3], sem).start()
            pltpu.make_async_copy(bed_in.at[self.other, rows], buffer.at[3], sem).start()
            pltpu.make_async_copy(manning_in.at[self.other, rows], buffer.at[4], sem).start()

    def middle(self):
        self.incoming.wait()
        self.outgoing.start()

    def end(self):
        self.outgoing.wait()


def rates_and_splitting(
    ctl, state_in, bed_in, manning_in, rate_out, leaving_low, leaving_high,
    state, bed, rate, sems, buffer, moving,
):
    leaving = leaving_low, leaving_high
    splitting = Splitting(ctl, state_in, bed_in, manning_in, leaving, buffer, moving)
    rates(ctl, state_in, bed_in, rate_out, state, bed, rate, sems, splitting)


def rates_and_leaving(
    ctl, state_in, bed_in, state_first, manning_in, arrived, rate_out, leaving,
    state, bed, rate, sems, buffer, moving,
):
    passing = Passing(
        ctl, PIECES[0], state_first, bed_in, manning_in, arrived, leaving, buffer, moving
    )
    rates(ctl, state_in, bed_in, rate_out, state, bed, rate, sems, passing)


def update_and_leaving(
    step, ctl, got_in, ground_in, columns_in, state_in, manning_in, rate_in,
    state_first, bed_in, arrived, fresh_out, first_out, second_out, delta_out, leaving, *rest
):
    *rest, buffer, moving = rest
    passing = Passing(
        ctl, PIECES[1], state_first, bed_in, manning_in, arrived, leaving, buffer, moving
    )
    passing.start()
    update(
        step, ctl, got_in, ground_in, columns_in, state_in, manning_in, rate_in,
        fresh_out, first_out, second_out, delta_out, *rest, passing=passing,
    )
    passing.end()


def rates_after(ctl, state_in, bed_in, order, *rest):
    del order
    rates(ctl, state_in, bed_in, *rest)


def rates(ctl, state_in, bed_in, rate_out, state, bed, rate, sems, passing=None):
    width = 2 * TILE
    row_ids = lax.broadcasted_iota(jnp.int32, (STRIP, width), 0)
    row8 = sublanes(width)
    lane = lax.broadcasted_iota(jnp.int32, (STRIP, LANES), 1)
    last = TILE // STRIP - 1
    chunk = TILE // CHUNKS
    slots = [slot_of(ctl, position) for position in range(2)]
    incoming = []
    for part in range(CHUNKS):
        rows = slice(part * chunk, (part + 1) * chunk)
        incoming.append(
            start_all(
                (
                    (state_in.at[:, :, rows], state.at[:, :, rows]),
                    (bed_in.at[:, rows], bed.at[:, rows]),
                ),
                sems,
                2 * part,
            )
        )
    if passing:
        passing.start()
    keep_west, keep_east, keep_south, keep_north = (
        jnp.where(flag(ctl, index), 1.0, 0.0)
        for index in (WALL_WEST, WALL_EAST, WALL_OUTER, WALL_OUTER + 1)
    )

    def strip(field, rows):
        if field == 3:
            return jnp.concatenate([bed[slot, rows, :] for slot in slots], 1)
        return jnp.concatenate([state[slot, field, rows, :] for slot in slots], 1)

    def blocks(value):
        return [value[:, k * LANES : (k + 1) * LANES] for k in range(4)]

    def right_of(value, end=None):
        turned = [pltpu.roll(part, LANES - 1, 1) for part in blocks(value)]
        after = turned[1:] + [turned[3] if end is None else end]
        return jnp.concatenate(
            [
                jnp.where(lane == LANES - 1, following, part)
                if following is not part
                else part
                for part, following in zip(turned, after)
            ],
            1,
        )

    def left_of(value, end):
        turned = [pltpu.roll(part, 1, 1) for part in blocks(value)]
        before = [end] + turned[:3]
        return jnp.concatenate(
            [jnp.where(lane == 0, previous, part) for part, previous in zip(turned, before)], 1
        )

    def down(value):
        return pltpu.roll(value, STRIP + 7, 0)[:STRIP]

    def group(index, carry):
        base = pl.multiple_of(index * STRIP, STRIP)
        rows = pl.ds(base, STRIP)
        after = pl.ds(pl.multiple_of(jnp.minimum(base + STRIP, TILE - 8), 8), 8)
        at_end = index == last
        fields = [
            jnp.concatenate([strip(field, rows), strip(field, after)], 0) for field in range(3)
        ]
        cells_x, cells_y = cell(*fields)
        here_x = tuple(value[:STRIP] for value in cells_x)
        here_y = tuple(value[:STRIP] for value in cells_y)

        ending = jnp.logical_and(row8 == 7, at_end)
        faces = list(face(here_x, tuple(down(value) for value in cells_x)))
        wall = keep_east * (2.0 * (here_x[3] + here_x[5] * here_x[1])[STRIP - 8 :])
        for component, value in enumerate((0.0, wall, 0.0)):
            upper = faces[component]
            faces[component] = jnp.concatenate(
                [upper[: STRIP - 8], jnp.where(ending, value, upper[STRIP - 8 :])], 0
            )
        turned = tuple(pltpu.roll(value, 1, 0) for value in faces)
        change_x = tuple(
            value - jnp.where(row_ids == 0, before, moved)
            for value, before, moved in zip(faces, carry[:3], turned)
        )
        ground = strip(3, rows)
        ground_after = jnp.where(
            at_end,
            jnp.broadcast_to(keep_east * ground[STRIP - 1 :], (8, width)),
            strip(3, after),
        )
        ground_up = pltpu.roll(ground, 1, 0)
        slope_x = down(jnp.concatenate([ground, ground_after], 0)) - jnp.where(
            row_ids == 0, carry[3], ground_up
        )
        carried = tuple(value[0:1, :] for value in turned) + (ground_up[0:1, :],)

        faces_y = list(face(here_y, tuple(right_of(value) for value in here_y)))
        normal = here_y[3]
        spread_y = here_y[5] * here_y[1]
        north = keep_north * (2.0 * (normal + spread_y)[:, width - LANES :])
        south = keep_south * (2.0 * (normal - spread_y)[:, :LANES])
        change_y = []
        for component, (high, low) in enumerate(((0.0, 0.0), (north, south), (0.0, 0.0))):
            parts = blocks(faces_y[component])
            parts[3] = jnp.where(lane == LANES - 1, high, parts[3])
            value = jnp.concatenate(parts, 1)
            change_y.append(value - left_of(value, low))
        slope_y = right_of(ground, keep_north * ground[:, width - LANES :]) - left_of(
            ground, keep_south * ground[:, :LANES]
        )
        weight = SLOPE * here_x[0]
        results = (
            SCALE * (change_x[0] + change_y[0]),
            SCALE * (change_x[1] + change_y[2]) + weight * slope_x,
            SCALE * (change_x[2] + change_y[1]) + weight * slope_y,
        )
        for field, value in enumerate(results):
            for position, slot in enumerate(slots):
                rate[slot, field, rows, :] = value[:, position * TILE : (position + 1) * TILE]
        return carried

    wait_all(incoming[0])
    top, _ = cell(*(strip(field, slice(0, 8)) for field in range(3)))
    nothing = jnp.zeros((1, width), jnp.float32)
    carry = (
        nothing,
        keep_west * (2.0 * (top[3] - top[5] * top[1])[0:1]),
        nothing,
        keep_west * strip(3, slice(0, 8))[0:1],
    )
    per_chunk = chunk // STRIP
    outgoing = []
    for part in range(CHUNKS):
        if part + 1 < CHUNKS:
            wait_all(incoming[part + 1])
        carry = lax.fori_loop(part * per_chunk, (part + 1) * per_chunk, group, carry)
        rows = slice(part * chunk, (part + 1) * chunk)
        outgoing += start_all(
            ((rate.at[:, :, rows], rate_out.at[:, :, rows]),), sems, 2 * CHUNKS + part
        )
        if passing and part == CHUNKS // 2:
            passing.middle()
    wait_all(outgoing)
    if passing:
        passing.end()


def moved_on(old, slopes, rough, delta, wet_now):
    h, hu, hv = (value - delta * slope for value, slope in zip(old, slopes))
    inverse = 1.0 / h
    u = hu * inverse
    v = hv * inverse
    speed = jnp.sqrt(u * u + v * v)
    power = jnp.exp((-4.0 / 3.0) * jnp.log(jnp.abs(h)))
    drag = (GRAVITY * delta) * (rough * rough) * (speed * power)
    factor = 1.0 / (1.0 + drag)
    fresh = (h, hu * factor, hv * factor)
    return tuple(jnp.where(wet_now, new, value) for new, value in zip(fresh, old))


def repeat_steps(ctl, wet_from, deltas, early, work, other, sems):
    incoming = []
    for ref in early:
        begin = 0 if ref is early[0] else early[0].shape[1]
        incoming += start_all(
            ((ref, work.at[:, begin : begin + ref.shape[1]]),), sems, len(incoming)
        )
    row_ids = lax.broadcasted_iota(jnp.int32, (AGAIN, TILE), 0)
    lane = lax.broadcasted_iota(jnp.int32, (AGAIN, LANES), 1)
    start = tuple(jnp.zeros((1, TILE), jnp.float32) for _ in range(4))

    def halves(value):
        return value[:, :LANES], value[:, LANES:]

    def right_of(value):
        low, high = (pltpu.roll(part, LANES - 1, 1) for part in halves(value))
        return jnp.concatenate([jnp.where(lane == LANES - 1, high, low), high], 1)

    def left_of(value):
        low, high = (pltpu.roll(part, 1, 1) for part in halves(value))
        return jnp.concatenate([low, jnp.where(lane == 0, low, high)], 1)

    def down(value):
        return pltpu.roll(value, AGAIN + 7, 0)[:AGAIN]

    for step in range(STEPS):
        source, target = (work, other) if step % 2 == 0 else (other, work)
        delta = deltas[step][0:1, :]
        wet_now = flag(ctl, wet_from + step)

        def group(index, carry, source=source, target=target, delta=delta, wet_now=wet_now):
            base = pl.multiple_of(index * AGAIN, AGAIN)
            rows = pl.ds(base, AGAIN)
            after = pl.ds(pl.multiple_of(jnp.minimum(base + AGAIN, EARLY - 8), 8), 8)
            refs = [source.at[field] for field in range(3)] + [work.at[3]]
            fields = [jnp.concatenate([ref[rows, :], ref[after, :]], 0) for ref in refs]
            cells_x, cells_y = cell(*fields[:3])
            here_x = tuple(value[:AGAIN] for value in cells_x)
            here_y = tuple(value[:AGAIN] for value in cells_y)
            faces_x = face(here_x, tuple(down(value) for value in cells_x))
            turned = tuple(pltpu.roll(value, 1, 0) for value in faces_x)
            change_x = tuple(
                value - jnp.where(row_ids == 0, before, moved)
                for value, before, moved in zip(faces_x, carry[:3], turned)
            )
            ground = fields[3][:AGAIN]
            ground_up = pltpu.roll(ground, 1, 0)
            slope_x = down(fields[3]) - jnp.where(row_ids == 0, carry[3], ground_up)
            carried = tuple(value[0:1, :] for value in turned) + (ground_up[0:1, :],)
            faces_y = face(here_y, tuple(right_of(value) for value in here_y))
            change_y = tuple(value - left_of(value) for value in faces_y)
            slope_y = right_of(ground) - left_of(ground)
            old = tuple(value[:AGAIN] for value in fields[:3])
            weight = SLOPE * old[0]
            slopes = (
                SCALE * (change_x[0] + change_y[0]),
                SCALE * (change_x[1] + change_y[2]) + weight * slope_x,
                SCALE * (change_x[2] + change_y[1]) + weight * slope_y,
            )
            for field, value in enumerate(
                moved_on(old, slopes, work[4, rows, :], delta, wet_now)
            ):
                target[field, rows, :] = value
            return carried

        if step == 0:
            wait_all(incoming)
        lax.fori_loop(0, EARLY // AGAIN, group, start)


def late_rows(tile, late):
    row = sublanes()
    kept = EARLY - 8
    lane = lax.broadcasted_iota(jnp.int32, (8, LANES), 1)
    for field in range(3):
        late[field, 0:8, :] = jnp.where(
            row < 3, tile[field, 0:8, :], tile[field, kept : kept + 8, :]
        )
        packed = [jnp.zeros((8, LANES), jnp.float32)] * 2
        for block in range(EARLY // 8):
            rows = slice(8 * block, 8 * block + 8)
            sides = jnp.where(lane < 64, tile[field, rows, :LANES], tile[field, rows, LANES:])
            turned = pltpu.roll(sides, (3 + 8 * block) % LANES, 1)
            which = block // 16
            packed[which] = jnp.where(lane // 8 == block % 16, turned, packed[which])
        late[field, 8:16, :] = jnp.concatenate(packed, 1)
        late[field, 16:, :] = tile[field, EARLY:, :]


def merge(late, rest, early, tile):
    for field in range(3):
        merge_field(field, late, rest, early, tile)


def merge_field(field, late, rest, early, tile):
    row = sublanes()
    lane = lax.broadcasted_iota(jnp.int32, (8, LANES), 1)
    first = late[field, 0:8, :]
    for block in range(EARLY // 8):
        rows = slice(8 * block, 8 * block + 8)
        which = block // 16
        packed = late[field, 8:16, which * LANES : (which + 1) * LANES]
        sides = pltpu.roll(packed, (-3 - 8 * block) % LANES, 1)
        value = early[field, rows, :]
        value = jnp.concatenate(
            [
                jnp.where(lane < 3, sides, value[:, :LANES]),
                jnp.where(lane >= LANES - 3, sides, value[:, LANES:]),
            ],
            1,
        )
        if block == 0:
            value = jnp.where(row < 3, first, value)
        if block == EARLY // 8 - 1:
            value = jnp.where(row < 5, value, first)
        tile[field, rows, :] = value
    tile[field, EARLY : TILE - HALF, :] = late[field, 16:, :]
    tile[field, TILE - HALF :, :] = rest[field]


def repeat_second(
    ctl, delta0, delta1, delta2, low, high, late, rest, out, late_out, rest_out, work, tile, sems
):
    near = start_all(((late, late_out), (rest, rest_out)), sems, 2)
    repeat_steps(ctl, WET_SECOND, (delta0, delta1, delta2), (low, high), work, tile, sems)
    wait_all(start_all(((tile, out),), sems) + near)


def repeat_first(
    ctl, delta0, delta1, delta2, low, high, late_in, rest_in, staying, out,
    work, other, tile, late, rest, sems,
):
    kept = out.at[1 - ctl[MOVE + 1]]
    again = ctl[MOVE] == ctl[MOVE + 1]

    @pl.when(again)
    def _():
        wait_all(start_all(((staying, tile),), sems))

    @pl.when(jnp.logical_not(again))
    def _():
        copies = start_all(((late_in, late), (rest_in, rest)), sems, 2)
        repeat_steps(ctl, WET_FIRST, (delta0, delta1, delta2), (low, high), work, other, sems)
        wait_all(copies)
        merge(late, rest, other, tile)

    wait_all(start_all(((tile, kept),), sems))


def finish(ctl, late, rest, early, before, out, tile, sems):
    del before
    copies = []
    for field in range(3):
        merge_field(field, late, rest, early, tile)
        copies += start_all(
            ((tile.at[field], out.at[ctl[MOVE + 1], field]),), sems, field
        )
    wait_all(copies)


def second_late(ctl, arrived, own, order, leaving):
    del order
    again = ctl[MOVE] == ctl[MOVE + 1]
    for field in range(3):
        leaving[field] = jnp.where(again, arrived[field], own[field])


def correct_rows(ctl, slot, got, ground, state, rate, bottom):
    position = jnp.where(ctl[SLOT_LOW] == slot, 0, 1)
    device = lax.axis_index("xb") * 2 + lax.axis_index("yb")
    wall = WALL_WEST if bottom else WALL_EAST

    @pl.when(jnp.logical_not(flag(ctl, wall + position)))
    def _():
        peer = device - 2 if bottom else device + 2
        block = pl.ds(pl.multiple_of(peer * 8, 8), 8)
        lines = got[block, :TILE]
        grounds = ground[block, :TILE]
        stride = 4 if got.shape[1] > TILE else 3

        def line(offset):
            other = offset + stride
            picked = jnp.where(
                position == 0, lines[offset : offset + 1, :], lines[other : other + 1, :]
            )
            return jnp.broadcast_to(picked, (8, TILE))

        ghost, _ = cell(*(line(field) for field in range(3)))
        ghost_ground = jnp.where(position == 0, grounds[3:4, :], grounds[7:8, :])
        rows = slice(0, 8) if bottom else slice(TILE - 8, TILE)
        own = [state[slot, field, rows, :] for field in range(3)]
        here, _ = cell(*own)
        fluxes = face(ghost, here) if bottom else face(here, ghost)
        push = SCALE * fluxes[1] + (SLOPE * own[0]) * ghost_ground
        row = sublanes()
        sign = -1.0 if bottom else 1.0
        chosen = row == (0 if bottom else 7)
        for field, value in enumerate((SCALE * fluxes[0], push, SCALE * fluxes[2])):
            rate[slot, field, rows, :] += jnp.where(chosen, sign * value, 0.0)


def column_fix(got, ground, columns):
    upper = lax.axis_index("yb")
    device = lax.axis_index("xb") * 2 + upper
    peer = device + 1 - 2 * upper
    block = pl.ds(pl.multiple_of(peer * 8, 8), 8)
    lines = got[block, :TILE]
    ghost_ground = ground[block, :TILE][3:4]
    mine = columns[...]
    _, ghost = cell(lines[0:1], lines[1:2], lines[2:3])
    _, own = cell(mine[0:1], mine[1:2], mine[2:3])
    low = upper == 0
    left = tuple(jnp.where(low, a, b) for a, b in zip(own, ghost))
    right = tuple(jnp.where(low, b, a) for a, b in zip(own, ghost))
    fluxes = face(left, right)
    sign = jnp.where(low, 1.0, -1.0)
    push = SCALE * fluxes[1] + (SLOPE * mine[0:1]) * ghost_ground
    block8 = stacked(
        [sign * SCALE * fluxes[0], sign * SCALE * fluxes[2], sign * push],
        jnp.zeros((8, TILE), jnp.float32),
    )
    return jnp.transpose(
        jnp.concatenate([block8, jnp.zeros((LANES - 8, TILE), jnp.float32)], 0)
    )


def last_update(moving, ctl, got, ground, columns, state, manning, rate, order, *rest):
    del order
    slot = ctl[MOVE] if moving else 1 - ctl[MOVE]
    update(STEPS - 1, ctl, got, ground, columns, state, manning, rate, *rest, slots=(slot,))


def update(
    step, ctl, got_in, ground_in, columns_in, state_in, manning_in, rate_in, *rest,
    passing=None, slots=(0, 1),
):
    more = step + 1 < STEPS
    fresh_out, first_out, second_out, delta_out = rest[:4]
    rest = rest[4:]
    state, manning, rate, fresh, got, ground, columns, first, second, delta_keep, sems = rest
    out, columns_out = first, second
    small = start_all(
        ((got_in, got), (ground_in, ground), (columns_in, columns)), sems, 5 * PARTS
    )
    size = 2 * TILE // PARTS
    parts = [
        (slot, slice(k * size, (k + 1) * size)) for slot in slots for k in range(PARTS // 2)
    ]
    incoming = []
    for index, (slot, rows) in enumerate(parts):
        incoming.append(
            start_all(
                (
                    (rate_in.at[slot, :, rows], rate.at[slot, :, rows]),
                    (state_in.at[slot, :, rows], state.at[slot, :, rows]),
                    (manning_in.at[slot, rows], manning.at[slot, rows]),
                ),
                sems,
                3 * index,
            )
        )
    wait_all(small)
    upper = lax.axis_index("yb")
    devices = 2 * lax.axis_size("xb")
    begin = TILE if got.shape[1] > TILE else 0
    tops = got[0:8, begin : begin + LANES]
    for peer in range(1, devices):
        tops = jnp.maximum(tops, got[peer * 8 : peer * 8 + 8, begin : begin + LANES])
    delta = (COURANT * SPACING) / tops[TOP : TOP + 1, :]
    delta = jnp.concatenate([delta, delta], 1)
    delta_keep[...] = jnp.broadcast_to(delta, (8, TILE))
    outgoing = start_all(((delta_keep, delta_out),), sems, 5 * PARTS + 3)
    fix = column_fix(got, ground, columns)
    facing = jnp.where(upper > 0, ctl[SLOT_LOW], 1 - ctl[SLOT_LOW])
    begin = pl.multiple_of((1 - upper) * LANES, LANES)
    goal = (1 - upper) * (LANES - 1)
    lane = lax.broadcasted_iota(jnp.int32, (size, LANES), 1)
    total = jnp.zeros((ROWS, TILE), jnp.float32)
    for index, (slot, part_rows) in enumerate(parts):
        wait_all(incoming[index])
        if part_rows.start == 0:
            correct_rows(ctl, slot, got, ground, state, rate, True)
        if part_rows.stop == TILE:
            correct_rows(ctl, slot, got, ground, state, rate, False)

        @pl.when(facing == slot)
        def _(slot=slot, part_rows=part_rows):
            for field in range(3):
                turned = pltpu.roll(
                    fix[part_rows], lax.rem(goal + LANES - field, LANES), 1
                )
                rate[slot, field, part_rows, pl.ds(begin, LANES)] += jnp.where(
                    lane == goal, turned, 0.0
                )

        wet_now = flag(ctl, WET + 2 * step + slot)

        def group(index, best, slot=slot, wet_now=wet_now):
            rows = pl.ds(pl.multiple_of(index * ROWS, ROWS), ROWS)
            old = tuple(state[slot, field, rows, :] for field in range(3))
            slopes = tuple(rate[slot, field, rows, :] for field in range(3))
            h, hu, hv = moved_on(old, slopes, manning[slot, rows, :], delta, wet_now)
            fresh[slot, 0, rows, :] = h
            fresh[slot, 1, rows, :] = hu
            fresh[slot, 2, rows, :] = hv
            if more:
                along_x, along_y = cell(h, hu, hv)
                best = jnp.maximum(best, jnp.maximum(along_x[5], along_y[5]))
            return best

        best = lax.fori_loop(
            part_rows.start // ROWS,
            part_rows.stop // ROWS,
            group,
            jnp.zeros((ROWS, TILE), jnp.float32),
        )
        if more:
            best = jnp.where(flag(ctl, WET + 2 * step + 2 + slot), best, 0.0)
            total = jnp.maximum(total, best)
        target = fresh_out.at[slot, :, part_rows] if more else fresh_out.at[:, part_rows]
        outgoing += start_all(
            ((fresh.at[slot, :, part_rows], target),), sems, 3 * PARTS + index
        )
        if passing and index == PARTS // 2:
            passing.middle()
    if more:
        messages(ctl, fresh, None, jnp.max(total, keepdims=True), out, columns_out)
        outgoing += start_all(((out, first_out), (columns_out, second_out)), sems, 4 * PARTS)
    else:
        late_rows(fresh.at[slots[0]], first)
        outgoing += start_all(
            ((first.at[:, :HALF], first_out), (first.at[:, HALF:], second_out)), sems, 4 * PARTS
        )
    wait_all(outgoing)


def vmem():
    return pl.BlockSpec(memory_space=pltpu.VMEM)


def smem():
    return pl.BlockSpec(memory_space=pltpu.SMEM)


def hbm():
    return pl.BlockSpec(memory_space=pltpu.HBM)


def anywhere():
    return pl.BlockSpec(memory_space=pl.ANY)


def call(
    kernel, outs, out_specs, in_specs, flops, scratch=(), aliases=None, room=VMEM_BYTES, moved=4
):
    return pl.pallas_call(
        kernel,
        scratch_shapes=scratch,
        input_output_aliases=aliases or {},
        out_shape=outs,
        in_specs=in_specs,
        out_specs=out_specs,
        compiler_params=pltpu.CompilerParams(vmem_limit_bytes=room),
        cost_estimate=pl.CostEstimate(flops=flops, bytes_accessed=moved << 20, transcendentals=0),
    )


def f32(*shape):
    return jax.ShapeDtypeStruct(shape, jnp.float32)


def spread(fast):
    return lax.all_to_all(fast, ("xb", "yb"), split_axis=0, concat_axis=0, tiled=True)


def body(state, bed, manning, neighbours, wet, moves):
    shape = f32(*state.shape)
    devices = lax.axis_size("xb") * lax.axis_size("yb")
    whole = pltpu.VMEM(state.shape, jnp.float32)
    part = pltpu.VMEM(bed.shape, jnp.float32)
    tile_shape = f32(*state.shape[1:])
    early_shape = f32(5, EARLY, TILE)
    early_state = f32(3, EARLY, TILE)
    late_shape = f32(3, LATE, TILE)
    half_shape = f32(3, HALF, TILE)
    delta_shape = f32(8, TILE)

    def buffer(like):
        return pltpu.VMEM(like.shape, jnp.float32)

    piece_shapes = tuple(f32(5, end - begin, TILE) for begin, end in PIECES)
    out, columns, ctl = call(
        opening,
        (
            f32(8 * devices, TILE + LANES),
            f32(8, TILE),
            jax.ShapeDtypeStruct((CONTROLS,), jnp.int32),
        ),
        (vmem(), vmem(), smem()),
        [hbm()] * 5,
        4 << 20,
        [
            whole,
            part,
            pltpu.SMEM(neighbours.shape[::-1], jnp.int32),
            pltpu.SMEM(wet.shape, jnp.int32),
            pltpu.SMEM(moves.shape, jnp.int32),
            pltpu.SemaphoreType.DMA((6,)),
        ],
    )(state, bed, neighbours.T, wet, moves)
    state_first = state
    ground = None
    deltas = []
    for step in range(STEPS):
        got = spread(out)
        ground = got if step == 0 else ground
        scratch = [whole, part, whole, pltpu.SemaphoreType.DMA((3 * CHUNKS,))]
        piece_scratch = [
            [buffer(piece), pltpu.SemaphoreType.DMA((2,))] for piece in piece_shapes
        ]
        if step == 1:
            rate, leaving = call(
                rates_and_leaving,
                (shape, piece_shapes[0]),
                (hbm(),) * 2,
                [smem()] + [hbm()] * 5,
                16 << 20,
                scratch + piece_scratch[0],
            )(ctl, state, bed, state_first, manning, early_first[0])
            early_second = [shifted(leaving, "xb", 1)]
        elif step == 2:
            rate = call(rates_after, shape, hbm(), [smem()] + [hbm()] * 3, 16 << 20, scratch)(
                ctl, state, bed, early_second[0]
            )
        else:
            rate, *leaving = call(
                rates_and_splitting,
                (shape,) + piece_shapes,
                (hbm(),) * 3,
                [smem()] + [hbm()] * 3,
                16 << 20,
                scratch + [buffer(early_shape), pltpu.SemaphoreType.DMA((5,))],
            )(ctl, state, bed, manning)
            held = call(
                hold, piece_shapes[0], hbm(), [hbm()] * 3, 1 << 10, aliases={2: 0}
            )(rate, got, leaving[0])
            early_first = [shifted(held, "xb", 1)]
        more = step + 1 < STEPS
        shapes = (f32(8 * devices, TILE), f32(8, TILE)) if more else (half_shape,) * 2
        passing = step == 1
        work = [
            whole,
            part,
            whole,
            whole,
            pltpu.VMEM(got.shape, jnp.float32),
            pltpu.VMEM(ground.shape, jnp.float32),
            pltpu.VMEM((8, TILE), jnp.float32),
            buffer(shapes[0] if more else late_shape),
            buffer(shapes[1]),
            buffer(delta_shape),
            pltpu.SemaphoreType.DMA((5 * PARTS + 4,)),
        ]
        operands = ctl, got, ground, columns, state, manning, rate
        if not more:
            break
        outs = call(
            functools.partial(update_and_leaving if passing else update, step),
            (shape,) + shapes + (delta_shape,) + ((piece_shapes[1],) if passing else ()),
            (hbm(),) * (5 if passing else 4),
            [smem()] + [hbm()] * (9 if passing else 6),
            8 << 20,
            work + (piece_scratch[1] if passing else []),
            moved=10,
        )(*operands, *((state_first, bed, early_first[1]) if passing else ()))
        state, out, columns, delta, *passed = outs
        deltas.append(delta)
        if step == 0:
            held = call(
                hold, piece_shapes[1], hbm(), [hbm()] * 3, 1 << 10, aliases={2: 0}
            )(delta, delta, leaving[1])
            early_first.append(shifted(held, "xb", 1))
        elif step == 1:
            early_second.append(shifted(passed[0], "xb", 1))

    def finish_step(moving, order):
        return call(
            functools.partial(last_update, moving),
            (tile_shape,) + shapes + (delta_shape,),
            (hbm(),) * 4,
            [smem()] + [hbm()] * 7,
            8 << 20,
            work,
            moved=10,
        )(*operands, order)

    _, late_first, rest_first, delta = finish_step(True, early_second[1])
    staying, late_second, rest_second, _ = finish_step(False, delta)
    deltas.append(delta)
    room = 16 << 20
    late_arrived = shifted(late_first, "xb", 1)
    rest_first = call(hold, half_shape, hbm(), [hbm()] * 3, 1 << 10, aliases={2: 0})(
        staying, staying, rest_first
    )
    rest_arrived = shifted(rest_first, "xb", 1)
    second, late_second, rest_second = call(
        repeat_second,
        (early_state, half_shape, half_shape),
        (anywhere(), vmem(), vmem()),
        [smem()] + [vmem()] * 3 + [anywhere()] * 4,
        8 << 20,
        [buffer(early_shape), buffer(early_state), pltpu.SemaphoreType.DMA((4,))],
        room=room,
    )(ctl, *deltas, *early_second, late_second, rest_second)

    def pass_late(arrived, own):
        leaving = call(
            second_late,
            half_shape,
            vmem(),
            [smem(), vmem(), vmem(), anywhere()],
            1 << 10,
            room=room,
        )(ctl, arrived, own, second)
        return shifted(leaving, "xb", 1)

    late_next = pass_late(late_arrived, late_second)
    rest_next = pass_late(rest_arrived, rest_second)
    final = call(
        repeat_first,
        shape,
        hbm(),
        [smem()] + [vmem()] * 3 + [anywhere()] * 5,
        8 << 20,
        [
            buffer(early_shape),
            buffer(early_state),
            buffer(tile_shape),
            buffer(half_shape),
            buffer(half_shape),
            pltpu.SemaphoreType.DMA((4,)),
        ],
        room=room,
    )(ctl, *deltas, *early_first, late_arrived, rest_arrived, staying)
    return call(
        finish,
        shape,
        hbm(),
        [smem(), vmem(), vmem(), vmem(), hbm()],
        1 << 20,
        [buffer(tile_shape), pltpu.SemaphoreType.DMA((3,))],
        {4: 0},
        room=room,
    )(ctl, late_next, rest_next, second, final)


def solution(mesh):
    placed = (
        P(("runs", "xb", "yb"), None, None, None),
        P(("runs", "xb", "yb"), None, None),
        P(("runs", "xb", "yb"), None, None),
        P("runs", None),
        P(None, "runs"),
        P(None, "runs"),
    )
    return jax.shard_map(
        body,
        mesh=mesh,
        in_specs=placed,
        out_specs=P(("runs", "xb", "yb"), None, None, None),
        check_vma=False,
    )
```

```python
import functools

import jax
import jax.numpy as jnp
from jax import lax
from jax.experimental import pallas as pl
from jax.experimental.pallas import tpu as pltpu
from jax.sharding import PartitionSpec as P

STEPS = 3
GRAVITY = 9.81
ROOT_G = GRAVITY**0.5
SPACING = 5.0
COURANT = 0.2
ROWS = 32
LANES = 128
TILE = 256
VMEM_BYTES = 60 * 1024 * 1024
SLOT_LOW, WALL_WEST, WALL_EAST, WALL_OUTER, WET, MOVE = 0, 1, 3, 5, 7, 13
WET_FIRST, WET_SECOND = 16, 19
CONTROLS = 24
EARLY = 144
PIECES = ((0, 80), (80, 144))
AGAIN = 48
LATE = TILE - EARLY + 16
HALF = LATE // 2
CHUNKS = 8
PARTS = 8
STRIP = 32
TOP = 6
SCALE = 0.5 / SPACING
SLOPE = GRAVITY / (2.0 * SPACING)


def shifted(value, axis, steps, around=True):
    count = lax.axis_size(axis)
    pairs = [(source, (source + steps) % count) for source in range(count)]
    if not around:
        pairs = [pair for pair in pairs if abs(pair[0] - pair[1]) == abs(steps)]
    return lax.ppermute(value, axis, pairs)


def cell(h, hu, hv):
    root = lax.rsqrt(h)
    inverse = root * root
    u = hu * inverse
    v = hv * inverse
    celerity = ROOT_G * (h * root)
    pressure = (0.5 * GRAVITY) * (h * h)
    cross = hu * v
    speed_x = jnp.abs(u) + celerity
    speed_y = jnp.abs(v) + celerity
    along_x = (h, hu, hv, hu * u + pressure, cross, speed_x)
    along_y = (h, hv, hu, hv * v + pressure, cross, speed_y)
    return along_x, along_y


def face(left, right):
    wave = jnp.maximum(left[5], right[5])
    return (
        (left[1] + right[1]) - wave * (right[0] - left[0]),
        (left[3] + right[3]) - wave * (right[1] - left[1]),
        (left[4] + right[4]) - wave * (right[2] - left[2]),
    )


def slot_of(ctl, position):
    low = ctl[SLOT_LOW]
    return low if position == 0 else 1 - low


def flag(ctl, index):
    return ctl[index] > 0


def start_all(pairs, sems, first=0):
    copies = [
        pltpu.make_async_copy(src, dst, sems.at[first + k]) for k, (src, dst) in enumerate(pairs)
    ]
    for copy in copies:
        copy.start()
    return copies


def wait_all(copies):
    for copy in copies:
        copy.wait()


def sublanes(width=TILE):
    return lax.broadcasted_iota(jnp.int32, (8, width), 0)


def stacked(lines, base):
    row = sublanes()
    for index, line in enumerate(lines):
        base = jnp.where(row == index, jnp.broadcast_to(line, (8, TILE)), base)
    return base


def messages(ctl, state, bed, fastest, out, columns):
    upper = lax.axis_index("yb")
    column = lax.axis_index("xb")
    last = lax.axis_size("xb") - 1
    devices = 2 * (last + 1)
    device = column * 2 + upper
    top = jnp.broadcast_to(fastest, (8, TILE))
    for peer in range(devices):
        out[peer * 8 : peer * 8 + 8, :TILE] = top
        if bed is not None:
            out[peer * 8 : peer * 8 + 8, TILE:] = top[:, :LANES]
    row = sublanes()

    def edge(line):
        rows = slice(line, line + 1)
        lines = []
        for position in range(2):
            slot = slot_of(ctl, position)
            lines += [state[slot, field, rows, :] for field in range(3)]
            if bed is not None:
                lines.append(bed[slot, rows, :])
        return stacked(lines, top)

    for inside, peer, line in (
        (column > 0, device - 2, 0),
        (column < last, device + 2, TILE - 1),
    ):

        @pl.when(inside)
        def _(peer=peer, line=line):
            out[pl.ds(pl.multiple_of(peer * 8, 8), 8), :TILE] = edge(line)

    slot = jnp.where(upper > 0, ctl[SLOT_LOW], 1 - ctl[SLOT_LOW])
    begin = pl.multiple_of((1 - upper) * LANES, LANES)
    lane = lax.broadcasted_iota(jnp.int32, (TILE, LANES), 1)
    packed = None
    for field in range(4 if bed is not None else 3):
        if field < 3:
            part = state[slot, field, :, pl.ds(begin, LANES)]
        else:
            part = bed[slot, :, pl.ds(begin, LANES)]
        turned = pltpu.roll(part, field + 1 - upper, 1)
        packed = turned if field == 0 else jnp.where(lane == field, turned, packed)
    lines = jnp.transpose(packed)[:8]
    columns[...] = lines
    start = pl.multiple_of((device + 1 - 2 * upper) * 8, 8)
    out[pl.ds(start, 8), :TILE] = jnp.where(row == TOP, top, lines)


def opening(
    state_in, bed_in, neighbours_in, wet_in, moves_in,
    out, columns, ctl,
    state, bed, neighbours, wet, moves, sems,
):
    copies = start_all(
        (
            (neighbours_in, neighbours),
            (wet_in, wet),
            (moves_in, moves),
            (state_in.at[0], state.at[0]),
            (state_in.at[1], state.at[1]),
            (bed_in, bed),
        ),
        sems,
    )
    device = lax.axis_index("xb") * 2 + lax.axis_index("yb")
    wait_all(copies[:3])
    first = device * 2
    low = jnp.where(neighbours[3, first] == first + 1, 0, 1)
    ctl[SLOT_LOW] = low
    for position in range(2):
        slot = low if position == 0 else 1 - low
        tile = first + slot
        ctl[WALL_WEST + position] = (neighbours[0, tile] < 0).astype(jnp.int32)
        ctl[WALL_EAST + position] = (neighbours[1, tile] < 0).astype(jnp.int32)
        ctl[WALL_OUTER + position] = (neighbours[2 + position, tile] < 0).astype(jnp.int32)
    for step in range(STEPS):
        for slot in range(2):
            ctl[WET + 2 * step + slot] = wet[step, first + slot]
        ctl[MOVE + step] = moves[step, device]
    count = lax.axis_size("xb")
    upper = lax.axis_index("yb")
    column = lax.axis_index("xb")
    source = lax.rem(column + count - 1, count) * 2 + upper
    before = lax.rem(column + count - 2, count) * 2 + upper
    again = moves[0, source] == moves[1, source]
    tile_first = source * 2 + moves[0, source]
    tile_second = jnp.where(
        again, before * 2 + moves[0, before], source * 2 + 1 - moves[0, source]
    )
    for step in range(STEPS):
        ctl[WET_FIRST + step] = wet[step, tile_first]
        ctl[WET_SECOND + step] = wet[step, tile_second]

    total = jnp.zeros((ROWS, TILE), jnp.float32)
    for slot in range(2):
        copies[3 + slot].wait()

        def group(index, best, slot=slot):
            rows = pl.ds(pl.multiple_of(index * ROWS, ROWS), ROWS)
            along_x, along_y = cell(*(state[slot, field, rows, :] for field in range(3)))
            return jnp.maximum(best, jnp.maximum(along_x[5], along_y[5]))

        best = lax.fori_loop(0, TILE // ROWS, group, jnp.zeros((ROWS, TILE), jnp.float32))
        total = jnp.maximum(total, jnp.where(wet[0, first + slot] > 0, best, 0.0))
    copies[5].wait()
    messages(ctl, state, bed, jnp.max(total, keepdims=True), out, columns)


def hold(first, second, leaving, same):
    del first, second, leaving, same


class Splitting:
    def __init__(self, ctl, state_in, bed_in, manning_in, leaving, buffer, sems):
        slot = ctl[MOVE]
        rows = slice(0, EARLY)
        pairs = (
            (state_in.at[slot, :, rows], buffer.at[0:3]),
            (bed_in.at[slot, rows], buffer.at[3]),
            (manning_in.at[slot, rows], buffer.at[4]),
        )
        self.incoming = [
            pltpu.make_async_copy(src, dst, sems.at[k]) for k, (src, dst) in enumerate(pairs)
        ]
        self.outgoing = [
            pltpu.make_async_copy(buffer.at[:, begin:end], piece, sems.at[3 + k])
            for k, ((begin, end), piece) in enumerate(zip(PIECES, leaving))
        ]

    def start(self):
        for copy in self.incoming:
            copy.start()

    def middle(self):
        wait_all(self.incoming)
        for copy in self.outgoing:
            copy.start()

    def end(self):
        wait_all(self.outgoing)


class Passing:
    def __init__(self, ctl, piece, state_in, bed_in, manning_in, arrived, leaving, buffer, sems):
        self.again = ctl[MOVE] == ctl[MOVE + 1]
        self.other = 1 - ctl[MOVE]
        self.rows = slice(*piece)
        self.refs = state_in, bed_in, manning_in
        self.incoming = pltpu.make_async_copy(arrived, buffer, sems.at[0])
        self.outgoing = pltpu.make_async_copy(buffer, leaving, sems.at[1])
        self.buffer = buffer
        self.sem = sems.at[0]

    def start(self):
        state_in, bed_in, manning_in = self.refs
        buffer, sem, rows = self.buffer, self.sem, self.rows

        @pl.when(self.again)
        def _():
            self.incoming.start()

        @pl.when(jnp.logical_not(self.again))
        def _():
            pltpu.make_async_copy(state_in.at[self.other, :, rows], buffer.at[0:3], sem).start()
            pltpu.make_async_copy(bed_in.at[self.other, rows], buffer.at[3], sem).start()
            pltpu.make_async_copy(manning_in.at[self.other, rows], buffer.at[4], sem).start()

    def middle(self):
        self.incoming.wait()
        self.outgoing.start()

    def end(self):
        self.outgoing.wait()


def rates_and_splitting(
    ctl, state_in, bed_in, manning_in, rate_out, leaving_low, leaving_high,
    state, bed, rate, sems, buffer, moving,
):
    leaving = leaving_low, leaving_high
    splitting = Splitting(ctl, state_in, bed_in, manning_in, leaving, buffer, moving)
    rates(ctl, state_in, bed_in, rate_out, state, bed, rate, sems, splitting)


def rates_and_leaving(
    ctl, state_in, bed_in, state_first, manning_in, arrived, rate_out, leaving,
    state, bed, rate, sems, buffer, moving,
):
    passing = Passing(
        ctl, PIECES[0], state_first, bed_in, manning_in, arrived, leaving, buffer, moving
    )
    rates(ctl, state_in, bed_in, rate_out, state, bed, rate, sems, passing)


def update_and_leaving(
    step, ctl, got_in, ground_in, columns_in, state_in, manning_in, rate_in,
    state_first, bed_in, arrived, fresh_out, first_out, second_out, delta_out, leaving, *rest
):
    *rest, buffer, moving = rest
    passing = Passing(
        ctl, PIECES[1], state_first, bed_in, manning_in, arrived, leaving, buffer, moving
    )
    passing.start()
    update(
        step, ctl, got_in, ground_in, columns_in, state_in, manning_in, rate_in,
        fresh_out, first_out, second_out, delta_out, *rest, passing=passing,
    )
    passing.end()


def rates_after(ctl, state_in, bed_in, order, *rest):
    del order
    rates(ctl, state_in, bed_in, *rest)


def rates(ctl, state_in, bed_in, rate_out, state, bed, rate, sems, passing=None):
    width = 2 * TILE
    row_ids = lax.broadcasted_iota(jnp.int32, (STRIP, width), 0)
    row8 = sublanes(width)
    lane = lax.broadcasted_iota(jnp.int32, (STRIP, LANES), 1)
    last = TILE // STRIP - 1
    chunk = TILE // CHUNKS
    slots = [slot_of(ctl, position) for position in range(2)]
    incoming = []
    for part in range(CHUNKS):
        rows = slice(part * chunk, (part + 1) * chunk)
        incoming.append(
            start_all(
                (
                    (state_in.at[:, :, rows], state.at[:, :, rows]),
                    (bed_in.at[:, rows], bed.at[:, rows]),
                ),
                sems,
                2 * part,
            )
        )
    if passing:
        passing.start()
    keep_west, keep_east, keep_south, keep_north = (
        jnp.where(flag(ctl, index), 1.0, 0.0)
        for index in (WALL_WEST, WALL_EAST, WALL_OUTER, WALL_OUTER + 1)
    )

    def strip(field, rows):
        if field == 3:
            return jnp.concatenate([bed[slot, rows, :] for slot in slots], 1)
        return jnp.concatenate([state[slot, field, rows, :] for slot in slots], 1)

    def blocks(value):
        return [value[:, k * LANES : (k + 1) * LANES] for k in range(4)]

    def right_of(value, end=None):
        turned = [pltpu.roll(part, LANES - 1, 1) for part in blocks(value)]
        after = turned[1:] + [turned[3] if end is None else end]
        return jnp.concatenate(
            [
                jnp.where(lane == LANES - 1, following, part)
                if following is not part
                else part
                for part, following in zip(turned, after)
            ],
            1,
        )

    def left_of(value, end):
        turned = [pltpu.roll(part, 1, 1) for part in blocks(value)]
        before = [end] + turned[:3]
        return jnp.concatenate(
            [jnp.where(lane == 0, previous, part) for part, previous in zip(turned, before)], 1
        )

    def down(value):
        return pltpu.roll(value, STRIP + 7, 0)[:STRIP]

    def group(index, carry):
        base = pl.multiple_of(index * STRIP, STRIP)
        rows = pl.ds(base, STRIP)
        after = pl.ds(pl.multiple_of(jnp.minimum(base + STRIP, TILE - 8), 8), 8)
        at_end = index == last
        fields = [
            jnp.concatenate([strip(field, rows), strip(field, after)], 0) for field in range(3)
        ]
        cells_x, cells_y = cell(*fields)
        here_x = tuple(value[:STRIP] for value in cells_x)
        here_y = tuple(value[:STRIP] for value in cells_y)

        ending = jnp.logical_and(row8 == 7, at_end)
        faces = list(face(here_x, tuple(down(value) for value in cells_x)))
        wall = keep_east * (2.0 * (here_x[3] + here_x[5] * here_x[1])[STRIP - 8 :])
        for component, value in enumerate((0.0, wall, 0.0)):
            upper = faces[component]
            faces[component] = jnp.concatenate(
                [upper[: STRIP - 8], jnp.where(ending, value, upper[STRIP - 8 :])], 0
            )
        turned = tuple(pltpu.roll(value, 1, 0) for value in faces)
        change_x = tuple(
            value - jnp.where(row_ids == 0, before, moved)
            for value, before, moved in zip(faces, carry[:3], turned)
        )
        ground = strip(3, rows)
        ground_after = jnp.where(
            at_end,
            jnp.broadcast_to(keep_east * ground[STRIP - 1 :], (8, width)),
            strip(3, after),
        )
        ground_up = pltpu.roll(ground, 1, 0)
        slope_x = down(jnp.concatenate([ground, ground_after], 0)) - jnp.where(
            row_ids == 0, carry[3], ground_up
        )
        carried = tuple(value[0:1, :] for value in turned) + (ground_up[0:1, :],)

        faces_y = list(face(here_y, tuple(right_of(value) for value in here_y)))
        normal = here_y[3]
        spread_y = here_y[5] * here_y[1]
        north = keep_north * (2.0 * (normal + spread_y)[:, width - LANES :])
        south = keep_south * (2.0 * (normal - spread_y)[:, :LANES])
        change_y = []
        for component, (high, low) in enumerate(((0.0, 0.0), (north, south), (0.0, 0.0))):
            parts = blocks(faces_y[component])
            parts[3] = jnp.where(lane == LANES - 1, high, parts[3])
            value = jnp.concatenate(parts, 1)
            change_y.append(value - left_of(value, low))
        slope_y = right_of(ground, keep_north * ground[:, width - LANES :]) - left_of(
            ground, keep_south * ground[:, :LANES]
        )
        weight = SLOPE * here_x[0]
        results = (
            SCALE * (change_x[0] + change_y[0]),
            SCALE * (change_x[1] + change_y[2]) + weight * slope_x,
            SCALE * (change_x[2] + change_y[1]) + weight * slope_y,
        )
        for field, value in enumerate(results):
            for position, slot in enumerate(slots):
                rate[slot, field, rows, :] = value[:, position * TILE : (position + 1) * TILE]
        return carried

    wait_all(incoming[0])
    top, _ = cell(*(strip(field, slice(0, 8)) for field in range(3)))
    nothing = jnp.zeros((1, width), jnp.float32)
    carry = (
        nothing,
        keep_west * (2.0 * (top[3] - top[5] * top[1])[0:1]),
        nothing,
        keep_west * strip(3, slice(0, 8))[0:1],
    )
    per_chunk = chunk // STRIP
    outgoing = []
    for part in range(CHUNKS):
        if part + 1 < CHUNKS:
            wait_all(incoming[part + 1])
        carry = lax.fori_loop(part * per_chunk, (part + 1) * per_chunk, group, carry)
        rows = slice(part * chunk, (part + 1) * chunk)
        outgoing += start_all(
            ((rate.at[:, :, rows], rate_out.at[:, :, rows]),), sems, 2 * CHUNKS + part
        )
        if passing and part == CHUNKS // 2:
            passing.middle()
    wait_all(outgoing)
    if passing:
        passing.end()


def moved_on(old, slopes, rough, delta, wet_now):
    h, hu, hv = (value - delta * slope for value, slope in zip(old, slopes))
    inverse = 1.0 / h
    u = hu * inverse
    v = hv * inverse
    speed = jnp.sqrt(u * u + v * v)
    power = jnp.exp((-4.0 / 3.0) * jnp.log(jnp.abs(h)))
    drag = (GRAVITY * delta) * (rough * rough) * (speed * power)
    factor = 1.0 / (1.0 + drag)
    fresh = (h, hu * factor, hv * factor)
    return tuple(jnp.where(wet_now, new, value) for new, value in zip(fresh, old))


def repeat_steps(ctl, wet_from, deltas, early, work, other, sems):
    incoming = []
    for ref in early:
        begin = 0 if ref is early[0] else early[0].shape[1]
        incoming += start_all(
            ((ref, work.at[:, begin : begin + ref.shape[1]]),), sems, len(incoming)
        )
    row_ids = lax.broadcasted_iota(jnp.int32, (AGAIN, TILE), 0)
    lane = lax.broadcasted_iota(jnp.int32, (AGAIN, LANES), 1)
    start = tuple(jnp.zeros((1, TILE), jnp.float32) for _ in range(4))

    def halves(value):
        return value[:, :LANES], value[:, LANES:]

    def right_of(value):
        low, high = (pltpu.roll(part, LANES - 1, 1) for part in halves(value))
        return jnp.concatenate([jnp.where(lane == LANES - 1, high, low), high], 1)

    def left_of(value):
        low, high = (pltpu.roll(part, 1, 1) for part in halves(value))
        return jnp.concatenate([low, jnp.where(lane == 0, low, high)], 1)

    def down(value):
        return pltpu.roll(value, AGAIN + 7, 0)[:AGAIN]

    for step in range(STEPS):
        source, target = (work, other) if step % 2 == 0 else (other, work)
        delta = deltas[step][0:1, :]
        wet_now = flag(ctl, wet_from + step)

        def group(index, carry, source=source, target=target, delta=delta, wet_now=wet_now):
            base = pl.multiple_of(index * AGAIN, AGAIN)
            rows = pl.ds(base, AGAIN)
            after = pl.ds(pl.multiple_of(jnp.minimum(base + AGAIN, EARLY - 8), 8), 8)
            refs = [source.at[field] for field in range(3)] + [work.at[3]]
            fields = [jnp.concatenate([ref[rows, :], ref[after, :]], 0) for ref in refs]
            cells_x, cells_y = cell(*fields[:3])
            here_x = tuple(value[:AGAIN] for value in cells_x)
            here_y = tuple(value[:AGAIN] for value in cells_y)
            faces_x = face(here_x, tuple(down(value) for value in cells_x))
            turned = tuple(pltpu.roll(value, 1, 0) for value in faces_x)
            change_x = tuple(
                value - jnp.where(row_ids == 0, before, moved)
                for value, before, moved in zip(faces_x, carry[:3], turned)
            )
            ground = fields[3][:AGAIN]
            ground_up = pltpu.roll(ground, 1, 0)
            slope_x = down(fields[3]) - jnp.where(row_ids == 0, carry[3], ground_up)
            carried = tuple(value[0:1, :] for value in turned) + (ground_up[0:1, :],)
            faces_y = face(here_y, tuple(right_of(value) for value in here_y))
            change_y = tuple(value - left_of(value) for value in faces_y)
            slope_y = right_of(ground) - left_of(ground)
            old = tuple(value[:AGAIN] for value in fields[:3])
            weight = SLOPE * old[0]
            slopes = (
                SCALE * (change_x[0] + change_y[0]),
                SCALE * (change_x[1] + change_y[2]) + weight * slope_x,
                SCALE * (change_x[2] + change_y[1]) + weight * slope_y,
            )
            for field, value in enumerate(
                moved_on(old, slopes, work[4, rows, :], delta, wet_now)
            ):
                target[field, rows, :] = value
            return carried

        if step == 0:
            wait_all(incoming)
        lax.fori_loop(0, EARLY // AGAIN, group, start)


def late_rows(tile, late):
    row = sublanes()
    kept = EARLY - 8
    lane = lax.broadcasted_iota(jnp.int32, (8, LANES), 1)
    for field in range(3):
        late[field, 0:8, :] = jnp.where(
            row < 3, tile[field, 0:8, :], tile[field, kept : kept + 8, :]
        )
        packed = [jnp.zeros((8, LANES), jnp.float32)] * 2
        for block in range(EARLY // 8):
            rows = slice(8 * block, 8 * block + 8)
            sides = jnp.where(lane < 64, tile[field, rows, :LANES], tile[field, rows, LANES:])
            turned = pltpu.roll(sides, (3 + 8 * block) % LANES, 1)
            which = block // 16
            packed[which] = jnp.where(lane // 8 == block % 16, turned, packed[which])
        late[field, 8:16, :] = jnp.concatenate(packed, 1)
        late[field, 16:, :] = tile[field, EARLY:, :]


def merge(late, rest, early, tile):
    for field in range(3):
        merge_field(field, late, rest, early, tile)


def merge_field(field, late, rest, early, tile):
    row = sublanes()
    lane = lax.broadcasted_iota(jnp.int32, (8, LANES), 1)
    first = late[field, 0:8, :]
    for block in range(EARLY // 8):
        rows = slice(8 * block, 8 * block + 8)
        which = block // 16
        packed = late[field, 8:16, which * LANES : (which + 1) * LANES]
        sides = pltpu.roll(packed, (-3 - 8 * block) % LANES, 1)
        value = early[field, rows, :]
        value = jnp.concatenate(
            [
                jnp.where(lane < 3, sides, value[:, :LANES]),
                jnp.where(lane >= LANES - 3, sides, value[:, LANES:]),
            ],
            1,
        )
        if block == 0:
            value = jnp.where(row < 3, first, value)
        if block == EARLY // 8 - 1:
            value = jnp.where(row < 5, value, first)
        tile[field, rows, :] = value
    tile[field, EARLY : TILE - HALF, :] = late[field, 16:, :]
    tile[field, TILE - HALF :, :] = rest[field]


def repeat_second(
    ctl, delta0, delta1, delta2, low, high, late, rest, out, late_out, rest_out, work, tile, sems
):
    near = start_all(((late, late_out), (rest, rest_out)), sems, 2)
    repeat_steps(ctl, WET_SECOND, (delta0, delta1, delta2), (low, high), work, tile, sems)
    wait_all(start_all(((tile, out),), sems) + near)


def repeat_first(
    ctl, delta0, delta1, delta2, low, high, late_in, rest_in, staying, out,
    work, other, tile, late, rest, sems,
):
    kept = out.at[1 - ctl[MOVE + 1]]
    again = ctl[MOVE] == ctl[MOVE + 1]

    @pl.when(again)
    def _():
        wait_all(start_all(((staying, tile),), sems))

    @pl.when(jnp.logical_not(again))
    def _():
        copies = start_all(((late_in, late), (rest_in, rest)), sems, 2)
        repeat_steps(ctl, WET_FIRST, (delta0, delta1, delta2), (low, high), work, other, sems)
        wait_all(copies)
        merge(late, rest, other, tile)

    wait_all(start_all(((tile, kept),), sems))


def finish(ctl, late, rest, early, before, out, tile, sems):
    del before
    copies = []
    for field in range(3):
        merge_field(field, late, rest, early, tile)
        copies += start_all(
            ((tile.at[field], out.at[ctl[MOVE + 1], field]),), sems, field
        )
    wait_all(copies)


def second_late(ctl, arrived, own, order, leaving):
    del order
    again = ctl[MOVE] == ctl[MOVE + 1]
    for field in range(3):
        leaving[field] = jnp.where(again, arrived[field], own[field])


def correct_rows(ctl, slot, got, ground, state, rate, bottom):
    position = jnp.where(ctl[SLOT_LOW] == slot, 0, 1)
    device = lax.axis_index("xb") * 2 + lax.axis_index("yb")
    wall = WALL_WEST if bottom else WALL_EAST

    @pl.when(jnp.logical_not(flag(ctl, wall + position)))
    def _():
        peer = device - 2 if bottom else device + 2
        block = pl.ds(pl.multiple_of(peer * 8, 8), 8)
        lines = got[block, :TILE]
        grounds = ground[block, :TILE]
        stride = 4 if got.shape[1] > TILE else 3

        def line(offset):
            other = offset + stride
            picked = jnp.where(
                position == 0, lines[offset : offset + 1, :], lines[other : other + 1, :]
            )
            return jnp.broadcast_to(picked, (8, TILE))

        ghost, _ = cell(*(line(field) for field in range(3)))
        ghost_ground = jnp.where(position == 0, grounds[3:4, :], grounds[7:8, :])
        rows = slice(0, 8) if bottom else slice(TILE - 8, TILE)
        own = [state[slot, field, rows, :] for field in range(3)]
        here, _ = cell(*own)
        fluxes = face(ghost, here) if bottom else face(here, ghost)
        push = SCALE * fluxes[1] + (SLOPE * own[0]) * ghost_ground
        row = sublanes()
        sign = -1.0 if bottom else 1.0
        chosen = row == (0 if bottom else 7)
        for field, value in enumerate((SCALE * fluxes[0], push, SCALE * fluxes[2])):
            rate[slot, field, rows, :] += jnp.where(chosen, sign * value, 0.0)


def column_fix(got, ground, columns):
    upper = lax.axis_index("yb")
    device = lax.axis_index("xb") * 2 + upper
    peer = device + 1 - 2 * upper
    block = pl.ds(pl.multiple_of(peer * 8, 8), 8)
    lines = got[block, :TILE]
    ghost_ground = ground[block, :TILE][3:4]
    mine = columns[...]
    _, ghost = cell(lines[0:1], lines[1:2], lines[2:3])
    _, own = cell(mine[0:1], mine[1:2], mine[2:3])
    low = upper == 0
    left = tuple(jnp.where(low, a, b) for a, b in zip(own, ghost))
    right = tuple(jnp.where(low, b, a) for a, b in zip(own, ghost))
    fluxes = face(left, right)
    sign = jnp.where(low, 1.0, -1.0)
    push = SCALE * fluxes[1] + (SLOPE * mine[0:1]) * ghost_ground
    block8 = stacked(
        [sign * SCALE * fluxes[0], sign * SCALE * fluxes[2], sign * push],
        jnp.zeros((8, TILE), jnp.float32),
    )
    return jnp.transpose(
        jnp.concatenate([block8, jnp.zeros((LANES - 8, TILE), jnp.float32)], 0)
    )


def last_update(ctl, got, ground, columns, state, manning, rate, order, *rest):
    del order
    slots = ctl[MOVE], 1 - ctl[MOVE]
    update(STEPS - 1, ctl, got, ground, columns, state, manning, rate, *rest, slots=slots)


def update(
    step, ctl, got_in, ground_in, columns_in, state_in, manning_in, rate_in, *rest,
    passing=None, slots=(0, 1),
):
    more = step + 1 < STEPS
    fresh_out, *lines_to, delta_out = rest[: 4 if more else 6]
    rest = rest[4 if more else 6 :]
    state, manning, rate, fresh, got, ground, columns, first, second, delta_keep, sems = rest
    out, columns_out = first, second
    small = start_all(
        ((got_in, got), (ground_in, ground), (columns_in, columns)), sems, 5 * PARTS
    )
    size = 2 * TILE // PARTS
    parts = [
        (slot, slice(k * size, (k + 1) * size)) for slot in slots for k in range(PARTS // 2)
    ]
    incoming = []
    for index, (slot, rows) in enumerate(parts):
        incoming.append(
            start_all(
                (
                    (rate_in.at[slot, :, rows], rate.at[slot, :, rows]),
                    (state_in.at[slot, :, rows], state.at[slot, :, rows]),
                    (manning_in.at[slot, rows], manning.at[slot, rows]),
                ),
                sems,
                3 * index,
            )
        )
    wait_all(small)
    upper = lax.axis_index("yb")
    devices = 2 * lax.axis_size("xb")
    begin = TILE if got.shape[1] > TILE else 0
    tops = got[0:8, begin : begin + LANES]
    for peer in range(1, devices):
        tops = jnp.maximum(tops, got[peer * 8 : peer * 8 + 8, begin : begin + LANES])
    delta = (COURANT * SPACING) / tops[TOP : TOP + 1, :]
    delta = jnp.concatenate([delta, delta], 1)
    delta_keep[...] = jnp.broadcast_to(delta, (8, TILE))
    outgoing = start_all(((delta_keep, delta_out),), sems, 5 * PARTS + 3)
    fix = column_fix(got, ground, columns)
    facing = jnp.where(upper > 0, ctl[SLOT_LOW], 1 - ctl[SLOT_LOW])
    begin = pl.multiple_of((1 - upper) * LANES, LANES)
    goal = (1 - upper) * (LANES - 1)
    lane = lax.broadcasted_iota(jnp.int32, (size, LANES), 1)
    total = jnp.zeros((ROWS, TILE), jnp.float32)
    for index, (slot, part_rows) in enumerate(parts):
        wait_all(incoming[index])
        if part_rows.start == 0:
            correct_rows(ctl, slot, got, ground, state, rate, True)
        if part_rows.stop == TILE:
            correct_rows(ctl, slot, got, ground, state, rate, False)

        @pl.when(facing == slot)
        def _(slot=slot, part_rows=part_rows):
            for field in range(3):
                turned = pltpu.roll(
                    fix[part_rows], lax.rem(goal + LANES - field, LANES), 1
                )
                rate[slot, field, part_rows, pl.ds(begin, LANES)] += jnp.where(
                    lane == goal, turned, 0.0
                )

        wet_now = flag(ctl, WET + 2 * step + slot)

        def group(index, best, slot=slot, wet_now=wet_now):
            rows = pl.ds(pl.multiple_of(index * ROWS, ROWS), ROWS)
            old = tuple(state[slot, field, rows, :] for field in range(3))
            slopes = tuple(rate[slot, field, rows, :] for field in range(3))
            h, hu, hv = moved_on(old, slopes, manning[slot, rows, :], delta, wet_now)
            fresh[slot, 0, rows, :] = h
            fresh[slot, 1, rows, :] = hu
            fresh[slot, 2, rows, :] = hv
            if more:
                along_x, along_y = cell(h, hu, hv)
                best = jnp.maximum(best, jnp.maximum(along_x[5], along_y[5]))
            return best

        best = lax.fori_loop(
            part_rows.start // ROWS,
            part_rows.stop // ROWS,
            group,
            jnp.zeros((ROWS, TILE), jnp.float32),
        )
        if more:
            best = jnp.where(flag(ctl, WET + 2 * step + 2 + slot), best, 0.0)
            total = jnp.maximum(total, best)
        if more:
            outgoing += start_all(
                ((fresh.at[slot, :, part_rows], fresh_out.at[slot, :, part_rows]),),
                sems,
                3 * PARTS + index,
            )
        elif index >= PARTS // 2:
            outgoing += start_all(
                ((fresh.at[slot, :, part_rows], fresh_out.at[:, part_rows]),),
                sems,
                3 * PARTS + index,
            )
        if not more and part_rows.stop == TILE:
            late, low, high = (
                (first, *lines_to[:2]) if index < PARTS // 2 else (second, *lines_to[2:])
            )
            late_rows(fresh.at[slot], late)
            outgoing += start_all(
                ((late.at[:, :HALF], low), (late.at[:, HALF:], high)),
                sems,
                4 * PARTS + (0 if index < PARTS // 2 else 2),
            )
        if passing and index == PARTS // 2:
            passing.middle()
    if more:
        messages(ctl, fresh, None, jnp.max(total, keepdims=True), out, columns_out)
        pairs = zip((out, columns_out), lines_to)
        outgoing += start_all(tuple(pairs), sems, 4 * PARTS)
    wait_all(outgoing)


def vmem():
    return pl.BlockSpec(memory_space=pltpu.VMEM)


def smem():
    return pl.BlockSpec(memory_space=pltpu.SMEM)


def hbm():
    return pl.BlockSpec(memory_space=pltpu.HBM)


def anywhere():
    return pl.BlockSpec(memory_space=pl.ANY)


def call(
    kernel, outs, out_specs, in_specs, flops, scratch=(), aliases=None, room=VMEM_BYTES, moved=4
):
    return pl.pallas_call(
        kernel,
        scratch_shapes=scratch,
        input_output_aliases=aliases or {},
        out_shape=outs,
        in_specs=in_specs,
        out_specs=out_specs,
        compiler_params=pltpu.CompilerParams(vmem_limit_bytes=room),
        cost_estimate=pl.CostEstimate(flops=flops, bytes_accessed=moved << 20, transcendentals=0),
    )


def f32(*shape):
    return jax.ShapeDtypeStruct(shape, jnp.float32)


def spread(fast):
    return lax.all_to_all(fast, ("xb", "yb"), split_axis=0, concat_axis=0, tiled=True)


def body(state, bed, manning, neighbours, wet, moves):
    shape = f32(*state.shape)
    devices = lax.axis_size("xb") * lax.axis_size("yb")
    whole = pltpu.VMEM(state.shape, jnp.float32)
    part = pltpu.VMEM(bed.shape, jnp.float32)
    tile_shape = f32(*state.shape[1:])
    early_shape = f32(5, EARLY, TILE)
    early_state = f32(3, EARLY, TILE)
    late_shape = f32(3, LATE, TILE)
    half_shape = f32(3, HALF, TILE)
    delta_shape = f32(8, TILE)

    def buffer(like):
        return pltpu.VMEM(like.shape, jnp.float32)

    piece_shapes = tuple(f32(5, end - begin, TILE) for begin, end in PIECES)
    out, columns, ctl = call(
        opening,
        (
            f32(8 * devices, TILE + LANES),
            f32(8, TILE),
            jax.ShapeDtypeStruct((CONTROLS,), jnp.int32),
        ),
        (vmem(), vmem(), smem()),
        [hbm()] * 5,
        4 << 20,
        [
            whole,
            part,
            pltpu.SMEM(neighbours.shape[::-1], jnp.int32),
            pltpu.SMEM(wet.shape, jnp.int32),
            pltpu.SMEM(moves.shape, jnp.int32),
            pltpu.SemaphoreType.DMA((6,)),
        ],
    )(state, bed, neighbours.T, wet, moves)
    state_first = state
    ground = None
    deltas = []
    for step in range(STEPS):
        got = spread(out)
        ground = got if step == 0 else ground
        scratch = [whole, part, whole, pltpu.SemaphoreType.DMA((3 * CHUNKS,))]
        piece_scratch = [
            [buffer(piece), pltpu.SemaphoreType.DMA((2,))] for piece in piece_shapes
        ]
        if step == 1:
            rate, leaving = call(
                rates_and_leaving,
                (shape, piece_shapes[0]),
                (hbm(),) * 2,
                [smem()] + [hbm()] * 5,
                16 << 20,
                scratch + piece_scratch[0],
            )(ctl, state, bed, state_first, manning, early_first[0])
            early_second = [shifted(leaving, "xb", 1)]
        elif step == 2:
            rate = call(rates_after, shape, hbm(), [smem()] + [hbm()] * 3, 16 << 20, scratch)(
                ctl, state, bed, early_second[0]
            )
        else:
            rate, *leaving = call(
                rates_and_splitting,
                (shape,) + piece_shapes,
                (hbm(),) * 3,
                [smem()] + [hbm()] * 3,
                16 << 20,
                scratch + [buffer(early_shape), pltpu.SemaphoreType.DMA((5,))],
            )(ctl, state, bed, manning)
            held = call(
                hold, piece_shapes[0], hbm(), [hbm()] * 3, 1 << 10, aliases={2: 0}
            )(rate, got, leaving[0])
            early_first = [shifted(held, "xb", 1)]
        more = step + 1 < STEPS
        shapes = (f32(8 * devices, TILE), f32(8, TILE)) if more else (half_shape,) * 4
        passing = step == 1
        work = [
            whole,
            part,
            whole,
            whole,
            pltpu.VMEM(got.shape, jnp.float32),
            pltpu.VMEM(ground.shape, jnp.float32),
            pltpu.VMEM((8, TILE), jnp.float32),
            buffer(shapes[0] if more else late_shape),
            buffer(shapes[1] if more else late_shape),
            buffer(delta_shape),
            pltpu.SemaphoreType.DMA((5 * PARTS + 4,)),
        ]
        operands = ctl, got, ground, columns, state, manning, rate
        if not more:
            break
        outs = call(
            functools.partial(update_and_leaving if passing else update, step),
            (shape,) + shapes + (delta_shape,) + ((piece_shapes[1],) if passing else ()),
            (hbm(),) * (5 if passing else 4),
            [smem()] + [hbm()] * (9 if passing else 6),
            8 << 20,
            work + (piece_scratch[1] if passing else []),
            moved=10,
        )(*operands, *((state_first, bed, early_first[1]) if passing else ()))
        state, out, columns, delta, *passed = outs
        deltas.append(delta)
        if step == 0:
            held = call(
                hold, piece_shapes[1], hbm(), [hbm()] * 3, 1 << 10, aliases={2: 0}
            )(delta, delta, leaving[1])
            early_first.append(shifted(held, "xb", 1))
        elif step == 1:
            early_second.append(shifted(passed[0], "xb", 1))

    staying, late_first, rest_first, late_second, rest_second, delta = call(
        last_update,
        (tile_shape,) + shapes + (delta_shape,),
        (hbm(),) * 6,
        [smem()] + [hbm()] * 7,
        8 << 20,
        work,
        moved=10,
    )(*operands, early_second[1])
    deltas.append(delta)
    room = 16 << 20
    late_arrived = shifted(late_first, "xb", 1)
    rest_arrived = shifted(rest_first, "xb", 1)
    second, late_second, rest_second = call(
        repeat_second,
        (early_state, half_shape, half_shape),
        (anywhere(), vmem(), vmem()),
        [smem()] + [vmem()] * 3 + [anywhere()] * 4,
        8 << 20,
        [buffer(early_shape), buffer(early_state), pltpu.SemaphoreType.DMA((4,))],
        room=room,
    )(ctl, *deltas, *early_second, late_second, rest_second)

    def pass_late(arrived, own):
        leaving = call(
            second_late,
            half_shape,
            vmem(),
            [smem(), vmem(), vmem(), anywhere()],
            1 << 10,
            room=room,
        )(ctl, arrived, own, second)
        return shifted(leaving, "xb", 1)

    late_next = pass_late(late_arrived, late_second)
    rest_next = pass_late(rest_arrived, rest_second)
    final = call(
        repeat_first,
        shape,
        hbm(),
        [smem()] + [vmem()] * 3 + [anywhere()] * 5,
        8 << 20,
        [
            buffer(early_shape),
            buffer(early_state),
            buffer(tile_shape),
            buffer(half_shape),
            buffer(half_shape),
            pltpu.SemaphoreType.DMA((4,)),
        ],
        room=room,
    )(ctl, *deltas, *early_first, late_arrived, rest_arrived, staying)
    return call(
        finish,
        shape,
        hbm(),
        [smem(), vmem(), vmem(), vmem(), hbm()],
        1 << 20,
        [buffer(tile_shape), pltpu.SemaphoreType.DMA((3,))],
        {4: 0},
        room=room,
    )(ctl, late_next, rest_next, second, final)


def solution(mesh):
    placed = (
        P(("runs", "xb", "yb"), None, None, None),
        P(("runs", "xb", "yb"), None, None),
        P(("runs", "xb", "yb"), None, None),
        P("runs", None),
        P(None, "runs"),
        P(None, "runs"),
    )
    return jax.shard_map(
        body,
        mesh=mesh,
        in_specs=placed,
        out_specs=P(("runs", "xb", "yb"), None, None, None),
        check_vma=False,
    )
```

```python
import functools

import jax
import jax.numpy as jnp
from jax import lax
from jax.experimental import pallas as pl
from jax.experimental.pallas import tpu as pltpu
from jax.sharding import PartitionSpec as P

STEPS = 3
GRAVITY = 9.81
ROOT_G = GRAVITY**0.5
SPACING = 5.0
COURANT = 0.2
ROWS = 32
LANES = 128
TILE = 256
VMEM_BYTES = 60 * 1024 * 1024
SLOT_LOW, WALL_WEST, WALL_EAST, WALL_OUTER, WET, MOVE = 0, 1, 3, 5, 7, 13
WET_FIRST, WET_SECOND = 16, 19
CONTROLS = 24
EARLY = 144
PIECES = ((0, 80), (80, 144))
AGAIN = 48
LATE = TILE - EARLY + 16
HALF = LATE // 2
CHUNKS = 8
PARTS = 4
STRIP = 32
TOP = 6
SCALE = 0.5 / SPACING
SLOPE = GRAVITY / (2.0 * SPACING)


def shifted(value, axis, steps, around=True):
    count = lax.axis_size(axis)
    pairs = [(source, (source + steps) % count) for source in range(count)]
    if not around:
        pairs = [pair for pair in pairs if abs(pair[0] - pair[1]) == abs(steps)]
    return lax.ppermute(value, axis, pairs)


def cell(h, hu, hv):
    root = lax.rsqrt(h)
    inverse = root * root
    u = hu * inverse
    v = hv * inverse
    celerity = ROOT_G * (h * root)
    pressure = (0.5 * GRAVITY) * (h * h)
    cross = hu * v
    speed_x = jnp.abs(u) + celerity
    speed_y = jnp.abs(v) + celerity
    along_x = (h, hu, hv, hu * u + pressure, cross, speed_x)
    along_y = (h, hv, hu, hv * v + pressure, cross, speed_y)
    return along_x, along_y


def face(left, right):
    wave = jnp.maximum(left[5], right[5])
    return (
        (left[1] + right[1]) - wave * (right[0] - left[0]),
        (left[3] + right[3]) - wave * (right[1] - left[1]),
        (left[4] + right[4]) - wave * (right[2] - left[2]),
    )


def slot_of(ctl, position):
    low = ctl[SLOT_LOW]
    return low if position == 0 else 1 - low


def flag(ctl, index):
    return ctl[index] > 0


def start_all(pairs, sems, first=0):
    copies = [
        pltpu.make_async_copy(src, dst, sems.at[first + k]) for k, (src, dst) in enumerate(pairs)
    ]
    for copy in copies:
        copy.start()
    return copies


def wait_all(copies):
    for copy in copies:
        copy.wait()


def sublanes(width=TILE):
    return lax.broadcasted_iota(jnp.int32, (8, width), 0)


def stacked(lines, base):
    row = sublanes()
    for index, line in enumerate(lines):
        base = jnp.where(row == index, jnp.broadcast_to(line, (8, TILE)), base)
    return base


def messages(ctl, state, bed, fastest, out, columns):
    upper = lax.axis_index("yb")
    column = lax.axis_index("xb")
    last = lax.axis_size("xb") - 1
    devices = 2 * (last + 1)
    device = column * 2 + upper
    top = jnp.broadcast_to(fastest, (8, TILE))
    for peer in range(devices):
        out[peer * 8 : peer * 8 + 8, :TILE] = top
        if bed is not None:
            out[peer * 8 : peer * 8 + 8, TILE:] = top[:, :LANES]
    row = sublanes()

    def edge(line):
        rows = slice(line, line + 1)
        lines = []
        for position in range(2):
            slot = slot_of(ctl, position)
            lines += [state[slot, field, rows, :] for field in range(3)]
            if bed is not None:
                lines.append(bed[slot, rows, :])
        return stacked(lines, top)

    for inside, peer, line in (
        (column > 0, device - 2, 0),
        (column < last, device + 2, TILE - 1),
    ):

        @pl.when(inside)
        def _(peer=peer, line=line):
            out[pl.ds(pl.multiple_of(peer * 8, 8), 8), :TILE] = edge(line)

    slot = jnp.where(upper > 0, ctl[SLOT_LOW], 1 - ctl[SLOT_LOW])
    begin = pl.multiple_of((1 - upper) * LANES, LANES)
    lane = lax.broadcasted_iota(jnp.int32, (TILE, LANES), 1)
    packed = None
    for field in range(4 if bed is not None else 3):
        if field < 3:
            part = state[slot, field, :, pl.ds(begin, LANES)]
        else:
            part = bed[slot, :, pl.ds(begin, LANES)]
        turned = pltpu.roll(part, field + 1 - upper, 1)
        packed = turned if field == 0 else jnp.where(lane == field, turned, packed)
    lines = jnp.transpose(packed)[:8]
    columns[...] = lines
    start = pl.multiple_of((device + 1 - 2 * upper) * 8, 8)
    out[pl.ds(start, 8), :TILE] = jnp.where(row == TOP, top, lines)


def opening(
    state_in, bed_in, neighbours_in, wet_in, moves_in,
    out, columns, ctl,
    state, bed, neighbours, wet, moves, sems,
):
    copies = start_all(
        (
            (neighbours_in, neighbours),
            (wet_in, wet),
            (moves_in, moves),
            (state_in.at[0], state.at[0]),
            (state_in.at[1], state.at[1]),
            (bed_in, bed),
        ),
        sems,
    )
    device = lax.axis_index("xb") * 2 + lax.axis_index("yb")
    wait_all(copies[:3])
    first = device * 2
    low = jnp.where(neighbours[3, first] == first + 1, 0, 1)
    ctl[SLOT_LOW] = low
    for position in range(2):
        slot = low if position == 0 else 1 - low
        tile = first + slot
        ctl[WALL_WEST + position] = (neighbours[0, tile] < 0).astype(jnp.int32)
        ctl[WALL_EAST + position] = (neighbours[1, tile] < 0).astype(jnp.int32)
        ctl[WALL_OUTER + position] = (neighbours[2 + position, tile] < 0).astype(jnp.int32)
    for step in range(STEPS):
        for slot in range(2):
            ctl[WET + 2 * step + slot] = wet[step, first + slot]
        ctl[MOVE + step] = moves[step, device]
    count = lax.axis_size("xb")
    upper = lax.axis_index("yb")
    column = lax.axis_index("xb")
    source = lax.rem(column + count - 1, count) * 2 + upper
    before = lax.rem(column + count - 2, count) * 2 + upper
    again = moves[0, source] == moves[1, source]
    tile_first = source * 2 + moves[0, source]
    tile_second = jnp.where(
        again, before * 2 + moves[0, before], source * 2 + 1 - moves[0, source]
    )
    for step in range(STEPS):
        ctl[WET_FIRST + step] = wet[step, tile_first]
        ctl[WET_SECOND + step] = wet[step, tile_second]

    total = jnp.zeros((ROWS, TILE), jnp.float32)
    for slot in range(2):
        copies[3 + slot].wait()

        def group(index, best, slot=slot):
            rows = pl.ds(pl.multiple_of(index * ROWS, ROWS), ROWS)
            along_x, along_y = cell(*(state[slot, field, rows, :] for field in range(3)))
            return jnp.maximum(best, jnp.maximum(along_x[5], along_y[5]))

        best = lax.fori_loop(0, TILE // ROWS, group, jnp.zeros((ROWS, TILE), jnp.float32))
        total = jnp.maximum(total, jnp.where(wet[0, first + slot] > 0, best, 0.0))
    copies[5].wait()
    messages(ctl, state, bed, jnp.max(total, keepdims=True), out, columns)


def hold(first, second, leaving, same):
    del first, second, leaving, same


class Splitting:
    def __init__(self, ctl, state_in, bed_in, manning_in, leaving, buffer, sems):
        slot = ctl[MOVE]
        rows = slice(0, EARLY)
        pairs = (
            (state_in.at[slot, :, rows], buffer.at[0:3]),
            (bed_in.at[slot, rows], buffer.at[3]),
            (manning_in.at[slot, rows], buffer.at[4]),
        )
        self.incoming = [
            pltpu.make_async_copy(src, dst, sems.at[k]) for k, (src, dst) in enumerate(pairs)
        ]
        self.outgoing = [
            pltpu.make_async_copy(buffer.at[:, begin:end], piece, sems.at[3 + k])
            for k, ((begin, end), piece) in enumerate(zip(PIECES, leaving))
        ]

    def start(self):
        for copy in self.incoming:
            copy.start()

    def middle(self):
        wait_all(self.incoming)
        for copy in self.outgoing:
            copy.start()

    def end(self):
        wait_all(self.outgoing)


class Passing:
    def __init__(self, ctl, piece, state_in, bed_in, manning_in, arrived, leaving, buffer, sems):
        self.again = ctl[MOVE] == ctl[MOVE + 1]
        self.other = 1 - ctl[MOVE]
        self.rows = slice(*piece)
        self.refs = state_in, bed_in, manning_in
        self.incoming = pltpu.make_async_copy(arrived, buffer, sems.at[0])
        self.outgoing = pltpu.make_async_copy(buffer, leaving, sems.at[1])
        self.buffer = buffer
        self.sem = sems.at[0]

    def start(self):
        state_in, bed_in, manning_in = self.refs
        buffer, sem, rows = self.buffer, self.sem, self.rows

        @pl.when(self.again)
        def _():
            self.incoming.start()

        @pl.when(jnp.logical_not(self.again))
        def _():
            pltpu.make_async_copy(state_in.at[self.other, :, rows], buffer.at[0:3], sem).start()
            pltpu.make_async_copy(bed_in.at[self.other, rows], buffer.at[3], sem).start()
            pltpu.make_async_copy(manning_in.at[self.other, rows], buffer.at[4], sem).start()

    def middle(self):
        self.incoming.wait()
        self.outgoing.start()

    def end(self):
        self.outgoing.wait()


def rates_and_splitting(
    ctl, state_in, bed_in, manning_in, rate_out, leaving_low, leaving_high,
    state, bed, rate, sems, buffer, moving,
):
    leaving = leaving_low, leaving_high
    splitting = Splitting(ctl, state_in, bed_in, manning_in, leaving, buffer, moving)
    rates(ctl, state_in, bed_in, rate_out, state, bed, rate, sems, splitting)


def rates_and_leaving(
    ctl, state_in, bed_in, state_first, manning_in, arrived, rate_out, leaving,
    state, bed, rate, sems, buffer, moving,
):
    passing = Passing(
        ctl, PIECES[0], state_first, bed_in, manning_in, arrived, leaving, buffer, moving
    )
    rates(ctl, state_in, bed_in, rate_out, state, bed, rate, sems, passing)


def update_and_leaving(
    step, ctl, got_in, ground_in, columns_in, state_in, manning_in, rate_in,
    state_first, bed_in, arrived, fresh_out, first_out, second_out, delta_out, leaving, *rest
):
    *rest, buffer, moving = rest
    passing = Passing(
        ctl, PIECES[1], state_first, bed_in, manning_in, arrived, leaving, buffer, moving
    )
    passing.start()
    update(
        step, ctl, got_in, ground_in, columns_in, state_in, manning_in, rate_in,
        fresh_out, first_out, second_out, delta_out, *rest, passing=passing,
    )
    passing.end()


def rates_after(ctl, state_in, bed_in, order, *rest):
    del order
    rates(ctl, state_in, bed_in, *rest)


def rates(ctl, state_in, bed_in, rate_out, state, bed, rate, sems, passing=None):
    width = 2 * TILE
    row_ids = lax.broadcasted_iota(jnp.int32, (STRIP, width), 0)
    row8 = sublanes(width)
    lane = lax.broadcasted_iota(jnp.int32, (STRIP, LANES), 1)
    last = TILE // STRIP - 1
    chunk = TILE // CHUNKS
    slots = [slot_of(ctl, position) for position in range(2)]
    incoming = []
    for part in range(CHUNKS):
        rows = slice(part * chunk, (part + 1) * chunk)
        incoming.append(
            start_all(
                (
                    (state_in.at[:, :, rows], state.at[:, :, rows]),
                    (bed_in.at[:, rows], bed.at[:, rows]),
                ),
                sems,
                2 * part,
            )
        )
    if passing:
        passing.start()
    keep_west, keep_east, keep_south, keep_north = (
        jnp.where(flag(ctl, index), 1.0, 0.0)
        for index in (WALL_WEST, WALL_EAST, WALL_OUTER, WALL_OUTER + 1)
    )

    def strip(field, rows):
        if field == 3:
            return jnp.concatenate([bed[slot, rows, :] for slot in slots], 1)
        return jnp.concatenate([state[slot, field, rows, :] for slot in slots], 1)

    def blocks(value):
        return [value[:, k * LANES : (k + 1) * LANES] for k in range(4)]

    def right_of(value, end=None):
        turned = [pltpu.roll(part, LANES - 1, 1) for part in blocks(value)]
        after = turned[1:] + [turned[3] if end is None else end]
        return jnp.concatenate(
            [
                jnp.where(lane == LANES - 1, following, part)
                if following is not part
                else part
                for part, following in zip(turned, after)
            ],
            1,
        )

    def left_of(value, end):
        turned = [pltpu.roll(part, 1, 1) for part in blocks(value)]
        before = [end] + turned[:3]
        return jnp.concatenate(
            [jnp.where(lane == 0, previous, part) for part, previous in zip(turned, before)], 1
        )

    def down(value):
        return pltpu.roll(value, STRIP + 7, 0)[:STRIP]

    def group(index, carry):
        base = pl.multiple_of(index * STRIP, STRIP)
        rows = pl.ds(base, STRIP)
        after = pl.ds(pl.multiple_of(jnp.minimum(base + STRIP, TILE - 8), 8), 8)
        at_end = index == last
        fields = [
            jnp.concatenate([strip(field, rows), strip(field, after)], 0) for field in range(3)
        ]
        cells_x, cells_y = cell(*fields)
        here_x = tuple(value[:STRIP] for value in cells_x)
        here_y = tuple(value[:STRIP] for value in cells_y)

        ending = jnp.logical_and(row8 == 7, at_end)
        faces = list(face(here_x, tuple(down(value) for value in cells_x)))
        wall = keep_east * (2.0 * (here_x[3] + here_x[5] * here_x[1])[STRIP - 8 :])
        for component, value in enumerate((0.0, wall, 0.0)):
            upper = faces[component]
            faces[component] = jnp.concatenate(
                [upper[: STRIP - 8], jnp.where(ending, value, upper[STRIP - 8 :])], 0
            )
        turned = tuple(pltpu.roll(value, 1, 0) for value in faces)
        change_x = tuple(
            value - jnp.where(row_ids == 0, before, moved)
            for value, before, moved in zip(faces, carry[:3], turned)
        )
        ground = strip(3, rows)
        ground_after = jnp.where(
            at_end,
            jnp.broadcast_to(keep_east * ground[STRIP - 1 :], (8, width)),
            strip(3, after),
        )
        ground_up = pltpu.roll(ground, 1, 0)
        slope_x = down(jnp.concatenate([ground, ground_after], 0)) - jnp.where(
            row_ids == 0, carry[3], ground_up
        )
        carried = tuple(value[0:1, :] for value in turned) + (ground_up[0:1, :],)

        faces_y = list(face(here_y, tuple(right_of(value) for value in here_y)))
        normal = here_y[3]
        spread_y = here_y[5] * here_y[1]
        north = keep_north * (2.0 * (normal + spread_y)[:, width - LANES :])
        south = keep_south * (2.0 * (normal - spread_y)[:, :LANES])
        change_y = []
        for component, (high, low) in enumerate(((0.0, 0.0), (north, south), (0.0, 0.0))):
            parts = blocks(faces_y[component])
            parts[3] = jnp.where(lane == LANES - 1, high, parts[3])
            value = jnp.concatenate(parts, 1)
            change_y.append(value - left_of(value, low))
        slope_y = right_of(ground, keep_north * ground[:, width - LANES :]) - left_of(
            ground, keep_south * ground[:, :LANES]
        )
        weight = SLOPE * here_x[0]
        results = (
            SCALE * (change_x[0] + change_y[0]),
            SCALE * (change_x[1] + change_y[2]) + weight * slope_x,
            SCALE * (change_x[2] + change_y[1]) + weight * slope_y,
        )
        for field, value in enumerate(results):
            for position, slot in enumerate(slots):
                rate[slot, field, rows, :] = value[:, position * TILE : (position + 1) * TILE]
        return carried

    wait_all(incoming[0])
    top, _ = cell(*(strip(field, slice(0, 8)) for field in range(3)))
    nothing = jnp.zeros((1, width), jnp.float32)
    carry = (
        nothing,
        keep_west * (2.0 * (top[3] - top[5] * top[1])[0:1]),
        nothing,
        keep_west * strip(3, slice(0, 8))[0:1],
    )
    per_chunk = chunk // STRIP
    outgoing = []
    for part in range(CHUNKS):
        if part + 1 < CHUNKS:
            wait_all(incoming[part + 1])
        carry = lax.fori_loop(part * per_chunk, (part + 1) * per_chunk, group, carry)
        rows = slice(part * chunk, (part + 1) * chunk)
        outgoing += start_all(
            ((rate.at[:, :, rows], rate_out.at[:, :, rows]),), sems, 2 * CHUNKS + part
        )
        if passing and part == CHUNKS // 2:
            passing.middle()
    wait_all(outgoing)
    if passing:
        passing.end()


def moved_on(old, slopes, rough, delta, wet_now):
    h, hu, hv = (value - delta * slope for value, slope in zip(old, slopes))
    inverse = 1.0 / h
    u = hu * inverse
    v = hv * inverse
    speed = jnp.sqrt(u * u + v * v)
    power = jnp.exp((-4.0 / 3.0) * jnp.log(jnp.abs(h)))
    drag = (GRAVITY * delta) * (rough * rough) * (speed * power)
    factor = 1.0 / (1.0 + drag)
    fresh = (h, hu * factor, hv * factor)
    return tuple(jnp.where(wet_now, new, value) for new, value in zip(fresh, old))


def repeat_steps(ctl, wet_from, deltas, early, work, other, sems):
    incoming = []
    for ref in early:
        begin = 0 if ref is early[0] else early[0].shape[1]
        incoming += start_all(
            ((ref, work.at[:, begin : begin + ref.shape[1]]),), sems, len(incoming)
        )
    row_ids = lax.broadcasted_iota(jnp.int32, (AGAIN, TILE), 0)
    lane = lax.broadcasted_iota(jnp.int32, (AGAIN, LANES), 1)
    start = tuple(jnp.zeros((1, TILE), jnp.float32) for _ in range(4))

    def halves(value):
        return value[:, :LANES], value[:, LANES:]

    def right_of(value):
        low, high = (pltpu.roll(part, LANES - 1, 1) for part in halves(value))
        return jnp.concatenate([jnp.where(lane == LANES - 1, high, low), high], 1)

    def left_of(value):
        low, high = (pltpu.roll(part, 1, 1) for part in halves(value))
        return jnp.concatenate([low, jnp.where(lane == 0, low, high)], 1)

    def down(value):
        return pltpu.roll(value, AGAIN + 7, 0)[:AGAIN]

    for step in range(STEPS):
        source, target = (work, other) if step % 2 == 0 else (other, work)
        delta = deltas[step][0:1, :]
        wet_now = flag(ctl, wet_from + step)

        def group(index, carry, source=source, target=target, delta=delta, wet_now=wet_now):
            base = pl.multiple_of(index * AGAIN, AGAIN)
            rows = pl.ds(base, AGAIN)
            after = pl.ds(pl.multiple_of(jnp.minimum(base + AGAIN, EARLY - 8), 8), 8)
            refs = [source.at[field] for field in range(3)] + [work.at[3]]
            fields = [jnp.concatenate([ref[rows, :], ref[after, :]], 0) for ref in refs]
            cells_x, cells_y = cell(*fields[:3])
            here_x = tuple(value[:AGAIN] for value in cells_x)
            here_y = tuple(value[:AGAIN] for value in cells_y)
            faces_x = face(here_x, tuple(down(value) for value in cells_x))
            turned = tuple(pltpu.roll(value, 1, 0) for value in faces_x)
            change_x = tuple(
                value - jnp.where(row_ids == 0, before, moved)
                for value, before, moved in zip(faces_x, carry[:3], turned)
            )
            ground = fields[3][:AGAIN]
            ground_up = pltpu.roll(ground, 1, 0)
            slope_x = down(fields[3]) - jnp.where(row_ids == 0, carry[3], ground_up)
            carried = tuple(value[0:1, :] for value in turned) + (ground_up[0:1, :],)
            faces_y = face(here_y, tuple(right_of(value) for value in here_y))
            change_y = tuple(value - left_of(value) for value in faces_y)
            slope_y = right_of(ground) - left_of(ground)
            old = tuple(value[:AGAIN] for value in fields[:3])
            weight = SLOPE * old[0]
            slopes = (
                SCALE * (change_x[0] + change_y[0]),
                SCALE * (change_x[1] + change_y[2]) + weight * slope_x,
                SCALE * (change_x[2] + change_y[1]) + weight * slope_y,
            )
            for field, value in enumerate(
                moved_on(old, slopes, work[4, rows, :], delta, wet_now)
            ):
                target[field, rows, :] = value
            return carried

        if step == 0:
            wait_all(incoming)
        lax.fori_loop(0, EARLY // AGAIN, group, start)


def late_rows(tile, late):
    row = sublanes()
    kept = EARLY - 8
    lane = lax.broadcasted_iota(jnp.int32, (8, LANES), 1)
    for field in range(3):
        late[field, 0:8, :] = jnp.where(
            row < 3, tile[field, 0:8, :], tile[field, kept : kept + 8, :]
        )
        packed = [jnp.zeros((8, LANES), jnp.float32)] * 2
        for block in range(EARLY // 8):
            rows = slice(8 * block, 8 * block + 8)
            sides = jnp.where(lane < 64, tile[field, rows, :LANES], tile[field, rows, LANES:])
            turned = pltpu.roll(sides, (3 + 8 * block) % LANES, 1)
            which = block // 16
            packed[which] = jnp.where(lane // 8 == block % 16, turned, packed[which])
        late[field, 8:16, :] = jnp.concatenate(packed, 1)
        late[field, 16:, :] = tile[field, EARLY:, :]


def merge(late, rest, early, tile):
    for field in range(3):
        merge_field(field, late, rest, early, tile)


def merge_field(field, late, rest, early, tile):
    row = sublanes()
    lane = lax.broadcasted_iota(jnp.int32, (8, LANES), 1)
    first = late[field, 0:8, :]
    for block in range(EARLY // 8):
        rows = slice(8 * block, 8 * block + 8)
        which = block // 16
        packed = late[field, 8:16, which * LANES : (which + 1) * LANES]
        sides = pltpu.roll(packed, (-3 - 8 * block) % LANES, 1)
        value = early[field, rows, :]
        value = jnp.concatenate(
            [
                jnp.where(lane < 3, sides, value[:, :LANES]),
                jnp.where(lane >= LANES - 3, sides, value[:, LANES:]),
            ],
            1,
        )
        if block == 0:
            value = jnp.where(row < 3, first, value)
        if block == EARLY // 8 - 1:
            value = jnp.where(row < 5, value, first)
        tile[field, rows, :] = value
    tile[field, EARLY : TILE - HALF, :] = late[field, 16:, :]
    tile[field, TILE - HALF :, :] = rest[field]


def repeat_second(
    ctl, delta0, delta1, delta2, low, high, late, rest, out, late_out, rest_out, work, tile, sems
):
    near = start_all(((late, late_out), (rest, rest_out)), sems, 2)
    repeat_steps(ctl, WET_SECOND, (delta0, delta1, delta2), (low, high), work, tile, sems)
    wait_all(start_all(((tile, out),), sems) + near)


def repeat_first(
    ctl, delta0, delta1, delta2, low, high, late_in, rest_in, staying, out,
    work, other, tile, late, rest, sems,
):
    kept = out.at[1 - ctl[MOVE + 1]]
    again = ctl[MOVE] == ctl[MOVE + 1]

    @pl.when(again)
    def _():
        wait_all(start_all(((staying, tile),), sems))

    @pl.when(jnp.logical_not(again))
    def _():
        copies = start_all(((late_in, late), (rest_in, rest)), sems, 2)
        repeat_steps(ctl, WET_FIRST, (delta0, delta1, delta2), (low, high), work, other, sems)
        wait_all(copies)
        merge(late, rest, other, tile)

    wait_all(start_all(((tile, kept),), sems))


def finish(ctl, late, rest, early, before, out, tile, sems):
    del before
    copies = []
    for field in range(3):
        merge_field(field, late, rest, early, tile)
        copies += start_all(
            ((tile.at[field], out.at[ctl[MOVE + 1], field]),), sems, field
        )
    wait_all(copies)


def second_late(ctl, arrived, own, order, leaving):
    del order
    again = ctl[MOVE] == ctl[MOVE + 1]
    for field in range(3):
        leaving[field] = jnp.where(again, arrived[field], own[field])


def correct_rows(ctl, slot, got, ground, state, rate, bottom):
    position = jnp.where(ctl[SLOT_LOW] == slot, 0, 1)
    device = lax.axis_index("xb") * 2 + lax.axis_index("yb")
    wall = WALL_WEST if bottom else WALL_EAST

    @pl.when(jnp.logical_not(flag(ctl, wall + position)))
    def _():
        peer = device - 2 if bottom else device + 2
        block = pl.ds(pl.multiple_of(peer * 8, 8), 8)
        lines = got[block, :TILE]
        grounds = ground[block, :TILE]
        stride = 4 if got.shape[1] > TILE else 3

        def line(offset):
            other = offset + stride
            picked = jnp.where(
                position == 0, lines[offset : offset + 1, :], lines[other : other + 1, :]
            )
            return jnp.broadcast_to(picked, (8, TILE))

        ghost, _ = cell(*(line(field) for field in range(3)))
        ghost_ground = jnp.where(position == 0, grounds[3:4, :], grounds[7:8, :])
        rows = slice(0, 8) if bottom else slice(TILE - 8, TILE)
        own = [state[slot, field, rows, :] for field in range(3)]
        here, _ = cell(*own)
        fluxes = face(ghost, here) if bottom else face(here, ghost)
        push = SCALE * fluxes[1] + (SLOPE * own[0]) * ghost_ground
        row = sublanes()
        sign = -1.0 if bottom else 1.0
        chosen = row == (0 if bottom else 7)
        for field, value in enumerate((SCALE * fluxes[0], push, SCALE * fluxes[2])):
            rate[slot, field, rows, :] += jnp.where(chosen, sign * value, 0.0)


def column_fix(got, ground, columns):
    upper = lax.axis_index("yb")
    device = lax.axis_index("xb") * 2 + upper
    peer = device + 1 - 2 * upper
    block = pl.ds(pl.multiple_of(peer * 8, 8), 8)
    lines = got[block, :TILE]
    ghost_ground = ground[block, :TILE][3:4]
    mine = columns[...]
    _, ghost = cell(lines[0:1], lines[1:2], lines[2:3])
    _, own = cell(mine[0:1], mine[1:2], mine[2:3])
    low = upper == 0
    left = tuple(jnp.where(low, a, b) for a, b in zip(own, ghost))
    right = tuple(jnp.where(low, b, a) for a, b in zip(own, ghost))
    fluxes = face(left, right)
    sign = jnp.where(low, 1.0, -1.0)
    push = SCALE * fluxes[1] + (SLOPE * mine[0:1]) * ghost_ground
    block8 = stacked(
        [sign * SCALE * fluxes[0], sign * SCALE * fluxes[2], sign * push],
        jnp.zeros((8, TILE), jnp.float32),
    )
    return jnp.transpose(
        jnp.concatenate([block8, jnp.zeros((LANES - 8, TILE), jnp.float32)], 0)
    )


def last_update(ctl, got, ground, columns, state, manning, rate, order, *rest):
    del order
    slots = ctl[MOVE], 1 - ctl[MOVE]
    update(STEPS - 1, ctl, got, ground, columns, state, manning, rate, *rest, slots=slots)


def update(
    step, ctl, got_in, ground_in, columns_in, state_in, manning_in, rate_in, *rest,
    passing=None, slots=(0, 1),
):
    more = step + 1 < STEPS
    fresh_out, *lines_to, delta_out = rest[: 4 if more else 6]
    rest = rest[4 if more else 6 :]
    state, manning, rate, fresh, got, ground, columns, first, second, delta_keep, sems = rest
    out, columns_out = first, second
    small = start_all(
        ((got_in, got), (ground_in, ground), (columns_in, columns)), sems, 5 * PARTS
    )
    size = 2 * TILE // PARTS
    parts = [
        (slot, slice(k * size, (k + 1) * size)) for slot in slots for k in range(PARTS // 2)
    ]
    incoming = []
    for index, (slot, rows) in enumerate(parts):
        incoming.append(
            start_all(
                (
                    (rate_in.at[slot, :, rows], rate.at[slot, :, rows]),
                    (state_in.at[slot, :, rows], state.at[slot, :, rows]),
                    (manning_in.at[slot, rows], manning.at[slot, rows]),
                ),
                sems,
                3 * index,
            )
        )
    wait_all(small)
    upper = lax.axis_index("yb")
    devices = 2 * lax.axis_size("xb")
    begin = TILE if got.shape[1] > TILE else 0
    tops = got[0:8, begin : begin + LANES]
    for peer in range(1, devices):
        tops = jnp.maximum(tops, got[peer * 8 : peer * 8 + 8, begin : begin + LANES])
    delta = (COURANT * SPACING) / tops[TOP : TOP + 1, :]
    delta = jnp.concatenate([delta, delta], 1)
    delta_keep[...] = jnp.broadcast_to(delta, (8, TILE))
    outgoing = start_all(((delta_keep, delta_out),), sems, 5 * PARTS + 3)
    fix = column_fix(got, ground, columns)
    facing = jnp.where(upper > 0, ctl[SLOT_LOW], 1 - ctl[SLOT_LOW])
    begin = pl.multiple_of((1 - upper) * LANES, LANES)
    goal = (1 - upper) * (LANES - 1)
    lane = lax.broadcasted_iota(jnp.int32, (size, LANES), 1)
    total = jnp.zeros((ROWS, TILE), jnp.float32)
    for index, (slot, part_rows) in enumerate(parts):
        wait_all(incoming[index])
        if part_rows.start == 0:
            correct_rows(ctl, slot, got, ground, state, rate, True)
        if part_rows.stop == TILE:
            correct_rows(ctl, slot, got, ground, state, rate, False)

        @pl.when(facing == slot)
        def _(slot=slot, part_rows=part_rows):
            for field in range(3):
                turned = pltpu.roll(
                    fix[part_rows], lax.rem(goal + LANES - field, LANES), 1
                )
                rate[slot, field, part_rows, pl.ds(begin, LANES)] += jnp.where(
                    lane == goal, turned, 0.0
                )

        wet_now = flag(ctl, WET + 2 * step + slot)

        def group(index, best, slot=slot, wet_now=wet_now):
            rows = pl.ds(pl.multiple_of(index * ROWS, ROWS), ROWS)
            old = tuple(state[slot, field, rows, :] for field in range(3))
            slopes = tuple(rate[slot, field, rows, :] for field in range(3))
            h, hu, hv = moved_on(old, slopes, manning[slot, rows, :], delta, wet_now)
            fresh[slot, 0, rows, :] = h
            fresh[slot, 1, rows, :] = hu
            fresh[slot, 2, rows, :] = hv
            if more:
                along_x, along_y = cell(h, hu, hv)
                best = jnp.maximum(best, jnp.maximum(along_x[5], along_y[5]))
            return best

        best = lax.fori_loop(
            part_rows.start // ROWS,
            part_rows.stop // ROWS,
            group,
            jnp.zeros((ROWS, TILE), jnp.float32),
        )
        if more:
            best = jnp.where(flag(ctl, WET + 2 * step + 2 + slot), best, 0.0)
            total = jnp.maximum(total, best)
        if more:
            outgoing += start_all(
                ((fresh.at[slot, :, part_rows], fresh_out.at[slot, :, part_rows]),),
                sems,
                3 * PARTS + index,
            )
        elif index >= PARTS // 2:
            outgoing += start_all(
                ((fresh.at[slot, :, part_rows], fresh_out.at[:, part_rows]),),
                sems,
                3 * PARTS + index,
            )
        if not more and part_rows.stop == TILE:
            late, low, high = (
                (first, *lines_to[:2]) if index < PARTS // 2 else (second, *lines_to[2:])
            )
            late_rows(fresh.at[slot], late)
            outgoing += start_all(
                ((late.at[:, :HALF], low), (late.at[:, HALF:], high)),
                sems,
                4 * PARTS + (0 if index < PARTS // 2 else 2),
            )
        if passing and index == PARTS // 2:
            passing.middle()
    if more:
        messages(ctl, fresh, None, jnp.max(total, keepdims=True), out, columns_out)
        pairs = zip((out, columns_out), lines_to)
        outgoing += start_all(tuple(pairs), sems, 4 * PARTS)
    wait_all(outgoing)


def vmem():
    return pl.BlockSpec(memory_space=pltpu.VMEM)


def smem():
    return pl.BlockSpec(memory_space=pltpu.SMEM)


def hbm():
    return pl.BlockSpec(memory_space=pltpu.HBM)


def anywhere():
    return pl.BlockSpec(memory_space=pl.ANY)


def call(
    kernel, outs, out_specs, in_specs, flops, scratch=(), aliases=None, room=VMEM_BYTES, moved=4
):
    return pl.pallas_call(
        kernel,
        scratch_shapes=scratch,
        input_output_aliases=aliases or {},
        out_shape=outs,
        in_specs=in_specs,
        out_specs=out_specs,
        compiler_params=pltpu.CompilerParams(vmem_limit_bytes=room),
        cost_estimate=pl.CostEstimate(flops=flops, bytes_accessed=moved << 20, transcendentals=0),
    )


def f32(*shape):
    return jax.ShapeDtypeStruct(shape, jnp.float32)


def spread(fast):
    return lax.all_to_all(fast, ("xb", "yb"), split_axis=0, concat_axis=0, tiled=True)


def body(state, bed, manning, neighbours, wet, moves):
    shape = f32(*state.shape)
    devices = lax.axis_size("xb") * lax.axis_size("yb")
    whole = pltpu.VMEM(state.shape, jnp.float32)
    part = pltpu.VMEM(bed.shape, jnp.float32)
    tile_shape = f32(*state.shape[1:])
    early_shape = f32(5, EARLY, TILE)
    early_state = f32(3, EARLY, TILE)
    late_shape = f32(3, LATE, TILE)
    half_shape = f32(3, HALF, TILE)
    delta_shape = f32(8, TILE)

    def buffer(like):
        return pltpu.VMEM(like.shape, jnp.float32)

    piece_shapes = tuple(f32(5, end - begin, TILE) for begin, end in PIECES)
    out, columns, ctl = call(
        opening,
        (
            f32(8 * devices, TILE + LANES),
            f32(8, TILE),
            jax.ShapeDtypeStruct((CONTROLS,), jnp.int32),
        ),
        (vmem(), vmem(), smem()),
        [hbm()] * 5,
        4 << 20,
        [
            whole,
            part,
            pltpu.SMEM(neighbours.shape[::-1], jnp.int32),
            pltpu.SMEM(wet.shape, jnp.int32),
            pltpu.SMEM(moves.shape, jnp.int32),
            pltpu.SemaphoreType.DMA((6,)),
        ],
    )(state, bed, neighbours.T, wet, moves)
    state_first = state
    ground = None
    deltas = []
    for step in range(STEPS):
        got = spread(out)
        ground = got if step == 0 else ground
        scratch = [whole, part, whole, pltpu.SemaphoreType.DMA((3 * CHUNKS,))]
        piece_scratch = [
            [buffer(piece), pltpu.SemaphoreType.DMA((2,))] for piece in piece_shapes
        ]
        if step == 1:
            rate, leaving = call(
                rates_and_leaving,
                (shape, piece_shapes[0]),
                (hbm(),) * 2,
                [smem()] + [hbm()] * 5,
                16 << 20,
                scratch + piece_scratch[0],
            )(ctl, state, bed, state_first, manning, early_first[0])
            early_second = [shifted(leaving, "xb", 1)]
        elif step == 2:
            rate = call(rates_after, shape, hbm(), [smem()] + [hbm()] * 3, 16 << 20, scratch)(
                ctl, state, bed, early_second[0]
            )
        else:
            rate, *leaving = call(
                rates_and_splitting,
                (shape,) + piece_shapes,
                (hbm(),) * 3,
                [smem()] + [hbm()] * 3,
                16 << 20,
                scratch + [buffer(early_shape), pltpu.SemaphoreType.DMA((5,))],
            )(ctl, state, bed, manning)
            held = call(
                hold, piece_shapes[0], hbm(), [hbm()] * 3, 1 << 10, aliases={2: 0}
            )(rate, got, leaving[0])
            early_first = [shifted(held, "xb", 1)]
        more = step + 1 < STEPS
        shapes = (f32(8 * devices, TILE), f32(8, TILE)) if more else (half_shape,) * 4
        passing = step == 1
        work = [
            whole,
            part,
            whole,
            whole,
            pltpu.VMEM(got.shape, jnp.float32),
            pltpu.VMEM(ground.shape, jnp.float32),
            pltpu.VMEM((8, TILE), jnp.float32),
            buffer(shapes[0] if more else late_shape),
            buffer(shapes[1] if more else late_shape),
            buffer(delta_shape),
            pltpu.SemaphoreType.DMA((5 * PARTS + 4,)),
        ]
        operands = ctl, got, ground, columns, state, manning, rate
        if not more:
            break
        outs = call(
            functools.partial(update_and_leaving if passing else update, step),
            (shape,) + shapes + (delta_shape,) + ((piece_shapes[1],) if passing else ()),
            (hbm(),) * (5 if passing else 4),
            [smem()] + [hbm()] * (9 if passing else 6),
            8 << 20,
            work + (piece_scratch[1] if passing else []),
            moved=10,
        )(*operands, *((state_first, bed, early_first[1]) if passing else ()))
        state, out, columns, delta, *passed = outs
        deltas.append(delta)
        if step == 0:
            held = call(
                hold, piece_shapes[1], hbm(), [hbm()] * 3, 1 << 10, aliases={2: 0}
            )(delta, delta, leaving[1])
            early_first.append(shifted(held, "xb", 1))
        elif step == 1:
            early_second.append(shifted(passed[0], "xb", 1))

    staying, late_first, rest_first, late_second, rest_second, delta = call(
        last_update,
        (tile_shape,) + shapes + (delta_shape,),
        (hbm(),) * 6,
        [smem()] + [hbm()] * 7,
        8 << 20,
        work,
        moved=10,
    )(*operands, early_second[1])
    deltas.append(delta)
    room = 16 << 20
    late_arrived = shifted(late_first, "xb", 1)
    rest_arrived = shifted(rest_first, "xb", 1)
    second, late_second, rest_second = call(
        repeat_second,
        (early_state, half_shape, half_shape),
        (anywhere(), vmem(), vmem()),
        [smem()] + [vmem()] * 3 + [hbm()] * 4,
        8 << 20,
        [buffer(early_shape), buffer(early_state), pltpu.SemaphoreType.DMA((4,))],
    )(ctl, *deltas, *early_second, late_second, rest_second)

    def pass_late(arrived, own):
        leaving = call(
            second_late,
            half_shape,
            vmem(),
            [smem(), vmem(), vmem(), anywhere()],
            1 << 10,
            room=room,
        )(ctl, arrived, own, second)
        return shifted(leaving, "xb", 1)

    late_next = pass_late(late_arrived, late_second)
    rest_next = pass_late(rest_arrived, rest_second)
    final = call(
        repeat_first,
        shape,
        hbm(),
        [smem()] + [vmem()] * 3 + [anywhere()] * 5,
        8 << 20,
        [
            buffer(early_shape),
            buffer(early_state),
            buffer(tile_shape),
            buffer(half_shape),
            buffer(half_shape),
            pltpu.SemaphoreType.DMA((4,)),
        ],
        room=room,
    )(ctl, *deltas, *early_first, late_arrived, rest_arrived, staying)
    return call(
        finish,
        shape,
        hbm(),
        [smem(), vmem(), vmem(), vmem(), hbm()],
        1 << 20,
        [buffer(tile_shape), pltpu.SemaphoreType.DMA((3,))],
        {4: 0},
        room=room,
    )(ctl, late_next, rest_next, second, final)


def solution(mesh):
    placed = (
        P(("runs", "xb", "yb"), None, None, None),
        P(("runs", "xb", "yb"), None, None),
        P(("runs", "xb", "yb"), None, None),
        P("runs", None),
        P(None, "runs"),
        P(None, "runs"),
    )
    return jax.shard_map(
        body,
        mesh=mesh,
        in_specs=placed,
        out_specs=P(("runs", "xb", "yb"), None, None, None),
        check_vma=False,
    )
```

```python
import functools

import jax
import jax.numpy as jnp
from jax import lax
from jax.experimental import pallas as pl
from jax.experimental.pallas import tpu as pltpu
from jax.sharding import PartitionSpec as P

STEPS = 3
GRAVITY = 9.81
ROOT_G = GRAVITY**0.5
SPACING = 5.0
COURANT = 0.2
ROWS = 32
LANES = 128
TILE = 256
VMEM_BYTES = 60 * 1024 * 1024
SLOT_LOW, WALL_WEST, WALL_EAST, WALL_OUTER, WET, MOVE = 0, 1, 3, 5, 7, 13
WET_FIRST, WET_SECOND = 16, 19
CONTROLS = 24
EARLY = 144
PIECES = ((0, 80), (80, 144))
AGAIN = 48
LATE = TILE - EARLY + 16
HALF = LATE // 2
CHUNKS = 8
PARTS = 4
STRIP = 32
TOP = 6
SCALE = 0.5 / SPACING
SLOPE = GRAVITY / (2.0 * SPACING)


def shifted(value, axis, steps, around=True):
    count = lax.axis_size(axis)
    pairs = [(source, (source + steps) % count) for source in range(count)]
    if not around:
        pairs = [pair for pair in pairs if abs(pair[0] - pair[1]) == abs(steps)]
    return lax.ppermute(value, axis, pairs)


def cell(h, hu, hv):
    root = lax.rsqrt(h)
    inverse = root * root
    u = hu * inverse
    v = hv * inverse
    celerity = ROOT_G * (h * root)
    pressure = (0.5 * GRAVITY) * (h * h)
    cross = hu * v
    speed_x = jnp.abs(u) + celerity
    speed_y = jnp.abs(v) + celerity
    along_x = (h, hu, hv, hu * u + pressure, cross, speed_x)
    along_y = (h, hv, hu, hv * v + pressure, cross, speed_y)
    return along_x, along_y


def face(left, right):
    wave = jnp.maximum(left[5], right[5])
    return (
        (left[1] + right[1]) - wave * (right[0] - left[0]),
        (left[3] + right[3]) - wave * (right[1] - left[1]),
        (left[4] + right[4]) - wave * (right[2] - left[2]),
    )


def slot_of(ctl, position):
    low = ctl[SLOT_LOW]
    return low if position == 0 else 1 - low


def flag(ctl, index):
    return ctl[index] > 0


def start_all(pairs, sems, first=0):
    copies = [
        pltpu.make_async_copy(src, dst, sems.at[first + k]) for k, (src, dst) in enumerate(pairs)
    ]
    for copy in copies:
        copy.start()
    return copies


def wait_all(copies):
    for copy in copies:
        copy.wait()


def sublanes(width=TILE):
    return lax.broadcasted_iota(jnp.int32, (8, width), 0)


def stacked(lines, base):
    row = sublanes()
    for index, line in enumerate(lines):
        base = jnp.where(row == index, jnp.broadcast_to(line, (8, TILE)), base)
    return base


def messages(ctl, state, bed, fastest, out, columns):
    upper = lax.axis_index("yb")
    column = lax.axis_index("xb")
    last = lax.axis_size("xb") - 1
    devices = 2 * (last + 1)
    device = column * 2 + upper
    top = jnp.broadcast_to(fastest, (8, TILE))
    for peer in range(devices):
        out[peer * 8 : peer * 8 + 8, :TILE] = top
        if bed is not None:
            out[peer * 8 : peer * 8 + 8, TILE:] = top[:, :LANES]
    row = sublanes()

    def edge(line):
        rows = slice(line, line + 1)
        lines = []
        for position in range(2):
            slot = slot_of(ctl, position)
            lines += [state[slot, field, rows, :] for field in range(3)]
            if bed is not None:
                lines.append(bed[slot, rows, :])
        return stacked(lines, top)

    for inside, peer, line in (
        (column > 0, device - 2, 0),
        (column < last, device + 2, TILE - 1),
    ):

        @pl.when(inside)
        def _(peer=peer, line=line):
            out[pl.ds(pl.multiple_of(peer * 8, 8), 8), :TILE] = edge(line)

    slot = jnp.where(upper > 0, ctl[SLOT_LOW], 1 - ctl[SLOT_LOW])
    begin = pl.multiple_of((1 - upper) * LANES, LANES)
    lane = lax.broadcasted_iota(jnp.int32, (TILE, LANES), 1)
    packed = None
    for field in range(4 if bed is not None else 3):
        if field < 3:
            part = state[slot, field, :, pl.ds(begin, LANES)]
        else:
            part = bed[slot, :, pl.ds(begin, LANES)]
        turned = pltpu.roll(part, field + 1 - upper, 1)
        packed = turned if field == 0 else jnp.where(lane == field, turned, packed)
    lines = jnp.transpose(packed)[:8]
    columns[...] = lines
    start = pl.multiple_of((device + 1 - 2 * upper) * 8, 8)
    out[pl.ds(start, 8), :TILE] = jnp.where(row == TOP, top, lines)


def opening(
    state_in, bed_in, neighbours_in, wet_in, moves_in,
    out, columns, ctl,
    state, bed, neighbours, wet, moves, sems,
):
    copies = start_all(
        (
            (neighbours_in, neighbours),
            (wet_in, wet),
            (moves_in, moves),
            (state_in.at[0], state.at[0]),
            (state_in.at[1], state.at[1]),
            (bed_in, bed),
        ),
        sems,
    )
    device = lax.axis_index("xb") * 2 + lax.axis_index("yb")
    wait_all(copies[:3])
    first = device * 2
    low = jnp.where(neighbours[3, first] == first + 1, 0, 1)
    ctl[SLOT_LOW] = low
    for position in range(2):
        slot = low if position == 0 else 1 - low
        tile = first + slot
        ctl[WALL_WEST + position] = (neighbours[0, tile] < 0).astype(jnp.int32)
        ctl[WALL_EAST + position] = (neighbours[1, tile] < 0).astype(jnp.int32)
        ctl[WALL_OUTER + position] = (neighbours[2 + position, tile] < 0).astype(jnp.int32)
    for step in range(STEPS):
        for slot in range(2):
            ctl[WET + 2 * step + slot] = wet[step, first + slot]
        ctl[MOVE + step] = moves[step, device]
    count = lax.axis_size("xb")
    upper = lax.axis_index("yb")
    column = lax.axis_index("xb")
    source = lax.rem(column + count - 1, count) * 2 + upper
    before = lax.rem(column + count - 2, count) * 2 + upper
    again = moves[0, source] == moves[1, source]
    tile_first = source * 2 + moves[0, source]
    tile_second = jnp.where(
        again, before * 2 + moves[0, before], source * 2 + 1 - moves[0, source]
    )
    for step in range(STEPS):
        ctl[WET_FIRST + step] = wet[step, tile_first]
        ctl[WET_SECOND + step] = wet[step, tile_second]

    total = jnp.zeros((ROWS, TILE), jnp.float32)
    for slot in range(2):
        copies[3 + slot].wait()

        def group(index, best, slot=slot):
            rows = pl.ds(pl.multiple_of(index * ROWS, ROWS), ROWS)
            along_x, along_y = cell(*(state[slot, field, rows, :] for field in range(3)))
            return jnp.maximum(best, jnp.maximum(along_x[5], along_y[5]))

        best = lax.fori_loop(0, TILE // ROWS, group, jnp.zeros((ROWS, TILE), jnp.float32))
        total = jnp.maximum(total, jnp.where(wet[0, first + slot] > 0, best, 0.0))
    copies[5].wait()
    messages(ctl, state, bed, jnp.max(total, keepdims=True), out, columns)


def hold(first, second, leaving, same):
    del first, second, leaving, same


class Splitting:
    def __init__(self, ctl, state_in, bed_in, manning_in, leaving, buffer, sems):
        slot = ctl[MOVE]
        rows = slice(0, EARLY)
        pairs = (
            (state_in.at[slot, :, rows], buffer.at[0:3]),
            (bed_in.at[slot, rows], buffer.at[3]),
            (manning_in.at[slot, rows], buffer.at[4]),
        )
        self.incoming = [
            pltpu.make_async_copy(src, dst, sems.at[k]) for k, (src, dst) in enumerate(pairs)
        ]
        self.outgoing = [
            pltpu.make_async_copy(buffer.at[:, begin:end], piece, sems.at[3 + k])
            for k, ((begin, end), piece) in enumerate(zip(PIECES, leaving))
        ]

    def start(self):
        for copy in self.incoming:
            copy.start()

    def middle(self):
        wait_all(self.incoming)
        for copy in self.outgoing:
            copy.start()

    def end(self):
        wait_all(self.outgoing)


class Passing:
    def __init__(self, ctl, piece, state_in, bed_in, manning_in, arrived, leaving, buffer, sems):
        self.again = ctl[MOVE] == ctl[MOVE + 1]
        self.other = 1 - ctl[MOVE]
        self.rows = slice(*piece)
        self.refs = state_in, bed_in, manning_in
        self.incoming = pltpu.make_async_copy(arrived, buffer, sems.at[0])
        self.outgoing = pltpu.make_async_copy(buffer, leaving, sems.at[1])
        self.buffer = buffer
        self.sem = sems.at[0]

    def start(self):
        state_in, bed_in, manning_in = self.refs
        buffer, sem, rows = self.buffer, self.sem, self.rows

        @pl.when(self.again)
        def _():
            self.incoming.start()

        @pl.when(jnp.logical_not(self.again))
        def _():
            pltpu.make_async_copy(state_in.at[self.other, :, rows], buffer.at[0:3], sem).start()
            pltpu.make_async_copy(bed_in.at[self.other, rows], buffer.at[3], sem).start()
            pltpu.make_async_copy(manning_in.at[self.other, rows], buffer.at[4], sem).start()

    def middle(self):
        self.incoming.wait()
        self.outgoing.start()

    def end(self):
        self.outgoing.wait()


def rates_and_splitting(
    ctl, state_in, bed_in, manning_in, rate_out, leaving_low, leaving_high,
    state, bed, rate, sems, buffer, moving,
):
    leaving = leaving_low, leaving_high
    splitting = Splitting(ctl, state_in, bed_in, manning_in, leaving, buffer, moving)
    rates(ctl, state_in, bed_in, rate_out, state, bed, rate, sems, splitting)


def rates_and_leaving(
    ctl, state_in, bed_in, state_first, manning_in, arrived, rate_out, leaving,
    state, bed, rate, sems, buffer, moving,
):
    passing = Passing(
        ctl, PIECES[0], state_first, bed_in, manning_in, arrived, leaving, buffer, moving
    )
    rates(ctl, state_in, bed_in, rate_out, state, bed, rate, sems, passing)


def update_and_leaving(
    step, ctl, got_in, ground_in, columns_in, state_in, manning_in, rate_in,
    state_first, bed_in, arrived, fresh_out, first_out, second_out, delta_out, leaving, *rest
):
    *rest, buffer, moving = rest
    passing = Passing(
        ctl, PIECES[1], state_first, bed_in, manning_in, arrived, leaving, buffer, moving
    )
    passing.start()
    update(
        step, ctl, got_in, ground_in, columns_in, state_in, manning_in, rate_in,
        fresh_out, first_out, second_out, delta_out, *rest, passing=passing,
    )
    passing.end()


def rates_after(ctl, state_in, bed_in, order, *rest):
    del order
    rates(ctl, state_in, bed_in, *rest)


def rates(ctl, state_in, bed_in, rate_out, state, bed, rate, sems, passing=None):
    width = 2 * TILE
    row_ids = lax.broadcasted_iota(jnp.int32, (STRIP, width), 0)
    row8 = sublanes(width)
    lane = lax.broadcasted_iota(jnp.int32, (STRIP, LANES), 1)
    last = TILE // STRIP - 1
    chunk = TILE // CHUNKS
    slots = [slot_of(ctl, position) for position in range(2)]
    incoming = []
    for part in range(CHUNKS):
        rows = slice(part * chunk, (part + 1) * chunk)
        incoming.append(
            start_all(
                (
                    (state_in.at[:, :, rows], state.at[:, :, rows]),
                    (bed_in.at[:, rows], bed.at[:, rows]),
                ),
                sems,
                2 * part,
            )
        )
    if passing:
        passing.start()
    keep_west, keep_east, keep_south, keep_north = (
        jnp.where(flag(ctl, index), 1.0, 0.0)
        for index in (WALL_WEST, WALL_EAST, WALL_OUTER, WALL_OUTER + 1)
    )

    def strip(field, rows):
        if field == 3:
            return jnp.concatenate([bed[slot, rows, :] for slot in slots], 1)
        return jnp.concatenate([state[slot, field, rows, :] for slot in slots], 1)

    def blocks(value):
        return [value[:, k * LANES : (k + 1) * LANES] for k in range(4)]

    def right_of(value, end=None):
        turned = [pltpu.roll(part, LANES - 1, 1) for part in blocks(value)]
        after = turned[1:] + [turned[3] if end is None else end]
        return jnp.concatenate(
            [
                jnp.where(lane == LANES - 1, following, part)
                if following is not part
                else part
                for part, following in zip(turned, after)
            ],
            1,
        )

    def left_of(value, end):
        turned = [pltpu.roll(part, 1, 1) for part in blocks(value)]
        before = [end] + turned[:3]
        return jnp.concatenate(
            [jnp.where(lane == 0, previous, part) for part, previous in zip(turned, before)], 1
        )

    def down(value):
        return pltpu.roll(value, STRIP + 7, 0)[:STRIP]

    def group(index, carry):
        base = pl.multiple_of(index * STRIP, STRIP)
        rows = pl.ds(base, STRIP)
        after = pl.ds(pl.multiple_of(jnp.minimum(base + STRIP, TILE - 8), 8), 8)
        at_end = index == last
        fields = [
            jnp.concatenate([strip(field, rows), strip(field, after)], 0) for field in range(3)
        ]
        cells_x, cells_y = cell(*fields)
        here_x = tuple(value[:STRIP] for value in cells_x)
        here_y = tuple(value[:STRIP] for value in cells_y)

        ending = jnp.logical_and(row8 == 7, at_end)
        faces = list(face(here_x, tuple(down(value) for value in cells_x)))
        wall = keep_east * (2.0 * (here_x[3] + here_x[5] * here_x[1])[STRIP - 8 :])
        for component, value in enumerate((0.0, wall, 0.0)):
            upper = faces[component]
            faces[component] = jnp.concatenate(
                [upper[: STRIP - 8], jnp.where(ending, value, upper[STRIP - 8 :])], 0
            )
        turned = tuple(pltpu.roll(value, 1, 0) for value in faces)
        change_x = tuple(
            value - jnp.where(row_ids == 0, before, moved)
            for value, before, moved in zip(faces, carry[:3], turned)
        )
        ground = strip(3, rows)
        ground_after = jnp.where(
            at_end,
            jnp.broadcast_to(keep_east * ground[STRIP - 1 :], (8, width)),
            strip(3, after),
        )
        ground_up = pltpu.roll(ground, 1, 0)
        slope_x = down(jnp.concatenate([ground, ground_after], 0)) - jnp.where(
            row_ids == 0, carry[3], ground_up
        )
        carried = tuple(value[0:1, :] for value in turned) + (ground_up[0:1, :],)

        faces_y = list(face(here_y, tuple(right_of(value) for value in here_y)))
        normal = here_y[3]
        spread_y = here_y[5] * here_y[1]
        north = keep_north * (2.0 * (normal + spread_y)[:, width - LANES :])
        south = keep_south * (2.0 * (normal - spread_y)[:, :LANES])
        change_y = []
        for component, (high, low) in enumerate(((0.0, 0.0), (north, south), (0.0, 0.0))):
            parts = blocks(faces_y[component])
            parts[3] = jnp.where(lane == LANES - 1, high, parts[3])
            value = jnp.concatenate(parts, 1)
            change_y.append(value - left_of(value, low))
        slope_y = right_of(ground, keep_north * ground[:, width - LANES :]) - left_of(
            ground, keep_south * ground[:, :LANES]
        )
        weight = SLOPE * here_x[0]
        results = (
            SCALE * (change_x[0] + change_y[0]),
            SCALE * (change_x[1] + change_y[2]) + weight * slope_x,
            SCALE * (change_x[2] + change_y[1]) + weight * slope_y,
        )
        for field, value in enumerate(results):
            for position, slot in enumerate(slots):
                rate[slot, field, rows, :] = value[:, position * TILE : (position + 1) * TILE]
        return carried

    wait_all(incoming[0])
    top, _ = cell(*(strip(field, slice(0, 8)) for field in range(3)))
    nothing = jnp.zeros((1, width), jnp.float32)
    carry = (
        nothing,
        keep_west * (2.0 * (top[3] - top[5] * top[1])[0:1]),
        nothing,
        keep_west * strip(3, slice(0, 8))[0:1],
    )
    per_chunk = chunk // STRIP
    outgoing = []
    for part in range(CHUNKS):
        if part + 1 < CHUNKS:
            wait_all(incoming[part + 1])
        carry = lax.fori_loop(part * per_chunk, (part + 1) * per_chunk, group, carry)
        rows = slice(part * chunk, (part + 1) * chunk)
        outgoing += start_all(
            ((rate.at[:, :, rows], rate_out.at[:, :, rows]),), sems, 2 * CHUNKS + part
        )
        if passing and part == CHUNKS // 2:
            passing.middle()
    wait_all(outgoing)
    if passing:
        passing.end()


def moved_on(old, slopes, rough, delta, wet_now):
    h, hu, hv = (value - delta * slope for value, slope in zip(old, slopes))
    inverse = 1.0 / h
    u = hu * inverse
    v = hv * inverse
    speed = jnp.sqrt(u * u + v * v)
    power = jnp.exp((-4.0 / 3.0) * jnp.log(jnp.abs(h)))
    drag = (GRAVITY * delta) * (rough * rough) * (speed * power)
    factor = 1.0 / (1.0 + drag)
    fresh = (h, hu * factor, hv * factor)
    return tuple(jnp.where(wet_now, new, value) for new, value in zip(fresh, old))


def repeat_steps(ctl, wet_from, deltas, early, work, other, sems):
    incoming = []
    for ref in early:
        begin = 0 if ref is early[0] else early[0].shape[1]
        incoming += start_all(
            ((ref, work.at[:, begin : begin + ref.shape[1]]),), sems, len(incoming)
        )
    row_ids = lax.broadcasted_iota(jnp.int32, (AGAIN, TILE), 0)
    lane = lax.broadcasted_iota(jnp.int32, (AGAIN, LANES), 1)
    start = tuple(jnp.zeros((1, TILE), jnp.float32) for _ in range(4))

    def halves(value):
        return value[:, :LANES], value[:, LANES:]

    def right_of(value):
        low, high = (pltpu.roll(part, LANES - 1, 1) for part in halves(value))
        return jnp.concatenate([jnp.where(lane == LANES - 1, high, low), high], 1)

    def left_of(value):
        low, high = (pltpu.roll(part, 1, 1) for part in halves(value))
        return jnp.concatenate([low, jnp.where(lane == 0, low, high)], 1)

    def down(value):
        return pltpu.roll(value, AGAIN + 7, 0)[:AGAIN]

    for step in range(STEPS):
        source, target = (work, other) if step % 2 == 0 else (other, work)
        delta = deltas[step][0:1, :]
        wet_now = flag(ctl, wet_from + step)

        def group(index, carry, source=source, target=target, delta=delta, wet_now=wet_now):
            base = pl.multiple_of(index * AGAIN, AGAIN)
            rows = pl.ds(base, AGAIN)
            after = pl.ds(pl.multiple_of(jnp.minimum(base + AGAIN, EARLY - 8), 8), 8)
            refs = [source.at[field] for field in range(3)] + [work.at[3]]
            fields = [jnp.concatenate([ref[rows, :], ref[after, :]], 0) for ref in refs]
            cells_x, cells_y = cell(*fields[:3])
            here_x = tuple(value[:AGAIN] for value in cells_x)
            here_y = tuple(value[:AGAIN] for value in cells_y)
            faces_x = face(here_x, tuple(down(value) for value in cells_x))
            turned = tuple(pltpu.roll(value, 1, 0) for value in faces_x)
            change_x = tuple(
                value - jnp.where(row_ids == 0, before, moved)
                for value, before, moved in zip(faces_x, carry[:3], turned)
            )
            ground = fields[3][:AGAIN]
            ground_up = pltpu.roll(ground, 1, 0)
            slope_x = down(fields[3]) - jnp.where(row_ids == 0, carry[3], ground_up)
            carried = tuple(value[0:1, :] for value in turned) + (ground_up[0:1, :],)
            faces_y = face(here_y, tuple(right_of(value) for value in here_y))
            change_y = tuple(value - left_of(value) for value in faces_y)
            slope_y = right_of(ground) - left_of(ground)
            old = tuple(value[:AGAIN] for value in fields[:3])
            weight = SLOPE * old[0]
            slopes = (
                SCALE * (change_x[0] + change_y[0]),
                SCALE * (change_x[1] + change_y[2]) + weight * slope_x,
                SCALE * (change_x[2] + change_y[1]) + weight * slope_y,
            )
            for field, value in enumerate(
                moved_on(old, slopes, work[4, rows, :], delta, wet_now)
            ):
                target[field, rows, :] = value
            return carried

        if step == 0:
            wait_all(incoming)
        lax.fori_loop(0, EARLY // AGAIN, group, start)


def late_rows(tile, late):
    row = sublanes()
    kept = EARLY - 8
    lane = lax.broadcasted_iota(jnp.int32, (8, LANES), 1)
    for field in range(3):
        late[field, 0:8, :] = jnp.where(
            row < 3, tile[field, 0:8, :], tile[field, kept : kept + 8, :]
        )
        packed = [jnp.zeros((8, LANES), jnp.float32)] * 2
        for block in range(EARLY // 8):
            rows = slice(8 * block, 8 * block + 8)
            sides = jnp.where(lane < 64, tile[field, rows, :LANES], tile[field, rows, LANES:])
            turned = pltpu.roll(sides, (3 + 8 * block) % LANES, 1)
            which = block // 16
            packed[which] = jnp.where(lane // 8 == block % 16, turned, packed[which])
        late[field, 8:16, :] = jnp.concatenate(packed, 1)
        late[field, 16:, :] = tile[field, EARLY:, :]


def merge(late, rest, early, tile):
    for field in range(3):
        merge_field(field, late, rest, early, tile)


def merge_field(field, late, rest, early, tile):
    row = sublanes()
    lane = lax.broadcasted_iota(jnp.int32, (8, LANES), 1)
    first = late[field, 0:8, :]
    for block in range(EARLY // 8):
        rows = slice(8 * block, 8 * block + 8)
        which = block // 16
        packed = late[field, 8:16, which * LANES : (which + 1) * LANES]
        sides = pltpu.roll(packed, (-3 - 8 * block) % LANES, 1)
        value = early[field, rows, :]
        value = jnp.concatenate(
            [
                jnp.where(lane < 3, sides, value[:, :LANES]),
                jnp.where(lane >= LANES - 3, sides, value[:, LANES:]),
            ],
            1,
        )
        if block == 0:
            value = jnp.where(row < 3, first, value)
        if block == EARLY // 8 - 1:
            value = jnp.where(row < 5, value, first)
        tile[field, rows, :] = value
    tile[field, EARLY : TILE - HALF, :] = late[field, 16:, :]
    tile[field, TILE - HALF :, :] = rest[field]


def repeat_second(
    ctl, delta0, delta1, delta2, low, high, late, rest, out, late_out, rest_out, work, tile, sems
):
    near = start_all(((late, late_out), (rest, rest_out)), sems, 2)
    repeat_steps(ctl, WET_SECOND, (delta0, delta1, delta2), (low, high), work, tile, sems)
    wait_all(start_all(((tile, out),), sems) + near)


def repeat_first(
    ctl, delta0, delta1, delta2, low, high, late_in, rest_in, staying, out,
    work, other, tile, late, rest, sems,
):
    kept = out.at[1 - ctl[MOVE + 1]]
    again = ctl[MOVE] == ctl[MOVE + 1]

    @pl.when(again)
    def _():
        wait_all(start_all(((staying, tile),), sems))

    @pl.when(jnp.logical_not(again))
    def _():
        copies = start_all(((late_in, late), (rest_in, rest)), sems, 2)
        repeat_steps(ctl, WET_FIRST, (delta0, delta1, delta2), (low, high), work, other, sems)
        wait_all(copies)
        merge(late, rest, other, tile)

    wait_all(start_all(((tile, kept),), sems))


def finish(ctl, late, rest, early, before, out, tile, sems):
    del before
    copies = []
    for field in range(3):
        merge_field(field, late, rest, early, tile)
        copies += start_all(
            ((tile.at[field], out.at[ctl[MOVE + 1], field]),), sems, field
        )
    wait_all(copies)


def second_late(ctl, arrived, own, order, leaving):
    del order
    again = ctl[MOVE] == ctl[MOVE + 1]
    for field in range(3):
        leaving[field] = jnp.where(again, arrived[field], own[field])


def correct_rows(ctl, slot, got, ground, state, rate, bottom):
    position = jnp.where(ctl[SLOT_LOW] == slot, 0, 1)
    device = lax.axis_index("xb") * 2 + lax.axis_index("yb")
    wall = WALL_WEST if bottom else WALL_EAST

    @pl.when(jnp.logical_not(flag(ctl, wall + position)))
    def _():
        peer = device - 2 if bottom else device + 2
        block = pl.ds(pl.multiple_of(peer * 8, 8), 8)
        lines = got[block, :TILE]
        grounds = ground[block, :TILE]
        stride = 4 if got.shape[1] > TILE else 3

        def line(offset):
            other = offset + stride
            picked = jnp.where(
                position == 0, lines[offset : offset + 1, :], lines[other : other + 1, :]
            )
            return jnp.broadcast_to(picked, (8, TILE))

        ghost, _ = cell(*(line(field) for field in range(3)))
        ghost_ground = jnp.where(position == 0, grounds[3:4, :], grounds[7:8, :])
        rows = slice(0, 8) if bottom else slice(TILE - 8, TILE)
        own = [state[slot, field, rows, :] for field in range(3)]
        here, _ = cell(*own)
        fluxes = face(ghost, here) if bottom else face(here, ghost)
        push = SCALE * fluxes[1] + (SLOPE * own[0]) * ghost_ground
        row = sublanes()
        sign = -1.0 if bottom else 1.0
        chosen = row == (0 if bottom else 7)
        for field, value in enumerate((SCALE * fluxes[0], push, SCALE * fluxes[2])):
            rate[slot, field, rows, :] += jnp.where(chosen, sign * value, 0.0)


def column_fix(got, ground, columns):
    upper = lax.axis_index("yb")
    device = lax.axis_index("xb") * 2 + upper
    peer = device + 1 - 2 * upper
    block = pl.ds(pl.multiple_of(peer * 8, 8), 8)
    lines = got[block, :TILE]
    ghost_ground = ground[block, :TILE][3:4]
    mine = columns[...]
    _, ghost = cell(lines[0:1], lines[1:2], lines[2:3])
    _, own = cell(mine[0:1], mine[1:2], mine[2:3])
    low = upper == 0
    left = tuple(jnp.where(low, a, b) for a, b in zip(own, ghost))
    right = tuple(jnp.where(low, b, a) for a, b in zip(own, ghost))
    fluxes = face(left, right)
    sign = jnp.where(low, 1.0, -1.0)
    push = SCALE * fluxes[1] + (SLOPE * mine[0:1]) * ghost_ground
    block8 = stacked(
        [sign * SCALE * fluxes[0], sign * SCALE * fluxes[2], sign * push],
        jnp.zeros((8, TILE), jnp.float32),
    )
    return jnp.transpose(
        jnp.concatenate([block8, jnp.zeros((LANES - 8, TILE), jnp.float32)], 0)
    )


def last_update(ctl, got, ground, columns, state, manning, rate, order, *rest):
    del order
    slots = ctl[MOVE], 1 - ctl[MOVE]
    update(STEPS - 1, ctl, got, ground, columns, state, manning, rate, *rest, slots=slots)


def update(
    step, ctl, got_in, ground_in, columns_in, state_in, manning_in, rate_in, *rest,
    passing=None, slots=(0, 1),
):
    more = step + 1 < STEPS
    fresh_out, *lines_to, delta_out = rest[: 4 if more else 6]
    rest = rest[4 if more else 6 :]
    state, manning, rate, fresh, got, ground, columns, first, second, delta_keep, sems = rest
    out, columns_out = first, second
    small = start_all(
        ((got_in, got), (ground_in, ground), (columns_in, columns)), sems, 5 * PARTS
    )
    size = 2 * TILE // PARTS
    parts = [
        (slot, slice(k * size, (k + 1) * size)) for slot in slots for k in range(PARTS // 2)
    ]
    incoming = []
    for index, (slot, rows) in enumerate(parts):
        incoming.append(
            start_all(
                (
                    (rate_in.at[slot, :, rows], rate.at[slot, :, rows]),
                    (state_in.at[slot, :, rows], state.at[slot, :, rows]),
                    (manning_in.at[slot, rows], manning.at[slot, rows]),
                ),
                sems,
                3 * index,
            )
        )
    wait_all(small)
    upper = lax.axis_index("yb")
    devices = 2 * lax.axis_size("xb")
    begin = TILE if got.shape[1] > TILE else 0
    tops = got[0:8, begin : begin + LANES]
    for peer in range(1, devices):
        tops = jnp.maximum(tops, got[peer * 8 : peer * 8 + 8, begin : begin + LANES])
    delta = (COURANT * SPACING) / tops[TOP : TOP + 1, :]
    delta = jnp.concatenate([delta, delta], 1)
    delta_keep[...] = jnp.broadcast_to(delta, (8, TILE))
    outgoing = start_all(((delta_keep, delta_out),), sems, 5 * PARTS + 3)
    fix = column_fix(got, ground, columns)
    facing = jnp.where(upper > 0, ctl[SLOT_LOW], 1 - ctl[SLOT_LOW])
    begin = pl.multiple_of((1 - upper) * LANES, LANES)
    goal = (1 - upper) * (LANES - 1)
    lane = lax.broadcasted_iota(jnp.int32, (size, LANES), 1)
    total = jnp.zeros((ROWS, TILE), jnp.float32)
    for index, (slot, part_rows) in enumerate(parts):
        wait_all(incoming[index])
        if part_rows.start == 0:
            correct_rows(ctl, slot, got, ground, state, rate, True)
        if part_rows.stop == TILE:
            correct_rows(ctl, slot, got, ground, state, rate, False)

        @pl.when(facing == slot)
        def _(slot=slot, part_rows=part_rows):
            for field in range(3):
                turned = pltpu.roll(
                    fix[part_rows], lax.rem(goal + LANES - field, LANES), 1
                )
                rate[slot, field, part_rows, pl.ds(begin, LANES)] += jnp.where(
                    lane == goal, turned, 0.0
                )

        wet_now = flag(ctl, WET + 2 * step + slot)

        def group(index, best, slot=slot, wet_now=wet_now):
            rows = pl.ds(pl.multiple_of(index * ROWS, ROWS), ROWS)
            old = tuple(state[slot, field, rows, :] for field in range(3))
            slopes = tuple(rate[slot, field, rows, :] for field in range(3))
            h, hu, hv = moved_on(old, slopes, manning[slot, rows, :], delta, wet_now)
            fresh[slot, 0, rows, :] = h
            fresh[slot, 1, rows, :] = hu
            fresh[slot, 2, rows, :] = hv
            if more:
                along_x, along_y = cell(h, hu, hv)
                best = jnp.maximum(best, jnp.maximum(along_x[5], along_y[5]))
            return best

        best = lax.fori_loop(
            part_rows.start // ROWS,
            part_rows.stop // ROWS,
            group,
            jnp.zeros((ROWS, TILE), jnp.float32),
        )
        if more:
            best = jnp.where(flag(ctl, WET + 2 * step + 2 + slot), best, 0.0)
            total = jnp.maximum(total, best)
        if more:
            outgoing += start_all(
                ((fresh.at[slot, :, part_rows], fresh_out.at[slot, :, part_rows]),),
                sems,
                3 * PARTS + index,
            )
        elif index >= PARTS // 2:
            outgoing += start_all(
                ((fresh.at[slot, :, part_rows], fresh_out.at[:, part_rows]),),
                sems,
                3 * PARTS + index,
            )
        if not more and part_rows.stop == TILE:
            late, low, high = (
                (first, *lines_to[:2]) if index < PARTS // 2 else (second, *lines_to[2:])
            )
            late_rows(fresh.at[slot], late)
            outgoing += start_all(
                ((late.at[:, :HALF], low), (late.at[:, HALF:], high)),
                sems,
                4 * PARTS + (0 if index < PARTS // 2 else 2),
            )
        if passing and index == PARTS // 2:
            passing.middle()
    if more:
        messages(ctl, fresh, None, jnp.max(total, keepdims=True), out, columns_out)
        pairs = zip((out, columns_out), lines_to)
        outgoing += start_all(tuple(pairs), sems, 4 * PARTS)
    wait_all(outgoing)


def vmem():
    return pl.BlockSpec(memory_space=pltpu.VMEM)


def smem():
    return pl.BlockSpec(memory_space=pltpu.SMEM)


def hbm():
    return pl.BlockSpec(memory_space=pltpu.HBM)


def anywhere():
    return pl.BlockSpec(memory_space=pl.ANY)


def call(
    kernel, outs, out_specs, in_specs, flops, scratch=(), aliases=None, room=VMEM_BYTES, moved=4
):
    return pl.pallas_call(
        kernel,
        scratch_shapes=scratch,
        input_output_aliases=aliases or {},
        out_shape=outs,
        in_specs=in_specs,
        out_specs=out_specs,
        compiler_params=pltpu.CompilerParams(vmem_limit_bytes=room),
        cost_estimate=pl.CostEstimate(flops=flops, bytes_accessed=moved << 20, transcendentals=0),
    )


def f32(*shape):
    return jax.ShapeDtypeStruct(shape, jnp.float32)


def spread(fast):
    return lax.all_to_all(fast, ("xb", "yb"), split_axis=0, concat_axis=0, tiled=True)


def body(state, bed, manning, neighbours, wet, moves):
    shape = f32(*state.shape)
    devices = lax.axis_size("xb") * lax.axis_size("yb")
    whole = pltpu.VMEM(state.shape, jnp.float32)
    part = pltpu.VMEM(bed.shape, jnp.float32)
    tile_shape = f32(*state.shape[1:])
    early_shape = f32(5, EARLY, TILE)
    early_state = f32(3, EARLY, TILE)
    late_shape = f32(3, LATE, TILE)
    half_shape = f32(3, HALF, TILE)
    delta_shape = f32(8, TILE)

    def buffer(like):
        return pltpu.VMEM(like.shape, jnp.float32)

    piece_shapes = tuple(f32(5, end - begin, TILE) for begin, end in PIECES)
    out, columns, ctl = call(
        opening,
        (
            f32(8 * devices, TILE + LANES),
            f32(8, TILE),
            jax.ShapeDtypeStruct((CONTROLS,), jnp.int32),
        ),
        (vmem(), vmem(), smem()),
        [hbm()] * 5,
        4 << 20,
        [
            whole,
            part,
            pltpu.SMEM(neighbours.shape[::-1], jnp.int32),
            pltpu.SMEM(wet.shape, jnp.int32),
            pltpu.SMEM(moves.shape, jnp.int32),
            pltpu.SemaphoreType.DMA((6,)),
        ],
    )(state, bed, neighbours.T, wet, moves)
    state_first = state
    ground = None
    deltas = []
    for step in range(STEPS):
        got = spread(out)
        ground = got if step == 0 else ground
        scratch = [whole, part, whole, pltpu.SemaphoreType.DMA((3 * CHUNKS,))]
        piece_scratch = [
            [buffer(piece), pltpu.SemaphoreType.DMA((2,))] for piece in piece_shapes
        ]
        if step == 1:
            rate, leaving = call(
                rates_and_leaving,
                (shape, piece_shapes[0]),
                (hbm(),) * 2,
                [smem()] + [hbm()] * 5,
                16 << 20,
                scratch + piece_scratch[0],
            )(ctl, state, bed, state_first, manning, early_first[0])
            early_second = [shifted(leaving, "xb", 1)]
        elif step == 2:
            rate = call(rates_after, shape, hbm(), [smem()] + [hbm()] * 3, 16 << 20, scratch)(
                ctl, state, bed, early_second[0]
            )
        else:
            rate, *leaving = call(
                rates_and_splitting,
                (shape,) + piece_shapes,
                (hbm(),) * 3,
                [smem()] + [hbm()] * 3,
                16 << 20,
                scratch + [buffer(early_shape), pltpu.SemaphoreType.DMA((5,))],
            )(ctl, state, bed, manning)
            held = call(
                hold, piece_shapes[0], hbm(), [hbm()] * 3, 1 << 10, aliases={2: 0}
            )(rate, got, leaving[0])
            early_first = [shifted(held, "xb", 1)]
        more = step + 1 < STEPS
        shapes = (f32(8 * devices, TILE), f32(8, TILE)) if more else (half_shape,) * 4
        passing = step == 1
        work = [
            whole,
            part,
            whole,
            whole,
            pltpu.VMEM(got.shape, jnp.float32),
            pltpu.VMEM(ground.shape, jnp.float32),
            pltpu.VMEM((8, TILE), jnp.float32),
            buffer(shapes[0] if more else late_shape),
            buffer(shapes[1] if more else late_shape),
            buffer(delta_shape),
            pltpu.SemaphoreType.DMA((5 * PARTS + 4,)),
        ]
        operands = ctl, got, ground, columns, state, manning, rate
        if not more:
            break
        outs = call(
            functools.partial(update_and_leaving if passing else update, step),
            (shape,) + shapes + (delta_shape,) + ((piece_shapes[1],) if passing else ()),
            (hbm(),) * (5 if passing else 4),
            [smem()] + [hbm()] * (9 if passing else 6),
            8 << 20,
            work + (piece_scratch[1] if passing else []),
            moved=10,
        )(*operands, *((state_first, bed, early_first[1]) if passing else ()))
        state, out, columns, delta, *passed = outs
        deltas.append(delta)
        if step == 0:
            held = call(
                hold, piece_shapes[1], hbm(), [hbm()] * 3, 1 << 10, aliases={2: 0}
            )(delta, delta, leaving[1])
            early_first.append(shifted(held, "xb", 1))
        elif step == 1:
            early_second.append(shifted(passed[0], "xb", 1))

    staying, late_first, rest_first, late_second, rest_second, delta = call(
        last_update,
        (tile_shape,) + shapes + (delta_shape,),
        (hbm(),) * 6,
        [smem()] + [hbm()] * 7,
        8 << 20,
        work,
        moved=10,
    )(*operands, early_second[1])
    deltas.append(delta)
    room = 16 << 20
    late_arrived = shifted(late_first, "xb", 1)
    rest_arrived = shifted(rest_first, "xb", 1)
    second, late_second, rest_second = call(
        repeat_second,
        (early_state, half_shape, half_shape),
        (anywhere(), vmem(), vmem()),
        [smem()] + [vmem()] * 3 + [anywhere()] * 4,
        8 << 20,
        [buffer(early_shape), buffer(early_state), pltpu.SemaphoreType.DMA((4,))],
        room=room,
    )(ctl, *deltas, *early_second, late_second, rest_second)

    def pass_late(arrived, own):
        leaving = call(
            second_late,
            half_shape,
            vmem(),
            [smem(), vmem(), vmem(), anywhere()],
            1 << 10,
            room=room,
        )(ctl, arrived, own, second)
        return shifted(leaving, "xb", 1)

    late_next = pass_late(late_arrived, late_second)
    rest_next = pass_late(rest_arrived, rest_second)
    final = call(
        repeat_first,
        shape,
        hbm(),
        [smem()] + [vmem()] * 3 + [anywhere()] * 5,
        8 << 20,
        [
            buffer(early_shape),
            buffer(early_state),
            buffer(tile_shape),
            buffer(half_shape),
            buffer(half_shape),
            pltpu.SemaphoreType.DMA((4,)),
        ],
        room=room,
    )(ctl, *deltas, *early_first, late_arrived, rest_arrived, staying)
    return call(
        finish,
        shape,
        hbm(),
        [smem(), vmem(), vmem(), vmem(), hbm()],
        1 << 20,
        [buffer(tile_shape), pltpu.SemaphoreType.DMA((3,))],
        {4: 0},
        room=room,
    )(ctl, late_next, rest_next, second, final)


def solution(mesh):
    placed = (
        P(("runs", "xb", "yb"), None, None, None),
        P(("runs", "xb", "yb"), None, None),
        P(("runs", "xb", "yb"), None, None),
        P("runs", None),
        P(None, "runs"),
        P(None, "runs"),
    )
    return jax.shard_map(
        body,
        mesh=mesh,
        in_specs=placed,
        out_specs=P(("runs", "xb", "yb"), None, None, None),
        check_vma=False,
    )
```

```python
import functools

import jax
import jax.numpy as jnp
from jax import lax
from jax.experimental import pallas as pl
from jax.experimental.pallas import tpu as pltpu
from jax.sharding import PartitionSpec as P

STEPS = 3
GRAVITY = 9.81
ROOT_G = GRAVITY**0.5
SPACING = 5.0
COURANT = 0.2
ROWS = 32
LANES = 128
TILE = 256
VMEM_BYTES = 60 * 1024 * 1024
SLOT_LOW, WALL_WEST, WALL_EAST, WALL_OUTER, WET, MOVE = 0, 1, 3, 5, 7, 13
WET_FIRST, WET_SECOND = 16, 19
CONTROLS = 24
EARLY = 144
PIECES = ((0, 72), (72, 144))
AGAIN = 48
LATE = TILE - EARLY + 16
HALF = LATE // 2
CHUNKS = 8
PARTS = 4
STRIP = 32
TOP = 6
SCALE = 0.5 / SPACING
SLOPE = GRAVITY / (2.0 * SPACING)


def shifted(value, axis, steps, around=True):
    count = lax.axis_size(axis)
    pairs = [(source, (source + steps) % count) for source in range(count)]
    if not around:
        pairs = [pair for pair in pairs if abs(pair[0] - pair[1]) == abs(steps)]
    return lax.ppermute(value, axis, pairs)


def cell(h, hu, hv):
    root = lax.rsqrt(h)
    inverse = root * root
    u = hu * inverse
    v = hv * inverse
    celerity = ROOT_G * (h * root)
    pressure = (0.5 * GRAVITY) * (h * h)
    cross = hu * v
    speed_x = jnp.abs(u) + celerity
    speed_y = jnp.abs(v) + celerity
    along_x = (h, hu, hv, hu * u + pressure, cross, speed_x)
    along_y = (h, hv, hu, hv * v + pressure, cross, speed_y)
    return along_x, along_y


def face(left, right):
    wave = jnp.maximum(left[5], right[5])
    return (
        (left[1] + right[1]) - wave * (right[0] - left[0]),
        (left[3] + right[3]) - wave * (right[1] - left[1]),
        (left[4] + right[4]) - wave * (right[2] - left[2]),
    )


def slot_of(ctl, position):
    low = ctl[SLOT_LOW]
    return low if position == 0 else 1 - low


def flag(ctl, index):
    return ctl[index] > 0


def start_all(pairs, sems, first=0):
    copies = [
        pltpu.make_async_copy(src, dst, sems.at[first + k]) for k, (src, dst) in enumerate(pairs)
    ]
    for copy in copies:
        copy.start()
    return copies


def wait_all(copies):
    for copy in copies:
        copy.wait()


def sublanes(width=TILE):
    return lax.broadcasted_iota(jnp.int32, (8, width), 0)


def stacked(lines, base):
    row = sublanes()
    for index, line in enumerate(lines):
        base = jnp.where(row == index, jnp.broadcast_to(line, (8, TILE)), base)
    return base


def messages(ctl, state, bed, fastest, out, columns):
    upper = lax.axis_index("yb")
    column = lax.axis_index("xb")
    last = lax.axis_size("xb") - 1
    devices = 2 * (last + 1)
    device = column * 2 + upper
    top = jnp.broadcast_to(fastest, (8, TILE))
    for peer in range(devices):
        out[peer * 8 : peer * 8 + 8, :TILE] = top
        if bed is not None:
            out[peer * 8 : peer * 8 + 8, TILE:] = top[:, :LANES]
    row = sublanes()

    def edge(line):
        rows = slice(line, line + 1)
        lines = []
        for position in range(2):
            slot = slot_of(ctl, position)
            lines += [state[slot, field, rows, :] for field in range(3)]
            if bed is not None:
                lines.append(bed[slot, rows, :])
        return stacked(lines, top)

    for inside, peer, line in (
        (column > 0, device - 2, 0),
        (column < last, device + 2, TILE - 1),
    ):

        @pl.when(inside)
        def _(peer=peer, line=line):
            out[pl.ds(pl.multiple_of(peer * 8, 8), 8), :TILE] = edge(line)

    slot = jnp.where(upper > 0, ctl[SLOT_LOW], 1 - ctl[SLOT_LOW])
    begin = pl.multiple_of((1 - upper) * LANES, LANES)
    lane = lax.broadcasted_iota(jnp.int32, (TILE, LANES), 1)
    packed = None
    for field in range(4 if bed is not None else 3):
        if field < 3:
            part = state[slot, field, :, pl.ds(begin, LANES)]
        else:
            part = bed[slot, :, pl.ds(begin, LANES)]
        turned = pltpu.roll(part, field + 1 - upper, 1)
        packed = turned if field == 0 else jnp.where(lane == field, turned, packed)
    lines = jnp.transpose(packed)[:8]
    columns[...] = lines
    start = pl.multiple_of((device + 1 - 2 * upper) * 8, 8)
    out[pl.ds(start, 8), :TILE] = jnp.where(row == TOP, top, lines)


def opening(
    state_in, bed_in, neighbours_in, wet_in, moves_in,
    out, columns, ctl,
    state, bed, neighbours, wet, moves, sems,
):
    copies = start_all(
        (
            (neighbours_in, neighbours),
            (wet_in, wet),
            (moves_in, moves),
            (state_in.at[0], state.at[0]),
            (state_in.at[1], state.at[1]),
            (bed_in, bed),
        ),
        sems,
    )
    device = lax.axis_index("xb") * 2 + lax.axis_index("yb")
    wait_all(copies[:3])
    first = device * 2
    low = jnp.where(neighbours[3, first] == first + 1, 0, 1)
    ctl[SLOT_LOW] = low
    for position in range(2):
        slot = low if position == 0 else 1 - low
        tile = first + slot
        ctl[WALL_WEST + position] = (neighbours[0, tile] < 0).astype(jnp.int32)
        ctl[WALL_EAST + position] = (neighbours[1, tile] < 0).astype(jnp.int32)
        ctl[WALL_OUTER + position] = (neighbours[2 + position, tile] < 0).astype(jnp.int32)
    for step in range(STEPS):
        for slot in range(2):
            ctl[WET + 2 * step + slot] = wet[step, first + slot]
        ctl[MOVE + step] = moves[step, device]
    count = lax.axis_size("xb")
    upper = lax.axis_index("yb")
    column = lax.axis_index("xb")
    source = lax.rem(column + count - 1, count) * 2 + upper
    before = lax.rem(column + count - 2, count) * 2 + upper
    again = moves[0, source] == moves[1, source]
    tile_first = source * 2 + moves[0, source]
    tile_second = jnp.where(
        again, before * 2 + moves[0, before], source * 2 + 1 - moves[0, source]
    )
    for step in range(STEPS):
        ctl[WET_FIRST + step] = wet[step, tile_first]
        ctl[WET_SECOND + step] = wet[step, tile_second]

    total = jnp.zeros((ROWS, TILE), jnp.float32)
    for slot in range(2):
        copies[3 + slot].wait()

        def group(index, best, slot=slot):
            rows = pl.ds(pl.multiple_of(index * ROWS, ROWS), ROWS)
            along_x, along_y = cell(*(state[slot, field, rows, :] for field in range(3)))
            return jnp.maximum(best, jnp.maximum(along_x[5], along_y[5]))

        best = lax.fori_loop(0, TILE // ROWS, group, jnp.zeros((ROWS, TILE), jnp.float32))
        total = jnp.maximum(total, jnp.where(wet[0, first + slot] > 0, best, 0.0))
    copies[5].wait()
    messages(ctl, state, bed, jnp.max(total, keepdims=True), out, columns)


def hold(first, second, leaving, same):
    del first, second, leaving, same


class Splitting:
    def __init__(self, ctl, state_in, bed_in, manning_in, leaving, buffer, sems):
        slot = ctl[MOVE]
        rows = slice(0, EARLY)
        pairs = (
            (state_in.at[slot, :, rows], buffer.at[0:3]),
            (bed_in.at[slot, rows], buffer.at[3]),
            (manning_in.at[slot, rows], buffer.at[4]),
        )
        self.incoming = [
            pltpu.make_async_copy(src, dst, sems.at[k]) for k, (src, dst) in enumerate(pairs)
        ]
        self.outgoing = [
            pltpu.make_async_copy(buffer.at[:, begin:end], piece, sems.at[3 + k])
            for k, ((begin, end), piece) in enumerate(zip(PIECES, leaving))
        ]

    def start(self):
        for copy in self.incoming:
            copy.start()

    def middle(self):
        wait_all(self.incoming)
        for copy in self.outgoing:
            copy.start()

    def end(self):
        wait_all(self.outgoing)


class Passing:
    def __init__(self, ctl, piece, state_in, bed_in, manning_in, arrived, leaving, buffer, sems):
        self.again = ctl[MOVE] == ctl[MOVE + 1]
        self.other = 1 - ctl[MOVE]
        self.rows = slice(*piece)
        self.refs = state_in, bed_in, manning_in
        self.incoming = pltpu.make_async_copy(arrived, buffer, sems.at[0])
        self.outgoing = pltpu.make_async_copy(buffer, leaving, sems.at[1])
        self.buffer = buffer
        self.sem = sems.at[0]

    def start(self):
        state_in, bed_in, manning_in = self.refs
        buffer, sem, rows = self.buffer, self.sem, self.rows

        @pl.when(self.again)
        def _():
            self.incoming.start()

        @pl.when(jnp.logical_not(self.again))
        def _():
            pltpu.make_async_copy(state_in.at[self.other, :, rows], buffer.at[0:3], sem).start()
            pltpu.make_async_copy(bed_in.at[self.other, rows], buffer.at[3], sem).start()
            pltpu.make_async_copy(manning_in.at[self.other, rows], buffer.at[4], sem).start()

    def middle(self):
        self.incoming.wait()
        self.outgoing.start()

    def end(self):
        self.outgoing.wait()


def rates_and_splitting(
    ctl, state_in, bed_in, manning_in, rate_out, leaving_low, leaving_high,
    state, bed, rate, sems, buffer, moving,
):
    leaving = leaving_low, leaving_high
    splitting = Splitting(ctl, state_in, bed_in, manning_in, leaving, buffer, moving)
    rates(ctl, state_in, bed_in, rate_out, state, bed, rate, sems, splitting)


def rates_and_leaving(
    ctl, state_in, bed_in, state_first, manning_in, arrived, rate_out, leaving,
    state, bed, rate, sems, buffer, moving,
):
    passing = Passing(
        ctl, PIECES[0], state_first, bed_in, manning_in, arrived, leaving, buffer, moving
    )
    rates(ctl, state_in, bed_in, rate_out, state, bed, rate, sems, passing)


def update_and_leaving(
    step, ctl, got_in, ground_in, columns_in, state_in, manning_in, rate_in,
    state_first, bed_in, arrived, fresh_out, first_out, second_out, delta_out, leaving, *rest
):
    *rest, buffer, moving = rest
    passing = Passing(
        ctl, PIECES[1], state_first, bed_in, manning_in, arrived, leaving, buffer, moving
    )
    passing.start()
    update(
        step, ctl, got_in, ground_in, columns_in, state_in, manning_in, rate_in,
        fresh_out, first_out, second_out, delta_out, *rest, passing=passing,
    )
    passing.end()


def rates_after(ctl, state_in, bed_in, order, *rest):
    del order
    rates(ctl, state_in, bed_in, *rest)


def rates(ctl, state_in, bed_in, rate_out, state, bed, rate, sems, passing=None):
    width = 2 * TILE
    row_ids = lax.broadcasted_iota(jnp.int32, (STRIP, width), 0)
    row8 = sublanes(width)
    lane = lax.broadcasted_iota(jnp.int32, (STRIP, LANES), 1)
    last = TILE // STRIP - 1
    chunk = TILE // CHUNKS
    slots = [slot_of(ctl, position) for position in range(2)]
    incoming = []
    for part in range(CHUNKS):
        rows = slice(part * chunk, (part + 1) * chunk)
        incoming.append(
            start_all(
                (
                    (state_in.at[:, :, rows], state.at[:, :, rows]),
                    (bed_in.at[:, rows], bed.at[:, rows]),
                ),
                sems,
                2 * part,
            )
        )
    if passing:
        passing.start()
    keep_west, keep_east, keep_south, keep_north = (
        jnp.where(flag(ctl, index), 1.0, 0.0)
        for index in (WALL_WEST, WALL_EAST, WALL_OUTER, WALL_OUTER + 1)
    )

    def strip(field, rows):
        if field == 3:
            return jnp.concatenate([bed[slot, rows, :] for slot in slots], 1)
        return jnp.concatenate([state[slot, field, rows, :] for slot in slots], 1)

    def blocks(value):
        return [value[:, k * LANES : (k + 1) * LANES] for k in range(4)]

    def right_of(value, end=None):
        turned = [pltpu.roll(part, LANES - 1, 1) for part in blocks(value)]
        after = turned[1:] + [turned[3] if end is None else end]
        return jnp.concatenate(
            [
                jnp.where(lane == LANES - 1, following, part)
                if following is not part
                else part
                for part, following in zip(turned, after)
            ],
            1,
        )

    def left_of(value, end):
        turned = [pltpu.roll(part, 1, 1) for part in blocks(value)]
        before = [end] + turned[:3]
        return jnp.concatenate(
            [jnp.where(lane == 0, previous, part) for part, previous in zip(turned, before)], 1
        )

    def down(value):
        return pltpu.roll(value, STRIP + 7, 0)[:STRIP]

    def group(index, carry):
        base = pl.multiple_of(index * STRIP, STRIP)
        rows = pl.ds(base, STRIP)
        after = pl.ds(pl.multiple_of(jnp.minimum(base + STRIP, TILE - 8), 8), 8)
        at_end = index == last
        fields = [
            jnp.concatenate([strip(field, rows), strip(field, after)], 0) for field in range(3)
        ]
        cells_x, cells_y = cell(*fields)
        here_x = tuple(value[:STRIP] for value in cells_x)
        here_y = tuple(value[:STRIP] for value in cells_y)

        ending = jnp.logical_and(row8 == 7, at_end)
        faces = list(face(here_x, tuple(down(value) for value in cells_x)))
        wall = keep_east * (2.0 * (here_x[3] + here_x[5] * here_x[1])[STRIP - 8 :])
        for component, value in enumerate((0.0, wall, 0.0)):
            upper = faces[component]
            faces[component] = jnp.concatenate(
                [upper[: STRIP - 8], jnp.where(ending, value, upper[STRIP - 8 :])], 0
            )
        turned = tuple(pltpu.roll(value, 1, 0) for value in faces)
        change_x = tuple(
            value - jnp.where(row_ids == 0, before, moved)
            for value, before, moved in zip(faces, carry[:3], turned)
        )
        ground = strip(3, rows)
        ground_after = jnp.where(
            at_end,
            jnp.broadcast_to(keep_east * ground[STRIP - 1 :], (8, width)),
            strip(3, after),
        )
        ground_up = pltpu.roll(ground, 1, 0)
        slope_x = down(jnp.concatenate([ground, ground_after], 0)) - jnp.where(
            row_ids == 0, carry[3], ground_up
        )
        carried = tuple(value[0:1, :] for value in turned) + (ground_up[0:1, :],)

        faces_y = list(face(here_y, tuple(right_of(value) for value in here_y)))
        normal = here_y[3]
        spread_y = here_y[5] * here_y[1]
        north = keep_north * (2.0 * (normal + spread_y)[:, width - LANES :])
        south = keep_south * (2.0 * (normal - spread_y)[:, :LANES])
        change_y = []
        for component, (high, low) in enumerate(((0.0, 0.0), (north, south), (0.0, 0.0))):
            parts = blocks(faces_y[component])
            parts[3] = jnp.where(lane == LANES - 1, high, parts[3])
            value = jnp.concatenate(parts, 1)
            change_y.append(value - left_of(value, low))
        slope_y = right_of(ground, keep_north * ground[:, width - LANES :]) - left_of(
            ground, keep_south * ground[:, :LANES]
        )
        weight = SLOPE * here_x[0]
        results = (
            SCALE * (change_x[0] + change_y[0]),
            SCALE * (change_x[1] + change_y[2]) + weight * slope_x,
            SCALE * (change_x[2] + change_y[1]) + weight * slope_y,
        )
        for field, value in enumerate(results):
            for position, slot in enumerate(slots):
                rate[slot, field, rows, :] = value[:, position * TILE : (position + 1) * TILE]
        return carried

    wait_all(incoming[0])
    top, _ = cell(*(strip(field, slice(0, 8)) for field in range(3)))
    nothing = jnp.zeros((1, width), jnp.float32)
    carry = (
        nothing,
        keep_west * (2.0 * (top[3] - top[5] * top[1])[0:1]),
        nothing,
        keep_west * strip(3, slice(0, 8))[0:1],
    )
    per_chunk = chunk // STRIP
    outgoing = []
    for part in range(CHUNKS):
        if part + 1 < CHUNKS:
            wait_all(incoming[part + 1])
        carry = lax.fori_loop(part * per_chunk, (part + 1) * per_chunk, group, carry)
        rows = slice(part * chunk, (part + 1) * chunk)
        outgoing += start_all(
            ((rate.at[:, :, rows], rate_out.at[:, :, rows]),), sems, 2 * CHUNKS + part
        )
        if passing and part == CHUNKS // 2:
            passing.middle()
    wait_all(outgoing)
    if passing:
        passing.end()


def moved_on(old, slopes, rough, delta, wet_now):
    h, hu, hv = (value - delta * slope for value, slope in zip(old, slopes))
    inverse = 1.0 / h
    u = hu * inverse
    v = hv * inverse
    speed = jnp.sqrt(u * u + v * v)
    power = jnp.exp((-4.0 / 3.0) * jnp.log(jnp.abs(h)))
    drag = (GRAVITY * delta) * (rough * rough) * (speed * power)
    factor = 1.0 / (1.0 + drag)
    fresh = (h, hu * factor, hv * factor)
    return tuple(jnp.where(wet_now, new, value) for new, value in zip(fresh, old))


def repeat_steps(ctl, wet_from, deltas, early, work, other, sems):
    incoming = []
    for ref in early:
        begin = 0 if ref is early[0] else early[0].shape[1]
        incoming += start_all(
            ((ref, work.at[:, begin : begin + ref.shape[1]]),), sems, len(incoming)
        )
    row_ids = lax.broadcasted_iota(jnp.int32, (AGAIN, TILE), 0)
    lane = lax.broadcasted_iota(jnp.int32, (AGAIN, LANES), 1)
    start = tuple(jnp.zeros((1, TILE), jnp.float32) for _ in range(4))

    def halves(value):
        return value[:, :LANES], value[:, LANES:]

    def right_of(value):
        low, high = (pltpu.roll(part, LANES - 1, 1) for part in halves(value))
        return jnp.concatenate([jnp.where(lane == LANES - 1, high, low), high], 1)

    def left_of(value):
        low, high = (pltpu.roll(part, 1, 1) for part in halves(value))
        return jnp.concatenate([low, jnp.where(lane == 0, low, high)], 1)

    def down(value):
        return pltpu.roll(value, AGAIN + 7, 0)[:AGAIN]

    for step in range(STEPS):
        source, target = (work, other) if step % 2 == 0 else (other, work)
        delta = deltas[step][0:1, :]
        wet_now = flag(ctl, wet_from + step)

        def group(index, carry, source=source, target=target, delta=delta, wet_now=wet_now):
            base = pl.multiple_of(index * AGAIN, AGAIN)
            rows = pl.ds(base, AGAIN)
            after = pl.ds(pl.multiple_of(jnp.minimum(base + AGAIN, EARLY - 8), 8), 8)
            refs = [source.at[field] for field in range(3)] + [work.at[3]]
            fields = [jnp.concatenate([ref[rows, :], ref[after, :]], 0) for ref in refs]
            cells_x, cells_y = cell(*fields[:3])
            here_x = tuple(value[:AGAIN] for value in cells_x)
            here_y = tuple(value[:AGAIN] for value in cells_y)
            faces_x = face(here_x, tuple(down(value) for value in cells_x))
            turned = tuple(pltpu.roll(value, 1, 0) for value in faces_x)
            change_x = tuple(
                value - jnp.where(row_ids == 0, before, moved)
                for value, before, moved in zip(faces_x, carry[:3], turned)
            )
            ground = fields[3][:AGAIN]
            ground_up = pltpu.roll(ground, 1, 0)
            slope_x = down(fields[3]) - jnp.where(row_ids == 0, carry[3], ground_up)
            carried = tuple(value[0:1, :] for value in turned) + (ground_up[0:1, :],)
            faces_y = face(here_y, tuple(right_of(value) for value in here_y))
            change_y = tuple(value - left_of(value) for value in faces_y)
            slope_y = right_of(ground) - left_of(ground)
            old = tuple(value[:AGAIN] for value in fields[:3])
            weight = SLOPE * old[0]
            slopes = (
                SCALE * (change_x[0] + change_y[0]),
                SCALE * (change_x[1] + change_y[2]) + weight * slope_x,
                SCALE * (change_x[2] + change_y[1]) + weight * slope_y,
            )
            for field, value in enumerate(
                moved_on(old, slopes, work[4, rows, :], delta, wet_now)
            ):
                target[field, rows, :] = value
            return carried

        if step == 0:
            wait_all(incoming)
        lax.fori_loop(0, EARLY // AGAIN, group, start)


def late_rows(tile, late):
    row = sublanes()
    kept = EARLY - 8
    lane = lax.broadcasted_iota(jnp.int32, (8, LANES), 1)
    for field in range(3):
        late[field, 0:8, :] = jnp.where(
            row < 3, tile[field, 0:8, :], tile[field, kept : kept + 8, :]
        )
        packed = [jnp.zeros((8, LANES), jnp.float32)] * 2
        for block in range(EARLY // 8):
            rows = slice(8 * block, 8 * block + 8)
            sides = jnp.where(lane < 64, tile[field, rows, :LANES], tile[field, rows, LANES:])
            turned = pltpu.roll(sides, (3 + 8 * block) % LANES, 1)
            which = block // 16
            packed[which] = jnp.where(lane // 8 == block % 16, turned, packed[which])
        late[field, 8:16, :] = jnp.concatenate(packed, 1)
        late[field, 16:, :] = tile[field, EARLY:, :]


def merge(late, rest, early, tile):
    for field in range(3):
        merge_field(field, late, rest, early, tile)


def merge_field(field, late, rest, early, tile):
    row = sublanes()
    lane = lax.broadcasted_iota(jnp.int32, (8, LANES), 1)
    first = late[field, 0:8, :]
    for block in range(EARLY // 8):
        rows = slice(8 * block, 8 * block + 8)
        which = block // 16
        packed = late[field, 8:16, which * LANES : (which + 1) * LANES]
        sides = pltpu.roll(packed, (-3 - 8 * block) % LANES, 1)
        value = early[field, rows, :]
        value = jnp.concatenate(
            [
                jnp.where(lane < 3, sides, value[:, :LANES]),
                jnp.where(lane >= LANES - 3, sides, value[:, LANES:]),
            ],
            1,
        )
        if block == 0:
            value = jnp.where(row < 3, first, value)
        if block == EARLY // 8 - 1:
            value = jnp.where(row < 5, value, first)
        tile[field, rows, :] = value
    tile[field, EARLY : TILE - HALF, :] = late[field, 16:, :]
    if rest is not None:
        tile[field, TILE - HALF :, :] = rest[field]


def repeat_second(
    ctl, delta0, delta1, delta2, low, high, late, rest, out, late_out, rest_out, work, tile, sems
):
    near = start_all(((late, late_out), (rest, rest_out)), sems, 2)
    repeat_steps(ctl, WET_SECOND, (delta0, delta1, delta2), (low, high), work, tile, sems)
    wait_all(start_all(((tile, out),), sems) + near)


def repeat_first(
    ctl, delta0, delta1, delta2, low, high, late_in, rest_in, staying, out,
    work, other, tile, late, rest, sems,
):
    kept = out.at[1 - ctl[MOVE + 1]]
    again = ctl[MOVE] == ctl[MOVE + 1]

    @pl.when(again)
    def _():
        wait_all(start_all(((staying, tile),), sems))

    @pl.when(jnp.logical_not(again))
    def _():
        copies = start_all(((late_in, late), (rest_in, rest)), sems, 2)
        repeat_steps(ctl, WET_FIRST, (delta0, delta1, delta2), (low, high), work, other, sems)
        wait_all(copies)
        merge(late, rest, other, tile)

    wait_all(start_all(((tile, kept),), sems))


def finish_late(ctl, late, early, before, out, tile, sems):
    del before
    copies = []
    for field in range(3):
        merge_field(field, late, None, early, tile)
        copies += start_all(
            ((tile.at[field], out.at[ctl[MOVE + 1], field, 0 : TILE - HALF]),), sems, field
        )
    wait_all(copies)


def finish_rest(ctl, rest, before, out, sems):
    del before
    wait_all(start_all(((rest, out.at[ctl[MOVE + 1], :, TILE - HALF :]),), sems))


def second_late(ctl, arrived, own, order, leaving):
    del order
    again = ctl[MOVE] == ctl[MOVE + 1]
    for field in range(3):
        leaving[field] = jnp.where(again, arrived[field], own[field])


def correct_rows(ctl, slot, got, ground, state, rate, bottom):
    position = jnp.where(ctl[SLOT_LOW] == slot, 0, 1)
    device = lax.axis_index("xb") * 2 + lax.axis_index("yb")
    wall = WALL_WEST if bottom else WALL_EAST

    @pl.when(jnp.logical_not(flag(ctl, wall + position)))
    def _():
        peer = device - 2 if bottom else device + 2
        block = pl.ds(pl.multiple_of(peer * 8, 8), 8)
        lines = got[block, :TILE]
        grounds = ground[block, :TILE]
        stride = 4 if got.shape[1] > TILE else 3

        def line(offset):
            other = offset + stride
            picked = jnp.where(
                position == 0, lines[offset : offset + 1, :], lines[other : other + 1, :]
            )
            return jnp.broadcast_to(picked, (8, TILE))

        ghost, _ = cell(*(line(field) for field in range(3)))
        ghost_ground = jnp.where(position == 0, grounds[3:4, :], grounds[7:8, :])
        rows = slice(0, 8) if bottom else slice(TILE - 8, TILE)
        own = [state[slot, field, rows, :] for field in range(3)]
        here, _ = cell(*own)
        fluxes = face(ghost, here) if bottom else face(here, ghost)
        push = SCALE * fluxes[1] + (SLOPE * own[0]) * ghost_ground
        row = sublanes()
        sign = -1.0 if bottom else 1.0
        chosen = row == (0 if bottom else 7)
        for field, value in enumerate((SCALE * fluxes[0], push, SCALE * fluxes[2])):
            rate[slot, field, rows, :] += jnp.where(chosen, sign * value, 0.0)


def column_fix(got, ground, columns):
    upper = lax.axis_index("yb")
    device = lax.axis_index("xb") * 2 + upper
    peer = device + 1 - 2 * upper
    block = pl.ds(pl.multiple_of(peer * 8, 8), 8)
    lines = got[block, :TILE]
    ghost_ground = ground[block, :TILE][3:4]
    mine = columns[...]
    _, ghost = cell(lines[0:1], lines[1:2], lines[2:3])
    _, own = cell(mine[0:1], mine[1:2], mine[2:3])
    low = upper == 0
    left = tuple(jnp.where(low, a, b) for a, b in zip(own, ghost))
    right = tuple(jnp.where(low, b, a) for a, b in zip(own, ghost))
    fluxes = face(left, right)
    sign = jnp.where(low, 1.0, -1.0)
    push = SCALE * fluxes[1] + (SLOPE * mine[0:1]) * ghost_ground
    block8 = stacked(
        [sign * SCALE * fluxes[0], sign * SCALE * fluxes[2], sign * push],
        jnp.zeros((8, TILE), jnp.float32),
    )
    return jnp.transpose(
        jnp.concatenate([block8, jnp.zeros((LANES - 8, TILE), jnp.float32)], 0)
    )


def last_update(ctl, got, ground, columns, state, manning, rate, order, *rest):
    del order
    slots = ctl[MOVE], 1 - ctl[MOVE]
    update(STEPS - 1, ctl, got, ground, columns, state, manning, rate, *rest, slots=slots)


def update(
    step, ctl, got_in, ground_in, columns_in, state_in, manning_in, rate_in, *rest,
    passing=None, slots=(0, 1),
):
    more = step + 1 < STEPS
    fresh_out, *lines_to, delta_out = rest[: 4 if more else 6]
    rest = rest[4 if more else 6 :]
    state, manning, rate, fresh, got, ground, columns, first, second, delta_keep, sems = rest
    out, columns_out = first, second
    small = start_all(
        ((got_in, got), (ground_in, ground), (columns_in, columns)), sems, 5 * PARTS
    )
    size = 2 * TILE // PARTS
    parts = [
        (slot, slice(k * size, (k + 1) * size)) for slot in slots for k in range(PARTS // 2)
    ]
    incoming = []
    for index, (slot, rows) in enumerate(parts):
        incoming.append(
            start_all(
                (
                    (rate_in.at[slot, :, rows], rate.at[slot, :, rows]),
                    (state_in.at[slot, :, rows], state.at[slot, :, rows]),
                    (manning_in.at[slot, rows], manning.at[slot, rows]),
                ),
                sems,
                3 * index,
            )
        )
    wait_all(small)
    upper = lax.axis_index("yb")
    devices = 2 * lax.axis_size("xb")
    begin = TILE if got.shape[1] > TILE else 0
    tops = got[0:8, begin : begin + LANES]
    for peer in range(1, devices):
        tops = jnp.maximum(tops, got[peer * 8 : peer * 8 + 8, begin : begin + LANES])
    delta = (COURANT * SPACING) / tops[TOP : TOP + 1, :]
    delta = jnp.concatenate([delta, delta], 1)
    delta_keep[...] = jnp.broadcast_to(delta, (8, TILE))
    outgoing = start_all(((delta_keep, delta_out),), sems, 5 * PARTS + 3)
    fix = column_fix(got, ground, columns)
    facing = jnp.where(upper > 0, ctl[SLOT_LOW], 1 - ctl[SLOT_LOW])
    begin = pl.multiple_of((1 - upper) * LANES, LANES)
    goal = (1 - upper) * (LANES - 1)
    lane = lax.broadcasted_iota(jnp.int32, (size, LANES), 1)
    total = jnp.zeros((ROWS, TILE), jnp.float32)
    for index, (slot, part_rows) in enumerate(parts):
        wait_all(incoming[index])
        if part_rows.start == 0:
            correct_rows(ctl, slot, got, ground, state, rate, True)
        if part_rows.stop == TILE:
            correct_rows(ctl, slot, got, ground, state, rate, False)

        @pl.when(facing == slot)
        def _(slot=slot, part_rows=part_rows):
            for field in range(3):
                turned = pltpu.roll(
                    fix[part_rows], lax.rem(goal + LANES - field, LANES), 1
                )
                rate[slot, field, part_rows, pl.ds(begin, LANES)] += jnp.where(
                    lane == goal, turned, 0.0
                )

        wet_now = flag(ctl, WET + 2 * step + slot)

        def group(index, best, slot=slot, wet_now=wet_now):
            rows = pl.ds(pl.multiple_of(index * ROWS, ROWS), ROWS)
            old = tuple(state[slot, field, rows, :] for field in range(3))
            slopes = tuple(rate[slot, field, rows, :] for field in range(3))
            h, hu, hv = moved_on(old, slopes, manning[slot, rows, :], delta, wet_now)
            fresh[slot, 0, rows, :] = h
            fresh[slot, 1, rows, :] = hu
            fresh[slot, 2, rows, :] = hv
            if more:
                along_x, along_y = cell(h, hu, hv)
                best = jnp.maximum(best, jnp.maximum(along_x[5], along_y[5]))
            return best

        best = lax.fori_loop(
            part_rows.start // ROWS,
            part_rows.stop // ROWS,
            group,
            jnp.zeros((ROWS, TILE), jnp.float32),
        )
        if more:
            best = jnp.where(flag(ctl, WET + 2 * step + 2 + slot), best, 0.0)
            total = jnp.maximum(total, best)
        if more:
            outgoing += start_all(
                ((fresh.at[slot, :, part_rows], fresh_out.at[slot, :, part_rows]),),
                sems,
                3 * PARTS + index,
            )
        elif index >= PARTS // 2:
            outgoing += start_all(
                ((fresh.at[slot, :, part_rows], fresh_out.at[:, part_rows]),),
                sems,
                3 * PARTS + index,
            )
        if not more and part_rows.stop == TILE:
            late, low, high = (
                (first, *lines_to[:2]) if index < PARTS // 2 else (second, *lines_to[2:])
            )
            late_rows(fresh.at[slot], late)
            outgoing += start_all(
                ((late.at[:, :HALF], low), (late.at[:, HALF:], high)),
                sems,
                4 * PARTS + (0 if index < PARTS // 2 else 2),
            )
        if passing and index == PARTS // 2:
            passing.middle()
    if more:
        messages(ctl, fresh, None, jnp.max(total, keepdims=True), out, columns_out)
        pairs = zip((out, columns_out), lines_to)
        outgoing += start_all(tuple(pairs), sems, 4 * PARTS)
    wait_all(outgoing)


def vmem():
    return pl.BlockSpec(memory_space=pltpu.VMEM)


def smem():
    return pl.BlockSpec(memory_space=pltpu.SMEM)


def hbm():
    return pl.BlockSpec(memory_space=pltpu.HBM)


def anywhere():
    return pl.BlockSpec(memory_space=pl.ANY)


def call(
    kernel, outs, out_specs, in_specs, flops, scratch=(), aliases=None, room=VMEM_BYTES, moved=4
):
    return pl.pallas_call(
        kernel,
        scratch_shapes=scratch,
        input_output_aliases=aliases or {},
        out_shape=outs,
        in_specs=in_specs,
        out_specs=out_specs,
        compiler_params=pltpu.CompilerParams(vmem_limit_bytes=room),
        cost_estimate=pl.CostEstimate(flops=flops, bytes_accessed=moved << 20, transcendentals=0),
    )


def f32(*shape):
    return jax.ShapeDtypeStruct(shape, jnp.float32)


def spread(fast):
    return lax.all_to_all(fast, ("xb", "yb"), split_axis=0, concat_axis=0, tiled=True)


def body(state, bed, manning, neighbours, wet, moves):
    shape = f32(*state.shape)
    devices = lax.axis_size("xb") * lax.axis_size("yb")
    whole = pltpu.VMEM(state.shape, jnp.float32)
    part = pltpu.VMEM(bed.shape, jnp.float32)
    tile_shape = f32(*state.shape[1:])
    early_shape = f32(5, EARLY, TILE)
    early_state = f32(3, EARLY, TILE)
    late_shape = f32(3, LATE, TILE)
    half_shape = f32(3, HALF, TILE)
    delta_shape = f32(8, TILE)

    def buffer(like):
        return pltpu.VMEM(like.shape, jnp.float32)

    piece_shapes = tuple(f32(5, end - begin, TILE) for begin, end in PIECES)
    out, columns, ctl = call(
        opening,
        (
            f32(8 * devices, TILE + LANES),
            f32(8, TILE),
            jax.ShapeDtypeStruct((CONTROLS,), jnp.int32),
        ),
        (vmem(), vmem(), smem()),
        [hbm()] * 5,
        4 << 20,
        [
            whole,
            part,
            pltpu.SMEM(neighbours.shape[::-1], jnp.int32),
            pltpu.SMEM(wet.shape, jnp.int32),
            pltpu.SMEM(moves.shape, jnp.int32),
            pltpu.SemaphoreType.DMA((6,)),
        ],
    )(state, bed, neighbours.T, wet, moves)
    state_first = state
    ground = None
    deltas = []
    for step in range(STEPS):
        got = spread(out)
        ground = got if step == 0 else ground
        scratch = [whole, part, whole, pltpu.SemaphoreType.DMA((3 * CHUNKS,))]
        piece_scratch = [
            [buffer(piece), pltpu.SemaphoreType.DMA((2,))] for piece in piece_shapes
        ]
        if step == 1:
            rate, leaving = call(
                rates_and_leaving,
                (shape, piece_shapes[0]),
                (hbm(),) * 2,
                [smem()] + [hbm()] * 5,
                16 << 20,
                scratch + piece_scratch[0],
            )(ctl, state, bed, state_first, manning, early_first[0])
            early_second = [shifted(leaving, "xb", 1)]
        elif step == 2:
            rate = call(rates_after, shape, hbm(), [smem()] + [hbm()] * 3, 16 << 20, scratch)(
                ctl, state, bed, early_second[0]
            )
        else:
            rate, *leaving = call(
                rates_and_splitting,
                (shape,) + piece_shapes,
                (hbm(),) * 3,
                [smem()] + [hbm()] * 3,
                16 << 20,
                scratch + [buffer(early_shape), pltpu.SemaphoreType.DMA((5,))],
            )(ctl, state, bed, manning)
            held = call(
                hold, piece_shapes[0], hbm(), [hbm()] * 3, 1 << 10, aliases={2: 0}
            )(rate, got, leaving[0])
            early_first = [shifted(held, "xb", 1)]
        more = step + 1 < STEPS
        shapes = (f32(8 * devices, TILE), f32(8, TILE)) if more else (half_shape,) * 4
        passing = step == 1
        work = [
            whole,
            part,
            whole,
            whole,
            pltpu.VMEM(got.shape, jnp.float32),
            pltpu.VMEM(ground.shape, jnp.float32),
            pltpu.VMEM((8, TILE), jnp.float32),
            buffer(shapes[0] if more else late_shape),
            buffer(shapes[1] if more else late_shape),
            buffer(delta_shape),
            pltpu.SemaphoreType.DMA((5 * PARTS + 4,)),
        ]
        operands = ctl, got, ground, columns, state, manning, rate
        if not more:
            break
        outs = call(
            functools.partial(update_and_leaving if passing else update, step),
            (shape,) + shapes + (delta_shape,) + ((piece_shapes[1],) if passing else ()),
            (hbm(),) * (5 if passing else 4),
            [smem()] + [hbm()] * (9 if passing else 6),
            8 << 20,
            work + (piece_scratch[1] if passing else []),
            moved=10,
        )(*operands, *((state_first, bed, early_first[1]) if passing else ()))
        state, out, columns, delta, *passed = outs
        deltas.append(delta)
        if step == 0:
            held = call(
                hold, piece_shapes[1], hbm(), [hbm()] * 3, 1 << 10, aliases={2: 0}
            )(delta, delta, leaving[1])
            early_first.append(shifted(held, "xb", 1))
        elif step == 1:
            early_second.append(shifted(passed[0], "xb", 1))

    staying, late_first, rest_first, late_second, rest_second, delta = call(
        last_update,
        (tile_shape,) + shapes + (delta_shape,),
        (hbm(),) * 6,
        [smem()] + [hbm()] * 7,
        8 << 20,
        work,
        moved=10,
    )(*operands, early_second[1])
    deltas.append(delta)
    room = 16 << 20
    late_arrived = shifted(late_first, "xb", 1)
    rest_arrived = shifted(rest_first, "xb", 1)
    second, late_second, rest_second = call(
        repeat_second,
        (early_state, half_shape, half_shape),
        (anywhere(), vmem(), vmem()),
        [smem()] + [vmem()] * 3 + [anywhere()] * 4,
        8 << 20,
        [buffer(early_shape), buffer(early_state), pltpu.SemaphoreType.DMA((4,))],
        room=room,
    )(ctl, *deltas, *early_second, late_second, rest_second)

    def pass_late(arrived, own):
        leaving = call(
            second_late,
            half_shape,
            vmem(),
            [smem(), vmem(), vmem(), anywhere()],
            1 << 10,
            room=room,
        )(ctl, arrived, own, second)
        return shifted(leaving, "xb", 1)

    late_next = pass_late(late_arrived, late_second)
    rest_next = pass_late(rest_arrived, rest_second)
    final = call(
        repeat_first,
        shape,
        hbm(),
        [smem()] + [vmem()] * 3 + [anywhere()] * 5,
        8 << 20,
        [
            buffer(early_shape),
            buffer(early_state),
            buffer(tile_shape),
            buffer(half_shape),
            buffer(half_shape),
            pltpu.SemaphoreType.DMA((4,)),
        ],
        room=room,
    )(ctl, *deltas, *early_first, late_arrived, rest_arrived, staying)
    final = call(
        finish_late,
        shape,
        hbm(),
        [smem(), vmem(), vmem(), hbm()],
        1 << 20,
        [pltpu.VMEM((3, TILE - HALF, TILE), jnp.float32), pltpu.SemaphoreType.DMA((3,))],
        {3: 0},
        room=room,
    )(ctl, late_next, second, final)
    return call(
        finish_rest,
        shape,
        hbm(),
        [smem(), vmem(), hbm()],
        1 << 20,
        [pltpu.SemaphoreType.DMA((1,))],
        {2: 0},
        room=room,
    )(ctl, rest_next, final)


def solution(mesh):
    placed = (
        P(("runs", "xb", "yb"), None, None, None),
        P(("runs", "xb", "yb"), None, None),
        P(("runs", "xb", "yb"), None, None),
        P("runs", None),
        P(None, "runs"),
        P(None, "runs"),
    )
    return jax.shard_map(
        body,
        mesh=mesh,
        in_specs=placed,
        out_specs=P(("runs", "xb", "yb"), None, None, None),
        check_vma=False,
    )
```

```python
import functools

import jax
import jax.numpy as jnp
from jax import lax
from jax.experimental import pallas as pl
from jax.experimental.pallas import tpu as pltpu
from jax.sharding import PartitionSpec as P

STEPS = 3
GRAVITY = 9.81
ROOT_G = GRAVITY**0.5
SPACING = 5.0
COURANT = 0.2
ROWS = 64
LANES = 128
TILE = 256
VMEM_BYTES = 60 * 1024 * 1024
SLOT_LOW, WALL_WEST, WALL_EAST, WALL_OUTER, WET, MOVE = 0, 1, 3, 5, 7, 13
WET_FIRST, WET_SECOND = 16, 19
CONTROLS = 24
EARLY = 144
PIECES = ((0, 80), (80, 144))
AGAIN = 48
LATE = TILE - EARLY + 16
HALF = LATE // 2
CHUNKS = 8
PARTS = 4
STRIP = 32
TOP = 6
SCALE = 0.5 / SPACING
SLOPE = GRAVITY / (2.0 * SPACING)


def shifted(value, axis, steps, around=True):
    count = lax.axis_size(axis)
    pairs = [(source, (source + steps) % count) for source in range(count)]
    if not around:
        pairs = [pair for pair in pairs if abs(pair[0] - pair[1]) == abs(steps)]
    return lax.ppermute(value, axis, pairs)


def cell(h, hu, hv):
    root = lax.rsqrt(h)
    inverse = root * root
    u = hu * inverse
    v = hv * inverse
    celerity = ROOT_G * (h * root)
    pressure = (0.5 * GRAVITY) * (h * h)
    cross = hu * v
    speed_x = jnp.abs(u) + celerity
    speed_y = jnp.abs(v) + celerity
    along_x = (h, hu, hv, hu * u + pressure, cross, speed_x)
    along_y = (h, hv, hu, hv * v + pressure, cross, speed_y)
    return along_x, along_y


def face(left, right):
    wave = jnp.maximum(left[5], right[5])
    return (
        (left[1] + right[1]) - wave * (right[0] - left[0]),
        (left[3] + right[3]) - wave * (right[1] - left[1]),
        (left[4] + right[4]) - wave * (right[2] - left[2]),
    )


def slot_of(ctl, position):
    low = ctl[SLOT_LOW]
    return low if position == 0 else 1 - low


def flag(ctl, index):
    return ctl[index] > 0


def start_all(pairs, sems, first=0):
    copies = [
        pltpu.make_async_copy(src, dst, sems.at[first + k]) for k, (src, dst) in enumerate(pairs)
    ]
    for copy in copies:
        copy.start()
    return copies


def wait_all(copies):
    for copy in copies:
        copy.wait()


def sublanes(width=TILE):
    return lax.broadcasted_iota(jnp.int32, (8, width), 0)


def stacked(lines, base):
    row = sublanes()
    for index, line in enumerate(lines):
        base = jnp.where(row == index, jnp.broadcast_to(line, (8, TILE)), base)
    return base


def messages(ctl, state, bed, fastest, out, columns):
    upper = lax.axis_index("yb")
    column = lax.axis_index("xb")
    last = lax.axis_size("xb") - 1
    devices = 2 * (last + 1)
    device = column * 2 + upper
    top = jnp.broadcast_to(fastest, (8, TILE))
    for peer in range(devices):
        out[peer * 8 : peer * 8 + 8, :TILE] = top
        if bed is not None:
            out[peer * 8 : peer * 8 + 8, TILE:] = top[:, :LANES]
    row = sublanes()

    def edge(line):
        rows = slice(line, line + 1)
        lines = []
        for position in range(2):
            slot = slot_of(ctl, position)
            lines += [state[slot, field, rows, :] for field in range(3)]
            if bed is not None:
                lines.append(bed[slot, rows, :])
        return stacked(lines, top)

    for inside, peer, line in (
        (column > 0, device - 2, 0),
        (column < last, device + 2, TILE - 1),
    ):

        @pl.when(inside)
        def _(peer=peer, line=line):
            out[pl.ds(pl.multiple_of(peer * 8, 8), 8), :TILE] = edge(line)

    slot = jnp.where(upper > 0, ctl[SLOT_LOW], 1 - ctl[SLOT_LOW])
    begin = pl.multiple_of((1 - upper) * LANES, LANES)
    lane = lax.broadcasted_iota(jnp.int32, (TILE, LANES), 1)
    packed = None
    for field in range(4 if bed is not None else 3):
        if field < 3:
            part = state[slot, field, :, pl.ds(begin, LANES)]
        else:
            part = bed[slot, :, pl.ds(begin, LANES)]
        turned = pltpu.roll(part, field + 1 - upper, 1)
        packed = turned if field == 0 else jnp.where(lane == field, turned, packed)
    lines = jnp.transpose(packed)[:8]
    columns[...] = lines
    start = pl.multiple_of((device + 1 - 2 * upper) * 8, 8)
    out[pl.ds(start, 8), :TILE] = jnp.where(row == TOP, top, lines)


def opening(
    state_in, bed_in, neighbours_in, wet_in, moves_in,
    out, columns, ctl,
    state, bed, neighbours, wet, moves, sems,
):
    copies = start_all(
        (
            (neighbours_in, neighbours),
            (wet_in, wet),
            (moves_in, moves),
            (state_in.at[0], state.at[0]),
            (state_in.at[1], state.at[1]),
            (bed_in, bed),
        ),
        sems,
    )
    device = lax.axis_index("xb") * 2 + lax.axis_index("yb")
    wait_all(copies[:3])
    first = device * 2
    low = jnp.where(neighbours[3, first] == first + 1, 0, 1)
    ctl[SLOT_LOW] = low
    for position in range(2):
        slot = low if position == 0 else 1 - low
        tile = first + slot
        ctl[WALL_WEST + position] = (neighbours[0, tile] < 0).astype(jnp.int32)
        ctl[WALL_EAST + position] = (neighbours[1, tile] < 0).astype(jnp.int32)
        ctl[WALL_OUTER + position] = (neighbours[2 + position, tile] < 0).astype(jnp.int32)
    for step in range(STEPS):
        for slot in range(2):
            ctl[WET + 2 * step + slot] = wet[step, first + slot]
        ctl[MOVE + step] = moves[step, device]
    count = lax.axis_size("xb")
    upper = lax.axis_index("yb")
    column = lax.axis_index("xb")
    source = lax.rem(column + count - 1, count) * 2 + upper
    before = lax.rem(column + count - 2, count) * 2 + upper
    again = moves[0, source] == moves[1, source]
    tile_first = source * 2 + moves[0, source]
    tile_second = jnp.where(
        again, before * 2 + moves[0, before], source * 2 + 1 - moves[0, source]
    )
    for step in range(STEPS):
        ctl[WET_FIRST + step] = wet[step, tile_first]
        ctl[WET_SECOND + step] = wet[step, tile_second]

    total = jnp.zeros((ROWS, TILE), jnp.float32)
    for slot in range(2):
        copies[3 + slot].wait()

        def group(index, best, slot=slot):
            rows = pl.ds(pl.multiple_of(index * ROWS, ROWS), ROWS)
            along_x, along_y = cell(*(state[slot, field, rows, :] for field in range(3)))
            return jnp.maximum(best, jnp.maximum(along_x[5], along_y[5]))

        best = lax.fori_loop(0, TILE // ROWS, group, jnp.zeros((ROWS, TILE), jnp.float32))
        total = jnp.maximum(total, jnp.where(wet[0, first + slot] > 0, best, 0.0))
    copies[5].wait()
    messages(ctl, state, bed, jnp.max(total, keepdims=True), out, columns)


def hold(first, second, leaving, same):
    del first, second, leaving, same


class Splitting:
    def __init__(self, ctl, state_in, bed_in, manning_in, leaving, buffer, sems):
        slot = ctl[MOVE]
        rows = slice(0, EARLY)
        pairs = (
            (state_in.at[slot, :, rows], buffer.at[0:3]),
            (bed_in.at[slot, rows], buffer.at[3]),
            (manning_in.at[slot, rows], buffer.at[4]),
        )
        self.incoming = [
            pltpu.make_async_copy(src, dst, sems.at[k]) for k, (src, dst) in enumerate(pairs)
        ]
        self.outgoing = [
            pltpu.make_async_copy(buffer.at[:, begin:end], piece, sems.at[3 + k])
            for k, ((begin, end), piece) in enumerate(zip(PIECES, leaving))
        ]

    def start(self):
        for copy in self.incoming:
            copy.start()

    def middle(self):
        wait_all(self.incoming)
        for copy in self.outgoing:
            copy.start()

    def end(self):
        wait_all(self.outgoing)


class Passing:
    def __init__(self, ctl, piece, state_in, bed_in, manning_in, arrived, leaving, buffer, sems):
        self.again = ctl[MOVE] == ctl[MOVE + 1]
        self.other = 1 - ctl[MOVE]
        self.rows = slice(*piece)
        self.refs = state_in, bed_in, manning_in
        self.incoming = pltpu.make_async_copy(arrived, buffer, sems.at[0])
        self.outgoing = pltpu.make_async_copy(buffer, leaving, sems.at[1])
        self.buffer = buffer
        self.sem = sems.at[0]

    def start(self):
        state_in, bed_in, manning_in = self.refs
        buffer, sem, rows = self.buffer, self.sem, self.rows

        @pl.when(self.again)
        def _():
            self.incoming.start()

        @pl.when(jnp.logical_not(self.again))
        def _():
            pltpu.make_async_copy(state_in.at[self.other, :, rows], buffer.at[0:3], sem).start()
            pltpu.make_async_copy(bed_in.at[self.other, rows], buffer.at[3], sem).start()
            pltpu.make_async_copy(manning_in.at[self.other, rows], buffer.at[4], sem).start()

    def middle(self):
        self.incoming.wait()
        self.outgoing.start()

    def end(self):
        self.outgoing.wait()


def rates_and_splitting(
    ctl, state_in, bed_in, manning_in, rate_out, leaving_low, leaving_high,
    state, bed, rate, sems, buffer, moving,
):
    leaving = leaving_low, leaving_high
    splitting = Splitting(ctl, state_in, bed_in, manning_in, leaving, buffer, moving)
    rates(ctl, state_in, bed_in, rate_out, state, bed, rate, sems, splitting)


def rates_and_leaving(
    ctl, state_in, bed_in, state_first, manning_in, arrived, rate_out, leaving,
    state, bed, rate, sems, buffer, moving,
):
    passing = Passing(
        ctl, PIECES[0], state_first, bed_in, manning_in, arrived, leaving, buffer, moving
    )
    rates(ctl, state_in, bed_in, rate_out, state, bed, rate, sems, passing)


def update_and_leaving(
    step, ctl, got_in, ground_in, columns_in, state_in, manning_in, rate_in,
    state_first, bed_in, arrived, fresh_out, first_out, second_out, delta_out, leaving, *rest
):
    *rest, buffer, moving = rest
    passing = Passing(
        ctl, PIECES[1], state_first, bed_in, manning_in, arrived, leaving, buffer, moving
    )
    passing.start()
    update(
        step, ctl, got_in, ground_in, columns_in, state_in, manning_in, rate_in,
        fresh_out, first_out, second_out, delta_out, *rest, passing=passing,
    )
    passing.end()


def rates_after(ctl, state_in, bed_in, order, *rest):
    del order
    rates(ctl, state_in, bed_in, *rest)


def rates(ctl, state_in, bed_in, rate_out, state, bed, rate, sems, passing=None):
    width = 2 * TILE
    row_ids = lax.broadcasted_iota(jnp.int32, (STRIP, width), 0)
    row8 = sublanes(width)
    lane = lax.broadcasted_iota(jnp.int32, (STRIP, LANES), 1)
    last = TILE // STRIP - 1
    chunk = TILE // CHUNKS
    slots = [slot_of(ctl, position) for position in range(2)]
    incoming = []
    for part in range(CHUNKS):
        rows = slice(part * chunk, (part + 1) * chunk)
        incoming.append(
            start_all(
                (
                    (state_in.at[:, :, rows], state.at[:, :, rows]),
                    (bed_in.at[:, rows], bed.at[:, rows]),
                ),
                sems,
                2 * part,
            )
        )
    if passing:
        passing.start()
    keep_west, keep_east, keep_south, keep_north = (
        jnp.where(flag(ctl, index), 1.0, 0.0)
        for index in (WALL_WEST, WALL_EAST, WALL_OUTER, WALL_OUTER + 1)
    )

    def strip(field, rows):
        if field == 3:
            return jnp.concatenate([bed[slot, rows, :] for slot in slots], 1)
        return jnp.concatenate([state[slot, field, rows, :] for slot in slots], 1)

    def blocks(value):
        return [value[:, k * LANES : (k + 1) * LANES] for k in range(4)]

    def right_of(value, end=None):
        turned = [pltpu.roll(part, LANES - 1, 1) for part in blocks(value)]
        after = turned[1:] + [turned[3] if end is None else end]
        return jnp.concatenate(
            [
                jnp.where(lane == LANES - 1, following, part)
                if following is not part
                else part
                for part, following in zip(turned, after)
            ],
            1,
        )

    def left_of(value, end):
        turned = [pltpu.roll(part, 1, 1) for part in blocks(value)]
        before = [end] + turned[:3]
        return jnp.concatenate(
            [jnp.where(lane == 0, previous, part) for part, previous in zip(turned, before)], 1
        )

    def down(value):
        return pltpu.roll(value, STRIP + 7, 0)[:STRIP]

    def group(index, carry):
        base = pl.multiple_of(index * STRIP, STRIP)
        rows = pl.ds(base, STRIP)
        after = pl.ds(pl.multiple_of(jnp.minimum(base + STRIP, TILE - 8), 8), 8)
        at_end = index == last
        fields = [
            jnp.concatenate([strip(field, rows), strip(field, after)], 0) for field in range(3)
        ]
        cells_x, cells_y = cell(*fields)
        here_x = tuple(value[:STRIP] for value in cells_x)
        here_y = tuple(value[:STRIP] for value in cells_y)

        ending = jnp.logical_and(row8 == 7, at_end)
        faces = list(face(here_x, tuple(down(value) for value in cells_x)))
        wall = keep_east * (2.0 * (here_x[3] + here_x[5] * here_x[1])[STRIP - 8 :])
        for component, value in enumerate((0.0, wall, 0.0)):
            upper = faces[component]
            faces[component] = jnp.concatenate(
                [upper[: STRIP - 8], jnp.where(ending, value, upper[STRIP - 8 :])], 0
            )
        turned = tuple(pltpu.roll(value, 1, 0) for value in faces)
        change_x = tuple(
            value - jnp.where(row_ids == 0, before, moved)
            for value, before, moved in zip(faces, carry[:3], turned)
        )
        ground = strip(3, rows)
        ground_after = jnp.where(
            at_end,
            jnp.broadcast_to(keep_east * ground[STRIP - 1 :], (8, width)),
            strip(3, after),
        )
        ground_up = pltpu.roll(ground, 1, 0)
        slope_x = down(jnp.concatenate([ground, ground_after], 0)) - jnp.where(
            row_ids == 0, carry[3], ground_up
        )
        carried = tuple(value[0:1, :] for value in turned) + (ground_up[0:1, :],)

        faces_y = list(face(here_y, tuple(right_of(value) for value in here_y)))
        normal = here_y[3]
        spread_y = here_y[5] * here_y[1]
        north = keep_north * (2.0 * (normal + spread_y)[:, width - LANES :])
        south = keep_south * (2.0 * (normal - spread_y)[:, :LANES])
        change_y = []
        for component, (high, low) in enumerate(((0.0, 0.0), (north, south), (0.0, 0.0))):
            parts = blocks(faces_y[component])
            parts[3] = jnp.where(lane == LANES - 1, high, parts[3])
            value = jnp.concatenate(parts, 1)
            change_y.append(value - left_of(value, low))
        slope_y = right_of(ground, keep_north * ground[:, width - LANES :]) - left_of(
            ground, keep_south * ground[:, :LANES]
        )
        weight = SLOPE * here_x[0]
        results = (
            SCALE * (change_x[0] + change_y[0]),
            SCALE * (change_x[1] + change_y[2]) + weight * slope_x,
            SCALE * (change_x[2] + change_y[1]) + weight * slope_y,
        )
        for field, value in enumerate(results):
            for position, slot in enumerate(slots):
                rate[slot, field, rows, :] = value[:, position * TILE : (position + 1) * TILE]
        return carried

    wait_all(incoming[0])
    top, _ = cell(*(strip(field, slice(0, 8)) for field in range(3)))
    nothing = jnp.zeros((1, width), jnp.float32)
    carry = (
        nothing,
        keep_west * (2.0 * (top[3] - top[5] * top[1])[0:1]),
        nothing,
        keep_west * strip(3, slice(0, 8))[0:1],
    )
    per_chunk = chunk // STRIP
    outgoing = []
    for part in range(CHUNKS):
        if part + 1 < CHUNKS:
            wait_all(incoming[part + 1])
        carry = lax.fori_loop(part * per_chunk, (part + 1) * per_chunk, group, carry)
        rows = slice(part * chunk, (part + 1) * chunk)
        outgoing += start_all(
            ((rate.at[:, :, rows], rate_out.at[:, :, rows]),), sems, 2 * CHUNKS + part
        )
        if passing and part == CHUNKS // 2:
            passing.middle()
    wait_all(outgoing)
    if passing:
        passing.end()


def moved_on(old, slopes, rough, delta, wet_now):
    h, hu, hv = (value - delta * slope for value, slope in zip(old, slopes))
    inverse = 1.0 / h
    u = hu * inverse
    v = hv * inverse
    speed = jnp.sqrt(u * u + v * v)
    power = jnp.exp((-4.0 / 3.0) * jnp.log(jnp.abs(h)))
    drag = (GRAVITY * delta) * (rough * rough) * (speed * power)
    factor = 1.0 / (1.0 + drag)
    fresh = (h, hu * factor, hv * factor)
    return tuple(jnp.where(wet_now, new, value) for new, value in zip(fresh, old))


def repeat_steps(ctl, wet_from, deltas, early, work, other, sems):
    incoming = []
    for ref in early:
        begin = 0 if ref is early[0] else early[0].shape[1]
        incoming += start_all(
            ((ref, work.at[:, begin : begin + ref.shape[1]]),), sems, len(incoming)
        )
    row_ids = lax.broadcasted_iota(jnp.int32, (AGAIN, TILE), 0)
    lane = lax.broadcasted_iota(jnp.int32, (AGAIN, LANES), 1)
    start = tuple(jnp.zeros((1, TILE), jnp.float32) for _ in range(4))

    def halves(value):
        return value[:, :LANES], value[:, LANES:]

    def right_of(value):
        low, high = (pltpu.roll(part, LANES - 1, 1) for part in halves(value))
        return jnp.concatenate([jnp.where(lane == LANES - 1, high, low), high], 1)

    def left_of(value):
        low, high = (pltpu.roll(part, 1, 1) for part in halves(value))
        return jnp.concatenate([low, jnp.where(lane == 0, low, high)], 1)

    def down(value):
        return pltpu.roll(value, AGAIN + 7, 0)[:AGAIN]

    for step in range(STEPS):
        source, target = (work, other) if step % 2 == 0 else (other, work)
        delta = deltas[step][0:1, :]
        wet_now = flag(ctl, wet_from + step)

        def group(index, carry, source=source, target=target, delta=delta, wet_now=wet_now):
            base = pl.multiple_of(index * AGAIN, AGAIN)
            rows = pl.ds(base, AGAIN)
            after = pl.ds(pl.multiple_of(jnp.minimum(base + AGAIN, EARLY - 8), 8), 8)
            refs = [source.at[field] for field in range(3)] + [work.at[3]]
            fields = [jnp.concatenate([ref[rows, :], ref[after, :]], 0) for ref in refs]
            cells_x, cells_y = cell(*fields[:3])
            here_x = tuple(value[:AGAIN] for value in cells_x)
            here_y = tuple(value[:AGAIN] for value in cells_y)
            faces_x = face(here_x, tuple(down(value) for value in cells_x))
            turned = tuple(pltpu.roll(value, 1, 0) for value in faces_x)
            change_x = tuple(
                value - jnp.where(row_ids == 0, before, moved)
                for value, before, moved in zip(faces_x, carry[:3], turned)
            )
            ground = fields[3][:AGAIN]
            ground_up = pltpu.roll(ground, 1, 0)
            slope_x = down(fields[3]) - jnp.where(row_ids == 0, carry[3], ground_up)
            carried = tuple(value[0:1, :] for value in turned) + (ground_up[0:1, :],)
            faces_y = face(here_y, tuple(right_of(value) for value in here_y))
            change_y = tuple(value - left_of(value) for value in faces_y)
            slope_y = right_of(ground) - left_of(ground)
            old = tuple(value[:AGAIN] for value in fields[:3])
            weight = SLOPE * old[0]
            slopes = (
                SCALE * (change_x[0] + change_y[0]),
                SCALE * (change_x[1] + change_y[2]) + weight * slope_x,
                SCALE * (change_x[2] + change_y[1]) + weight * slope_y,
            )
            for field, value in enumerate(
                moved_on(old, slopes, work[4, rows, :], delta, wet_now)
            ):
                target[field, rows, :] = value
            return carried

        if step == 0:
            wait_all(incoming)
        lax.fori_loop(0, EARLY // AGAIN, group, start)


def late_rows(tile, late):
    row = sublanes()
    kept = EARLY - 8
    lane = lax.broadcasted_iota(jnp.int32, (8, LANES), 1)
    for field in range(3):
        late[field, 0:8, :] = jnp.where(
            row < 3, tile[field, 0:8, :], tile[field, kept : kept + 8, :]
        )
        packed = [jnp.zeros((8, LANES), jnp.float32)] * 2
        for block in range(EARLY // 8):
            rows = slice(8 * block, 8 * block + 8)
            sides = jnp.where(lane < 64, tile[field, rows, :LANES], tile[field, rows, LANES:])
            turned = pltpu.roll(sides, (3 + 8 * block) % LANES, 1)
            which = block // 16
            packed[which] = jnp.where(lane // 8 == block % 16, turned, packed[which])
        late[field, 8:16, :] = jnp.concatenate(packed, 1)
        late[field, 16:, :] = tile[field, EARLY:, :]


def merge(late, rest, early, tile):
    for field in range(3):
        merge_field(field, late, rest, early, tile)


def merge_field(field, late, rest, early, tile):
    row = sublanes()
    lane = lax.broadcasted_iota(jnp.int32, (8, LANES), 1)
    first = late[field, 0:8, :]
    for block in range(EARLY // 8):
        rows = slice(8 * block, 8 * block + 8)
        which = block // 16
        packed = late[field, 8:16, which * LANES : (which + 1) * LANES]
        sides = pltpu.roll(packed, (-3 - 8 * block) % LANES, 1)
        value = early[field, rows, :]
        value = jnp.concatenate(
            [
                jnp.where(lane < 3, sides, value[:, :LANES]),
                jnp.where(lane >= LANES - 3, sides, value[:, LANES:]),
            ],
            1,
        )
        if block == 0:
            value = jnp.where(row < 3, first, value)
        if block == EARLY // 8 - 1:
            value = jnp.where(row < 5, value, first)
        tile[field, rows, :] = value
    tile[field, EARLY : TILE - HALF, :] = late[field, 16:, :]
    if rest is not None:
        tile[field, TILE - HALF :, :] = rest[field]


def repeat_second(
    ctl, delta0, delta1, delta2, low, high, late, rest, out, late_out, rest_out, work, tile, sems
):
    near = start_all(((late, late_out), (rest, rest_out)), sems, 2)
    repeat_steps(ctl, WET_SECOND, (delta0, delta1, delta2), (low, high), work, tile, sems)
    wait_all(start_all(((tile, out),), sems) + near)


def repeat_first(
    ctl, delta0, delta1, delta2, low, high, late_in, rest_in, staying, out,
    work, other, tile, late, rest, sems,
):
    kept = out.at[1 - ctl[MOVE + 1]]
    again = ctl[MOVE] == ctl[MOVE + 1]

    @pl.when(again)
    def _():
        wait_all(start_all(((staying, tile),), sems))

    @pl.when(jnp.logical_not(again))
    def _():
        copies = start_all(((late_in, late), (rest_in, rest)), sems, 2)
        repeat_steps(ctl, WET_FIRST, (delta0, delta1, delta2), (low, high), work, other, sems)
        wait_all(copies)
        merge(late, rest, other, tile)

    wait_all(start_all(((tile, kept),), sems))


def finish_late(ctl, late, early, before, out, tile, sems):
    del before
    copies = []
    for field in range(3):
        merge_field(field, late, None, early, tile)
        copies += start_all(
            ((tile.at[field], out.at[ctl[MOVE + 1], field, 0 : TILE - HALF]),), sems, field
        )
    wait_all(copies)


def finish_rest(ctl, rest, before, out, sems):
    del before
    wait_all(start_all(((rest, out.at[ctl[MOVE + 1], :, TILE - HALF :]),), sems))


def second_late(ctl, arrived, own, order, leaving):
    del order
    again = ctl[MOVE] == ctl[MOVE + 1]
    for field in range(3):
        leaving[field] = jnp.where(again, arrived[field], own[field])


def correct_rows(ctl, slot, got, ground, state, rate, bottom):
    position = jnp.where(ctl[SLOT_LOW] == slot, 0, 1)
    device = lax.axis_index("xb") * 2 + lax.axis_index("yb")
    wall = WALL_WEST if bottom else WALL_EAST

    @pl.when(jnp.logical_not(flag(ctl, wall + position)))
    def _():
        peer = device - 2 if bottom else device + 2
        block = pl.ds(pl.multiple_of(peer * 8, 8), 8)
        lines = got[block, :TILE]
        grounds = ground[block, :TILE]
        stride = 4 if got.shape[1] > TILE else 3

        def line(offset):
            other = offset + stride
            picked = jnp.where(
                position == 0, lines[offset : offset + 1, :], lines[other : other + 1, :]
            )
            return jnp.broadcast_to(picked, (8, TILE))

        ghost, _ = cell(*(line(field) for field in range(3)))
        ghost_ground = jnp.where(position == 0, grounds[3:4, :], grounds[7:8, :])
        rows = slice(0, 8) if bottom else slice(TILE - 8, TILE)
        own = [state[slot, field, rows, :] for field in range(3)]
        here, _ = cell(*own)
        fluxes = face(ghost, here) if bottom else face(here, ghost)
        push = SCALE * fluxes[1] + (SLOPE * own[0]) * ghost_ground
        row = sublanes()
        sign = -1.0 if bottom else 1.0
        chosen = row == (0 if bottom else 7)
        for field, value in enumerate((SCALE * fluxes[0], push, SCALE * fluxes[2])):
            rate[slot, field, rows, :] += jnp.where(chosen, sign * value, 0.0)


def column_fix(got, ground, columns):
    upper = lax.axis_index("yb")
    device = lax.axis_index("xb") * 2 + upper
    peer = device + 1 - 2 * upper
    block = pl.ds(pl.multiple_of(peer * 8, 8), 8)
    lines = got[block, :TILE]
    ghost_ground = ground[block, :TILE][3:4]
    mine = columns[...]
    _, ghost = cell(lines[0:1], lines[1:2], lines[2:3])
    _, own = cell(mine[0:1], mine[1:2], mine[2:3])
    low = upper == 0
    left = tuple(jnp.where(low, a, b) for a, b in zip(own, ghost))
    right = tuple(jnp.where(low, b, a) for a, b in zip(own, ghost))
    fluxes = face(left, right)
    sign = jnp.where(low, 1.0, -1.0)
    push = SCALE * fluxes[1] + (SLOPE * mine[0:1]) * ghost_ground
    block8 = stacked(
        [sign * SCALE * fluxes[0], sign * SCALE * fluxes[2], sign * push],
        jnp.zeros((8, TILE), jnp.float32),
    )
    return jnp.transpose(
        jnp.concatenate([block8, jnp.zeros((LANES - 8, TILE), jnp.float32)], 0)
    )


def last_update(ctl, got, ground, columns, state, manning, rate, order, *rest):
    del order
    slots = ctl[MOVE], 1 - ctl[MOVE]
    update(STEPS - 1, ctl, got, ground, columns, state, manning, rate, *rest, slots=slots)


def update(
    step, ctl, got_in, ground_in, columns_in, state_in, manning_in, rate_in, *rest,
    passing=None, slots=(0, 1),
):
    more = step + 1 < STEPS
    fresh_out, *lines_to, delta_out = rest[: 4 if more else 6]
    rest = rest[4 if more else 6 :]
    state, manning, rate, fresh, got, ground, columns, first, second, delta_keep, sems = rest
    out, columns_out = first, second
    small = start_all(
        ((got_in, got), (ground_in, ground), (columns_in, columns)), sems, 5 * PARTS
    )
    size = 2 * TILE // PARTS
    parts = [
        (slot, slice(k * size, (k + 1) * size)) for slot in slots for k in range(PARTS // 2)
    ]
    incoming = []
    for index, (slot, rows) in enumerate(parts):
        incoming.append(
            start_all(
                (
                    (rate_in.at[slot, :, rows], rate.at[slot, :, rows]),
                    (state_in.at[slot, :, rows], state.at[slot, :, rows]),
                    (manning_in.at[slot, rows], manning.at[slot, rows]),
                ),
                sems,
                3 * index,
            )
        )
    wait_all(small)
    upper = lax.axis_index("yb")
    devices = 2 * lax.axis_size("xb")
    begin = TILE if got.shape[1] > TILE else 0
    tops = got[0:8, begin : begin + LANES]
    for peer in range(1, devices):
        tops = jnp.maximum(tops, got[peer * 8 : peer * 8 + 8, begin : begin + LANES])
    delta = (COURANT * SPACING) / tops[TOP : TOP + 1, :]
    delta = jnp.concatenate([delta, delta], 1)
    delta_keep[...] = jnp.broadcast_to(delta, (8, TILE))
    outgoing = start_all(((delta_keep, delta_out),), sems, 5 * PARTS + 3)
    fix = column_fix(got, ground, columns)
    facing = jnp.where(upper > 0, ctl[SLOT_LOW], 1 - ctl[SLOT_LOW])
    begin = pl.multiple_of((1 - upper) * LANES, LANES)
    goal = (1 - upper) * (LANES - 1)
    lane = lax.broadcasted_iota(jnp.int32, (size, LANES), 1)
    total = jnp.zeros((ROWS, TILE), jnp.float32)
    for index, (slot, part_rows) in enumerate(parts):
        wait_all(incoming[index])
        if part_rows.start == 0:
            correct_rows(ctl, slot, got, ground, state, rate, True)
        if part_rows.stop == TILE:
            correct_rows(ctl, slot, got, ground, state, rate, False)

        @pl.when(facing == slot)
        def _(slot=slot, part_rows=part_rows):
            for field in range(3):
                turned = pltpu.roll(
                    fix[part_rows], lax.rem(goal + LANES - field, LANES), 1
                )
                rate[slot, field, part_rows, pl.ds(begin, LANES)] += jnp.where(
                    lane == goal, turned, 0.0
                )

        wet_now = flag(ctl, WET + 2 * step + slot)

        def group(index, best, slot=slot, wet_now=wet_now):
            rows = pl.ds(pl.multiple_of(index * ROWS, ROWS), ROWS)
            old = tuple(state[slot, field, rows, :] for field in range(3))
            slopes = tuple(rate[slot, field, rows, :] for field in range(3))
            h, hu, hv = moved_on(old, slopes, manning[slot, rows, :], delta, wet_now)
            fresh[slot, 0, rows, :] = h
            fresh[slot, 1, rows, :] = hu
            fresh[slot, 2, rows, :] = hv
            if more:
                along_x, along_y = cell(h, hu, hv)
                best = jnp.maximum(best, jnp.maximum(along_x[5], along_y[5]))
            return best

        best = lax.fori_loop(
            part_rows.start // ROWS,
            part_rows.stop // ROWS,
            group,
            jnp.zeros((ROWS, TILE), jnp.float32),
        )
        if more:
            best = jnp.where(flag(ctl, WET + 2 * step + 2 + slot), best, 0.0)
            total = jnp.maximum(total, best)
        if more:
            outgoing += start_all(
                ((fresh.at[slot, :, part_rows], fresh_out.at[slot, :, part_rows]),),
                sems,
                3 * PARTS + index,
            )
        elif index >= PARTS // 2:
            outgoing += start_all(
                ((fresh.at[slot, :, part_rows], fresh_out.at[:, part_rows]),),
                sems,
                3 * PARTS + index,
            )
        if not more and part_rows.stop == TILE:
            late, low, high = (
                (first, *lines_to[:2]) if index < PARTS // 2 else (second, *lines_to[2:])
            )
            late_rows(fresh.at[slot], late)
            outgoing += start_all(
                ((late.at[:, :HALF], low), (late.at[:, HALF:], high)),
                sems,
                4 * PARTS + (0 if index < PARTS // 2 else 2),
            )
        if passing and index == PARTS // 2:
            passing.middle()
    if more:
        messages(ctl, fresh, None, jnp.max(total, keepdims=True), out, columns_out)
        pairs = zip((out, columns_out), lines_to)
        outgoing += start_all(tuple(pairs), sems, 4 * PARTS)
    wait_all(outgoing)


def vmem():
    return pl.BlockSpec(memory_space=pltpu.VMEM)


def smem():
    return pl.BlockSpec(memory_space=pltpu.SMEM)


def hbm():
    return pl.BlockSpec(memory_space=pltpu.HBM)


def anywhere():
    return pl.BlockSpec(memory_space=pl.ANY)


def call(
    kernel, outs, out_specs, in_specs, flops, scratch=(), aliases=None, room=VMEM_BYTES, moved=4
):
    return pl.pallas_call(
        kernel,
        scratch_shapes=scratch,
        input_output_aliases=aliases or {},
        out_shape=outs,
        in_specs=in_specs,
        out_specs=out_specs,
        compiler_params=pltpu.CompilerParams(vmem_limit_bytes=room),
        cost_estimate=pl.CostEstimate(flops=flops, bytes_accessed=moved << 20, transcendentals=0),
    )


def f32(*shape):
    return jax.ShapeDtypeStruct(shape, jnp.float32)


def spread(fast):
    return lax.all_to_all(fast, ("xb", "yb"), split_axis=0, concat_axis=0, tiled=True)


def body(state, bed, manning, neighbours, wet, moves):
    shape = f32(*state.shape)
    devices = lax.axis_size("xb") * lax.axis_size("yb")
    whole = pltpu.VMEM(state.shape, jnp.float32)
    part = pltpu.VMEM(bed.shape, jnp.float32)
    tile_shape = f32(*state.shape[1:])
    early_shape = f32(5, EARLY, TILE)
    early_state = f32(3, EARLY, TILE)
    late_shape = f32(3, LATE, TILE)
    half_shape = f32(3, HALF, TILE)
    delta_shape = f32(8, TILE)

    def buffer(like):
        return pltpu.VMEM(like.shape, jnp.float32)

    piece_shapes = tuple(f32(5, end - begin, TILE) for begin, end in PIECES)
    out, columns, ctl = call(
        opening,
        (
            f32(8 * devices, TILE + LANES),
            f32(8, TILE),
            jax.ShapeDtypeStruct((CONTROLS,), jnp.int32),
        ),
        (vmem(), vmem(), smem()),
        [hbm()] * 5,
        4 << 20,
        [
            whole,
            part,
            pltpu.SMEM(neighbours.shape[::-1], jnp.int32),
            pltpu.SMEM(wet.shape, jnp.int32),
            pltpu.SMEM(moves.shape, jnp.int32),
            pltpu.SemaphoreType.DMA((6,)),
        ],
    )(state, bed, neighbours.T, wet, moves)
    state_first = state
    ground = None
    deltas = []
    for step in range(STEPS):
        got = spread(out)
        ground = got if step == 0 else ground
        scratch = [whole, part, whole, pltpu.SemaphoreType.DMA((3 * CHUNKS,))]
        piece_scratch = [
            [buffer(piece), pltpu.SemaphoreType.DMA((2,))] for piece in piece_shapes
        ]
        if step == 1:
            rate, leaving = call(
                rates_and_leaving,
                (shape, piece_shapes[0]),
                (hbm(),) * 2,
                [smem()] + [hbm()] * 5,
                16 << 20,
                scratch + piece_scratch[0],
            )(ctl, state, bed, state_first, manning, early_first[0])
            early_second = [shifted(leaving, "xb", 1)]
        elif step == 2:
            rate = call(rates_after, shape, hbm(), [smem()] + [hbm()] * 3, 16 << 20, scratch)(
                ctl, state, bed, early_second[0]
            )
        else:
            rate, *leaving = call(
                rates_and_splitting,
                (shape,) + piece_shapes,
                (hbm(),) * 3,
                [smem()] + [hbm()] * 3,
                16 << 20,
                scratch + [buffer(early_shape), pltpu.SemaphoreType.DMA((5,))],
            )(ctl, state, bed, manning)
            held = call(
                hold, piece_shapes[0], hbm(), [hbm()] * 3, 1 << 10, aliases={2: 0}
            )(rate, got, leaving[0])
            early_first = [shifted(held, "xb", 1)]
        more = step + 1 < STEPS
        shapes = (f32(8 * devices, TILE), f32(8, TILE)) if more else (half_shape,) * 4
        passing = step == 1
        work = [
            whole,
            part,
            whole,
            whole,
            pltpu.VMEM(got.shape, jnp.float32),
            pltpu.VMEM(ground.shape, jnp.float32),
            pltpu.VMEM((8, TILE), jnp.float32),
            buffer(shapes[0] if more else late_shape),
            buffer(shapes[1] if more else late_shape),
            buffer(delta_shape),
            pltpu.SemaphoreType.DMA((5 * PARTS + 4,)),
        ]
        operands = ctl, got, ground, columns, state, manning, rate
        if not more:
            break
        outs = call(
            functools.partial(update_and_leaving if passing else update, step),
            (shape,) + shapes + (delta_shape,) + ((piece_shapes[1],) if passing else ()),
            (hbm(),) * (5 if passing else 4),
            [smem()] + [hbm()] * (9 if passing else 6),
            8 << 20,
            work + (piece_scratch[1] if passing else []),
            moved=10,
        )(*operands, *((state_first, bed, early_first[1]) if passing else ()))
        state, out, columns, delta, *passed = outs
        deltas.append(delta)
        if step == 0:
            held = call(
                hold, piece_shapes[1], hbm(), [hbm()] * 3, 1 << 10, aliases={2: 0}
            )(delta, delta, leaving[1])
            early_first.append(shifted(held, "xb", 1))
        elif step == 1:
            early_second.append(shifted(passed[0], "xb", 1))

    staying, late_first, rest_first, late_second, rest_second, delta = call(
        last_update,
        (tile_shape,) + shapes + (delta_shape,),
        (hbm(),) * 6,
        [smem()] + [hbm()] * 7,
        8 << 20,
        work,
        moved=10,
    )(*operands, early_second[1])
    deltas.append(delta)
    room = 16 << 20
    late_arrived = shifted(late_first, "xb", 1)
    rest_arrived = shifted(rest_first, "xb", 1)
    second, late_second, rest_second = call(
        repeat_second,
        (early_state, half_shape, half_shape),
        (anywhere(), vmem(), vmem()),
        [smem()] + [vmem()] * 3 + [anywhere()] * 4,
        8 << 20,
        [buffer(early_shape), buffer(early_state), pltpu.SemaphoreType.DMA((4,))],
        room=room,
    )(ctl, *deltas, *early_second, late_second, rest_second)

    def pass_late(arrived, own):
        leaving = call(
            second_late,
            half_shape,
            vmem(),
            [smem(), vmem(), vmem(), anywhere()],
            1 << 10,
            room=room,
        )(ctl, arrived, own, second)
        return shifted(leaving, "xb", 1)

    late_next = pass_late(late_arrived, late_second)
    rest_next = pass_late(rest_arrived, rest_second)
    final = call(
        repeat_first,
        shape,
        hbm(),
        [smem()] + [vmem()] * 3 + [anywhere()] * 5,
        8 << 20,
        [
            buffer(early_shape),
            buffer(early_state),
            buffer(tile_shape),
            buffer(half_shape),
            buffer(half_shape),
            pltpu.SemaphoreType.DMA((4,)),
        ],
        room=room,
    )(ctl, *deltas, *early_first, late_arrived, rest_arrived, staying)
    final = call(
        finish_late,
        shape,
        hbm(),
        [smem(), vmem(), vmem(), hbm()],
        1 << 20,
        [pltpu.VMEM((3, TILE - HALF, TILE), jnp.float32), pltpu.SemaphoreType.DMA((3,))],
        {3: 0},
        room=room,
    )(ctl, late_next, second, final)
    return call(
        finish_rest,
        shape,
        hbm(),
        [smem(), vmem(), hbm()],
        1 << 20,
        [pltpu.SemaphoreType.DMA((1,))],
        {2: 0},
        room=room,
    )(ctl, rest_next, final)


def solution(mesh):
    placed = (
        P(("runs", "xb", "yb"), None, None, None),
        P(("runs", "xb", "yb"), None, None),
        P(("runs", "xb", "yb"), None, None),
        P("runs", None),
        P(None, "runs"),
        P(None, "runs"),
    )
    return jax.shard_map(
        body,
        mesh=mesh,
        in_specs=placed,
        out_specs=P(("runs", "xb", "yb"), None, None, None),
        check_vma=False,
    )
```

```python
import functools

import jax
import jax.numpy as jnp
from jax import lax
from jax.experimental import pallas as pl
from jax.experimental.pallas import tpu as pltpu
from jax.sharding import PartitionSpec as P

STEPS = 3
GRAVITY = 9.81
ROOT_G = GRAVITY**0.5
SPACING = 5.0
COURANT = 0.2
ROWS = 64
LANES = 128
TILE = 256
VMEM_BYTES = 60 * 1024 * 1024
SLOT_LOW, WALL_WEST, WALL_EAST, WALL_OUTER, WET, MOVE = 0, 1, 3, 5, 7, 13
WET_FIRST, WET_SECOND = 16, 19
CONTROLS = 24
EARLY = 128
PIECES = ((0, 64), (64, 128))
AGAIN = 64
LATE = TILE - EARLY + 16
HALF = LATE // 2
CHUNKS = 8
PARTS = 4
STRIP = 32
TOP = 6
SCALE = 0.5 / SPACING
SLOPE = GRAVITY / (2.0 * SPACING)


def shifted(value, axis, steps, around=True):
    count = lax.axis_size(axis)
    pairs = [(source, (source + steps) % count) for source in range(count)]
    if not around:
        pairs = [pair for pair in pairs if abs(pair[0] - pair[1]) == abs(steps)]
    return lax.ppermute(value, axis, pairs)


def cell(h, hu, hv):
    root = lax.rsqrt(h)
    inverse = root * root
    u = hu * inverse
    v = hv * inverse
    celerity = ROOT_G * (h * root)
    pressure = (0.5 * GRAVITY) * (h * h)
    cross = hu * v
    speed_x = jnp.abs(u) + celerity
    speed_y = jnp.abs(v) + celerity
    along_x = (h, hu, hv, hu * u + pressure, cross, speed_x)
    along_y = (h, hv, hu, hv * v + pressure, cross, speed_y)
    return along_x, along_y


def face(left, right):
    wave = jnp.maximum(left[5], right[5])
    return (
        (left[1] + right[1]) - wave * (right[0] - left[0]),
        (left[3] + right[3]) - wave * (right[1] - left[1]),
        (left[4] + right[4]) - wave * (right[2] - left[2]),
    )


def slot_of(ctl, position):
    low = ctl[SLOT_LOW]
    return low if position == 0 else 1 - low


def flag(ctl, index):
    return ctl[index] > 0


def start_all(pairs, sems, first=0):
    copies = [
        pltpu.make_async_copy(src, dst, sems.at[first + k]) for k, (src, dst) in enumerate(pairs)
    ]
    for copy in copies:
        copy.start()
    return copies


def wait_all(copies):
    for copy in copies:
        copy.wait()


def sublanes(width=TILE):
    return lax.broadcasted_iota(jnp.int32, (8, width), 0)


def stacked(lines, base):
    row = sublanes()
    for index, line in enumerate(lines):
        base = jnp.where(row == index, jnp.broadcast_to(line, (8, TILE)), base)
    return base


def messages(ctl, state, bed, fastest, out, columns):
    upper = lax.axis_index("yb")
    column = lax.axis_index("xb")
    last = lax.axis_size("xb") - 1
    devices = 2 * (last + 1)
    device = column * 2 + upper
    top = jnp.broadcast_to(fastest, (8, TILE))
    for peer in range(devices):
        out[peer * 8 : peer * 8 + 8, :TILE] = top
        if bed is not None:
            out[peer * 8 : peer * 8 + 8, TILE:] = top[:, :LANES]
    row = sublanes()

    def edge(line):
        rows = slice(line, line + 1)
        lines = []
        for position in range(2):
            slot = slot_of(ctl, position)
            lines += [state[slot, field, rows, :] for field in range(3)]
            if bed is not None:
                lines.append(bed[slot, rows, :])
        return stacked(lines, top)

    for inside, peer, line in (
        (column > 0, device - 2, 0),
        (column < last, device + 2, TILE - 1),
    ):

        @pl.when(inside)
        def _(peer=peer, line=line):
            out[pl.ds(pl.multiple_of(peer * 8, 8), 8), :TILE] = edge(line)

    slot = jnp.where(upper > 0, ctl[SLOT_LOW], 1 - ctl[SLOT_LOW])
    begin = pl.multiple_of((1 - upper) * LANES, LANES)
    lane = lax.broadcasted_iota(jnp.int32, (TILE, LANES), 1)
    packed = None
    for field in range(4 if bed is not None else 3):
        if field < 3:
            part = state[slot, field, :, pl.ds(begin, LANES)]
        else:
            part = bed[slot, :, pl.ds(begin, LANES)]
        turned = pltpu.roll(part, field + 1 - upper, 1)
        packed = turned if field == 0 else jnp.where(lane == field, turned, packed)
    lines = jnp.transpose(packed)[:8]
    columns[...] = lines
    start = pl.multiple_of((device + 1 - 2 * upper) * 8, 8)
    out[pl.ds(start, 8), :TILE] = jnp.where(row == TOP, top, lines)


def opening(
    state_in, bed_in, neighbours_in, wet_in, moves_in,
    out, columns, ctl,
    state, bed, neighbours, wet, moves, sems,
):
    copies = start_all(
        (
            (neighbours_in, neighbours),
            (wet_in, wet),
            (moves_in, moves),
            (state_in.at[0], state.at[0]),
            (state_in.at[1], state.at[1]),
            (bed_in, bed),
        ),
        sems,
    )
    device = lax.axis_index("xb") * 2 + lax.axis_index("yb")
    wait_all(copies[:3])
    first = device * 2
    low = jnp.where(neighbours[3, first] == first + 1, 0, 1)
    ctl[SLOT_LOW] = low
    for position in range(2):
        slot = low if position == 0 else 1 - low
        tile = first + slot
        ctl[WALL_WEST + position] = (neighbours[0, tile] < 0).astype(jnp.int32)
        ctl[WALL_EAST + position] = (neighbours[1, tile] < 0).astype(jnp.int32)
        ctl[WALL_OUTER + position] = (neighbours[2 + position, tile] < 0).astype(jnp.int32)
    for step in range(STEPS):
        for slot in range(2):
            ctl[WET + 2 * step + slot] = wet[step, first + slot]
        ctl[MOVE + step] = moves[step, device]
    count = lax.axis_size("xb")
    upper = lax.axis_index("yb")
    column = lax.axis_index("xb")
    source = lax.rem(column + count - 1, count) * 2 + upper
    before = lax.rem(column + count - 2, count) * 2 + upper
    again = moves[0, source] == moves[1, source]
    tile_first = source * 2 + moves[0, source]
    tile_second = jnp.where(
        again, before * 2 + moves[0, before], source * 2 + 1 - moves[0, source]
    )
    for step in range(STEPS):
        ctl[WET_FIRST + step] = wet[step, tile_first]
        ctl[WET_SECOND + step] = wet[step, tile_second]

    total = jnp.zeros((ROWS, TILE), jnp.float32)
    for slot in range(2):
        copies[3 + slot].wait()

        def group(index, best, slot=slot):
            rows = pl.ds(pl.multiple_of(index * ROWS, ROWS), ROWS)
            along_x, along_y = cell(*(state[slot, field, rows, :] for field in range(3)))
            return jnp.maximum(best, jnp.maximum(along_x[5], along_y[5]))

        best = lax.fori_loop(0, TILE // ROWS, group, jnp.zeros((ROWS, TILE), jnp.float32))
        total = jnp.maximum(total, jnp.where(wet[0, first + slot] > 0, best, 0.0))
    copies[5].wait()
    messages(ctl, state, bed, jnp.max(total, keepdims=True), out, columns)


def hold(first, second, leaving, same):
    del first, second, leaving, same


class Splitting:
    def __init__(self, ctl, state_in, bed_in, manning_in, leaving, buffer, sems):
        slot = ctl[MOVE]
        rows = slice(0, EARLY)
        pairs = (
            (state_in.at[slot, :, rows], buffer.at[0:3]),
            (bed_in.at[slot, rows], buffer.at[3]),
            (manning_in.at[slot, rows], buffer.at[4]),
        )
        self.incoming = [
            pltpu.make_async_copy(src, dst, sems.at[k]) for k, (src, dst) in enumerate(pairs)
        ]
        self.outgoing = [
            pltpu.make_async_copy(buffer.at[:, begin:end], piece, sems.at[3 + k])
            for k, ((begin, end), piece) in enumerate(zip(PIECES, leaving))
        ]

    def start(self):
        for copy in self.incoming:
            copy.start()

    def middle(self):
        wait_all(self.incoming)
        for copy in self.outgoing:
            copy.start()

    def end(self):
        wait_all(self.outgoing)


class Passing:
    def __init__(self, ctl, piece, state_in, bed_in, manning_in, arrived, leaving, buffer, sems):
        self.again = ctl[MOVE] == ctl[MOVE + 1]
        self.other = 1 - ctl[MOVE]
        self.rows = slice(*piece)
        self.refs = state_in, bed_in, manning_in
        self.incoming = pltpu.make_async_copy(arrived, buffer, sems.at[0])
        self.outgoing = pltpu.make_async_copy(buffer, leaving, sems.at[1])
        self.buffer = buffer
        self.sem = sems.at[0]

    def start(self):
        state_in, bed_in, manning_in = self.refs
        buffer, sem, rows = self.buffer, self.sem, self.rows

        @pl.when(self.again)
        def _():
            self.incoming.start()

        @pl.when(jnp.logical_not(self.again))
        def _():
            pltpu.make_async_copy(state_in.at[self.other, :, rows], buffer.at[0:3], sem).start()
            pltpu.make_async_copy(bed_in.at[self.other, rows], buffer.at[3], sem).start()
            pltpu.make_async_copy(manning_in.at[self.other, rows], buffer.at[4], sem).start()

    def middle(self):
        self.incoming.wait()
        self.outgoing.start()

    def end(self):
        self.outgoing.wait()


def rates_and_splitting(
    ctl, state_in, bed_in, manning_in, rate_out, leaving_low, leaving_high,
    state, bed, rate, sems, buffer, moving,
):
    leaving = leaving_low, leaving_high
    splitting = Splitting(ctl, state_in, bed_in, manning_in, leaving, buffer, moving)
    rates(ctl, state_in, bed_in, rate_out, state, bed, rate, sems, splitting)


def rates_and_leaving(
    ctl, state_in, bed_in, state_first, manning_in, arrived, rate_out, leaving,
    state, bed, rate, sems, buffer, moving,
):
    passing = Passing(
        ctl, PIECES[0], state_first, bed_in, manning_in, arrived, leaving, buffer, moving
    )
    rates(ctl, state_in, bed_in, rate_out, state, bed, rate, sems, passing)


def update_and_leaving(
    step, ctl, got_in, ground_in, columns_in, state_in, manning_in, rate_in,
    state_first, bed_in, arrived, fresh_out, first_out, second_out, delta_out, leaving, *rest
):
    *rest, buffer, moving = rest
    passing = Passing(
        ctl, PIECES[1], state_first, bed_in, manning_in, arrived, leaving, buffer, moving
    )
    passing.start()
    update(
        step, ctl, got_in, ground_in, columns_in, state_in, manning_in, rate_in,
        fresh_out, first_out, second_out, delta_out, *rest, passing=passing,
    )
    passing.end()


def rates_after(ctl, state_in, bed_in, order, *rest):
    del order
    rates(ctl, state_in, bed_in, *rest)


def rates(ctl, state_in, bed_in, rate_out, state, bed, rate, sems, passing=None):
    width = 2 * TILE
    row_ids = lax.broadcasted_iota(jnp.int32, (STRIP, width), 0)
    row8 = sublanes(width)
    lane = lax.broadcasted_iota(jnp.int32, (STRIP, LANES), 1)
    last = TILE // STRIP - 1
    chunk = TILE // CHUNKS
    slots = [slot_of(ctl, position) for position in range(2)]
    incoming = []
    for part in range(CHUNKS):
        rows = slice(part * chunk, (part + 1) * chunk)
        incoming.append(
            start_all(
                (
                    (state_in.at[:, :, rows], state.at[:, :, rows]),
                    (bed_in.at[:, rows], bed.at[:, rows]),
                ),
                sems,
                2 * part,
            )
        )
    if passing:
        passing.start()
    keep_west, keep_east, keep_south, keep_north = (
        jnp.where(flag(ctl, index), 1.0, 0.0)
        for index in (WALL_WEST, WALL_EAST, WALL_OUTER, WALL_OUTER + 1)
    )

    def strip(field, rows):
        if field == 3:
            return jnp.concatenate([bed[slot, rows, :] for slot in slots], 1)
        return jnp.concatenate([state[slot, field, rows, :] for slot in slots], 1)

    def blocks(value):
        return [value[:, k * LANES : (k + 1) * LANES] for k in range(4)]

    def right_of(value, end=None):
        turned = [pltpu.roll(part, LANES - 1, 1) for part in blocks(value)]
        after = turned[1:] + [turned[3] if end is None else end]
        return jnp.concatenate(
            [
                jnp.where(lane == LANES - 1, following, part)
                if following is not part
                else part
                for part, following in zip(turned, after)
            ],
            1,
        )

    def left_of(value, end):
        turned = [pltpu.roll(part, 1, 1) for part in blocks(value)]
        before = [end] + turned[:3]
        return jnp.concatenate(
            [jnp.where(lane == 0, previous, part) for part, previous in zip(turned, before)], 1
        )

    def down(value):
        return pltpu.roll(value, STRIP + 7, 0)[:STRIP]

    def group(index, carry):
        base = pl.multiple_of(index * STRIP, STRIP)
        rows = pl.ds(base, STRIP)
        after = pl.ds(pl.multiple_of(jnp.minimum(base + STRIP, TILE - 8), 8), 8)
        at_end = index == last
        fields = [
            jnp.concatenate([strip(field, rows), strip(field, after)], 0) for field in range(3)
        ]
        cells_x, cells_y = cell(*fields)
        here_x = tuple(value[:STRIP] for value in cells_x)
        here_y = tuple(value[:STRIP] for value in cells_y)

        ending = jnp.logical_and(row8 == 7, at_end)
        faces = list(face(here_x, tuple(down(value) for value in cells_x)))
        wall = keep_east * (2.0 * (here_x[3] + here_x[5] * here_x[1])[STRIP - 8 :])
        for component, value in enumerate((0.0, wall, 0.0)):
            upper = faces[component]
            faces[component] = jnp.concatenate(
                [upper[: STRIP - 8], jnp.where(ending, value, upper[STRIP - 8 :])], 0
            )
        turned = tuple(pltpu.roll(value, 1, 0) for value in faces)
        change_x = tuple(
            value - jnp.where(row_ids == 0, before, moved)
            for value, before, moved in zip(faces, carry[:3], turned)
        )
        ground = strip(3, rows)
        ground_after = jnp.where(
            at_end,
            jnp.broadcast_to(keep_east * ground[STRIP - 1 :], (8, width)),
            strip(3, after),
        )
        ground_up = pltpu.roll(ground, 1, 0)
        slope_x = down(jnp.concatenate([ground, ground_after], 0)) - jnp.where(
            row_ids == 0, carry[3], ground_up
        )
        carried = tuple(value[0:1, :] for value in turned) + (ground_up[0:1, :],)

        faces_y = list(face(here_y, tuple(right_of(value) for value in here_y)))
        normal = here_y[3]
        spread_y = here_y[5] * here_y[1]
        north = keep_north * (2.0 * (normal + spread_y)[:, width - LANES :])
        south = keep_south * (2.0 * (normal - spread_y)[:, :LANES])
        change_y = []
        for component, (high, low) in enumerate(((0.0, 0.0), (north, south), (0.0, 0.0))):
            parts = blocks(faces_y[component])
            parts[3] = jnp.where(lane == LANES - 1, high, parts[3])
            value = jnp.concatenate(parts, 1)
            change_y.append(value - left_of(value, low))
        slope_y = right_of(ground, keep_north * ground[:, width - LANES :]) - left_of(
            ground, keep_south * ground[:, :LANES]
        )
        weight = SLOPE * here_x[0]
        results = (
            SCALE * (change_x[0] + change_y[0]),
            SCALE * (change_x[1] + change_y[2]) + weight * slope_x,
            SCALE * (change_x[2] + change_y[1]) + weight * slope_y,
        )
        for field, value in enumerate(results):
            for position, slot in enumerate(slots):
                rate[slot, field, rows, :] = value[:, position * TILE : (position + 1) * TILE]
        return carried

    wait_all(incoming[0])
    top, _ = cell(*(strip(field, slice(0, 8)) for field in range(3)))
    nothing = jnp.zeros((1, width), jnp.float32)
    carry = (
        nothing,
        keep_west * (2.0 * (top[3] - top[5] * top[1])[0:1]),
        nothing,
        keep_west * strip(3, slice(0, 8))[0:1],
    )
    per_chunk = chunk // STRIP
    outgoing = []
    for part in range(CHUNKS):
        if part + 1 < CHUNKS:
            wait_all(incoming[part + 1])
        carry = lax.fori_loop(part * per_chunk, (part + 1) * per_chunk, group, carry)
        rows = slice(part * chunk, (part + 1) * chunk)
        outgoing += start_all(
            ((rate.at[:, :, rows], rate_out.at[:, :, rows]),), sems, 2 * CHUNKS + part
        )
        if passing and part == CHUNKS // 2:
            passing.middle()
    wait_all(outgoing)
    if passing:
        passing.end()


def moved_on(old, slopes, rough, delta, wet_now):
    h, hu, hv = (value - delta * slope for value, slope in zip(old, slopes))
    inverse = 1.0 / h
    u = hu * inverse
    v = hv * inverse
    speed = jnp.sqrt(u * u + v * v)
    power = jnp.exp((-4.0 / 3.0) * jnp.log(jnp.abs(h)))
    drag = (GRAVITY * delta) * (rough * rough) * (speed * power)
    factor = 1.0 / (1.0 + drag)
    fresh = (h, hu * factor, hv * factor)
    return tuple(jnp.where(wet_now, new, value) for new, value in zip(fresh, old))


def repeat_steps(ctl, wet_from, deltas, early, work, other, sems):
    incoming = []
    for ref in early:
        begin = 0 if ref is early[0] else early[0].shape[1]
        incoming += start_all(
            ((ref, work.at[:, begin : begin + ref.shape[1]]),), sems, len(incoming)
        )
    row_ids = lax.broadcasted_iota(jnp.int32, (AGAIN, TILE), 0)
    lane = lax.broadcasted_iota(jnp.int32, (AGAIN, LANES), 1)
    start = tuple(jnp.zeros((1, TILE), jnp.float32) for _ in range(4))

    def halves(value):
        return value[:, :LANES], value[:, LANES:]

    def right_of(value):
        low, high = (pltpu.roll(part, LANES - 1, 1) for part in halves(value))
        return jnp.concatenate([jnp.where(lane == LANES - 1, high, low), high], 1)

    def left_of(value):
        low, high = (pltpu.roll(part, 1, 1) for part in halves(value))
        return jnp.concatenate([low, jnp.where(lane == 0, low, high)], 1)

    def down(value):
        return pltpu.roll(value, AGAIN + 7, 0)[:AGAIN]

    for step in range(STEPS):
        source, target = (work, other) if step % 2 == 0 else (other, work)
        delta = deltas[step][0:1, :]
        wet_now = flag(ctl, wet_from + step)

        def group(index, carry, source=source, target=target, delta=delta, wet_now=wet_now):
            base = pl.multiple_of(index * AGAIN, AGAIN)
            rows = pl.ds(base, AGAIN)
            after = pl.ds(pl.multiple_of(jnp.minimum(base + AGAIN, EARLY - 8), 8), 8)
            refs = [source.at[field] for field in range(3)] + [work.at[3]]
            fields = [jnp.concatenate([ref[rows, :], ref[after, :]], 0) for ref in refs]
            cells_x, cells_y = cell(*fields[:3])
            here_x = tuple(value[:AGAIN] for value in cells_x)
            here_y = tuple(value[:AGAIN] for value in cells_y)
            faces_x = face(here_x, tuple(down(value) for value in cells_x))
            turned = tuple(pltpu.roll(value, 1, 0) for value in faces_x)
            change_x = tuple(
                value - jnp.where(row_ids == 0, before, moved)
                for value, before, moved in zip(faces_x, carry[:3], turned)
            )
            ground = fields[3][:AGAIN]
            ground_up = pltpu.roll(ground, 1, 0)
            slope_x = down(fields[3]) - jnp.where(row_ids == 0, carry[3], ground_up)
            carried = tuple(value[0:1, :] for value in turned) + (ground_up[0:1, :],)
            faces_y = face(here_y, tuple(right_of(value) for value in here_y))
            change_y = tuple(value - left_of(value) for value in faces_y)
            slope_y = right_of(ground) - left_of(ground)
            old = tuple(value[:AGAIN] for value in fields[:3])
            weight = SLOPE * old[0]
            slopes = (
                SCALE * (change_x[0] + change_y[0]),
                SCALE * (change_x[1] + change_y[2]) + weight * slope_x,
                SCALE * (change_x[2] + change_y[1]) + weight * slope_y,
            )
            for field, value in enumerate(
                moved_on(old, slopes, work[4, rows, :], delta, wet_now)
            ):
                target[field, rows, :] = value
            return carried

        if step == 0:
            wait_all(incoming)
        lax.fori_loop(0, EARLY // AGAIN, group, start)


def late_rows(tile, late):
    row = sublanes()
    kept = EARLY - 8
    lane = lax.broadcasted_iota(jnp.int32, (8, LANES), 1)
    for field in range(3):
        late[field, 0:8, :] = jnp.where(
            row < 3, tile[field, 0:8, :], tile[field, kept : kept + 8, :]
        )
        packed = [jnp.zeros((8, LANES), jnp.float32)] * 2
        for block in range(EARLY // 8):
            rows = slice(8 * block, 8 * block + 8)
            sides = jnp.where(lane < 64, tile[field, rows, :LANES], tile[field, rows, LANES:])
            turned = pltpu.roll(sides, (3 + 8 * block) % LANES, 1)
            which = block // 16
            packed[which] = jnp.where(lane // 8 == block % 16, turned, packed[which])
        late[field, 8:16, :] = jnp.concatenate(packed, 1)
        late[field, 16:, :] = tile[field, EARLY:, :]


def merge(late, rest, early, tile):
    for field in range(3):
        merge_field(field, late, rest, early, tile)


def merge_field(field, late, rest, early, tile):
    row = sublanes()
    lane = lax.broadcasted_iota(jnp.int32, (8, LANES), 1)
    first = late[field, 0:8, :]
    for block in range(EARLY // 8):
        rows = slice(8 * block, 8 * block + 8)
        which = block // 16
        packed = late[field, 8:16, which * LANES : (which + 1) * LANES]
        sides = pltpu.roll(packed, (-3 - 8 * block) % LANES, 1)
        value = early[field, rows, :]
        value = jnp.concatenate(
            [
                jnp.where(lane < 3, sides, value[:, :LANES]),
                jnp.where(lane >= LANES - 3, sides, value[:, LANES:]),
            ],
            1,
        )
        if block == 0:
            value = jnp.where(row < 3, first, value)
        if block == EARLY // 8 - 1:
            value = jnp.where(row < 5, value, first)
        tile[field, rows, :] = value
    tile[field, EARLY : TILE - HALF, :] = late[field, 16:, :]
    if rest is not None:
        tile[field, TILE - HALF :, :] = rest[field]


def repeat_second(
    ctl, delta0, delta1, delta2, low, high, late, rest, out, late_out, rest_out, work, tile, sems
):
    near = start_all(((late, late_out), (rest, rest_out)), sems, 2)
    repeat_steps(ctl, WET_SECOND, (delta0, delta1, delta2), (low, high), work, tile, sems)
    wait_all(start_all(((tile, out),), sems) + near)


def repeat_first(
    ctl, delta0, delta1, delta2, low, high, late_in, rest_in, staying, out,
    work, other, tile, late, rest, sems,
):
    kept = out.at[1 - ctl[MOVE + 1]]
    again = ctl[MOVE] == ctl[MOVE + 1]

    @pl.when(again)
    def _():
        wait_all(start_all(((staying, tile),), sems))

    @pl.when(jnp.logical_not(again))
    def _():
        copies = start_all(((late_in, late), (rest_in, rest)), sems, 2)
        repeat_steps(ctl, WET_FIRST, (delta0, delta1, delta2), (low, high), work, other, sems)
        wait_all(copies)
        merge(late, rest, other, tile)

    wait_all(start_all(((tile, kept),), sems))


def finish_late(ctl, late, early, before, out, tile, sems):
    del before
    copies = []
    for field in range(3):
        merge_field(field, late, None, early, tile)
        copies += start_all(
            ((tile.at[field], out.at[ctl[MOVE + 1], field, 0 : TILE - HALF]),), sems, field
        )
    wait_all(copies)


def finish_rest(ctl, rest, before, out, sems):
    del before
    wait_all(start_all(((rest, out.at[ctl[MOVE + 1], :, TILE - HALF :]),), sems))


def second_late(ctl, arrived, own, order, leaving):
    del order
    again = ctl[MOVE] == ctl[MOVE + 1]
    for field in range(3):
        leaving[field] = jnp.where(again, arrived[field], own[field])


def correct_rows(ctl, slot, got, ground, state, rate, bottom):
    position = jnp.where(ctl[SLOT_LOW] == slot, 0, 1)
    device = lax.axis_index("xb") * 2 + lax.axis_index("yb")
    wall = WALL_WEST if bottom else WALL_EAST

    @pl.when(jnp.logical_not(flag(ctl, wall + position)))
    def _():
        peer = device - 2 if bottom else device + 2
        block = pl.ds(pl.multiple_of(peer * 8, 8), 8)
        lines = got[block, :TILE]
        grounds = ground[block, :TILE]
        stride = 4 if got.shape[1] > TILE else 3

        def line(offset):
            other = offset + stride
            picked = jnp.where(
                position == 0, lines[offset : offset + 1, :], lines[other : other + 1, :]
            )
            return jnp.broadcast_to(picked, (8, TILE))

        ghost, _ = cell(*(line(field) for field in range(3)))
        ghost_ground = jnp.where(position == 0, grounds[3:4, :], grounds[7:8, :])
        rows = slice(0, 8) if bottom else slice(TILE - 8, TILE)
        own = [state[slot, field, rows, :] for field in range(3)]
        here, _ = cell(*own)
        fluxes = face(ghost, here) if bottom else face(here, ghost)
        push = SCALE * fluxes[1] + (SLOPE * own[0]) * ghost_ground
        row = sublanes()
        sign = -1.0 if bottom else 1.0
        chosen = row == (0 if bottom else 7)
        for field, value in enumerate((SCALE * fluxes[0], push, SCALE * fluxes[2])):
            rate[slot, field, rows, :] += jnp.where(chosen, sign * value, 0.0)


def column_fix(got, ground, columns):
    upper = lax.axis_index("yb")
    device = lax.axis_index("xb") * 2 + upper
    peer = device + 1 - 2 * upper
    block = pl.ds(pl.multiple_of(peer * 8, 8), 8)
    lines = got[block, :TILE]
    ghost_ground = ground[block, :TILE][3:4]
    mine = columns[...]
    _, ghost = cell(lines[0:1], lines[1:2], lines[2:3])
    _, own = cell(mine[0:1], mine[1:2], mine[2:3])
    low = upper == 0
    left = tuple(jnp.where(low, a, b) for a, b in zip(own, ghost))
    right = tuple(jnp.where(low, b, a) for a, b in zip(own, ghost))
    fluxes = face(left, right)
    sign = jnp.where(low, 1.0, -1.0)
    push = SCALE * fluxes[1] + (SLOPE * mine[0:1]) * ghost_ground
    block8 = stacked(
        [sign * SCALE * fluxes[0], sign * SCALE * fluxes[2], sign * push],
        jnp.zeros((8, TILE), jnp.float32),
    )
    return jnp.transpose(
        jnp.concatenate([block8, jnp.zeros((LANES - 8, TILE), jnp.float32)], 0)
    )


def last_update(ctl, got, ground, columns, state, manning, rate, order, *rest):
    del order
    slots = ctl[MOVE], 1 - ctl[MOVE]
    update(STEPS - 1, ctl, got, ground, columns, state, manning, rate, *rest, slots=slots)


def update(
    step, ctl, got_in, ground_in, columns_in, state_in, manning_in, rate_in, *rest,
    passing=None, slots=(0, 1),
):
    more = step + 1 < STEPS
    fresh_out, *lines_to, delta_out = rest[: 4 if more else 6]
    rest = rest[4 if more else 6 :]
    state, manning, rate, fresh, got, ground, columns, first, second, delta_keep, sems = rest
    out, columns_out = first, second
    small = start_all(
        ((got_in, got), (ground_in, ground), (columns_in, columns)), sems, 5 * PARTS
    )
    size = 2 * TILE // PARTS
    parts = [
        (slot, slice(k * size, (k + 1) * size)) for slot in slots for k in range(PARTS // 2)
    ]
    incoming = []
    for index, (slot, rows) in enumerate(parts):
        incoming.append(
            start_all(
                (
                    (rate_in.at[slot, :, rows], rate.at[slot, :, rows]),
                    (state_in.at[slot, :, rows], state.at[slot, :, rows]),
                    (manning_in.at[slot, rows], manning.at[slot, rows]),
                ),
                sems,
                3 * index,
            )
        )
    wait_all(small)
    upper = lax.axis_index("yb")
    devices = 2 * lax.axis_size("xb")
    begin = TILE if got.shape[1] > TILE else 0
    tops = got[0:8, begin : begin + LANES]
    for peer in range(1, devices):
        tops = jnp.maximum(tops, got[peer * 8 : peer * 8 + 8, begin : begin + LANES])
    delta = (COURANT * SPACING) / tops[TOP : TOP + 1, :]
    delta = jnp.concatenate([delta, delta], 1)
    delta_keep[...] = jnp.broadcast_to(delta, (8, TILE))
    outgoing = start_all(((delta_keep, delta_out),), sems, 5 * PARTS + 3)
    fix = column_fix(got, ground, columns)
    facing = jnp.where(upper > 0, ctl[SLOT_LOW], 1 - ctl[SLOT_LOW])
    begin = pl.multiple_of((1 - upper) * LANES, LANES)
    goal = (1 - upper) * (LANES - 1)
    lane = lax.broadcasted_iota(jnp.int32, (size, LANES), 1)
    total = jnp.zeros((ROWS, TILE), jnp.float32)
    for index, (slot, part_rows) in enumerate(parts):
        wait_all(incoming[index])
        if part_rows.start == 0:
            correct_rows(ctl, slot, got, ground, state, rate, True)
        if part_rows.stop == TILE:
            correct_rows(ctl, slot, got, ground, state, rate, False)

        @pl.when(facing == slot)
        def _(slot=slot, part_rows=part_rows):
            for field in range(3):
                turned = pltpu.roll(
                    fix[part_rows], lax.rem(goal + LANES - field, LANES), 1
                )
                rate[slot, field, part_rows, pl.ds(begin, LANES)] += jnp.where(
                    lane == goal, turned, 0.0
                )

        wet_now = flag(ctl, WET + 2 * step + slot)

        def group(index, best, slot=slot, wet_now=wet_now):
            rows = pl.ds(pl.multiple_of(index * ROWS, ROWS), ROWS)
            old = tuple(state[slot, field, rows, :] for field in range(3))
            slopes = tuple(rate[slot, field, rows, :] for field in range(3))
            h, hu, hv = moved_on(old, slopes, manning[slot, rows, :], delta, wet_now)
            fresh[slot, 0, rows, :] = h
            fresh[slot, 1, rows, :] = hu
            fresh[slot, 2, rows, :] = hv
            if more:
                along_x, along_y = cell(h, hu, hv)
                best = jnp.maximum(best, jnp.maximum(along_x[5], along_y[5]))
            return best

        best = lax.fori_loop(
            part_rows.start // ROWS,
            part_rows.stop // ROWS,
            group,
            jnp.zeros((ROWS, TILE), jnp.float32),
        )
        if more:
            best = jnp.where(flag(ctl, WET + 2 * step + 2 + slot), best, 0.0)
            total = jnp.maximum(total, best)
        if more:
            outgoing += start_all(
                ((fresh.at[slot, :, part_rows], fresh_out.at[slot, :, part_rows]),),
                sems,
                3 * PARTS + index,
            )
        elif index >= PARTS // 2:
            outgoing += start_all(
                ((fresh.at[slot, :, part_rows], fresh_out.at[:, part_rows]),),
                sems,
                3 * PARTS + index,
            )
        if not more and part_rows.stop == TILE:
            late, low, high = (
                (first, *lines_to[:2]) if index < PARTS // 2 else (second, *lines_to[2:])
            )
            late_rows(fresh.at[slot], late)
            outgoing += start_all(
                ((late.at[:, :HALF], low), (late.at[:, HALF:], high)),
                sems,
                4 * PARTS + (0 if index < PARTS // 2 else 2),
            )
        if passing and index == PARTS // 2:
            passing.middle()
    if more:
        messages(ctl, fresh, None, jnp.max(total, keepdims=True), out, columns_out)
        pairs = zip((out, columns_out), lines_to)
        outgoing += start_all(tuple(pairs), sems, 4 * PARTS)
    wait_all(outgoing)


def vmem():
    return pl.BlockSpec(memory_space=pltpu.VMEM)


def smem():
    return pl.BlockSpec(memory_space=pltpu.SMEM)


def hbm():
    return pl.BlockSpec(memory_space=pltpu.HBM)


def anywhere():
    return pl.BlockSpec(memory_space=pl.ANY)


def call(
    kernel, outs, out_specs, in_specs, flops, scratch=(), aliases=None, room=VMEM_BYTES, moved=4
):
    return pl.pallas_call(
        kernel,
        scratch_shapes=scratch,
        input_output_aliases=aliases or {},
        out_shape=outs,
        in_specs=in_specs,
        out_specs=out_specs,
        compiler_params=pltpu.CompilerParams(vmem_limit_bytes=room),
        cost_estimate=pl.CostEstimate(flops=flops, bytes_accessed=moved << 20, transcendentals=0),
    )


def f32(*shape):
    return jax.ShapeDtypeStruct(shape, jnp.float32)


def spread(fast):
    return lax.all_to_all(fast, ("xb", "yb"), split_axis=0, concat_axis=0, tiled=True)


def body(state, bed, manning, neighbours, wet, moves):
    shape = f32(*state.shape)
    devices = lax.axis_size("xb") * lax.axis_size("yb")
    whole = pltpu.VMEM(state.shape, jnp.float32)
    part = pltpu.VMEM(bed.shape, jnp.float32)
    tile_shape = f32(*state.shape[1:])
    early_shape = f32(5, EARLY, TILE)
    early_state = f32(3, EARLY, TILE)
    late_shape = f32(3, LATE, TILE)
    half_shape = f32(3, HALF, TILE)
    delta_shape = f32(8, TILE)

    def buffer(like):
        return pltpu.VMEM(like.shape, jnp.float32)

    piece_shapes = tuple(f32(5, end - begin, TILE) for begin, end in PIECES)
    out, columns, ctl = call(
        opening,
        (
            f32(8 * devices, TILE + LANES),
            f32(8, TILE),
            jax.ShapeDtypeStruct((CONTROLS,), jnp.int32),
        ),
        (vmem(), vmem(), smem()),
        [hbm()] * 5,
        4 << 20,
        [
            whole,
            part,
            pltpu.SMEM(neighbours.shape[::-1], jnp.int32),
            pltpu.SMEM(wet.shape, jnp.int32),
            pltpu.SMEM(moves.shape, jnp.int32),
            pltpu.SemaphoreType.DMA((6,)),
        ],
    )(state, bed, neighbours.T, wet, moves)
    state_first = state
    ground = None
    deltas = []
    for step in range(STEPS):
        got = spread(out)
        ground = got if step == 0 else ground
        scratch = [whole, part, whole, pltpu.SemaphoreType.DMA((3 * CHUNKS,))]
        piece_scratch = [
            [buffer(piece), pltpu.SemaphoreType.DMA((2,))] for piece in piece_shapes
        ]
        if step == 1:
            rate, leaving = call(
                rates_and_leaving,
                (shape, piece_shapes[0]),
                (hbm(),) * 2,
                [smem()] + [hbm()] * 5,
                16 << 20,
                scratch + piece_scratch[0],
            )(ctl, state, bed, state_first, manning, early_first[0])
            early_second = [shifted(leaving, "xb", 1)]
        elif step == 2:
            rate = call(rates_after, shape, hbm(), [smem()] + [hbm()] * 3, 16 << 20, scratch)(
                ctl, state, bed, early_second[0]
            )
        else:
            rate, *leaving = call(
                rates_and_splitting,
                (shape,) + piece_shapes,
                (hbm(),) * 3,
                [smem()] + [hbm()] * 3,
                16 << 20,
                scratch + [buffer(early_shape), pltpu.SemaphoreType.DMA((5,))],
            )(ctl, state, bed, manning)
            held = call(
                hold, piece_shapes[0], hbm(), [hbm()] * 3, 1 << 10, aliases={2: 0}
            )(rate, got, leaving[0])
            early_first = [shifted(held, "xb", 1)]
        more = step + 1 < STEPS
        shapes = (f32(8 * devices, TILE), f32(8, TILE)) if more else (half_shape,) * 4
        passing = step == 1
        work = [
            whole,
            part,
            whole,
            whole,
            pltpu.VMEM(got.shape, jnp.float32),
            pltpu.VMEM(ground.shape, jnp.float32),
            pltpu.VMEM((8, TILE), jnp.float32),
            buffer(shapes[0] if more else late_shape),
            buffer(shapes[1] if more else late_shape),
            buffer(delta_shape),
            pltpu.SemaphoreType.DMA((5 * PARTS + 4,)),
        ]
        operands = ctl, got, ground, columns, state, manning, rate
        if not more:
            break
        outs = call(
            functools.partial(update_and_leaving if passing else update, step),
            (shape,) + shapes + (delta_shape,) + ((piece_shapes[1],) if passing else ()),
            (hbm(),) * (5 if passing else 4),
            [smem()] + [hbm()] * (9 if passing else 6),
            8 << 20,
            work + (piece_scratch[1] if passing else []),
            moved=10,
        )(*operands, *((state_first, bed, early_first[1]) if passing else ()))
        state, out, columns, delta, *passed = outs
        deltas.append(delta)
        if step == 0:
            held = call(
                hold, piece_shapes[1], hbm(), [hbm()] * 3, 1 << 10, aliases={2: 0}
            )(delta, delta, leaving[1])
            early_first.append(shifted(held, "xb", 1))
        elif step == 1:
            early_second.append(shifted(passed[0], "xb", 1))

    staying, late_first, rest_first, late_second, rest_second, delta = call(
        last_update,
        (tile_shape,) + shapes + (delta_shape,),
        (hbm(),) * 6,
        [smem()] + [hbm()] * 7,
        8 << 20,
        work,
        moved=10,
    )(*operands, early_second[1])
    deltas.append(delta)
    room = 16 << 20
    late_arrived = shifted(late_first, "xb", 1)
    rest_arrived = shifted(rest_first, "xb", 1)
    second, late_second, rest_second = call(
        repeat_second,
        (early_state, half_shape, half_shape),
        (anywhere(), vmem(), vmem()),
        [smem()] + [vmem()] * 3 + [anywhere()] * 4,
        8 << 20,
        [buffer(early_shape), buffer(early_state), pltpu.SemaphoreType.DMA((4,))],
        room=room,
    )(ctl, *deltas, *early_second, late_second, rest_second)

    def pass_late(arrived, own):
        leaving = call(
            second_late,
            half_shape,
            vmem(),
            [smem(), vmem(), vmem(), anywhere()],
            1 << 10,
            room=room,
        )(ctl, arrived, own, second)
        return shifted(leaving, "xb", 1)

    late_next = pass_late(late_arrived, late_second)
    rest_next = pass_late(rest_arrived, rest_second)
    final = call(
        repeat_first,
        shape,
        hbm(),
        [smem()] + [vmem()] * 3 + [anywhere()] * 5,
        8 << 20,
        [
            buffer(early_shape),
            buffer(early_state),
            buffer(tile_shape),
            buffer(half_shape),
            buffer(half_shape),
            pltpu.SemaphoreType.DMA((4,)),
        ],
        room=room,
    )(ctl, *deltas, *early_first, late_arrived, rest_arrived, staying)
    final = call(
        finish_late,
        shape,
        hbm(),
        [smem(), vmem(), vmem(), hbm()],
        1 << 20,
        [pltpu.VMEM((3, TILE - HALF, TILE), jnp.float32), pltpu.SemaphoreType.DMA((3,))],
        {3: 0},
        room=room,
    )(ctl, late_next, second, final)
    return call(
        finish_rest,
        shape,
        hbm(),
        [smem(), vmem(), hbm()],
        1 << 20,
        [pltpu.SemaphoreType.DMA((1,))],
        {2: 0},
        room=room,
    )(ctl, rest_next, final)


def solution(mesh):
    placed = (
        P(("runs", "xb", "yb"), None, None, None),
        P(("runs", "xb", "yb"), None, None),
        P(("runs", "xb", "yb"), None, None),
        P("runs", None),
        P(None, "runs"),
        P(None, "runs"),
    )
    return jax.shard_map(
        body,
        mesh=mesh,
        in_specs=placed,
        out_specs=P(("runs", "xb", "yb"), None, None, None),
        check_vma=False,
    )
```

```python
import functools

import jax
import jax.numpy as jnp
from jax import lax
from jax.experimental import pallas as pl
from jax.experimental.pallas import tpu as pltpu
from jax.sharding import PartitionSpec as P

STEPS = 3
GRAVITY = 9.81
ROOT_G = GRAVITY**0.5
SPACING = 5.0
COURANT = 0.2
ROWS = 64
LANES = 128
TILE = 256
VMEM_BYTES = 60 * 1024 * 1024
SLOT_LOW, WALL_WEST, WALL_EAST, WALL_OUTER, WET, MOVE = 0, 1, 3, 5, 7, 13
WET_FIRST, WET_SECOND = 16, 19
CONTROLS = 24
EARLY = 128
PIECES = ((0, 64), (64, 128))
AGAIN = 64
LATE = TILE - EARLY + 16
HALF = LATE // 2
CHUNKS = 8
PARTS = 4
STRIP = 32
TOP = 6
SCALE = 0.5 / SPACING
SLOPE = GRAVITY / (2.0 * SPACING)


def shifted(value, axis, steps, around=True):
    count = lax.axis_size(axis)
    pairs = [(source, (source + steps) % count) for source in range(count)]
    if not around:
        pairs = [pair for pair in pairs if abs(pair[0] - pair[1]) == abs(steps)]
    return lax.ppermute(value, axis, pairs)


def cell(h, hu, hv):
    root = lax.rsqrt(h)
    inverse = root * root
    u = hu * inverse
    v = hv * inverse
    celerity = ROOT_G * (h * root)
    pressure = (0.5 * GRAVITY) * (h * h)
    cross = hu * v
    speed_x = jnp.abs(u) + celerity
    speed_y = jnp.abs(v) + celerity
    along_x = (h, hu, hv, hu * u + pressure, cross, speed_x)
    along_y = (h, hv, hu, hv * v + pressure, cross, speed_y)
    return along_x, along_y


def face(left, right):
    wave = jnp.maximum(left[5], right[5])
    return (
        (left[1] + right[1]) - wave * (right[0] - left[0]),
        (left[3] + right[3]) - wave * (right[1] - left[1]),
        (left[4] + right[4]) - wave * (right[2] - left[2]),
    )


def slot_of(ctl, position):
    low = ctl[SLOT_LOW]
    return low if position == 0 else 1 - low


def flag(ctl, index):
    return ctl[index] > 0


def start_all(pairs, sems, first=0):
    copies = [
        pltpu.make_async_copy(src, dst, sems.at[first + k]) for k, (src, dst) in enumerate(pairs)
    ]
    for copy in copies:
        copy.start()
    return copies


def wait_all(copies):
    for copy in copies:
        copy.wait()


def sublanes(width=TILE):
    return lax.broadcasted_iota(jnp.int32, (8, width), 0)


def stacked(lines, base):
    row = sublanes()
    for index, line in enumerate(lines):
        base = jnp.where(row == index, jnp.broadcast_to(line, (8, TILE)), base)
    return base


def messages(ctl, state, bed, fastest, out, columns):
    upper = lax.axis_index("yb")
    column = lax.axis_index("xb")
    last = lax.axis_size("xb") - 1
    devices = 2 * (last + 1)
    device = column * 2 + upper
    top = jnp.broadcast_to(fastest, (8, TILE))
    for peer in range(devices):
        out[peer * 8 : peer * 8 + 8, :TILE] = top
        if bed is not None:
            out[peer * 8 : peer * 8 + 8, TILE:] = top[:, :LANES]
    row = sublanes()

    def edge(line):
        rows = slice(line, line + 1)
        lines = []
        for position in range(2):
            slot = slot_of(ctl, position)
            lines += [state[slot, field, rows, :] for field in range(3)]
            if bed is not None:
                lines.append(bed[slot, rows, :])
        return stacked(lines, top)

    for inside, peer, line in (
        (column > 0, device - 2, 0),
        (column < last, device + 2, TILE - 1),
    ):

        @pl.when(inside)
        def _(peer=peer, line=line):
            out[pl.ds(pl.multiple_of(peer * 8, 8), 8), :TILE] = edge(line)

    slot = jnp.where(upper > 0, ctl[SLOT_LOW], 1 - ctl[SLOT_LOW])
    begin = pl.multiple_of((1 - upper) * LANES, LANES)
    lane = lax.broadcasted_iota(jnp.int32, (TILE, LANES), 1)
    packed = None
    for field in range(4 if bed is not None else 3):
        if field < 3:
            part = state[slot, field, :, pl.ds(begin, LANES)]
        else:
            part = bed[slot, :, pl.ds(begin, LANES)]
        turned = pltpu.roll(part, field + 1 - upper, 1)
        packed = turned if field == 0 else jnp.where(lane == field, turned, packed)
    lines = jnp.transpose(packed)[:8]
    columns[...] = lines
    start = pl.multiple_of((device + 1 - 2 * upper) * 8, 8)
    out[pl.ds(start, 8), :TILE] = jnp.where(row == TOP, top, lines)


def opening(
    state_in, bed_in, neighbours_in, wet_in, moves_in,
    out, columns, ctl,
    state, bed, neighbours, wet, moves, sems,
):
    copies = start_all(
        (
            (neighbours_in, neighbours),
            (wet_in, wet),
            (moves_in, moves),
            (state_in.at[0], state.at[0]),
            (state_in.at[1], state.at[1]),
            (bed_in, bed),
        ),
        sems,
    )
    device = lax.axis_index("xb") * 2 + lax.axis_index("yb")
    wait_all(copies[:3])
    first = device * 2
    low = jnp.where(neighbours[3, first] == first + 1, 0, 1)
    ctl[SLOT_LOW] = low
    for position in range(2):
        slot = low if position == 0 else 1 - low
        tile = first + slot
        ctl[WALL_WEST + position] = (neighbours[0, tile] < 0).astype(jnp.int32)
        ctl[WALL_EAST + position] = (neighbours[1, tile] < 0).astype(jnp.int32)
        ctl[WALL_OUTER + position] = (neighbours[2 + position, tile] < 0).astype(jnp.int32)
    for step in range(STEPS):
        for slot in range(2):
            ctl[WET + 2 * step + slot] = wet[step, first + slot]
        ctl[MOVE + step] = moves[step, device]
    count = lax.axis_size("xb")
    upper = lax.axis_index("yb")
    column = lax.axis_index("xb")
    source = lax.rem(column + count - 1, count) * 2 + upper
    before = lax.rem(column + count - 2, count) * 2 + upper
    again = moves[0, source] == moves[1, source]
    tile_first = source * 2 + moves[0, source]
    tile_second = jnp.where(
        again, before * 2 + moves[0, before], source * 2 + 1 - moves[0, source]
    )
    for step in range(STEPS):
        ctl[WET_FIRST + step] = wet[step, tile_first]
        ctl[WET_SECOND + step] = wet[step, tile_second]

    total = jnp.zeros((ROWS, TILE), jnp.float32)
    for slot in range(2):
        copies[3 + slot].wait()

        def group(index, best, slot=slot):
            rows = pl.ds(pl.multiple_of(index * ROWS, ROWS), ROWS)
            along_x, along_y = cell(*(state[slot, field, rows, :] for field in range(3)))
            return jnp.maximum(best, jnp.maximum(along_x[5], along_y[5]))

        best = lax.fori_loop(0, TILE // ROWS, group, jnp.zeros((ROWS, TILE), jnp.float32))
        total = jnp.maximum(total, jnp.where(wet[0, first + slot] > 0, best, 0.0))
    copies[5].wait()
    messages(ctl, state, bed, jnp.max(total, keepdims=True), out, columns)


def hold(first, second, leaving, same):
    del first, second, leaving, same


class Splitting:
    def __init__(self, ctl, state_in, bed_in, manning_in, leaving, buffer, sems):
        slot = ctl[MOVE]
        rows = slice(0, EARLY)
        pairs = (
            (state_in.at[slot, :, rows], buffer.at[0:3]),
            (bed_in.at[slot, rows], buffer.at[3]),
            (manning_in.at[slot, rows], buffer.at[4]),
        )
        self.incoming = [
            pltpu.make_async_copy(src, dst, sems.at[k]) for k, (src, dst) in enumerate(pairs)
        ]
        self.outgoing = [
            pltpu.make_async_copy(buffer.at[:, begin:end], piece, sems.at[3 + k])
            for k, ((begin, end), piece) in enumerate(zip(PIECES, leaving))
        ]

    def start(self):
        for copy in self.incoming:
            copy.start()

    def middle(self):
        wait_all(self.incoming)
        for copy in self.outgoing:
            copy.start()

    def end(self):
        wait_all(self.outgoing)


class Passing:
    def __init__(self, ctl, piece, state_in, bed_in, manning_in, arrived, leaving, buffer, sems):
        self.again = ctl[MOVE] == ctl[MOVE + 1]
        self.other = 1 - ctl[MOVE]
        self.rows = slice(*piece)
        self.refs = state_in, bed_in, manning_in
        self.incoming = pltpu.make_async_copy(arrived, buffer, sems.at[0])
        self.outgoing = pltpu.make_async_copy(buffer, leaving, sems.at[1])
        self.buffer = buffer
        self.sem = sems.at[0]

    def start(self):
        state_in, bed_in, manning_in = self.refs
        buffer, sem, rows = self.buffer, self.sem, self.rows

        @pl.when(self.again)
        def _():
            self.incoming.start()

        @pl.when(jnp.logical_not(self.again))
        def _():
            pltpu.make_async_copy(state_in.at[self.other, :, rows], buffer.at[0:3], sem).start()
            pltpu.make_async_copy(bed_in.at[self.other, rows], buffer.at[3], sem).start()
            pltpu.make_async_copy(manning_in.at[self.other, rows], buffer.at[4], sem).start()

    def middle(self):
        self.incoming.wait()
        self.outgoing.start()

    def end(self):
        self.outgoing.wait()


def rates_and_splitting(
    ctl, state_in, bed_in, manning_in, rate_out, leaving_low, leaving_high,
    state, bed, rate, sems, buffer, moving,
):
    leaving = leaving_low, leaving_high
    splitting = Splitting(ctl, state_in, bed_in, manning_in, leaving, buffer, moving)
    rates(ctl, state_in, bed_in, rate_out, state, bed, rate, sems, splitting)


def rates_and_leaving(
    ctl, state_in, bed_in, state_first, manning_in, arrived, rate_out, leaving,
    state, bed, rate, sems, buffer, moving,
):
    passing = Passing(
        ctl, PIECES[0], state_first, bed_in, manning_in, arrived, leaving, buffer, moving
    )
    rates(ctl, state_in, bed_in, rate_out, state, bed, rate, sems, passing)


def update_and_leaving(
    step, ctl, got_in, ground_in, columns_in, state_in, manning_in, rate_in,
    state_first, bed_in, arrived, fresh_out, first_out, second_out, delta_out, leaving, *rest
):
    *rest, buffer, moving = rest
    passing = Passing(
        ctl, PIECES[1], state_first, bed_in, manning_in, arrived, leaving, buffer, moving
    )
    passing.start()
    update(
        step, ctl, got_in, ground_in, columns_in, state_in, manning_in, rate_in,
        fresh_out, first_out, second_out, delta_out, *rest, passing=passing,
    )
    passing.end()


def rates_after(ctl, state_in, bed_in, order, *rest):
    del order
    rates(ctl, state_in, bed_in, *rest)


def rates(ctl, state_in, bed_in, rate_out, state, bed, rate, sems, passing=None):
    width = 2 * TILE
    row_ids = lax.broadcasted_iota(jnp.int32, (STRIP, width), 0)
    row8 = sublanes(width)
    lane = lax.broadcasted_iota(jnp.int32, (STRIP, LANES), 1)
    last = TILE // STRIP - 1
    chunk = TILE // CHUNKS
    slots = [slot_of(ctl, position) for position in range(2)]
    incoming = []
    for part in range(CHUNKS):
        rows = slice(part * chunk, (part + 1) * chunk)
        incoming.append(
            start_all(
                (
                    (state_in.at[:, :, rows], state.at[:, :, rows]),
                    (bed_in.at[:, rows], bed.at[:, rows]),
                ),
                sems,
                2 * part,
            )
        )
    if passing:
        passing.start()
    keep_west, keep_east, keep_south, keep_north = (
        jnp.where(flag(ctl, index), 1.0, 0.0)
        for index in (WALL_WEST, WALL_EAST, WALL_OUTER, WALL_OUTER + 1)
    )

    def strip(field, rows):
        if field == 3:
            return jnp.concatenate([bed[slot, rows, :] for slot in slots], 1)
        return jnp.concatenate([state[slot, field, rows, :] for slot in slots], 1)

    def blocks(value):
        return [value[:, k * LANES : (k + 1) * LANES] for k in range(4)]

    def right_of(value, end=None):
        turned = [pltpu.roll(part, LANES - 1, 1) for part in blocks(value)]
        after = turned[1:] + [turned[3] if end is None else end]
        return jnp.concatenate(
            [
                jnp.where(lane == LANES - 1, following, part)
                if following is not part
                else part
                for part, following in zip(turned, after)
            ],
            1,
        )

    def left_of(value, end):
        turned = [pltpu.roll(part, 1, 1) for part in blocks(value)]
        before = [end] + turned[:3]
        return jnp.concatenate(
            [jnp.where(lane == 0, previous, part) for part, previous in zip(turned, before)], 1
        )

    def down(value):
        return pltpu.roll(value, STRIP + 7, 0)[:STRIP]

    def group(index, carry):
        base = pl.multiple_of(index * STRIP, STRIP)
        rows = pl.ds(base, STRIP)
        after = pl.ds(pl.multiple_of(jnp.minimum(base + STRIP, TILE - 8), 8), 8)
        at_end = index == last
        fields = [
            jnp.concatenate([strip(field, rows), strip(field, after)], 0) for field in range(3)
        ]
        cells_x, cells_y = cell(*fields)
        here_x = tuple(value[:STRIP] for value in cells_x)
        here_y = tuple(value[:STRIP] for value in cells_y)

        ending = jnp.logical_and(row8 == 7, at_end)
        faces = list(face(here_x, tuple(down(value) for value in cells_x)))
        wall = keep_east * (2.0 * (here_x[3] + here_x[5] * here_x[1])[STRIP - 8 :])
        for component, value in enumerate((0.0, wall, 0.0)):
            upper = faces[component]
            faces[component] = jnp.concatenate(
                [upper[: STRIP - 8], jnp.where(ending, value, upper[STRIP - 8 :])], 0
            )
        turned = tuple(pltpu.roll(value, 1, 0) for value in faces)
        change_x = tuple(
            value - jnp.where(row_ids == 0, before, moved)
            for value, before, moved in zip(faces, carry[:3], turned)
        )
        ground = strip(3, rows)
        ground_after = jnp.where(
            at_end,
            jnp.broadcast_to(keep_east * ground[STRIP - 1 :], (8, width)),
            strip(3, after),
        )
        ground_up = pltpu.roll(ground, 1, 0)
        slope_x = down(jnp.concatenate([ground, ground_after], 0)) - jnp.where(
            row_ids == 0, carry[3], ground_up
        )
        carried = tuple(value[0:1, :] for value in turned) + (ground_up[0:1, :],)

        faces_y = list(face(here_y, tuple(right_of(value) for value in here_y)))
        normal = here_y[3]
        spread_y = here_y[5] * here_y[1]
        north = keep_north * (2.0 * (normal + spread_y)[:, width - LANES :])
        south = keep_south * (2.0 * (normal - spread_y)[:, :LANES])
        change_y = []
        for component, (high, low) in enumerate(((0.0, 0.0), (north, south), (0.0, 0.0))):
            parts = blocks(faces_y[component])
            parts[3] = jnp.where(lane == LANES - 1, high, parts[3])
            value = jnp.concatenate(parts, 1)
            change_y.append(value - left_of(value, low))
        slope_y = right_of(ground, keep_north * ground[:, width - LANES :]) - left_of(
            ground, keep_south * ground[:, :LANES]
        )
        weight = SLOPE * here_x[0]
        results = (
            SCALE * (change_x[0] + change_y[0]),
            SCALE * (change_x[1] + change_y[2]) + weight * slope_x,
            SCALE * (change_x[2] + change_y[1]) + weight * slope_y,
        )
        for field, value in enumerate(results):
            for position, slot in enumerate(slots):
                rate[slot, field, rows, :] = value[:, position * TILE : (position + 1) * TILE]
        return carried

    wait_all(incoming[0])
    top, _ = cell(*(strip(field, slice(0, 8)) for field in range(3)))
    nothing = jnp.zeros((1, width), jnp.float32)
    carry = (
        nothing,
        keep_west * (2.0 * (top[3] - top[5] * top[1])[0:1]),
        nothing,
        keep_west * strip(3, slice(0, 8))[0:1],
    )
    per_chunk = chunk // STRIP
    outgoing = []
    for part in range(CHUNKS):
        if part + 1 < CHUNKS:
            wait_all(incoming[part + 1])
        carry = lax.fori_loop(part * per_chunk, (part + 1) * per_chunk, group, carry)
        rows = slice(part * chunk, (part + 1) * chunk)
        outgoing += start_all(
            ((rate.at[:, :, rows], rate_out.at[:, :, rows]),), sems, 2 * CHUNKS + part
        )
        if passing and part == CHUNKS // 2:
            passing.middle()
    wait_all(outgoing)
    if passing:
        passing.end()


def moved_on(old, slopes, rough, delta, wet_now):
    h, hu, hv = (value - delta * slope for value, slope in zip(old, slopes))
    inverse = 1.0 / h
    u = hu * inverse
    v = hv * inverse
    speed = jnp.sqrt(u * u + v * v)
    power = jnp.exp((-4.0 / 3.0) * jnp.log(jnp.abs(h)))
    drag = (GRAVITY * delta) * (rough * rough) * (speed * power)
    factor = 1.0 / (1.0 + drag)
    fresh = (h, hu * factor, hv * factor)
    return tuple(jnp.where(wet_now, new, value) for new, value in zip(fresh, old))


def repeat_steps(ctl, wet_from, deltas, early, work, other, sems):
    incoming = []
    for ref in early:
        begin = 0 if ref is early[0] else early[0].shape[1]
        incoming += start_all(
            ((ref, work.at[:, begin : begin + ref.shape[1]]),), sems, len(incoming)
        )
    row_ids = lax.broadcasted_iota(jnp.int32, (AGAIN, TILE), 0)
    lane = lax.broadcasted_iota(jnp.int32, (AGAIN, LANES), 1)
    start = tuple(jnp.zeros((1, TILE), jnp.float32) for _ in range(4))

    def halves(value):
        return value[:, :LANES], value[:, LANES:]

    def right_of(value):
        low, high = (pltpu.roll(part, LANES - 1, 1) for part in halves(value))
        return jnp.concatenate([jnp.where(lane == LANES - 1, high, low), high], 1)

    def left_of(value):
        low, high = (pltpu.roll(part, 1, 1) for part in halves(value))
        return jnp.concatenate([low, jnp.where(lane == 0, low, high)], 1)

    def down(value):
        return pltpu.roll(value, AGAIN + 7, 0)[:AGAIN]

    for step in range(STEPS):
        source, target = (work, other) if step % 2 == 0 else (other, work)
        delta = deltas[step][0:1, :]
        wet_now = flag(ctl, wet_from + step)

        def group(index, carry, source=source, target=target, delta=delta, wet_now=wet_now):
            base = pl.multiple_of(index * AGAIN, AGAIN)
            rows = pl.ds(base, AGAIN)
            after = pl.ds(pl.multiple_of(jnp.minimum(base + AGAIN, EARLY - 8), 8), 8)
            refs = [source.at[field] for field in range(3)] + [work.at[3]]
            fields = [jnp.concatenate([ref[rows, :], ref[after, :]], 0) for ref in refs]
            cells_x, cells_y = cell(*fields[:3])
            here_x = tuple(value[:AGAIN] for value in cells_x)
            here_y = tuple(value[:AGAIN] for value in cells_y)
            faces_x = face(here_x, tuple(down(value) for value in cells_x))
            turned = tuple(pltpu.roll(value, 1, 0) for value in faces_x)
            change_x = tuple(
                value - jnp.where(row_ids == 0, before, moved)
                for value, before, moved in zip(faces_x, carry[:3], turned)
            )
            ground = fields[3][:AGAIN]
            ground_up = pltpu.roll(ground, 1, 0)
            slope_x = down(fields[3]) - jnp.where(row_ids == 0, carry[3], ground_up)
            carried = tuple(value[0:1, :] for value in turned) + (ground_up[0:1, :],)
            faces_y = face(here_y, tuple(right_of(value) for value in here_y))
            change_y = tuple(value - left_of(value) for value in faces_y)
            slope_y = right_of(ground) - left_of(ground)
            old = tuple(value[:AGAIN] for value in fields[:3])
            weight = SLOPE * old[0]
            slopes = (
                SCALE * (change_x[0] + change_y[0]),
                SCALE * (change_x[1] + change_y[2]) + weight * slope_x,
                SCALE * (change_x[2] + change_y[1]) + weight * slope_y,
            )
            for field, value in enumerate(
                moved_on(old, slopes, work[4, rows, :], delta, wet_now)
            ):
                target[field, rows, :] = value
            return carried

        if step == 0:
            wait_all(incoming)
        lax.fori_loop(0, EARLY // AGAIN, group, start)


def late_rows(tile, late):
    row = sublanes()
    kept = EARLY - 8
    lane = lax.broadcasted_iota(jnp.int32, (8, LANES), 1)
    for field in range(3):
        late[field, 0:8, :] = jnp.where(
            row < 3, tile[field, 0:8, :], tile[field, kept : kept + 8, :]
        )
        packed = [jnp.zeros((8, LANES), jnp.float32)] * 2
        for block in range(EARLY // 8):
            rows = slice(8 * block, 8 * block + 8)
            sides = jnp.where(lane < 64, tile[field, rows, :LANES], tile[field, rows, LANES:])
            turned = pltpu.roll(sides, (3 + 8 * block) % LANES, 1)
            which = block // 16
            packed[which] = jnp.where(lane // 8 == block % 16, turned, packed[which])
        late[field, 8:16, :] = jnp.concatenate(packed, 1)
        late[field, 16:, :] = tile[field, EARLY:, :]


def merge(late, rest, early, tile):
    for field in range(3):
        merge_field(field, late, rest, early, tile)


def merge_field(field, late, rest, early, tile):
    row = sublanes()
    lane = lax.broadcasted_iota(jnp.int32, (8, LANES), 1)
    first = late[field, 0:8, :]
    for block in range(EARLY // 8):
        rows = slice(8 * block, 8 * block + 8)
        which = block // 16
        packed = late[field, 8:16, which * LANES : (which + 1) * LANES]
        sides = pltpu.roll(packed, (-3 - 8 * block) % LANES, 1)
        value = early[field, rows, :]
        value = jnp.concatenate(
            [
                jnp.where(lane < 3, sides, value[:, :LANES]),
                jnp.where(lane >= LANES - 3, sides, value[:, LANES:]),
            ],
            1,
        )
        if block == 0:
            value = jnp.where(row < 3, first, value)
        if block == EARLY // 8 - 1:
            value = jnp.where(row < 5, value, first)
        tile[field, rows, :] = value
    tile[field, EARLY : TILE - HALF, :] = late[field, 16:, :]
    if rest is not None:
        tile[field, TILE - HALF :, :] = rest[field]


def repeat_second(
    ctl, delta0, delta1, delta2, low, high, late, rest, out, late_out, rest_out, work, tile, sems
):
    near = start_all(((late, late_out), (rest, rest_out)), sems, 2)
    repeat_steps(ctl, WET_SECOND, (delta0, delta1, delta2), (low, high), work, tile, sems)
    wait_all(start_all(((tile, out),), sems) + near)


def repeat_first(
    ctl, delta0, delta1, delta2, low, high, late_in, rest_in, staying, out,
    work, other, tile, late, rest, sems,
):
    kept = out.at[1 - ctl[MOVE + 1]]
    again = ctl[MOVE] == ctl[MOVE + 1]

    @pl.when(again)
    def _():
        wait_all(start_all(((staying, tile),), sems))

    @pl.when(jnp.logical_not(again))
    def _():
        copies = start_all(((late_in, late), (rest_in, rest)), sems, 2)
        repeat_steps(ctl, WET_FIRST, (delta0, delta1, delta2), (low, high), work, other, sems)
        wait_all(copies)
        merge(late, rest, other, tile)

    wait_all(start_all(((tile, kept),), sems))


def finish_late(ctl, late, early, before, out, tile, sems):
    del before
    copies = []
    for field in range(3):
        merge_field(field, late, None, early, tile)
        copies += start_all(
            ((tile.at[field], out.at[ctl[MOVE + 1], field, 0 : TILE - HALF]),), sems, field
        )
    wait_all(copies)


def finish_rest(ctl, rest, before, out, sems):
    del before
    wait_all(start_all(((rest, out.at[ctl[MOVE + 1], :, TILE - HALF :]),), sems))


def second_late(ctl, arrived, own, order, leaving):
    del order
    again = ctl[MOVE] == ctl[MOVE + 1]
    for field in range(3):
        leaving[field] = jnp.where(again, arrived[field], own[field])


def correct_rows(ctl, slot, got, ground, state, rate, bottom):
    position = jnp.where(ctl[SLOT_LOW] == slot, 0, 1)
    device = lax.axis_index("xb") * 2 + lax.axis_index("yb")
    wall = WALL_WEST if bottom else WALL_EAST

    @pl.when(jnp.logical_not(flag(ctl, wall + position)))
    def _():
        peer = device - 2 if bottom else device + 2
        block = pl.ds(pl.multiple_of(peer * 8, 8), 8)
        lines = got[block, :TILE]
        grounds = ground[block, :TILE]
        stride = 4 if got.shape[1] > TILE else 3

        def line(offset):
            other = offset + stride
            picked = jnp.where(
                position == 0, lines[offset : offset + 1, :], lines[other : other + 1, :]
            )
            return jnp.broadcast_to(picked, (8, TILE))

        ghost, _ = cell(*(line(field) for field in range(3)))
        ghost_ground = jnp.where(position == 0, grounds[3:4, :], grounds[7:8, :])
        rows = slice(0, 8) if bottom else slice(TILE - 8, TILE)
        own = [state[slot, field, rows, :] for field in range(3)]
        here, _ = cell(*own)
        fluxes = face(ghost, here) if bottom else face(here, ghost)
        push = SCALE * fluxes[1] + (SLOPE * own[0]) * ghost_ground
        row = sublanes()
        sign = -1.0 if bottom else 1.0
        chosen = row == (0 if bottom else 7)
        for field, value in enumerate((SCALE * fluxes[0], push, SCALE * fluxes[2])):
            rate[slot, field, rows, :] += jnp.where(chosen, sign * value, 0.0)


def column_fix(got, ground, columns):
    upper = lax.axis_index("yb")
    device = lax.axis_index("xb") * 2 + upper
    peer = device + 1 - 2 * upper
    block = pl.ds(pl.multiple_of(peer * 8, 8), 8)
    lines = got[block, :TILE]
    ghost_ground = ground[block, :TILE][3:4]
    mine = columns[...]
    _, ghost = cell(lines[0:1], lines[1:2], lines[2:3])
    _, own = cell(mine[0:1], mine[1:2], mine[2:3])
    low = upper == 0
    left = tuple(jnp.where(low, a, b) for a, b in zip(own, ghost))
    right = tuple(jnp.where(low, b, a) for a, b in zip(own, ghost))
    fluxes = face(left, right)
    sign = jnp.where(low, 1.0, -1.0)
    push = SCALE * fluxes[1] + (SLOPE * mine[0:1]) * ghost_ground
    block8 = stacked(
        [sign * SCALE * fluxes[0], sign * SCALE * fluxes[2], sign * push],
        jnp.zeros((8, TILE), jnp.float32),
    )
    return jnp.transpose(
        jnp.concatenate([block8, jnp.zeros((LANES - 8, TILE), jnp.float32)], 0)
    )


def last_update(ctl, got, ground, columns, state, manning, rate, order, *rest):
    del order
    slots = ctl[MOVE], 1 - ctl[MOVE]
    update(STEPS - 1, ctl, got, ground, columns, state, manning, rate, *rest, slots=slots)


def update(
    step, ctl, got_in, ground_in, columns_in, state_in, manning_in, rate_in, *rest,
    passing=None, slots=(0, 1),
):
    more = step + 1 < STEPS
    fresh_out, *lines_to, delta_out = rest[: 4 if more else 6]
    rest = rest[4 if more else 6 :]
    state, manning, rate, fresh, got, ground, columns, first, second, delta_keep, sems = rest
    out, columns_out = first, second
    small = start_all(
        ((got_in, got), (ground_in, ground), (columns_in, columns)), sems, 5 * PARTS
    )
    size = 2 * TILE // PARTS
    parts = [
        (slot, slice(k * size, (k + 1) * size)) for slot in slots for k in range(PARTS // 2)
    ]
    incoming = []
    for index, (slot, rows) in enumerate(parts):
        incoming.append(
            start_all(
                (
                    (rate_in.at[slot, :, rows], rate.at[slot, :, rows]),
                    (state_in.at[slot, :, rows], state.at[slot, :, rows]),
                    (manning_in.at[slot, rows], manning.at[slot, rows]),
                ),
                sems,
                3 * index,
            )
        )
    wait_all(small)
    upper = lax.axis_index("yb")
    devices = 2 * lax.axis_size("xb")
    begin = TILE if got.shape[1] > TILE else 0
    tops = got[0:8, begin : begin + LANES]
    for peer in range(1, devices):
        tops = jnp.maximum(tops, got[peer * 8 : peer * 8 + 8, begin : begin + LANES])
    delta = (COURANT * SPACING) / tops[TOP : TOP + 1, :]
    delta = jnp.concatenate([delta, delta], 1)
    delta_keep[...] = jnp.broadcast_to(delta, (8, TILE))
    outgoing = start_all(((delta_keep, delta_out),), sems, 5 * PARTS + 3)
    fix = column_fix(got, ground, columns)
    facing = jnp.where(upper > 0, ctl[SLOT_LOW], 1 - ctl[SLOT_LOW])
    begin = pl.multiple_of((1 - upper) * LANES, LANES)
    goal = (1 - upper) * (LANES - 1)
    lane = lax.broadcasted_iota(jnp.int32, (size, LANES), 1)
    total = jnp.zeros((ROWS, TILE), jnp.float32)
    for index, (slot, part_rows) in enumerate(parts):
        wait_all(incoming[index])
        if part_rows.start == 0:
            correct_rows(ctl, slot, got, ground, state, rate, True)
        if part_rows.stop == TILE:
            correct_rows(ctl, slot, got, ground, state, rate, False)

        @pl.when(facing == slot)
        def _(slot=slot, part_rows=part_rows):
            for field in range(3):
                turned = pltpu.roll(
                    fix[part_rows], lax.rem(goal + LANES - field, LANES), 1
                )
                rate[slot, field, part_rows, pl.ds(begin, LANES)] += jnp.where(
                    lane == goal, turned, 0.0
                )

        wet_now = flag(ctl, WET + 2 * step + slot)

        def group(index, best, slot=slot, wet_now=wet_now):
            rows = pl.ds(pl.multiple_of(index * ROWS, ROWS), ROWS)
            old = tuple(state[slot, field, rows, :] for field in range(3))
            slopes = tuple(rate[slot, field, rows, :] for field in range(3))
            h, hu, hv = moved_on(old, slopes, manning[slot, rows, :], delta, wet_now)
            fresh[slot, 0, rows, :] = h
            fresh[slot, 1, rows, :] = hu
            fresh[slot, 2, rows, :] = hv
            if more:
                along_x, along_y = cell(h, hu, hv)
                best = jnp.maximum(best, jnp.maximum(along_x[5], along_y[5]))
            return best

        best = lax.fori_loop(
            part_rows.start // ROWS,
            part_rows.stop // ROWS,
            group,
            jnp.zeros((ROWS, TILE), jnp.float32),
        )
        if more:
            best = jnp.where(flag(ctl, WET + 2 * step + 2 + slot), best, 0.0)
            total = jnp.maximum(total, best)
        if more:
            outgoing += start_all(
                ((fresh.at[slot, :, part_rows], fresh_out.at[slot, :, part_rows]),),
                sems,
                3 * PARTS + index,
            )
        elif index >= PARTS // 2:
            outgoing += start_all(
                ((fresh.at[slot, :, part_rows], fresh_out.at[:, part_rows]),),
                sems,
                3 * PARTS + index,
            )
        if not more and part_rows.stop == TILE:
            late, low, high = (
                (first, *lines_to[:2]) if index < PARTS // 2 else (second, *lines_to[2:])
            )
            late_rows(fresh.at[slot], late)
            outgoing += start_all(
                ((late.at[:, :HALF], low), (late.at[:, HALF:], high)),
                sems,
                4 * PARTS + (0 if index < PARTS // 2 else 2),
            )
        if passing and index == PARTS // 2:
            passing.middle()
    if more:
        messages(ctl, fresh, None, jnp.max(total, keepdims=True), out, columns_out)
        pairs = zip((out, columns_out), lines_to)
        outgoing += start_all(tuple(pairs), sems, 4 * PARTS)
    wait_all(outgoing)


def vmem():
    return pl.BlockSpec(memory_space=pltpu.VMEM)


def smem():
    return pl.BlockSpec(memory_space=pltpu.SMEM)


def hbm():
    return pl.BlockSpec(memory_space=pltpu.HBM)


def anywhere():
    return pl.BlockSpec(memory_space=pl.ANY)


def call(
    kernel, outs, out_specs, in_specs, flops, scratch=(), aliases=None, room=VMEM_BYTES, moved=4
):
    return pl.pallas_call(
        kernel,
        scratch_shapes=scratch,
        input_output_aliases=aliases or {},
        out_shape=outs,
        in_specs=in_specs,
        out_specs=out_specs,
        compiler_params=pltpu.CompilerParams(vmem_limit_bytes=room),
        cost_estimate=pl.CostEstimate(flops=flops, bytes_accessed=moved << 20, transcendentals=0),
    )


def f32(*shape):
    return jax.ShapeDtypeStruct(shape, jnp.float32)


def spread(fast):
    return lax.all_to_all(fast, ("xb", "yb"), split_axis=0, concat_axis=0, tiled=True)


def body(state, bed, manning, neighbours, wet, moves):
    shape = f32(*state.shape)
    devices = lax.axis_size("xb") * lax.axis_size("yb")
    whole = pltpu.VMEM(state.shape, jnp.float32)
    part = pltpu.VMEM(bed.shape, jnp.float32)
    tile_shape = f32(*state.shape[1:])
    early_shape = f32(5, EARLY, TILE)
    early_state = f32(3, EARLY, TILE)
    late_shape = f32(3, LATE, TILE)
    half_shape = f32(3, HALF, TILE)
    delta_shape = f32(8, TILE)

    def buffer(like):
        return pltpu.VMEM(like.shape, jnp.float32)

    piece_shapes = tuple(f32(5, end - begin, TILE) for begin, end in PIECES)
    out, columns, ctl = call(
        opening,
        (
            f32(8 * devices, TILE + LANES),
            f32(8, TILE),
            jax.ShapeDtypeStruct((CONTROLS,), jnp.int32),
        ),
        (vmem(), vmem(), smem()),
        [hbm()] * 5,
        4 << 20,
        [
            whole,
            part,
            pltpu.SMEM(neighbours.shape[::-1], jnp.int32),
            pltpu.SMEM(wet.shape, jnp.int32),
            pltpu.SMEM(moves.shape, jnp.int32),
            pltpu.SemaphoreType.DMA((6,)),
        ],
    )(state, bed, neighbours.T, wet, moves)
    state_first = state
    ground = None
    deltas = []
    for step in range(STEPS):
        got = spread(out)
        ground = got if step == 0 else ground
        scratch = [whole, part, whole, pltpu.SemaphoreType.DMA((3 * CHUNKS,))]
        piece_scratch = [
            [buffer(piece), pltpu.SemaphoreType.DMA((2,))] for piece in piece_shapes
        ]
        if step == 1:
            rate, leaving = call(
                rates_and_leaving,
                (shape, piece_shapes[0]),
                (hbm(),) * 2,
                [smem()] + [hbm()] * 5,
                16 << 20,
                scratch + piece_scratch[0],
            )(ctl, state, bed, state_first, manning, early_first[0])
            early_second = [shifted(leaving, "xb", 1)]
        elif step == 2:
            rate = call(rates_after, shape, hbm(), [smem()] + [hbm()] * 3, 16 << 20, scratch)(
                ctl, state, bed, early_second[0]
            )
        else:
            rate, *leaving = call(
                rates_and_splitting,
                (shape,) + piece_shapes,
                (hbm(),) * 3,
                [smem()] + [hbm()] * 3,
                16 << 20,
                scratch + [buffer(early_shape), pltpu.SemaphoreType.DMA((5,))],
            )(ctl, state, bed, manning)
            held = call(
                hold,
                piece_shapes[0],
                hbm(),
                [anywhere(), anywhere(), hbm()],
                1 << 10,
                aliases={2: 0},
                room=1 << 20,
            )(got, got, leaving[0])
            early_first = [shifted(held, "xb", 1)]
        more = step + 1 < STEPS
        shapes = (f32(8 * devices, TILE), f32(8, TILE)) if more else (half_shape,) * 4
        passing = step == 1
        work = [
            whole,
            part,
            whole,
            whole,
            pltpu.VMEM(got.shape, jnp.float32),
            pltpu.VMEM(ground.shape, jnp.float32),
            pltpu.VMEM((8, TILE), jnp.float32),
            buffer(shapes[0] if more else late_shape),
            buffer(shapes[1] if more else late_shape),
            buffer(delta_shape),
            pltpu.SemaphoreType.DMA((5 * PARTS + 4,)),
        ]
        operands = ctl, got, ground, columns, state, manning, rate
        if not more:
            break
        outs = call(
            functools.partial(update_and_leaving if passing else update, step),
            (shape,) + shapes + (delta_shape,) + ((piece_shapes[1],) if passing else ()),
            (hbm(),) * (5 if passing else 4),
            [smem()] + [hbm()] * (9 if passing else 6),
            8 << 20,
            work + (piece_scratch[1] if passing else []),
            moved=10,
        )(*operands, *((state_first, bed, early_first[1]) if passing else ()))
        state, out, columns, delta, *passed = outs
        deltas.append(delta)
        if step == 0:
            held = call(
                hold, piece_shapes[1], hbm(), [hbm()] * 3, 1 << 10, aliases={2: 0}
            )(delta, delta, leaving[1])
            early_first.append(shifted(held, "xb", 1))
        elif step == 1:
            early_second.append(shifted(passed[0], "xb", 1))

    staying, late_first, rest_first, late_second, rest_second, delta = call(
        last_update,
        (tile_shape,) + shapes + (delta_shape,),
        (hbm(),) * 6,
        [smem()] + [hbm()] * 7,
        8 << 20,
        work,
        moved=10,
    )(*operands, early_second[1])
    deltas.append(delta)
    room = 16 << 20
    late_arrived = shifted(late_first, "xb", 1)
    rest_arrived = shifted(rest_first, "xb", 1)
    second, late_second, rest_second = call(
        repeat_second,
        (early_state, half_shape, half_shape),
        (anywhere(), vmem(), vmem()),
        [smem()] + [vmem()] * 3 + [anywhere()] * 4,
        8 << 20,
        [buffer(early_shape), buffer(early_state), pltpu.SemaphoreType.DMA((4,))],
        room=room,
    )(ctl, *deltas, *early_second, late_second, rest_second)

    def pass_late(arrived, own):
        leaving = call(
            second_late,
            half_shape,
            vmem(),
            [smem(), vmem(), vmem(), anywhere()],
            1 << 10,
            room=room,
        )(ctl, arrived, own, second)
        return shifted(leaving, "xb", 1)

    late_next = pass_late(late_arrived, late_second)
    rest_next = pass_late(rest_arrived, rest_second)
    final = call(
        repeat_first,
        shape,
        hbm(),
        [smem()] + [vmem()] * 3 + [anywhere()] * 5,
        8 << 20,
        [
            buffer(early_shape),
            buffer(early_state),
            buffer(tile_shape),
            buffer(half_shape),
            buffer(half_shape),
            pltpu.SemaphoreType.DMA((4,)),
        ],
        room=room,
    )(ctl, *deltas, *early_first, late_arrived, rest_arrived, staying)
    final = call(
        finish_late,
        shape,
        hbm(),
        [smem(), vmem(), vmem(), hbm()],
        1 << 20,
        [pltpu.VMEM((3, TILE - HALF, TILE), jnp.float32), pltpu.SemaphoreType.DMA((3,))],
        {3: 0},
        room=room,
    )(ctl, late_next, second, final)
    return call(
        finish_rest,
        shape,
        hbm(),
        [smem(), vmem(), hbm()],
        1 << 20,
        [pltpu.SemaphoreType.DMA((1,))],
        {2: 0},
        room=room,
    )(ctl, rest_next, final)


def solution(mesh):
    placed = (
        P(("runs", "xb", "yb"), None, None, None),
        P(("runs", "xb", "yb"), None, None),
        P(("runs", "xb", "yb"), None, None),
        P("runs", None),
        P(None, "runs"),
        P(None, "runs"),
    )
    return jax.shard_map(
        body,
        mesh=mesh,
        in_specs=placed,
        out_specs=P(("runs", "xb", "yb"), None, None, None),
        check_vma=False,
    )
```

```python
import functools

import jax
import jax.numpy as jnp
from jax import lax
from jax.experimental import pallas as pl
from jax.experimental.pallas import tpu as pltpu
from jax.sharding import PartitionSpec as P

STEPS = 3
GRAVITY = 9.81
ROOT_G = GRAVITY**0.5
SPACING = 5.0
COURANT = 0.2
ROWS = 128
LANES = 128
TILE = 256
VMEM_BYTES = 60 * 1024 * 1024
SLOT_LOW, WALL_WEST, WALL_EAST, WALL_OUTER, WET, MOVE = 0, 1, 3, 5, 7, 13
WET_FIRST, WET_SECOND = 16, 19
CONTROLS = 24
EARLY = 128
PIECES = ((0, 64), (64, 128))
AGAIN = 64
LATE = TILE - EARLY + 16
HALF = LATE // 2
CHUNKS = 8
PARTS = 4
STRIP = 32
TOP = 6
SCALE = 0.5 / SPACING
SLOPE = GRAVITY / (2.0 * SPACING)


def shifted(value, axis, steps, around=True):
    count = lax.axis_size(axis)
    pairs = [(source, (source + steps) % count) for source in range(count)]
    if not around:
        pairs = [pair for pair in pairs if abs(pair[0] - pair[1]) == abs(steps)]
    return lax.ppermute(value, axis, pairs)


def cell(h, hu, hv):
    root = lax.rsqrt(h)
    inverse = root * root
    u = hu * inverse
    v = hv * inverse
    celerity = ROOT_G * (h * root)
    pressure = (0.5 * GRAVITY) * (h * h)
    cross = hu * v
    speed_x = jnp.abs(u) + celerity
    speed_y = jnp.abs(v) + celerity
    along_x = (h, hu, hv, hu * u + pressure, cross, speed_x)
    along_y = (h, hv, hu, hv * v + pressure, cross, speed_y)
    return along_x, along_y


def face(left, right):
    wave = jnp.maximum(left[5], right[5])
    return (
        (left[1] + right[1]) - wave * (right[0] - left[0]),
        (left[3] + right[3]) - wave * (right[1] - left[1]),
        (left[4] + right[4]) - wave * (right[2] - left[2]),
    )


def slot_of(ctl, position):
    low = ctl[SLOT_LOW]
    return low if position == 0 else 1 - low


def flag(ctl, index):
    return ctl[index] > 0


def start_all(pairs, sems, first=0):
    copies = [
        pltpu.make_async_copy(src, dst, sems.at[first + k]) for k, (src, dst) in enumerate(pairs)
    ]
    for copy in copies:
        copy.start()
    return copies


def wait_all(copies):
    for copy in copies:
        copy.wait()


def sublanes(width=TILE):
    return lax.broadcasted_iota(jnp.int32, (8, width), 0)


def stacked(lines, base):
    row = sublanes()
    for index, line in enumerate(lines):
        base = jnp.where(row == index, jnp.broadcast_to(line, (8, TILE)), base)
    return base


def messages(ctl, state, bed, fastest, out, columns):
    upper = lax.axis_index("yb")
    column = lax.axis_index("xb")
    last = lax.axis_size("xb") - 1
    devices = 2 * (last + 1)
    device = column * 2 + upper
    top = jnp.broadcast_to(fastest, (8, TILE))
    for peer in range(devices):
        out[peer * 8 : peer * 8 + 8, :TILE] = top
        if bed is not None:
            out[peer * 8 : peer * 8 + 8, TILE:] = top[:, :LANES]
    row = sublanes()

    def edge(line):
        rows = slice(line, line + 1)
        lines = []
        for position in range(2):
            slot = slot_of(ctl, position)
            lines += [state[slot, field, rows, :] for field in range(3)]
            if bed is not None:
                lines.append(bed[slot, rows, :])
        return stacked(lines, top)

    for inside, peer, line in (
        (column > 0, device - 2, 0),
        (column < last, device + 2, TILE - 1),
    ):

        @pl.when(inside)
        def _(peer=peer, line=line):
            out[pl.ds(pl.multiple_of(peer * 8, 8), 8), :TILE] = edge(line)

    slot = jnp.where(upper > 0, ctl[SLOT_LOW], 1 - ctl[SLOT_LOW])
    begin = pl.multiple_of((1 - upper) * LANES, LANES)
    lane = lax.broadcasted_iota(jnp.int32, (TILE, LANES), 1)
    packed = None
    for field in range(4 if bed is not None else 3):
        if field < 3:
            part = state[slot, field, :, pl.ds(begin, LANES)]
        else:
            part = bed[slot, :, pl.ds(begin, LANES)]
        turned = pltpu.roll(part, field + 1 - upper, 1)
        packed = turned if field == 0 else jnp.where(lane == field, turned, packed)
    lines = jnp.transpose(packed)[:8]
    columns[...] = lines
    start = pl.multiple_of((device + 1 - 2 * upper) * 8, 8)
    out[pl.ds(start, 8), :TILE] = jnp.where(row == TOP, top, lines)


def opening(
    state_in, bed_in, neighbours_in, wet_in, moves_in,
    out, columns, ctl,
    state, bed, neighbours, wet, moves, sems,
):
    copies = start_all(
        (
            (neighbours_in, neighbours),
            (wet_in, wet),
            (moves_in, moves),
            (state_in.at[0], state.at[0]),
            (state_in.at[1], state.at[1]),
            (bed_in, bed),
        ),
        sems,
    )
    device = lax.axis_index("xb") * 2 + lax.axis_index("yb")
    wait_all(copies[:3])
    first = device * 2
    low = jnp.where(neighbours[3, first] == first + 1, 0, 1)
    ctl[SLOT_LOW] = low
    for position in range(2):
        slot = low if position == 0 else 1 - low
        tile = first + slot
        ctl[WALL_WEST + position] = (neighbours[0, tile] < 0).astype(jnp.int32)
        ctl[WALL_EAST + position] = (neighbours[1, tile] < 0).astype(jnp.int32)
        ctl[WALL_OUTER + position] = (neighbours[2 + position, tile] < 0).astype(jnp.int32)
    for step in range(STEPS):
        for slot in range(2):
            ctl[WET + 2 * step + slot] = wet[step, first + slot]
        ctl[MOVE + step] = moves[step, device]
    count = lax.axis_size("xb")
    upper = lax.axis_index("yb")
    column = lax.axis_index("xb")
    source = lax.rem(column + count - 1, count) * 2 + upper
    before = lax.rem(column + count - 2, count) * 2 + upper
    again = moves[0, source] == moves[1, source]
    tile_first = source * 2 + moves[0, source]
    tile_second = jnp.where(
        again, before * 2 + moves[0, before], source * 2 + 1 - moves[0, source]
    )
    for step in range(STEPS):
        ctl[WET_FIRST + step] = wet[step, tile_first]
        ctl[WET_SECOND + step] = wet[step, tile_second]

    total = jnp.zeros((ROWS, TILE), jnp.float32)
    for slot in range(2):
        copies[3 + slot].wait()

        def group(index, best, slot=slot):
            rows = pl.ds(pl.multiple_of(index * ROWS, ROWS), ROWS)
            along_x, along_y = cell(*(state[slot, field, rows, :] for field in range(3)))
            return jnp.maximum(best, jnp.maximum(along_x[5], along_y[5]))

        best = lax.fori_loop(0, TILE // ROWS, group, jnp.zeros((ROWS, TILE), jnp.float32))
        total = jnp.maximum(total, jnp.where(wet[0, first + slot] > 0, best, 0.0))
    copies[5].wait()
    messages(ctl, state, bed, jnp.max(total, keepdims=True), out, columns)


def hold(first, second, leaving, same):
    del first, second, leaving, same


class Splitting:
    def __init__(self, ctl, state_in, bed_in, manning_in, leaving, buffer, sems):
        slot = ctl[MOVE]
        rows = slice(0, EARLY)
        pairs = (
            (state_in.at[slot, :, rows], buffer.at[0:3]),
            (bed_in.at[slot, rows], buffer.at[3]),
            (manning_in.at[slot, rows], buffer.at[4]),
        )
        self.incoming = [
            pltpu.make_async_copy(src, dst, sems.at[k]) for k, (src, dst) in enumerate(pairs)
        ]
        self.outgoing = [
            pltpu.make_async_copy(buffer.at[:, begin:end], piece, sems.at[3 + k])
            for k, ((begin, end), piece) in enumerate(zip(PIECES, leaving))
        ]

    def start(self):
        for copy in self.incoming:
            copy.start()

    def middle(self):
        wait_all(self.incoming)
        for copy in self.outgoing:
            copy.start()

    def end(self):
        wait_all(self.outgoing)


class Passing:
    def __init__(self, ctl, piece, state_in, bed_in, manning_in, arrived, leaving, buffer, sems):
        self.again = ctl[MOVE] == ctl[MOVE + 1]
        self.other = 1 - ctl[MOVE]
        self.rows = slice(*piece)
        self.refs = state_in, bed_in, manning_in
        self.incoming = pltpu.make_async_copy(arrived, buffer, sems.at[0])
        self.outgoing = pltpu.make_async_copy(buffer, leaving, sems.at[1])
        self.buffer = buffer
        self.sem = sems.at[0]

    def start(self):
        state_in, bed_in, manning_in = self.refs
        buffer, sem, rows = self.buffer, self.sem, self.rows

        @pl.when(self.again)
        def _():
            self.incoming.start()

        @pl.when(jnp.logical_not(self.again))
        def _():
            pltpu.make_async_copy(state_in.at[self.other, :, rows], buffer.at[0:3], sem).start()
            pltpu.make_async_copy(bed_in.at[self.other, rows], buffer.at[3], sem).start()
            pltpu.make_async_copy(manning_in.at[self.other, rows], buffer.at[4], sem).start()

    def middle(self):
        self.incoming.wait()
        self.outgoing.start()

    def end(self):
        self.outgoing.wait()


def rates_and_splitting(
    ctl, state_in, bed_in, manning_in, rate_out, leaving_low, leaving_high,
    state, bed, rate, sems, buffer, moving,
):
    leaving = leaving_low, leaving_high
    splitting = Splitting(ctl, state_in, bed_in, manning_in, leaving, buffer, moving)
    rates(ctl, state_in, bed_in, rate_out, state, bed, rate, sems, splitting)


def rates_and_leaving(
    ctl, state_in, bed_in, state_first, manning_in, arrived, rate_out, leaving,
    state, bed, rate, sems, buffer, moving,
):
    passing = Passing(
        ctl, PIECES[0], state_first, bed_in, manning_in, arrived, leaving, buffer, moving
    )
    rates(ctl, state_in, bed_in, rate_out, state, bed, rate, sems, passing)


def update_and_leaving(
    step, ctl, got_in, ground_in, columns_in, state_in, manning_in, rate_in,
    state_first, bed_in, arrived, fresh_out, first_out, second_out, delta_out, leaving, *rest
):
    *rest, buffer, moving = rest
    passing = Passing(
        ctl, PIECES[1], state_first, bed_in, manning_in, arrived, leaving, buffer, moving
    )
    passing.start()
    update(
        step, ctl, got_in, ground_in, columns_in, state_in, manning_in, rate_in,
        fresh_out, first_out, second_out, delta_out, *rest, passing=passing,
    )
    passing.end()


def rates_after(ctl, state_in, bed_in, order, *rest):
    del order
    rates(ctl, state_in, bed_in, *rest)


def rates(ctl, state_in, bed_in, rate_out, state, bed, rate, sems, passing=None):
    width = 2 * TILE
    row_ids = lax.broadcasted_iota(jnp.int32, (STRIP, width), 0)
    row8 = sublanes(width)
    lane = lax.broadcasted_iota(jnp.int32, (STRIP, LANES), 1)
    last = TILE // STRIP - 1
    chunk = TILE // CHUNKS
    slots = [slot_of(ctl, position) for position in range(2)]
    incoming = []
    for part in range(CHUNKS):
        rows = slice(part * chunk, (part + 1) * chunk)
        incoming.append(
            start_all(
                (
                    (state_in.at[:, :, rows], state.at[:, :, rows]),
                    (bed_in.at[:, rows], bed.at[:, rows]),
                ),
                sems,
                2 * part,
            )
        )
    if passing:
        passing.start()
    keep_west, keep_east, keep_south, keep_north = (
        jnp.where(flag(ctl, index), 1.0, 0.0)
        for index in (WALL_WEST, WALL_EAST, WALL_OUTER, WALL_OUTER + 1)
    )

    def strip(field, rows):
        if field == 3:
            return jnp.concatenate([bed[slot, rows, :] for slot in slots], 1)
        return jnp.concatenate([state[slot, field, rows, :] for slot in slots], 1)

    def blocks(value):
        return [value[:, k * LANES : (k + 1) * LANES] for k in range(4)]

    def right_of(value, end=None):
        turned = [pltpu.roll(part, LANES - 1, 1) for part in blocks(value)]
        after = turned[1:] + [turned[3] if end is None else end]
        return jnp.concatenate(
            [
                jnp.where(lane == LANES - 1, following, part)
                if following is not part
                else part
                for part, following in zip(turned, after)
            ],
            1,
        )

    def left_of(value, end):
        turned = [pltpu.roll(part, 1, 1) for part in blocks(value)]
        before = [end] + turned[:3]
        return jnp.concatenate(
            [jnp.where(lane == 0, previous, part) for part, previous in zip(turned, before)], 1
        )

    def down(value):
        return pltpu.roll(value, STRIP + 7, 0)[:STRIP]

    def group(index, carry):
        base = pl.multiple_of(index * STRIP, STRIP)
        rows = pl.ds(base, STRIP)
        after = pl.ds(pl.multiple_of(jnp.minimum(base + STRIP, TILE - 8), 8), 8)
        at_end = index == last
        fields = [
            jnp.concatenate([strip(field, rows), strip(field, after)], 0) for field in range(3)
        ]
        cells_x, cells_y = cell(*fields)
        here_x = tuple(value[:STRIP] for value in cells_x)
        here_y = tuple(value[:STRIP] for value in cells_y)

        ending = jnp.logical_and(row8 == 7, at_end)
        faces = list(face(here_x, tuple(down(value) for value in cells_x)))
        wall = keep_east * (2.0 * (here_x[3] + here_x[5] * here_x[1])[STRIP - 8 :])
        for component, value in enumerate((0.0, wall, 0.0)):
            upper = faces[component]
            faces[component] = jnp.concatenate(
                [upper[: STRIP - 8], jnp.where(ending, value, upper[STRIP - 8 :])], 0
            )
        turned = tuple(pltpu.roll(value, 1, 0) for value in faces)
        change_x = tuple(
            value - jnp.where(row_ids == 0, before, moved)
            for value, before, moved in zip(faces, carry[:3], turned)
        )
        ground = strip(3, rows)
        ground_after = jnp.where(
            at_end,
            jnp.broadcast_to(keep_east * ground[STRIP - 1 :], (8, width)),
            strip(3, after),
        )
        ground_up = pltpu.roll(ground, 1, 0)
        slope_x = down(jnp.concatenate([ground, ground_after], 0)) - jnp.where(
            row_ids == 0, carry[3], ground_up
        )
        carried = tuple(value[0:1, :] for value in turned) + (ground_up[0:1, :],)

        faces_y = list(face(here_y, tuple(right_of(value) for value in here_y)))
        normal = here_y[3]
        spread_y = here_y[5] * here_y[1]
        north = keep_north * (2.0 * (normal + spread_y)[:, width - LANES :])
        south = keep_south * (2.0 * (normal - spread_y)[:, :LANES])
        change_y = []
        for component, (high, low) in enumerate(((0.0, 0.0), (north, south), (0.0, 0.0))):
            parts = blocks(faces_y[component])
            parts[3] = jnp.where(lane == LANES - 1, high, parts[3])
            value = jnp.concatenate(parts, 1)
            change_y.append(value - left_of(value, low))
        slope_y = right_of(ground, keep_north * ground[:, width - LANES :]) - left_of(
            ground, keep_south * ground[:, :LANES]
        )
        weight = SLOPE * here_x[0]
        results = (
            SCALE * (change_x[0] + change_y[0]),
            SCALE * (change_x[1] + change_y[2]) + weight * slope_x,
            SCALE * (change_x[2] + change_y[1]) + weight * slope_y,
        )
        for field, value in enumerate(results):
            for position, slot in enumerate(slots):
                rate[slot, field, rows, :] = value[:, position * TILE : (position + 1) * TILE]
        return carried

    wait_all(incoming[0])
    top, _ = cell(*(strip(field, slice(0, 8)) for field in range(3)))
    nothing = jnp.zeros((1, width), jnp.float32)
    carry = (
        nothing,
        keep_west * (2.0 * (top[3] - top[5] * top[1])[0:1]),
        nothing,
        keep_west * strip(3, slice(0, 8))[0:1],
    )
    per_chunk = chunk // STRIP
    outgoing = []
    for part in range(CHUNKS):
        if part + 1 < CHUNKS:
            wait_all(incoming[part + 1])
        carry = lax.fori_loop(part * per_chunk, (part + 1) * per_chunk, group, carry)
        rows = slice(part * chunk, (part + 1) * chunk)
        outgoing += start_all(
            ((rate.at[:, :, rows], rate_out.at[:, :, rows]),), sems, 2 * CHUNKS + part
        )
        if passing and part == CHUNKS // 2:
            passing.middle()
    wait_all(outgoing)
    if passing:
        passing.end()


def moved_on(old, slopes, rough, delta, wet_now):
    h, hu, hv = (value - delta * slope for value, slope in zip(old, slopes))
    inverse = 1.0 / h
    u = hu * inverse
    v = hv * inverse
    speed = jnp.sqrt(u * u + v * v)
    power = jnp.exp((-4.0 / 3.0) * jnp.log(jnp.abs(h)))
    drag = (GRAVITY * delta) * (rough * rough) * (speed * power)
    factor = 1.0 / (1.0 + drag)
    fresh = (h, hu * factor, hv * factor)
    return tuple(jnp.where(wet_now, new, value) for new, value in zip(fresh, old))


def repeat_steps(ctl, wet_from, deltas, early, work, other, sems):
    incoming = []
    for ref in early:
        begin = 0 if ref is early[0] else early[0].shape[1]
        incoming += start_all(
            ((ref, work.at[:, begin : begin + ref.shape[1]]),), sems, len(incoming)
        )
    row_ids = lax.broadcasted_iota(jnp.int32, (AGAIN, TILE), 0)
    lane = lax.broadcasted_iota(jnp.int32, (AGAIN, LANES), 1)
    start = tuple(jnp.zeros((1, TILE), jnp.float32) for _ in range(4))

    def halves(value):
        return value[:, :LANES], value[:, LANES:]

    def right_of(value):
        low, high = (pltpu.roll(part, LANES - 1, 1) for part in halves(value))
        return jnp.concatenate([jnp.where(lane == LANES - 1, high, low), high], 1)

    def left_of(value):
        low, high = (pltpu.roll(part, 1, 1) for part in halves(value))
        return jnp.concatenate([low, jnp.where(lane == 0, low, high)], 1)

    def down(value):
        return pltpu.roll(value, AGAIN + 7, 0)[:AGAIN]

    for step in range(STEPS):
        source, target = (work, other) if step % 2 == 0 else (other, work)
        delta = deltas[step][0:1, :]
        wet_now = flag(ctl, wet_from + step)

        def group(index, carry, source=source, target=target, delta=delta, wet_now=wet_now):
            base = pl.multiple_of(index * AGAIN, AGAIN)
            rows = pl.ds(base, AGAIN)
            after = pl.ds(pl.multiple_of(jnp.minimum(base + AGAIN, EARLY - 8), 8), 8)
            refs = [source.at[field] for field in range(3)] + [work.at[3]]
            fields = [jnp.concatenate([ref[rows, :], ref[after, :]], 0) for ref in refs]
            cells_x, cells_y = cell(*fields[:3])
            here_x = tuple(value[:AGAIN] for value in cells_x)
            here_y = tuple(value[:AGAIN] for value in cells_y)
            faces_x = face(here_x, tuple(down(value) for value in cells_x))
            turned = tuple(pltpu.roll(value, 1, 0) for value in faces_x)
            change_x = tuple(
                value - jnp.where(row_ids == 0, before, moved)
                for value, before, moved in zip(faces_x, carry[:3], turned)
            )
            ground = fields[3][:AGAIN]
            ground_up = pltpu.roll(ground, 1, 0)
            slope_x = down(fields[3]) - jnp.where(row_ids == 0, carry[3], ground_up)
            carried = tuple(value[0:1, :] for value in turned) + (ground_up[0:1, :],)
            faces_y = face(here_y, tuple(right_of(value) for value in here_y))
            change_y = tuple(value - left_of(value) for value in faces_y)
            slope_y = right_of(ground) - left_of(ground)
            old = tuple(value[:AGAIN] for value in fields[:3])
            weight = SLOPE * old[0]
            slopes = (
                SCALE * (change_x[0] + change_y[0]),
                SCALE * (change_x[1] + change_y[2]) + weight * slope_x,
                SCALE * (change_x[2] + change_y[1]) + weight * slope_y,
            )
            for field, value in enumerate(
                moved_on(old, slopes, work[4, rows, :], delta, wet_now)
            ):
                target[field, rows, :] = value
            return carried

        if step == 0:
            wait_all(incoming)
        lax.fori_loop(0, EARLY // AGAIN, group, start)


def late_rows(tile, late):
    row = sublanes()
    kept = EARLY - 8
    lane = lax.broadcasted_iota(jnp.int32, (8, LANES), 1)
    for field in range(3):
        late[field, 0:8, :] = jnp.where(
            row < 3, tile[field, 0:8, :], tile[field, kept : kept + 8, :]
        )
        packed = [jnp.zeros((8, LANES), jnp.float32)] * 2
        for block in range(EARLY // 8):
            rows = slice(8 * block, 8 * block + 8)
            sides = jnp.where(lane < 64, tile[field, rows, :LANES], tile[field, rows, LANES:])
            turned = pltpu.roll(sides, (3 + 8 * block) % LANES, 1)
            which = block // 16
            packed[which] = jnp.where(lane // 8 == block % 16, turned, packed[which])
        late[field, 8:16, :] = jnp.concatenate(packed, 1)
        late[field, 16:, :] = tile[field, EARLY:, :]


def merge(late, rest, early, tile):
    for field in range(3):
        merge_field(field, late, rest, early, tile)


def merge_field(field, late, rest, early, tile):
    row = sublanes()
    lane = lax.broadcasted_iota(jnp.int32, (8, LANES), 1)
    first = late[field, 0:8, :]
    for block in range(EARLY // 8):
        rows = slice(8 * block, 8 * block + 8)
        which = block // 16
        packed = late[field, 8:16, which * LANES : (which + 1) * LANES]
        sides = pltpu.roll(packed, (-3 - 8 * block) % LANES, 1)
        value = early[field, rows, :]
        value = jnp.concatenate(
            [
                jnp.where(lane < 3, sides, value[:, :LANES]),
                jnp.where(lane >= LANES - 3, sides, value[:, LANES:]),
            ],
            1,
        )
        if block == 0:
            value = jnp.where(row < 3, first, value)
        if block == EARLY // 8 - 1:
            value = jnp.where(row < 5, value, first)
        tile[field, rows, :] = value
    tile[field, EARLY : TILE - HALF, :] = late[field, 16:, :]
    if rest is not None:
        tile[field, TILE - HALF :, :] = rest[field]


def repeat_second(
    ctl, delta0, delta1, delta2, low, high, late, rest, out, late_out, rest_out, work, tile, sems
):
    near = start_all(((late, late_out), (rest, rest_out)), sems, 2)
    repeat_steps(ctl, WET_SECOND, (delta0, delta1, delta2), (low, high), work, tile, sems)
    wait_all(start_all(((tile, out),), sems) + near)


def repeat_first(
    ctl, delta0, delta1, delta2, low, high, late_in, rest_in, staying, out,
    work, other, tile, late, rest, sems,
):
    kept = out.at[1 - ctl[MOVE + 1]]
    again = ctl[MOVE] == ctl[MOVE + 1]

    @pl.when(again)
    def _():
        wait_all(start_all(((staying, tile),), sems))

    @pl.when(jnp.logical_not(again))
    def _():
        copies = start_all(((late_in, late), (rest_in, rest)), sems, 2)
        repeat_steps(ctl, WET_FIRST, (delta0, delta1, delta2), (low, high), work, other, sems)
        wait_all(copies)
        merge(late, rest, other, tile)

    wait_all(start_all(((tile, kept),), sems))


def finish_late(ctl, late, early, before, out, tile, sems):
    del before
    copies = []
    for field in range(3):
        merge_field(field, late, None, early, tile)
        copies += start_all(
            ((tile.at[field], out.at[ctl[MOVE + 1], field, 0 : TILE - HALF]),), sems, field
        )
    wait_all(copies)


def finish_rest(ctl, rest, before, out, sems):
    del before
    wait_all(start_all(((rest, out.at[ctl[MOVE + 1], :, TILE - HALF :]),), sems))


def second_late(ctl, arrived, own, order, leaving):
    del order
    again = ctl[MOVE] == ctl[MOVE + 1]
    for field in range(3):
        leaving[field] = jnp.where(again, arrived[field], own[field])


def correct_rows(ctl, slot, got, ground, state, rate, bottom):
    position = jnp.where(ctl[SLOT_LOW] == slot, 0, 1)
    device = lax.axis_index("xb") * 2 + lax.axis_index("yb")
    wall = WALL_WEST if bottom else WALL_EAST

    @pl.when(jnp.logical_not(flag(ctl, wall + position)))
    def _():
        peer = device - 2 if bottom else device + 2
        block = pl.ds(pl.multiple_of(peer * 8, 8), 8)
        lines = got[block, :TILE]
        grounds = ground[block, :TILE]
        stride = 4 if got.shape[1] > TILE else 3

        def line(offset):
            other = offset + stride
            picked = jnp.where(
                position == 0, lines[offset : offset + 1, :], lines[other : other + 1, :]
            )
            return jnp.broadcast_to(picked, (8, TILE))

        ghost, _ = cell(*(line(field) for field in range(3)))
        ghost_ground = jnp.where(position == 0, grounds[3:4, :], grounds[7:8, :])
        rows = slice(0, 8) if bottom else slice(TILE - 8, TILE)
        own = [state[slot, field, rows, :] for field in range(3)]
        here, _ = cell(*own)
        fluxes = face(ghost, here) if bottom else face(here, ghost)
        push = SCALE * fluxes[1] + (SLOPE * own[0]) * ghost_ground
        row = sublanes()
        sign = -1.0 if bottom else 1.0
        chosen = row == (0 if bottom else 7)
        for field, value in enumerate((SCALE * fluxes[0], push, SCALE * fluxes[2])):
            rate[slot, field, rows, :] += jnp.where(chosen, sign * value, 0.0)


def column_fix(got, ground, columns):
    upper = lax.axis_index("yb")
    device = lax.axis_index("xb") * 2 + upper
    peer = device + 1 - 2 * upper
    block = pl.ds(pl.multiple_of(peer * 8, 8), 8)
    lines = got[block, :TILE]
    ghost_ground = ground[block, :TILE][3:4]
    mine = columns[...]
    _, ghost = cell(lines[0:1], lines[1:2], lines[2:3])
    _, own = cell(mine[0:1], mine[1:2], mine[2:3])
    low = upper == 0
    left = tuple(jnp.where(low, a, b) for a, b in zip(own, ghost))
    right = tuple(jnp.where(low, b, a) for a, b in zip(own, ghost))
    fluxes = face(left, right)
    sign = jnp.where(low, 1.0, -1.0)
    push = SCALE * fluxes[1] + (SLOPE * mine[0:1]) * ghost_ground
    block8 = stacked(
        [sign * SCALE * fluxes[0], sign * SCALE * fluxes[2], sign * push],
        jnp.zeros((8, TILE), jnp.float32),
    )
    return jnp.transpose(
        jnp.concatenate([block8, jnp.zeros((LANES - 8, TILE), jnp.float32)], 0)
    )


def last_update(ctl, got, ground, columns, state, manning, rate, order, *rest):
    del order
    slots = ctl[MOVE], 1 - ctl[MOVE]
    update(STEPS - 1, ctl, got, ground, columns, state, manning, rate, *rest, slots=slots)


def update(
    step, ctl, got_in, ground_in, columns_in, state_in, manning_in, rate_in, *rest,
    passing=None, slots=(0, 1),
):
    more = step + 1 < STEPS
    fresh_out, *lines_to, delta_out = rest[: 4 if more else 6]
    rest = rest[4 if more else 6 :]
    state, manning, rate, fresh, got, ground, columns, first, second, delta_keep, sems = rest
    out, columns_out = first, second
    small = start_all(
        ((got_in, got), (ground_in, ground), (columns_in, columns)), sems, 5 * PARTS
    )
    size = 2 * TILE // PARTS
    parts = [
        (slot, slice(k * size, (k + 1) * size)) for slot in slots for k in range(PARTS // 2)
    ]
    incoming = []
    for index, (slot, rows) in enumerate(parts):
        incoming.append(
            start_all(
                (
                    (rate_in.at[slot, :, rows], rate.at[slot, :, rows]),
                    (state_in.at[slot, :, rows], state.at[slot, :, rows]),
                    (manning_in.at[slot, rows], manning.at[slot, rows]),
                ),
                sems,
                3 * index,
            )
        )
    wait_all(small)
    upper = lax.axis_index("yb")
    devices = 2 * lax.axis_size("xb")
    begin = TILE if got.shape[1] > TILE else 0
    tops = got[0:8, begin : begin + LANES]
    for peer in range(1, devices):
        tops = jnp.maximum(tops, got[peer * 8 : peer * 8 + 8, begin : begin + LANES])
    delta = (COURANT * SPACING) / tops[TOP : TOP + 1, :]
    delta = jnp.concatenate([delta, delta], 1)
    delta_keep[...] = jnp.broadcast_to(delta, (8, TILE))
    outgoing = start_all(((delta_keep, delta_out),), sems, 5 * PARTS + 3)
    fix = column_fix(got, ground, columns)
    facing = jnp.where(upper > 0, ctl[SLOT_LOW], 1 - ctl[SLOT_LOW])
    begin = pl.multiple_of((1 - upper) * LANES, LANES)
    goal = (1 - upper) * (LANES - 1)
    lane = lax.broadcasted_iota(jnp.int32, (size, LANES), 1)
    total = jnp.zeros((ROWS, TILE), jnp.float32)
    for index, (slot, part_rows) in enumerate(parts):
        wait_all(incoming[index])
        if part_rows.start == 0:
            correct_rows(ctl, slot, got, ground, state, rate, True)
        if part_rows.stop == TILE:
            correct_rows(ctl, slot, got, ground, state, rate, False)

        @pl.when(facing == slot)
        def _(slot=slot, part_rows=part_rows):
            for field in range(3):
                turned = pltpu.roll(
                    fix[part_rows], lax.rem(goal + LANES - field, LANES), 1
                )
                rate[slot, field, part_rows, pl.ds(begin, LANES)] += jnp.where(
                    lane == goal, turned, 0.0
                )

        wet_now = flag(ctl, WET + 2 * step + slot)

        def group(index, best, slot=slot, wet_now=wet_now):
            rows = pl.ds(pl.multiple_of(index * ROWS, ROWS), ROWS)
            old = tuple(state[slot, field, rows, :] for field in range(3))
            slopes = tuple(rate[slot, field, rows, :] for field in range(3))
            h, hu, hv = moved_on(old, slopes, manning[slot, rows, :], delta, wet_now)
            fresh[slot, 0, rows, :] = h
            fresh[slot, 1, rows, :] = hu
            fresh[slot, 2, rows, :] = hv
            if more:
                along_x, along_y = cell(h, hu, hv)
                best = jnp.maximum(best, jnp.maximum(along_x[5], along_y[5]))
            return best

        best = lax.fori_loop(
            part_rows.start // ROWS,
            part_rows.stop // ROWS,
            group,
            jnp.zeros((ROWS, TILE), jnp.float32),
        )
        if more:
            best = jnp.where(flag(ctl, WET + 2 * step + 2 + slot), best, 0.0)
            total = jnp.maximum(total, best)
        if more:
            outgoing += start_all(
                ((fresh.at[slot, :, part_rows], fresh_out.at[slot, :, part_rows]),),
                sems,
                3 * PARTS + index,
            )
        elif index >= PARTS // 2:
            outgoing += start_all(
                ((fresh.at[slot, :, part_rows], fresh_out.at[:, part_rows]),),
                sems,
                3 * PARTS + index,
            )
        if not more and part_rows.stop == TILE:
            late, low, high = (
                (first, *lines_to[:2]) if index < PARTS // 2 else (second, *lines_to[2:])
            )
            late_rows(fresh.at[slot], late)
            outgoing += start_all(
                ((late.at[:, :HALF], low), (late.at[:, HALF:], high)),
                sems,
                4 * PARTS + (0 if index < PARTS // 2 else 2),
            )
        if passing and index == PARTS // 2:
            passing.middle()
    if more:
        messages(ctl, fresh, None, jnp.max(total, keepdims=True), out, columns_out)
        pairs = zip((out, columns_out), lines_to)
        outgoing += start_all(tuple(pairs), sems, 4 * PARTS)
    wait_all(outgoing)


def vmem():
    return pl.BlockSpec(memory_space=pltpu.VMEM)


def smem():
    return pl.BlockSpec(memory_space=pltpu.SMEM)


def hbm():
    return pl.BlockSpec(memory_space=pltpu.HBM)


def anywhere():
    return pl.BlockSpec(memory_space=pl.ANY)


def call(
    kernel, outs, out_specs, in_specs, flops, scratch=(), aliases=None, room=VMEM_BYTES, moved=4
):
    return pl.pallas_call(
        kernel,
        scratch_shapes=scratch,
        input_output_aliases=aliases or {},
        out_shape=outs,
        in_specs=in_specs,
        out_specs=out_specs,
        compiler_params=pltpu.CompilerParams(vmem_limit_bytes=room),
        cost_estimate=pl.CostEstimate(flops=flops, bytes_accessed=moved << 20, transcendentals=0),
    )


def f32(*shape):
    return jax.ShapeDtypeStruct(shape, jnp.float32)


def spread(fast):
    return lax.all_to_all(fast, ("xb", "yb"), split_axis=0, concat_axis=0, tiled=True)


def body(state, bed, manning, neighbours, wet, moves):
    shape = f32(*state.shape)
    devices = lax.axis_size("xb") * lax.axis_size("yb")
    whole = pltpu.VMEM(state.shape, jnp.float32)
    part = pltpu.VMEM(bed.shape, jnp.float32)
    tile_shape = f32(*state.shape[1:])
    early_shape = f32(5, EARLY, TILE)
    early_state = f32(3, EARLY, TILE)
    late_shape = f32(3, LATE, TILE)
    half_shape = f32(3, HALF, TILE)
    delta_shape = f32(8, TILE)

    def buffer(like):
        return pltpu.VMEM(like.shape, jnp.float32)

    piece_shapes = tuple(f32(5, end - begin, TILE) for begin, end in PIECES)
    out, columns, ctl = call(
        opening,
        (
            f32(8 * devices, TILE + LANES),
            f32(8, TILE),
            jax.ShapeDtypeStruct((CONTROLS,), jnp.int32),
        ),
        (vmem(), vmem(), smem()),
        [hbm()] * 5,
        4 << 20,
        [
            whole,
            part,
            pltpu.SMEM(neighbours.shape[::-1], jnp.int32),
            pltpu.SMEM(wet.shape, jnp.int32),
            pltpu.SMEM(moves.shape, jnp.int32),
            pltpu.SemaphoreType.DMA((6,)),
        ],
    )(state, bed, neighbours.T, wet, moves)
    state_first = state
    ground = None
    deltas = []
    for step in range(STEPS):
        got = spread(out)
        ground = got if step == 0 else ground
        scratch = [whole, part, whole, pltpu.SemaphoreType.DMA((3 * CHUNKS,))]
        piece_scratch = [
            [buffer(piece), pltpu.SemaphoreType.DMA((2,))] for piece in piece_shapes
        ]
        if step == 1:
            rate, leaving = call(
                rates_and_leaving,
                (shape, piece_shapes[0]),
                (hbm(),) * 2,
                [smem()] + [hbm()] * 5,
                16 << 20,
                scratch + piece_scratch[0],
            )(ctl, state, bed, state_first, manning, early_first[0])
            early_second = [shifted(leaving, "xb", 1)]
        elif step == 2:
            rate = call(rates_after, shape, hbm(), [smem()] + [hbm()] * 3, 16 << 20, scratch)(
                ctl, state, bed, early_second[0]
            )
        else:
            rate, *leaving = call(
                rates_and_splitting,
                (shape,) + piece_shapes,
                (hbm(),) * 3,
                [smem()] + [hbm()] * 3,
                16 << 20,
                scratch + [buffer(early_shape), pltpu.SemaphoreType.DMA((5,))],
            )(ctl, state, bed, manning)
            held = call(
                hold, piece_shapes[0], hbm(), [hbm()] * 3, 1 << 10, aliases={2: 0}
            )(rate, got, leaving[0])
            early_first = [shifted(held, "xb", 1)]
        more = step + 1 < STEPS
        shapes = (f32(8 * devices, TILE), f32(8, TILE)) if more else (half_shape,) * 4
        passing = step == 1
        work = [
            whole,
            part,
            whole,
            whole,
            pltpu.VMEM(got.shape, jnp.float32),
            pltpu.VMEM(ground.shape, jnp.float32),
            pltpu.VMEM((8, TILE), jnp.float32),
            buffer(shapes[0] if more else late_shape),
            buffer(shapes[1] if more else late_shape),
            buffer(delta_shape),
            pltpu.SemaphoreType.DMA((5 * PARTS + 4,)),
        ]
        operands = ctl, got, ground, columns, state, manning, rate
        if not more:
            break
        outs = call(
            functools.partial(update_and_leaving if passing else update, step),
            (shape,) + shapes + (delta_shape,) + ((piece_shapes[1],) if passing else ()),
            (hbm(),) * (5 if passing else 4),
            [smem()] + [hbm()] * (9 if passing else 6),
            8 << 20,
            work + (piece_scratch[1] if passing else []),
            moved=10,
        )(*operands, *((state_first, bed, early_first[1]) if passing else ()))
        state, out, columns, delta, *passed = outs
        deltas.append(delta)
        if step == 0:
            held = call(
                hold, piece_shapes[1], hbm(), [hbm()] * 3, 1 << 10, aliases={2: 0}
            )(delta, delta, leaving[1])
            early_first.append(shifted(held, "xb", 1))
        elif step == 1:
            early_second.append(shifted(passed[0], "xb", 1))

    staying, late_first, rest_first, late_second, rest_second, delta = call(
        last_update,
        (tile_shape,) + shapes + (delta_shape,),
        (hbm(),) * 6,
        [smem()] + [hbm()] * 7,
        8 << 20,
        work,
        moved=10,
    )(*operands, early_second[1])
    deltas.append(delta)
    room = 16 << 20
    late_arrived = shifted(late_first, "xb", 1)
    rest_arrived = shifted(rest_first, "xb", 1)
    second, late_second, rest_second = call(
        repeat_second,
        (early_state, half_shape, half_shape),
        (anywhere(), vmem(), vmem()),
        [smem()] + [vmem()] * 3 + [anywhere()] * 4,
        8 << 20,
        [buffer(early_shape), buffer(early_state), pltpu.SemaphoreType.DMA((4,))],
        room=room,
    )(ctl, *deltas, *early_second, late_second, rest_second)

    def pass_late(arrived, own):
        leaving = call(
            second_late,
            half_shape,
            vmem(),
            [smem(), vmem(), vmem(), anywhere()],
            1 << 10,
            room=room,
        )(ctl, arrived, own, second)
        return shifted(leaving, "xb", 1)

    late_next = pass_late(late_arrived, late_second)
    rest_next = pass_late(rest_arrived, rest_second)
    final = call(
        repeat_first,
        shape,
        hbm(),
        [smem()] + [vmem()] * 3 + [anywhere()] * 5,
        8 << 20,
        [
            buffer(early_shape),
            buffer(early_state),
            buffer(tile_shape),
            buffer(half_shape),
            buffer(half_shape),
            pltpu.SemaphoreType.DMA((4,)),
        ],
        room=room,
    )(ctl, *deltas, *early_first, late_arrived, rest_arrived, staying)
    final = call(
        finish_late,
        shape,
        hbm(),
        [smem(), vmem(), vmem(), hbm()],
        1 << 20,
        [pltpu.VMEM((3, TILE - HALF, TILE), jnp.float32), pltpu.SemaphoreType.DMA((3,))],
        {3: 0},
        room=room,
    )(ctl, late_next, second, final)
    return call(
        finish_rest,
        shape,
        hbm(),
        [smem(), vmem(), hbm()],
        1 << 20,
        [pltpu.SemaphoreType.DMA((1,))],
        {2: 0},
        room=room,
    )(ctl, rest_next, final)


def solution(mesh):
    placed = (
        P(("runs", "xb", "yb"), None, None, None),
        P(("runs", "xb", "yb"), None, None),
        P(("runs", "xb", "yb"), None, None),
        P("runs", None),
        P(None, "runs"),
        P(None, "runs"),
    )
    return jax.shard_map(
        body,
        mesh=mesh,
        in_specs=placed,
        out_specs=P(("runs", "xb", "yb"), None, None, None),
        check_vma=False,
    )
```
